32 devices in a mesh: row: 8 (over z, y), col: 4 (over x, core).
Axes of the slice: x: 2, y: 2, z: 4, core: 2. Of those that a mesh axis runs over, the one named last changes fastest.
Arguments:
- features: bfloat16 [4096, 128], P(('row', 'col')), may hold values from -6 to 6
- node_valid: int32 [4096], P(('row', 'col')), may hold values 0 or 1
- cluster: int32 [4096], P(('row', 'col')), may hold values from 0 to 15
- block_keep: int32 [32, 32], P('row', 'col'), may hold values from 0 to 1, as said below
- edge_weight: bfloat16 [4096, 4096], P('row', 'col'), may hold values from 0 to 3, as said below
- weight_one: bfloat16 [13, 128, 256], replicated, may hold values from -0.15625 to 0.15625
- bias_one: float32 [256], replicated, may hold values from -3 to 3
- gain_one: float32 [256], replicated, may hold values from 0.25 to 1.75
- shift_one: float32 [256], replicated, may hold values from -3 to 3
- weight_two: bfloat16 [13, 256, 256], replicated, may hold values from -0.109375 to 0.109375
- bias_two: float32 [256], replicated, may hold values from -3 to 3
- gain_two: float32 [256], replicated, may hold values from 0.25 to 1.75
- shift_two: float32 [256], replicated, may hold values from -3 to 3
- cotangent: bfloat16 [4096, 256], P(('row', 'col')), may hold values from -6 to 6
Outputs:
- activations: float32 [4096, 256], P(('row', 'col'))
- input_grad: float32 [4096, 128], P(('row', 'col'))
- weight_grad_one: float32 [13, 128, 256], replicated
- bias_grad_one: float32 [256], replicated
- gain_grad_one: float32 [256], replicated
- shift_grad_one: float32 [256], replicated
- weight_grad_two: float32 [13, 256, 256], replicated
- bias_grad_two: float32 [256], replicated
- gain_grad_two: float32 [256], replicated
- shift_grad_two: float32 [256], replicated
The draws below stay inside these ranges and needn't reach their ends.
Inputs may be any that keep to these rules, and one draw needn't show every extreme that they name: `block_keep`: symmetric in node-block order: the entry in row block i and column block b equals the entry in row block sigma(b * 128) // 128 and the column block b' with sigma(b' * 128) = i * 128. `edge_weight`: the graph is undirected: the entry in row a and grid column c equals the entry in row sigma(c) and the grid column c' with sigma(c') = a.
All inputs are finite; a program needn't handle non-finite values. No bound on the sum of `node_valid` on one device may be relied on, other than what follows from the above.
Results may differ from the reference program's by a relative error of at most 0.028.
Values may be sent and summed in bfloat16 or wider, within the bound.
No kernel may reach another device: no remote copies, remote signals or barrier semaphores. Data moves between devices by JAX's collectives and lax.ppermute only.
A program may use at most 128 MiB of HBM per device.

```python
import math
import jax
import jax.numpy as jnp
import numpy as np
from jax import lax

IN_WIDTH = 128
WIDTH = 256
ORDER = 13
EDGE_BLOCK = 128
CLUSTERS = 16
NODE_DEV = 128
NODES = 4096
BLOCK_COUNT = 32
N_ROW = 8
N_COL = 4


def grid_nodes(count, unit):
    column = jnp.arange(count, dtype=jnp.int32) * unit
    block_col = column // (NODE_DEV * N_ROW)
    block_row = column // NODE_DEV % N_ROW
    return ((block_row * N_COL + block_col) * NODE_DEV + column % NODE_DEV) // unit


def draw_edge_weight(key, part):
    key = jax.random.fold_in(key, 11)
    presence_key, value_key = jax.random.split(key)
    chance = jax.random.uniform(presence_key, (NODES, NODES), dtype=jnp.float32)
    values = jax.random.uniform(value_key, (NODES, NODES), dtype=jnp.float32, minval=0.25, maxval=1.75)
    sparse = jnp.where(chance < min(0.5, 512.0 / NODES), values, jnp.float32(0.0))
    upper = jnp.arange(NODES)[:, None] <= jnp.arange(NODES)[None, :]
    mirrored = jnp.where(upper, sparse, sparse.T)
    return mirrored[:, grid_nodes(NODES, 1)].astype(jnp.bfloat16)


def draw_block_keep(key, part):
    key = jax.random.fold_in(key, 12)
    level_key, roll_key = jax.random.split(key)
    level = jax.random.randint(level_key, (BLOCK_COUNT,), 2, 9)
    roll = jax.random.randint(roll_key, (BLOCK_COUNT, BLOCK_COUNT), 0, 8)
    upper = jnp.arange(BLOCK_COUNT)[:, None] <= jnp.arange(BLOCK_COUNT)[None, :]
    mirrored = jnp.where(upper, roll, roll.T)
    kept = (mirrored < jnp.minimum(level[:, None], level[None, :])).astype(jnp.int32)
    return kept[:, grid_nodes(BLOCK_COUNT, EDGE_BLOCK)]


def place_ends(array, stream_key, least, largest):
    extent = array.shape
    index_at = [jax.random.randint(jax.random.fold_in(stream_key, axis), (), 0, extent[axis]) for axis in range(len(extent))]
    array = array.at[tuple(index_at)].set(least)
    longest = extent.index(max(extent))
    index_at[longest] = (index_at[longest] + 1) % extent[longest]
    return array.at[tuple(index_at)].set(largest)


def levels(stream_key, dims, cuts, least, top_value):
    factor_of = 1.0
    for dim, parts in cuts:
        steps = jax.random.uniform(jax.random.fold_in(jax.random.fold_in(stream_key, 6), dim), (parts,), jnp.float32, least / len(cuts), top_value / len(cuts))
        factor_of = factor_of * jnp.repeat(jnp.exp(steps), dims[dim] // parts).reshape((-1,) + (1,) * (len(dims) - 1 - dim))
    return factor_of


def cumulative_ranks(number_of, skew):
    portions = [(1 << 20) // math.isqrt(standing ** skew) + 1 for standing in range(1, number_of + 1)]
    deviation = 1 + sum(portions) // (1 << 30)
    return np.cumsum(np.array([max(1, weight // deviation) for weight in portions]))


def skewed_ids(rng, shape, number_of, skew):
    table = cumulative_ranks(number_of, skew)
    pick = jax.random.randint(jax.random.fold_in(rng, 1), shape, 0, int(table[number_of - 1]))
    standing = jnp.searchsorted(jnp.asarray(table, jnp.int32), pick, side="right")
    return jax.random.permutation(jax.random.fold_in(rng, 2), number_of)[standing].astype(jnp.int32)


def scatter_about(rng, dims, deviation, most, shards=(), held_as=jnp.bfloat16):
    drawn = deviation * jax.random.normal(rng, dims, jnp.float32)
    if shards:
        drawn = drawn * levels(rng, dims, shards, -0.22, 0.18)
    return jnp.clip(drawn, -most, most).astype(held_as)


def setup_inputs(seed: int = 0) -> dict:
    arg_keys = jax.random.split(jax.random.key(seed), 15)
    features = scatter_about(arg_keys[0], (NODES, IN_WIDTH), 1.0, 6.0, ((0, 32),))
    node_valid = place_ends((jax.random.randint(arg_keys[1], (NODES,), 0, 8) < 7).astype(jnp.int32), jax.random.fold_in(arg_keys[1], 1), 0, 1)
    cluster = place_ends(skewed_ids(arg_keys[2], (NODES,), CLUSTERS, 2), jax.random.fold_in(arg_keys[2], 3), 0, CLUSTERS - 1).astype(jnp.int32)
    block_keep = draw_block_keep(jax.random.fold_in(arg_keys[14], 71), 0)
    edge_weight = draw_edge_weight(jax.random.fold_in(arg_keys[14], 71), 0)
    weight_one = scatter_about(arg_keys[5], (ORDER, IN_WIDTH, WIDTH), (ORDER * IN_WIDTH) ** -0.5, 0.15625)
    bias_one = scatter_about(arg_keys[6], (WIDTH,), 0.5, 3.0, (), jnp.float32)
    gain_one = jnp.clip(1.0 + 0.15 * jax.random.normal(arg_keys[7], (WIDTH,), jnp.float32), 0.25, 1.75)
    shift_one = scatter_about(arg_keys[8], (WIDTH,), 0.3, 3.0, (), jnp.float32)
    weight_two = scatter_about(arg_keys[9], (ORDER, WIDTH, WIDTH), (ORDER * WIDTH) ** -0.5, 0.109375)
    bias_two = scatter_about(arg_keys[10], (WIDTH,), 0.5, 3.0, (), jnp.float32)
    gain_two = jnp.clip(1.0 + 0.15 * jax.random.normal(arg_keys[11], (WIDTH,), jnp.float32), 0.25, 1.75)
    shift_two = scatter_about(arg_keys[12], (WIDTH,), 0.3, 3.0, (), jnp.float32)
    cotangent = scatter_about(arg_keys[13], (NODES, WIDTH), 1.0, 6.0, ((0, 32),))
    return {"features": features, "node_valid": node_valid, "cluster": cluster, "block_keep": block_keep, "edge_weight": edge_weight, "weight_one": weight_one, "bias_one": bias_one, "gain_one": gain_one, "shift_one": shift_one, "weight_two": weight_two, "bias_two": bias_two, "gain_two": gain_two, "shift_two": shift_two, "cotangent": cotangent}


@jax.custom_vjp
def low(v):
    return lax.optimization_barrier(v.astype(jnp.bfloat16)).astype(jnp.float32)

@jax.custom_vjp
def low_back(v):
    return v

def low_keep(v):
    return (low(v), None)

def low_pass(kept, grad):
    return (grad,)

def back_keep(v):
    return (v, None)

def back_low(kept, grad):
    return (low(grad),)
low.defvjp(low_keep, low_pass)
low_back.defvjp(back_keep, back_low)

def grid_order():
    column = jnp.arange(NODES, dtype=jnp.int32)
    block_col = column // (NODE_DEV * N_ROW)
    block_row = column // NODE_DEV % N_ROW
    return (block_row * N_COL + block_col) * NODE_DEV + column % NODE_DEV

def normalized(node_valid, cluster, block_keep, edge_weight, order):
    blocks = jnp.repeat(jnp.repeat(block_keep, EDGE_BLOCK, axis=0), EDGE_BLOCK, axis=1)
    linked = (cluster[:, None] == cluster[order][None, :]) & (node_valid[:, None] == 1)
    linked = linked & (node_valid[order][None, :] == 1) & (blocks == 1)
    masked = jnp.where(linked, edge_weight.astype(jnp.float32), jnp.float32(0.0))
    degree = 1.0 + lax.optimization_barrier(jnp.sum(masked, axis=1))
    scale = lax.rsqrt(degree)
    return low(masked * scale[:, None] * scale[order][None, :])

def finish(mixed, gain, shift, valid_rows):
    active = jax.nn.gelu(mixed, approximate=False)
    centered = active - lax.optimization_barrier(jnp.mean(active, axis=-1, keepdims=True))
    variance = lax.optimization_barrier(jnp.mean(centered * centered, axis=-1, keepdims=True))
    return (centered * lax.rsqrt(variance + 1e-05) * gain + shift) * valid_rows[:, None]

def propagate(adjacency, order, value):
    return low_back(jnp.dot(adjacency, value[order], precision=lax.Precision.HIGHEST))

def layer(inputs, adjacency, order, weight, bias, gain, shift, valid_rows):
    previous = inputs
    first_low = low(previous)
    current = -propagate(adjacency, order, first_low)
    lowered = [first_low, low(current)]
    for position in range(2, ORDER):
        upcoming = -2.0 * propagate(adjacency, order, lowered[-1]) - previous
        previous, current = (current, upcoming)
        lowered.append(low(current))
    stacked = jnp.stack(lowered)
    mixed = jnp.einsum('kni,kio->no', stacked, weight, precision=lax.Precision.HIGHEST) + bias
    return finish(low_back(mixed), gain, shift, valid_rows)

def reference(features, node_valid, cluster, block_keep, edge_weight, weight_one, bias_one, gain_one, shift_one, weight_two, bias_two, gain_two, shift_two, cotangent):
    order = grid_order()
    adjacency = normalized(node_valid, cluster, block_keep, edge_weight, order)
    valid_rows = node_valid.astype(jnp.float32)

    def forward(inputs, first_weight, first_bias, first_gain, first_shift, second_weight, second_bias, second_gain, second_shift):
        hidden = layer(inputs, adjacency, order, first_weight, first_bias, first_gain, first_shift, valid_rows)
        return layer(hidden, adjacency, order, second_weight, second_bias, second_gain, second_shift, valid_rows)
    activations, pullback = jax.vjp(forward, features.astype(jnp.float32), weight_one.astype(jnp.float32), bias_one, gain_one, shift_one, weight_two.astype(jnp.float32), bias_two, gain_two, shift_two)
    grads = pullback(cotangent.astype(jnp.float32))
    return (activations, grads[0], grads[1], grads[2], grads[3], grads[4], grads[5], grads[6], grads[7], grads[8])
```

```python
import functools

import jax
import jax.numpy as jnp
from jax import lax
from jax.sharding import PartitionSpec as P

ORDER = 13
CLUSTERS = 16
HELD_BYTES = 1 << 25


def finish(mixed, gain, shift, valid_rows):
    active = jax.nn.gelu(mixed, approximate=False)
    centered = active - jnp.mean(active, axis=-1, keepdims=True)
    variance = jnp.mean(centered * centered, axis=-1, keepdims=True)
    return (centered * lax.rsqrt(variance + 1e-05) * gain + shift) * valid_rows[:, None]


def forward_product(adjacency, piece_low):
    partial_value = jnp.dot(
        adjacency,
        lax.all_gather(piece_low, "row", axis=0, tiled=True),
        preferred_element_type=jnp.float32,
    )
    return lax.psum_scatter(partial_value, "col", scatter_dimension=0, tiled=True)


def backward_product(adjacency, piece_low):
    partial_value = lax.dot_general(
        adjacency,
        lax.all_gather(piece_low, "col", axis=0, tiled=True),
        (((0,), (0,)), ((), ())),
        preferred_element_type=jnp.float32,
    )
    return lax.psum_scatter(
        partial_value.astype(jnp.bfloat16), "row", scatter_dimension=0, tiled=True
    ).astype(jnp.float32)


def layer_forward(adjacency, inputs, weight, bias, gain, shift, valid_rows):
    first_low = inputs.astype(jnp.bfloat16)
    second = -forward_product(adjacency, first_low)
    second_low = second.astype(jnp.bfloat16)

    def advance(state_pair, unused):
        previous, current, current_low = state_pair
        upcoming = -2.0 * forward_product(adjacency, current_low) - previous
        upcoming_low = upcoming.astype(jnp.bfloat16)
        return ((current, upcoming, upcoming_low), upcoming_low)

    ignored, others = lax.scan(advance, (inputs, second, second_low), None, length=ORDER - 2)
    stacked = jnp.concatenate([first_low[None], second_low[None], others], axis=0)
    mixed = jnp.einsum("kni,kio->no", stacked, weight, preferred_element_type=jnp.float32) + bias
    return (stacked, mixed, finish(mixed, gain, shift, valid_rows))


def layer_backward(adjacency, stacked, mixed, upstream, weight, gain, shift, valid_rows):

    def local_finish(mixed_in, gain_in, shift_in):
        return finish(mixed_in, gain_in, shift_in, valid_rows)

    ignored, pullback = jax.vjp(local_finish, mixed, gain, shift)
    mixed_grad, gain_grad, shift_grad = pullback(upstream)
    mixed_low = mixed_grad.astype(jnp.bfloat16)
    bias_grad = jnp.sum(mixed_low.astype(jnp.float32), axis=0)
    weight_grad = jnp.einsum("kni,no->kio", stacked, mixed_low, preferred_element_type=jnp.float32)
    direct = jnp.einsum("no,kio->kni", mixed_low, weight, preferred_element_type=jnp.float32)

    def retreat(state_pair, direct_term):
        later_two, later_one = state_pair
        current = (
            direct_term
            - 2.0 * backward_product(adjacency, later_one.astype(jnp.bfloat16))
            - later_two
        )
        return ((later_one, current), None)

    start_pair = (jnp.zeros_like(direct[0]), direct[ORDER - 1])
    (second_grad, first_grad), unused = lax.scan(
        retreat, start_pair, direct[1 : ORDER - 1], reverse=True
    )
    input_grad = (
        direct[0] - backward_product(adjacency, first_grad.astype(jnp.bfloat16)) - second_grad
    )
    return (input_grad, weight_grad, bias_grad, gain_grad, shift_grad)


def exchange(value, axis, size, step):
    return lax.ppermute(value, axis, [(place, place ^ step) for place in range(size)])


def natural_order(pieces, index, size):
    rest = pieces.shape[1:]
    bits = size.bit_length() - 1
    for bit in range(bits):
        split = pieces.reshape((size >> (bit + 1), 2, 1 << bit) + rest)
        split = jnp.where((index >> bit) & 1 == 1, split[:, ::-1], split)
        pieces = split.reshape((size,) + rest)
    return pieces


def gather_along(value, axis, size):
    index = lax.axis_index(axis)
    pieces = [value] + [exchange(value, axis, size, step) for step in range(1, size)]
    return natural_order(jnp.stack(pieces), index, size)


def sum_everywhere(part, n_row, n_col):
    row, col = lax.axis_index("row"), lax.axis_index("col")
    width = part.shape[1]
    bits = n_col.bit_length() - 1
    held = part
    for bit in range(bits):
        upper = (col >> bit) & 1 == 1
        half = held.shape[0] // 2
        low_half, high_half = held[:half], held[half:]
        sent = jnp.where(upper, low_half, high_half).astype(jnp.bfloat16)
        kept = jnp.where(upper, high_half, low_half)
        held = kept + exchange(sent, "col", n_col, 1 << bit).astype(jnp.float32)
    pieces = held.reshape(n_row, held.shape[0] // n_row, width)
    total = lax.dynamic_index_in_dim(pieces, row, 0, False)
    for step in range(1, n_row):
        sent = lax.dynamic_index_in_dim(pieces, row ^ step, 0, False).astype(jnp.bfloat16)
        total = total + exchange(sent, "row", n_row, step).astype(jnp.float32)
    whole = gather_along(total.astype(jnp.bfloat16), "row", n_row)
    whole = whole.reshape(held.shape[0], width)
    for bit in reversed(range(bits)):
        upper = (col >> bit) & 1 == 1
        other = exchange(whole, "col", n_col, 1 << bit)
        whole = jnp.where(
            upper, jnp.concatenate([other, whole]), jnp.concatenate([whole, other])
        )
    return whole.astype(jnp.float32)


def exclusive_counts(member):
    count = member.shape[-1]
    before = jnp.arange(count)[:, None] < jnp.arange(count)[None, :]
    return jnp.dot(
        member.astype(jnp.bfloat16),
        before.astype(jnp.bfloat16),
        preferred_element_type=jnp.float32,
    ).astype(jnp.int32)


def assign(codes, n_row):
    cluster, valid = codes >> 1, codes & 1
    labels = jnp.arange(CLUSTERS)
    sizes = jnp.sum(
        (cluster.reshape(1, -1) == labels[:, None]) & (valid.reshape(1, -1) == 1), axis=1
    )
    ahead = (sizes[None, :] > sizes[:, None]) | (
        (sizes[None, :] == sizes[:, None]) & (labels[None, :] < labels[:, None])
    )
    rank = jnp.sum(ahead, axis=1)
    others = n_row - 1
    turn, place = (rank - 1) // others, (rank - 1) % others
    group = jnp.where(rank == 0, 0, 1 + jnp.where(turn == 0, place, others - 1 - place))
    of_node = jnp.sum(
        jnp.where(cluster[None] == labels[:, None, None, None], group[:, None, None, None], 0),
        axis=0,
    )
    return jnp.where(valid == 1, of_node, n_row)


def compact(
    codes,
    group,
    features,
    block_keep,
    edge_weight,
    weight_one,
    bias_one,
    gain_one,
    shift_one,
    weight_two,
    bias_two,
    gain_two,
    shift_two,
    cotangent,
    places,
    slots,
    n_row,
    n_col,
    own_cap,
    send_cap,
):
    row, col = lax.axis_index("row"), lax.axis_index("col")
    own_nodes = features.shape[0]
    span = n_col * own_cap
    targets = row ^ jnp.arange(n_row)

    def in_col(value):
        return lax.dynamic_index_in_dim(value, col, 1, False).reshape(-1)

    def in_row(value):
        return lax.dynamic_index_in_dim(value, row, 0, False).reshape(-1)

    both = gather_along(jnp.concatenate([features, cotangent], axis=1), "row", n_row)
    both = both.reshape(n_row * own_nodes, -1)

    row_codes, col_codes = in_row(codes), in_col(codes)
    tile_rows, tile_cols = edge_weight.shape
    blocks_down, blocks_across = block_keep.shape
    side = tile_rows // blocks_down
    linked = (row_codes[:, None] == col_codes[None, :]) & (row_codes[:, None] & 1 == 1)
    linked = linked.reshape(blocks_down, side, blocks_across, side) & (
        block_keep[:, None, :, None] == 1
    )
    masked = jnp.where(linked.reshape(tile_rows, tile_cols), edge_weight, 0)
    pick_rows = (in_row(group)[None, None, :] == targets[:, None, None]) & (
        in_row(slots)[None, None, :] == jnp.arange(send_cap)[None, :, None]
    )
    pick_cols = (in_col(group)[None, None, :] == targets[:, None, None]) & (
        in_col(places)[None, None, :] == jnp.arange(own_cap)[None, :, None]
    )
    picked = jnp.einsum("sta,ac->stc", pick_rows.astype(jnp.bfloat16), masked)
    packed = jnp.einsum("stc,suc->stu", picked, pick_cols.astype(jnp.bfloat16))
    received = jnp.stack(
        [packed[0]] + [exchange(packed[step], "row", n_row, step) for step in range(1, n_row)]
    )

    standing = jnp.arange(n_col)[None, :, None] * own_cap + places
    fits_here = jnp.where(group == row, standing, -1).reshape(n_row, -1)
    slot_of = slots.reshape(n_row, -1)
    target = jnp.max(
        jnp.where(
            slot_of[:, None, :] == jnp.arange(send_cap)[None, :, None], fits_here[:, None, :], -1
        ),
        axis=2,
    )
    target = natural_order(target, row, n_row)
    spread = (target[:, :, None] == jnp.arange(span)[None, None, :]).astype(jnp.bfloat16)
    own_block = jnp.einsum("stu,stw->uw", received, spread).astype(jnp.bfloat16)
    block = lax.all_gather(own_block, "col", axis=0, tiled=True)

    scale = lax.rsqrt(1.0 + jnp.sum(block, axis=1, dtype=jnp.float32))
    adjacency = (block.astype(jnp.float32) * scale[:, None] * scale[None, :]).astype(jnp.bfloat16)

    first = (col * own_cap + jnp.arange(own_cap))[:, None] == jnp.arange(span)[None, :]
    previous = first.astype(jnp.float32)
    current = -lax.dynamic_slice_in_dim(adjacency, col * own_cap, own_cap, 0).astype(jnp.float32)
    lowered = [current.astype(jnp.bfloat16)]
    for position in range(2, ORDER):
        upcoming = (
            -2.0 * jnp.dot(lowered[-1], adjacency, preferred_element_type=jnp.float32) - previous
        )
        previous, current = current, upcoming
        lowered.append(upcoming.astype(jnp.bfloat16))
    polynomials = jnp.concatenate(lowered, axis=0)

    def apply(value_low):
        everyone = lax.all_gather(value_low, "col", axis=0, tiled=True)
        result = jnp.dot(polynomials, everyone, preferred_element_type=jnp.float32)
        result = result.astype(jnp.bfloat16).reshape(ORDER - 1, own_cap, -1)
        return jnp.concatenate([value_low[None], result], axis=0)

    pick_own = (
        (in_col(group)[None, :] == row) & (in_col(places)[None, :] == jnp.arange(own_cap)[:, None])
    ).astype(jnp.bfloat16)
    mine = jnp.dot(pick_own, both)
    features_own, cotangent_own = mine[:, : features.shape[1]], mine[:, features.shape[1] :]
    held_count = jnp.sum(in_col(group) == row)
    valid_rows = (jnp.arange(own_cap) < held_count).astype(jnp.float32)

    def forward(value_low, weight, bias, gain, shift):
        stacked = apply(value_low)
        mixed = jnp.einsum("kni,kio->no", stacked, weight, preferred_element_type=jnp.float32)
        mixed = mixed + bias
        return stacked, mixed, finish(mixed, gain, shift, valid_rows)

    def backward(stacked, mixed, upstream, weight, gain, shift):
        ignored, pullback = jax.vjp(
            lambda mixed_in, gain_in, shift_in: finish(mixed_in, gain_in, shift_in, valid_rows),
            mixed,
            gain,
            shift,
        )
        mixed_grad, gain_grad, shift_grad = pullback(upstream)
        mixed_low = mixed_grad.astype(jnp.bfloat16)
        bias_grad = jnp.sum(mixed_low.astype(jnp.float32), axis=0)
        weight_grad = jnp.einsum(
            "kni,no->kio", stacked, mixed_low, preferred_element_type=jnp.float32
        )
        spread_grad = apply(mixed_low)
        input_grad = jnp.einsum(
            "kno,kio->ni", spread_grad, weight, preferred_element_type=jnp.float32
        )
        return input_grad, weight_grad, jnp.stack([bias_grad, gain_grad, shift_grad])

    def send_home(value):
        homes = row ^ jnp.arange(n_row)
        node_group = lax.dynamic_index_in_dim(group, col, 1, False)
        node_place = lax.dynamic_index_in_dim(places, col, 1, False)
        pick = (node_group == row)[:, :, None] & (
            node_place[:, :, None] == jnp.arange(own_cap)[None, None, :]
        )
        pieces = jnp.einsum("ilu,uf->ilf", pick.astype(jnp.bfloat16), value.astype(jnp.bfloat16))
        total = lax.dynamic_index_in_dim(pieces, row, 0, False).astype(jnp.float32)
        for step in range(1, n_row):
            sent = lax.dynamic_index_in_dim(pieces, row ^ step, 0, False)
            total = total + exchange(sent, "row", n_row, step).astype(jnp.float32)
        return total

    stacked_one, mixed_one, hidden = forward(features_own, weight_one, bias_one, gain_one, shift_one)
    stacked_two, mixed_two, activations = forward(
        hidden.astype(jnp.bfloat16), weight_two, bias_two, gain_two, shift_two
    )
    activations = send_home(activations)
    hidden_grad, weight_two_grad, rest_two = backward(
        stacked_two, mixed_two, cotangent_own.astype(jnp.float32), weight_two, gain_two, shift_two
    )
    width = weight_two.shape[2]
    part_two = weight_two_grad.reshape(-1, width)
    whole_two = sum_everywhere(part_two, n_row, n_col)
    input_grad, weight_one_grad, rest_one = backward(
        stacked_one, mixed_one, hidden_grad, weight_one, gain_one, shift_one
    )
    part_one = jnp.concatenate([weight_one_grad.reshape(-1, width), rest_one, rest_two])
    unit = n_row * n_col * 8
    extra = -part_one.shape[0] % unit
    part_one = jnp.concatenate([part_one, jnp.zeros((extra, width), jnp.float32)])
    whole_one = sum_everywhere(part_one, n_row, n_col)
    input_grad = send_home(input_grad)
    tail = weight_one.shape[0] * weight_one.shape[1]
    rest = whole_one[tail : tail + 6]
    return (
        activations,
        input_grad,
        whole_one[:tail].reshape(weight_one.shape),
        rest[0],
        rest[1],
        rest[2],
        whole_two.reshape(weight_two.shape),
        rest[3],
        rest[4],
        rest[5],
    )


def general(
    codes,
    features,
    block_keep,
    edge_weight,
    weight_one,
    bias_one,
    gain_one,
    shift_one,
    weight_two,
    bias_two,
    gain_two,
    shift_two,
    cotangent,
    node_valid,
):
    row, col = lax.axis_index("row"), lax.axis_index("col")
    row_codes = lax.dynamic_index_in_dim(codes, row, 0, False).reshape(-1)
    col_codes = lax.dynamic_index_in_dim(codes, col, 1, False).reshape(-1)
    tile_rows, tile_cols = edge_weight.shape
    blocks_down, blocks_across = block_keep.shape
    block_side = tile_rows // blocks_down
    linked = (row_codes[:, None] == col_codes[None, :]) & (row_codes[:, None] & 1 == 1)
    linked = linked.reshape(blocks_down, block_side, blocks_across, block_side) & (
        block_keep[:, None, :, None] == 1
    )
    masked = edge_weight * linked.reshape(tile_rows, tile_cols).astype(jnp.bfloat16)
    degree_rows = 1.0 + lax.psum(jnp.sum(masked, axis=1, dtype=jnp.float32), "col")
    own_nodes = features.shape[0]
    own_degree = lax.dynamic_slice_in_dim(
        degree_rows, lax.axis_index("col") * own_nodes, own_nodes, 0
    )
    degree_cols = lax.all_gather(own_degree, "row", axis=0, tiled=True)
    adjacency = (
        masked.astype(jnp.float32)
        * lax.rsqrt(degree_rows)[:, None]
        * lax.rsqrt(degree_cols)[None, :]
    ).astype(jnp.bfloat16)
    valid_rows = node_valid.astype(jnp.float32)
    stacked_one, mixed_one, hidden = layer_forward(
        adjacency,
        features.astype(jnp.float32),
        weight_one,
        bias_one,
        gain_one,
        shift_one,
        valid_rows,
    )
    stacked_two, mixed_two, activations = layer_forward(
        adjacency, hidden, weight_two, bias_two, gain_two, shift_two, valid_rows
    )
    hidden_grad, weight_two_grad, bias_two_grad, gain_two_grad, shift_two_grad = layer_backward(
        adjacency,
        stacked_two,
        mixed_two,
        cotangent.astype(jnp.float32),
        weight_two,
        gain_two,
        shift_two,
        valid_rows,
    )
    input_grad, weight_one_grad, bias_one_grad, gain_one_grad, shift_one_grad = layer_backward(
        adjacency, stacked_one, mixed_one, hidden_grad, weight_one, gain_one, shift_one, valid_rows
    )
    summed = lax.psum(
        (
            weight_one_grad,
            bias_one_grad,
            gain_one_grad,
            shift_one_grad,
            weight_two_grad,
            bias_two_grad,
            gain_two_grad,
            shift_two_grad,
        ),
        ("row", "col"),
    )
    weight_one_grad, bias_one_grad, gain_one_grad, shift_one_grad = (
        summed[0],
        summed[1],
        summed[2],
        summed[3],
    )
    weight_two_grad, bias_two_grad, gain_two_grad, shift_two_grad = (
        summed[4],
        summed[5],
        summed[6],
        summed[7],
    )
    return (
        activations,
        input_grad,
        weight_one_grad,
        bias_one_grad,
        gain_one_grad,
        shift_one_grad,
        weight_two_grad,
        bias_two_grad,
        gain_two_grad,
        shift_two_grad,
    )


def local(n_row, n_col, *args):
    (
        features,
        node_valid,
        cluster,
        block_keep,
        edge_weight,
        weight_one,
        bias_one,
        gain_one,
        shift_one,
        weight_two,
        bias_two,
        gain_two,
        shift_two,
        cotangent,
    ) = args
    own_nodes = features.shape[0]
    own_cap = own_nodes * n_row * 5 // 16
    send_cap = own_nodes * n_col * 3 // 8
    codes = lax.all_gather(cluster * 2 + node_valid, ("row", "col"), axis=0)
    codes = codes.reshape(n_row, n_col, own_nodes)
    shared = (
        block_keep,
        edge_weight,
        weight_one,
        bias_one,
        gain_one,
        shift_one,
        weight_two,
        bias_two,
        gain_two,
        shift_two,
        cotangent,
    )

    def slow():
        return general(codes, features, *shared, node_valid)

    held = (ORDER - 1) * own_cap * own_cap * n_col * 2
    if held > HELD_BYTES or n_row & (n_row - 1) or n_col & (n_col - 1) or n_row < 2:
        return slow()
    group = assign(codes, n_row)
    member = group[None] == jnp.arange(n_row)[:, None, None, None]
    by_col = member.transpose(0, 2, 1, 3).reshape(n_row, n_col, -1)
    by_row = member.reshape(n_row, n_row, -1)
    places = jnp.sum(jnp.where(by_col, exclusive_counts(by_col), 0), axis=0)
    places = places.reshape(n_col, n_row, own_nodes).transpose(1, 0, 2)
    slots = jnp.sum(jnp.where(by_row, exclusive_counts(by_row), 0), axis=0)
    slots = slots.reshape(n_row, n_col, own_nodes)
    fits = (jnp.max(jnp.sum(by_col, axis=2)) <= own_cap) & (
        jnp.max(jnp.sum(by_row, axis=2)) <= send_cap
    )

    def fast():
        return compact(
            codes, group, features, *shared, places, slots, n_row, n_col, own_cap, send_cap
        )

    return lax.cond(fits, fast, slow)


def solution(mesh):
    placed = (
        P(("row", "col"), None),
        P(("row", "col")),
        P(("row", "col")),
        P("row", "col"),
        P("row", "col"),
        P(),
        P(),
        P(),
        P(),
        P(),
        P(),
        P(),
        P(),
        P(("row", "col"), None),
    )
    return jax.shard_map(
        functools.partial(local, mesh.shape["row"], mesh.shape["col"]),
        mesh=mesh,
        in_specs=placed,
        out_specs=(
            P(("row", "col"), None),
            P(("row", "col"), None),
            P(),
            P(),
            P(),
            P(),
            P(),
            P(),
            P(),
            P(),
        ),
        check_vma=False,
    )
```

```python
import functools

import jax
import jax.numpy as jnp
from jax import lax
from jax.sharding import PartitionSpec as P

ORDER = 13
CLUSTERS = 16
HELD_BYTES = 1 << 25


def finish(mixed, gain, shift, valid_rows):
    active = jax.nn.gelu(mixed, approximate=False)
    centered = active - jnp.mean(active, axis=-1, keepdims=True)
    variance = jnp.mean(centered * centered, axis=-1, keepdims=True)
    return (centered * lax.rsqrt(variance + 1e-05) * gain + shift) * valid_rows[:, None]


def forward_product(adjacency, piece_low):
    partial_value = jnp.dot(
        adjacency,
        lax.all_gather(piece_low, "row", axis=0, tiled=True),
        preferred_element_type=jnp.float32,
    )
    return lax.psum_scatter(partial_value, "col", scatter_dimension=0, tiled=True)


def backward_product(adjacency, piece_low):
    partial_value = lax.dot_general(
        adjacency,
        lax.all_gather(piece_low, "col", axis=0, tiled=True),
        (((0,), (0,)), ((), ())),
        preferred_element_type=jnp.float32,
    )
    return lax.psum_scatter(
        partial_value.astype(jnp.bfloat16), "row", scatter_dimension=0, tiled=True
    ).astype(jnp.float32)


def layer_forward(adjacency, inputs, weight, bias, gain, shift, valid_rows):
    first_low = inputs.astype(jnp.bfloat16)
    second = -forward_product(adjacency, first_low)
    second_low = second.astype(jnp.bfloat16)

    def advance(state_pair, unused):
        previous, current, current_low = state_pair
        upcoming = -2.0 * forward_product(adjacency, current_low) - previous
        upcoming_low = upcoming.astype(jnp.bfloat16)
        return ((current, upcoming, upcoming_low), upcoming_low)

    ignored, others = lax.scan(advance, (inputs, second, second_low), None, length=ORDER - 2)
    stacked = jnp.concatenate([first_low[None], second_low[None], others], axis=0)
    mixed = jnp.einsum("kni,kio->no", stacked, weight, preferred_element_type=jnp.float32) + bias
    return (stacked, mixed, finish(mixed, gain, shift, valid_rows))


def layer_backward(adjacency, stacked, mixed, upstream, weight, gain, shift, valid_rows):

    def local_finish(mixed_in, gain_in, shift_in):
        return finish(mixed_in, gain_in, shift_in, valid_rows)

    ignored, pullback = jax.vjp(local_finish, mixed, gain, shift)
    mixed_grad, gain_grad, shift_grad = pullback(upstream)
    mixed_low = mixed_grad.astype(jnp.bfloat16)
    bias_grad = jnp.sum(mixed_low.astype(jnp.float32), axis=0)
    weight_grad = jnp.einsum("kni,no->kio", stacked, mixed_low, preferred_element_type=jnp.float32)
    direct = jnp.einsum("no,kio->kni", mixed_low, weight, preferred_element_type=jnp.float32)

    def retreat(state_pair, direct_term):
        later_two, later_one = state_pair
        current = (
            direct_term
            - 2.0 * backward_product(adjacency, later_one.astype(jnp.bfloat16))
            - later_two
        )
        return ((later_one, current), None)

    start_pair = (jnp.zeros_like(direct[0]), direct[ORDER - 1])
    (second_grad, first_grad), unused = lax.scan(
        retreat, start_pair, direct[1 : ORDER - 1], reverse=True
    )
    input_grad = (
        direct[0] - backward_product(adjacency, first_grad.astype(jnp.bfloat16)) - second_grad
    )
    return (input_grad, weight_grad, bias_grad, gain_grad, shift_grad)


def exchange(value, axis, size, step):
    return lax.ppermute(value, axis, [(place, place ^ step) for place in range(size)])


def trade(pieces, axis):
    return lax.all_to_all(pieces, axis, 0, 0, tiled=False)


def gather_along(value, axis, size):
    return trade(jnp.broadcast_to(value[None], (size,) + value.shape), axis)


def sum_everywhere(part, n_row, n_col):
    col = lax.axis_index("col")
    width = part.shape[1]
    bits = n_col.bit_length() - 1
    held = part
    for bit in range(bits):
        upper = (col >> bit) & 1 == 1
        half = held.shape[0] // 2
        low_half, high_half = held[:half], held[half:]
        sent = jnp.where(upper, low_half, high_half).astype(jnp.bfloat16)
        kept = jnp.where(upper, high_half, low_half)
        held = kept + exchange(sent, "col", n_col, 1 << bit).astype(jnp.float32)
    pieces = held.reshape(n_row, held.shape[0] // n_row, width)
    total = jnp.sum(trade(pieces.astype(jnp.bfloat16), "row").astype(jnp.float32), axis=0)
    whole = gather_along(total.astype(jnp.bfloat16), "row", n_row)
    whole = whole.reshape(held.shape[0], width)
    for bit in reversed(range(bits)):
        upper = (col >> bit) & 1 == 1
        other = exchange(whole, "col", n_col, 1 << bit)
        whole = jnp.where(
            upper, jnp.concatenate([other, whole]), jnp.concatenate([whole, other])
        )
    return whole.astype(jnp.float32)


def exclusive_counts(member):
    count = member.shape[-1]
    before = jnp.arange(count)[:, None] < jnp.arange(count)[None, :]
    return jnp.dot(
        member.astype(jnp.bfloat16),
        before.astype(jnp.bfloat16),
        preferred_element_type=jnp.float32,
    ).astype(jnp.int32)


def assign(codes, n_row):
    cluster, valid = codes >> 1, codes & 1
    labels = jnp.arange(CLUSTERS)
    sizes = jnp.sum(
        (cluster.reshape(1, -1) == labels[:, None]) & (valid.reshape(1, -1) == 1), axis=1
    )
    ahead = (sizes[None, :] > sizes[:, None]) | (
        (sizes[None, :] == sizes[:, None]) & (labels[None, :] < labels[:, None])
    )
    rank = jnp.sum(ahead, axis=1)
    others = n_row - 1
    turn, place = (rank - 1) // others, (rank - 1) % others
    group = jnp.where(rank == 0, 0, 1 + jnp.where(turn == 0, place, others - 1 - place))
    of_node = jnp.sum(
        jnp.where(cluster[None] == labels[:, None, None, None], group[:, None, None, None], 0),
        axis=0,
    )
    return jnp.where(valid == 1, of_node, n_row)


def compact(
    codes,
    group,
    features,
    block_keep,
    edge_weight,
    weight_one,
    bias_one,
    gain_one,
    shift_one,
    weight_two,
    bias_two,
    gain_two,
    shift_two,
    cotangent,
    places,
    slots,
    n_row,
    n_col,
    own_cap,
    send_cap,
):
    row, col = lax.axis_index("row"), lax.axis_index("col")
    own_nodes = features.shape[0]
    span = n_col * own_cap
    targets = jnp.arange(n_row)

    def in_col(value):
        return lax.dynamic_index_in_dim(value, col, 1, False).reshape(-1)

    def in_row(value):
        return lax.dynamic_index_in_dim(value, row, 0, False).reshape(-1)

    both = lax.all_gather(jnp.concatenate([features, cotangent], axis=1), "row", axis=0, tiled=True)

    row_codes, col_codes = in_row(codes), in_col(codes)
    tile_rows, tile_cols = edge_weight.shape
    blocks_down, blocks_across = block_keep.shape
    side = tile_rows // blocks_down
    linked = (row_codes[:, None] == col_codes[None, :]) & (row_codes[:, None] & 1 == 1)
    linked = linked.reshape(blocks_down, side, blocks_across, side) & (
        block_keep[:, None, :, None] == 1
    )
    masked = jnp.where(linked.reshape(tile_rows, tile_cols), edge_weight, 0)
    pick_rows = (in_row(group)[None, None, :] == targets[:, None, None]) & (
        in_row(slots)[None, None, :] == jnp.arange(send_cap)[None, :, None]
    )
    pick_cols = (in_col(group)[None, None, :] == targets[:, None, None]) & (
        in_col(places)[None, None, :] == jnp.arange(own_cap)[None, :, None]
    )
    picked = jnp.einsum("sta,ac->stc", pick_rows.astype(jnp.bfloat16), masked)
    packed = jnp.einsum("stc,suc->stu", picked, pick_cols.astype(jnp.bfloat16))
    received = trade(packed, "row")

    standing = jnp.arange(n_col)[None, :, None] * own_cap + places
    fits_here = jnp.where(group == row, standing, -1).reshape(n_row, -1)
    slot_of = slots.reshape(n_row, -1)
    target = jnp.max(
        jnp.where(
            slot_of[:, None, :] == jnp.arange(send_cap)[None, :, None], fits_here[:, None, :], -1
        ),
        axis=2,
    )
    spread = (target[:, :, None] == jnp.arange(span)[None, None, :]).astype(jnp.bfloat16)
    own_block = jnp.einsum("stu,stw->uw", received, spread).astype(jnp.bfloat16)
    block = lax.all_gather(own_block, "col", axis=0, tiled=True)

    scale = lax.rsqrt(1.0 + jnp.sum(block, axis=1, dtype=jnp.float32))
    adjacency = (block.astype(jnp.float32) * scale[:, None] * scale[None, :]).astype(jnp.bfloat16)

    first = (col * own_cap + jnp.arange(own_cap))[:, None] == jnp.arange(span)[None, :]
    previous = first.astype(jnp.float32)
    current = -lax.dynamic_slice_in_dim(adjacency, col * own_cap, own_cap, 0).astype(jnp.float32)
    lowered = [current.astype(jnp.bfloat16)]
    for position in range(2, ORDER):
        upcoming = (
            -2.0 * jnp.dot(lowered[-1], adjacency, preferred_element_type=jnp.float32) - previous
        )
        previous, current = current, upcoming
        lowered.append(upcoming.astype(jnp.bfloat16))
    polynomials = jnp.concatenate(lowered, axis=0)

    def apply(value_low):
        everyone = lax.all_gather(value_low, "col", axis=0, tiled=True)
        result = jnp.dot(polynomials, everyone, preferred_element_type=jnp.float32)
        result = result.astype(jnp.bfloat16).reshape(ORDER - 1, own_cap, -1)
        return jnp.concatenate([value_low[None], result], axis=0)

    pick_own = (
        (in_col(group)[None, :] == row) & (in_col(places)[None, :] == jnp.arange(own_cap)[:, None])
    ).astype(jnp.bfloat16)
    mine = jnp.dot(pick_own, both)
    features_own, cotangent_own = mine[:, : features.shape[1]], mine[:, features.shape[1] :]
    held_count = jnp.sum(in_col(group) == row)
    valid_rows = (jnp.arange(own_cap) < held_count).astype(jnp.float32)

    def forward(value_low, weight, bias, gain, shift):
        stacked = apply(value_low)
        mixed = jnp.einsum("kni,kio->no", stacked, weight, preferred_element_type=jnp.float32)
        mixed = mixed + bias
        return stacked, mixed, finish(mixed, gain, shift, valid_rows)

    def backward(value_low, turned, mixed, upstream, weight, gain, shift):
        ignored, pullback = jax.vjp(
            lambda mixed_in, gain_in, shift_in: finish(mixed_in, gain_in, shift_in, valid_rows),
            mixed,
            gain,
            shift,
        )
        mixed_grad, gain_grad, shift_grad = pullback(upstream)
        mixed_low = mixed_grad.astype(jnp.bfloat16)
        bias_grad = jnp.sum(mixed_low.astype(jnp.float32), axis=0)
        spread_grad = apply(mixed_low)
        if turned is None:
            weight_grad = jnp.einsum(
                "ni,kno->kio", value_low, spread_grad, preferred_element_type=jnp.float32
            )
        else:
            weight_grad = jnp.einsum(
                "kin,no->kio", turned, mixed_low, preferred_element_type=jnp.float32
            )
        input_grad = jnp.einsum(
            "kno,kio->ni", spread_grad, weight, preferred_element_type=jnp.float32
        )
        return input_grad, weight_grad, jnp.stack([bias_grad, gain_grad, shift_grad])

    def send_home(value):
        node_group = lax.dynamic_index_in_dim(group, col, 1, False)
        node_place = lax.dynamic_index_in_dim(places, col, 1, False)
        pick = (node_group == row)[:, :, None] & (
            node_place[:, :, None] == jnp.arange(own_cap)[None, None, :]
        )
        pieces = jnp.einsum("ilu,uf->ilf", pick.astype(jnp.bfloat16), value.astype(jnp.bfloat16))
        return jnp.sum(trade(pieces, "row").astype(jnp.float32), axis=0)

    stacked_one, mixed_one, hidden = forward(features_own, weight_one, bias_one, gain_one, shift_one)
    turned_one = lax.optimization_barrier(stacked_one.transpose(0, 2, 1))
    hidden_low = hidden.astype(jnp.bfloat16)
    ignored, mixed_two, activations = forward(
        hidden_low, weight_two, bias_two, gain_two, shift_two
    )
    activations = send_home(activations)
    hidden_grad, weight_two_grad, rest_two = backward(
        hidden_low,
        None,
        mixed_two,
        cotangent_own.astype(jnp.float32),
        weight_two,
        gain_two,
        shift_two,
    )
    width = weight_two.shape[2]
    part_two = weight_two_grad.reshape(-1, width)
    whole_two = sum_everywhere(part_two, n_row, n_col)
    input_grad, weight_one_grad, rest_one = backward(
        features_own, turned_one, mixed_one, hidden_grad, weight_one, gain_one, shift_one
    )
    part_one = jnp.concatenate([weight_one_grad.reshape(-1, width), rest_one, rest_two])
    unit = n_row * n_col * 8
    extra = -part_one.shape[0] % unit
    part_one = jnp.concatenate([part_one, jnp.zeros((extra, width), jnp.float32)])
    whole_one = sum_everywhere(part_one, n_row, n_col)
    input_grad = send_home(input_grad)
    tail = weight_one.shape[0] * weight_one.shape[1]
    rest = whole_one[tail : tail + 6]
    return (
        activations,
        input_grad,
        whole_one[:tail].reshape(weight_one.shape),
        rest[0],
        rest[1],
        rest[2],
        whole_two.reshape(weight_two.shape),
        rest[3],
        rest[4],
        rest[5],
    )


def general(
    codes,
    features,
    block_keep,
    edge_weight,
    weight_one,
    bias_one,
    gain_one,
    shift_one,
    weight_two,
    bias_two,
    gain_two,
    shift_two,
    cotangent,
    node_valid,
):
    row, col = lax.axis_index("row"), lax.axis_index("col")
    row_codes = lax.dynamic_index_in_dim(codes, row, 0, False).reshape(-1)
    col_codes = lax.dynamic_index_in_dim(codes, col, 1, False).reshape(-1)
    tile_rows, tile_cols = edge_weight.shape
    blocks_down, blocks_across = block_keep.shape
    block_side = tile_rows // blocks_down
    linked = (row_codes[:, None] == col_codes[None, :]) & (row_codes[:, None] & 1 == 1)
    linked = linked.reshape(blocks_down, block_side, blocks_across, block_side) & (
        block_keep[:, None, :, None] == 1
    )
    masked = edge_weight * linked.reshape(tile_rows, tile_cols).astype(jnp.bfloat16)
    degree_rows = 1.0 + lax.psum(jnp.sum(masked, axis=1, dtype=jnp.float32), "col")
    own_nodes = features.shape[0]
    own_degree = lax.dynamic_slice_in_dim(
        degree_rows, lax.axis_index("col") * own_nodes, own_nodes, 0
    )
    degree_cols = lax.all_gather(own_degree, "row", axis=0, tiled=True)
    adjacency = (
        masked.astype(jnp.float32)
        * lax.rsqrt(degree_rows)[:, None]
        * lax.rsqrt(degree_cols)[None, :]
    ).astype(jnp.bfloat16)
    valid_rows = node_valid.astype(jnp.float32)
    stacked_one, mixed_one, hidden = layer_forward(
        adjacency,
        features.astype(jnp.float32),
        weight_one,
        bias_one,
        gain_one,
        shift_one,
        valid_rows,
    )
    stacked_two, mixed_two, activations = layer_forward(
        adjacency, hidden, weight_two, bias_two, gain_two, shift_two, valid_rows
    )
    hidden_grad, weight_two_grad, bias_two_grad, gain_two_grad, shift_two_grad = layer_backward(
        adjacency,
        stacked_two,
        mixed_two,
        cotangent.astype(jnp.float32),
        weight_two,
        gain_two,
        shift_two,
        valid_rows,
    )
    input_grad, weight_one_grad, bias_one_grad, gain_one_grad, shift_one_grad = layer_backward(
        adjacency, stacked_one, mixed_one, hidden_grad, weight_one, gain_one, shift_one, valid_rows
    )
    summed = lax.psum(
        (
            weight_one_grad,
            bias_one_grad,
            gain_one_grad,
            shift_one_grad,
            weight_two_grad,
            bias_two_grad,
            gain_two_grad,
            shift_two_grad,
        ),
        ("row", "col"),
    )
    weight_one_grad, bias_one_grad, gain_one_grad, shift_one_grad = (
        summed[0],
        summed[1],
        summed[2],
        summed[3],
    )
    weight_two_grad, bias_two_grad, gain_two_grad, shift_two_grad = (
        summed[4],
        summed[5],
        summed[6],
        summed[7],
    )
    return (
        activations,
        input_grad,
        weight_one_grad,
        bias_one_grad,
        gain_one_grad,
        shift_one_grad,
        weight_two_grad,
        bias_two_grad,
        gain_two_grad,
        shift_two_grad,
    )


def local(n_row, n_col, *args):
    (
        features,
        node_valid,
        cluster,
        block_keep,
        edge_weight,
        weight_one,
        bias_one,
        gain_one,
        shift_one,
        weight_two,
        bias_two,
        gain_two,
        shift_two,
        cotangent,
    ) = args
    own_nodes = features.shape[0]
    own_cap = own_nodes * n_row * 5 // 16
    send_cap = own_nodes * n_col * 3 // 8
    codes = gather_along(lax.all_gather(cluster * 2 + node_valid, "col", axis=0), "row", n_row)
    shared = (
        block_keep,
        edge_weight,
        weight_one,
        bias_one,
        gain_one,
        shift_one,
        weight_two,
        bias_two,
        gain_two,
        shift_two,
        cotangent,
    )

    def slow():
        return general(codes, features, *shared, node_valid)

    held = (ORDER - 1) * own_cap * own_cap * n_col * 2
    if held > HELD_BYTES or n_row & (n_row - 1) or n_col & (n_col - 1) or n_row < 2:
        return slow()
    group = assign(codes, n_row)
    member = group[None] == jnp.arange(n_row)[:, None, None, None]
    by_col = member.transpose(0, 2, 1, 3).reshape(n_row, n_col, -1)
    by_row = member.reshape(n_row, n_row, -1)
    places = jnp.sum(jnp.where(by_col, exclusive_counts(by_col), 0), axis=0)
    places = places.reshape(n_col, n_row, own_nodes).transpose(1, 0, 2)
    slots = jnp.sum(jnp.where(by_row, exclusive_counts(by_row), 0), axis=0)
    slots = slots.reshape(n_row, n_col, own_nodes)
    fits = (jnp.max(jnp.sum(by_col, axis=2)) <= own_cap) & (
        jnp.max(jnp.sum(by_row, axis=2)) <= send_cap
    )

    results = compact(
        codes, group, features, *shared, places, slots, n_row, n_col, own_cap, send_cap
    )
    return lax.while_loop(
        lambda state: jnp.logical_not(state[0]), lambda state: (True, slow()), (fits, results)
    )[1]


def solution(mesh):
    placed = (
        P(("row", "col"), None),
        P(("row", "col")),
        P(("row", "col")),
        P("row", "col"),
        P("row", "col"),
        P(),
        P(),
        P(),
        P(),
        P(),
        P(),
        P(),
        P(),
        P(("row", "col"), None),
    )
    return jax.shard_map(
        functools.partial(local, mesh.shape["row"], mesh.shape["col"]),
        mesh=mesh,
        in_specs=placed,
        out_specs=(
            P(("row", "col"), None),
            P(("row", "col"), None),
            P(),
            P(),
            P(),
            P(),
            P(),
            P(),
            P(),
            P(),
        ),
        check_vma=False,
    )
```

```python
import functools

import jax
import jax.numpy as jnp
from jax import lax
from jax.sharding import PartitionSpec as P

ORDER = 13
CLUSTERS = 16
HELD_BYTES = 1 << 25
COL = ("chip", "core")


def finish(mixed, gain, shift, valid_rows):
    active = jax.nn.gelu(mixed, approximate=False)
    centered = active - jnp.mean(active, axis=-1, keepdims=True)
    variance = jnp.mean(centered * centered, axis=-1, keepdims=True)
    return (centered * lax.rsqrt(variance + 1e-05) * gain + shift) * valid_rows[:, None]


def forward_product(adjacency, piece_low):
    partial_value = jnp.dot(
        adjacency,
        lax.all_gather(piece_low, "row", axis=0, tiled=True),
        preferred_element_type=jnp.float32,
    )
    return lax.psum_scatter(partial_value, COL, scatter_dimension=0, tiled=True)


def backward_product(adjacency, piece_low):
    partial_value = lax.dot_general(
        adjacency,
        lax.all_gather(piece_low, COL, axis=0, tiled=True),
        (((0,), (0,)), ((), ())),
        preferred_element_type=jnp.float32,
    )
    return lax.psum_scatter(
        partial_value.astype(jnp.bfloat16), "row", scatter_dimension=0, tiled=True
    ).astype(jnp.float32)


def layer_forward(adjacency, inputs, weight, bias, gain, shift, valid_rows):
    first_low = inputs.astype(jnp.bfloat16)
    second = -forward_product(adjacency, first_low)
    second_low = second.astype(jnp.bfloat16)

    def advance(state_pair, unused):
        previous, current, current_low = state_pair
        upcoming = -2.0 * forward_product(adjacency, current_low) - previous
        upcoming_low = upcoming.astype(jnp.bfloat16)
        return ((current, upcoming, upcoming_low), upcoming_low)

    ignored, others = lax.scan(advance, (inputs, second, second_low), None, length=ORDER - 2)
    stacked = jnp.concatenate([first_low[None], second_low[None], others], axis=0)
    mixed = jnp.einsum("kni,kio->no", stacked, weight, preferred_element_type=jnp.float32) + bias
    return (stacked, mixed, finish(mixed, gain, shift, valid_rows))


def layer_backward(adjacency, stacked, mixed, upstream, weight, gain, shift, valid_rows):

    def local_finish(mixed_in, gain_in, shift_in):
        return finish(mixed_in, gain_in, shift_in, valid_rows)

    ignored, pullback = jax.vjp(local_finish, mixed, gain, shift)
    mixed_grad, gain_grad, shift_grad = pullback(upstream)
    mixed_low = mixed_grad.astype(jnp.bfloat16)
    bias_grad = jnp.sum(mixed_low.astype(jnp.float32), axis=0)
    weight_grad = jnp.einsum("kni,no->kio", stacked, mixed_low, preferred_element_type=jnp.float32)
    direct = jnp.einsum("no,kio->kni", mixed_low, weight, preferred_element_type=jnp.float32)

    def retreat(state_pair, direct_term):
        later_two, later_one = state_pair
        current = (
            direct_term
            - 2.0 * backward_product(adjacency, later_one.astype(jnp.bfloat16))
            - later_two
        )
        return ((later_one, current), None)

    start_pair = (jnp.zeros_like(direct[0]), direct[ORDER - 1])
    (second_grad, first_grad), unused = lax.scan(
        retreat, start_pair, direct[1 : ORDER - 1], reverse=True
    )
    input_grad = (
        direct[0] - backward_product(adjacency, first_grad.astype(jnp.bfloat16)) - second_grad
    )
    return (input_grad, weight_grad, bias_grad, gain_grad, shift_grad)


def swap(value, axis):
    return lax.ppermute(value, axis, [(0, 1), (1, 0)])


def trade(pieces, axis):
    return lax.all_to_all(pieces, axis, 0, 0, tiled=False)


def broadcast_along(value, axis, size):
    return trade(jnp.broadcast_to(value[None], (size,) + value.shape), axis)


def halves(value, index):
    half = value.shape[0] // 2
    mine = lax.dynamic_slice_in_dim(value, index * half, half, 0)
    other = lax.dynamic_slice_in_dim(value, (1 - index) * half, half, 0)
    return mine, other


def joined(mine, other, index):
    return jnp.where(
        index == 0, jnp.concatenate([mine, other]), jnp.concatenate([other, mine])
    )


def sum_everywhere(part, n_row, n_chip):
    core = lax.axis_index("core")
    mine, other = halves(part, core)
    held = mine.astype(jnp.float32) + swap(other, "core").astype(jnp.float32)
    chips = n_row * n_chip
    pieces = held.astype(jnp.bfloat16).reshape(chips, held.shape[0] // chips, -1)
    total = jnp.sum(trade(pieces, ("row", "chip")).astype(jnp.float32), axis=0)
    whole = broadcast_along(total.astype(jnp.bfloat16), ("row", "chip"), chips)
    whole = whole.reshape(held.shape)
    return joined(whole, swap(whole, "core"), core)


def exclusive_counts(member):
    count = member.shape[-1]
    before = jnp.arange(count)[:, None] < jnp.arange(count)[None, :]
    return jnp.dot(
        member.astype(jnp.bfloat16),
        before.astype(jnp.bfloat16),
        preferred_element_type=jnp.float32,
    ).astype(jnp.int32)


def assign(codes, n_row):
    cluster, valid = codes >> 1, codes & 1
    labels = jnp.arange(CLUSTERS)
    sizes = jnp.sum(
        (cluster.reshape(1, -1) == labels[:, None]) & (valid.reshape(1, -1) == 1), axis=1
    )
    ahead = (sizes[None, :] > sizes[:, None]) | (
        (sizes[None, :] == sizes[:, None]) & (labels[None, :] < labels[:, None])
    )
    rank = jnp.sum(ahead, axis=1)
    others = n_row - 1
    turn, place = (rank - 1) // others, (rank - 1) % others
    group = jnp.where(rank == 0, 0, 1 + jnp.where(turn == 0, place, others - 1 - place))
    of_node = jnp.sum(
        jnp.where(cluster[None] == labels[:, None, None, None], group[:, None, None, None], 0),
        axis=0,
    )
    return jnp.where(valid == 1, of_node, n_row)


def compact(
    codes,
    group,
    features,
    block_keep,
    edge_weight,
    weight_one,
    bias_one,
    gain_one,
    shift_one,
    weight_two,
    bias_two,
    gain_two,
    shift_two,
    cotangent,
    places,
    slots,
    seats,
    sizes,
    caps,
):
    row, col = lax.axis_index("row"), lax.axis_index(COL)
    chip, core = lax.axis_index("chip"), lax.axis_index("core")
    n_row, n_col = sizes
    own_cap, send_cap, seat_cap = caps
    own_nodes, in_width = features.shape
    span = n_col * own_cap
    targets = jnp.arange(n_row)

    def in_col(value):
        return lax.dynamic_index_in_dim(value, col, 1, False).reshape(-1)

    def in_row(value):
        return lax.dynamic_index_in_dim(value, row, 0, False).reshape(-1)

    row_codes, col_codes = in_row(codes), in_col(codes)
    tile_rows, tile_cols = edge_weight.shape
    blocks_down, blocks_across = block_keep.shape
    side = tile_rows // blocks_down
    linked = (row_codes[:, None] == col_codes[None, :]) & (row_codes[:, None] & 1 == 1)
    linked = linked.reshape(blocks_down, side, blocks_across, side) & (
        block_keep[:, None, :, None] == 1
    )
    masked = jnp.where(linked.reshape(tile_rows, tile_cols), edge_weight, 0)
    pick_rows = (in_row(group)[None, None, :] == targets[:, None, None]) & (
        in_row(slots)[None, None, :] == jnp.arange(send_cap)[None, :, None]
    )
    pick_cols = (in_col(group)[None, None, :] == targets[:, None, None]) & (
        in_col(places)[None, None, :] == jnp.arange(own_cap)[None, :, None]
    )
    picked = jnp.einsum("sta,ac->stc", pick_rows.astype(jnp.bfloat16), masked)
    packed = jnp.einsum("stc,suc->stu", picked, pick_cols.astype(jnp.bfloat16))
    received = trade(packed, "row")

    both = broadcast_along(jnp.concatenate([features, cotangent], axis=1), "row", n_row)
    both = both.reshape(n_row * own_nodes, -1)
    pick_own = (
        (in_col(group)[None, :] == row) & (in_col(places)[None, :] == jnp.arange(own_cap)[:, None])
    ).astype(jnp.bfloat16)
    mine = jnp.dot(pick_own, both)
    features_own, cotangent_own = mine[:, :in_width], mine[:, in_width:]
    features_all = lax.all_gather(features_own, COL, axis=0, tiled=True)
    held_count = jnp.sum(in_col(group) == row)
    valid_rows = (jnp.arange(own_cap) < held_count).astype(jnp.float32)

    standing = jnp.arange(n_col)[None, :, None] * own_cap + places
    fits_here = jnp.where(group == row, standing, -1).reshape(n_row, -1)
    slot_of = slots.reshape(n_row, -1)
    target = jnp.max(
        jnp.where(
            slot_of[:, None, :] == jnp.arange(send_cap)[None, :, None], fits_here[:, None, :], -1
        ),
        axis=2,
    )
    spread = (target[:, :, None] == jnp.arange(span)[None, None, :]).astype(jnp.bfloat16)
    own_block = jnp.einsum("stu,stw->uw", received, spread).astype(jnp.bfloat16)

    quadrant = lax.dynamic_slice_in_dim(own_block, chip * (span // 2), span // 2, 1)
    quadrant = swap(quadrant, "chip")
    top = joined(own_block, swap(own_block, "core"), core)
    quadrant = joined(quadrant, swap(quadrant, "core"), core)
    across = lax.dynamic_slice_in_dim(top, (1 - chip) * (span // 2), span // 2, 1)
    bottom = jnp.where(
        chip == 0,
        jnp.concatenate([across.T, quadrant], axis=1),
        jnp.concatenate([quadrant, across.T], axis=1),
    )
    block = joined(top, bottom, chip)

    scale = lax.rsqrt(1.0 + jnp.sum(block, axis=1, dtype=jnp.float32))
    adjacency = (block.astype(jnp.float32) * scale[:, None] * scale[None, :]).astype(jnp.bfloat16)

    first = (col * own_cap + jnp.arange(own_cap))[:, None] == jnp.arange(span)[None, :]
    previous = first.astype(jnp.float32)
    current = -lax.dynamic_slice_in_dim(adjacency, col * own_cap, own_cap, 0).astype(jnp.float32)
    lowered = [current.astype(jnp.bfloat16)]
    for position in range(2, ORDER):
        upcoming = (
            -2.0 * jnp.dot(lowered[-1], adjacency, preferred_element_type=jnp.float32) - previous
        )
        previous, current = current, upcoming
        lowered.append(upcoming.astype(jnp.bfloat16))
    polynomials = jnp.concatenate(lowered, axis=0)

    def apply(value_low, everyone):
        result = jnp.dot(polynomials, everyone, preferred_element_type=jnp.float32)
        result = result.astype(jnp.bfloat16).reshape(ORDER - 1, own_cap, -1)
        return jnp.concatenate([value_low[None], result], axis=0)

    def everywhere(value_low):
        return lax.all_gather(value_low, COL, axis=0, tiled=True)

    def forward(value_low, everyone, weight, bias, gain, shift):
        stacked = apply(value_low, everyone)
        mixed = jnp.einsum("kni,kio->no", stacked, weight, preferred_element_type=jnp.float32)
        mixed = mixed + bias
        turned = lax.optimization_barrier(stacked.transpose(0, 2, 1))
        return turned, mixed, finish(mixed, gain, shift, valid_rows)

    def through_norm(turned, mixed, upstream, gain, shift):
        ignored, pullback = jax.vjp(
            lambda mixed_in, gain_in, shift_in: finish(mixed_in, gain_in, shift_in, valid_rows),
            mixed,
            gain,
            shift,
        )
        mixed_grad, gain_grad, shift_grad = pullback(upstream)
        mixed_low = mixed_grad.astype(jnp.bfloat16)
        bias_grad = jnp.sum(mixed_low.astype(jnp.float32), axis=0)
        weight_grad = jnp.einsum(
            "kin,no->kio", turned, mixed_low, preferred_element_type=jnp.float32
        ).astype(jnp.bfloat16)
        return mixed_low, weight_grad, [bias_grad, gain_grad, shift_grad]

    def to_input(mixed_low, weight):
        spread_grad = apply(mixed_low, everywhere(mixed_low))
        return jnp.einsum("kno,kio->ni", spread_grad, weight, preferred_element_type=jnp.float32)

    turned_one, mixed_one, hidden = forward(
        features_own, features_all, weight_one, bias_one, gain_one, shift_one
    )
    hidden_low = hidden.astype(jnp.bfloat16)
    turned_two, mixed_two, activations = forward(
        hidden_low, everywhere(hidden_low), weight_two, bias_two, gain_two, shift_two
    )
    low_two, weight_two_grad, rest_two = through_norm(
        turned_two, mixed_two, cotangent_own.astype(jnp.float32), gain_two, shift_two
    )
    weight_two_grad = lax.psum(weight_two_grad, ("row",) + COL)
    hidden_grad = to_input(low_two, weight_two)
    low_one, weight_one_grad, rest_one = through_norm(
        turned_one, mixed_one, hidden_grad, gain_one, shift_one
    )
    width = weight_two.shape[2]
    tail = weight_one.shape[0] * weight_one.shape[1]
    rest = jnp.stack(rest_one + rest_two).astype(jnp.bfloat16)
    unit = n_row * n_col * 16
    extra = jnp.zeros((-(tail + 6) % unit, width), jnp.bfloat16)
    part = jnp.concatenate([weight_one_grad.reshape(-1, width), rest, extra])
    whole = sum_everywhere(part, n_row, n_col // 2)
    input_grad = to_input(low_one, weight_one)

    results = jnp.concatenate([activations, input_grad], axis=1).astype(jnp.bfloat16)
    seat_pick = pick_seats(group, seats, row, col, seat_cap)
    place_here = lax.dynamic_index_in_dim(places, col, 1, False)
    place_of_seat = jnp.max(jnp.where(seat_pick, place_here[:, None, :], -1), axis=2)
    take = place_of_seat[:, :, None] == jnp.arange(own_cap)[None, None, :]
    sent = jnp.einsum("rtu,uf->rtf", take.astype(jnp.bfloat16), results)
    back = trade(sent, "row")
    group_here = lax.dynamic_index_in_dim(
        lax.dynamic_index_in_dim(group, row, 0, False), col, 0, False
    )
    seat_here = lax.dynamic_index_in_dim(
        lax.dynamic_index_in_dim(seats, row, 0, False), col, 0, False
    )
    put = (group_here[None, None, :] == targets[:, None, None]) & (
        seat_here[None, None, :] == jnp.arange(seat_cap)[None, :, None]
    )
    home = jnp.einsum(
        "rtl,rtf->lf", put.astype(jnp.bfloat16), back, preferred_element_type=jnp.float32
    )
    return home, whole[: tail + 6], weight_two_grad.reshape(-1, width)


def pick_seats(group, seats, row, col, seat_cap):
    group_col = lax.dynamic_index_in_dim(group, col, 1, False)
    seats_col = lax.dynamic_index_in_dim(seats, col, 1, False)
    return (group_col == row)[:, None, :] & (
        seats_col[:, None, :] == jnp.arange(seat_cap)[None, :, None]
    )


def general(
    codes,
    features,
    block_keep,
    edge_weight,
    weight_one,
    bias_one,
    gain_one,
    shift_one,
    weight_two,
    bias_two,
    gain_two,
    shift_two,
    cotangent,
    node_valid,
):
    row, col = lax.axis_index("row"), lax.axis_index(COL)
    row_codes = lax.dynamic_index_in_dim(codes, row, 0, False).reshape(-1)
    col_codes = lax.dynamic_index_in_dim(codes, col, 1, False).reshape(-1)
    tile_rows, tile_cols = edge_weight.shape
    blocks_down, blocks_across = block_keep.shape
    block_side = tile_rows // blocks_down
    linked = (row_codes[:, None] == col_codes[None, :]) & (row_codes[:, None] & 1 == 1)
    linked = linked.reshape(blocks_down, block_side, blocks_across, block_side) & (
        block_keep[:, None, :, None] == 1
    )
    masked = edge_weight * linked.reshape(tile_rows, tile_cols).astype(jnp.bfloat16)
    degree_rows = 1.0 + lax.psum(jnp.sum(masked, axis=1, dtype=jnp.float32), COL)
    own_nodes = features.shape[0]
    own_degree = lax.dynamic_slice_in_dim(
        degree_rows, lax.axis_index(COL) * own_nodes, own_nodes, 0
    )
    degree_cols = lax.all_gather(own_degree, "row", axis=0, tiled=True)
    adjacency = (
        masked.astype(jnp.float32)
        * lax.rsqrt(degree_rows)[:, None]
        * lax.rsqrt(degree_cols)[None, :]
    ).astype(jnp.bfloat16)
    valid_rows = node_valid.astype(jnp.float32)
    stacked_one, mixed_one, hidden = layer_forward(
        adjacency,
        features.astype(jnp.float32),
        weight_one,
        bias_one,
        gain_one,
        shift_one,
        valid_rows,
    )
    stacked_two, mixed_two, activations = layer_forward(
        adjacency, hidden, weight_two, bias_two, gain_two, shift_two, valid_rows
    )
    hidden_grad, weight_two_grad, bias_two_grad, gain_two_grad, shift_two_grad = layer_backward(
        adjacency,
        stacked_two,
        mixed_two,
        cotangent.astype(jnp.float32),
        weight_two,
        gain_two,
        shift_two,
        valid_rows,
    )
    input_grad, weight_one_grad, bias_one_grad, gain_one_grad, shift_one_grad = layer_backward(
        adjacency, stacked_one, mixed_one, hidden_grad, weight_one, gain_one, shift_one, valid_rows
    )
    summed = lax.psum(
        (
            weight_one_grad,
            bias_one_grad,
            gain_one_grad,
            shift_one_grad,
            weight_two_grad,
            bias_two_grad,
            gain_two_grad,
            shift_two_grad,
        ),
        ("row",) + COL,
    )
    weight_one_grad, bias_one_grad, gain_one_grad, shift_one_grad = (
        summed[0],
        summed[1],
        summed[2],
        summed[3],
    )
    weight_two_grad, bias_two_grad, gain_two_grad, shift_two_grad = (
        summed[4],
        summed[5],
        summed[6],
        summed[7],
    )
    return (
        activations,
        input_grad,
        weight_one_grad,
        bias_one_grad,
        gain_one_grad,
        shift_one_grad,
        weight_two_grad,
        bias_two_grad,
        gain_two_grad,
        shift_two_grad,
    )


def local(n_row, n_col, *args):
    (
        features,
        node_valid,
        cluster,
        block_keep,
        edge_weight,
        weight_one,
        bias_one,
        gain_one,
        shift_one,
        weight_two,
        bias_two,
        gain_two,
        shift_two,
        cotangent,
    ) = args
    own_nodes, in_width = features.shape
    own_cap = own_nodes * n_row * 5 // 16
    send_cap = own_nodes * n_col * 3 // 8
    seat_cap = own_nodes // 2
    codes = lax.all_gather(cluster * 2 + node_valid, COL, axis=0)
    codes = broadcast_along(codes, "row", n_row)
    shared = (
        block_keep,
        edge_weight,
        weight_one,
        bias_one,
        gain_one,
        shift_one,
        weight_two,
        bias_two,
        gain_two,
        shift_two,
        cotangent,
    )

    def slow():
        return general(codes, features, *shared, node_valid)

    held = (ORDER - 1) * own_cap * own_cap * n_col * 2
    if held > HELD_BYTES or n_col != 4 or n_row < 2:
        return slow()
    group = assign(codes, n_row)
    member = group[None] == jnp.arange(n_row)[:, None, None, None]
    by_col = member.transpose(0, 2, 1, 3).reshape(n_row, n_col, -1)
    by_row = member.reshape(n_row, n_row, -1)
    places = jnp.sum(jnp.where(by_col, exclusive_counts(by_col), 0), axis=0)
    places = places.reshape(n_col, n_row, own_nodes).transpose(1, 0, 2)
    slots = jnp.sum(jnp.where(by_row, exclusive_counts(by_row), 0), axis=0)
    slots = slots.reshape(n_row, n_col, own_nodes)
    seats = jnp.sum(jnp.where(member, exclusive_counts(member), 0), axis=0)
    fits = (
        (jnp.max(jnp.sum(by_col, axis=2)) <= own_cap)
        & (jnp.max(jnp.sum(by_row, axis=2)) <= send_cap)
        & (jnp.max(jnp.sum(member, axis=3)) <= seat_cap)
    )
    results = compact(
        codes,
        group,
        features,
        *shared,
        places,
        slots,
        seats,
        (n_row, n_col),
        (own_cap, send_cap, seat_cap),
    )

    def again(state):
        made = slow()
        home = jnp.concatenate(made[:2], axis=1)
        small = [made[place][None] for place in (3, 4, 5, 7, 8, 9)]
        whole = jnp.concatenate([made[2].reshape(-1, made[2].shape[2])] + small)
        return True, (
            home,
            whole.astype(jnp.bfloat16),
            made[6].reshape(-1, made[6].shape[2]).astype(jnp.bfloat16),
        )

    home, whole, second = lax.while_loop(
        lambda state: jnp.logical_not(state[0]), again, (fits, results)
    )[1]
    whole, second = whole.astype(jnp.float32), second.astype(jnp.float32)
    width = weight_two.shape[2]
    tail = weight_one.shape[0] * weight_one.shape[1]
    return (
        home[:, :width],
        home[:, width:],
        whole[:tail].reshape(weight_one.shape),
        whole[tail],
        whole[tail + 1],
        whole[tail + 2],
        second.reshape(weight_two.shape),
        whole[tail + 3],
        whole[tail + 4],
        whole[tail + 5],
    )


def solution(mesh):
    n_row, n_col = mesh.shape["row"], mesh.shape["col"]
    by_core = jax.sharding.Mesh(
        mesh.devices.reshape(n_row, n_col // 2, 2), ("row", "chip", "core")
    )
    nodes = ("row", "chip", "core")
    placed = (
        P(nodes, None),
        P(nodes),
        P(nodes),
        P("row", COL),
        P("row", COL),
        P(),
        P(),
        P(),
        P(),
        P(),
        P(),
        P(),
        P(),
        P(nodes, None),
    )
    return jax.shard_map(
        functools.partial(local, n_row, n_col),
        mesh=by_core,
        in_specs=placed,
        out_specs=(P(nodes, None), P(nodes, None), P(), P(), P(), P(), P(), P(), P(), P()),
        check_vma=False,
    )
```

```python
import functools

import jax
import jax.numpy as jnp
from jax import lax
from jax.experimental import pallas as pl
from jax.experimental.pallas import tpu as pltpu
from jax.sharding import PartitionSpec as P

ORDER = 13
CLUSTERS = 16
HELD_BYTES = 1 << 25
COL = ("chip", "core")


def finish(mixed, gain, shift, valid_rows):
    active = jax.nn.gelu(mixed, approximate=False)
    centered = active - jnp.mean(active, axis=-1, keepdims=True)
    variance = jnp.mean(centered * centered, axis=-1, keepdims=True)
    return (centered * lax.rsqrt(variance + 1e-05) * gain + shift) * valid_rows[:, None]


def forward_product(adjacency, piece_low):
    partial_value = jnp.dot(
        adjacency,
        lax.all_gather(piece_low, "row", axis=0, tiled=True),
        preferred_element_type=jnp.float32,
    )
    return lax.psum_scatter(partial_value, COL, scatter_dimension=0, tiled=True)


def backward_product(adjacency, piece_low):
    partial_value = lax.dot_general(
        adjacency,
        lax.all_gather(piece_low, COL, axis=0, tiled=True),
        (((0,), (0,)), ((), ())),
        preferred_element_type=jnp.float32,
    )
    return lax.psum_scatter(
        partial_value.astype(jnp.bfloat16), "row", scatter_dimension=0, tiled=True
    ).astype(jnp.float32)


def layer_forward(adjacency, inputs, weight, bias, gain, shift, valid_rows):
    first_low = inputs.astype(jnp.bfloat16)
    second = -forward_product(adjacency, first_low)
    second_low = second.astype(jnp.bfloat16)

    def advance(state_pair, unused):
        previous, current, current_low = state_pair
        upcoming = -2.0 * forward_product(adjacency, current_low) - previous
        upcoming_low = upcoming.astype(jnp.bfloat16)
        return ((current, upcoming, upcoming_low), upcoming_low)

    ignored, others = lax.scan(advance, (inputs, second, second_low), None, length=ORDER - 2)
    stacked = jnp.concatenate([first_low[None], second_low[None], others], axis=0)
    mixed = jnp.einsum("kni,kio->no", stacked, weight, preferred_element_type=jnp.float32) + bias
    return (stacked, mixed, finish(mixed, gain, shift, valid_rows))


def layer_backward(adjacency, stacked, mixed, upstream, weight, gain, shift, valid_rows):

    def local_finish(mixed_in, gain_in, shift_in):
        return finish(mixed_in, gain_in, shift_in, valid_rows)

    ignored, pullback = jax.vjp(local_finish, mixed, gain, shift)
    mixed_grad, gain_grad, shift_grad = pullback(upstream)
    mixed_low = mixed_grad.astype(jnp.bfloat16)
    bias_grad = jnp.sum(mixed_low.astype(jnp.float32), axis=0)
    weight_grad = jnp.einsum("kni,no->kio", stacked, mixed_low, preferred_element_type=jnp.float32)
    direct = jnp.einsum("no,kio->kni", mixed_low, weight, preferred_element_type=jnp.float32)

    def retreat(state_pair, direct_term):
        later_two, later_one = state_pair
        current = (
            direct_term
            - 2.0 * backward_product(adjacency, later_one.astype(jnp.bfloat16))
            - later_two
        )
        return ((later_one, current), None)

    start_pair = (jnp.zeros_like(direct[0]), direct[ORDER - 1])
    (second_grad, first_grad), unused = lax.scan(
        retreat, start_pair, direct[1 : ORDER - 1], reverse=True
    )
    input_grad = (
        direct[0] - backward_product(adjacency, first_grad.astype(jnp.bfloat16)) - second_grad
    )
    return (input_grad, weight_grad, bias_grad, gain_grad, shift_grad)


def swap(value, axis):
    return lax.ppermute(value, axis, [(0, 1), (1, 0)])


def trade(pieces, axis):
    return lax.all_to_all(pieces, axis, 0, 0, tiled=False)


def broadcast_along(value, axis, size):
    return trade(jnp.broadcast_to(value[None], (size,) + value.shape), axis)


def joined(mine, other, index):
    return jnp.where(
        index == 0, jnp.concatenate([mine, other]), jnp.concatenate([other, mine])
    )


def add_cores(part):
    core = lax.axis_index("core")
    mine = lax.dynamic_index_in_dim(part, core, 1, False)
    other = lax.dynamic_index_in_dim(part, 1 - core, 1, False)
    return (mine.astype(jnp.float32) + swap(other, "core").astype(jnp.float32)).astype(jnp.bfloat16)


def add_chips(part):
    chip = lax.axis_index("chip")
    mine = lax.dynamic_index_in_dim(part, chip, 0, False)
    other = lax.dynamic_index_in_dim(part, 1 - chip, 0, False)
    return (mine.astype(jnp.float32) + swap(other, "chip").astype(jnp.float32)).astype(jnp.bfloat16)


def block_kernel(place_ref, own_ref, sibling_ref, near_ref, far_ref, out_ref):
    chip, core = place_ref[0], place_ref[1]
    own_cap, span = own_ref.shape
    half = span // 2

    def rows(of_chip, of_core):
        return pl.ds(pl.multiple_of((2 * of_chip + of_core) * own_cap, own_cap), own_cap)

    out_ref[rows(chip, core), :] = own_ref[...]
    out_ref[rows(chip, 1 - core), :] = sibling_ref[...]

    def other_chip(here):
        there = 1 - here
        here_cols, there_cols = pl.ds(here * half, half), pl.ds(there * half, half)
        out_ref[rows(there, core), there_cols] = near_ref[...]
        out_ref[rows(there, 1 - core), there_cols] = far_ref[...]
        for tile in range(half // 128):
            strip = out_ref[here_cols, pl.ds(there * half + tile * 128, 128)]
            turned = jnp.transpose(strip.astype(jnp.float32)).astype(jnp.bfloat16)
            out_ref[pl.ds(there * half + tile * 128, 128), here_cols] = turned

    @pl.when(chip == 0)
    def first():
        other_chip(0)

    @pl.when(chip == 1)
    def second():
        other_chip(1)

    across = jnp.ones((1, span), jnp.float32)
    for tile in range(span // 128):
        across = across + jnp.sum(
            out_ref[pl.ds(tile * 128, 128), :].astype(jnp.float32), axis=0, keepdims=True
        )
    across = lax.rsqrt(across)
    for tile in range(span // 128):
        strip = out_ref[pl.ds(tile * 128, 128), :].astype(jnp.float32)
        down = lax.rsqrt(1.0 + jnp.sum(strip, axis=1, keepdims=True))
        out_ref[pl.ds(tile * 128, 128), :] = (strip * down * across).astype(jnp.bfloat16)


def normalized_block(own, sibling, near, far, chip, core):
    span = own.shape[1]
    whole = pl.BlockSpec(memory_space=pltpu.VMEM)
    return pl.pallas_call(
        block_kernel,
        out_shape=jax.ShapeDtypeStruct((span, span), jnp.bfloat16),
        in_specs=[pl.BlockSpec(memory_space=pltpu.SMEM), whole, whole, whole, whole],
        out_specs=whole,
        compiler_params=pltpu.CompilerParams(vmem_limit_bytes=32 << 20),
        cost_estimate=pl.CostEstimate(
            flops=8 * span * span, bytes_accessed=8 * span * span, transcendentals=0
        ),
        name="normalized_block",
    )(jnp.stack([chip, core]).astype(jnp.int32), own, sibling, near, far)


def exclusive_counts(member):
    count = member.shape[-1]
    before = jnp.arange(count)[:, None] < jnp.arange(count)[None, :]
    return jnp.dot(
        member.astype(jnp.bfloat16),
        before.astype(jnp.bfloat16),
        preferred_element_type=jnp.float32,
    ).astype(jnp.int32)


def assign(codes, n_row):
    cluster, valid = codes >> 1, codes & 1
    labels = jnp.arange(CLUSTERS)
    sizes = jnp.sum(
        (cluster.reshape(1, -1) == labels[:, None]) & (valid.reshape(1, -1) == 1), axis=1
    )
    ahead = (sizes[None, :] > sizes[:, None]) | (
        (sizes[None, :] == sizes[:, None]) & (labels[None, :] < labels[:, None])
    )
    rank = jnp.sum(ahead, axis=1)
    others = n_row - 1
    turn, place = (rank - 1) // others, (rank - 1) % others
    group = jnp.where(rank == 0, 0, 1 + jnp.where(turn == 0, place, others - 1 - place))
    of_node = jnp.sum(
        jnp.where(cluster[None] == labels[:, None, None, None], group[:, None, None, None], 0),
        axis=0,
    )
    return jnp.where(valid == 1, of_node, n_row)


def compact(
    codes,
    group,
    features,
    block_keep,
    edge_weight,
    weight_one,
    bias_one,
    gain_one,
    shift_one,
    weight_two,
    bias_two,
    gain_two,
    shift_two,
    cotangent,
    places,
    slots,
    seats,
    sizes,
    caps,
):
    row, col = lax.axis_index("row"), lax.axis_index(COL)
    chip, core = lax.axis_index("chip"), lax.axis_index("core")
    n_row, n_col = sizes
    own_cap, send_cap, seat_cap = caps
    own_nodes, in_width = features.shape
    span = n_col * own_cap
    targets = jnp.arange(n_row)

    def in_col(value):
        return lax.dynamic_index_in_dim(value, col, 1, False).reshape(-1)

    def in_row(value):
        return lax.dynamic_index_in_dim(value, row, 0, False).reshape(-1)

    row_codes, col_codes = in_row(codes), in_col(codes)
    tile_rows, tile_cols = edge_weight.shape
    blocks_down, blocks_across = block_keep.shape
    side = tile_rows // blocks_down
    linked = (row_codes[:, None] == col_codes[None, :]) & (row_codes[:, None] & 1 == 1)
    linked = linked.reshape(blocks_down, side, blocks_across, side) & (
        block_keep[:, None, :, None] == 1
    )
    masked = jnp.where(linked.reshape(tile_rows, tile_cols), edge_weight, 0)
    pick_rows = (in_row(group)[None, None, :] == targets[:, None, None]) & (
        in_row(slots)[None, None, :] == jnp.arange(send_cap)[None, :, None]
    )
    pick_cols = (in_col(group)[None, None, :] == targets[:, None, None]) & (
        in_col(places)[None, None, :] == jnp.arange(own_cap)[None, :, None]
    )
    picked = jnp.einsum("sta,ac->stc", pick_rows.astype(jnp.bfloat16), masked)
    packed = jnp.einsum("stc,suc->stu", picked, pick_cols.astype(jnp.bfloat16))
    received = trade(packed, "row")

    group_here = lax.dynamic_index_in_dim(in_row(group).reshape(n_col, -1), col, 0, False)
    seat_here = lax.dynamic_index_in_dim(in_row(seats).reshape(n_col, -1), col, 0, False)
    leave = (group_here[None, None, :] == targets[:, None, None]) & (
        seat_here[None, None, :] == jnp.arange(seat_cap)[None, :, None]
    )
    leave = leave.astype(jnp.bfloat16).reshape(n_row * seat_cap, own_nodes)
    both = jnp.dot(leave, jnp.concatenate([features, cotangent], axis=1))
    both = trade(both.reshape(n_row, seat_cap, -1), "row")
    group_col = lax.dynamic_index_in_dim(group, col, 1, False)
    seats_col = lax.dynamic_index_in_dim(seats, col, 1, False)
    places_col = lax.dynamic_index_in_dim(places, col, 1, False)
    seated = (group_col == row)[:, None, :] & (
        seats_col[:, None, :] == jnp.arange(seat_cap)[None, :, None]
    )
    place_of_seat = jnp.max(jnp.where(seated, places_col[:, None, :], -1), axis=2)
    place_of_seat = place_of_seat.reshape(n_row * seat_cap)
    held_count = jnp.sum(group_col == row)
    valid_rows = (jnp.arange(own_cap) < held_count).astype(jnp.float32)

    standing = jnp.arange(n_col)[None, :, None] * own_cap + places
    fits_here = jnp.where(group == row, standing, -1).reshape(n_row, -1)
    slot_of = slots.reshape(n_row, -1)
    target = jnp.max(
        jnp.where(
            slot_of[:, None, :] == jnp.arange(send_cap)[None, :, None], fits_here[:, None, :], -1
        ),
        axis=2,
    )
    spread = (target[:, :, None] == jnp.arange(span)[None, None, :]).astype(jnp.bfloat16)
    own_block = jnp.einsum("stu,stw->uw", received, spread).astype(jnp.bfloat16)

    quadrant = lax.dynamic_slice_in_dim(own_block, chip * (span // 2), span // 2, 1)
    quadrant = swap(quadrant, "chip")
    adjacency = normalized_block(
        own_block, swap(own_block, "core"), quadrant, swap(quadrant, "core"), chip, core
    )

    both, adjacency = lax.optimization_barrier((both, adjacency))
    arrive = (place_of_seat[None, :] == jnp.arange(own_cap)[:, None]).astype(jnp.bfloat16)
    mine = jnp.dot(arrive, both.reshape(n_row * seat_cap, -1))
    features_own, cotangent_own = mine[:, :in_width], mine[:, in_width:]
    features_all = joined(features_own, swap(features_own, "core"), core)
    features_all = joined(features_all, swap(features_all, "chip"), chip)

    first = (col * own_cap + jnp.arange(own_cap))[:, None] == jnp.arange(span)[None, :]
    previous = first.astype(jnp.float32)
    current = -lax.dynamic_slice_in_dim(adjacency, col * own_cap, own_cap, 0).astype(jnp.float32)
    lowered = [current.astype(jnp.bfloat16)]
    for position in range(2, ORDER):
        upcoming = (
            -2.0 * jnp.dot(lowered[-1], adjacency, preferred_element_type=jnp.float32) - previous
        )
        previous, current = current, upcoming
        lowered.append(upcoming.astype(jnp.bfloat16))
    polynomials = jnp.concatenate(lowered, axis=0)

    def apply(value_low, everyone):
        result = jnp.dot(polynomials, everyone, preferred_element_type=jnp.float32)
        result = result.astype(jnp.bfloat16).reshape(ORDER - 1, own_cap, -1)
        return jnp.concatenate([value_low[None], result], axis=0)

    def everywhere(value_low):
        return lax.all_gather(value_low, COL, axis=0, tiled=True)

    def forward(value_low, everyone, weight, bias, gain, shift):
        stacked = apply(value_low, everyone)
        mixed = jnp.einsum("kni,kio->no", stacked, weight, preferred_element_type=jnp.float32)
        mixed = mixed + bias
        turned = lax.optimization_barrier(stacked.transpose(0, 2, 1))
        return turned, mixed, finish(mixed, gain, shift, valid_rows)

    def through_norm(turned, mixed, upstream, gain, shift):
        ignored, pullback = jax.vjp(
            lambda mixed_in, gain_in, shift_in: finish(mixed_in, gain_in, shift_in, valid_rows),
            mixed,
            gain,
            shift,
        )
        mixed_grad, gain_grad, shift_grad = pullback(upstream)
        mixed_low = mixed_grad.astype(jnp.bfloat16)
        bias_grad = jnp.sum(mixed_low.astype(jnp.float32), axis=0)
        weight_grad = jnp.einsum(
            "kin,no->kio", turned, mixed_low, preferred_element_type=jnp.float32
        ).astype(jnp.bfloat16)
        return mixed_low, weight_grad, [bias_grad, gain_grad, shift_grad]

    def to_input(mixed_low, weight):
        spread_grad = apply(mixed_low, everywhere(mixed_low))
        return jnp.einsum("kno,kio->ni", spread_grad, weight, preferred_element_type=jnp.float32)

    turned_one, mixed_one, hidden = forward(
        features_own, features_all, weight_one, bias_one, gain_one, shift_one
    )
    hidden_low = hidden.astype(jnp.bfloat16)
    turned_two, mixed_two, activations = forward(
        hidden_low, everywhere(hidden_low), weight_two, bias_two, gain_two, shift_two
    )
    width = weight_two.shape[2]
    low_two, weight_two_grad, rest_two = through_norm(
        turned_two, mixed_two, cotangent_own.astype(jnp.float32), gain_two, shift_two
    )
    low_two, weight_two_grad = lax.optimization_barrier((low_two, weight_two_grad))
    second = add_cores(weight_two_grad.reshape(2, 2, -1, width))
    second = add_chips(second)
    hidden_grad = to_input(low_two, weight_two)
    low_one, weight_one_grad, rest_one = through_norm(
        turned_one, mixed_one, hidden_grad, gain_one, shift_one
    )
    tail = weight_one.shape[0] * weight_one.shape[1]
    rest = jnp.stack(rest_one + rest_two).astype(jnp.bfloat16)
    extra = jnp.zeros((-(tail + 6) % (n_row * n_col * 8), width), jnp.bfloat16)
    first = jnp.concatenate([weight_one_grad.reshape(-1, width), rest, extra])
    low_one, first, second = lax.optimization_barrier((low_one, first, second))
    first = add_cores(first.reshape(2, 2, -1, width))
    first = add_chips(first)

    take = place_of_seat[:, None] == jnp.arange(own_cap)[None, :]
    take = take.astype(jnp.bfloat16)
    second = trade(second.reshape(n_row, -1, width), "row")
    second = jnp.sum(second.astype(jnp.float32), axis=0).astype(jnp.bfloat16)
    leaving = jnp.dot(take, activations.astype(jnp.bfloat16)).reshape(n_row, seat_cap, width)
    share = first.shape[0] // n_row
    first = trade(jnp.concatenate([first.reshape(n_row, share, width), leaving], axis=1), "row")
    back = first[:, share:]
    first = jnp.sum(first[:, :share].astype(jnp.float32), axis=0).astype(jnp.bfloat16)
    input_grad = to_input(low_one, weight_one)
    leaving = jnp.dot(take, input_grad.astype(jnp.bfloat16))
    leaving = leaving.reshape(n_row, seat_cap * in_width // width, width)
    summed = jnp.concatenate([second, first])
    share = summed.shape[0]
    summed = jnp.broadcast_to(summed[None], (n_row,) + summed.shape)
    summed = trade(jnp.concatenate([summed, leaving], axis=1), "row")
    back_grad = summed[:, share:].reshape(n_row * seat_cap, in_width)
    summed = lax.all_gather(summed[:, :share], COL, axis=0)
    put = leave.T
    home = jnp.dot(put, back.reshape(-1, width), preferred_element_type=jnp.float32)
    home_grad = jnp.dot(put, back_grad, preferred_element_type=jnp.float32)
    return home, home_grad, summed


def general(
    codes,
    features,
    block_keep,
    edge_weight,
    weight_one,
    bias_one,
    gain_one,
    shift_one,
    weight_two,
    bias_two,
    gain_two,
    shift_two,
    cotangent,
    node_valid,
):
    row, col = lax.axis_index("row"), lax.axis_index(COL)
    row_codes = lax.dynamic_index_in_dim(codes, row, 0, False).reshape(-1)
    col_codes = lax.dynamic_index_in_dim(codes, col, 1, False).reshape(-1)
    tile_rows, tile_cols = edge_weight.shape
    blocks_down, blocks_across = block_keep.shape
    block_side = tile_rows // blocks_down
    linked = (row_codes[:, None] == col_codes[None, :]) & (row_codes[:, None] & 1 == 1)
    linked = linked.reshape(blocks_down, block_side, blocks_across, block_side) & (
        block_keep[:, None, :, None] == 1
    )
    masked = edge_weight * linked.reshape(tile_rows, tile_cols).astype(jnp.bfloat16)
    degree_rows = 1.0 + lax.psum(jnp.sum(masked, axis=1, dtype=jnp.float32), COL)
    own_nodes = features.shape[0]
    own_degree = lax.dynamic_slice_in_dim(
        degree_rows, lax.axis_index(COL) * own_nodes, own_nodes, 0
    )
    degree_cols = lax.all_gather(own_degree, "row", axis=0, tiled=True)
    adjacency = (
        masked.astype(jnp.float32)
        * lax.rsqrt(degree_rows)[:, None]
        * lax.rsqrt(degree_cols)[None, :]
    ).astype(jnp.bfloat16)
    valid_rows = node_valid.astype(jnp.float32)
    stacked_one, mixed_one, hidden = layer_forward(
        adjacency,
        features.astype(jnp.float32),
        weight_one,
        bias_one,
        gain_one,
        shift_one,
        valid_rows,
    )
    stacked_two, mixed_two, activations = layer_forward(
        adjacency, hidden, weight_two, bias_two, gain_two, shift_two, valid_rows
    )
    hidden_grad, weight_two_grad, bias_two_grad, gain_two_grad, shift_two_grad = layer_backward(
        adjacency,
        stacked_two,
        mixed_two,
        cotangent.astype(jnp.float32),
        weight_two,
        gain_two,
        shift_two,
        valid_rows,
    )
    input_grad, weight_one_grad, bias_one_grad, gain_one_grad, shift_one_grad = layer_backward(
        adjacency, stacked_one, mixed_one, hidden_grad, weight_one, gain_one, shift_one, valid_rows
    )
    summed = lax.psum(
        (
            weight_one_grad,
            bias_one_grad,
            gain_one_grad,
            shift_one_grad,
            weight_two_grad,
            bias_two_grad,
            gain_two_grad,
            shift_two_grad,
        ),
        ("row",) + COL,
    )
    weight_one_grad, bias_one_grad, gain_one_grad, shift_one_grad = (
        summed[0],
        summed[1],
        summed[2],
        summed[3],
    )
    weight_two_grad, bias_two_grad, gain_two_grad, shift_two_grad = (
        summed[4],
        summed[5],
        summed[6],
        summed[7],
    )
    return (
        activations,
        input_grad,
        weight_one_grad,
        bias_one_grad,
        gain_one_grad,
        shift_one_grad,
        weight_two_grad,
        bias_two_grad,
        gain_two_grad,
        shift_two_grad,
    )


def local(n_row, n_col, *args):
    (
        features,
        node_valid,
        cluster,
        block_keep,
        edge_weight,
        weight_one,
        bias_one,
        gain_one,
        shift_one,
        weight_two,
        bias_two,
        gain_two,
        shift_two,
        cotangent,
    ) = args
    own_nodes, in_width = features.shape
    own_cap = own_nodes * n_row * 5 // 16
    send_cap = own_nodes * n_col * 3 // 8
    seat_cap = own_nodes // 2
    codes = lax.all_gather(cluster * 2 + node_valid, COL, axis=0)
    codes = broadcast_along(codes, "row", n_row)
    shared = (
        block_keep,
        edge_weight,
        weight_one,
        bias_one,
        gain_one,
        shift_one,
        weight_two,
        bias_two,
        gain_two,
        shift_two,
        cotangent,
    )

    def slow():
        return general(codes, features, *shared, node_valid)

    held = (ORDER - 1) * own_cap * own_cap * n_col * 2
    if held > HELD_BYTES or n_col != 4 or n_row < 2:
        return slow()
    group = assign(codes, n_row)
    member = group[None] == jnp.arange(n_row)[:, None, None, None]
    by_col = member.transpose(0, 2, 1, 3).reshape(n_row, n_col, -1)
    by_row = member.reshape(n_row, n_row, -1)
    places = jnp.sum(jnp.where(by_col, exclusive_counts(by_col), 0), axis=0)
    places = places.reshape(n_col, n_row, own_nodes).transpose(1, 0, 2)
    slots = jnp.sum(jnp.where(by_row, exclusive_counts(by_row), 0), axis=0)
    slots = slots.reshape(n_row, n_col, own_nodes)
    seats = jnp.sum(jnp.where(member, exclusive_counts(member), 0), axis=0)
    fits = (
        (jnp.max(jnp.sum(by_col, axis=2)) <= own_cap)
        & (jnp.max(jnp.sum(by_row, axis=2)) <= send_cap)
        & (jnp.max(jnp.sum(member, axis=3)) <= seat_cap)
    )
    results = compact(
        codes,
        group,
        features,
        *shared,
        places,
        slots,
        seats,
        (n_row, n_col),
        (own_cap, send_cap, seat_cap),
    )

    width = weight_two.shape[2]
    tail = weight_one.shape[0] * weight_one.shape[1]
    many = weight_two.shape[0] * weight_two.shape[1] // (n_row * n_col)

    def again(state):
        made = slow()
        small = [made[place][None] for place in (3, 4, 5, 7, 8, 9)]
        first = jnp.concatenate([made[2].reshape(-1, width)] + small)
        first = jnp.pad(first, ((0, -first.shape[0] % (n_row * n_col * 8)), (0, 0)))
        pieces = [value.reshape(n_col, n_row, -1, width) for value in (made[6], first)]
        return True, (made[0], made[1], jnp.concatenate(pieces, axis=2).astype(jnp.bfloat16))

    activations, input_grad, summed = lax.while_loop(
        lambda state: jnp.logical_not(state[0]), again, (fits, results)
    )[1]
    second = summed[:, :, :many].astype(jnp.float32)
    first = summed[:, :, many:].astype(jnp.float32).reshape(-1, width)
    return (
        activations,
        input_grad,
        first[:tail].reshape(weight_one.shape),
        first[tail],
        first[tail + 1],
        first[tail + 2],
        second.reshape(weight_two.shape),
        first[tail + 3],
        first[tail + 4],
        first[tail + 5],
    )


def solution(mesh):
    n_row, n_col = mesh.shape["row"], mesh.shape["col"]
    by_core = jax.sharding.Mesh(
        mesh.devices.reshape(n_row, n_col // 2, 2), ("row", "chip", "core")
    )
    nodes = ("row", "chip", "core")
    placed = (
        P(nodes, None),
        P(nodes),
        P(nodes),
        P("row", COL),
        P("row", COL),
        P(),
        P(),
        P(),
        P(),
        P(),
        P(),
        P(),
        P(),
        P(nodes, None),
    )
    return jax.shard_map(
        functools.partial(local, n_row, n_col),
        mesh=by_core,
        in_specs=placed,
        out_specs=(P(nodes, None), P(nodes, None), P(), P(), P(), P(), P(), P(), P(), P()),
        check_vma=False,
    )
```

```python
import functools

import jax
import jax.numpy as jnp
from jax import lax
from jax.experimental import pallas as pl
from jax.experimental.pallas import tpu as pltpu
from jax.sharding import PartitionSpec as P

ORDER = 13
CLUSTERS = 16
HELD_BYTES = 1 << 25
COL = ("chip", "core")


def finish(mixed, gain, shift, valid_rows):
    active = jax.nn.gelu(mixed, approximate=False)
    centered = active - jnp.mean(active, axis=-1, keepdims=True)
    variance = jnp.mean(centered * centered, axis=-1, keepdims=True)
    return (centered * lax.rsqrt(variance + 1e-05) * gain + shift) * valid_rows[:, None]


def forward_product(adjacency, piece_low):
    partial_value = jnp.dot(
        adjacency,
        lax.all_gather(piece_low, "row", axis=0, tiled=True),
        preferred_element_type=jnp.float32,
    )
    return lax.psum_scatter(partial_value, COL, scatter_dimension=0, tiled=True)


def backward_product(adjacency, piece_low):
    partial_value = lax.dot_general(
        adjacency,
        lax.all_gather(piece_low, COL, axis=0, tiled=True),
        (((0,), (0,)), ((), ())),
        preferred_element_type=jnp.float32,
    )
    return lax.psum_scatter(
        partial_value.astype(jnp.bfloat16), "row", scatter_dimension=0, tiled=True
    ).astype(jnp.float32)


def layer_forward(adjacency, inputs, weight, bias, gain, shift, valid_rows):
    first_low = inputs.astype(jnp.bfloat16)
    second = -forward_product(adjacency, first_low)
    second_low = second.astype(jnp.bfloat16)

    def advance(state_pair, unused):
        previous, current, current_low = state_pair
        upcoming = -2.0 * forward_product(adjacency, current_low) - previous
        upcoming_low = upcoming.astype(jnp.bfloat16)
        return ((current, upcoming, upcoming_low), upcoming_low)

    ignored, others = lax.scan(advance, (inputs, second, second_low), None, length=ORDER - 2)
    stacked = jnp.concatenate([first_low[None], second_low[None], others], axis=0)
    mixed = jnp.einsum("kni,kio->no", stacked, weight, preferred_element_type=jnp.float32) + bias
    return (stacked, mixed, finish(mixed, gain, shift, valid_rows))


def layer_backward(adjacency, stacked, mixed, upstream, weight, gain, shift, valid_rows):

    def local_finish(mixed_in, gain_in, shift_in):
        return finish(mixed_in, gain_in, shift_in, valid_rows)

    ignored, pullback = jax.vjp(local_finish, mixed, gain, shift)
    mixed_grad, gain_grad, shift_grad = pullback(upstream)
    mixed_low = mixed_grad.astype(jnp.bfloat16)
    bias_grad = jnp.sum(mixed_low.astype(jnp.float32), axis=0)
    weight_grad = jnp.einsum("kni,no->kio", stacked, mixed_low, preferred_element_type=jnp.float32)
    direct = jnp.einsum("no,kio->kni", mixed_low, weight, preferred_element_type=jnp.float32)

    def retreat(state_pair, direct_term):
        later_two, later_one = state_pair
        current = (
            direct_term
            - 2.0 * backward_product(adjacency, later_one.astype(jnp.bfloat16))
            - later_two
        )
        return ((later_one, current), None)

    start_pair = (jnp.zeros_like(direct[0]), direct[ORDER - 1])
    (second_grad, first_grad), unused = lax.scan(
        retreat, start_pair, direct[1 : ORDER - 1], reverse=True
    )
    input_grad = (
        direct[0] - backward_product(adjacency, first_grad.astype(jnp.bfloat16)) - second_grad
    )
    return (input_grad, weight_grad, bias_grad, gain_grad, shift_grad)


def swap(value, axis):
    return lax.ppermute(value, axis, [(0, 1), (1, 0)])


def trade(pieces, axis):
    return lax.all_to_all(pieces, axis, 0, 0, tiled=False)


def broadcast_along(value, axis, size):
    return trade(jnp.broadcast_to(value[None], (size,) + value.shape), axis)


def joined(mine, other, index):
    return jnp.where(
        index == 0, jnp.concatenate([mine, other]), jnp.concatenate([other, mine])
    )


def split(pair, index):
    mine = lax.dynamic_index_in_dim(pair, index, 0, False)
    return mine, lax.dynamic_index_in_dim(pair, 1 - index, 0, False)


def added(mine, received):
    return (mine.astype(jnp.float32) + received.astype(jnp.float32)).astype(jnp.bfloat16)


def block_kernel(place_ref, own_ref, sibling_ref, near_ref, far_ref, out_ref):
    chip, core = place_ref[0], place_ref[1]
    own_cap, span = own_ref.shape
    half = span // 2

    def rows(of_chip, of_core):
        return pl.ds(pl.multiple_of((2 * of_chip + of_core) * own_cap, own_cap), own_cap)

    out_ref[rows(chip, core), :] = own_ref[...]
    out_ref[rows(chip, 1 - core), :] = sibling_ref[...]

    def other_chip(here):
        there = 1 - here
        here_cols, there_cols = pl.ds(here * half, half), pl.ds(there * half, half)
        out_ref[rows(there, core), there_cols] = near_ref[...]
        out_ref[rows(there, 1 - core), there_cols] = far_ref[...]
        for tile in range(half // 128):
            strip = out_ref[here_cols, pl.ds(there * half + tile * 128, 128)]
            turned = jnp.transpose(strip.astype(jnp.float32)).astype(jnp.bfloat16)
            out_ref[pl.ds(there * half + tile * 128, 128), here_cols] = turned

    @pl.when(chip == 0)
    def first():
        other_chip(0)

    @pl.when(chip == 1)
    def second():
        other_chip(1)

    across = jnp.ones((1, span), jnp.float32)
    for tile in range(span // 128):
        across = across + jnp.sum(
            out_ref[pl.ds(tile * 128, 128), :].astype(jnp.float32), axis=0, keepdims=True
        )
    across = lax.rsqrt(across)
    for tile in range(span // 128):
        strip = out_ref[pl.ds(tile * 128, 128), :].astype(jnp.float32)
        down = lax.rsqrt(1.0 + jnp.sum(strip, axis=1, keepdims=True))
        out_ref[pl.ds(tile * 128, 128), :] = (strip * down * across).astype(jnp.bfloat16)


def normalized_block(own, sibling, near, far, chip, core):
    span = own.shape[1]

    def whole(shape):
        return pl.BlockSpec(shape, lambda step: (0, 0))

    return pl.pallas_call(
        block_kernel,
        grid=(1,),
        out_shape=jax.ShapeDtypeStruct((span, span), jnp.bfloat16),
        in_specs=[pl.BlockSpec(memory_space=pltpu.SMEM)]
        + [whole(value.shape) for value in (own, sibling, near, far)],
        out_specs=whole((span, span)),
        compiler_params=pltpu.CompilerParams(vmem_limit_bytes=32 << 20),
        cost_estimate=pl.CostEstimate(
            flops=8 * span * span, bytes_accessed=8 * span * span, transcendentals=0
        ),
        name="normalized_block",
    )(jnp.stack([chip, core]).astype(jnp.int32), own, sibling, near, far)


def exclusive_counts(member):
    count = member.shape[-1]
    before = jnp.arange(count)[:, None] < jnp.arange(count)[None, :]
    return jnp.dot(
        member.astype(jnp.bfloat16),
        before.astype(jnp.bfloat16),
        preferred_element_type=jnp.float32,
    ).astype(jnp.int32)


def assign(codes, n_row):
    cluster, valid = codes >> 1, codes & 1
    labels = jnp.arange(CLUSTERS)
    sizes = jnp.sum(
        (cluster.reshape(1, -1) == labels[:, None]) & (valid.reshape(1, -1) == 1), axis=1
    )
    ahead = (sizes[None, :] > sizes[:, None]) | (
        (sizes[None, :] == sizes[:, None]) & (labels[None, :] < labels[:, None])
    )
    rank = jnp.sum(ahead, axis=1)
    others = n_row - 1
    turn, place = (rank - 1) // others, (rank - 1) % others
    group = jnp.where(rank == 0, 0, 1 + jnp.where(turn == 0, place, others - 1 - place))
    of_node = jnp.sum(
        jnp.where(cluster[None] == labels[:, None, None, None], group[:, None, None, None], 0),
        axis=0,
    )
    return jnp.where(valid == 1, of_node, n_row)


def compact(
    codes,
    group,
    features,
    block_keep,
    edge_weight,
    weight_one,
    bias_one,
    gain_one,
    shift_one,
    weight_two,
    bias_two,
    gain_two,
    shift_two,
    cotangent,
    places,
    slots,
    seats,
    sizes,
    caps,
):
    row, col = lax.axis_index("row"), lax.axis_index(COL)
    chip, core = lax.axis_index("chip"), lax.axis_index("core")
    n_row, n_col = sizes
    own_cap, send_cap, seat_cap = caps
    own_nodes, in_width = features.shape
    span = n_col * own_cap
    targets = jnp.arange(n_row)

    def in_col(value):
        return lax.dynamic_index_in_dim(value, col, 1, False).reshape(-1)

    def in_row(value):
        return lax.dynamic_index_in_dim(value, row, 0, False).reshape(-1)

    row_codes, col_codes = in_row(codes), in_col(codes)
    tile_rows, tile_cols = edge_weight.shape
    blocks_down, blocks_across = block_keep.shape
    side = tile_rows // blocks_down
    linked = (row_codes[:, None] == col_codes[None, :]) & (row_codes[:, None] & 1 == 1)
    linked = linked.reshape(blocks_down, side, blocks_across, side) & (
        block_keep[:, None, :, None] == 1
    )
    masked = jnp.where(linked.reshape(tile_rows, tile_cols), edge_weight, 0)
    pick_rows = (in_row(group)[None, None, :] == targets[:, None, None]) & (
        in_row(slots)[None, None, :] == jnp.arange(send_cap)[None, :, None]
    )
    pick_cols = (in_col(group)[None, None, :] == targets[:, None, None]) & (
        in_col(places)[None, None, :] == jnp.arange(own_cap)[None, :, None]
    )
    picked = jnp.einsum("sta,ac->stc", pick_rows.astype(jnp.bfloat16), masked)
    packed = jnp.einsum("stc,suc->stu", picked, pick_cols.astype(jnp.bfloat16))
    received = trade(packed, "row")

    group_here = lax.dynamic_index_in_dim(in_row(group).reshape(n_col, -1), col, 0, False)
    seat_here = lax.dynamic_index_in_dim(in_row(seats).reshape(n_col, -1), col, 0, False)
    leave = (group_here[None, None, :] == targets[:, None, None]) & (
        seat_here[None, None, :] == jnp.arange(seat_cap)[None, :, None]
    )
    leave = leave.astype(jnp.bfloat16).reshape(n_row * seat_cap, own_nodes)
    both = jnp.dot(leave, jnp.concatenate([features, cotangent], axis=1))
    received, both = lax.optimization_barrier((received, both))
    both = trade(both.reshape(n_row, seat_cap, -1), "row")
    group_col = lax.dynamic_index_in_dim(group, col, 1, False)
    seats_col = lax.dynamic_index_in_dim(seats, col, 1, False)
    places_col = lax.dynamic_index_in_dim(places, col, 1, False)
    seated = (group_col == row)[:, None, :] & (
        seats_col[:, None, :] == jnp.arange(seat_cap)[None, :, None]
    )
    place_of_seat = jnp.max(jnp.where(seated, places_col[:, None, :], -1), axis=2)
    place_of_seat = place_of_seat.reshape(n_row * seat_cap)
    held_count = jnp.sum(group_col == row)
    valid_rows = (jnp.arange(own_cap) < held_count).astype(jnp.float32)

    standing = jnp.arange(n_col)[None, :, None] * own_cap + places
    fits_here = jnp.where(group == row, standing, -1).reshape(n_row, -1)
    slot_of = slots.reshape(n_row, -1)
    target = jnp.max(
        jnp.where(
            slot_of[:, None, :] == jnp.arange(send_cap)[None, :, None], fits_here[:, None, :], -1
        ),
        axis=2,
    )
    spread = (target[:, :, None] == jnp.arange(span)[None, None, :]).astype(jnp.bfloat16)
    own_block = jnp.einsum("stu,stw->uw", received, spread).astype(jnp.bfloat16)

    quadrant = lax.dynamic_slice_in_dim(own_block, chip * (span // 2), span // 2, 1)
    quadrant = swap(quadrant, "chip")
    adjacency = normalized_block(
        own_block, swap(own_block, "core"), quadrant, swap(quadrant, "core"), chip, core
    )

    both, adjacency = lax.optimization_barrier((both, adjacency))
    arrive = (place_of_seat[None, :] == jnp.arange(own_cap)[:, None]).astype(jnp.bfloat16)
    mine = jnp.dot(arrive, both.reshape(n_row * seat_cap, -1))
    features_own, cotangent_own = mine[:, :in_width], mine[:, in_width:]
    features_all = joined(features_own, swap(features_own, "core"), core)
    features_all = joined(features_all, swap(features_all, "chip"), chip)

    first = (col * own_cap + jnp.arange(own_cap))[:, None] == jnp.arange(span)[None, :]
    previous = first.astype(jnp.float32)
    current = -lax.dynamic_slice_in_dim(adjacency, col * own_cap, own_cap, 0).astype(jnp.float32)
    lowered = [current.astype(jnp.bfloat16)]
    for position in range(2, ORDER):
        upcoming = (
            -2.0 * jnp.dot(lowered[-1], adjacency, preferred_element_type=jnp.float32) - previous
        )
        previous, current = current, upcoming
        lowered.append(upcoming.astype(jnp.bfloat16))
    polynomials = jnp.concatenate(lowered, axis=0)

    def apply(value_low, everyone):
        result = jnp.dot(polynomials, everyone, preferred_element_type=jnp.float32)
        result = result.astype(jnp.bfloat16).reshape(ORDER - 1, own_cap, -1)
        return jnp.concatenate([value_low[None], result], axis=0)

    def everywhere(value_low):
        return lax.all_gather(value_low, COL, axis=0, tiled=True)

    def forward(value_low, everyone, weight, bias, gain, shift):
        stacked = apply(value_low, everyone)
        mixed = jnp.einsum("kni,kio->no", stacked, weight, preferred_element_type=jnp.float32)
        mixed = mixed + bias
        turned = lax.optimization_barrier(stacked.transpose(0, 2, 1))
        return turned, mixed, finish(mixed, gain, shift, valid_rows)

    def through_norm(turned, mixed, upstream, gain, shift):
        ignored, pullback = jax.vjp(
            lambda mixed_in, gain_in, shift_in: finish(mixed_in, gain_in, shift_in, valid_rows),
            mixed,
            gain,
            shift,
        )
        mixed_grad, gain_grad, shift_grad = pullback(upstream)
        mixed_low = mixed_grad.astype(jnp.bfloat16)
        bias_grad = jnp.sum(mixed_low.astype(jnp.float32), axis=0)
        weight_grad = jnp.einsum(
            "kin,no->kio", turned, mixed_low, preferred_element_type=jnp.float32
        ).astype(jnp.bfloat16)
        return mixed_low, weight_grad, [bias_grad, gain_grad, shift_grad]

    def to_input(mixed_low, everyone, weight):
        spread_grad = apply(mixed_low, everyone)
        return jnp.einsum("kno,kio->ni", spread_grad, weight, preferred_element_type=jnp.float32)

    width = weight_two.shape[2]
    turned_one, mixed_one, hidden = forward(
        features_own, features_all, weight_one, bias_one, gain_one, shift_one
    )
    hidden_low = hidden.astype(jnp.bfloat16)
    turned_two, mixed_two, activations = forward(
        hidden_low, everywhere(hidden_low), weight_two, bias_two, gain_two, shift_two
    )
    width = weight_two.shape[2]
    take = place_of_seat[:, None] == jnp.arange(own_cap)[None, :]
    take = take.astype(jnp.bfloat16)
    leaving = jnp.dot(take, activations.astype(jnp.bfloat16)).reshape(n_row, seat_cap, width)

    low_two, second, rest_two = through_norm(
        turned_two, mixed_two, cotangent_own.astype(jnp.float32), gain_two, shift_two
    )
    mine, other = split(second.reshape(2, -1, width), core)
    low_two, other = lax.optimization_barrier((low_two, other))
    everyone_two = everywhere(low_two)
    mine, other = split(added(mine, swap(other, "core")).reshape(2, -1, width), chip)
    everyone_two, other = lax.optimization_barrier((everyone_two, other))
    second = added(mine, swap(other, "chip"))
    hidden_grad = to_input(low_two, everyone_two, weight_two)

    low_one, first, rest_one = through_norm(
        turned_one, mixed_one, hidden_grad, gain_one, shift_one
    )
    tail = weight_one.shape[0] * weight_one.shape[1]
    rest = jnp.stack(rest_one + rest_two).astype(jnp.bfloat16)
    extra = jnp.zeros((-(tail + 6) % (n_row * n_col * 8), width), jnp.bfloat16)
    first = jnp.concatenate([first.reshape(-1, width), rest, extra])
    mine, other = split(first.reshape(2, -1, width), core)
    first = added(mine, swap(other, "core")).reshape(n_row, 2, -1, width)
    mine, other = split(first.swapaxes(0, 1), chip)
    first = added(mine, swap(other, "chip"))

    share_two, share_one = second.shape[0] // n_row, first.shape[1]
    shares = jnp.concatenate([second.reshape(n_row, share_two, width), first, leaving], axis=1)
    low_one, shares = lax.optimization_barrier((low_one, shares))
    everyone_one = everywhere(low_one)
    shares = trade(shares, "row")
    back = shares[:, share_two + share_one :]
    total = jnp.sum(shares[:, : share_two + share_one].astype(jnp.float32), axis=0)
    total = total.astype(jnp.bfloat16)
    second, first = total[:share_two], total[share_two:]
    second = broadcast_along(second, "row", n_row).reshape(n_row * share_two, width)
    first = joined(first, swap(first, "chip"), chip)
    input_grad = to_input(low_one, everyone_one, weight_one)
    leaving = jnp.dot(take, input_grad.astype(jnp.bfloat16))
    leaving = leaving.reshape(n_row, seat_cap * in_width // width, width)
    first = jnp.broadcast_to(first[None], (n_row,) + first.shape)
    first = trade(jnp.concatenate([first, leaving], axis=1), "row")
    back_grad = first[:, 2 * share_one :].reshape(n_row * seat_cap, in_width)
    first = first[:, : 2 * share_one].reshape(-1, width)
    second = joined(second, swap(second, "chip"), chip)
    put = leave.T
    home = jnp.dot(put, back.reshape(-1, width), preferred_element_type=jnp.float32)
    home_grad = jnp.dot(put, back_grad, preferred_element_type=jnp.float32)
    return home, home_grad, first, swap(first, "core"), second, swap(second, "core")


def general(
    codes,
    features,
    block_keep,
    edge_weight,
    weight_one,
    bias_one,
    gain_one,
    shift_one,
    weight_two,
    bias_two,
    gain_two,
    shift_two,
    cotangent,
    node_valid,
):
    row, col = lax.axis_index("row"), lax.axis_index(COL)
    row_codes = lax.dynamic_index_in_dim(codes, row, 0, False).reshape(-1)
    col_codes = lax.dynamic_index_in_dim(codes, col, 1, False).reshape(-1)
    tile_rows, tile_cols = edge_weight.shape
    blocks_down, blocks_across = block_keep.shape
    block_side = tile_rows // blocks_down
    linked = (row_codes[:, None] == col_codes[None, :]) & (row_codes[:, None] & 1 == 1)
    linked = linked.reshape(blocks_down, block_side, blocks_across, block_side) & (
        block_keep[:, None, :, None] == 1
    )
    masked = edge_weight * linked.reshape(tile_rows, tile_cols).astype(jnp.bfloat16)
    degree_rows = 1.0 + lax.psum(jnp.sum(masked, axis=1, dtype=jnp.float32), COL)
    own_nodes = features.shape[0]
    own_degree = lax.dynamic_slice_in_dim(
        degree_rows, lax.axis_index(COL) * own_nodes, own_nodes, 0
    )
    degree_cols = lax.all_gather(own_degree, "row", axis=0, tiled=True)
    adjacency = (
        masked.astype(jnp.float32)
        * lax.rsqrt(degree_rows)[:, None]
        * lax.rsqrt(degree_cols)[None, :]
    ).astype(jnp.bfloat16)
    valid_rows = node_valid.astype(jnp.float32)
    stacked_one, mixed_one, hidden = layer_forward(
        adjacency,
        features.astype(jnp.float32),
        weight_one,
        bias_one,
        gain_one,
        shift_one,
        valid_rows,
    )
    stacked_two, mixed_two, activations = layer_forward(
        adjacency, hidden, weight_two, bias_two, gain_two, shift_two, valid_rows
    )
    hidden_grad, weight_two_grad, bias_two_grad, gain_two_grad, shift_two_grad = layer_backward(
        adjacency,
        stacked_two,
        mixed_two,
        cotangent.astype(jnp.float32),
        weight_two,
        gain_two,
        shift_two,
        valid_rows,
    )
    input_grad, weight_one_grad, bias_one_grad, gain_one_grad, shift_one_grad = layer_backward(
        adjacency, stacked_one, mixed_one, hidden_grad, weight_one, gain_one, shift_one, valid_rows
    )
    summed = lax.psum(
        (
            weight_one_grad,
            bias_one_grad,
            gain_one_grad,
            shift_one_grad,
            weight_two_grad,
            bias_two_grad,
            gain_two_grad,
            shift_two_grad,
        ),
        ("row",) + COL,
    )
    weight_one_grad, bias_one_grad, gain_one_grad, shift_one_grad = (
        summed[0],
        summed[1],
        summed[2],
        summed[3],
    )
    weight_two_grad, bias_two_grad, gain_two_grad, shift_two_grad = (
        summed[4],
        summed[5],
        summed[6],
        summed[7],
    )
    return (
        activations,
        input_grad,
        weight_one_grad,
        bias_one_grad,
        gain_one_grad,
        shift_one_grad,
        weight_two_grad,
        bias_two_grad,
        gain_two_grad,
        shift_two_grad,
    )


def local(n_row, n_col, *args):
    (
        features,
        node_valid,
        cluster,
        block_keep,
        edge_weight,
        weight_one,
        bias_one,
        gain_one,
        shift_one,
        weight_two,
        bias_two,
        gain_two,
        shift_two,
        cotangent,
    ) = args
    own_nodes, in_width = features.shape
    own_cap = own_nodes * n_row * 5 // 16
    send_cap = own_nodes * n_col * 3 // 8
    seat_cap = own_nodes // 2
    codes = lax.all_gather(cluster * 2 + node_valid, COL, axis=0)
    codes = broadcast_along(codes, "row", n_row)
    shared = (
        block_keep,
        edge_weight,
        weight_one,
        bias_one,
        gain_one,
        shift_one,
        weight_two,
        bias_two,
        gain_two,
        shift_two,
        cotangent,
    )

    def slow():
        return general(codes, features, *shared, node_valid)

    held = (ORDER - 1) * own_cap * own_cap * n_col * 2
    if held > HELD_BYTES or n_col != 4 or n_row < 2:
        return slow()
    group = assign(codes, n_row)
    member = group[None] == jnp.arange(n_row)[:, None, None, None]
    by_col = member.transpose(0, 2, 1, 3).reshape(n_row, n_col, -1)
    by_row = member.reshape(n_row, n_row, -1)
    places = jnp.sum(jnp.where(by_col, exclusive_counts(by_col), 0), axis=0)
    places = places.reshape(n_col, n_row, own_nodes).transpose(1, 0, 2)
    slots = jnp.sum(jnp.where(by_row, exclusive_counts(by_row), 0), axis=0)
    slots = slots.reshape(n_row, n_col, own_nodes)
    seats = jnp.sum(jnp.where(member, exclusive_counts(member), 0), axis=0)
    fits = (
        (jnp.max(jnp.sum(by_col, axis=2)) <= own_cap)
        & (jnp.max(jnp.sum(by_row, axis=2)) <= send_cap)
        & (jnp.max(jnp.sum(member, axis=3)) <= seat_cap)
    )
    results = compact(
        codes,
        group,
        features,
        *shared,
        places,
        slots,
        seats,
        (n_row, n_col),
        (own_cap, send_cap, seat_cap),
    )

    width = weight_two.shape[2]
    tail = weight_one.shape[0] * weight_one.shape[1]
    core = lax.axis_index("core")

    def again(state):
        made = slow()
        small = [made[place][None] for place in (3, 4, 5, 7, 8, 9)]
        first = jnp.concatenate([made[2].reshape(-1, width)] + small).astype(jnp.bfloat16)
        first = jnp.pad(first, ((0, -first.shape[0] % (n_row * n_col * 8)), (0, 0)))
        second = made[6].astype(jnp.bfloat16).reshape(2, -1, width)
        return True, made[:2] + split(first.reshape(2, -1, width), core) + split(second, core)

    activations, input_grad, *parts = lax.while_loop(
        lambda state: jnp.logical_not(state[0]), again, (fits, results)
    )[1]
    first = joined(parts[0], parts[1], core).astype(jnp.float32)
    second = joined(parts[2], parts[3], core).astype(jnp.float32)
    return (
        activations,
        input_grad,
        first[:tail].reshape(weight_one.shape),
        first[tail],
        first[tail + 1],
        first[tail + 2],
        second.reshape(weight_two.shape),
        first[tail + 3],
        first[tail + 4],
        first[tail + 5],
    )


def solution(mesh):
    n_row, n_col = mesh.shape["row"], mesh.shape["col"]
    by_core = jax.sharding.Mesh(
        mesh.devices.reshape(n_row, n_col // 2, 2), ("row", "chip", "core")
    )
    nodes = ("row", "chip", "core")
    placed = (
        P(nodes, None),
        P(nodes),
        P(nodes),
        P("row", COL),
        P("row", COL),
        P(),
        P(),
        P(),
        P(),
        P(),
        P(),
        P(),
        P(),
        P(nodes, None),
    )
    return jax.shard_map(
        functools.partial(local, n_row, n_col),
        mesh=by_core,
        in_specs=placed,
        out_specs=(P(nodes, None), P(nodes, None), P(), P(), P(), P(), P(), P(), P(), P()),
        check_vma=False,
    )
```

```python
import functools
import math

import jax
import jax.numpy as jnp
from jax import lax
from jax.experimental import pallas as pl
from jax.experimental.pallas import tpu as pltpu
from jax.sharding import PartitionSpec as P

ORDER = 13
CLUSTERS = 16
HELD_BYTES = 1 << 25
VMEM_BYTES = 40 << 20
COL = ("chip", "core")


def finish(mixed, gain, shift, valid_rows):
    active = jax.nn.gelu(mixed, approximate=False)
    centered = active - jnp.mean(active, axis=-1, keepdims=True)
    variance = jnp.mean(centered * centered, axis=-1, keepdims=True)
    return (centered * lax.rsqrt(variance + 1e-05) * gain + shift) * valid_rows[:, None]


def forward_product(adjacency, piece_low):
    partial_value = jnp.dot(
        adjacency,
        lax.all_gather(piece_low, "row", axis=0, tiled=True),
        preferred_element_type=jnp.float32,
    )
    return lax.psum_scatter(partial_value, COL, scatter_dimension=0, tiled=True)


def backward_product(adjacency, piece_low):
    partial_value = lax.dot_general(
        adjacency,
        lax.all_gather(piece_low, COL, axis=0, tiled=True),
        (((0,), (0,)), ((), ())),
        preferred_element_type=jnp.float32,
    )
    return lax.psum_scatter(
        partial_value.astype(jnp.bfloat16), "row", scatter_dimension=0, tiled=True
    ).astype(jnp.float32)


def layer_forward(adjacency, inputs, weight, bias, gain, shift, valid_rows):
    first_low = inputs.astype(jnp.bfloat16)
    second = -forward_product(adjacency, first_low)
    second_low = second.astype(jnp.bfloat16)

    def advance(state_pair, unused):
        previous, current, current_low = state_pair
        upcoming = -2.0 * forward_product(adjacency, current_low) - previous
        upcoming_low = upcoming.astype(jnp.bfloat16)
        return ((current, upcoming, upcoming_low), upcoming_low)

    ignored, others = lax.scan(advance, (inputs, second, second_low), None, length=ORDER - 2)
    stacked = jnp.concatenate([first_low[None], second_low[None], others], axis=0)
    mixed = jnp.einsum("kni,kio->no", stacked, weight, preferred_element_type=jnp.float32) + bias
    return (stacked, mixed, finish(mixed, gain, shift, valid_rows))


def layer_backward(adjacency, stacked, mixed, upstream, weight, gain, shift, valid_rows):

    def local_finish(mixed_in, gain_in, shift_in):
        return finish(mixed_in, gain_in, shift_in, valid_rows)

    ignored, pullback = jax.vjp(local_finish, mixed, gain, shift)
    mixed_grad, gain_grad, shift_grad = pullback(upstream)
    mixed_low = mixed_grad.astype(jnp.bfloat16)
    bias_grad = jnp.sum(mixed_low.astype(jnp.float32), axis=0)
    weight_grad = jnp.einsum("kni,no->kio", stacked, mixed_low, preferred_element_type=jnp.float32)
    direct = jnp.einsum("no,kio->kni", mixed_low, weight, preferred_element_type=jnp.float32)

    def retreat(state_pair, direct_term):
        later_two, later_one = state_pair
        current = (
            direct_term
            - 2.0 * backward_product(adjacency, later_one.astype(jnp.bfloat16))
            - later_two
        )
        return ((later_one, current), None)

    start_pair = (jnp.zeros_like(direct[0]), direct[ORDER - 1])
    (second_grad, first_grad), unused = lax.scan(
        retreat, start_pair, direct[1 : ORDER - 1], reverse=True
    )
    input_grad = (
        direct[0] - backward_product(adjacency, first_grad.astype(jnp.bfloat16)) - second_grad
    )
    return (input_grad, weight_grad, bias_grad, gain_grad, shift_grad)


def swap(value, axis):
    return lax.ppermute(value, axis, [(0, 1), (1, 0)])


def trade(pieces, axis):
    return lax.all_to_all(pieces, axis, 0, 0, tiled=False)


def broadcast_along(value, axis, size):
    return trade(jnp.broadcast_to(value[None], (size,) + value.shape), axis)


def joined(mine, other, index):
    return jnp.where(
        index == 0, jnp.concatenate([mine, other]), jnp.concatenate([other, mine])
    )


def split(pair, index):
    mine = lax.dynamic_index_in_dim(pair, index, 0, False)
    return mine, lax.dynamic_index_in_dim(pair, 1 - index, 0, False)


def added(mine, received):
    return (mine.astype(jnp.float32) + received.astype(jnp.float32)).astype(jnp.bfloat16)


def assemble(place_ref, own_ref, sibling_ref, near_ref, far_ref, out_ref):
    chip, core = place_ref[0], place_ref[1]
    own_cap, span = own_ref.shape
    half = span // 2

    def rows(of_chip, of_core):
        return pl.ds(pl.multiple_of((2 * of_chip + of_core) * own_cap, own_cap), own_cap)

    out_ref[rows(chip, core), :] = own_ref[...]
    out_ref[rows(chip, 1 - core), :] = sibling_ref[...]

    def other_chip(here):
        there = 1 - here
        here_cols, there_cols = pl.ds(here * half, half), pl.ds(there * half, half)
        out_ref[rows(there, core), there_cols] = near_ref[...]
        out_ref[rows(there, 1 - core), there_cols] = far_ref[...]
        for tile in range(half // 128):
            strip = out_ref[here_cols, pl.ds(there * half + tile * 128, 128)]
            turned = jnp.transpose(strip.astype(jnp.float32)).astype(jnp.bfloat16)
            out_ref[pl.ds(there * half + tile * 128, 128), here_cols] = turned

    @pl.when(chip == 0)
    def first():
        other_chip(0)

    @pl.when(chip == 1)
    def second():
        other_chip(1)

    across = jnp.ones((1, span), jnp.float32)
    for tile in range(span // 128):
        across = across + jnp.sum(
            out_ref[pl.ds(tile * 128, 128), :].astype(jnp.float32), axis=0, keepdims=True
        )
    across = lax.rsqrt(across)
    for tile in range(span // 128):
        strip = out_ref[pl.ds(tile * 128, 128), :].astype(jnp.float32)
        down = lax.rsqrt(1.0 + jnp.sum(strip, axis=1, keepdims=True))
        out_ref[pl.ds(tile * 128, 128), :] = (strip * down * across).astype(jnp.bfloat16)


def polynomial_kernel(
    place_ref, own_ref, sibling_ref, near_ref, far_ref, out_ref, matrix, states, lowered
):
    step = pl.program_id(0)
    own_cap, span = own_ref.shape
    new, old = (step + 1) % 2, step % 2

    @pl.when(step == 0)
    def begin():
        assemble(place_ref, own_ref, sibling_ref, near_ref, far_ref, matrix)
        start = pl.multiple_of((2 * place_ref[0] + place_ref[1]) * own_cap, own_cap)
        current = -matrix[pl.ds(start, own_cap), :].astype(jnp.float32)
        states[new] = current
        lowered[new] = current.astype(jnp.bfloat16)
        row = lax.broadcasted_iota(jnp.int32, (own_cap, span), 0) + start
        column = lax.broadcasted_iota(jnp.int32, (own_cap, span), 1)
        states[old] = (row == column).astype(jnp.float32)
        out_ref[0] = current.astype(jnp.bfloat16)

    @pl.when(step > 0)
    def advance():
        for tile in range(span // 256):
            columns = pl.ds(tile * 256, 256)
            upcoming = -2.0 * jnp.dot(
                lowered[old], matrix[:, columns], preferred_element_type=jnp.float32
            )
            upcoming = upcoming - states[new, :, columns]
            states[new, :, columns] = upcoming
            lowered[new, :, columns] = upcoming.astype(jnp.bfloat16)
            out_ref[0, :, columns] = upcoming.astype(jnp.bfloat16)


def polynomials_of(own, sibling, near, far, chip, core):
    own_cap, span = own.shape

    def whole(value):
        return pl.BlockSpec(value.shape, lambda step: (0, 0))

    return pl.pallas_call(
        polynomial_kernel,
        grid=(ORDER - 1,),
        out_shape=jax.ShapeDtypeStruct((ORDER - 1, own_cap, span), jnp.bfloat16),
        in_specs=[pl.BlockSpec(memory_space=pltpu.SMEM)]
        + [whole(value) for value in (own, sibling, near, far)],
        out_specs=pl.BlockSpec((1, own_cap, span), lambda step: (step, 0, 0)),
        scratch_shapes=[
            pltpu.VMEM((span, span), jnp.bfloat16),
            pltpu.VMEM((2, own_cap, span), jnp.float32),
            pltpu.VMEM((2, own_cap, span), jnp.bfloat16),
        ],
        compiler_params=pltpu.CompilerParams(vmem_limit_bytes=VMEM_BYTES),
        cost_estimate=pl.CostEstimate(
            flops=2 * (ORDER - 2) * own_cap * span * span,
            bytes_accessed=2 * ORDER * own_cap * span,
            transcendentals=0,
        ),
        name="polynomials",
    )(jnp.stack([chip, core]).astype(jnp.int32), own, sibling, near, far)


def normal_share(mixed):
    return 0.5 * (1.0 + lax.erf(mixed * 0.5**0.5))


def norm_forward(mixed):
    active = mixed * normal_share(mixed)
    centered = active - jnp.mean(active, axis=-1, keepdims=True)
    scale = lax.rsqrt(jnp.mean(centered * centered, axis=-1, keepdims=True) + 1e-05)
    return centered * scale, scale


def norm_backward(mixed, upstream, gain, valid):
    normed, scale = norm_forward(mixed)
    upstream = upstream * valid
    inner = upstream * gain
    inner = inner - jnp.mean(inner, axis=-1, keepdims=True) - normed * jnp.mean(
        inner * normed, axis=-1, keepdims=True
    )
    density = jnp.exp(-0.5 * mixed * mixed) * (1.0 / (2.0 * math.pi) ** 0.5)
    low = (inner * scale * (normal_share(mixed) + mixed * density)).astype(jnp.bfloat16)
    rest = [low.astype(jnp.float32), upstream * normed, upstream]
    return low, [jnp.sum(value, axis=0, keepdims=True) for value in rest]


def weight_gradient(stacked_ref, low, core, mine_ref, other_ref):
    order, ignored, fan_in = stacked_ref.shape
    half = order * fan_in // 2

    def halves(first_ref, second_ref):
        for term in range(order):
            value = lax.dot_general(
                stacked_ref[term],
                low,
                (((0,), (0,)), ((), ())),
                preferred_element_type=jnp.float32,
            ).astype(jnp.bfloat16)
            start = term * fan_in
            if start + fan_in <= half:
                first_ref[start : start + fan_in, :] = value
            elif start >= half:
                second_ref[start - half : start - half + fan_in, :] = value
            else:
                first_ref[start:half, :] = value[: half - start]
                second_ref[: start + fan_in - half, :] = value[half - start :]

    @pl.when(core == 0)
    def low_half_first():
        halves(mine_ref, other_ref)

    @pl.when(core == 1)
    def high_half_first():
        halves(other_ref, mine_ref)


def forward_step(step, powers_ref, all_ref, own_ref, weight_ref, bias_ref, stacked, mixed):
    @pl.when(step == 0)
    def first():
        stacked[0] = own_ref[...]
        mixed[...] = bias_ref[...] + jnp.dot(
            own_ref[...], weight_ref[0], preferred_element_type=jnp.float32
        )

    @pl.when(step > 0)
    def others():
        low = jnp.dot(powers_ref[0], all_ref[...], preferred_element_type=jnp.float32)
        low = low.astype(jnp.bfloat16)
        stacked[step] = low
        mixed[...] += jnp.dot(low, weight_ref[0], preferred_element_type=jnp.float32)


def layer_one_kernel(
    powers_ref,
    all_ref,
    own_ref,
    weight_ref,
    bias_ref,
    gain_ref,
    shift_ref,
    valid_ref,
    hidden_ref,
    stacked_ref,
    mixed_ref,
):
    step = pl.program_id(0)
    forward_step(
        step, powers_ref, all_ref, own_ref, weight_ref, bias_ref, stacked_ref, mixed_ref
    )

    @pl.when(step == ORDER - 1)
    def finish_layer():
        normed, ignored = norm_forward(mixed_ref[...])
        hidden = (normed * gain_ref[...] + shift_ref[...]) * valid_ref[...]
        hidden_ref[...] = hidden.astype(jnp.bfloat16)


def layer_two_kernel(
    place_ref,
    powers_ref,
    all_ref,
    own_ref,
    weight_ref,
    bias_ref,
    gain_ref,
    shift_ref,
    valid_ref,
    upstream_ref,
    active_ref,
    low_ref,
    rest_ref,
    mine_ref,
    other_ref,
    stacked,
    mixed,
):
    step = pl.program_id(0)
    forward_step(step, powers_ref, all_ref, own_ref, weight_ref, bias_ref, stacked, mixed)

    @pl.when(step == ORDER - 1)
    def finish_layer():
        normed, ignored = norm_forward(mixed[...])
        active = (normed * gain_ref[...] + shift_ref[...]) * valid_ref[...]
        active_ref[...] = active.astype(jnp.bfloat16)
        low, rest = norm_backward(
            mixed[...], upstream_ref[...].astype(jnp.float32), gain_ref[...], valid_ref[...]
        )
        low_ref[...] = low
        for place in range(3):
            rest_ref[place : place + 1, :] = rest[place]
        weight_gradient(stacked, low, place_ref[1], mine_ref, other_ref)


def backward_step(step, powers_ref, all_ref, own_ref, weight_ref, total):
    transposed = (((1,), (1,)), ((), ()))

    @pl.when(step == 0)
    def first():
        total[...] = lax.dot_general(
            own_ref[...], weight_ref[0], transposed, preferred_element_type=jnp.float32
        )

    @pl.when(step > 0)
    def others():
        low = jnp.dot(powers_ref[0], all_ref[...], preferred_element_type=jnp.float32)
        total[...] += lax.dot_general(
            low.astype(jnp.bfloat16), weight_ref[0], transposed, preferred_element_type=jnp.float32
        )


def back_two_kernel(
    place_ref,
    powers_ref,
    all_ref,
    own_ref,
    weight_ref,
    stacked_ref,
    mixed_ref,
    gain_ref,
    valid_ref,
    rest_ref,
    low_ref,
    mine_ref,
    other_ref,
    total,
):
    step = pl.program_id(0)
    backward_step(step, powers_ref, all_ref, own_ref, weight_ref, total)

    @pl.when(step == ORDER - 1)
    def finish_layer():
        low, rest = norm_backward(mixed_ref[...], total[...], gain_ref[...], valid_ref[...])
        low_ref[...] = low
        weight_gradient(stacked_ref, low, place_ref[1], mine_ref, other_ref)
        half = stacked_ref.shape[0] * stacked_ref.shape[2] // 2
        extra = jnp.zeros((mine_ref.shape[0] - half, mine_ref.shape[1]), jnp.bfloat16)
        rows = rest + [rest_ref[place : place + 1, :] for place in range(3)]
        rows = jnp.concatenate(rows + [jnp.zeros((10, rows[0].shape[1]), jnp.float32)], axis=0)

        def below(first_ref, second_ref):
            first_ref[half:, :] = extra
            second_ref[half:, :] = extra
            first_ref[half : half + 16, :] = rows.astype(jnp.bfloat16)

        @pl.when(place_ref[1] == 0)
        def low_half_here():
            below(mine_ref, other_ref)

        @pl.when(place_ref[1] == 1)
        def low_half_there():
            below(other_ref, mine_ref)


def back_one_kernel(powers_ref, all_ref, own_ref, weight_ref, out_ref, total):
    step = pl.program_id(0)
    backward_step(step, powers_ref, all_ref, own_ref, weight_ref, total)

    @pl.when(step == ORDER - 1)
    def finish_layer():
        out_ref[...] = total[...].astype(jnp.bfloat16)


def layer_pass(kernel, name, place, powers, everyone, own, weight, others, outs, scratch):
    ignored, own_cap, span = powers.shape
    fan_in, width = weight.shape[1:]

    def whole(value):
        return pl.BlockSpec(value.shape, lambda step: (0,) * len(value.shape))

    in_specs = [
        pl.BlockSpec((1, own_cap, span), lambda step: (jnp.maximum(step - 1, 0), 0, 0)),
        whole(everyone),
        whole(own),
        pl.BlockSpec((1, fan_in, width), lambda step: (step, 0, 0)),
    ] + [whole(value) for value in others]
    operands = [powers, everyone, own, weight] + list(others)
    if place is not None:
        in_specs = [pl.BlockSpec(memory_space=pltpu.SMEM)] + in_specs
        operands = [place] + operands
    return pl.pallas_call(
        kernel,
        grid=(ORDER,),
        out_shape=outs,
        in_specs=in_specs,
        out_specs=[whole(value) for value in outs],
        scratch_shapes=[pltpu.VMEM(shape, dtype) for shape, dtype in scratch],
        compiler_params=pltpu.CompilerParams(vmem_limit_bytes=VMEM_BYTES),
        cost_estimate=pl.CostEstimate(
            flops=2 * ORDER * own_cap * (span * everyone.shape[1] + fan_in * width),
            bytes_accessed=2 * ORDER * (own_cap * span + fan_in * width),
            transcendentals=2 * own_cap * width,
        ),
        name=name,
    )(*operands)


def exclusive_counts(member):
    count = member.shape[-1]
    before = jnp.arange(count)[:, None] < jnp.arange(count)[None, :]
    return jnp.dot(
        member.astype(jnp.bfloat16),
        before.astype(jnp.bfloat16),
        preferred_element_type=jnp.float32,
    ).astype(jnp.int32)


def assign(codes, n_row):
    cluster, valid = codes >> 1, codes & 1
    labels = jnp.arange(CLUSTERS)
    sizes = jnp.sum(
        (cluster.reshape(1, -1) == labels[:, None]) & (valid.reshape(1, -1) == 1), axis=1
    )
    ahead = (sizes[None, :] > sizes[:, None]) | (
        (sizes[None, :] == sizes[:, None]) & (labels[None, :] < labels[:, None])
    )
    rank = jnp.sum(ahead, axis=1)
    others = n_row - 1
    turn, place = (rank - 1) // others, (rank - 1) % others
    group = jnp.where(rank == 0, 0, 1 + jnp.where(turn == 0, place, others - 1 - place))
    of_node = jnp.sum(
        jnp.where(cluster[None] == labels[:, None, None, None], group[:, None, None, None], 0),
        axis=0,
    )
    return jnp.where(valid == 1, of_node, n_row)


def compact(
    codes,
    group,
    features,
    block_keep,
    edge_weight,
    weight_one,
    bias_one,
    gain_one,
    shift_one,
    weight_two,
    bias_two,
    gain_two,
    shift_two,
    cotangent,
    places,
    slots,
    seats,
    nodes_all,
    sizes,
    caps,
):
    row, col = lax.axis_index("row"), lax.axis_index(COL)
    chip, core = lax.axis_index("chip"), lax.axis_index("core")
    n_row, n_col = sizes
    own_cap, send_cap, seat_cap = caps
    in_width = features.shape[1]
    span = n_col * own_cap
    targets = jnp.arange(n_row)

    def in_col(value):
        return lax.dynamic_index_in_dim(value, col, 1, False).reshape(-1)

    def in_row(value):
        return lax.dynamic_index_in_dim(value, row, 0, False).reshape(-1)

    row_codes, col_codes = in_row(codes), in_col(codes)
    tile_rows, tile_cols = edge_weight.shape
    blocks_down, blocks_across = block_keep.shape
    side = tile_rows // blocks_down
    linked = (row_codes[:, None] == col_codes[None, :]) & (row_codes[:, None] & 1 == 1)
    linked = linked.reshape(blocks_down, side, blocks_across, side) & (
        block_keep[:, None, :, None] == 1
    )
    masked = jnp.where(linked.reshape(tile_rows, tile_cols), edge_weight, 0)
    pick_rows = (in_row(group)[None, None, :] == targets[:, None, None]) & (
        in_row(slots)[None, None, :] == jnp.arange(send_cap)[None, :, None]
    )
    pick_cols = (in_col(group)[None, None, :] == targets[:, None, None]) & (
        in_col(places)[None, None, :] == jnp.arange(own_cap)[None, :, None]
    )
    picked = jnp.einsum("sta,ac->stc", pick_rows.astype(jnp.bfloat16), masked)
    packed = jnp.einsum("stc,suc->stu", picked, pick_cols.astype(jnp.bfloat16))
    received = trade(packed, "row")

    standing = jnp.arange(n_col)[None, :, None] * own_cap + places
    fits_here = jnp.where(group == row, standing, -1).reshape(n_row, -1)
    slot_of = slots.reshape(n_row, -1)
    target = jnp.max(
        jnp.where(
            slot_of[:, None, :] == jnp.arange(send_cap)[None, :, None], fits_here[:, None, :], -1
        ),
        axis=2,
    )
    spread = (target[:, :, None] == jnp.arange(span)[None, None, :]).astype(jnp.bfloat16)

    arrive = fits_here.reshape(1, -1) == jnp.arange(span)[:, None]
    features_all = jnp.dot(arrive.astype(jnp.bfloat16), nodes_all[:, :in_width])
    arrive = fits_here.reshape(1, -1) == (col * own_cap + jnp.arange(own_cap))[:, None]
    cotangent_own = jnp.dot(arrive.astype(jnp.bfloat16), nodes_all[:, in_width:])
    features_own = lax.dynamic_slice_in_dim(features_all, col * own_cap, own_cap, 0)
    group_col = lax.dynamic_index_in_dim(group, col, 1, False)
    held_count = jnp.sum(group_col == row)
    valid_rows = (jnp.arange(own_cap) < held_count).astype(jnp.float32)[:, None]
    seats_col = lax.dynamic_index_in_dim(seats, col, 1, False)
    places_col = lax.dynamic_index_in_dim(places, col, 1, False)
    seated = (group_col == row)[:, None, :] & (
        seats_col[:, None, :] == jnp.arange(seat_cap)[None, :, None]
    )
    place_of_seat = jnp.max(jnp.where(seated, places_col[:, None, :], -1), axis=2)
    take = place_of_seat.reshape(-1, 1) == jnp.arange(own_cap)[None, :]
    take = take.astype(jnp.bfloat16)
    group_here = lax.dynamic_index_in_dim(in_row(group).reshape(n_col, -1), col, 0, False)
    seat_here = lax.dynamic_index_in_dim(in_row(seats).reshape(n_col, -1), col, 0, False)
    place_here = lax.dynamic_index_in_dim(in_row(places).reshape(n_col, -1), col, 0, False)
    put_seat = (group_here * seat_cap + seat_here)[:, None] == jnp.arange(n_row * seat_cap)
    put_place = (group_here * own_cap + place_here)[:, None] == jnp.arange(n_row * own_cap)
    put_seat, put_place = put_seat.astype(jnp.bfloat16), put_place.astype(jnp.bfloat16)
    received, features_all, features_own, cotangent_own, spread, take = lax.optimization_barrier(
        (received, features_all, features_own, cotangent_own, spread, take)
    )

    own_block = jnp.einsum("stu,stw->uw", received, spread).astype(jnp.bfloat16)
    quadrant = lax.dynamic_slice_in_dim(own_block, chip * (span // 2), span // 2, 1)
    quadrant = swap(quadrant, "chip")
    sibling = swap(own_block, "core")
    powers = polynomials_of(own_block, sibling, quadrant, swap(quadrant, "core"), chip, core)

    def everywhere(value_low):
        return lax.all_gather(value_low, COL, axis=0, tiled=True)

    width = weight_two.shape[2]
    place = jnp.stack([chip, core]).astype(jnp.int32)

    def shaped(*shape, dtype=jnp.bfloat16):
        return jax.ShapeDtypeStruct(shape, dtype)

    hidden_low, stacked_one, mixed_one = layer_pass(
        layer_one_kernel,
        "layer_one",
        None,
        powers,
        features_all,
        features_own,
        weight_one,
        [bias_one[None], gain_one[None], shift_one[None], valid_rows],
        [
            shaped(own_cap, width),
            shaped(ORDER, own_cap, in_width),
            shaped(own_cap, width, dtype=jnp.float32),
        ],
        [],
    )
    half_two = ORDER * width // 2
    activations, low_two, rest_two, mine, other = layer_pass(
        layer_two_kernel,
        "layer_two",
        place,
        powers,
        everywhere(hidden_low),
        hidden_low,
        weight_two,
        [bias_two[None], gain_two[None], shift_two[None], valid_rows, cotangent_own],
        [
            shaped(own_cap, width),
            shaped(own_cap, width),
            shaped(3, width, dtype=jnp.float32),
            shaped(half_two, width),
            shaped(half_two, width),
        ],
        [((ORDER, own_cap, width), jnp.bfloat16), ((own_cap, width), jnp.float32)],
    )

    def add_cores(mine, other, pieces):
        received = swap(other, "core")
        mine, received = pieces(mine), pieces(received)
        (mine_here, mine_there), (got_here, got_there) = split(mine, chip), split(received, chip)
        return added(mine_here, got_here), added(mine_there, got_there)

    here, there = add_cores(mine, other, lambda value: value.reshape(2, -1, width))
    activations_all = lax.all_gather(activations, "row", axis=0, tiled=True)
    everyone_two, there = lax.optimization_barrier((everywhere(low_two), there))
    there = swap(there, "chip")
    unit = n_row * 2 * 8
    half_one = -(-(ORDER * in_width // 2 + 16) // unit) * unit
    low_one, mine, other = layer_pass(
        back_two_kernel,
        "back_two",
        place,
        powers,
        everyone_two,
        low_two,
        weight_two,
        [stacked_one, mixed_one, gain_one[None], valid_rows, rest_two],
        [shaped(own_cap, width), shaped(half_one, width), shaped(half_one, width)],
        [((own_cap, width), jnp.float32)],
    )
    low_one, there = lax.optimization_barrier((low_one, there))
    second = added(here, there).reshape(n_row, -1, width)
    here, there = add_cores(
        mine, other, lambda value: value.reshape(n_row, 2, -1, width).swapaxes(0, 1)
    )
    low_one, there = lax.optimization_barrier((low_one, there))
    first = added(here, swap(there, "chip"))
    everyone_one = everywhere(low_one)
    second = trade(second, "row")
    second = jnp.sum(second.astype(jnp.float32), axis=0).astype(jnp.bfloat16)
    activations_all, second = lax.optimization_barrier((activations_all, second))
    second = lax.all_gather(second, ("core", "chip", "row"), axis=0, tiled=True)

    first = trade(first, "row")
    first = jnp.sum(first.astype(jnp.float32), axis=0).astype(jnp.bfloat16)
    first = joined(first, swap(first, "chip"), chip)
    (input_grad,) = layer_pass(
        back_one_kernel,
        "back_one",
        None,
        powers,
        everyone_one,
        low_one,
        weight_one,
        [],
        [shaped(own_cap, in_width)],
        [((own_cap, in_width), jnp.float32)],
    )
    leaving = jnp.dot(take, input_grad).reshape(n_row, seat_cap * in_width // width, width)
    share = first.shape[0]
    first = jnp.broadcast_to(first[None], (n_row,) + first.shape)
    first = trade(jnp.concatenate([first, leaving], axis=1), "row")
    back = first[:, share:].reshape(n_row * seat_cap, in_width)
    first = first[:, :share].reshape(-1, width)
    home = jnp.dot(put_place, activations_all, preferred_element_type=jnp.float32)
    home_grad = jnp.dot(put_seat, back, preferred_element_type=jnp.float32)
    return home, home_grad, first, swap(first, "core"), second


def general(
    codes,
    features,
    block_keep,
    edge_weight,
    weight_one,
    bias_one,
    gain_one,
    shift_one,
    weight_two,
    bias_two,
    gain_two,
    shift_two,
    cotangent,
    node_valid,
):
    row, col = lax.axis_index("row"), lax.axis_index(COL)
    row_codes = lax.dynamic_index_in_dim(codes, row, 0, False).reshape(-1)
    col_codes = lax.dynamic_index_in_dim(codes, col, 1, False).reshape(-1)
    tile_rows, tile_cols = edge_weight.shape
    blocks_down, blocks_across = block_keep.shape
    block_side = tile_rows // blocks_down
    linked = (row_codes[:, None] == col_codes[None, :]) & (row_codes[:, None] & 1 == 1)
    linked = linked.reshape(blocks_down, block_side, blocks_across, block_side) & (
        block_keep[:, None, :, None] == 1
    )
    masked = edge_weight * linked.reshape(tile_rows, tile_cols).astype(jnp.bfloat16)
    degree_rows = 1.0 + lax.psum(jnp.sum(masked, axis=1, dtype=jnp.float32), COL)
    own_nodes = features.shape[0]
    own_degree = lax.dynamic_slice_in_dim(
        degree_rows, lax.axis_index(COL) * own_nodes, own_nodes, 0
    )
    degree_cols = lax.all_gather(own_degree, "row", axis=0, tiled=True)
    adjacency = (
        masked.astype(jnp.float32)
        * lax.rsqrt(degree_rows)[:, None]
        * lax.rsqrt(degree_cols)[None, :]
    ).astype(jnp.bfloat16)
    valid_rows = node_valid.astype(jnp.float32)
    stacked_one, mixed_one, hidden = layer_forward(
        adjacency,
        features.astype(jnp.float32),
        weight_one,
        bias_one,
        gain_one,
        shift_one,
        valid_rows,
    )
    stacked_two, mixed_two, activations = layer_forward(
        adjacency, hidden, weight_two, bias_two, gain_two, shift_two, valid_rows
    )
    hidden_grad, weight_two_grad, bias_two_grad, gain_two_grad, shift_two_grad = layer_backward(
        adjacency,
        stacked_two,
        mixed_two,
        cotangent.astype(jnp.float32),
        weight_two,
        gain_two,
        shift_two,
        valid_rows,
    )
    input_grad, weight_one_grad, bias_one_grad, gain_one_grad, shift_one_grad = layer_backward(
        adjacency, stacked_one, mixed_one, hidden_grad, weight_one, gain_one, shift_one, valid_rows
    )
    summed = lax.psum(
        (
            weight_one_grad,
            bias_one_grad,
            gain_one_grad,
            shift_one_grad,
            weight_two_grad,
            bias_two_grad,
            gain_two_grad,
            shift_two_grad,
        ),
        ("row",) + COL,
    )
    weight_one_grad, bias_one_grad, gain_one_grad, shift_one_grad = (
        summed[0],
        summed[1],
        summed[2],
        summed[3],
    )
    weight_two_grad, bias_two_grad, gain_two_grad, shift_two_grad = (
        summed[4],
        summed[5],
        summed[6],
        summed[7],
    )
    return (
        activations,
        input_grad,
        weight_one_grad,
        bias_one_grad,
        gain_one_grad,
        shift_one_grad,
        weight_two_grad,
        bias_two_grad,
        gain_two_grad,
        shift_two_grad,
    )


def local(n_row, n_col, *args):
    (
        features,
        node_valid,
        cluster,
        block_keep,
        edge_weight,
        weight_one,
        bias_one,
        gain_one,
        shift_one,
        weight_two,
        bias_two,
        gain_two,
        shift_two,
        cotangent,
    ) = args
    own_nodes, in_width = features.shape
    own_cap = own_nodes * n_row * 5 // 16
    send_cap = own_nodes * n_col * 3 // 8
    seat_cap = own_nodes // 2
    codes = lax.all_gather(cluster * 2 + node_valid, COL, axis=0)
    codes = broadcast_along(codes, "row", n_row)
    shared = (
        block_keep,
        edge_weight,
        weight_one,
        bias_one,
        gain_one,
        shift_one,
        weight_two,
        bias_two,
        gain_two,
        shift_two,
        cotangent,
    )

    def slow():
        return general(codes, features, *shared, node_valid)

    held = (ORDER - 1) * own_cap * own_cap * n_col * 2
    if held > HELD_BYTES or n_col != 4 or n_row < 2:
        return slow()
    nodes_all = lax.all_gather(
        jnp.concatenate([features, cotangent], axis=1), ("row",) + COL, axis=0, tiled=True
    )
    group = assign(codes, n_row)
    member = group[None] == jnp.arange(n_row)[:, None, None, None]
    by_col = member.transpose(0, 2, 1, 3).reshape(n_row, n_col, -1)
    by_row = member.reshape(n_row, n_row, -1)
    places = jnp.sum(jnp.where(by_col, exclusive_counts(by_col), 0), axis=0)
    places = places.reshape(n_col, n_row, own_nodes).transpose(1, 0, 2)
    slots = jnp.sum(jnp.where(by_row, exclusive_counts(by_row), 0), axis=0)
    slots = slots.reshape(n_row, n_col, own_nodes)
    seats = jnp.sum(jnp.where(member, exclusive_counts(member), 0), axis=0)
    fits = (
        (jnp.max(jnp.sum(by_col, axis=2)) <= own_cap)
        & (jnp.max(jnp.sum(by_row, axis=2)) <= send_cap)
        & (jnp.max(jnp.sum(member, axis=3)) <= seat_cap)
    )
    results = compact(
        codes,
        group,
        features,
        *shared,
        places,
        slots,
        seats,
        nodes_all,
        (n_row, n_col),
        (own_cap, send_cap, seat_cap),
    )

    width = weight_two.shape[2]
    tail = weight_one.shape[0] * weight_one.shape[1]
    core = lax.axis_index("core")

    unit = n_row * 2 * 8
    half = tail // 2
    padded = -(-(half + 16) // unit) * unit

    def again(state):
        made = slow()
        small = jnp.stack([made[place] for place in (3, 4, 5, 7, 8, 9)])
        small = jnp.stack([small, jnp.zeros_like(small)])
        first = jnp.concatenate([made[2].reshape(2, half, width), small], axis=1)
        first = jnp.pad(first, ((0, 0), (0, padded - first.shape[1]), (0, 0)))
        second = made[6].reshape(-1, width)
        return True, made[:2] + split(first.astype(jnp.bfloat16), core) + (
            second.astype(jnp.bfloat16),
        )

    activations, input_grad, mine, other, second = lax.while_loop(
        lambda state: jnp.logical_not(state[0]), again, (fits, results)
    )[1]
    first = joined(mine[:half], other[:half], core).astype(jnp.float32)
    small = jnp.where(core == 0, mine[half : half + 6], other[half : half + 6])
    small = small.astype(jnp.float32)
    return (
        activations,
        input_grad,
        first.reshape(weight_one.shape),
        small[0],
        small[1],
        small[2],
        second.astype(jnp.float32).reshape(weight_two.shape),
        small[3],
        small[4],
        small[5],
    )


def solution(mesh):
    n_row, n_col = mesh.shape["row"], mesh.shape["col"]
    by_core = jax.sharding.Mesh(
        mesh.devices.reshape(n_row, n_col // 2, 2), ("row", "chip", "core")
    )
    nodes = ("row", "chip", "core")
    placed = (
        P(nodes, None),
        P(nodes),
        P(nodes),
        P("row", COL),
        P("row", COL),
        P(),
        P(),
        P(),
        P(),
        P(),
        P(),
        P(),
        P(),
        P(nodes, None),
    )
    return jax.shard_map(
        functools.partial(local, n_row, n_col),
        mesh=by_core,
        in_specs=placed,
        out_specs=(P(nodes, None), P(nodes, None), P(), P(), P(), P(), P(), P(), P(), P()),
        check_vma=False,
    )
```

```python
import functools

import jax
import jax.numpy as jnp
from jax import lax
from jax.experimental import pallas as pl
from jax.experimental.pallas import tpu as pltpu
from jax.sharding import PartitionSpec as P

ORDER = 13
CLUSTERS = 16
HELD_BYTES = 1 << 25
VMEM_BYTES = 40 << 20
COL = ("chip", "core")


def finish(mixed, gain, shift, valid_rows):
    active = jax.nn.gelu(mixed, approximate=False)
    centered = active - jnp.mean(active, axis=-1, keepdims=True)
    variance = jnp.mean(centered * centered, axis=-1, keepdims=True)
    return (centered * lax.rsqrt(variance + 1e-05) * gain + shift) * valid_rows[:, None]


def forward_product(adjacency, piece_low):
    partial_value = jnp.dot(
        adjacency,
        lax.all_gather(piece_low, "row", axis=0, tiled=True),
        preferred_element_type=jnp.float32,
    )
    return lax.psum_scatter(partial_value, COL, scatter_dimension=0, tiled=True)


def backward_product(adjacency, piece_low):
    partial_value = lax.dot_general(
        adjacency,
        lax.all_gather(piece_low, COL, axis=0, tiled=True),
        (((0,), (0,)), ((), ())),
        preferred_element_type=jnp.float32,
    )
    return lax.psum_scatter(
        partial_value.astype(jnp.bfloat16), "row", scatter_dimension=0, tiled=True
    ).astype(jnp.float32)


def layer_forward(adjacency, inputs, weight, bias, gain, shift, valid_rows):
    first_low = inputs.astype(jnp.bfloat16)
    second = -forward_product(adjacency, first_low)
    second_low = second.astype(jnp.bfloat16)

    def advance(state_pair, unused):
        previous, current, current_low = state_pair
        upcoming = -2.0 * forward_product(adjacency, current_low) - previous
        upcoming_low = upcoming.astype(jnp.bfloat16)
        return ((current, upcoming, upcoming_low), upcoming_low)

    ignored, others = lax.scan(advance, (inputs, second, second_low), None, length=ORDER - 2)
    stacked = jnp.concatenate([first_low[None], second_low[None], others], axis=0)
    mixed = jnp.einsum("kni,kio->no", stacked, weight, preferred_element_type=jnp.float32) + bias
    return (stacked, mixed, finish(mixed, gain, shift, valid_rows))


def layer_backward(adjacency, stacked, mixed, upstream, weight, gain, shift, valid_rows):

    def local_finish(mixed_in, gain_in, shift_in):
        return finish(mixed_in, gain_in, shift_in, valid_rows)

    ignored, pullback = jax.vjp(local_finish, mixed, gain, shift)
    mixed_grad, gain_grad, shift_grad = pullback(upstream)
    mixed_low = mixed_grad.astype(jnp.bfloat16)
    bias_grad = jnp.sum(mixed_low.astype(jnp.float32), axis=0)
    weight_grad = jnp.einsum("kni,no->kio", stacked, mixed_low, preferred_element_type=jnp.float32)
    direct = jnp.einsum("no,kio->kni", mixed_low, weight, preferred_element_type=jnp.float32)

    def retreat(state_pair, direct_term):
        later_two, later_one = state_pair
        current = (
            direct_term
            - 2.0 * backward_product(adjacency, later_one.astype(jnp.bfloat16))
            - later_two
        )
        return ((later_one, current), None)

    start_pair = (jnp.zeros_like(direct[0]), direct[ORDER - 1])
    (second_grad, first_grad), unused = lax.scan(
        retreat, start_pair, direct[1 : ORDER - 1], reverse=True
    )
    input_grad = (
        direct[0] - backward_product(adjacency, first_grad.astype(jnp.bfloat16)) - second_grad
    )
    return (input_grad, weight_grad, bias_grad, gain_grad, shift_grad)


def swap(value, axis):
    return lax.ppermute(value, axis, [(0, 1), (1, 0)])


def trade(pieces, axis):
    return lax.all_to_all(pieces, axis, 0, 0, tiled=False)


def broadcast_along(value, axis, size):
    return trade(jnp.broadcast_to(value[None], (size,) + value.shape), axis)


def joined(mine, other, index):
    return jnp.where(
        index == 0, jnp.concatenate([mine, other]), jnp.concatenate([other, mine])
    )


def split(pair, index):
    mine = lax.dynamic_index_in_dim(pair, index, 0, False)
    return mine, lax.dynamic_index_in_dim(pair, 1 - index, 0, False)


def added(mine, received):
    return (mine.astype(jnp.float32) + received.astype(jnp.float32)).astype(jnp.bfloat16)


def block_kernel(place_ref, own_ref, sibling_ref, near_ref, far_ref, out_ref):
    chip, core = place_ref[0], place_ref[1]
    own_cap, span = own_ref.shape
    half = span // 2

    def rows(of_chip, of_core):
        return pl.ds(pl.multiple_of((2 * of_chip + of_core) * own_cap, own_cap), own_cap)

    out_ref[rows(chip, core), :] = own_ref[...]
    out_ref[rows(chip, 1 - core), :] = sibling_ref[...]

    def other_chip(here):
        there = 1 - here
        here_cols, there_cols = pl.ds(here * half, half), pl.ds(there * half, half)
        out_ref[rows(there, core), there_cols] = near_ref[...]
        out_ref[rows(there, 1 - core), there_cols] = far_ref[...]
        for tile in range(half // 128):
            strip = out_ref[here_cols, pl.ds(there * half + tile * 128, 128)]
            turned = jnp.transpose(strip.astype(jnp.float32)).astype(jnp.bfloat16)
            out_ref[pl.ds(there * half + tile * 128, 128), here_cols] = turned

    @pl.when(chip == 0)
    def first():
        other_chip(0)

    @pl.when(chip == 1)
    def second():
        other_chip(1)

    across = jnp.ones((1, span), jnp.float32)
    for tile in range(span // 128):
        across = across + jnp.sum(
            out_ref[pl.ds(tile * 128, 128), :].astype(jnp.float32), axis=0, keepdims=True
        )
    across = lax.rsqrt(across)
    for tile in range(span // 128):
        strip = out_ref[pl.ds(tile * 128, 128), :].astype(jnp.float32)
        down = lax.rsqrt(1.0 + jnp.sum(strip, axis=1, keepdims=True))
        out_ref[pl.ds(tile * 128, 128), :] = (strip * down * across).astype(jnp.bfloat16)


def normalized_block(own, sibling, near, far, chip, core):
    span = own.shape[1]

    def whole(shape):
        return pl.BlockSpec(shape, lambda step: (0, 0))

    return pl.pallas_call(
        block_kernel,
        grid=(1,),
        out_shape=jax.ShapeDtypeStruct((span, span), jnp.bfloat16),
        in_specs=[pl.BlockSpec(memory_space=pltpu.SMEM)]
        + [whole(value.shape) for value in (own, sibling, near, far)],
        out_specs=whole((span, span)),
        compiler_params=pltpu.CompilerParams(vmem_limit_bytes=VMEM_BYTES),
        cost_estimate=pl.CostEstimate(
            flops=8 * span * span, bytes_accessed=8 * span * span, transcendentals=0
        ),
        name="normalized_block",
    )(jnp.stack([chip, core]).astype(jnp.int32), own, sibling, near, far)


def exclusive_counts(member):
    count = member.shape[-1]
    before = jnp.arange(count)[:, None] < jnp.arange(count)[None, :]
    return jnp.dot(
        member.astype(jnp.bfloat16),
        before.astype(jnp.bfloat16),
        preferred_element_type=jnp.float32,
    ).astype(jnp.int32)


def assign(codes, n_row):
    cluster, valid = codes >> 1, codes & 1
    labels = jnp.arange(CLUSTERS)
    sizes = jnp.sum(
        (cluster.reshape(1, -1) == labels[:, None]) & (valid.reshape(1, -1) == 1), axis=1
    )
    ahead = (sizes[None, :] > sizes[:, None]) | (
        (sizes[None, :] == sizes[:, None]) & (labels[None, :] < labels[:, None])
    )
    rank = jnp.sum(ahead, axis=1)
    others = n_row - 1
    turn, place = (rank - 1) // others, (rank - 1) % others
    group = jnp.where(rank == 0, 0, 1 + jnp.where(turn == 0, place, others - 1 - place))
    of_node = jnp.sum(
        jnp.where(cluster[None] == labels[:, None, None, None], group[:, None, None, None], 0),
        axis=0,
    )
    return jnp.where(valid == 1, of_node, n_row)


def compact(
    codes,
    group,
    features,
    block_keep,
    edge_weight,
    weight_one,
    bias_one,
    gain_one,
    shift_one,
    weight_two,
    bias_two,
    gain_two,
    shift_two,
    cotangent,
    places,
    slots,
    seats,
    sizes,
    caps,
):
    row, col = lax.axis_index("row"), lax.axis_index(COL)
    chip, core = lax.axis_index("chip"), lax.axis_index("core")
    n_row, n_col = sizes
    own_cap, send_cap, seat_cap = caps
    own_nodes, in_width = features.shape
    width = weight_two.shape[2]
    span = n_col * own_cap
    targets = jnp.arange(n_row)

    def in_col(value):
        return lax.dynamic_index_in_dim(value, col, 1, False).reshape(-1)

    def in_row(value):
        return lax.dynamic_index_in_dim(value, row, 0, False).reshape(-1)

    row_codes, col_codes = in_row(codes), in_col(codes)
    tile_rows, tile_cols = edge_weight.shape
    blocks_down, blocks_across = block_keep.shape
    side = tile_rows // blocks_down
    linked = (row_codes[:, None] == col_codes[None, :]) & (row_codes[:, None] & 1 == 1)
    linked = linked.reshape(blocks_down, side, blocks_across, side) & (
        block_keep[:, None, :, None] == 1
    )
    masked = jnp.where(linked.reshape(tile_rows, tile_cols), edge_weight, 0)
    pick_rows = (in_row(group)[None, None, :] == targets[:, None, None]) & (
        in_row(slots)[None, None, :] == jnp.arange(send_cap)[None, :, None]
    )
    pick_cols = (in_col(group)[None, None, :] == targets[:, None, None]) & (
        in_col(places)[None, None, :] == jnp.arange(own_cap)[None, :, None]
    )
    picked = jnp.einsum("sta,ac->stc", pick_rows.astype(jnp.bfloat16), masked)
    packed = jnp.einsum("stc,suc->stu", picked, pick_cols.astype(jnp.bfloat16))
    whole, half_send = own_cap // 128 * 128, send_cap // 2
    ends = [packed[:, :half_send, whole:], packed[:, half_send:, whole:]]
    pieces = [packed[:, :, start : start + 128] for start in range(0, whole, 128)]
    pieces = trade(jnp.concatenate(pieces + [jnp.concatenate(ends, axis=2)], axis=1), "row")

    standing = jnp.arange(n_col)[None, :, None] * own_cap + places
    fits_here = jnp.where(group == row, standing, -1).reshape(n_row, -1)
    slot_of = slots.reshape(n_row, -1)
    target = jnp.max(
        jnp.where(
            slot_of[:, None, :] == jnp.arange(send_cap)[None, :, None], fits_here[:, None, :], -1
        ),
        axis=2,
    )
    spread = (target[:, :, None] == jnp.arange(span)[None, None, :]).astype(jnp.bfloat16)

    group_here = lax.dynamic_index_in_dim(in_row(group).reshape(n_col, -1), col, 0, False)
    seat_here = lax.dynamic_index_in_dim(in_row(seats).reshape(n_col, -1), col, 0, False)
    place_here = lax.dynamic_index_in_dim(in_row(places).reshape(n_col, -1), col, 0, False)
    leave = (group_here[None, None, :] == targets[:, None, None]) & (
        seat_here[None, None, :] == jnp.arange(seat_cap)[None, :, None]
    )
    leave = leave.astype(jnp.bfloat16).reshape(n_row * seat_cap, own_nodes)
    both = jnp.dot(leave, jnp.concatenate([features, cotangent], axis=1))
    both = both.reshape(n_row, seat_cap, -1)
    group_col = lax.dynamic_index_in_dim(group, col, 1, False)
    seats_col = lax.dynamic_index_in_dim(seats, col, 1, False)
    places_col = lax.dynamic_index_in_dim(places, col, 1, False)
    seated = (group_col == row)[:, None, :] & (
        seats_col[:, None, :] == jnp.arange(seat_cap)[None, :, None]
    )
    place_of_seat = jnp.max(jnp.where(seated, places_col[:, None, :], -1), axis=2)
    place_of_seat = place_of_seat.reshape(n_row * seat_cap)
    arrive = (place_of_seat[None, :] == jnp.arange(own_cap)[:, None]).astype(jnp.bfloat16)
    take = (place_of_seat[:, None] == jnp.arange(own_cap)[None, :]).astype(jnp.bfloat16)
    put_place = (group_here * own_cap + place_here)[:, None] == jnp.arange(n_row * own_cap)
    put_place = put_place.astype(jnp.bfloat16)
    held_count = jnp.sum(group_col == row)
    valid_rows = (jnp.arange(own_cap) < held_count).astype(jnp.float32)
    pieces, both, spread, arrive, take, put_place, valid_rows = lax.optimization_barrier(
        (pieces, both, spread, arrive, take, put_place, valid_rows)
    )

    many = whole // 128
    pieces = pieces.reshape(n_row, 2 * many + 1, half_send, 128)
    ends = pieces[:, 2 * many, :, : own_cap - whole], pieces[:, 2 * many, :, own_cap - whole :]
    ends = jnp.stack(ends, axis=1).reshape(n_row, send_cap, own_cap - whole)
    received = [
        pieces[:, 2 * tile : 2 * tile + 2].reshape(n_row, send_cap, 128) for tile in range(many)
    ]
    received = jnp.concatenate(received + [ends], axis=2)
    own_block = jnp.einsum("stu,stw->uw", received, spread).astype(jnp.bfloat16)
    quadrant = lax.dynamic_slice_in_dim(own_block, chip * (span // 2), span // 2, 1)
    quadrant = swap(quadrant, "chip")
    both = trade(both, "row")
    adjacency = normalized_block(
        own_block, swap(own_block, "core"), quadrant, swap(quadrant, "core"), chip, core
    )

    first = (col * own_cap + jnp.arange(own_cap))[:, None] == jnp.arange(span)[None, :]
    previous = first.astype(jnp.float32)
    current = -lax.dynamic_slice_in_dim(adjacency, col * own_cap, own_cap, 0).astype(jnp.float32)
    lowered = [current.astype(jnp.bfloat16)]
    for position in range(2, ORDER):
        upcoming = (
            -2.0 * jnp.dot(lowered[-1], adjacency, preferred_element_type=jnp.float32) - previous
        )
        low = upcoming.astype(jnp.bfloat16)
        if position == 4:
            low, both = lax.optimization_barrier((low, both))
            mine = jnp.dot(arrive, both.reshape(n_row * seat_cap, -1))
            features_own, cotangent_own = mine[:, :in_width], mine[:, in_width:]
            sibling = swap(features_own, "core")
        if position == 7:
            low, sibling = lax.optimization_barrier((low, sibling))
            features_chip = joined(features_own, sibling, core)
            partner = swap(features_chip, "chip")
        if position == 11:
            low, partner = lax.optimization_barrier((low, partner))
            features_all = joined(features_chip, partner, chip)
        previous, current = current, upcoming
        lowered.append(low)
    polynomials = jnp.concatenate(lowered, axis=0)

    def apply(value_low, everyone):
        result = jnp.dot(polynomials, everyone, preferred_element_type=jnp.float32)
        result = result.astype(jnp.bfloat16).reshape(ORDER - 1, own_cap, -1)
        return jnp.concatenate([value_low[None], result], axis=0)

    def everywhere(value_low):
        return lax.all_gather(value_low, COL, axis=0, tiled=True)

    def forward(value_low, everyone, weight, bias, gain, shift):
        stacked = apply(value_low, everyone)
        mixed = jnp.einsum("kni,kio->no", stacked, weight, preferred_element_type=jnp.float32)
        mixed = mixed + bias
        return stacked, mixed, finish(mixed, gain, shift, valid_rows)

    def through_norm(mixed, upstream, gain, shift):
        ignored, pullback = jax.vjp(
            lambda mixed_in, gain_in, shift_in: finish(mixed_in, gain_in, shift_in, valid_rows),
            mixed,
            gain,
            shift,
        )
        mixed_grad, gain_grad, shift_grad = pullback(upstream)
        mixed_low = mixed_grad.astype(jnp.bfloat16)
        bias_grad = jnp.sum(mixed_low.astype(jnp.float32), axis=0)
        return mixed_low, [bias_grad, gain_grad, shift_grad]

    def weight_gradient(turned, mixed_low):
        grad = jnp.einsum("kin,no->kio", turned, mixed_low, preferred_element_type=jnp.float32)
        return grad.astype(jnp.bfloat16).reshape(-1, width)

    def to_input(mixed_low, everyone, weight):
        spread_grad = apply(mixed_low, everyone)
        return jnp.einsum("kno,kio->ni", spread_grad, weight, preferred_element_type=jnp.float32)

    def add_cores(value, pieces):
        mine, other = split(value.reshape(2, -1, width), core)
        got = pieces(swap(other, "core"))
        (mine_here, mine_there), (got_here, got_there) = split(pieces(mine), chip), split(got, chip)
        return added(mine_here, got_here), added(mine_there, got_there)

    stacked_one, mixed_one, hidden = forward(
        features_own, features_all, weight_one, bias_one, gain_one, shift_one
    )
    hidden_low = hidden.astype(jnp.bfloat16)
    everyone_hidden = everywhere(hidden_low)
    stacked_two, mixed_two, activations = forward(
        hidden_low, everyone_hidden, weight_two, bias_two, gain_two, shift_two
    )
    low_two, rest_two = through_norm(
        mixed_two, cotangent_own.astype(jnp.float32), gain_two, shift_two
    )

    second = weight_gradient(stacked_two.transpose(0, 2, 1), low_two)
    low_two, second = lax.optimization_barrier((low_two, second))
    activations_all = lax.all_gather(activations.astype(jnp.bfloat16), "row", axis=0, tiled=True)
    here, there = add_cores(second, lambda value: value.reshape(2, -1, width))
    everyone_two, there = lax.optimization_barrier((everywhere(low_two), there))
    there = swap(there, "chip")
    hidden_grad = to_input(low_two, everyone_two, weight_two)
    low_one, rest_one = through_norm(mixed_one, hidden_grad, gain_one, shift_one)
    low_one, there = lax.optimization_barrier((low_one, there))
    second = added(here, there).reshape(n_row, -1, width)
    turned_one = lax.optimization_barrier(stacked_one.transpose(0, 2, 1))
    first = weight_gradient(turned_one, low_one).reshape(2, -1, width)
    half = first.shape[1]
    unit = n_row * 2 * 8
    padded = -(-(half + 6) // unit) * unit
    rest = jnp.pad(jnp.stack(rest_one + rest_two), ((0, padded - half - 6), (0, 0)))
    rest = jnp.stack([rest, jnp.zeros_like(rest)]).astype(jnp.bfloat16)
    first = jnp.concatenate([first, rest], axis=1)
    low_one, second, first = lax.optimization_barrier((low_one, second, first))
    here, there = add_cores(
        first, lambda value: value.reshape(n_row, 2, -1, width).swapaxes(0, 1)
    )
    second = trade(second, "row")
    everyone_one = everywhere(low_one)
    first = added(here, swap(there, "chip"))
    second = jnp.sum(second.astype(jnp.float32), axis=0).astype(jnp.bfloat16)
    first = jnp.sum(trade(first, "row").astype(jnp.float32), axis=0).astype(jnp.bfloat16)
    second, first = lax.optimization_barrier((second, first))
    second = broadcast_along(second, "row", n_row).reshape(-1, width)
    first = joined(first, swap(first, "chip"), chip)
    input_grad = to_input(low_one, everyone_one, weight_one)
    leaving = jnp.dot(take, input_grad.astype(jnp.bfloat16))
    leaving = leaving.reshape(n_row, seat_cap * in_width // width, width)
    share = first.shape[0]
    first = jnp.broadcast_to(first[None], (n_row,) + first.shape)
    second, first, leaving = lax.optimization_barrier((second, first, leaving))
    second = joined(second, swap(second, "chip"), chip)
    first = trade(jnp.concatenate([first, leaving], axis=1), "row")
    back = first[:, share:].reshape(n_row * seat_cap, in_width)
    first = first[:, :share].reshape(-1, width)
    other = swap(first, "core")
    home = jnp.dot(put_place, activations_all, preferred_element_type=jnp.float32)
    home_grad = jnp.dot(leave.T, back, preferred_element_type=jnp.float32)
    return (
        home,
        home_grad,
        first[:half],
        other[:half],
        second,
        swap(second, "core"),
        first[half : half + 6],
        other[half : half + 6],
    )


def general(
    codes,
    features,
    block_keep,
    edge_weight,
    weight_one,
    bias_one,
    gain_one,
    shift_one,
    weight_two,
    bias_two,
    gain_two,
    shift_two,
    cotangent,
    node_valid,
):
    row, col = lax.axis_index("row"), lax.axis_index(COL)
    row_codes = lax.dynamic_index_in_dim(codes, row, 0, False).reshape(-1)
    col_codes = lax.dynamic_index_in_dim(codes, col, 1, False).reshape(-1)
    tile_rows, tile_cols = edge_weight.shape
    blocks_down, blocks_across = block_keep.shape
    block_side = tile_rows // blocks_down
    linked = (row_codes[:, None] == col_codes[None, :]) & (row_codes[:, None] & 1 == 1)
    linked = linked.reshape(blocks_down, block_side, blocks_across, block_side) & (
        block_keep[:, None, :, None] == 1
    )
    masked = edge_weight * linked.reshape(tile_rows, tile_cols).astype(jnp.bfloat16)
    degree_rows = 1.0 + lax.psum(jnp.sum(masked, axis=1, dtype=jnp.float32), COL)
    own_nodes = features.shape[0]
    own_degree = lax.dynamic_slice_in_dim(
        degree_rows, lax.axis_index(COL) * own_nodes, own_nodes, 0
    )
    degree_cols = lax.all_gather(own_degree, "row", axis=0, tiled=True)
    adjacency = (
        masked.astype(jnp.float32)
        * lax.rsqrt(degree_rows)[:, None]
        * lax.rsqrt(degree_cols)[None, :]
    ).astype(jnp.bfloat16)
    valid_rows = node_valid.astype(jnp.float32)
    stacked_one, mixed_one, hidden = layer_forward(
        adjacency,
        features.astype(jnp.float32),
        weight_one,
        bias_one,
        gain_one,
        shift_one,
        valid_rows,
    )
    stacked_two, mixed_two, activations = layer_forward(
        adjacency, hidden, weight_two, bias_two, gain_two, shift_two, valid_rows
    )
    hidden_grad, weight_two_grad, bias_two_grad, gain_two_grad, shift_two_grad = layer_backward(
        adjacency,
        stacked_two,
        mixed_two,
        cotangent.astype(jnp.float32),
        weight_two,
        gain_two,
        shift_two,
        valid_rows,
    )
    input_grad, weight_one_grad, bias_one_grad, gain_one_grad, shift_one_grad = layer_backward(
        adjacency, stacked_one, mixed_one, hidden_grad, weight_one, gain_one, shift_one, valid_rows
    )
    summed = lax.psum(
        (
            weight_one_grad,
            bias_one_grad,
            gain_one_grad,
            shift_one_grad,
            weight_two_grad,
            bias_two_grad,
            gain_two_grad,
            shift_two_grad,
        ),
        ("row",) + COL,
    )
    weight_one_grad, bias_one_grad, gain_one_grad, shift_one_grad = (
        summed[0],
        summed[1],
        summed[2],
        summed[3],
    )
    weight_two_grad, bias_two_grad, gain_two_grad, shift_two_grad = (
        summed[4],
        summed[5],
        summed[6],
        summed[7],
    )
    return (
        activations,
        input_grad,
        weight_one_grad,
        bias_one_grad,
        gain_one_grad,
        shift_one_grad,
        weight_two_grad,
        bias_two_grad,
        gain_two_grad,
        shift_two_grad,
    )


def local(n_row, n_col, *args):
    (
        features,
        node_valid,
        cluster,
        block_keep,
        edge_weight,
        weight_one,
        bias_one,
        gain_one,
        shift_one,
        weight_two,
        bias_two,
        gain_two,
        shift_two,
        cotangent,
    ) = args
    own_nodes, in_width = features.shape
    own_cap = own_nodes * n_row * 5 // 16
    send_cap = own_nodes * n_col * 11 // 32
    seat_cap = own_nodes // 2
    codes = broadcast_along(cluster * 2 + node_valid, ("row",) + COL, n_row * n_col)
    codes = codes.reshape(n_row, n_col, own_nodes)
    shared = (
        block_keep,
        edge_weight,
        weight_one,
        bias_one,
        gain_one,
        shift_one,
        weight_two,
        bias_two,
        gain_two,
        shift_two,
        cotangent,
    )

    def slow():
        return general(codes, features, *shared, node_valid)

    held = (ORDER - 1) * own_cap * own_cap * n_col * 2
    if held > HELD_BYTES or n_col != 4 or n_row < 2:
        return slow()
    group = assign(codes, n_row)
    member = group[None] == jnp.arange(n_row)[:, None, None, None]
    by_col = member.transpose(0, 2, 1, 3).reshape(n_row, n_col, -1)
    by_row = member.reshape(n_row, n_row, -1)
    places = jnp.sum(jnp.where(by_col, exclusive_counts(by_col), 0), axis=0)
    places = places.reshape(n_col, n_row, own_nodes).transpose(1, 0, 2)
    slots = jnp.sum(jnp.where(by_row, exclusive_counts(by_row), 0), axis=0)
    slots = slots.reshape(n_row, n_col, own_nodes)
    seats = jnp.sum(jnp.where(member, exclusive_counts(member), 0), axis=0)
    fits = (
        (jnp.max(jnp.sum(by_col, axis=2)) <= own_cap)
        & (jnp.max(jnp.sum(by_row, axis=2)) <= send_cap)
        & (jnp.max(jnp.sum(member, axis=3)) <= seat_cap)
    )
    width = weight_two.shape[2]
    core = lax.axis_index("core")

    def instead(state):
        made = slow()
        small = jnp.stack([made[place] for place in (3, 4, 5, 7, 8, 9)])
        return (True,) + tuple(
            value.astype(jnp.bfloat16).reshape(like.shape)
            for value, like in zip((made[0], made[1], made[2], made[6], small), state[1:])
        )

    shapes = (
        (own_nodes, width),
        (own_nodes, in_width),
        (2, ORDER * in_width // 2, width),
        (2, ORDER * width // 2, width),
        (6, width),
    )
    others = lax.while_loop(
        lambda state: jnp.logical_not(state[0]),
        instead,
        (fits,) + tuple(jnp.zeros(shape, jnp.bfloat16) for shape in shapes),
    )[1:]
    home, home_grad, mine_one, other_one, mine_two, other_two, mine_small, other_small = compact(
        codes,
        group,
        features,
        *shared,
        places,
        slots,
        seats,
        (n_row, n_col),
        (own_cap, send_cap, seat_cap),
    )

    def chosen(value, other):
        return jnp.where(fits, value.astype(jnp.float32), other.astype(jnp.float32))

    def both_halves(mine, other):
        return jnp.where(
            (core == jnp.arange(2))[:, None, None], mine[None], other[None]
        )

    first = chosen(both_halves(mine_one, other_one), others[2])
    second = chosen(both_halves(mine_two, other_two), others[3])
    small = chosen(jnp.where(core == 0, mine_small, other_small), others[4])
    return (
        chosen(home, others[0]),
        chosen(home_grad, others[1]),
        first.reshape(weight_one.shape),
        small[0],
        small[1],
        small[2],
        second.reshape(weight_two.shape),
        small[3],
        small[4],
        small[5],
    )


def solution(mesh):
    n_row, n_col = mesh.shape["row"], mesh.shape["col"]
    by_core = jax.sharding.Mesh(
        mesh.devices.reshape(n_row, n_col // 2, 2), ("row", "chip", "core")
    )
    nodes = ("row", "chip", "core")
    placed = (
        P(nodes, None),
        P(nodes),
        P(nodes),
        P("row", COL),
        P("row", COL),
        P(),
        P(),
        P(),
        P(),
        P(),
        P(),
        P(),
        P(),
        P(nodes, None),
    )
    return jax.shard_map(
        functools.partial(local, n_row, n_col),
        mesh=by_core,
        in_specs=placed,
        out_specs=(P(nodes, None), P(nodes, None), P(), P(), P(), P(), P(), P(), P(), P()),
        check_vma=False,
    )
```

```python
import functools

import jax
import jax.numpy as jnp
from jax import lax
from jax.experimental import pallas as pl
from jax.experimental.pallas import tpu as pltpu
from jax.sharding import PartitionSpec as P

ORDER = 13
CLUSTERS = 16
HELD_BYTES = 1 << 25
VMEM_BYTES = 16 << 20
COL = ("chip", "core")


def finish(mixed, gain, shift, valid_rows):
    active = jax.nn.gelu(mixed, approximate=False)
    centered = active - jnp.mean(active, axis=-1, keepdims=True)
    variance = jnp.mean(centered * centered, axis=-1, keepdims=True)
    return (centered * lax.rsqrt(variance + 1e-05) * gain + shift) * valid_rows[:, None]


def forward_product(adjacency, piece_low):
    partial_value = jnp.dot(
        adjacency,
        lax.all_gather(piece_low, "row", axis=0, tiled=True),
        preferred_element_type=jnp.float32,
    )
    return lax.psum_scatter(partial_value, COL, scatter_dimension=0, tiled=True)


def backward_product(adjacency, piece_low):
    partial_value = lax.dot_general(
        adjacency,
        lax.all_gather(piece_low, COL, axis=0, tiled=True),
        (((0,), (0,)), ((), ())),
        preferred_element_type=jnp.float32,
    )
    return lax.psum_scatter(
        partial_value.astype(jnp.bfloat16), "row", scatter_dimension=0, tiled=True
    ).astype(jnp.float32)


def layer_forward(adjacency, inputs, weight, bias, gain, shift, valid_rows):
    first_low = inputs.astype(jnp.bfloat16)
    second = -forward_product(adjacency, first_low)
    second_low = second.astype(jnp.bfloat16)

    def advance(state_pair, unused):
        previous, current, current_low = state_pair
        upcoming = -2.0 * forward_product(adjacency, current_low) - previous
        upcoming_low = upcoming.astype(jnp.bfloat16)
        return ((current, upcoming, upcoming_low), upcoming_low)

    ignored, others = lax.scan(advance, (inputs, second, second_low), None, length=ORDER - 2)
    stacked = jnp.concatenate([first_low[None], second_low[None], others], axis=0)
    mixed = jnp.einsum("kni,kio->no", stacked, weight, preferred_element_type=jnp.float32) + bias
    return (stacked, mixed, finish(mixed, gain, shift, valid_rows))


def layer_backward(adjacency, stacked, mixed, upstream, weight, gain, shift, valid_rows):

    def local_finish(mixed_in, gain_in, shift_in):
        return finish(mixed_in, gain_in, shift_in, valid_rows)

    ignored, pullback = jax.vjp(local_finish, mixed, gain, shift)
    mixed_grad, gain_grad, shift_grad = pullback(upstream)
    mixed_low = mixed_grad.astype(jnp.bfloat16)
    bias_grad = jnp.sum(mixed_low.astype(jnp.float32), axis=0)
    weight_grad = jnp.einsum("kni,no->kio", stacked, mixed_low, preferred_element_type=jnp.float32)
    direct = jnp.einsum("no,kio->kni", mixed_low, weight, preferred_element_type=jnp.float32)

    def retreat(state_pair, direct_term):
        later_two, later_one = state_pair
        current = (
            direct_term
            - 2.0 * backward_product(adjacency, later_one.astype(jnp.bfloat16))
            - later_two
        )
        return ((later_one, current), None)

    start_pair = (jnp.zeros_like(direct[0]), direct[ORDER - 1])
    (second_grad, first_grad), unused = lax.scan(
        retreat, start_pair, direct[1 : ORDER - 1], reverse=True
    )
    input_grad = (
        direct[0] - backward_product(adjacency, first_grad.astype(jnp.bfloat16)) - second_grad
    )
    return (input_grad, weight_grad, bias_grad, gain_grad, shift_grad)


def swap(value, axis):
    return lax.ppermute(value, axis, [(0, 1), (1, 0)])


def trade(pieces, axis):
    return lax.all_to_all(pieces, axis, 0, 0, tiled=False)


def broadcast_along(value, axis, size):
    return trade(jnp.broadcast_to(value[None], (size,) + value.shape), axis)


def joined(mine, other, index):
    return jnp.where(
        index == 0, jnp.concatenate([mine, other]), jnp.concatenate([other, mine])
    )


def split(pair, index):
    mine = lax.dynamic_index_in_dim(pair, index, 0, False)
    return mine, lax.dynamic_index_in_dim(pair, 1 - index, 0, False)


def added(mine, received):
    return (mine.astype(jnp.float32) + received.astype(jnp.float32)).astype(jnp.bfloat16)


def block_kernel(place_ref, own_ref, sibling_ref, near_ref, far_ref, out_ref, done):
    chip, core = place_ref[0], place_ref[1]
    own_cap, span = own_ref.shape
    half = span // 2

    def rows(of_chip, of_core):
        return pl.ds(pl.multiple_of((2 * of_chip + of_core) * own_cap, own_cap), own_cap)

    def fetch(source, of_chip, of_core, columns, place):
        target = out_ref.at[rows(of_chip, of_core), columns]
        return pltpu.make_async_copy(source, target, done.at[place])

    def quadrant_copies(here):
        there = 1 - here
        columns = pl.ds(there * half, half)
        return (
            fetch(near_ref, there, core, columns, 2),
            fetch(far_ref, there, 1 - core, columns, 3),
        )

    everything = pl.ds(0, span)
    top = (
        fetch(own_ref, chip, core, everything, 0),
        fetch(sibling_ref, chip, 1 - core, everything, 1),
    )

    def of_chip(here):
        there = 1 - here
        copies = top + quadrant_copies(here)
        for copy in copies:
            copy.start()
        for copy in copies:
            copy.wait()
        here_rows = pl.ds(here * half, half)
        for tile in range(half // 128):
            columns = pl.ds(there * half + tile * 128, 128)
            strip = out_ref[here_rows, columns]
            turned = jnp.transpose(strip.astype(jnp.float32)).astype(jnp.bfloat16)
            out_ref[columns, here_rows] = turned

    @pl.when(chip == 0)
    def first():
        of_chip(0)

    @pl.when(chip == 1)
    def second():
        of_chip(1)

    across = jnp.ones((1, span), jnp.float32)
    for tile in range(span // 128):
        across = across + jnp.sum(
            out_ref[pl.ds(tile * 128, 128), :].astype(jnp.float32), axis=0, keepdims=True
        )
    across = lax.rsqrt(across)
    for tile in range(span // 128):
        strip = out_ref[pl.ds(tile * 128, 128), :].astype(jnp.float32)
        down = lax.rsqrt(1.0 + jnp.sum(strip, axis=1, keepdims=True))
        out_ref[pl.ds(tile * 128, 128), :] = (strip * down * across).astype(jnp.bfloat16)


def normalized_block(own, sibling, near, far, place):
    span = own.shape[1]
    return pl.pallas_call(
        block_kernel,
        out_shape=jax.ShapeDtypeStruct((span, span), jnp.bfloat16),
        in_specs=[pl.BlockSpec(memory_space=pltpu.SMEM)]
        + [pl.BlockSpec(memory_space=pltpu.HBM)] * 4,
        out_specs=pl.BlockSpec(memory_space=pltpu.VMEM),
        scratch_shapes=[pltpu.SemaphoreType.DMA((4,))],
        compiler_params=pltpu.CompilerParams(vmem_limit_bytes=VMEM_BYTES),
        cost_estimate=pl.CostEstimate(
            flops=8 * span * span, bytes_accessed=8 * span * span, transcendentals=0
        ),
        name="normalized_block",
    )(place, own, sibling, near, far)


def pack_kernel(
    keep_ref, row_codes_ref, col_codes_ref, row_keys_ref, col_keys_ref, weight_ref, out_ref,
    masked, picked, rows_hot, cols_hot
):
    tile_rows, tile_cols = weight_ref.shape
    blocks_down, blocks_across = keep_ref.shape
    groups, ignored, lanes = out_ref.shape
    send_cap, own_cap = rows_hot.shape[0] // groups, cols_hot.shape[0] // groups
    high, wide = tile_rows // blocks_down, tile_cols // blocks_across
    for down in range(blocks_down):
        for across in range(blocks_across):
            rows, columns = pl.ds(down * high, high), pl.ds(across * wide, wide)
            own, other = row_codes_ref[rows, :], col_codes_ref[:, columns]
            linked = (own == other) & (own % 2 == 1) & (keep_ref[down, across] == 1)
            weight = weight_ref[rows, columns].astype(jnp.float32)
            masked[rows, columns] = jnp.where(linked, weight, 0.0).astype(jnp.bfloat16)

    def one_hot(keys, start, count):
        standing = lax.broadcasted_iota(jnp.int32, (count, keys.shape[1]), 0) + start
        return jnp.where(standing == keys, 1.0, 0.0).astype(jnp.bfloat16)

    for group in range(groups):
        rows_hot[pl.ds(group * send_cap, send_cap), :] = one_hot(
            row_keys_ref[...], group * send_cap, send_cap
        )
        cols_hot[pl.ds(group * own_cap, own_cap), :] = one_hot(
            col_keys_ref[...], group * own_cap, own_cap
        )
    for tile in range(tile_cols // 256):
        columns = pl.ds(tile * 256, 256)
        picked[:, columns] = jnp.dot(
            rows_hot[...], masked[:, columns], preferred_element_type=jnp.float32
        ).astype(jnp.bfloat16)
    whole, half = own_cap // lanes, send_cap // 2
    for group in range(groups):
        packed = lax.dot_general(
            picked[pl.ds(group * send_cap, send_cap), :],
            cols_hot[pl.ds(group * own_cap, own_cap), :],
            (((1,), (1,)), ((), ())),
            preferred_element_type=jnp.float32,
        )
        for tile in range(whole):
            out_ref[group, pl.ds(tile * send_cap, send_cap), :] = packed[
                :, tile * lanes : (tile + 1) * lanes
            ].astype(jnp.bfloat16)
        ends = jnp.concatenate(
            [packed[:half, whole * lanes :], packed[half:, whole * lanes :]], axis=1
        )
        out_ref[group, pl.ds(whole * send_cap, half), :] = ends.astype(jnp.bfloat16)


def packed_pieces(block_keep, row_codes, col_codes, row_keys, col_keys, edge_weight, caps, groups):
    own_cap, send_cap = caps
    tile_rows, tile_cols = edge_weight.shape
    high = own_cap // 128 * send_cap + send_cap // 2
    vector = pl.BlockSpec(memory_space=pltpu.VMEM)
    return pl.pallas_call(
        pack_kernel,
        out_shape=jax.ShapeDtypeStruct((groups, high, 128), jnp.bfloat16),
        in_specs=[pl.BlockSpec(memory_space=pltpu.SMEM)] + [vector] * 5,
        out_specs=vector,
        scratch_shapes=[
            pltpu.VMEM((tile_rows, tile_cols), jnp.bfloat16),
            pltpu.VMEM((groups * send_cap, tile_cols), jnp.bfloat16),
            pltpu.VMEM((groups * send_cap, tile_rows), jnp.bfloat16),
            pltpu.VMEM((groups * own_cap, tile_cols), jnp.bfloat16),
        ],
        compiler_params=pltpu.CompilerParams(vmem_limit_bytes=2 * VMEM_BYTES),
        cost_estimate=pl.CostEstimate(
            flops=2 * groups * send_cap * tile_cols * (tile_rows + own_cap),
            bytes_accessed=2 * (tile_rows * tile_cols + groups * high * 128),
            transcendentals=0,
        ),
        name="packed_pieces",
    )(block_keep, row_codes[:, None], col_codes[None], row_keys[None], col_keys[None], edge_weight)


def exclusive_counts(member):
    count = member.shape[-1]
    before = jnp.arange(count)[:, None] < jnp.arange(count)[None, :]
    return jnp.dot(
        member.astype(jnp.bfloat16),
        before.astype(jnp.bfloat16),
        preferred_element_type=jnp.float32,
    ).astype(jnp.int32)


def assign(codes, n_row):
    cluster, valid = codes >> 1, codes & 1
    labels = jnp.arange(CLUSTERS)
    sizes = jnp.sum(
        (cluster.reshape(1, -1) == labels[:, None]) & (valid.reshape(1, -1) == 1), axis=1
    )
    ahead = (sizes[None, :] > sizes[:, None]) | (
        (sizes[None, :] == sizes[:, None]) & (labels[None, :] < labels[:, None])
    )
    rank = jnp.sum(ahead, axis=1)
    others = n_row - 1
    turn, place = (rank - 1) // others, (rank - 1) % others
    group = jnp.where(rank == 0, 0, 1 + jnp.where(turn == 0, place, others - 1 - place))
    of_node = jnp.sum(
        jnp.where(cluster[None] == labels[:, None, None, None], group[:, None, None, None], 0),
        axis=0,
    )
    return jnp.where(valid == 1, of_node, n_row)


def compact(
    codes,
    group,
    features,
    block_keep,
    edge_weight,
    weight_one,
    bias_one,
    gain_one,
    shift_one,
    weight_two,
    bias_two,
    gain_two,
    shift_two,
    cotangent,
    places,
    slots,
    seats,
    fits,
    others,
    sizes,
    caps,
):
    row, col = lax.axis_index("row"), lax.axis_index(COL)
    chip, core = lax.axis_index("chip"), lax.axis_index("core")
    n_row, n_col = sizes
    own_cap, send_cap, seat_cap = caps
    own_nodes, in_width = features.shape
    width = weight_two.shape[2]
    span = n_col * own_cap
    targets = jnp.arange(n_row)

    def in_col(value):
        return lax.dynamic_index_in_dim(value, col, 1, False).reshape(-1)

    def in_row(value):
        return lax.dynamic_index_in_dim(value, row, 0, False).reshape(-1)

    row_group, col_group = in_row(group), in_col(group)
    row_keys = jnp.where(in_row(slots) < send_cap, row_group * send_cap + in_row(slots), -1)
    col_keys = jnp.where(in_col(places) < own_cap, col_group * own_cap + in_col(places), -1)
    pieces = packed_pieces(
        block_keep,
        in_row(codes),
        in_col(codes),
        row_keys,
        col_keys,
        edge_weight,
        (own_cap, send_cap),
        n_row,
    )
    pieces = trade(pieces, "row")
    whole, half_send = own_cap // 128 * 128, send_cap // 2

    standing = jnp.arange(n_col)[None, :, None] * own_cap + places
    fits_here = jnp.where(group == row, standing, -1).reshape(n_row, -1)
    slot_of = slots.reshape(n_row, -1)
    target = jnp.max(
        jnp.where(
            slot_of[:, None, :] == jnp.arange(send_cap)[None, :, None], fits_here[:, None, :], -1
        ),
        axis=2,
    )
    spread = (target[:, :, None] == jnp.arange(span)[None, None, :]).astype(jnp.bfloat16)

    group_here = lax.dynamic_index_in_dim(in_row(group).reshape(n_col, -1), col, 0, False)
    seat_here = lax.dynamic_index_in_dim(in_row(seats).reshape(n_col, -1), col, 0, False)
    place_here = lax.dynamic_index_in_dim(in_row(places).reshape(n_col, -1), col, 0, False)
    leave = (group_here[None, None, :] == targets[:, None, None]) & (
        seat_here[None, None, :] == jnp.arange(seat_cap)[None, :, None]
    )
    leave = leave.astype(jnp.bfloat16).reshape(n_row * seat_cap, own_nodes)
    both = jnp.dot(leave, jnp.concatenate([features, cotangent], axis=1))
    both = both.reshape(n_row, seat_cap, -1)
    group_col = lax.dynamic_index_in_dim(group, col, 1, False)
    seats_col = lax.dynamic_index_in_dim(seats, col, 1, False)
    places_col = lax.dynamic_index_in_dim(places, col, 1, False)
    seated = (group_col == row)[:, None, :] & (
        seats_col[:, None, :] == jnp.arange(seat_cap)[None, :, None]
    )
    place_of_seat = jnp.max(jnp.where(seated, places_col[:, None, :], -1), axis=2)
    place_of_seat = place_of_seat.reshape(n_row * seat_cap)
    arrive = (place_of_seat[None, :] == jnp.arange(own_cap)[:, None]).astype(jnp.bfloat16)
    take = (place_of_seat[:, None] == jnp.arange(own_cap)[None, :]).astype(jnp.bfloat16)
    put_place = (group_here * own_cap + place_here)[:, None] == jnp.arange(n_row * own_cap)
    put_place = put_place.astype(jnp.bfloat16)
    held_count = jnp.sum(group_col == row)
    valid_rows = (jnp.arange(own_cap) < held_count).astype(jnp.float32)
    pieces, both, spread, arrive, take, put_place, valid_rows, others = lax.optimization_barrier(
        (pieces, both, spread, arrive, take, put_place, valid_rows, others)
    )

    many = whole // 128
    pieces = pieces.reshape(n_row, 2 * many + 1, half_send, 128)
    ends = pieces[:, 2 * many, :, : own_cap - whole], pieces[:, 2 * many, :, own_cap - whole :]
    ends = jnp.stack(ends, axis=1).reshape(n_row, send_cap, own_cap - whole)
    received = [
        pieces[:, 2 * tile : 2 * tile + 2].reshape(n_row, send_cap, 128) for tile in range(many)
    ]
    received = jnp.concatenate(received + [ends], axis=2)
    own_block = jnp.einsum("stu,stw->uw", received, spread).astype(jnp.bfloat16)
    quadrant = lax.dynamic_slice_in_dim(own_block, chip * (span // 2), span // 2, 1)
    quadrant = swap(quadrant, "chip")
    both = trade(both, "row")
    place = jnp.stack([chip, core]).astype(jnp.int32)
    sibling = swap(own_block, "core")
    adjacency = normalized_block(own_block, sibling, quadrant, swap(quadrant, "core"), place)
    both, adjacency = lax.optimization_barrier((both, adjacency))
    mine = jnp.dot(arrive, both.reshape(n_row * seat_cap, -1))
    features_own, cotangent_own = mine[:, :in_width], mine[:, in_width:]
    sibling = swap(features_own, "core")

    first = (col * own_cap + jnp.arange(own_cap))[:, None] == jnp.arange(span)[None, :]
    previous = first.astype(jnp.float32)
    current = -lax.dynamic_slice_in_dim(adjacency, col * own_cap, own_cap, 0).astype(jnp.float32)
    lowered = [current.astype(jnp.bfloat16)]
    for position in range(2, ORDER):
        upcoming = (
            -2.0 * jnp.dot(lowered[-1], adjacency, preferred_element_type=jnp.float32) - previous
        )
        low = upcoming.astype(jnp.bfloat16)
        if position == 4:
            low, sibling = lax.optimization_barrier((low, sibling))
            features_chip = joined(features_own, sibling, core)
            partner = swap(features_chip, "chip")
        if position == 8:
            low, partner = lax.optimization_barrier((low, partner))
            features_all = joined(features_chip, partner, chip)
        previous, current = current, upcoming
        lowered.append(low)
    polynomials = jnp.concatenate(lowered, axis=0)

    def apply(value_low, everyone):
        result = jnp.dot(polynomials, everyone, preferred_element_type=jnp.float32)
        result = result.astype(jnp.bfloat16).reshape(ORDER - 1, own_cap, -1)
        return jnp.concatenate([value_low[None], result], axis=0)

    def everywhere(value_low):
        return lax.all_gather(value_low, COL, axis=0, tiled=True)

    def forward(value_low, everyone, weight, bias, gain, shift):
        stacked = apply(value_low, everyone)
        mixed = jnp.einsum("kni,kio->no", stacked, weight, preferred_element_type=jnp.float32)
        mixed = mixed + bias
        return stacked, mixed, finish(mixed, gain, shift, valid_rows)

    def through_norm(mixed, upstream, gain, shift):
        ignored, pullback = jax.vjp(
            lambda mixed_in, gain_in, shift_in: finish(mixed_in, gain_in, shift_in, valid_rows),
            mixed,
            gain,
            shift,
        )
        mixed_grad, gain_grad, shift_grad = pullback(upstream)
        mixed_low = mixed_grad.astype(jnp.bfloat16)
        bias_grad = jnp.sum(mixed_low.astype(jnp.float32), axis=0)
        return mixed_low, [bias_grad, gain_grad, shift_grad]

    def weight_gradient(turned, mixed_low):
        grad = jnp.einsum("kin,no->kio", turned, mixed_low, preferred_element_type=jnp.float32)
        return grad.astype(jnp.bfloat16).reshape(-1, width)

    def to_input(mixed_low, everyone, weight):
        spread_grad = apply(mixed_low, everyone)
        return jnp.einsum("kno,kio->ni", spread_grad, weight, preferred_element_type=jnp.float32)

    def chosen(value, other):
        return jnp.where(fits, value.astype(jnp.float32), other.astype(jnp.float32))

    def both_halves(mine, other):
        return jnp.where((core == jnp.arange(2))[:, None, None], mine[None], other[None])

    stacked_one, mixed_one, hidden = forward(
        features_own, features_all, weight_one, bias_one, gain_one, shift_one
    )
    hidden_low = hidden.astype(jnp.bfloat16)
    everyone_hidden = everywhere(hidden_low)
    stacked_two, mixed_two, activations = forward(
        hidden_low, everyone_hidden, weight_two, bias_two, gain_two, shift_two
    )
    low_two, rest_two = through_norm(
        mixed_two, cotangent_own.astype(jnp.float32), gain_two, shift_two
    )

    second = weight_gradient(stacked_two.transpose(0, 2, 1), low_two)
    mine, other = split(second.reshape(2, -1, width), core)
    low_two, other = lax.optimization_barrier((low_two, other))
    activations_all = lax.all_gather(activations.astype(jnp.bfloat16), "row", axis=0, tiled=True)
    second = added(mine, swap(other, "core")).reshape(2, -1, width)
    everyone_two, second = lax.optimization_barrier((everywhere(low_two), second))
    second = trade(second, "chip")
    hidden_grad = to_input(low_two, everyone_two, weight_two)
    low_one, rest_one = through_norm(mixed_one, hidden_grad, gain_one, shift_one)
    turned_one = lax.optimization_barrier(stacked_one.transpose(0, 2, 1))
    first = weight_gradient(turned_one, low_one).reshape(2, -1, width)
    half = first.shape[1]
    unit = n_row * 2 * 8
    padded = -(-(half + 6) // unit) * unit
    rest = jnp.pad(jnp.stack(rest_one + rest_two), ((0, padded - half - 6), (0, 0)))
    rest = jnp.stack([rest, jnp.zeros_like(rest)]).astype(jnp.bfloat16)
    first = jnp.concatenate([first, rest], axis=1)
    mine, other = split(first, core)
    second = added(second[0], second[1]).reshape(n_row, -1, width)
    low_one, second, other = lax.optimization_barrier((low_one, second, other))
    second = trade(second, "row")
    first = added(mine, swap(other, "core")).reshape(n_row, 2, -1, width).swapaxes(0, 1)
    mine, other = split(first, chip)
    low_one, other = lax.optimization_barrier((low_one, other))
    everyone_one = everywhere(low_one)
    first = added(mine, swap(other, "chip"))
    second = jnp.sum(second.astype(jnp.float32), axis=0).astype(jnp.bfloat16)
    first = jnp.sum(trade(first, "row").astype(jnp.float32), axis=0).astype(jnp.bfloat16)
    second, first, activations_all = lax.optimization_barrier((second, first, activations_all))
    second = broadcast_along(second, "row", n_row).reshape(-1, width)
    first = joined(first, swap(first, "chip"), chip)
    home = jnp.dot(put_place, activations_all, preferred_element_type=jnp.float32)
    home = chosen(home, others[0])
    input_grad = to_input(low_one, everyone_one, weight_one)
    leaving = jnp.dot(take, input_grad.astype(jnp.bfloat16))
    leaving = leaving.reshape(n_row, seat_cap * in_width // width, width)
    share = first.shape[0]
    first = jnp.broadcast_to(first[None], (n_row,) + first.shape)
    second, first, leaving, home = lax.optimization_barrier((second, first, leaving, home))
    second = joined(second, swap(second, "chip"), chip)
    second = chosen(both_halves(second, swap(second, "core")), others[3])
    first = trade(jnp.concatenate([first, leaving], axis=1), "row")
    first, second = lax.optimization_barrier((first, second))
    back = first[:, share:].reshape(n_row * seat_cap, in_width)
    first = first[:, :share].reshape(-1, width)
    other = swap(first, "core")
    home_grad = jnp.dot(leave.T, back, preferred_element_type=jnp.float32)
    small = jnp.where(core == 0, first[half : half + 6], other[half : half + 6])
    first = chosen(both_halves(first[:half], other[:half]), others[2])
    return home, chosen(home_grad, others[1]), first, second, chosen(small, others[4])


def general(
    codes,
    features,
    block_keep,
    edge_weight,
    weight_one,
    bias_one,
    gain_one,
    shift_one,
    weight_two,
    bias_two,
    gain_two,
    shift_two,
    cotangent,
    node_valid,
):
    row, col = lax.axis_index("row"), lax.axis_index(COL)
    row_codes = lax.dynamic_index_in_dim(codes, row, 0, False).reshape(-1)
    col_codes = lax.dynamic_index_in_dim(codes, col, 1, False).reshape(-1)
    tile_rows, tile_cols = edge_weight.shape
    blocks_down, blocks_across = block_keep.shape
    block_side = tile_rows // blocks_down
    linked = (row_codes[:, None] == col_codes[None, :]) & (row_codes[:, None] & 1 == 1)
    linked = linked.reshape(blocks_down, block_side, blocks_across, block_side) & (
        block_keep[:, None, :, None] == 1
    )
    masked = edge_weight * linked.reshape(tile_rows, tile_cols).astype(jnp.bfloat16)
    degree_rows = 1.0 + lax.psum(jnp.sum(masked, axis=1, dtype=jnp.float32), COL)
    own_nodes = features.shape[0]
    own_degree = lax.dynamic_slice_in_dim(
        degree_rows, lax.axis_index(COL) * own_nodes, own_nodes, 0
    )
    degree_cols = lax.all_gather(own_degree, "row", axis=0, tiled=True)
    adjacency = (
        masked.astype(jnp.float32)
        * lax.rsqrt(degree_rows)[:, None]
        * lax.rsqrt(degree_cols)[None, :]
    ).astype(jnp.bfloat16)
    valid_rows = node_valid.astype(jnp.float32)
    stacked_one, mixed_one, hidden = layer_forward(
        adjacency,
        features.astype(jnp.float32),
        weight_one,
        bias_one,
        gain_one,
        shift_one,
        valid_rows,
    )
    stacked_two, mixed_two, activations = layer_forward(
        adjacency, hidden, weight_two, bias_two, gain_two, shift_two, valid_rows
    )
    hidden_grad, weight_two_grad, bias_two_grad, gain_two_grad, shift_two_grad = layer_backward(
        adjacency,
        stacked_two,
        mixed_two,
        cotangent.astype(jnp.float32),
        weight_two,
        gain_two,
        shift_two,
        valid_rows,
    )
    input_grad, weight_one_grad, bias_one_grad, gain_one_grad, shift_one_grad = layer_backward(
        adjacency, stacked_one, mixed_one, hidden_grad, weight_one, gain_one, shift_one, valid_rows
    )
    summed = lax.psum(
        (
            weight_one_grad,
            bias_one_grad,
            gain_one_grad,
            shift_one_grad,
            weight_two_grad,
            bias_two_grad,
            gain_two_grad,
            shift_two_grad,
        ),
        ("row",) + COL,
    )
    weight_one_grad, bias_one_grad, gain_one_grad, shift_one_grad = (
        summed[0],
        summed[1],
        summed[2],
        summed[3],
    )
    weight_two_grad, bias_two_grad, gain_two_grad, shift_two_grad = (
        summed[4],
        summed[5],
        summed[6],
        summed[7],
    )
    return (
        activations,
        input_grad,
        weight_one_grad,
        bias_one_grad,
        gain_one_grad,
        shift_one_grad,
        weight_two_grad,
        bias_two_grad,
        gain_two_grad,
        shift_two_grad,
    )


def local(n_row, n_col, *args):
    (
        features,
        node_valid,
        cluster,
        block_keep,
        edge_weight,
        weight_one,
        bias_one,
        gain_one,
        shift_one,
        weight_two,
        bias_two,
        gain_two,
        shift_two,
        cotangent,
    ) = args
    own_nodes, in_width = features.shape
    own_cap = own_nodes * n_row * 5 // 16
    send_cap = own_nodes * n_col * 11 // 32
    seat_cap = own_nodes // 2
    codes = broadcast_along(cluster * 2 + node_valid, ("row",) + COL, n_row * n_col)
    codes = codes.reshape(n_row, n_col, own_nodes)
    shared = (
        block_keep,
        edge_weight,
        weight_one,
        bias_one,
        gain_one,
        shift_one,
        weight_two,
        bias_two,
        gain_two,
        shift_two,
        cotangent,
    )

    def slow():
        return general(codes, features, *shared, node_valid)

    held = (ORDER - 1) * own_cap * own_cap * n_col * 2
    if held > HELD_BYTES or n_col != 4 or n_row < 2:
        return slow()
    group = assign(codes, n_row)
    member = group[None] == jnp.arange(n_row)[:, None, None, None]
    by_col = member.transpose(0, 2, 1, 3).reshape(n_row, n_col, -1)
    by_row = member.reshape(n_row, n_row, -1)
    places = jnp.sum(jnp.where(by_col, exclusive_counts(by_col), 0), axis=0)
    places = places.reshape(n_col, n_row, own_nodes).transpose(1, 0, 2)
    slots = jnp.sum(jnp.where(by_row, exclusive_counts(by_row), 0), axis=0)
    slots = slots.reshape(n_row, n_col, own_nodes)
    seats = jnp.sum(jnp.where(member, exclusive_counts(member), 0), axis=0)
    fits = (
        (jnp.max(jnp.sum(by_col, axis=2)) <= own_cap)
        & (jnp.max(jnp.sum(by_row, axis=2)) <= send_cap)
        & (jnp.max(jnp.sum(member, axis=3)) <= seat_cap)
    )
    width = weight_two.shape[2]

    def instead(state):
        made = slow()
        small = jnp.stack([made[place] for place in (3, 4, 5, 7, 8, 9)])
        return (True,) + tuple(
            value.astype(jnp.bfloat16).reshape(like.shape)
            for value, like in zip((made[0], made[1], made[2], made[6], small), state[1:])
        )

    shapes = (
        (own_nodes, width),
        (own_nodes, in_width),
        (2, ORDER * in_width // 2, width),
        (2, ORDER * width // 2, width),
        (6, width),
    )
    others = lax.while_loop(
        lambda state: jnp.logical_not(state[0]),
        instead,
        (fits,) + tuple(jnp.zeros(shape, jnp.bfloat16) for shape in shapes),
    )[1:]
    home, home_grad, first, second, small = compact(
        codes,
        group,
        features,
        *shared,
        places,
        slots,
        seats,
        fits,
        others,
        (n_row, n_col),
        (own_cap, send_cap, seat_cap),
    )
    return (
        home,
        home_grad,
        first.reshape(weight_one.shape),
        small[0],
        small[1],
        small[2],
        second.reshape(weight_two.shape),
        small[3],
        small[4],
        small[5],
    )


def solution(mesh):
    n_row, n_col = mesh.shape["row"], mesh.shape["col"]
    by_core = jax.sharding.Mesh(
        mesh.devices.reshape(n_row, n_col // 2, 2), ("row", "chip", "core")
    )
    nodes = ("row", "chip", "core")
    placed = (
        P(nodes, None),
        P(nodes),
        P(nodes),
        P("row", COL),
        P("row", COL),
        P(),
        P(),
        P(),
        P(),
        P(),
        P(),
        P(),
        P(),
        P(nodes, None),
    )
    return jax.shard_map(
        functools.partial(local, n_row, n_col),
        mesh=by_core,
        in_specs=placed,
        out_specs=(P(nodes, None), P(nodes, None), P(), P(), P(), P(), P(), P(), P(), P()),
        check_vma=False,
    )
```

```python
import functools
import math

import jax
import jax.numpy as jnp
from jax import lax
from jax.experimental import pallas as pl
from jax.experimental.pallas import tpu as pltpu
from jax.sharding import PartitionSpec as P

ORDER = 13
CLUSTERS = 16
HELD_BYTES = 1 << 25
VMEM_BYTES = 32 << 20
TERMS = 3
NO_COST = pl.CostEstimate(flops=1, bytes_accessed=1, transcendentals=0)
COL = ("chip", "core")


def finish(mixed, gain, shift, valid_rows):
    active = jax.nn.gelu(mixed, approximate=False)
    centered = active - jnp.mean(active, axis=-1, keepdims=True)
    variance = jnp.mean(centered * centered, axis=-1, keepdims=True)
    return (centered * lax.rsqrt(variance + 1e-05) * gain + shift) * valid_rows[:, None]


def forward_product(adjacency, piece_low):
    partial_value = jnp.dot(
        adjacency,
        lax.all_gather(piece_low, "row", axis=0, tiled=True),
        preferred_element_type=jnp.float32,
    )
    return lax.psum_scatter(partial_value, COL, scatter_dimension=0, tiled=True)


def backward_product(adjacency, piece_low):
    partial_value = lax.dot_general(
        adjacency,
        lax.all_gather(piece_low, COL, axis=0, tiled=True),
        (((0,), (0,)), ((), ())),
        preferred_element_type=jnp.float32,
    )
    return lax.psum_scatter(
        partial_value.astype(jnp.bfloat16), "row", scatter_dimension=0, tiled=True
    ).astype(jnp.float32)


def layer_forward(adjacency, inputs, weight, bias, gain, shift, valid_rows):
    first_low = inputs.astype(jnp.bfloat16)
    second = -forward_product(adjacency, first_low)
    second_low = second.astype(jnp.bfloat16)

    def advance(state_pair, unused):
        previous, current, current_low = state_pair
        upcoming = -2.0 * forward_product(adjacency, current_low) - previous
        upcoming_low = upcoming.astype(jnp.bfloat16)
        return ((current, upcoming, upcoming_low), upcoming_low)

    ignored, others = lax.scan(advance, (inputs, second, second_low), None, length=ORDER - 2)
    stacked = jnp.concatenate([first_low[None], second_low[None], others], axis=0)
    mixed = jnp.einsum("kni,kio->no", stacked, weight, preferred_element_type=jnp.float32) + bias
    return (stacked, mixed, finish(mixed, gain, shift, valid_rows))


def layer_backward(adjacency, stacked, mixed, upstream, weight, gain, shift, valid_rows):

    def local_finish(mixed_in, gain_in, shift_in):
        return finish(mixed_in, gain_in, shift_in, valid_rows)

    ignored, pullback = jax.vjp(local_finish, mixed, gain, shift)
    mixed_grad, gain_grad, shift_grad = pullback(upstream)
    mixed_low = mixed_grad.astype(jnp.bfloat16)
    bias_grad = jnp.sum(mixed_low.astype(jnp.float32), axis=0)
    weight_grad = jnp.einsum("kni,no->kio", stacked, mixed_low, preferred_element_type=jnp.float32)
    direct = jnp.einsum("no,kio->kni", mixed_low, weight, preferred_element_type=jnp.float32)

    def retreat(state_pair, direct_term):
        later_two, later_one = state_pair
        current = (
            direct_term
            - 2.0 * backward_product(adjacency, later_one.astype(jnp.bfloat16))
            - later_two
        )
        return ((later_one, current), None)

    start_pair = (jnp.zeros_like(direct[0]), direct[ORDER - 1])
    (second_grad, first_grad), unused = lax.scan(
        retreat, start_pair, direct[1 : ORDER - 1], reverse=True
    )
    input_grad = (
        direct[0] - backward_product(adjacency, first_grad.astype(jnp.bfloat16)) - second_grad
    )
    return (input_grad, weight_grad, bias_grad, gain_grad, shift_grad)


def swap(value, axis):
    return lax.ppermute(value, axis, [(0, 1), (1, 0)])


def trade(pieces, axis):
    return lax.all_to_all(pieces, axis, 0, 0, tiled=False)


def broadcast_along(value, axis, size):
    return trade(jnp.broadcast_to(value[None], (size,) + value.shape), axis)


def joined(mine, other, index):
    return jnp.where(
        index == 0, jnp.concatenate([mine, other]), jnp.concatenate([other, mine])
    )


def split(pair, index):
    mine = lax.dynamic_index_in_dim(pair, index, 0, False)
    return mine, lax.dynamic_index_in_dim(pair, 1 - index, 0, False)


def added(mine, received):
    return (mine.astype(jnp.float32) + received.astype(jnp.float32)).astype(jnp.bfloat16)


def assemble(place_ref, own_ref, sibling_ref, near_ref, far_ref, out_ref, done):
    chip, core = place_ref[0], place_ref[1]
    own_cap, span = own_ref.shape
    half = span // 2

    def rows(of_chip, of_core):
        return pl.ds(pl.multiple_of((2 * of_chip + of_core) * own_cap, own_cap), own_cap)

    def fetch(source, of_chip, of_core, columns, place):
        target = out_ref.at[rows(of_chip, of_core), columns]
        return pltpu.make_async_copy(source, target, done.at[place])

    def quadrant_copies(here):
        there = 1 - here
        columns = pl.ds(there * half, half)
        return (
            fetch(near_ref, there, core, columns, 2),
            fetch(far_ref, there, 1 - core, columns, 3),
        )

    everything = pl.ds(0, span)
    top = (
        fetch(own_ref, chip, core, everything, 0),
        fetch(sibling_ref, chip, 1 - core, everything, 1),
    )

    def of_chip(here):
        there = 1 - here
        copies = top + quadrant_copies(here)
        for copy in copies:
            copy.start()
        for copy in copies:
            copy.wait()
        here_rows = pl.ds(here * half, half)
        for tile in range(half // 128):
            columns = pl.ds(there * half + tile * 128, 128)
            strip = out_ref[here_rows, columns]
            turned = jnp.transpose(strip.astype(jnp.float32)).astype(jnp.bfloat16)
            out_ref[columns, here_rows] = turned

    @pl.when(chip == 0)
    def first():
        of_chip(0)

    @pl.when(chip == 1)
    def second():
        of_chip(1)

    across = jnp.ones((1, span), jnp.float32)
    for tile in range(span // 128):
        across = across + jnp.sum(
            out_ref[pl.ds(tile * 128, 128), :].astype(jnp.float32), axis=0, keepdims=True
        )
    across = lax.rsqrt(across)
    for tile in range(span // 128):
        strip = out_ref[pl.ds(tile * 128, 128), :].astype(jnp.float32)
        down = lax.rsqrt(1.0 + jnp.sum(strip, axis=1, keepdims=True))
        out_ref[pl.ds(tile * 128, 128), :] = (strip * down * across).astype(jnp.bfloat16)


def polynomial_kernel(
    place_ref, own_ref, sibling_ref, near_ref, far_ref, out_ref, matrix, powers, done, left
):
    order, own_cap, span = powers.shape
    assemble(place_ref, own_ref, sibling_ref, near_ref, far_ref, matrix, done)
    start = pl.multiple_of((2 * place_ref[0] + place_ref[1]) * own_cap, own_cap)
    powers[0] = -matrix[pl.ds(start, own_cap), :]

    def leave(term):
        return pltpu.make_async_copy(powers.at[term], out_ref.at[term], left.at[term])

    leave(0).start()
    for tile in range(span // 256):
        columns = pl.ds(tile * 256, 256)
        row = lax.broadcasted_iota(jnp.int32, (own_cap, 256), 0) + (start - tile * 256)
        column = lax.broadcasted_iota(jnp.int32, (own_cap, 256), 1)
        product = jnp.dot(powers[0], matrix[:, columns], preferred_element_type=jnp.float32)
        first = jnp.where(row == column, 1.0, 0.0)
        powers[1, :, columns] = (-2.0 * product - first).astype(jnp.bfloat16)
    leave(1).start()

    def advance(term, ignored):
        for tile in range(span // 256):
            columns = pl.ds(tile * 256, 256)
            product = jnp.dot(
                powers[term - 1], matrix[:, columns], preferred_element_type=jnp.float32
            )
            earlier = powers[term - 2, :, columns].astype(jnp.float32)
            powers[term, :, columns] = (-2.0 * product - earlier).astype(jnp.bfloat16)
        leave(term).start()
        return ignored

    lax.fori_loop(2, order, advance, 0)

    def finished(term, ignored):
        leave(term).wait()
        return ignored

    lax.fori_loop(0, order, finished, 0)


def polynomials_of(own, sibling, near, far, place):
    own_cap, span = own.shape
    return pl.pallas_call(
        polynomial_kernel,
        out_shape=jax.ShapeDtypeStruct((ORDER - 1, own_cap, span), jnp.bfloat16),
        in_specs=[pl.BlockSpec(memory_space=pltpu.SMEM)]
        + [pl.BlockSpec(memory_space=pltpu.HBM)] * 4,
        out_specs=pl.BlockSpec(memory_space=pltpu.HBM),
        scratch_shapes=[
            pltpu.VMEM((span, span), jnp.bfloat16),
            pltpu.VMEM((ORDER - 1, own_cap, span), jnp.bfloat16),
            pltpu.SemaphoreType.DMA((4,)),
            pltpu.SemaphoreType.DMA((ORDER - 1,)),
        ],
        compiler_params=pltpu.CompilerParams(vmem_limit_bytes=VMEM_BYTES),
        cost_estimate=NO_COST,
        name="polynomials",
    )(place, own, sibling, near, far)


def pack_kernel(
    keep_ref, row_codes_ref, col_codes_ref, row_keys_ref, col_keys_ref, weight_ref, out_ref,
    masked, picked, rows_hot, cols_hot
):
    tile_rows, tile_cols = weight_ref.shape
    blocks_down, blocks_across = keep_ref.shape
    groups, ignored, lanes = out_ref.shape
    send_cap, own_cap = rows_hot.shape[0] // groups, cols_hot.shape[0] // groups
    high, wide = tile_rows // blocks_down, tile_cols // blocks_across
    for down in range(blocks_down):
        for across in range(blocks_across):
            rows, columns = pl.ds(down * high, high), pl.ds(across * wide, wide)
            own, other = row_codes_ref[rows, :], col_codes_ref[:, columns]
            linked = (own == other) & (own % 2 == 1) & (keep_ref[down, across] == 1)
            weight = weight_ref[rows, columns].astype(jnp.float32)
            masked[rows, columns] = jnp.where(linked, weight, 0.0).astype(jnp.bfloat16)

    def one_hot(keys, start, count):
        standing = lax.broadcasted_iota(jnp.int32, (count, keys.shape[1]), 0) + start
        return jnp.where(standing == keys, 1.0, 0.0).astype(jnp.bfloat16)

    for group in range(groups):
        rows_hot[pl.ds(group * send_cap, send_cap), :] = one_hot(
            row_keys_ref[...], group * send_cap, send_cap
        )
        cols_hot[pl.ds(group * own_cap, own_cap), :] = one_hot(
            col_keys_ref[...], group * own_cap, own_cap
        )
    for tile in range(tile_cols // 256):
        columns = pl.ds(tile * 256, 256)
        picked[:, columns] = jnp.dot(
            rows_hot[...], masked[:, columns], preferred_element_type=jnp.float32
        ).astype(jnp.bfloat16)
    whole, half = own_cap // lanes, send_cap // 2
    for group in range(groups):
        packed = lax.dot_general(
            picked[pl.ds(group * send_cap, send_cap), :],
            cols_hot[pl.ds(group * own_cap, own_cap), :],
            (((1,), (1,)), ((), ())),
            preferred_element_type=jnp.float32,
        )
        for tile in range(whole):
            out_ref[group, pl.ds(tile * send_cap, send_cap), :] = packed[
                :, tile * lanes : (tile + 1) * lanes
            ].astype(jnp.bfloat16)
        ends = jnp.concatenate(
            [packed[:half, whole * lanes :], packed[half:, whole * lanes :]], axis=1
        )
        out_ref[group, pl.ds(whole * send_cap, half), :] = ends.astype(jnp.bfloat16)


def packed_pieces(block_keep, row_codes, col_codes, row_keys, col_keys, edge_weight, caps, groups):
    own_cap, send_cap = caps
    tile_rows, tile_cols = edge_weight.shape
    high = own_cap // 128 * send_cap + send_cap // 2
    vector = pl.BlockSpec(memory_space=pltpu.VMEM)
    return pl.pallas_call(
        pack_kernel,
        out_shape=jax.ShapeDtypeStruct((groups, high, 128), jnp.bfloat16),
        in_specs=[pl.BlockSpec(memory_space=pltpu.SMEM)] + [vector] * 5,
        out_specs=vector,
        scratch_shapes=[
            pltpu.VMEM((tile_rows, tile_cols), jnp.bfloat16),
            pltpu.VMEM((groups * send_cap, tile_cols), jnp.bfloat16),
            pltpu.VMEM((groups * send_cap, tile_rows), jnp.bfloat16),
            pltpu.VMEM((groups * own_cap, tile_cols), jnp.bfloat16),
        ],
        compiler_params=pltpu.CompilerParams(vmem_limit_bytes=VMEM_BYTES),
        cost_estimate=NO_COST,
        name="packed_pieces",
    )(block_keep, row_codes[:, None], col_codes[None], row_keys[None], col_keys[None], edge_weight)


def normal_share(mixed):
    return 0.5 * (1.0 + lax.erf(mixed * 0.5**0.5))


def norm_forward(mixed):
    active = mixed * normal_share(mixed)
    centered = active - jnp.mean(active, axis=-1, keepdims=True)
    scale = lax.rsqrt(jnp.mean(centered * centered, axis=-1, keepdims=True) + 1e-05)
    return centered * scale, scale


def norm_backward(mixed, upstream, gain, valid):
    normed, scale = norm_forward(mixed)
    upstream = upstream * valid
    inner = upstream * gain
    inner = inner - jnp.mean(inner, axis=-1, keepdims=True) - normed * jnp.mean(
        inner * normed, axis=-1, keepdims=True
    )
    density = jnp.exp(-0.5 * mixed * mixed) * (1.0 / (2.0 * math.pi) ** 0.5)
    low = (inner * scale * (normal_share(mixed) + mixed * density)).astype(jnp.bfloat16)
    rest = [low.astype(jnp.float32), upstream * normed, upstream]
    return low, [jnp.sum(value, axis=0, keepdims=True) for value in rest]


def weight_gradient(turned_ref, low, core, mine_ref, other_ref):
    half = turned_ref.shape[0] // 2

    def halves(first_ref, second_ref):
        for out_ref, start in ((first_ref, 0), (second_ref, half)):
            out_ref[:half, :] = jnp.dot(
                turned_ref[start : start + half, :], low, preferred_element_type=jnp.float32
            ).astype(jnp.bfloat16)

    @pl.when(core == 0)
    def low_half_first():
        halves(mine_ref, other_ref)

    @pl.when(core == 1)
    def high_half_first():
        halves(other_ref, mine_ref)


def forward_step(step, powers_ref, all_ref, own_ref, weights, bias_ref, turned, mixed):
    terms, own_cap, span = powers_ref.shape
    fan_in = own_ref.shape[1]

    @pl.when(step == 0)
    def first():
        turned[:fan_in, :] = own_ref[...].T
        mixed[...] = bias_ref[...] + jnp.dot(
            own_ref[...], weights[0][0], preferred_element_type=jnp.float32
        )

    low = jnp.dot(
        powers_ref[...].reshape(terms * own_cap, span),
        all_ref[...],
        preferred_element_type=jnp.float32,
    ).astype(jnp.bfloat16)
    total = mixed[...]
    for term in range(terms):
        part = low[term * own_cap : (term + 1) * own_cap]
        start = pl.multiple_of((1 + step * terms + term) * fan_in, fan_in)
        turned[pl.ds(start, fan_in), :] = part.T
        total = total + jnp.dot(part, weights[1 + term][0], preferred_element_type=jnp.float32)
    mixed[...] = total


def layer_one_kernel(
    powers_ref,
    all_ref,
    own_ref,
    weight_0,
    weight_a,
    weight_b,
    weight_c,
    bias_ref,
    gain_ref,
    shift_ref,
    valid_ref,
    hidden_ref,
    turned_ref,
    mixed_ref,
):
    step = pl.program_id(0)
    weights = (weight_0, weight_a, weight_b, weight_c)
    forward_step(step, powers_ref, all_ref, own_ref, weights, bias_ref, turned_ref, mixed_ref)

    @pl.when(step == pl.num_programs(0) - 1)
    def finish_layer():
        normed, ignored = norm_forward(mixed_ref[...])
        hidden = (normed * gain_ref[...] + shift_ref[...]) * valid_ref[...]
        hidden_ref[...] = hidden.astype(jnp.bfloat16)


def layer_two_kernel(
    place_ref,
    powers_ref,
    all_ref,
    own_ref,
    weight_0,
    weight_a,
    weight_b,
    weight_c,
    bias_ref,
    gain_ref,
    shift_ref,
    valid_ref,
    upstream_ref,
    active_ref,
    low_ref,
    rest_ref,
    mine_ref,
    other_ref,
    turned,
    mixed,
):
    step = pl.program_id(0)
    weights = (weight_0, weight_a, weight_b, weight_c)
    forward_step(step, powers_ref, all_ref, own_ref, weights, bias_ref, turned, mixed)

    @pl.when(step == pl.num_programs(0) - 1)
    def finish_layer():
        normed, ignored = norm_forward(mixed[...])
        active = (normed * gain_ref[...] + shift_ref[...]) * valid_ref[...]
        active_ref[...] = active.astype(jnp.bfloat16)
        low, rest = norm_backward(
            mixed[...], upstream_ref[...].astype(jnp.float32), gain_ref[...], valid_ref[...]
        )
        low_ref[...] = low
        for place in range(3):
            rest_ref[place : place + 1, :] = rest[place]
        weight_gradient(turned, low, place_ref[1], mine_ref, other_ref)


def backward_step(step, powers_ref, all_ref, own_ref, weights, total):
    terms, own_cap, span = powers_ref.shape
    transposed = (((1,), (1,)), ((), ()))

    @pl.when(step == 0)
    def first():
        total[...] = lax.dot_general(
            own_ref[...], weights[0][0], transposed, preferred_element_type=jnp.float32
        )

    low = jnp.dot(
        powers_ref[...].reshape(terms * own_cap, span),
        all_ref[...],
        preferred_element_type=jnp.float32,
    ).astype(jnp.bfloat16)
    value = total[...]
    for term in range(terms):
        value = value + lax.dot_general(
            low[term * own_cap : (term + 1) * own_cap],
            weights[1 + term][0],
            transposed,
            preferred_element_type=jnp.float32,
        )
    total[...] = value


def back_two_kernel(
    place_ref,
    powers_ref,
    all_ref,
    own_ref,
    weight_0,
    weight_a,
    weight_b,
    weight_c,
    turned_ref,
    mixed_ref,
    gain_ref,
    valid_ref,
    rest_ref,
    low_ref,
    mine_ref,
    other_ref,
    total,
):
    step = pl.program_id(0)
    weights = (weight_0, weight_a, weight_b, weight_c)
    backward_step(step, powers_ref, all_ref, own_ref, weights, total)

    @pl.when(step == pl.num_programs(0) - 1)
    def finish_layer():
        low, rest = norm_backward(mixed_ref[...], total[...], gain_ref[...], valid_ref[...])
        low_ref[...] = low
        weight_gradient(turned_ref, low, place_ref[1], mine_ref, other_ref)
        half = turned_ref.shape[0] // 2
        extra = jnp.zeros((mine_ref.shape[0] - half, mine_ref.shape[1]), jnp.bfloat16)
        rows = rest + [rest_ref[place : place + 1, :] for place in range(3)]
        rows = jnp.concatenate(rows + [jnp.zeros((10, rows[0].shape[1]), jnp.float32)], axis=0)

        def below(first_ref, second_ref):
            first_ref[half:, :] = extra
            second_ref[half:, :] = extra
            first_ref[half : half + 16, :] = rows.astype(jnp.bfloat16)

        @pl.when(place_ref[1] == 0)
        def low_half_here():
            below(mine_ref, other_ref)

        @pl.when(place_ref[1] == 1)
        def low_half_there():
            below(other_ref, mine_ref)


def back_one_kernel(
    powers_ref, all_ref, own_ref, weight_0, weight_a, weight_b, weight_c, out_ref, total
):
    step = pl.program_id(0)
    weights = (weight_0, weight_a, weight_b, weight_c)
    backward_step(step, powers_ref, all_ref, own_ref, weights, total)

    @pl.when(step == pl.num_programs(0) - 1)
    def finish_layer():
        out_ref[...] = total[...].astype(jnp.bfloat16)


def layer_pass(kernel, name, place, powers, everyone, own, weight, others, outs, scratch):
    ignored, own_cap, span = powers.shape
    fan_in, width = weight.shape[1:]

    def whole(value):
        return pl.BlockSpec(value.shape, lambda step: (0,) * len(value.shape))

    def term_weight(term):
        return pl.BlockSpec((1, fan_in, width), lambda step: (1 + step * TERMS + term, 0, 0))

    in_specs = [
        pl.BlockSpec((TERMS, own_cap, span), lambda step: (step, 0, 0)),
        whole(everyone),
        whole(own),
        pl.BlockSpec((1, fan_in, width), lambda step: (0, 0, 0)),
    ]
    in_specs += [term_weight(term) for term in range(TERMS)] + [whole(value) for value in others]
    operands = [powers, everyone, own] + [weight] * (1 + TERMS) + list(others)
    if place is not None:
        in_specs = [pl.BlockSpec(memory_space=pltpu.SMEM)] + in_specs
        operands = [place] + operands
    return pl.pallas_call(
        kernel,
        grid=((ORDER - 1) // TERMS,),
        out_shape=outs,
        in_specs=in_specs,
        out_specs=[whole(value) for value in outs],
        scratch_shapes=[pltpu.VMEM(shape, dtype) for shape, dtype in scratch],
        compiler_params=pltpu.CompilerParams(vmem_limit_bytes=VMEM_BYTES),
        cost_estimate=NO_COST,
        name=name,
    )(*operands)


def exclusive_counts(member):
    count = member.shape[-1]
    before = jnp.arange(count)[:, None] < jnp.arange(count)[None, :]
    return jnp.dot(
        member.astype(jnp.bfloat16),
        before.astype(jnp.bfloat16),
        preferred_element_type=jnp.float32,
    ).astype(jnp.int32)


def assign(codes, n_row):
    cluster, valid = codes >> 1, codes & 1
    labels = jnp.arange(CLUSTERS)
    sizes = jnp.sum(
        (cluster.reshape(1, -1) == labels[:, None]) & (valid.reshape(1, -1) == 1), axis=1
    )
    ahead = (sizes[None, :] > sizes[:, None]) | (
        (sizes[None, :] == sizes[:, None]) & (labels[None, :] < labels[:, None])
    )
    rank = jnp.sum(ahead, axis=1)
    others = n_row - 1
    turn, place = (rank - 1) // others, (rank - 1) % others
    group = jnp.where(rank == 0, 0, 1 + jnp.where(turn == 0, place, others - 1 - place))
    of_node = jnp.sum(
        jnp.where(cluster[None] == labels[:, None, None, None], group[:, None, None, None], 0),
        axis=0,
    )
    return jnp.where(valid == 1, of_node, n_row)


def compact(
    codes,
    group,
    features,
    block_keep,
    edge_weight,
    weight_one,
    bias_one,
    gain_one,
    shift_one,
    weight_two,
    bias_two,
    gain_two,
    shift_two,
    cotangent,
    places,
    slots,
    seats,
    fits,
    others,
    sizes,
    caps,
):
    row, col = lax.axis_index("row"), lax.axis_index(COL)
    chip, core = lax.axis_index("chip"), lax.axis_index("core")
    n_row, n_col = sizes
    own_cap, send_cap, seat_cap = caps
    own_nodes, in_width = features.shape
    width = weight_two.shape[2]
    span = n_col * own_cap
    targets = jnp.arange(n_row)

    def in_col(value):
        return lax.dynamic_index_in_dim(value, col, 1, False).reshape(-1)

    def in_row(value):
        return lax.dynamic_index_in_dim(value, row, 0, False).reshape(-1)

    row_group, col_group = in_row(group), in_col(group)
    row_keys = jnp.where(in_row(slots) < send_cap, row_group * send_cap + in_row(slots), -1)
    col_keys = jnp.where(in_col(places) < own_cap, col_group * own_cap + in_col(places), -1)
    pieces = packed_pieces(
        block_keep,
        in_row(codes),
        in_col(codes),
        row_keys,
        col_keys,
        edge_weight,
        (own_cap, send_cap),
        n_row,
    )
    pieces = trade(pieces, "row")
    whole, half_send = own_cap // 128 * 128, send_cap // 2

    standing = jnp.arange(n_col)[None, :, None] * own_cap + places
    fits_here = jnp.where(group == row, standing, -1).reshape(n_row, -1)
    slot_of = slots.reshape(n_row, -1)
    target = jnp.max(
        jnp.where(
            slot_of[:, None, :] == jnp.arange(send_cap)[None, :, None], fits_here[:, None, :], -1
        ),
        axis=2,
    )
    spread = (target[:, :, None] == jnp.arange(span)[None, None, :]).astype(jnp.bfloat16)

    group_here = lax.dynamic_index_in_dim(in_row(group).reshape(n_col, -1), col, 0, False)
    seat_here = lax.dynamic_index_in_dim(in_row(seats).reshape(n_col, -1), col, 0, False)
    place_here = lax.dynamic_index_in_dim(in_row(places).reshape(n_col, -1), col, 0, False)
    leave = (group_here[None, None, :] == targets[:, None, None]) & (
        seat_here[None, None, :] == jnp.arange(seat_cap)[None, :, None]
    )
    leave = leave.astype(jnp.bfloat16).reshape(n_row * seat_cap, own_nodes)
    both = jnp.dot(leave, jnp.concatenate([features, cotangent], axis=1))
    both = both.reshape(n_row, seat_cap, -1)
    group_col = lax.dynamic_index_in_dim(group, col, 1, False)
    seats_col = lax.dynamic_index_in_dim(seats, col, 1, False)
    places_col = lax.dynamic_index_in_dim(places, col, 1, False)
    seated = (group_col == row)[:, None, :] & (
        seats_col[:, None, :] == jnp.arange(seat_cap)[None, :, None]
    )
    place_of_seat = jnp.max(jnp.where(seated, places_col[:, None, :], -1), axis=2)
    place_of_seat = place_of_seat.reshape(n_row * seat_cap)
    arrive = (place_of_seat[None, :] == jnp.arange(own_cap)[:, None]).astype(jnp.bfloat16)
    take = (place_of_seat[:, None] == jnp.arange(own_cap)[None, :]).astype(jnp.bfloat16)
    put_place = (group_here * own_cap + place_here)[:, None] == jnp.arange(n_row * own_cap)
    put_place = put_place.astype(jnp.bfloat16)
    held_count = jnp.sum(group_col == row)
    valid_rows = (jnp.arange(own_cap) < held_count).astype(jnp.float32)[:, None]
    pieces, both, spread, arrive, take, put_place, valid_rows, others = lax.optimization_barrier(
        (pieces, both, spread, arrive, take, put_place, valid_rows, others)
    )

    many = whole // 128
    tiles = pieces[:, : many * send_cap].reshape(n_row, many, send_cap, 128)
    ends = pieces[:, many * send_cap :].reshape(n_row, half_send, 2, own_cap - whole)
    own_block = jnp.concatenate(
        [
            jnp.einsum("sktu,stw->kuw", tiles, spread).reshape(whole, span),
            jnp.einsum("sthu,shtw->uw", ends, spread.reshape(n_row, 2, half_send, span)),
        ]
    ).astype(jnp.bfloat16)
    quadrant = lax.dynamic_slice_in_dim(own_block, chip * (span // 2), span // 2, 1)
    quadrant = swap(quadrant, "chip")
    both = trade(both, "row")
    place = jnp.stack([chip, core]).astype(jnp.int32)
    sibling = swap(own_block, "core")
    powers = polynomials_of(own_block, sibling, quadrant, swap(quadrant, "core"), place)
    mine = jnp.dot(arrive, both.reshape(n_row * seat_cap, -1))
    features_own, cotangent_own = mine[:, :in_width], mine[:, in_width:]

    def everywhere(value_low):
        return lax.all_gather(value_low, COL, axis=0, tiled=True)

    def chosen(value, other):
        return jnp.where(fits, value.astype(jnp.float32), other.astype(jnp.float32))

    def shaped(*shape, dtype=jnp.bfloat16):
        return jax.ShapeDtypeStruct(shape, dtype)

    half_one, half_two = ORDER * in_width // 2, ORDER * width // 2
    hidden, turned_one, mixed_one = layer_pass(
        layer_one_kernel,
        "layer_one",
        None,
        powers,
        everywhere(features_own),
        features_own,
        weight_one,
        [bias_one[None], gain_one[None], shift_one[None], valid_rows],
        [
            shaped(own_cap, width),
            shaped(2 * half_one, own_cap),
            shaped(own_cap, width, dtype=jnp.float32),
        ],
        [],
    )
    activations, low_two, rest_two, mine, other = layer_pass(
        layer_two_kernel,
        "layer_two",
        place,
        powers,
        everywhere(hidden),
        hidden,
        weight_two,
        [bias_two[None], gain_two[None], shift_two[None], valid_rows, cotangent_own],
        [
            shaped(own_cap, width),
            shaped(own_cap, width),
            shaped(3, width, dtype=jnp.float32),
            shaped(half_two, width),
            shaped(half_two, width),
        ],
        [((2 * half_two, own_cap), jnp.bfloat16), ((own_cap, width), jnp.float32)],
    )

    def add_cores(mine, other, pieces):
        got = pieces(swap(other, "core"))
        (mine_here, mine_there), (got_here, got_there) = split(pieces(mine), chip), split(got, chip)
        return added(mine_here, got_here), added(mine_there, got_there)

    activations_all = lax.all_gather(activations, "row", axis=0, tiled=True)
    here, there = add_cores(mine, other, lambda value: value.reshape(2, -1, width))
    everyone_two, there = lax.optimization_barrier((everywhere(low_two), there))
    there = swap(there, "chip")
    unit = n_row * 2 * 8
    padded = -(-(half_one + 16) // unit) * unit
    low_one, mine, other = layer_pass(
        back_two_kernel,
        "back_two",
        place,
        powers,
        everyone_two,
        low_two,
        weight_two,
        [turned_one, mixed_one, gain_one[None], valid_rows, rest_two],
        [shaped(own_cap, width), shaped(padded, width), shaped(padded, width)],
        [((own_cap, width), jnp.float32)],
    )
    low_one, there = lax.optimization_barrier((low_one, there))
    second = added(here, there).reshape(n_row, -1, width)
    low_one, second = lax.optimization_barrier((low_one, second))
    second = trade(second, "row")
    here, there = add_cores(
        mine, other, lambda value: value.reshape(n_row, 2, -1, width).swapaxes(0, 1)
    )
    low_one, there = lax.optimization_barrier((low_one, there))
    everyone_one = everywhere(low_one)
    there = swap(there, "chip")
    everyone_one, second, there = lax.optimization_barrier((everyone_one, second, there))
    first = added(here, there)
    share = first.shape[1]
    second = jnp.sum(second.astype(jnp.float32), axis=0).astype(jnp.bfloat16)
    second = jnp.broadcast_to(second[None], (n_row,) + second.shape)
    mixed = jnp.concatenate([first, second], axis=1)
    everyone_one, mixed = lax.optimization_barrier((everyone_one, mixed))
    mixed = trade(mixed, "row")
    (input_grad,) = layer_pass(
        back_one_kernel,
        "back_one",
        None,
        powers,
        everyone_one,
        low_one,
        weight_one,
        [],
        [shaped(own_cap, in_width)],
        [((own_cap, in_width), jnp.float32)],
    )
    leaving = jnp.dot(take, input_grad).reshape(n_row, seat_cap * in_width // width, width)
    home = jnp.dot(put_place, activations_all, preferred_element_type=jnp.float32)
    home = chosen(home, others[0])
    mixed, leaving, home = lax.optimization_barrier((mixed, leaving, home))
    second = mixed[:, share:].reshape(-1, width)
    second = lax.all_gather(second, COL, axis=0).reshape((n_col // 2, 2) + second.shape)
    first = jnp.sum(mixed[:, :share].astype(jnp.float32), axis=0).astype(jnp.bfloat16)
    first = joined(first, swap(first, "chip"), chip)
    first = jnp.broadcast_to(first[None], (n_row,) + first.shape)
    first = trade(jnp.concatenate([first, leaving], axis=1), "row")
    second = chosen(second.swapaxes(0, 1), others[3].reshape((2, n_col // 2) + second.shape[2:]))
    first, second = lax.optimization_barrier((first, second))
    back = first[:, 2 * share :].reshape(n_row * seat_cap, in_width)
    first = first[:, : 2 * share].reshape(-1, width)
    other = swap(first, "core")
    home_grad = jnp.dot(leave.T, back, preferred_element_type=jnp.float32)
    small = slice(half_one, half_one + 6)
    small = jnp.where(core == 0, first[small], other[small])
    mine, other = first[None, :half_one], other[None, :half_one]
    first = jnp.where((core == jnp.arange(2))[:, None, None], mine, other)
    return (
        home,
        chosen(home_grad, others[1]),
        chosen(first, others[2]),
        second,
        chosen(small, others[4]),
    )


def general(
    codes,
    features,
    block_keep,
    edge_weight,
    weight_one,
    bias_one,
    gain_one,
    shift_one,
    weight_two,
    bias_two,
    gain_two,
    shift_two,
    cotangent,
    node_valid,
):
    row, col = lax.axis_index("row"), lax.axis_index(COL)
    row_codes = lax.dynamic_index_in_dim(codes, row, 0, False).reshape(-1)
    col_codes = lax.dynamic_index_in_dim(codes, col, 1, False).reshape(-1)
    tile_rows, tile_cols = edge_weight.shape
    blocks_down, blocks_across = block_keep.shape
    block_side = tile_rows // blocks_down
    linked = (row_codes[:, None] == col_codes[None, :]) & (row_codes[:, None] & 1 == 1)
    linked = linked.reshape(blocks_down, block_side, blocks_across, block_side) & (
        block_keep[:, None, :, None] == 1
    )
    masked = edge_weight * linked.reshape(tile_rows, tile_cols).astype(jnp.bfloat16)
    degree_rows = 1.0 + lax.psum(jnp.sum(masked, axis=1, dtype=jnp.float32), COL)
    own_nodes = features.shape[0]
    own_degree = lax.dynamic_slice_in_dim(
        degree_rows, lax.axis_index(COL) * own_nodes, own_nodes, 0
    )
    degree_cols = lax.all_gather(own_degree, "row", axis=0, tiled=True)
    adjacency = (
        masked.astype(jnp.float32)
        * lax.rsqrt(degree_rows)[:, None]
        * lax.rsqrt(degree_cols)[None, :]
    ).astype(jnp.bfloat16)
    valid_rows = node_valid.astype(jnp.float32)
    stacked_one, mixed_one, hidden = layer_forward(
        adjacency,
        features.astype(jnp.float32),
        weight_one,
        bias_one,
        gain_one,
        shift_one,
        valid_rows,
    )
    stacked_two, mixed_two, activations = layer_forward(
        adjacency, hidden, weight_two, bias_two, gain_two, shift_two, valid_rows
    )
    hidden_grad, weight_two_grad, bias_two_grad, gain_two_grad, shift_two_grad = layer_backward(
        adjacency,
        stacked_two,
        mixed_two,
        cotangent.astype(jnp.float32),
        weight_two,
        gain_two,
        shift_two,
        valid_rows,
    )
    input_grad, weight_one_grad, bias_one_grad, gain_one_grad, shift_one_grad = layer_backward(
        adjacency, stacked_one, mixed_one, hidden_grad, weight_one, gain_one, shift_one, valid_rows
    )
    summed = lax.psum(
        (
            weight_one_grad,
            bias_one_grad,
            gain_one_grad,
            shift_one_grad,
            weight_two_grad,
            bias_two_grad,
            gain_two_grad,
            shift_two_grad,
        ),
        ("row",) + COL,
    )
    weight_one_grad, bias_one_grad, gain_one_grad, shift_one_grad = (
        summed[0],
        summed[1],
        summed[2],
        summed[3],
    )
    weight_two_grad, bias_two_grad, gain_two_grad, shift_two_grad = (
        summed[4],
        summed[5],
        summed[6],
        summed[7],
    )
    return (
        activations,
        input_grad,
        weight_one_grad,
        bias_one_grad,
        gain_one_grad,
        shift_one_grad,
        weight_two_grad,
        bias_two_grad,
        gain_two_grad,
        shift_two_grad,
    )


def local(n_row, n_col, *args):
    (
        features,
        node_valid,
        cluster,
        block_keep,
        edge_weight,
        weight_one,
        bias_one,
        gain_one,
        shift_one,
        weight_two,
        bias_two,
        gain_two,
        shift_two,
        cotangent,
    ) = args
    own_nodes, in_width = features.shape
    own_cap = own_nodes * n_row * 5 // 16
    send_cap = own_nodes * n_col * 11 // 32
    seat_cap = own_nodes // 2
    codes = broadcast_along(cluster * 2 + node_valid, ("row",) + COL, n_row * n_col)
    codes = codes.reshape(n_row, n_col, own_nodes)
    shared = (
        block_keep,
        edge_weight,
        weight_one,
        bias_one,
        gain_one,
        shift_one,
        weight_two,
        bias_two,
        gain_two,
        shift_two,
        cotangent,
    )

    def slow():
        return general(codes, features, *shared, node_valid)

    held = (ORDER - 1) * own_cap * own_cap * n_col * 2
    if held > HELD_BYTES or n_col != 4 or n_row < 2:
        return slow()
    group = assign(codes, n_row)
    member = group[None] == jnp.arange(n_row)[:, None, None, None]
    by_col = member.transpose(0, 2, 1, 3).reshape(n_row, n_col, -1)
    by_row = member.reshape(n_row, n_row, -1)
    places = jnp.sum(jnp.where(by_col, exclusive_counts(by_col), 0), axis=0)
    places = places.reshape(n_col, n_row, own_nodes).transpose(1, 0, 2)
    slots = jnp.sum(jnp.where(by_row, exclusive_counts(by_row), 0), axis=0)
    slots = slots.reshape(n_row, n_col, own_nodes)
    seats = jnp.sum(jnp.where(member, exclusive_counts(member), 0), axis=0)
    fits = (
        (jnp.max(jnp.sum(by_col, axis=2)) <= own_cap)
        & (jnp.max(jnp.sum(by_row, axis=2)) <= send_cap)
        & (jnp.max(jnp.sum(member, axis=3)) <= seat_cap)
    )
    width = weight_two.shape[2]

    def instead(state):
        made = slow()
        small = jnp.stack([made[place] for place in (3, 4, 5, 7, 8, 9)])
        return (True,) + tuple(
            value.astype(jnp.bfloat16).reshape(like.shape)
            for value, like in zip((made[0], made[1], made[2], made[6], small), state[1:])
        )

    shapes = (
        (own_nodes, width),
        (own_nodes, in_width),
        (2, ORDER * in_width // 2, width),
        (2, ORDER * width // 2, width),
        (6, width),
    )
    others = lax.while_loop(
        lambda state: jnp.logical_not(state[0]),
        instead,
        (fits,) + tuple(jnp.zeros(shape, jnp.bfloat16) for shape in shapes),
    )[1:]
    home, home_grad, first, second, small = compact(
        codes,
        group,
        features,
        *shared,
        places,
        slots,
        seats,
        fits,
        others,
        (n_row, n_col),
        (own_cap, send_cap, seat_cap),
    )
    return (
        home,
        home_grad,
        first.reshape(weight_one.shape),
        small[0],
        small[1],
        small[2],
        second.reshape(weight_two.shape),
        small[3],
        small[4],
        small[5],
    )


def solution(mesh):
    n_row, n_col = mesh.shape["row"], mesh.shape["col"]
    by_core = jax.sharding.Mesh(
        mesh.devices.reshape(n_row, n_col // 2, 2), ("row", "chip", "core")
    )
    nodes = ("row", "chip", "core")
    placed = (
        P(nodes, None),
        P(nodes),
        P(nodes),
        P("row", COL),
        P("row", COL),
        P(),
        P(),
        P(),
        P(),
        P(),
        P(),
        P(),
        P(),
        P(nodes, None),
    )
    return jax.shard_map(
        functools.partial(local, n_row, n_col),
        mesh=by_core,
        in_specs=placed,
        out_specs=(P(nodes, None), P(nodes, None), P(), P(), P(), P(), P(), P(), P(), P()),
        check_vma=False,
    )
```

```python
import functools
import math

import jax
import jax.numpy as jnp
from jax import lax
from jax.experimental import pallas as pl
from jax.experimental.pallas import tpu as pltpu
from jax.sharding import PartitionSpec as P

ORDER = 13
CLUSTERS = 16
HELD_BYTES = 1 << 25
VMEM_BYTES = 32 << 20
TERMS = 3
NO_COST = pl.CostEstimate(flops=1, bytes_accessed=1, transcendentals=0)
COL = ("chip", "core")


def finish(mixed, gain, shift, valid_rows):
    active = jax.nn.gelu(mixed, approximate=False)
    centered = active - jnp.mean(active, axis=-1, keepdims=True)
    variance = jnp.mean(centered * centered, axis=-1, keepdims=True)
    return (centered * lax.rsqrt(variance + 1e-05) * gain + shift) * valid_rows[:, None]


def forward_product(adjacency, piece_low):
    partial_value = jnp.dot(
        adjacency,
        lax.all_gather(piece_low, "row", axis=0, tiled=True),
        preferred_element_type=jnp.float32,
    )
    return lax.psum_scatter(partial_value, COL, scatter_dimension=0, tiled=True)


def backward_product(adjacency, piece_low):
    partial_value = lax.dot_general(
        adjacency,
        lax.all_gather(piece_low, COL, axis=0, tiled=True),
        (((0,), (0,)), ((), ())),
        preferred_element_type=jnp.float32,
    )
    return lax.psum_scatter(
        partial_value.astype(jnp.bfloat16), "row", scatter_dimension=0, tiled=True
    ).astype(jnp.float32)


def layer_forward(adjacency, inputs, weight, bias, gain, shift, valid_rows):
    first_low = inputs.astype(jnp.bfloat16)
    second = -forward_product(adjacency, first_low)
    second_low = second.astype(jnp.bfloat16)

    def advance(state_pair, unused):
        previous, current, current_low = state_pair
        upcoming = -2.0 * forward_product(adjacency, current_low) - previous
        upcoming_low = upcoming.astype(jnp.bfloat16)
        return ((current, upcoming, upcoming_low), upcoming_low)

    ignored, others = lax.scan(advance, (inputs, second, second_low), None, length=ORDER - 2)
    stacked = jnp.concatenate([first_low[None], second_low[None], others], axis=0)
    mixed = jnp.einsum("kni,kio->no", stacked, weight, preferred_element_type=jnp.float32) + bias
    return (stacked, mixed, finish(mixed, gain, shift, valid_rows))


def layer_backward(adjacency, stacked, mixed, upstream, weight, gain, shift, valid_rows):

    def local_finish(mixed_in, gain_in, shift_in):
        return finish(mixed_in, gain_in, shift_in, valid_rows)

    ignored, pullback = jax.vjp(local_finish, mixed, gain, shift)
    mixed_grad, gain_grad, shift_grad = pullback(upstream)
    mixed_low = mixed_grad.astype(jnp.bfloat16)
    bias_grad = jnp.sum(mixed_low.astype(jnp.float32), axis=0)
    weight_grad = jnp.einsum("kni,no->kio", stacked, mixed_low, preferred_element_type=jnp.float32)
    direct = jnp.einsum("no,kio->kni", mixed_low, weight, preferred_element_type=jnp.float32)

    def retreat(state_pair, direct_term):
        later_two, later_one = state_pair
        current = (
            direct_term
            - 2.0 * backward_product(adjacency, later_one.astype(jnp.bfloat16))
            - later_two
        )
        return ((later_one, current), None)

    start_pair = (jnp.zeros_like(direct[0]), direct[ORDER - 1])
    (second_grad, first_grad), unused = lax.scan(
        retreat, start_pair, direct[1 : ORDER - 1], reverse=True
    )
    input_grad = (
        direct[0] - backward_product(adjacency, first_grad.astype(jnp.bfloat16)) - second_grad
    )
    return (input_grad, weight_grad, bias_grad, gain_grad, shift_grad)


def swap(value, axis):
    return lax.ppermute(value, axis, [(0, 1), (1, 0)])


def trade(pieces, axis):
    return lax.all_to_all(pieces, axis, 0, 0, tiled=False)


def broadcast_along(value, axis, size):
    return trade(jnp.broadcast_to(value[None], (size,) + value.shape), axis)


def joined(mine, other, index):
    return jnp.where(
        index == 0, jnp.concatenate([mine, other]), jnp.concatenate([other, mine])
    )


def split(pair, index):
    mine = lax.dynamic_index_in_dim(pair, index, 0, False)
    return mine, lax.dynamic_index_in_dim(pair, 1 - index, 0, False)


def added(mine, received):
    return (mine.astype(jnp.float32) + received.astype(jnp.float32)).astype(jnp.bfloat16)


def assemble(place_ref, own_ref, sibling_ref, near_ref, far_ref, out_ref, done):
    chip, core = place_ref[0], place_ref[1]
    own_cap, span = own_ref.shape
    half = span // 2

    def rows(of_chip, of_core):
        return pl.ds(pl.multiple_of((2 * of_chip + of_core) * own_cap, own_cap), own_cap)

    def fetch(source, of_chip, of_core, columns, place):
        target = out_ref.at[rows(of_chip, of_core), columns]
        return pltpu.make_async_copy(source, target, done.at[place])

    def quadrant_copies(here):
        there = 1 - here
        columns = pl.ds(there * half, half)
        return (
            fetch(near_ref, there, core, columns, 2),
            fetch(far_ref, there, 1 - core, columns, 3),
        )

    everything = pl.ds(0, span)
    top = (
        fetch(own_ref, chip, core, everything, 0),
        fetch(sibling_ref, chip, 1 - core, everything, 1),
    )

    def of_chip(here):
        there = 1 - here
        copies = top + quadrant_copies(here)
        for copy in copies:
            copy.start()
        for copy in copies:
            copy.wait()
        here_rows = pl.ds(here * half, half)
        for tile in range(half // 128):
            columns = pl.ds(there * half + tile * 128, 128)
            strip = out_ref[here_rows, columns]
            turned = jnp.transpose(strip.astype(jnp.float32)).astype(jnp.bfloat16)
            out_ref[columns, here_rows] = turned

    @pl.when(chip == 0)
    def first():
        of_chip(0)

    @pl.when(chip == 1)
    def second():
        of_chip(1)

    across = jnp.ones((1, span), jnp.float32)
    for tile in range(span // 128):
        across = across + jnp.sum(
            out_ref[pl.ds(tile * 128, 128), :].astype(jnp.float32), axis=0, keepdims=True
        )
    across = lax.rsqrt(across)
    for tile in range(span // 128):
        strip = out_ref[pl.ds(tile * 128, 128), :].astype(jnp.float32)
        down = lax.rsqrt(1.0 + jnp.sum(strip, axis=1, keepdims=True))
        out_ref[pl.ds(tile * 128, 128), :] = (strip * down * across).astype(jnp.bfloat16)


def normalized_block(own, sibling, near, far, place):
    span = own.shape[1]
    return pl.pallas_call(
        assemble,
        out_shape=jax.ShapeDtypeStruct((span, span), jnp.bfloat16),
        in_specs=[pl.BlockSpec(memory_space=pltpu.SMEM)]
        + [pl.BlockSpec(memory_space=pltpu.HBM)] * 4,
        out_specs=pl.BlockSpec(memory_space=pltpu.VMEM),
        scratch_shapes=[pltpu.SemaphoreType.DMA((4,))],
        compiler_params=pltpu.CompilerParams(vmem_limit_bytes=VMEM_BYTES),
        cost_estimate=NO_COST,
        name="normalized_block",
    )(place, own, sibling, near, far)


def pack_kernel(
    keep_ref, row_codes_ref, col_codes_ref, row_keys_ref, col_keys_ref, weight_ref, out_ref,
    masked, picked, rows_hot, cols_hot
):
    tile_rows, tile_cols = weight_ref.shape
    blocks_down, blocks_across = keep_ref.shape
    groups, ignored, lanes = out_ref.shape
    send_cap, own_cap = rows_hot.shape[0] // groups, cols_hot.shape[0] // groups
    high, wide = tile_rows // blocks_down, tile_cols // blocks_across
    for down in range(blocks_down):
        for across in range(blocks_across):
            rows, columns = pl.ds(down * high, high), pl.ds(across * wide, wide)
            own, other = row_codes_ref[rows, :], col_codes_ref[:, columns]
            linked = (own == other) & (own % 2 == 1) & (keep_ref[down, across] == 1)
            weight = weight_ref[rows, columns].astype(jnp.float32)
            masked[rows, columns] = jnp.where(linked, weight, 0.0).astype(jnp.bfloat16)

    def one_hot(keys, start, count):
        standing = lax.broadcasted_iota(jnp.int32, (count, keys.shape[1]), 0) + start
        return jnp.where(standing == keys, 1.0, 0.0).astype(jnp.bfloat16)

    for group in range(groups):
        rows_hot[pl.ds(group * send_cap, send_cap), :] = one_hot(
            row_keys_ref[...], group * send_cap, send_cap
        )
        cols_hot[pl.ds(group * own_cap, own_cap), :] = one_hot(
            col_keys_ref[...], group * own_cap, own_cap
        )
    for tile in range(tile_cols // 256):
        columns = pl.ds(tile * 256, 256)
        picked[:, columns] = jnp.dot(
            rows_hot[...], masked[:, columns], preferred_element_type=jnp.float32
        ).astype(jnp.bfloat16)
    whole, half = own_cap // lanes, send_cap // 2
    for group in range(groups):
        packed = lax.dot_general(
            picked[pl.ds(group * send_cap, send_cap), :],
            cols_hot[pl.ds(group * own_cap, own_cap), :],
            (((1,), (1,)), ((), ())),
            preferred_element_type=jnp.float32,
        )
        for tile in range(whole):
            out_ref[group, pl.ds(tile * send_cap, send_cap), :] = packed[
                :, tile * lanes : (tile + 1) * lanes
            ].astype(jnp.bfloat16)
        ends = jnp.concatenate(
            [packed[:half, whole * lanes :], packed[half:, whole * lanes :]], axis=1
        )
        out_ref[group, pl.ds(whole * send_cap, half), :] = ends.astype(jnp.bfloat16)


def packed_pieces(block_keep, row_codes, col_codes, row_keys, col_keys, edge_weight, caps, groups):
    own_cap, send_cap = caps
    tile_rows, tile_cols = edge_weight.shape
    high = own_cap // 128 * send_cap + send_cap // 2
    vector = pl.BlockSpec(memory_space=pltpu.VMEM)
    return pl.pallas_call(
        pack_kernel,
        out_shape=jax.ShapeDtypeStruct((groups, high, 128), jnp.bfloat16),
        in_specs=[pl.BlockSpec(memory_space=pltpu.SMEM)] + [vector] * 5,
        out_specs=vector,
        scratch_shapes=[
            pltpu.VMEM((tile_rows, tile_cols), jnp.bfloat16),
            pltpu.VMEM((groups * send_cap, tile_cols), jnp.bfloat16),
            pltpu.VMEM((groups * send_cap, tile_rows), jnp.bfloat16),
            pltpu.VMEM((groups * own_cap, tile_cols), jnp.bfloat16),
        ],
        compiler_params=pltpu.CompilerParams(vmem_limit_bytes=VMEM_BYTES),
        cost_estimate=NO_COST,
        name="packed_pieces",
    )(block_keep, row_codes[:, None], col_codes[None], row_keys[None], col_keys[None], edge_weight)


def normal_share(mixed):
    return 0.5 * (1.0 + lax.erf(mixed * 0.5**0.5))


def norm_forward(mixed):
    active = mixed * normal_share(mixed)
    centered = active - jnp.mean(active, axis=-1, keepdims=True)
    scale = lax.rsqrt(jnp.mean(centered * centered, axis=-1, keepdims=True) + 1e-05)
    return centered * scale, scale


def norm_backward(mixed, upstream, gain, valid):
    normed, scale = norm_forward(mixed)
    upstream = upstream * valid
    inner = upstream * gain
    inner = inner - jnp.mean(inner, axis=-1, keepdims=True) - normed * jnp.mean(
        inner * normed, axis=-1, keepdims=True
    )
    density = jnp.exp(-0.5 * mixed * mixed) * (1.0 / (2.0 * math.pi) ** 0.5)
    low = (inner * scale * (normal_share(mixed) + mixed * density)).astype(jnp.bfloat16)
    rest = [low.astype(jnp.float32), upstream * normed, upstream]
    return low, [jnp.sum(value, axis=0, keepdims=True) for value in rest]


def weight_gradient(turned_ref, low, core, mine_ref, other_ref):
    part = turned_ref.shape[0] // 4

    def halves(first_ref, second_ref):
        for place in range(4):
            out_ref = first_ref if place < 2 else second_ref
            out_ref[place % 2, :part, :] = jnp.dot(
                turned_ref[place * part : (place + 1) * part, :],
                low,
                preferred_element_type=jnp.float32,
            ).astype(jnp.bfloat16)

    @pl.when(core == 0)
    def low_half_first():
        halves(mine_ref, other_ref)

    @pl.when(core == 1)
    def high_half_first():
        halves(other_ref, mine_ref)


def forward_step(step, powers_ref, all_ref, own_ref, weights, bias_ref, turned, mixed):
    terms, own_cap, span = powers_ref.shape
    fan_in = own_ref.shape[1]

    @pl.when(step == 0)
    def first():
        turned[:fan_in, :] = own_ref[...].T
        mixed[...] = bias_ref[...] + jnp.dot(
            own_ref[...], weights[0][0], preferred_element_type=jnp.float32
        )

    low = jnp.dot(
        powers_ref[...].reshape(terms * own_cap, span),
        all_ref[...],
        preferred_element_type=jnp.float32,
    ).astype(jnp.bfloat16)
    total = mixed[...]
    for term in range(terms):
        part = low[term * own_cap : (term + 1) * own_cap]
        start = pl.multiple_of((1 + step * terms + term) * fan_in, fan_in)
        turned[pl.ds(start, fan_in), :] = part.T
        total = total + jnp.dot(part, weights[1 + term][0], preferred_element_type=jnp.float32)
    mixed[...] = total


def layer_one_kernel(
    powers_ref,
    all_ref,
    own_ref,
    weight_0,
    weight_a,
    weight_b,
    weight_c,
    bias_ref,
    gain_ref,
    shift_ref,
    valid_ref,
    hidden_ref,
    turned_ref,
    mixed_ref,
):
    step = pl.program_id(0)
    weights = (weight_0, weight_a, weight_b, weight_c)
    forward_step(step, powers_ref, all_ref, own_ref, weights, bias_ref, turned_ref, mixed_ref)

    @pl.when(step == pl.num_programs(0) - 1)
    def finish_layer():
        normed, ignored = norm_forward(mixed_ref[...])
        hidden = (normed * gain_ref[...] + shift_ref[...]) * valid_ref[...]
        hidden_ref[...] = hidden.astype(jnp.bfloat16)


def layer_two_kernel(
    place_ref,
    powers_ref,
    all_ref,
    own_ref,
    weight_0,
    weight_a,
    weight_b,
    weight_c,
    bias_ref,
    gain_ref,
    shift_ref,
    valid_ref,
    upstream_ref,
    active_ref,
    low_ref,
    rest_ref,
    mine_ref,
    other_ref,
    turned,
    mixed,
):
    step = pl.program_id(0)
    weights = (weight_0, weight_a, weight_b, weight_c)
    forward_step(step, powers_ref, all_ref, own_ref, weights, bias_ref, turned, mixed)

    @pl.when(step == pl.num_programs(0) - 1)
    def finish_layer():
        normed, ignored = norm_forward(mixed[...])
        active = (normed * gain_ref[...] + shift_ref[...]) * valid_ref[...]
        active_ref[...] = active.astype(jnp.bfloat16)
        low, rest = norm_backward(
            mixed[...], upstream_ref[...].astype(jnp.float32), gain_ref[...], valid_ref[...]
        )
        low_ref[...] = low
        for place in range(3):
            rest_ref[place : place + 1, :] = rest[place]
        weight_gradient(turned, low, place_ref[1], mine_ref, other_ref)


def backward_step(step, powers_ref, all_ref, own_ref, weights, total):
    terms, own_cap, span = powers_ref.shape
    transposed = (((1,), (1,)), ((), ()))

    @pl.when(step == 0)
    def first():
        total[...] = lax.dot_general(
            own_ref[...], weights[0][0], transposed, preferred_element_type=jnp.float32
        )

    low = jnp.dot(
        powers_ref[...].reshape(terms * own_cap, span),
        all_ref[...],
        preferred_element_type=jnp.float32,
    ).astype(jnp.bfloat16)
    value = total[...]
    for term in range(terms):
        value = value + lax.dot_general(
            low[term * own_cap : (term + 1) * own_cap],
            weights[1 + term][0],
            transposed,
            preferred_element_type=jnp.float32,
        )
    total[...] = value


def back_two_kernel(
    place_ref,
    powers_ref,
    all_ref,
    own_ref,
    weight_0,
    weight_a,
    weight_b,
    weight_c,
    turned_ref,
    mixed_ref,
    gain_ref,
    valid_ref,
    rest_ref,
    low_ref,
    mine_ref,
    other_ref,
    total,
):
    step = pl.program_id(0)
    weights = (weight_0, weight_a, weight_b, weight_c)
    backward_step(step, powers_ref, all_ref, own_ref, weights, total)

    @pl.when(step == pl.num_programs(0) - 1)
    def finish_layer():
        low, rest = norm_backward(mixed_ref[...], total[...], gain_ref[...], valid_ref[...])
        low_ref[...] = low
        weight_gradient(turned_ref, low, place_ref[1], mine_ref, other_ref)
        part = turned_ref.shape[0] // 4
        extra = jnp.zeros((2, mine_ref.shape[1] - part, mine_ref.shape[2]), jnp.bfloat16)
        rows = rest + [rest_ref[place : place + 1, :] for place in range(3)]
        rows = jnp.concatenate(rows + [jnp.zeros((10, rows[0].shape[1]), jnp.float32)], axis=0)

        def below(first_ref, second_ref):
            first_ref[:, part:, :] = extra
            second_ref[:, part:, :] = extra
            first_ref[0, part : part + 16, :] = rows.astype(jnp.bfloat16)

        @pl.when(place_ref[1] == 0)
        def low_half_here():
            below(mine_ref, other_ref)

        @pl.when(place_ref[1] == 1)
        def low_half_there():
            below(other_ref, mine_ref)


def back_one_kernel(
    powers_ref, all_ref, own_ref, weight_0, weight_a, weight_b, weight_c, out_ref, total
):
    step = pl.program_id(0)
    weights = (weight_0, weight_a, weight_b, weight_c)
    backward_step(step, powers_ref, all_ref, own_ref, weights, total)

    @pl.when(step == pl.num_programs(0) - 1)
    def finish_layer():
        out_ref[...] = total[...].astype(jnp.bfloat16)


def layer_pass(kernel, name, place, powers, everyone, own, weight, others, outs, scratch):
    ignored, own_cap, span = powers.shape
    fan_in, width = weight.shape[1:]

    def whole(value):
        return pl.BlockSpec(value.shape, lambda step: (0,) * len(value.shape))

    def term_weight(term):
        return pl.BlockSpec((1, fan_in, width), lambda step: (1 + step * TERMS + term, 0, 0))

    in_specs = [
        pl.BlockSpec((TERMS, own_cap, span), lambda step: (step, 0, 0)),
        whole(everyone),
        whole(own),
        pl.BlockSpec((1, fan_in, width), lambda step: (0, 0, 0)),
    ]
    in_specs += [term_weight(term) for term in range(TERMS)] + [whole(value) for value in others]
    operands = [powers, everyone, own] + [weight] * (1 + TERMS) + list(others)
    if place is not None:
        in_specs = [pl.BlockSpec(memory_space=pltpu.SMEM)] + in_specs
        operands = [place] + operands
    return pl.pallas_call(
        kernel,
        grid=((ORDER - 1) // TERMS,),
        out_shape=outs,
        in_specs=in_specs,
        out_specs=[whole(value) for value in outs],
        scratch_shapes=[pltpu.VMEM(shape, dtype) for shape, dtype in scratch],
        compiler_params=pltpu.CompilerParams(vmem_limit_bytes=VMEM_BYTES),
        cost_estimate=NO_COST,
        name=name,
    )(*operands)


def exclusive_counts(member):
    count = member.shape[-1]
    before = jnp.arange(count)[:, None] < jnp.arange(count)[None, :]
    return jnp.dot(
        member.astype(jnp.bfloat16),
        before.astype(jnp.bfloat16),
        preferred_element_type=jnp.float32,
    ).astype(jnp.int32)


def assign(codes, n_row):
    cluster, valid = codes >> 1, codes & 1
    labels = jnp.arange(CLUSTERS)
    sizes = jnp.sum(
        (cluster.reshape(1, -1) == labels[:, None]) & (valid.reshape(1, -1) == 1), axis=1
    )
    ahead = (sizes[None, :] > sizes[:, None]) | (
        (sizes[None, :] == sizes[:, None]) & (labels[None, :] < labels[:, None])
    )
    rank = jnp.sum(ahead, axis=1)
    others = n_row - 1
    turn, place = (rank - 1) // others, (rank - 1) % others
    group = jnp.where(rank == 0, 0, 1 + jnp.where(turn == 0, place, others - 1 - place))
    of_node = jnp.sum(
        jnp.where(cluster[None] == labels[:, None, None, None], group[:, None, None, None], 0),
        axis=0,
    )
    return jnp.where(valid == 1, of_node, n_row)


def compact(
    codes,
    group,
    features,
    block_keep,
    edge_weight,
    weight_one,
    bias_one,
    gain_one,
    shift_one,
    weight_two,
    bias_two,
    gain_two,
    shift_two,
    cotangent,
    places,
    slots,
    seats,
    fits,
    others,
    sizes,
    caps,
):
    row, col = lax.axis_index("row"), lax.axis_index(COL)
    chip, core = lax.axis_index("chip"), lax.axis_index("core")
    n_row, n_col = sizes
    own_cap, send_cap, seat_cap = caps
    own_nodes, in_width = features.shape
    width = weight_two.shape[2]
    span = n_col * own_cap
    targets = jnp.arange(n_row)

    def in_col(value):
        return lax.dynamic_index_in_dim(value, col, 1, False).reshape(-1)

    def in_row(value):
        return lax.dynamic_index_in_dim(value, row, 0, False).reshape(-1)

    row_group, col_group = in_row(group), in_col(group)
    row_keys = jnp.where(in_row(slots) < send_cap, row_group * send_cap + in_row(slots), -1)
    col_keys = jnp.where(in_col(places) < own_cap, col_group * own_cap + in_col(places), -1)
    pieces = packed_pieces(
        block_keep,
        in_row(codes),
        in_col(codes),
        row_keys,
        col_keys,
        edge_weight,
        (own_cap, send_cap),
        n_row,
    )
    pieces = trade(pieces, "row")
    whole, half_send = own_cap // 128 * 128, send_cap // 2

    standing = jnp.arange(n_col)[None, :, None] * own_cap + places
    fits_here = jnp.where(group == row, standing, -1).reshape(n_row, -1)
    slot_of = slots.reshape(n_row, -1)
    target = jnp.max(
        jnp.where(
            slot_of[:, None, :] == jnp.arange(send_cap)[None, :, None], fits_here[:, None, :], -1
        ),
        axis=2,
    )
    spread = (target[:, :, None] == jnp.arange(span)[None, None, :]).astype(jnp.bfloat16)

    group_here = lax.dynamic_index_in_dim(in_row(group).reshape(n_col, -1), col, 0, False)
    seat_here = lax.dynamic_index_in_dim(in_row(seats).reshape(n_col, -1), col, 0, False)
    leave = (group_here[None, None, :] == targets[:, None, None]) & (
        seat_here[None, None, :] == jnp.arange(seat_cap)[None, :, None]
    )
    leave = leave.astype(jnp.bfloat16).reshape(n_row * seat_cap, own_nodes)
    both = jnp.dot(leave, jnp.concatenate([features, cotangent], axis=1))
    both = both.reshape(n_row, seat_cap, -1)
    group_col = lax.dynamic_index_in_dim(group, col, 1, False)
    seats_col = lax.dynamic_index_in_dim(seats, col, 1, False)
    places_col = lax.dynamic_index_in_dim(places, col, 1, False)
    seated = (group_col == row)[:, None, :] & (
        seats_col[:, None, :] == jnp.arange(seat_cap)[None, :, None]
    )
    place_of_seat = jnp.max(jnp.where(seated, places_col[:, None, :], -1), axis=2)
    place_of_seat = place_of_seat.reshape(n_row * seat_cap)
    arrive = (place_of_seat[None, :] == jnp.arange(own_cap)[:, None]).astype(jnp.bfloat16)
    take = (place_of_seat[:, None] == jnp.arange(own_cap)[None, :]).astype(jnp.bfloat16)
    held_count = jnp.sum(group_col == row)
    valid_rows = (jnp.arange(own_cap) < held_count).astype(jnp.float32)[:, None]
    pieces, both, spread, arrive, take, valid_rows, others = lax.optimization_barrier(
        (pieces, both, spread, arrive, take, valid_rows, others)
    )

    many = whole // 128
    tiles = pieces[:, : many * send_cap].reshape(n_row, many, send_cap, 128)
    ends = pieces[:, many * send_cap :].reshape(n_row, half_send, 2, own_cap - whole)
    own_block = jnp.concatenate(
        [
            jnp.einsum("sktu,stw->kuw", tiles, spread).reshape(whole, span),
            jnp.einsum("sthu,shtw->uw", ends, spread.reshape(n_row, 2, half_send, span)),
        ]
    ).astype(jnp.bfloat16)
    quadrant = lax.dynamic_slice_in_dim(own_block, chip * (span // 2), span // 2, 1)
    quadrant = swap(quadrant, "chip")
    both = trade(both, "row")
    place = jnp.stack([chip, core]).astype(jnp.int32)
    sibling = swap(own_block, "core")
    adjacency = normalized_block(own_block, sibling, quadrant, swap(quadrant, "core"), place)
    both, adjacency = lax.optimization_barrier((both, adjacency))
    mine = jnp.dot(arrive, both.reshape(n_row * seat_cap, -1))
    features_own, cotangent_own = mine[:, :in_width], mine[:, in_width:]
    sibling = swap(features_own, "core")

    first = (col * own_cap + jnp.arange(own_cap))[:, None] == jnp.arange(span)[None, :]
    previous = first.astype(jnp.float32)
    current = -lax.dynamic_slice_in_dim(adjacency, col * own_cap, own_cap, 0).astype(jnp.float32)
    lowered = [current.astype(jnp.bfloat16)]
    for position in range(2, ORDER):
        upcoming = (
            -2.0 * jnp.dot(lowered[-1], adjacency, preferred_element_type=jnp.float32) - previous
        )
        low = upcoming.astype(jnp.bfloat16)
        if position == 4:
            low, sibling = lax.optimization_barrier((low, sibling))
            features_chip = joined(features_own, sibling, core)
            partner = swap(features_chip, "chip")
        if position == 8:
            low, partner = lax.optimization_barrier((low, partner))
            features_all = joined(features_chip, partner, chip)
        previous, current = current, upcoming
        lowered.append(low)
    powers = jnp.concatenate(lowered, axis=0).reshape(ORDER - 1, own_cap, span)

    def everywhere(value_low):
        return lax.all_gather(value_low, COL, axis=0, tiled=True)

    def chosen(value, other):
        return jnp.where(fits, value.astype(jnp.float32), other.astype(jnp.float32))

    def shaped(*shape, dtype=jnp.bfloat16):
        return jax.ShapeDtypeStruct(shape, dtype)

    part_one, part_two = ORDER * in_width // n_col, ORDER * width // n_col
    padded = -(-(part_one + 16) // (8 * n_row)) * (8 * n_row)
    hidden, turned_one, mixed_one = layer_pass(
        layer_one_kernel,
        "layer_one",
        None,
        powers,
        features_all,
        features_own,
        weight_one,
        [bias_one[None], gain_one[None], shift_one[None], valid_rows],
        [
            shaped(own_cap, width),
            shaped(n_col * part_one, own_cap),
            shaped(own_cap, width, dtype=jnp.float32),
        ],
        [],
    )
    activations, low_two, rest_two, mine, other = layer_pass(
        layer_two_kernel,
        "layer_two",
        place,
        powers,
        everywhere(hidden),
        hidden,
        weight_two,
        [bias_two[None], gain_two[None], shift_two[None], valid_rows, cotangent_own],
        [
            shaped(own_cap, width),
            shaped(own_cap, width),
            shaped(3, width, dtype=jnp.float32),
            shaped(2, part_two, width),
            shaped(2, part_two, width),
        ],
        [((n_col * part_two, own_cap), jnp.bfloat16), ((own_cap, width), jnp.float32)],
    )

    def add_cores(mine, other):
        got = swap(other, "core")
        (mine_here, mine_there), (got_here, got_there) = split(mine, chip), split(got, chip)
        return added(mine_here, got_here), added(mine_there, got_there)

    leaving = jnp.dot(take, activations).reshape(n_row, seat_cap, width)
    here, there = add_cores(mine, other)
    everyone_two, there, leaving = lax.optimization_barrier(
        (everywhere(low_two), there, leaving)
    )
    there = swap(there, "chip")
    back = trade(leaving, "row")
    low_one, mine, other = layer_pass(
        back_two_kernel,
        "back_two",
        place,
        powers,
        everyone_two,
        low_two,
        weight_two,
        [turned_one, mixed_one, gain_one[None], valid_rows, rest_two],
        [shaped(own_cap, width), shaped(2, padded, width), shaped(2, padded, width)],
        [((own_cap, width), jnp.float32)],
    )
    low_one, there, back = lax.optimization_barrier((low_one, there, back))
    second = added(here, there).reshape(n_row, -1, width)
    low_one, second = lax.optimization_barrier((low_one, second))
    second = trade(second, "row")
    here, there = add_cores(mine, other)
    low_one, there = lax.optimization_barrier((low_one, there))
    everyone_one = everywhere(low_one)
    there = swap(there, "chip")
    everyone_one, second, there = lax.optimization_barrier((everyone_one, second, there))
    first = added(here, there).reshape(n_row, -1, width)
    share = first.shape[1]
    second = jnp.sum(second.astype(jnp.float32), axis=0).astype(jnp.bfloat16)
    second = jnp.broadcast_to(second[None], (n_row,) + second.shape)
    mixed = jnp.concatenate([first, second], axis=1)
    everyone_one, mixed = lax.optimization_barrier((everyone_one, mixed))
    mixed = trade(mixed, "row")
    (input_grad,) = layer_pass(
        back_one_kernel,
        "back_one",
        None,
        powers,
        everyone_one,
        low_one,
        weight_one,
        [],
        [shaped(own_cap, in_width)],
        [((own_cap, in_width), jnp.float32)],
    )
    leaving = jnp.dot(take, input_grad).reshape(n_row, seat_cap * in_width // width, width)
    home = jnp.dot(leave.T, back.reshape(-1, width), preferred_element_type=jnp.float32)
    mixed, leaving, home = lax.optimization_barrier((mixed, leaving, home))
    first = jnp.sum(mixed[:, :share].astype(jnp.float32), axis=0).astype(jnp.bfloat16)
    first = jnp.broadcast_to(first[None], (n_row,) + first.shape)
    first = trade(jnp.concatenate([first, leaving], axis=1), "row")
    second = lax.all_gather(mixed[:, share:].reshape(-1, width), COL, axis=0)
    back = first[:, share:].reshape(n_row * seat_cap, in_width)
    first = lax.all_gather(first[:, :share].reshape(-1, width), COL, axis=0)
    home_grad = jnp.dot(leave.T, back, preferred_element_type=jnp.float32)

    def by_core(value):
        return value.reshape(n_col // 2, 2, -1, width).swapaxes(0, 1)

    first = by_core(first)
    return (
        chosen(home, others[0]),
        chosen(home_grad, others[1]),
        chosen(first[:, :, :part_one], others[2]),
        chosen(by_core(second), others[3]),
        chosen(first[0, 0, part_one : part_one + 6], others[4]),
    )


def general(
    codes,
    features,
    block_keep,
    edge_weight,
    weight_one,
    bias_one,
    gain_one,
    shift_one,
    weight_two,
    bias_two,
    gain_two,
    shift_two,
    cotangent,
    node_valid,
):
    row, col = lax.axis_index("row"), lax.axis_index(COL)
    row_codes = lax.dynamic_index_in_dim(codes, row, 0, False).reshape(-1)
    col_codes = lax.dynamic_index_in_dim(codes, col, 1, False).reshape(-1)
    tile_rows, tile_cols = edge_weight.shape
    blocks_down, blocks_across = block_keep.shape
    block_side = tile_rows // blocks_down
    linked = (row_codes[:, None] == col_codes[None, :]) & (row_codes[:, None] & 1 == 1)
    linked = linked.reshape(blocks_down, block_side, blocks_across, block_side) & (
        block_keep[:, None, :, None] == 1
    )
    masked = edge_weight * linked.reshape(tile_rows, tile_cols).astype(jnp.bfloat16)
    degree_rows = 1.0 + lax.psum(jnp.sum(masked, axis=1, dtype=jnp.float32), COL)
    own_nodes = features.shape[0]
    own_degree = lax.dynamic_slice_in_dim(
        degree_rows, lax.axis_index(COL) * own_nodes, own_nodes, 0
    )
    degree_cols = lax.all_gather(own_degree, "row", axis=0, tiled=True)
    adjacency = (
        masked.astype(jnp.float32)
        * lax.rsqrt(degree_rows)[:, None]
        * lax.rsqrt(degree_cols)[None, :]
    ).astype(jnp.bfloat16)
    valid_rows = node_valid.astype(jnp.float32)
    stacked_one, mixed_one, hidden = layer_forward(
        adjacency,
        features.astype(jnp.float32),
        weight_one,
        bias_one,
        gain_one,
        shift_one,
        valid_rows,
    )
    stacked_two, mixed_two, activations = layer_forward(
        adjacency, hidden, weight_two, bias_two, gain_two, shift_two, valid_rows
    )
    hidden_grad, weight_two_grad, bias_two_grad, gain_two_grad, shift_two_grad = layer_backward(
        adjacency,
        stacked_two,
        mixed_two,
        cotangent.astype(jnp.float32),
        weight_two,
        gain_two,
        shift_two,
        valid_rows,
    )
    input_grad, weight_one_grad, bias_one_grad, gain_one_grad, shift_one_grad = layer_backward(
        adjacency, stacked_one, mixed_one, hidden_grad, weight_one, gain_one, shift_one, valid_rows
    )
    summed = lax.psum(
        (
            weight_one_grad,
            bias_one_grad,
            gain_one_grad,
            shift_one_grad,
            weight_two_grad,
            bias_two_grad,
            gain_two_grad,
            shift_two_grad,
        ),
        ("row",) + COL,
    )
    weight_one_grad, bias_one_grad, gain_one_grad, shift_one_grad = (
        summed[0],
        summed[1],
        summed[2],
        summed[3],
    )
    weight_two_grad, bias_two_grad, gain_two_grad, shift_two_grad = (
        summed[4],
        summed[5],
        summed[6],
        summed[7],
    )
    return (
        activations,
        input_grad,
        weight_one_grad,
        bias_one_grad,
        gain_one_grad,
        shift_one_grad,
        weight_two_grad,
        bias_two_grad,
        gain_two_grad,
        shift_two_grad,
    )


def local(n_row, n_col, *args):
    (
        features,
        node_valid,
        cluster,
        block_keep,
        edge_weight,
        weight_one,
        bias_one,
        gain_one,
        shift_one,
        weight_two,
        bias_two,
        gain_two,
        shift_two,
        cotangent,
    ) = args
    own_nodes, in_width = features.shape
    own_cap = own_nodes * n_row * 5 // 16
    send_cap = own_nodes * n_col * 11 // 32
    seat_cap = own_nodes // 2
    codes = broadcast_along(cluster * 2 + node_valid, ("row",) + COL, n_row * n_col)
    codes = codes.reshape(n_row, n_col, own_nodes)
    shared = (
        block_keep,
        edge_weight,
        weight_one,
        bias_one,
        gain_one,
        shift_one,
        weight_two,
        bias_two,
        gain_two,
        shift_two,
        cotangent,
    )

    def slow():
        return general(codes, features, *shared, node_valid)

    held = (ORDER - 1) * own_cap * own_cap * n_col * 2
    if held > HELD_BYTES or n_col != 4 or n_row < 2:
        return slow()
    group = assign(codes, n_row)
    member = group[None] == jnp.arange(n_row)[:, None, None, None]
    by_col = member.transpose(0, 2, 1, 3).reshape(n_row, n_col, -1)
    by_row = member.reshape(n_row, n_row, -1)
    places = jnp.sum(jnp.where(by_col, exclusive_counts(by_col), 0), axis=0)
    places = places.reshape(n_col, n_row, own_nodes).transpose(1, 0, 2)
    slots = jnp.sum(jnp.where(by_row, exclusive_counts(by_row), 0), axis=0)
    slots = slots.reshape(n_row, n_col, own_nodes)
    seats = jnp.sum(jnp.where(member, exclusive_counts(member), 0), axis=0)
    fits = (
        (jnp.max(jnp.sum(by_col, axis=2)) <= own_cap)
        & (jnp.max(jnp.sum(by_row, axis=2)) <= send_cap)
        & (jnp.max(jnp.sum(member, axis=3)) <= seat_cap)
    )
    width = weight_two.shape[2]

    def instead(state):
        made = slow()
        small = jnp.stack([made[place] for place in (3, 4, 5, 7, 8, 9)])
        return (True,) + tuple(
            value.astype(jnp.bfloat16).reshape(like.shape)
            for value, like in zip((made[0], made[1], made[2], made[6], small), state[1:])
        )

    shapes = (
        (own_nodes, width),
        (own_nodes, in_width),
        (2, n_col // 2, ORDER * in_width // n_col, width),
        (2, n_col // 2, ORDER * width // n_col, width),
        (6, width),
    )
    others = lax.while_loop(
        lambda state: jnp.logical_not(state[0]),
        instead,
        (fits,) + tuple(jnp.zeros(shape, jnp.bfloat16) for shape in shapes),
    )[1:]
    home, home_grad, first, second, small = compact(
        codes,
        group,
        features,
        *shared,
        places,
        slots,
        seats,
        fits,
        others,
        (n_row, n_col),
        (own_cap, send_cap, seat_cap),
    )
    return (
        home,
        home_grad,
        first.reshape(weight_one.shape),
        small[0],
        small[1],
        small[2],
        second.reshape(weight_two.shape),
        small[3],
        small[4],
        small[5],
    )


def solution(mesh):
    n_row, n_col = mesh.shape["row"], mesh.shape["col"]
    by_core = jax.sharding.Mesh(
        mesh.devices.reshape(n_row, n_col // 2, 2), ("row", "chip", "core")
    )
    nodes = ("row", "chip", "core")
    placed = (
        P(nodes, None),
        P(nodes),
        P(nodes),
        P("row", COL),
        P("row", COL),
        P(),
        P(),
        P(),
        P(),
        P(),
        P(),
        P(),
        P(),
        P(nodes, None),
    )
    return jax.shard_map(
        functools.partial(local, n_row, n_col),
        mesh=by_core,
        in_specs=placed,
        out_specs=(P(nodes, None), P(nodes, None), P(), P(), P(), P(), P(), P(), P(), P()),
        check_vma=False,
    )
```

```python
import functools
import math

import jax
import jax.numpy as jnp
from jax import lax
from jax.experimental import pallas as pl
from jax.experimental.pallas import tpu as pltpu
from jax.sharding import PartitionSpec as P

ORDER = 13
CLUSTERS = 16
HELD_BYTES = 1 << 25
VMEM_BYTES = 32 << 20
ALONE_BYTES = 56 << 20
TERMS = 3
NO_COST = pl.CostEstimate(flops=1, bytes_accessed=1, transcendentals=0)
COL = ("chip", "core")


def finish(mixed, gain, shift, valid_rows):
    active = jax.nn.gelu(mixed, approximate=False)
    centered = active - jnp.mean(active, axis=-1, keepdims=True)
    variance = jnp.mean(centered * centered, axis=-1, keepdims=True)
    return (centered * lax.rsqrt(variance + 1e-05) * gain + shift) * valid_rows[:, None]


def forward_product(adjacency, piece_low):
    partial_value = jnp.dot(
        adjacency,
        lax.all_gather(piece_low, "row", axis=0, tiled=True),
        preferred_element_type=jnp.float32,
    )
    return lax.psum_scatter(partial_value, COL, scatter_dimension=0, tiled=True)


def backward_product(adjacency, piece_low):
    partial_value = lax.dot_general(
        adjacency,
        lax.all_gather(piece_low, COL, axis=0, tiled=True),
        (((0,), (0,)), ((), ())),
        preferred_element_type=jnp.float32,
    )
    return lax.psum_scatter(
        partial_value.astype(jnp.bfloat16), "row", scatter_dimension=0, tiled=True
    ).astype(jnp.float32)


def layer_forward(adjacency, inputs, weight, bias, gain, shift, valid_rows):
    first_low = inputs.astype(jnp.bfloat16)
    second = -forward_product(adjacency, first_low)
    second_low = second.astype(jnp.bfloat16)

    def advance(state_pair, unused):
        previous, current, current_low = state_pair
        upcoming = -2.0 * forward_product(adjacency, current_low) - previous
        upcoming_low = upcoming.astype(jnp.bfloat16)
        return ((current, upcoming, upcoming_low), upcoming_low)

    ignored, others = lax.scan(advance, (inputs, second, second_low), None, length=ORDER - 2)
    stacked = jnp.concatenate([first_low[None], second_low[None], others], axis=0)
    mixed = jnp.einsum("kni,kio->no", stacked, weight, preferred_element_type=jnp.float32) + bias
    return (stacked, mixed, finish(mixed, gain, shift, valid_rows))


def layer_backward(adjacency, stacked, mixed, upstream, weight, gain, shift, valid_rows):

    def local_finish(mixed_in, gain_in, shift_in):
        return finish(mixed_in, gain_in, shift_in, valid_rows)

    ignored, pullback = jax.vjp(local_finish, mixed, gain, shift)
    mixed_grad, gain_grad, shift_grad = pullback(upstream)
    mixed_low = mixed_grad.astype(jnp.bfloat16)
    bias_grad = jnp.sum(mixed_low.astype(jnp.float32), axis=0)
    weight_grad = jnp.einsum("kni,no->kio", stacked, mixed_low, preferred_element_type=jnp.float32)
    direct = jnp.einsum("no,kio->kni", mixed_low, weight, preferred_element_type=jnp.float32)

    def retreat(state_pair, direct_term):
        later_two, later_one = state_pair
        current = (
            direct_term
            - 2.0 * backward_product(adjacency, later_one.astype(jnp.bfloat16))
            - later_two
        )
        return ((later_one, current), None)

    start_pair = (jnp.zeros_like(direct[0]), direct[ORDER - 1])
    (second_grad, first_grad), unused = lax.scan(
        retreat, start_pair, direct[1 : ORDER - 1], reverse=True
    )
    input_grad = (
        direct[0] - backward_product(adjacency, first_grad.astype(jnp.bfloat16)) - second_grad
    )
    return (input_grad, weight_grad, bias_grad, gain_grad, shift_grad)


def swap(value, axis):
    return lax.ppermute(value, axis, [(0, 1), (1, 0)])


def trade(pieces, axis):
    return lax.all_to_all(pieces, axis, 0, 0, tiled=False)


def broadcast_along(value, axis, size):
    return trade(jnp.broadcast_to(value[None], (size,) + value.shape), axis)


def joined(mine, other, index):
    return jnp.where(
        index == 0, jnp.concatenate([mine, other]), jnp.concatenate([other, mine])
    )


def split(pair, index):
    mine = lax.dynamic_index_in_dim(pair, index, 0, False)
    return mine, lax.dynamic_index_in_dim(pair, 1 - index, 0, False)


def added(mine, received):
    return (mine.astype(jnp.float32) + received.astype(jnp.float32)).astype(jnp.bfloat16)


def assemble(place_ref, own_ref, sibling_ref, near_ref, far_ref, out_ref, done):
    chip, core = place_ref[0], place_ref[1]
    own_cap, span = own_ref.shape
    half = span // 2

    def rows(of_chip, of_core):
        return pl.ds(pl.multiple_of((2 * of_chip + of_core) * own_cap, own_cap), own_cap)

    def fetch(source, of_chip, of_core, columns, place):
        target = out_ref.at[rows(of_chip, of_core), columns]
        return pltpu.make_async_copy(source, target, done.at[place])

    def quadrant_copies(here):
        there = 1 - here
        columns = pl.ds(there * half, half)
        return (
            fetch(near_ref, there, core, columns, 2),
            fetch(far_ref, there, 1 - core, columns, 3),
        )

    everything = pl.ds(0, span)
    top = (
        fetch(own_ref, chip, core, everything, 0),
        fetch(sibling_ref, chip, 1 - core, everything, 1),
    )

    def of_chip(here):
        there = 1 - here
        copies = top + quadrant_copies(here)
        for copy in copies:
            copy.start()
        for copy in copies:
            copy.wait()
        here_rows = pl.ds(here * half, half)
        for tile in range(half // 128):
            columns = pl.ds(there * half + tile * 128, 128)
            strip = out_ref[here_rows, columns]
            turned = jnp.transpose(strip.astype(jnp.float32)).astype(jnp.bfloat16)
            out_ref[columns, here_rows] = turned

    @pl.when(chip == 0)
    def first():
        of_chip(0)

    @pl.when(chip == 1)
    def second():
        of_chip(1)

    across = jnp.ones((1, span), jnp.float32)
    for tile in range(span // 128):
        across = across + jnp.sum(
            out_ref[pl.ds(tile * 128, 128), :].astype(jnp.float32), axis=0, keepdims=True
        )
    across = lax.rsqrt(across)
    for tile in range(span // 128):
        strip = out_ref[pl.ds(tile * 128, 128), :].astype(jnp.float32)
        down = lax.rsqrt(1.0 + jnp.sum(strip, axis=1, keepdims=True))
        out_ref[pl.ds(tile * 128, 128), :] = (strip * down * across).astype(jnp.bfloat16)


def normalized_block(own, sibling, near, far, place):
    span = own.shape[1]
    return pl.pallas_call(
        assemble,
        out_shape=jax.ShapeDtypeStruct((span, span), jnp.bfloat16),
        in_specs=[pl.BlockSpec(memory_space=pltpu.SMEM)]
        + [pl.BlockSpec(memory_space=pltpu.HBM)] * 4,
        out_specs=pl.BlockSpec(memory_space=pltpu.VMEM),
        scratch_shapes=[pltpu.SemaphoreType.DMA((4,))],
        compiler_params=pltpu.CompilerParams(vmem_limit_bytes=ALONE_BYTES),
        cost_estimate=NO_COST,
        name="normalized_block",
    )(place, own, sibling, near, far)


def pack_kernel(
    keep_ref, row_codes_ref, col_codes_ref, row_keys_ref, col_keys_ref, weight_ref, out_ref,
    masked, picked, rows_hot, cols_hot
):
    tile_rows, tile_cols = weight_ref.shape
    blocks_down, blocks_across = keep_ref.shape
    groups, ignored, lanes = out_ref.shape
    send_cap, own_cap = rows_hot.shape[0] // groups, cols_hot.shape[0] // groups
    high, wide = tile_rows // blocks_down, tile_cols // blocks_across
    for down in range(blocks_down):
        for across in range(blocks_across):
            rows, columns = pl.ds(down * high, high), pl.ds(across * wide, wide)
            own, other = row_codes_ref[rows, :], col_codes_ref[:, columns]
            linked = (own == other) & (own % 2 == 1) & (keep_ref[down, across] == 1)
            weight = weight_ref[rows, columns].astype(jnp.float32)
            masked[rows, columns] = jnp.where(linked, weight, 0.0).astype(jnp.bfloat16)

    def one_hot(keys, start, count):
        standing = lax.broadcasted_iota(jnp.int32, (count, keys.shape[1]), 0) + start
        return jnp.where(standing == keys, 1.0, 0.0).astype(jnp.bfloat16)

    for group in range(groups):
        rows_hot[pl.ds(group * send_cap, send_cap), :] = one_hot(
            row_keys_ref[...], group * send_cap, send_cap
        )
        cols_hot[pl.ds(group * own_cap, own_cap), :] = one_hot(
            col_keys_ref[...], group * own_cap, own_cap
        )
    for tile in range(tile_cols // 256):
        columns = pl.ds(tile * 256, 256)
        picked[:, columns] = jnp.dot(
            rows_hot[...], masked[:, columns], preferred_element_type=jnp.float32
        ).astype(jnp.bfloat16)
    whole, half = own_cap // lanes, send_cap // 2
    for group in range(groups):
        packed = lax.dot_general(
            picked[pl.ds(group * send_cap, send_cap), :],
            cols_hot[pl.ds(group * own_cap, own_cap), :],
            (((1,), (1,)), ((), ())),
            preferred_element_type=jnp.float32,
        )
        for tile in range(whole):
            out_ref[group, pl.ds(tile * send_cap, send_cap), :] = packed[
                :, tile * lanes : (tile + 1) * lanes
            ].astype(jnp.bfloat16)
        ends = jnp.concatenate(
            [packed[:half, whole * lanes :], packed[half:, whole * lanes :]], axis=1
        )
        out_ref[group, pl.ds(whole * send_cap, half), :] = ends.astype(jnp.bfloat16)


def packed_pieces(block_keep, row_codes, col_codes, row_keys, col_keys, edge_weight, caps, groups):
    own_cap, send_cap = caps
    tile_rows, tile_cols = edge_weight.shape
    high = own_cap // 128 * send_cap + send_cap // 2
    vector = pl.BlockSpec(memory_space=pltpu.VMEM)
    return pl.pallas_call(
        pack_kernel,
        out_shape=jax.ShapeDtypeStruct((groups, high, 128), jnp.bfloat16),
        in_specs=[pl.BlockSpec(memory_space=pltpu.SMEM)] + [vector] * 5,
        out_specs=vector,
        scratch_shapes=[
            pltpu.VMEM((tile_rows, tile_cols), jnp.bfloat16),
            pltpu.VMEM((groups * send_cap, tile_cols), jnp.bfloat16),
            pltpu.VMEM((groups * send_cap, tile_rows), jnp.bfloat16),
            pltpu.VMEM((groups * own_cap, tile_cols), jnp.bfloat16),
        ],
        compiler_params=pltpu.CompilerParams(vmem_limit_bytes=VMEM_BYTES),
        cost_estimate=NO_COST,
        name="packed_pieces",
    )(block_keep, row_codes[:, None], col_codes[None], row_keys[None], col_keys[None], edge_weight)


def normal_share(mixed):
    return 0.5 * (1.0 + lax.erf(mixed * 0.5**0.5))


def norm_forward(mixed):
    active = mixed * normal_share(mixed)
    centered = active - jnp.mean(active, axis=-1, keepdims=True)
    scale = lax.rsqrt(jnp.mean(centered * centered, axis=-1, keepdims=True) + 1e-05)
    return centered * scale, scale


def norm_backward(mixed, upstream, gain, valid):
    normed, scale = norm_forward(mixed)
    upstream = upstream * valid
    inner = upstream * gain
    inner = inner - jnp.mean(inner, axis=-1, keepdims=True) - normed * jnp.mean(
        inner * normed, axis=-1, keepdims=True
    )
    density = jnp.exp(-0.5 * mixed * mixed) * (1.0 / (2.0 * math.pi) ** 0.5)
    low = (inner * scale * (normal_share(mixed) + mixed * density)).astype(jnp.bfloat16)
    rest = [low.astype(jnp.float32), upstream * normed, upstream]
    return low, [jnp.sum(value, axis=0, keepdims=True) for value in rest]


def weight_gradient(turned_ref, low, core, mine_ref, other_ref):
    part = turned_ref.shape[0] // 4

    def halves(first_ref, second_ref):
        for place in range(4):
            out_ref = first_ref if place < 2 else second_ref
            out_ref[place % 2, :part, :] = jnp.dot(
                turned_ref[place * part : (place + 1) * part, :],
                low,
                preferred_element_type=jnp.float32,
            ).astype(jnp.bfloat16)

    @pl.when(core == 0)
    def low_half_first():
        halves(mine_ref, other_ref)

    @pl.when(core == 1)
    def high_half_first():
        halves(other_ref, mine_ref)


def fetch_terms(powers_refs, weight_ref, powers, weights, done):
    order = len(powers_refs)
    first = pltpu.make_async_copy(weight_ref.at[0], weights.at[0], done.at[2 * order])
    first.start()
    copies = []
    for term in range(order):
        rows = pltpu.make_async_copy(powers_refs[term], powers.at[term], done.at[term])
        weight = pltpu.make_async_copy(
            weight_ref.at[term + 1], weights.at[term + 1], done.at[order + term]
        )
        rows.start()
        weight.start()
        copies.append((rows, weight))

    def arrive(step):
        if step == 0:
            first.wait()
        for rows, weight in copies[step * TERMS : (step + 1) * TERMS]:
            rows.wait()
            weight.wait()

    return arrive


def product(powers, everyone, step):
    ignored, own_cap, span = powers.shape
    rows = powers[step * TERMS : (step + 1) * TERMS].reshape(TERMS * own_cap, span)
    low = jnp.dot(rows, everyone, preferred_element_type=jnp.float32).astype(jnp.bfloat16)
    return [low[term * own_cap : (term + 1) * own_cap] for term in range(TERMS)]


def forward_terms(refs, all_ref, own_ref, weight_ref, bias_ref, powers, weights, done, turned):
    arrive = fetch_terms(refs, weight_ref, powers, weights, done)
    fan_in = own_ref.shape[1]
    turned[:fan_in, :] = own_ref[...].T
    mixed = bias_ref[...]
    for step in range(len(refs) // TERMS):
        arrive(step)
        if step == 0:
            mixed = mixed + jnp.dot(own_ref[...], weights[0], preferred_element_type=jnp.float32)
        for place, low in enumerate(product(powers, all_ref[...], step)):
            term = 1 + step * TERMS + place
            turned[term * fan_in : (term + 1) * fan_in, :] = low.T
            mixed = mixed + jnp.dot(low, weights[term], preferred_element_type=jnp.float32)
    return mixed


def backward_terms(refs, all_ref, own_ref, weight_ref, powers, weights, done):
    arrive = fetch_terms(refs, weight_ref, powers, weights, done)
    transposed = (((1,), (1,)), ((), ()))

    def through(low, term):
        return lax.dot_general(
            low, weights[term], transposed, preferred_element_type=jnp.float32
        )

    total = None
    for step in range(len(refs) // TERMS):
        arrive(step)
        if step == 0:
            total = through(own_ref[...], 0)
        for place, low in enumerate(product(powers, all_ref[...], step)):
            total = total + through(low, 1 + step * TERMS + place)
    return total


def layer_one_kernel(*refs):
    terms, refs = refs[: ORDER - 1], refs[ORDER - 1 :]
    weight_ref, all_ref, own_ref, bias_ref, gain_ref, shift_ref, valid_ref = refs[:7]
    hidden_ref, turned_ref, mixed_ref, powers, weights, done = refs[7:]
    mixed = forward_terms(
        terms, all_ref, own_ref, weight_ref, bias_ref, powers, weights, done, turned_ref
    )
    mixed_ref[...] = mixed
    normed, ignored = norm_forward(mixed)
    hidden = (normed * gain_ref[...] + shift_ref[...]) * valid_ref[...]
    hidden_ref[...] = hidden.astype(jnp.bfloat16)


def layer_two_kernel(*refs):
    terms, refs = refs[: ORDER - 1], refs[ORDER - 1 :]
    weight_ref, all_ref, own_ref, bias_ref, gain_ref, shift_ref, valid_ref = refs[:7]
    upstream_ref, place_ref, active_ref, low_ref, rest_ref, mine_ref, other_ref = refs[7:14]
    powers, weights, done, turned = refs[14:]
    mixed = forward_terms(
        terms, all_ref, own_ref, weight_ref, bias_ref, powers, weights, done, turned
    )
    normed, ignored = norm_forward(mixed)
    active = (normed * gain_ref[...] + shift_ref[...]) * valid_ref[...]
    active_ref[...] = active.astype(jnp.bfloat16)
    low, rest = norm_backward(
        mixed, upstream_ref[...].astype(jnp.float32), gain_ref[...], valid_ref[...]
    )
    low_ref[...] = low
    for place in range(3):
        rest_ref[place : place + 1, :] = rest[place]
    weight_gradient(turned, low, place_ref[1], mine_ref, other_ref)


def back_two_kernel(*refs):
    terms, refs = refs[: ORDER - 1], refs[ORDER - 1 :]
    weight_ref, all_ref, own_ref, turned_ref, mixed_ref, gain_ref, valid_ref = refs[:7]
    rest_ref, place_ref, low_ref, mine_ref, other_ref, powers, weights, done = refs[7:]
    total = backward_terms(terms, all_ref, own_ref, weight_ref, powers, weights, done)
    low, rest = norm_backward(mixed_ref[...], total, gain_ref[...], valid_ref[...])
    low_ref[...] = low
    weight_gradient(turned_ref, low, place_ref[1], mine_ref, other_ref)
    part = turned_ref.shape[0] // 4
    extra = jnp.zeros((2, mine_ref.shape[1] - part, mine_ref.shape[2]), jnp.bfloat16)
    rows = rest + [rest_ref[place : place + 1, :] for place in range(3)]
    rows = jnp.concatenate(rows + [jnp.zeros((10, rows[0].shape[1]), jnp.float32)], axis=0)

    def below(first_ref, second_ref):
        first_ref[:, part:, :] = extra
        second_ref[:, part:, :] = extra
        first_ref[0, part : part + 16, :] = rows.astype(jnp.bfloat16)

    @pl.when(place_ref[1] == 0)
    def low_half_here():
        below(mine_ref, other_ref)

    @pl.when(place_ref[1] == 1)
    def low_half_there():
        below(other_ref, mine_ref)


def back_one_kernel(*refs):
    terms, refs = refs[: ORDER - 1], refs[ORDER - 1 :]
    weight_ref, all_ref, own_ref, out_ref, powers, weights, done = refs
    total = backward_terms(terms, all_ref, own_ref, weight_ref, powers, weights, done)
    out_ref[...] = total.astype(jnp.bfloat16)


def layer_pass(kernel, name, powers, weight, operands, place, outs, scratch=()):
    far, near = pl.BlockSpec(memory_space=pltpu.HBM), pl.BlockSpec(memory_space=pltpu.VMEM)
    in_specs = [far] * (len(powers) + 1) + [near] * len(operands)
    operands = list(powers) + [weight] + list(operands)
    if place is not None:
        in_specs.append(pl.BlockSpec(memory_space=pltpu.SMEM))
        operands.append(place)
    return pl.pallas_call(
        kernel,
        out_shape=outs,
        in_specs=in_specs,
        out_specs=[near] * len(outs),
        scratch_shapes=[
            pltpu.VMEM((len(powers),) + powers[0].shape, jnp.bfloat16),
            pltpu.VMEM(weight.shape, jnp.bfloat16),
            pltpu.SemaphoreType.DMA((2 * len(powers) + 1,)),
        ]
        + [pltpu.VMEM(shape, jnp.bfloat16) for shape in scratch],
        compiler_params=pltpu.CompilerParams(vmem_limit_bytes=VMEM_BYTES),
        cost_estimate=NO_COST,
        name=name,
    )(*operands)


def exclusive_counts(member):
    count = member.shape[-1]
    before = jnp.arange(count)[:, None] < jnp.arange(count)[None, :]
    return jnp.dot(
        member.astype(jnp.bfloat16),
        before.astype(jnp.bfloat16),
        preferred_element_type=jnp.float32,
    ).astype(jnp.int32)


def assign(codes, n_row):
    cluster, valid = codes >> 1, codes & 1
    labels = jnp.arange(CLUSTERS)
    sizes = jnp.sum(
        (cluster.reshape(1, -1) == labels[:, None]) & (valid.reshape(1, -1) == 1), axis=1
    )
    ahead = (sizes[None, :] > sizes[:, None]) | (
        (sizes[None, :] == sizes[:, None]) & (labels[None, :] < labels[:, None])
    )
    rank = jnp.sum(ahead, axis=1)
    others = n_row - 1
    turn, place = (rank - 1) // others, (rank - 1) % others
    group = jnp.where(rank == 0, 0, 1 + jnp.where(turn == 0, place, others - 1 - place))
    of_node = jnp.sum(
        jnp.where(cluster[None] == labels[:, None, None, None], group[:, None, None, None], 0),
        axis=0,
    )
    return jnp.where(valid == 1, of_node, n_row)


def compact(
    codes,
    group,
    features,
    block_keep,
    edge_weight,
    weight_one,
    bias_one,
    gain_one,
    shift_one,
    weight_two,
    bias_two,
    gain_two,
    shift_two,
    cotangent,
    places,
    slots,
    decide,
    sizes,
    caps,
):
    row, col = lax.axis_index("row"), lax.axis_index(COL)
    chip, core = lax.axis_index("chip"), lax.axis_index("core")
    n_row, n_col = sizes
    own_cap, send_cap, seat_cap = caps
    own_nodes, in_width = features.shape
    width = weight_two.shape[2]
    span = n_col * own_cap
    targets = jnp.arange(n_row)

    def in_col(value):
        return lax.dynamic_index_in_dim(value, col, 1, False).reshape(-1)

    def in_row(value):
        return lax.dynamic_index_in_dim(value, row, 0, False).reshape(-1)

    row_group, col_group = in_row(group), in_col(group)
    row_keys = jnp.where(in_row(slots) < send_cap, row_group * send_cap + in_row(slots), -1)
    col_keys = jnp.where(in_col(places) < own_cap, col_group * own_cap + in_col(places), -1)
    pieces = packed_pieces(
        block_keep,
        in_row(codes),
        in_col(codes),
        row_keys,
        col_keys,
        edge_weight,
        (own_cap, send_cap),
        n_row,
    )
    pieces, group, places, slots = lax.optimization_barrier((pieces, group, places, slots))
    fits, others = decide(group)
    member = group[None] == targets[:, None, None, None]
    seats = jnp.sum(jnp.where(member, exclusive_counts(member), 0), axis=0)
    pieces = trade(pieces, "row")
    whole, half_send = own_cap // 128 * 128, send_cap // 2

    standing = jnp.arange(n_col)[None, :, None] * own_cap + places
    fits_here = jnp.where(group == row, standing, -1).reshape(n_row, -1)
    slot_of = slots.reshape(n_row, -1)
    target = jnp.max(
        jnp.where(
            slot_of[:, None, :] == jnp.arange(send_cap)[None, :, None], fits_here[:, None, :], -1
        ),
        axis=2,
    )
    spread = (target[:, :, None] == jnp.arange(span)[None, None, :]).astype(jnp.bfloat16)

    group_here = lax.dynamic_index_in_dim(in_row(group).reshape(n_col, -1), col, 0, False)
    seat_here = lax.dynamic_index_in_dim(in_row(seats).reshape(n_col, -1), col, 0, False)
    leave = (group_here[None, None, :] == targets[:, None, None]) & (
        seat_here[None, None, :] == jnp.arange(seat_cap)[None, :, None]
    )
    leave = leave.astype(jnp.bfloat16).reshape(n_row * seat_cap, own_nodes)
    both = jnp.dot(leave, jnp.concatenate([features, cotangent], axis=1))
    both = both.reshape(n_row, seat_cap, -1)
    group_col = lax.dynamic_index_in_dim(group, col, 1, False)
    seats_col = lax.dynamic_index_in_dim(seats, col, 1, False)
    places_col = lax.dynamic_index_in_dim(places, col, 1, False)
    seated = (group_col == row)[:, None, :] & (
        seats_col[:, None, :] == jnp.arange(seat_cap)[None, :, None]
    )
    place_of_seat = jnp.max(jnp.where(seated, places_col[:, None, :], -1), axis=2)
    place_of_seat = place_of_seat.reshape(n_row * seat_cap)
    arrive = (place_of_seat[None, :] == jnp.arange(own_cap)[:, None]).astype(jnp.bfloat16)
    take = (place_of_seat[:, None] == jnp.arange(own_cap)[None, :]).astype(jnp.bfloat16)
    held_count = jnp.sum(group_col == row)
    valid_rows = (jnp.arange(own_cap) < held_count).astype(jnp.float32)[:, None]
    pieces, both, spread, arrive, take, valid_rows, others = lax.optimization_barrier(
        (pieces, both, spread, arrive, take, valid_rows, others)
    )

    many = whole // 128
    tiles = pieces[:, : many * send_cap].reshape(n_row, many, send_cap, 128)
    ends = pieces[:, many * send_cap :].reshape(n_row, half_send, 2, own_cap - whole)
    own_block = jnp.concatenate(
        [
            jnp.einsum("sktu,stw->kuw", tiles, spread).reshape(whole, span),
            jnp.einsum("sthu,shtw->uw", ends, spread.reshape(n_row, 2, half_send, span)),
        ]
    ).astype(jnp.bfloat16)
    quadrant = lax.dynamic_slice_in_dim(own_block, chip * (span // 2), span // 2, 1)
    quadrant = swap(quadrant, "chip")
    both = trade(both, "row")
    place = jnp.stack([chip, core]).astype(jnp.int32)
    sibling = swap(own_block, "core")
    adjacency = normalized_block(own_block, sibling, quadrant, swap(quadrant, "core"), place)
    both, adjacency = lax.optimization_barrier((both, adjacency))
    mine = jnp.dot(arrive, both.reshape(n_row * seat_cap, -1))
    features_own, cotangent_own = mine[:, :in_width], mine[:, in_width:]
    sibling = swap(features_own, "core")

    first = (col * own_cap + jnp.arange(own_cap))[:, None] == jnp.arange(span)[None, :]
    previous = first.astype(jnp.float32)
    current = -lax.dynamic_slice_in_dim(adjacency, col * own_cap, own_cap, 0).astype(jnp.float32)
    lowered = [current.astype(jnp.bfloat16)]
    for position in range(2, ORDER):
        upcoming = (
            -2.0 * jnp.dot(lowered[-1], adjacency, preferred_element_type=jnp.float32) - previous
        )
        low = upcoming.astype(jnp.bfloat16)
        if position == 4:
            low, sibling = lax.optimization_barrier((low, sibling))
            features_chip = joined(features_own, sibling, core)
            partner = swap(features_chip, "chip")
        if position == 8:
            low, partner = lax.optimization_barrier((low, partner))
            features_all = joined(features_chip, partner, chip)
        previous, current = current, upcoming
        lowered.append(low)
    powers = lowered

    def everywhere(value_low):
        return lax.all_gather(value_low, COL, axis=0, tiled=True)

    def chosen(value, other):
        return jnp.where(fits, value.astype(jnp.float32), other.astype(jnp.float32))

    def shaped(*shape, dtype=jnp.bfloat16):
        return jax.ShapeDtypeStruct(shape, dtype)

    part_one, part_two = ORDER * in_width // n_col, ORDER * width // n_col
    padded = -(-(part_one + 16) // (8 * n_row)) * (8 * n_row)
    hidden, turned_one, mixed_one = layer_pass(
        layer_one_kernel,
        "layer_one",
        powers,
        weight_one,
        [features_all, features_own, bias_one[None], gain_one[None], shift_one[None], valid_rows],
        None,
        [
            shaped(own_cap, width),
            shaped(n_col * part_one, own_cap),
            shaped(own_cap, width, dtype=jnp.float32),
        ],
    )
    activations, low_two, rest_two, mine, other = layer_pass(
        layer_two_kernel,
        "layer_two",
        powers,
        weight_two,
        [
            everywhere(hidden),
            hidden,
            bias_two[None],
            gain_two[None],
            shift_two[None],
            valid_rows,
            cotangent_own,
        ],
        place,
        [
            shaped(own_cap, width),
            shaped(own_cap, width),
            shaped(3, width, dtype=jnp.float32),
            shaped(2, part_two, width),
            shaped(2, part_two, width),
        ],
        [(n_col * part_two, own_cap)],
    )

    def add_cores(mine, other):
        got = swap(other, "core")
        (mine_here, mine_there), (got_here, got_there) = split(mine, chip), split(got, chip)
        return added(mine_here, got_here), added(mine_there, got_there)

    leaving = jnp.dot(take, activations).reshape(n_row, seat_cap, width)
    here, there = add_cores(mine, other)
    everyone_two, there, leaving = lax.optimization_barrier(
        (everywhere(low_two), there, leaving)
    )
    there = swap(there, "chip")
    back = trade(leaving, "row")
    low_one, mine, other = layer_pass(
        back_two_kernel,
        "back_two",
        powers,
        weight_two,
        [everyone_two, low_two, turned_one, mixed_one, gain_one[None], valid_rows, rest_two],
        place,
        [shaped(own_cap, width), shaped(2, padded, width), shaped(2, padded, width)],
    )
    low_one, there, back = lax.optimization_barrier((low_one, there, back))
    second = added(here, there).reshape(n_row, -1, width)
    low_one, second = lax.optimization_barrier((low_one, second))
    second = trade(second, "row")
    here, there = add_cores(mine, other)
    low_one, there = lax.optimization_barrier((low_one, there))
    everyone_one = everywhere(low_one)
    there = swap(there, "chip")
    everyone_one, second, there = lax.optimization_barrier((everyone_one, second, there))
    first = added(here, there).reshape(n_row, -1, width)
    share = first.shape[1]
    second = jnp.sum(second.astype(jnp.float32), axis=0).astype(jnp.bfloat16)
    second = jnp.broadcast_to(second[None], (n_row,) + second.shape)
    mixed = jnp.concatenate([first, second], axis=1)
    everyone_one, mixed = lax.optimization_barrier((everyone_one, mixed))
    mixed = trade(mixed, "row")
    (input_grad,) = layer_pass(
        back_one_kernel,
        "back_one",
        powers,
        weight_one,
        [everyone_one, low_one],
        None,
        [shaped(own_cap, in_width)],
    )
    leaving = jnp.dot(take, input_grad).reshape(n_row, seat_cap * in_width // width, width)
    home = jnp.dot(leave.T, back.reshape(-1, width), preferred_element_type=jnp.float32)
    mixed, leaving, home = lax.optimization_barrier((mixed, leaving, home))
    first = jnp.sum(mixed[:, :share].astype(jnp.float32), axis=0).astype(jnp.bfloat16)
    first = jnp.broadcast_to(first[None], (n_row,) + first.shape)
    first = trade(jnp.concatenate([first, leaving], axis=1), "row")
    second = lax.all_gather(mixed[:, share:].reshape(-1, width), COL, axis=0)
    back = first[:, share:].reshape(n_row * seat_cap, in_width)
    first = lax.all_gather(first[:, :share].reshape(-1, width), COL, axis=0)
    home_grad = jnp.dot(leave.T, back, preferred_element_type=jnp.float32)

    def by_core(value):
        return value.reshape(n_col // 2, 2, -1, width).swapaxes(0, 1)

    first = by_core(first)
    return (
        chosen(home, others[0]),
        chosen(home_grad, others[1]),
        chosen(first[:, :, :part_one], others[2]),
        chosen(by_core(second), others[3]),
        chosen(first[0, 0, part_one : part_one + 6], others[4]),
    )


def general(
    codes,
    features,
    block_keep,
    edge_weight,
    weight_one,
    bias_one,
    gain_one,
    shift_one,
    weight_two,
    bias_two,
    gain_two,
    shift_two,
    cotangent,
    node_valid,
):
    row, col = lax.axis_index("row"), lax.axis_index(COL)
    row_codes = lax.dynamic_index_in_dim(codes, row, 0, False).reshape(-1)
    col_codes = lax.dynamic_index_in_dim(codes, col, 1, False).reshape(-1)
    tile_rows, tile_cols = edge_weight.shape
    blocks_down, blocks_across = block_keep.shape
    block_side = tile_rows // blocks_down
    linked = (row_codes[:, None] == col_codes[None, :]) & (row_codes[:, None] & 1 == 1)
    linked = linked.reshape(blocks_down, block_side, blocks_across, block_side) & (
        block_keep[:, None, :, None] == 1
    )
    masked = edge_weight * linked.reshape(tile_rows, tile_cols).astype(jnp.bfloat16)
    degree_rows = 1.0 + lax.psum(jnp.sum(masked, axis=1, dtype=jnp.float32), COL)
    own_nodes = features.shape[0]
    own_degree = lax.dynamic_slice_in_dim(
        degree_rows, lax.axis_index(COL) * own_nodes, own_nodes, 0
    )
    degree_cols = lax.all_gather(own_degree, "row", axis=0, tiled=True)
    adjacency = (
        masked.astype(jnp.float32)
        * lax.rsqrt(degree_rows)[:, None]
        * lax.rsqrt(degree_cols)[None, :]
    ).astype(jnp.bfloat16)
    valid_rows = node_valid.astype(jnp.float32)
    stacked_one, mixed_one, hidden = layer_forward(
        adjacency,
        features.astype(jnp.float32),
        weight_one,
        bias_one,
        gain_one,
        shift_one,
        valid_rows,
    )
    stacked_two, mixed_two, activations = layer_forward(
        adjacency, hidden, weight_two, bias_two, gain_two, shift_two, valid_rows
    )
    hidden_grad, weight_two_grad, bias_two_grad, gain_two_grad, shift_two_grad = layer_backward(
        adjacency,
        stacked_two,
        mixed_two,
        cotangent.astype(jnp.float32),
        weight_two,
        gain_two,
        shift_two,
        valid_rows,
    )
    input_grad, weight_one_grad, bias_one_grad, gain_one_grad, shift_one_grad = layer_backward(
        adjacency, stacked_one, mixed_one, hidden_grad, weight_one, gain_one, shift_one, valid_rows
    )
    summed = lax.psum(
        (
            weight_one_grad,
            bias_one_grad,
            gain_one_grad,
            shift_one_grad,
            weight_two_grad,
            bias_two_grad,
            gain_two_grad,
            shift_two_grad,
        ),
        ("row",) + COL,
    )
    weight_one_grad, bias_one_grad, gain_one_grad, shift_one_grad = (
        summed[0],
        summed[1],
        summed[2],
        summed[3],
    )
    weight_two_grad, bias_two_grad, gain_two_grad, shift_two_grad = (
        summed[4],
        summed[5],
        summed[6],
        summed[7],
    )
    return (
        activations,
        input_grad,
        weight_one_grad,
        bias_one_grad,
        gain_one_grad,
        shift_one_grad,
        weight_two_grad,
        bias_two_grad,
        gain_two_grad,
        shift_two_grad,
    )


def local(n_row, n_col, *args):
    (
        features,
        node_valid,
        cluster,
        block_keep,
        edge_weight,
        weight_one,
        bias_one,
        gain_one,
        shift_one,
        weight_two,
        bias_two,
        gain_two,
        shift_two,
        cotangent,
    ) = args
    own_nodes, in_width = features.shape
    own_cap = own_nodes * n_row * 5 // 16
    send_cap = own_nodes * n_col * 11 // 32
    seat_cap = own_nodes // 2
    codes = broadcast_along(cluster * 2 + node_valid, ("row",) + COL, n_row * n_col)
    codes = codes.reshape(n_row, n_col, own_nodes)
    shared = (
        block_keep,
        edge_weight,
        weight_one,
        bias_one,
        gain_one,
        shift_one,
        weight_two,
        bias_two,
        gain_two,
        shift_two,
        cotangent,
    )

    def slow():
        return general(codes, features, *shared, node_valid)

    held = (ORDER - 1) * own_cap * own_cap * n_col * 2
    if held > HELD_BYTES or n_col != 4 or n_row < 2:
        return slow()
    group = assign(codes, n_row)
    member = group[None] == jnp.arange(n_row)[:, None, None, None]
    by_col = member.transpose(0, 2, 1, 3).reshape(n_row, n_col, -1)
    by_row = member.reshape(n_row, n_row, -1)
    places = jnp.sum(jnp.where(by_col, exclusive_counts(by_col), 0), axis=0)
    places = places.reshape(n_col, n_row, own_nodes).transpose(1, 0, 2)
    slots = jnp.sum(jnp.where(by_row, exclusive_counts(by_row), 0), axis=0)
    slots = slots.reshape(n_row, n_col, own_nodes)
    width = weight_two.shape[2]

    def instead(state):
        made = slow()
        small = jnp.stack([made[place] for place in (3, 4, 5, 7, 8, 9)])
        return (True,) + tuple(
            value.astype(jnp.bfloat16).reshape(like.shape)
            for value, like in zip((made[0], made[1], made[2], made[6], small), state[1:])
        )

    shapes = (
        (own_nodes, width),
        (own_nodes, in_width),
        (2, n_col // 2, ORDER * in_width // n_col, width),
        (2, n_col // 2, ORDER * width // n_col, width),
        (6, width),
    )

    def decide(group):
        member = group[None] == jnp.arange(n_row)[:, None, None, None]
        fits = (
            (jnp.max(jnp.sum(member, axis=(1, 3))) <= own_cap)
            & (jnp.max(jnp.sum(member, axis=(2, 3))) <= send_cap)
            & (jnp.max(jnp.sum(member, axis=3)) <= seat_cap)
        )
        others = lax.while_loop(
            lambda state: jnp.logical_not(state[0]),
            instead,
            (fits,) + tuple(jnp.zeros(shape, jnp.bfloat16) for shape in shapes),
        )[1:]
        return fits, others

    home, home_grad, first, second, small = compact(
        codes,
        group,
        features,
        *shared,
        places,
        slots,
        decide,
        (n_row, n_col),
        (own_cap, send_cap, seat_cap),
    )
    return (
        home,
        home_grad,
        first.reshape(weight_one.shape),
        small[0],
        small[1],
        small[2],
        second.reshape(weight_two.shape),
        small[3],
        small[4],
        small[5],
    )


def solution(mesh):
    n_row, n_col = mesh.shape["row"], mesh.shape["col"]
    by_core = jax.sharding.Mesh(
        mesh.devices.reshape(n_row, n_col // 2, 2), ("row", "chip", "core")
    )
    nodes = ("row", "chip", "core")
    placed = (
        P(nodes, None),
        P(nodes),
        P(nodes),
        P("row", COL),
        P("row", COL),
        P(),
        P(),
        P(),
        P(),
        P(),
        P(),
        P(),
        P(),
        P(nodes, None),
    )
    return jax.shard_map(
        functools.partial(local, n_row, n_col),
        mesh=by_core,
        in_specs=placed,
        out_specs=(P(nodes, None), P(nodes, None), P(), P(), P(), P(), P(), P(), P(), P()),
        check_vma=False,
    )
```

```python
import functools
import math

import jax
import jax.numpy as jnp
from jax import lax
from jax.experimental import pallas as pl
from jax.experimental.pallas import tpu as pltpu
from jax.sharding import PartitionSpec as P

ORDER = 13
CLUSTERS = 16
HELD_BYTES = 1 << 25
VMEM_BYTES = 32 << 20
TERMS = 3
NO_COST = pl.CostEstimate(flops=1, bytes_accessed=1, transcendentals=0)
COL = ("chip", "core")


def finish(mixed, gain, shift, valid_rows):
    active = jax.nn.gelu(mixed, approximate=False)
    centered = active - jnp.mean(active, axis=-1, keepdims=True)
    variance = jnp.mean(centered * centered, axis=-1, keepdims=True)
    return (centered * lax.rsqrt(variance + 1e-05) * gain + shift) * valid_rows[:, None]


def forward_product(adjacency, piece_low):
    partial_value = jnp.dot(
        adjacency,
        lax.all_gather(piece_low, "row", axis=0, tiled=True),
        preferred_element_type=jnp.float32,
    )
    return lax.psum_scatter(partial_value, COL, scatter_dimension=0, tiled=True)


def backward_product(adjacency, piece_low):
    partial_value = lax.dot_general(
        adjacency,
        lax.all_gather(piece_low, COL, axis=0, tiled=True),
        (((0,), (0,)), ((), ())),
        preferred_element_type=jnp.float32,
    )
    return lax.psum_scatter(
        partial_value.astype(jnp.bfloat16), "row", scatter_dimension=0, tiled=True
    ).astype(jnp.float32)


def layer_forward(adjacency, inputs, weight, bias, gain, shift, valid_rows):
    first_low = inputs.astype(jnp.bfloat16)
    second = -forward_product(adjacency, first_low)
    second_low = second.astype(jnp.bfloat16)

    def advance(state_pair, unused):
        previous, current, current_low = state_pair
        upcoming = -2.0 * forward_product(adjacency, current_low) - previous
        upcoming_low = upcoming.astype(jnp.bfloat16)
        return ((current, upcoming, upcoming_low), upcoming_low)

    ignored, others = lax.scan(advance, (inputs, second, second_low), None, length=ORDER - 2)
    stacked = jnp.concatenate([first_low[None], second_low[None], others], axis=0)
    mixed = jnp.einsum("kni,kio->no", stacked, weight, preferred_element_type=jnp.float32) + bias
    return (stacked, mixed, finish(mixed, gain, shift, valid_rows))


def layer_backward(adjacency, stacked, mixed, upstream, weight, gain, shift, valid_rows):

    def local_finish(mixed_in, gain_in, shift_in):
        return finish(mixed_in, gain_in, shift_in, valid_rows)

    ignored, pullback = jax.vjp(local_finish, mixed, gain, shift)
    mixed_grad, gain_grad, shift_grad = pullback(upstream)
    mixed_low = mixed_grad.astype(jnp.bfloat16)
    bias_grad = jnp.sum(mixed_low.astype(jnp.float32), axis=0)
    weight_grad = jnp.einsum("kni,no->kio", stacked, mixed_low, preferred_element_type=jnp.float32)
    direct = jnp.einsum("no,kio->kni", mixed_low, weight, preferred_element_type=jnp.float32)

    def retreat(state_pair, direct_term):
        later_two, later_one = state_pair
        current = (
            direct_term
            - 2.0 * backward_product(adjacency, later_one.astype(jnp.bfloat16))
            - later_two
        )
        return ((later_one, current), None)

    start_pair = (jnp.zeros_like(direct[0]), direct[ORDER - 1])
    (second_grad, first_grad), unused = lax.scan(
        retreat, start_pair, direct[1 : ORDER - 1], reverse=True
    )
    input_grad = (
        direct[0] - backward_product(adjacency, first_grad.astype(jnp.bfloat16)) - second_grad
    )
    return (input_grad, weight_grad, bias_grad, gain_grad, shift_grad)


def swap(value, axis):
    return lax.ppermute(value, axis, [(0, 1), (1, 0)])


def trade(pieces, axis):
    return lax.all_to_all(pieces, axis, 0, 0, tiled=False)


def broadcast_along(value, axis, size):
    return trade(jnp.broadcast_to(value[None], (size,) + value.shape), axis)


def joined(mine, other, index):
    return jnp.where(
        index == 0, jnp.concatenate([mine, other]), jnp.concatenate([other, mine])
    )


def split(pair, index):
    mine = lax.dynamic_index_in_dim(pair, index, 0, False)
    return mine, lax.dynamic_index_in_dim(pair, 1 - index, 0, False)


def added(mine, received):
    return (mine.astype(jnp.float32) + received.astype(jnp.float32)).astype(jnp.bfloat16)


def assemble(place_ref, own_ref, sibling_ref, near_ref, far_ref, out_ref, done):
    chip, core = place_ref[0], place_ref[1]
    own_cap, span = own_ref.shape
    half = span // 2

    def rows(of_chip, of_core):
        return pl.ds(pl.multiple_of((2 * of_chip + of_core) * own_cap, own_cap), own_cap)

    def fetch(source, of_chip, of_core, columns, place):
        target = out_ref.at[rows(of_chip, of_core), columns]
        return pltpu.make_async_copy(source, target, done.at[place])

    def quadrant_copies(here):
        there = 1 - here
        columns = pl.ds(there * half, half)
        return (
            fetch(near_ref, there, core, columns, 2),
            fetch(far_ref, there, 1 - core, columns, 3),
        )

    everything = pl.ds(0, span)
    top = (
        fetch(own_ref, chip, core, everything, 0),
        fetch(sibling_ref, chip, 1 - core, everything, 1),
    )

    def of_chip(here):
        there = 1 - here
        copies = top + quadrant_copies(here)
        for copy in copies:
            copy.start()
        for copy in copies:
            copy.wait()
        here_rows = pl.ds(here * half, half)
        for tile in range(half // 128):
            columns = pl.ds(there * half + tile * 128, 128)
            strip = out_ref[here_rows, columns]
            turned = jnp.transpose(strip.astype(jnp.float32)).astype(jnp.bfloat16)
            out_ref[columns, here_rows] = turned

    @pl.when(chip == 0)
    def first():
        of_chip(0)

    @pl.when(chip == 1)
    def second():
        of_chip(1)

    across = jnp.ones((1, span), jnp.float32)
    for tile in range(span // 128):
        across = across + jnp.sum(
            out_ref[pl.ds(tile * 128, 128), :].astype(jnp.float32), axis=0, keepdims=True
        )
    across = lax.rsqrt(across)
    for tile in range(span // 128):
        strip = out_ref[pl.ds(tile * 128, 128), :].astype(jnp.float32)
        down = lax.rsqrt(1.0 + jnp.sum(strip, axis=1, keepdims=True))
        out_ref[pl.ds(tile * 128, 128), :] = (strip * down * across).astype(jnp.bfloat16)


def normalized_block(own, sibling, near, far, place):
    span = own.shape[1]
    return pl.pallas_call(
        assemble,
        out_shape=jax.ShapeDtypeStruct((span, span), jnp.bfloat16),
        in_specs=[pl.BlockSpec(memory_space=pltpu.SMEM)]
        + [pl.BlockSpec(memory_space=pltpu.HBM)] * 4,
        out_specs=pl.BlockSpec(memory_space=pltpu.VMEM),
        scratch_shapes=[pltpu.SemaphoreType.DMA((4,))],
        compiler_params=pltpu.CompilerParams(vmem_limit_bytes=VMEM_BYTES),
        cost_estimate=NO_COST,
        name="normalized_block",
    )(place, own, sibling, near, far)


def pack_kernel(
    keep_ref, row_codes_ref, col_codes_ref, row_keys_ref, col_keys_ref, weight_ref, out_ref,
    masked, picked, rows_hot, cols_hot
):
    tile_rows, tile_cols = weight_ref.shape
    blocks_down, blocks_across = keep_ref.shape
    groups, ignored, lanes = out_ref.shape
    send_cap, own_cap = rows_hot.shape[0] // groups, cols_hot.shape[0] // groups
    high, wide = tile_rows // blocks_down, tile_cols // blocks_across
    for down in range(blocks_down):
        for across in range(blocks_across):
            rows, columns = pl.ds(down * high, high), pl.ds(across * wide, wide)
            own, other = row_codes_ref[rows, :], col_codes_ref[:, columns]
            linked = (own == other) & (own % 2 == 1) & (keep_ref[down, across] == 1)
            weight = weight_ref[rows, columns].astype(jnp.float32)
            masked[rows, columns] = jnp.where(linked, weight, 0.0).astype(jnp.bfloat16)

    def one_hot(keys, start, count):
        standing = lax.broadcasted_iota(jnp.int32, (count, keys.shape[1]), 0) + start
        return jnp.where(standing == keys, 1.0, 0.0).astype(jnp.bfloat16)

    for group in range(groups):
        rows_hot[pl.ds(group * send_cap, send_cap), :] = one_hot(
            row_keys_ref[...], group * send_cap, send_cap
        )
        cols_hot[pl.ds(group * own_cap, own_cap), :] = one_hot(
            col_keys_ref[...], group * own_cap, own_cap
        )
    for tile in range(tile_cols // 256):
        columns = pl.ds(tile * 256, 256)
        picked[:, columns] = jnp.dot(
            rows_hot[...], masked[:, columns], preferred_element_type=jnp.float32
        ).astype(jnp.bfloat16)
    whole, half = own_cap // lanes, send_cap // 2
    for group in range(groups):
        packed = lax.dot_general(
            picked[pl.ds(group * send_cap, send_cap), :],
            cols_hot[pl.ds(group * own_cap, own_cap), :],
            (((1,), (1,)), ((), ())),
            preferred_element_type=jnp.float32,
        )
        for tile in range(whole):
            out_ref[group, pl.ds(tile * send_cap, send_cap), :] = packed[
                :, tile * lanes : (tile + 1) * lanes
            ].astype(jnp.bfloat16)
        ends = jnp.concatenate(
            [packed[:half, whole * lanes :], packed[half:, whole * lanes :]], axis=1
        )
        out_ref[group, pl.ds(whole * send_cap, half), :] = ends.astype(jnp.bfloat16)


def packed_pieces(block_keep, row_codes, col_codes, row_keys, col_keys, edge_weight, caps, groups):
    own_cap, send_cap = caps
    tile_rows, tile_cols = edge_weight.shape
    high = own_cap // 128 * send_cap + send_cap // 2
    vector = pl.BlockSpec(memory_space=pltpu.VMEM)
    return pl.pallas_call(
        pack_kernel,
        out_shape=jax.ShapeDtypeStruct((groups, high, 128), jnp.bfloat16),
        in_specs=[pl.BlockSpec(memory_space=pltpu.SMEM)] + [vector] * 5,
        out_specs=vector,
        scratch_shapes=[
            pltpu.VMEM((tile_rows, tile_cols), jnp.bfloat16),
            pltpu.VMEM((groups * send_cap, tile_cols), jnp.bfloat16),
            pltpu.VMEM((groups * send_cap, tile_rows), jnp.bfloat16),
            pltpu.VMEM((groups * own_cap, tile_cols), jnp.bfloat16),
        ],
        compiler_params=pltpu.CompilerParams(vmem_limit_bytes=VMEM_BYTES),
        cost_estimate=NO_COST,
        name="packed_pieces",
    )(block_keep, row_codes[:, None], col_codes[None], row_keys[None], col_keys[None], edge_weight)


def normal_share(mixed):
    return 0.5 * (1.0 + lax.erf(mixed * 0.5**0.5))


def norm_forward(mixed):
    active = mixed * normal_share(mixed)
    centered = active - jnp.mean(active, axis=-1, keepdims=True)
    scale = lax.rsqrt(jnp.mean(centered * centered, axis=-1, keepdims=True) + 1e-05)
    return centered * scale, scale


def norm_backward(mixed, upstream, gain, valid):
    normed, scale = norm_forward(mixed)
    upstream = upstream * valid
    inner = upstream * gain
    inner = inner - jnp.mean(inner, axis=-1, keepdims=True) - normed * jnp.mean(
        inner * normed, axis=-1, keepdims=True
    )
    density = jnp.exp(-0.5 * mixed * mixed) * (1.0 / (2.0 * math.pi) ** 0.5)
    low = (inner * scale * (normal_share(mixed) + mixed * density)).astype(jnp.bfloat16)
    rest = [low.astype(jnp.float32), upstream * normed, upstream]
    return low, [jnp.sum(value, axis=0, keepdims=True) for value in rest]


def weight_gradient(turned_ref, low, core, mine_ref, other_ref):
    part = turned_ref.shape[0] // 4

    def halves(first_ref, second_ref):
        for place in range(4):
            out_ref = first_ref if place < 2 else second_ref
            out_ref[place % 2, :part, :] = jnp.dot(
                turned_ref[place * part : (place + 1) * part, :],
                low,
                preferred_element_type=jnp.float32,
            ).astype(jnp.bfloat16)

    @pl.when(core == 0)
    def low_half_first():
        halves(mine_ref, other_ref)

    @pl.when(core == 1)
    def high_half_first():
        halves(other_ref, mine_ref)


def forward_step(step, powers_ref, all_ref, own_ref, weights, bias_ref, turned, mixed):
    terms, own_cap, span = powers_ref.shape
    fan_in = own_ref.shape[1]

    @pl.when(step == 0)
    def first():
        turned[:fan_in, :] = own_ref[...].T
        mixed[...] = bias_ref[...] + jnp.dot(
            own_ref[...], weights[0][0], preferred_element_type=jnp.float32
        )

    low = jnp.dot(
        powers_ref[...].reshape(terms * own_cap, span),
        all_ref[...],
        preferred_element_type=jnp.float32,
    ).astype(jnp.bfloat16)
    total = mixed[...]
    for term in range(terms):
        part = low[term * own_cap : (term + 1) * own_cap]
        start = pl.multiple_of((1 + step * terms + term) * fan_in, fan_in)
        turned[pl.ds(start, fan_in), :] = part.T
        total = total + jnp.dot(part, weights[1 + term][0], preferred_element_type=jnp.float32)
    mixed[...] = total


def layer_one_kernel(
    powers_ref,
    all_ref,
    own_ref,
    weight_0,
    weight_a,
    weight_b,
    weight_c,
    bias_ref,
    gain_ref,
    shift_ref,
    valid_ref,
    hidden_ref,
    turned_ref,
    mixed_ref,
):
    step = pl.program_id(0)
    weights = (weight_0, weight_a, weight_b, weight_c)
    forward_step(step, powers_ref, all_ref, own_ref, weights, bias_ref, turned_ref, mixed_ref)

    @pl.when(step == pl.num_programs(0) - 1)
    def finish_layer():
        normed, ignored = norm_forward(mixed_ref[...])
        hidden = (normed * gain_ref[...] + shift_ref[...]) * valid_ref[...]
        hidden_ref[...] = hidden.astype(jnp.bfloat16)


def layer_two_kernel(
    place_ref,
    powers_ref,
    all_ref,
    own_ref,
    weight_0,
    weight_a,
    weight_b,
    weight_c,
    bias_ref,
    gain_ref,
    shift_ref,
    valid_ref,
    upstream_ref,
    active_ref,
    low_ref,
    rest_ref,
    mine_ref,
    other_ref,
    turned,
    mixed,
):
    step = pl.program_id(0)
    weights = (weight_0, weight_a, weight_b, weight_c)
    forward_step(step, powers_ref, all_ref, own_ref, weights, bias_ref, turned, mixed)

    @pl.when(step == pl.num_programs(0) - 1)
    def finish_layer():
        normed, ignored = norm_forward(mixed[...])
        active = (normed * gain_ref[...] + shift_ref[...]) * valid_ref[...]
        active_ref[...] = active.astype(jnp.bfloat16)
        low, rest = norm_backward(
            mixed[...], upstream_ref[...].astype(jnp.float32), gain_ref[...], valid_ref[...]
        )
        low_ref[...] = low
        for place in range(3):
            rest_ref[place : place + 1, :] = rest[place]
        weight_gradient(turned, low, place_ref[1], mine_ref, other_ref)


def backward_step(step, powers_ref, all_ref, own_ref, weights, total):
    terms, own_cap, span = powers_ref.shape
    transposed = (((1,), (1,)), ((), ()))

    @pl.when(step == 0)
    def first():
        total[...] = lax.dot_general(
            own_ref[...], weights[0][0], transposed, preferred_element_type=jnp.float32
        )

    low = jnp.dot(
        powers_ref[...].reshape(terms * own_cap, span),
        all_ref[...],
        preferred_element_type=jnp.float32,
    ).astype(jnp.bfloat16)
    value = total[...]
    for term in range(terms):
        value = value + lax.dot_general(
            low[term * own_cap : (term + 1) * own_cap],
            weights[1 + term][0],
            transposed,
            preferred_element_type=jnp.float32,
        )
    total[...] = value


def back_two_kernel(
    place_ref,
    powers_ref,
    all_ref,
    own_ref,
    weight_0,
    weight_a,
    weight_b,
    weight_c,
    turned_ref,
    mixed_ref,
    gain_ref,
    valid_ref,
    rest_ref,
    low_ref,
    mine_ref,
    other_ref,
    total,
):
    step = pl.program_id(0)
    weights = (weight_0, weight_a, weight_b, weight_c)
    backward_step(step, powers_ref, all_ref, own_ref, weights, total)

    @pl.when(step == pl.num_programs(0) - 1)
    def finish_layer():
        low, rest = norm_backward(mixed_ref[...], total[...], gain_ref[...], valid_ref[...])
        low_ref[...] = low
        weight_gradient(turned_ref, low, place_ref[1], mine_ref, other_ref)
        part = turned_ref.shape[0] // 4
        extra = jnp.zeros((2, mine_ref.shape[1] - part, mine_ref.shape[2]), jnp.bfloat16)
        rows = rest + [rest_ref[place : place + 1, :] for place in range(3)]
        rows = jnp.concatenate(rows + [jnp.zeros((10, rows[0].shape[1]), jnp.float32)], axis=0)

        def below(first_ref, second_ref):
            first_ref[:, part:, :] = extra
            second_ref[:, part:, :] = extra
            first_ref[0, part : part + 16, :] = rows.astype(jnp.bfloat16)

        @pl.when(place_ref[1] == 0)
        def low_half_here():
            below(mine_ref, other_ref)

        @pl.when(place_ref[1] == 1)
        def low_half_there():
            below(other_ref, mine_ref)


def back_one_kernel(
    powers_ref, all_ref, own_ref, weight_0, weight_a, weight_b, weight_c, out_ref, total
):
    step = pl.program_id(0)
    weights = (weight_0, weight_a, weight_b, weight_c)
    backward_step(step, powers_ref, all_ref, own_ref, weights, total)

    @pl.when(step == pl.num_programs(0) - 1)
    def finish_layer():
        out_ref[...] = total[...].astype(jnp.bfloat16)


def layer_pass(kernel, name, place, powers, everyone, own, weight, others, outs, scratch):
    ignored, own_cap, span = powers.shape
    fan_in, width = weight.shape[1:]

    def whole(value):
        return pl.BlockSpec(value.shape, lambda step: (0,) * len(value.shape))

    def term_weight(term):
        return pl.BlockSpec((1, fan_in, width), lambda step: (1 + step * TERMS + term, 0, 0))

    in_specs = [
        pl.BlockSpec((TERMS, own_cap, span), lambda step: (step, 0, 0)),
        whole(everyone),
        whole(own),
        pl.BlockSpec((1, fan_in, width), lambda step: (0, 0, 0)),
    ]
    in_specs += [term_weight(term) for term in range(TERMS)] + [whole(value) for value in others]
    operands = [powers, everyone, own] + [weight] * (1 + TERMS) + list(others)
    if place is not None:
        in_specs = [pl.BlockSpec(memory_space=pltpu.SMEM)] + in_specs
        operands = [place] + operands
    return pl.pallas_call(
        kernel,
        grid=((ORDER - 1) // TERMS,),
        out_shape=outs,
        in_specs=in_specs,
        out_specs=[whole(value) for value in outs],
        scratch_shapes=[pltpu.VMEM(shape, dtype) for shape, dtype in scratch],
        compiler_params=pltpu.CompilerParams(vmem_limit_bytes=VMEM_BYTES),
        cost_estimate=NO_COST,
        name=name,
    )(*operands)


def exclusive_counts(member):
    count = member.shape[-1]
    before = jnp.arange(count)[:, None] < jnp.arange(count)[None, :]
    return jnp.dot(
        member.astype(jnp.bfloat16),
        before.astype(jnp.bfloat16),
        preferred_element_type=jnp.float32,
    ).astype(jnp.int32)


def assign(codes, n_row):
    cluster, valid = codes >> 1, codes & 1
    labels = jnp.arange(CLUSTERS)
    sizes = jnp.sum(
        (cluster.reshape(1, -1) == labels[:, None]) & (valid.reshape(1, -1) == 1), axis=1
    )
    ahead = (sizes[None, :] > sizes[:, None]) | (
        (sizes[None, :] == sizes[:, None]) & (labels[None, :] < labels[:, None])
    )
    rank = jnp.sum(ahead, axis=1)
    others = n_row - 1
    turn, place = (rank - 1) // others, (rank - 1) % others
    group = jnp.where(rank == 0, 0, 1 + jnp.where(turn == 0, place, others - 1 - place))
    of_node = jnp.sum(
        jnp.where(cluster[None] == labels[:, None, None, None], group[:, None, None, None], 0),
        axis=0,
    )
    return jnp.where(valid == 1, of_node, n_row)


def compact(
    codes,
    group,
    features,
    block_keep,
    edge_weight,
    weight_one,
    bias_one,
    gain_one,
    shift_one,
    weight_two,
    bias_two,
    gain_two,
    shift_two,
    cotangent,
    places_of,
    slots_of,
    seats_of,
    decide,
    sizes,
    caps,
):
    row, col = lax.axis_index("row"), lax.axis_index(COL)
    chip, core = lax.axis_index("chip"), lax.axis_index("core")
    n_row, n_col = sizes
    own_cap, send_cap, seat_cap = caps
    own_nodes, in_width = features.shape
    width = weight_two.shape[2]
    span = n_col * own_cap
    targets = jnp.arange(n_row)

    def in_col(value):
        return lax.dynamic_index_in_dim(value, col, 1, False).reshape(-1)

    def in_row(value):
        return lax.dynamic_index_in_dim(value, row, 0, False).reshape(-1)

    row_group, col_group = in_row(group), in_col(group)
    row_slots, col_places = in_row(slots_of(group)), in_col(places_of(group))
    row_keys = jnp.where(row_slots < send_cap, row_group * send_cap + row_slots, -1)
    col_keys = jnp.where(col_places < own_cap, col_group * own_cap + col_places, -1)
    pieces = packed_pieces(
        block_keep,
        in_row(codes),
        in_col(codes),
        row_keys,
        col_keys,
        edge_weight,
        (own_cap, send_cap),
        n_row,
    )
    pieces, group = lax.optimization_barrier((pieces, group))
    pieces = trade(pieces, "row")
    whole, half_send = own_cap // 128 * 128, send_cap // 2
    fits, others = decide(group)
    places, slots, seats = places_of(group), slots_of(group), seats_of(group)

    standing = jnp.arange(n_col)[None, :, None] * own_cap + places
    fits_here = jnp.where(group == row, standing, -1).reshape(n_row, -1)
    slot_of = slots.reshape(n_row, -1)
    target = jnp.max(
        jnp.where(
            slot_of[:, None, :] == jnp.arange(send_cap)[None, :, None], fits_here[:, None, :], -1
        ),
        axis=2,
    )
    spread = (target[:, :, None] == jnp.arange(span)[None, None, :]).astype(jnp.bfloat16)

    partners = row ^ targets
    group_here = lax.dynamic_index_in_dim(in_row(group).reshape(n_col, -1), col, 0, False)
    seat_here = lax.dynamic_index_in_dim(in_row(seats).reshape(n_col, -1), col, 0, False)

    def seat_of_node(groups):
        hot = (group_here[None, None, :] == groups[:, None, None]) & (
            seat_here[None, None, :] == jnp.arange(seat_cap)[None, :, None]
        )
        return hot.astype(jnp.bfloat16).reshape(n_row * seat_cap, own_nodes)

    both = jnp.dot(seat_of_node(partners), jnp.concatenate([features, cotangent], axis=1))
    both = both.reshape(n_row, seat_cap, -1)
    enter_home = seat_of_node(targets).T
    group_col = lax.dynamic_index_in_dim(group, col, 1, False)
    seats_col = lax.dynamic_index_in_dim(seats, col, 1, False)
    places_col = lax.dynamic_index_in_dim(places, col, 1, False)
    seated = (group_col == row)[:, None, :] & (
        seats_col[:, None, :] == jnp.arange(seat_cap)[None, :, None]
    )
    place_of_seat = jnp.max(jnp.where(seated, places_col[:, None, :], -1), axis=2)
    from_partner = jnp.max(
        jnp.where((partners[:, None] == targets)[:, :, None], place_of_seat[None], -1), axis=1
    )
    arrive = from_partner.reshape(1, -1) == jnp.arange(own_cap)[:, None]
    arrive = arrive.astype(jnp.bfloat16)
    leave_group = place_of_seat.reshape(-1, 1) == jnp.arange(own_cap)[None, :]
    leave_group = leave_group.astype(jnp.bfloat16)
    held_count = jnp.sum(group_col == row)
    valid_rows = (jnp.arange(own_cap) < held_count).astype(jnp.float32)[:, None]
    pieces, both, spread, arrive, leave_group, enter_home, valid_rows, others = (
        lax.optimization_barrier(
            (pieces, both, spread, arrive, leave_group, enter_home, valid_rows, others)
        )
    )

    many = whole // 128
    tiles = pieces[:, : many * send_cap].reshape(n_row, many, send_cap, 128)
    ends = pieces[:, many * send_cap :].reshape(n_row, half_send, 2, own_cap - whole)
    own_block = jnp.concatenate(
        [
            jnp.einsum("sktu,stw->kuw", tiles, spread).reshape(whole, span),
            jnp.einsum("sthu,shtw->uw", ends, spread.reshape(n_row, 2, half_send, span)),
        ]
    ).astype(jnp.bfloat16)
    quadrant = lax.dynamic_slice_in_dim(own_block, chip * (span // 2), span // 2, 1)
    quadrant = swap(quadrant, "chip")
    both = [both[0]] + [
        lax.ppermute(both[step], "row", [(place, place ^ step) for place in range(n_row)])
        for step in range(1, n_row)
    ]
    place = jnp.stack([chip, core]).astype(jnp.int32)
    sibling = swap(own_block, "core")
    adjacency = normalized_block(own_block, sibling, quadrant, swap(quadrant, "core"), place)
    both, adjacency = lax.optimization_barrier((both, adjacency))
    mine = jnp.dot(arrive, jnp.concatenate(both))
    features_own, cotangent_own = mine[:, :in_width], mine[:, in_width:]
    sibling = swap(features_own, "core")

    first = (col * own_cap + jnp.arange(own_cap))[:, None] == jnp.arange(span)[None, :]
    previous = first.astype(jnp.float32)
    current = -lax.dynamic_slice_in_dim(adjacency, col * own_cap, own_cap, 0).astype(jnp.float32)
    lowered = [current.astype(jnp.bfloat16)]
    for position in range(2, ORDER):
        upcoming = (
            -2.0 * jnp.dot(lowered[-1], adjacency, preferred_element_type=jnp.float32) - previous
        )
        low = upcoming.astype(jnp.bfloat16)
        if position == 4:
            low, sibling = lax.optimization_barrier((low, sibling))
            features_chip = joined(features_own, sibling, core)
            partner = swap(features_chip, "chip")
        if position == 8:
            low, partner = lax.optimization_barrier((low, partner))
            features_all = joined(features_chip, partner, chip)
        previous, current = current, upcoming
        lowered.append(low)
    powers = jnp.concatenate(lowered, axis=0).reshape(ORDER - 1, own_cap, span)

    def everywhere(value_low):
        return lax.all_gather(value_low, COL, axis=0, tiled=True)

    def chosen(value, other):
        return jnp.where(fits, value.astype(jnp.float32), other.astype(jnp.float32))

    def shaped(*shape, dtype=jnp.bfloat16):
        return jax.ShapeDtypeStruct(shape, dtype)

    part_one, part_two = ORDER * in_width // n_col, ORDER * width // n_col
    padded = -(-(part_one + 16) // (8 * n_row)) * (8 * n_row)
    hidden, turned_one, mixed_one = layer_pass(
        layer_one_kernel,
        "layer_one",
        None,
        powers,
        features_all,
        features_own,
        weight_one,
        [bias_one[None], gain_one[None], shift_one[None], valid_rows],
        [
            shaped(own_cap, width),
            shaped(n_col * part_one, own_cap),
            shaped(own_cap, width, dtype=jnp.float32),
        ],
        [],
    )
    activations, low_two, rest_two, mine, other = layer_pass(
        layer_two_kernel,
        "layer_two",
        place,
        powers,
        everywhere(hidden),
        hidden,
        weight_two,
        [bias_two[None], gain_two[None], shift_two[None], valid_rows, cotangent_own],
        [
            shaped(own_cap, width),
            shaped(own_cap, width),
            shaped(3, width, dtype=jnp.float32),
            shaped(2, part_two, width),
            shaped(2, part_two, width),
        ],
        [((n_col * part_two, own_cap), jnp.bfloat16), ((own_cap, width), jnp.float32)],
    )

    def add_cores(mine, other):
        got = swap(other, "core")
        (mine_here, mine_there), (got_here, got_there) = split(mine, chip), split(got, chip)
        return added(mine_here, got_here), added(mine_there, got_there)

    leaving = jnp.dot(leave_group, activations).reshape(n_row, seat_cap, width)
    here, there = add_cores(mine, other)
    everyone_two, there = lax.optimization_barrier((everywhere(low_two), there))
    there = swap(there, "chip")
    low_one, mine, other = layer_pass(
        back_two_kernel,
        "back_two",
        place,
        powers,
        everyone_two,
        low_two,
        weight_two,
        [turned_one, mixed_one, gain_one[None], valid_rows, rest_two],
        [shaped(own_cap, width), shaped(2, padded, width), shaped(2, padded, width)],
        [((own_cap, width), jnp.float32)],
    )
    low_one, there = lax.optimization_barrier((low_one, there))
    second = added(here, there).reshape(n_row, -1, width)
    many = second.shape[1]
    second = jnp.concatenate([second, leaving], axis=1)
    low_one, second = lax.optimization_barrier((low_one, second))
    second = trade(second, "row")
    here, there = add_cores(mine, other)
    low_one, there = lax.optimization_barrier((low_one, there))
    everyone_one = everywhere(low_one)
    there = swap(there, "chip")
    everyone_one, second, there = lax.optimization_barrier((everyone_one, second, there))
    first = added(here, there).reshape(n_row, -1, width)
    share = first.shape[1]
    back = second[:, many:]
    second = jnp.sum(second[:, :many].astype(jnp.float32), axis=0).astype(jnp.bfloat16)
    second = jnp.broadcast_to(second[None], (n_row,) + second.shape)
    mixed = jnp.concatenate([first, second], axis=1)
    everyone_one, mixed = lax.optimization_barrier((everyone_one, mixed))
    mixed = trade(mixed, "row")
    (input_grad,) = layer_pass(
        back_one_kernel,
        "back_one",
        None,
        powers,
        everyone_one,
        low_one,
        weight_one,
        [],
        [shaped(own_cap, in_width)],
        [((own_cap, in_width), jnp.float32)],
    )
    leaving = jnp.dot(leave_group, input_grad).reshape(n_row, seat_cap * in_width // width, width)
    home = jnp.dot(enter_home, back.reshape(-1, width), preferred_element_type=jnp.float32)
    mixed, leaving, home = lax.optimization_barrier((mixed, leaving, home))
    first = jnp.sum(mixed[:, :share].astype(jnp.float32), axis=0).astype(jnp.bfloat16)
    first = jnp.broadcast_to(first[None], (n_row,) + first.shape)
    first = trade(jnp.concatenate([first, leaving], axis=1), "row")
    second = lax.all_gather(mixed[:, share:].reshape(-1, width), ("core", "chip"), axis=0)
    back = first[:, share:].reshape(n_row * seat_cap, in_width)
    first = lax.all_gather(first[:, :share].reshape(-1, width), ("core", "chip"), axis=0)
    home_grad = jnp.dot(enter_home, back, preferred_element_type=jnp.float32)

    return (
        chosen(home, others[0]),
        chosen(home_grad, others[1]),
        chosen(first[:, :part_one], others[2]),
        chosen(second, others[3]),
        chosen(first[0, part_one : part_one + 6], others[4]),
    )


def general(
    codes,
    features,
    block_keep,
    edge_weight,
    weight_one,
    bias_one,
    gain_one,
    shift_one,
    weight_two,
    bias_two,
    gain_two,
    shift_two,
    cotangent,
    node_valid,
):
    row, col = lax.axis_index("row"), lax.axis_index(COL)
    row_codes = lax.dynamic_index_in_dim(codes, row, 0, False).reshape(-1)
    col_codes = lax.dynamic_index_in_dim(codes, col, 1, False).reshape(-1)
    tile_rows, tile_cols = edge_weight.shape
    blocks_down, blocks_across = block_keep.shape
    block_side = tile_rows // blocks_down
    linked = (row_codes[:, None] == col_codes[None, :]) & (row_codes[:, None] & 1 == 1)
    linked = linked.reshape(blocks_down, block_side, blocks_across, block_side) & (
        block_keep[:, None, :, None] == 1
    )
    masked = edge_weight * linked.reshape(tile_rows, tile_cols).astype(jnp.bfloat16)
    degree_rows = 1.0 + lax.psum(jnp.sum(masked, axis=1, dtype=jnp.float32), COL)
    own_nodes = features.shape[0]
    own_degree = lax.dynamic_slice_in_dim(
        degree_rows, lax.axis_index(COL) * own_nodes, own_nodes, 0
    )
    degree_cols = lax.all_gather(own_degree, "row", axis=0, tiled=True)
    adjacency = (
        masked.astype(jnp.float32)
        * lax.rsqrt(degree_rows)[:, None]
        * lax.rsqrt(degree_cols)[None, :]
    ).astype(jnp.bfloat16)
    valid_rows = node_valid.astype(jnp.float32)
    stacked_one, mixed_one, hidden = layer_forward(
        adjacency,
        features.astype(jnp.float32),
        weight_one,
        bias_one,
        gain_one,
        shift_one,
        valid_rows,
    )
    stacked_two, mixed_two, activations = layer_forward(
        adjacency, hidden, weight_two, bias_two, gain_two, shift_two, valid_rows
    )
    hidden_grad, weight_two_grad, bias_two_grad, gain_two_grad, shift_two_grad = layer_backward(
        adjacency,
        stacked_two,
        mixed_two,
        cotangent.astype(jnp.float32),
        weight_two,
        gain_two,
        shift_two,
        valid_rows,
    )
    input_grad, weight_one_grad, bias_one_grad, gain_one_grad, shift_one_grad = layer_backward(
        adjacency, stacked_one, mixed_one, hidden_grad, weight_one, gain_one, shift_one, valid_rows
    )
    summed = lax.psum(
        (
            weight_one_grad,
            bias_one_grad,
            gain_one_grad,
            shift_one_grad,
            weight_two_grad,
            bias_two_grad,
            gain_two_grad,
            shift_two_grad,
        ),
        ("row",) + COL,
    )
    weight_one_grad, bias_one_grad, gain_one_grad, shift_one_grad = (
        summed[0],
        summed[1],
        summed[2],
        summed[3],
    )
    weight_two_grad, bias_two_grad, gain_two_grad, shift_two_grad = (
        summed[4],
        summed[5],
        summed[6],
        summed[7],
    )
    return (
        activations,
        input_grad,
        weight_one_grad,
        bias_one_grad,
        gain_one_grad,
        shift_one_grad,
        weight_two_grad,
        bias_two_grad,
        gain_two_grad,
        shift_two_grad,
    )


def local(n_row, n_col, *args):
    (
        features,
        node_valid,
        cluster,
        block_keep,
        edge_weight,
        weight_one,
        bias_one,
        gain_one,
        shift_one,
        weight_two,
        bias_two,
        gain_two,
        shift_two,
        cotangent,
    ) = args
    own_nodes, in_width = features.shape
    own_cap = own_nodes * n_row * 5 // 16
    send_cap = own_nodes * n_col * 11 // 32
    seat_cap = own_nodes // 2
    codes = broadcast_along(cluster * 2 + node_valid, ("row",) + COL, n_row * n_col)
    codes = codes.reshape(n_row, n_col, own_nodes)
    shared = (
        block_keep,
        edge_weight,
        weight_one,
        bias_one,
        gain_one,
        shift_one,
        weight_two,
        bias_two,
        gain_two,
        shift_two,
        cotangent,
    )

    def slow():
        return general(codes, features, *shared, node_valid)

    held = (ORDER - 1) * own_cap * own_cap * n_col * 2
    if held > HELD_BYTES or n_col != 4 or n_row < 2 or n_row & (n_row - 1):
        return slow()
    group = assign(codes, n_row)

    def member_of(group):
        return group[None] == jnp.arange(n_row)[:, None, None, None]

    def places_of(group):
        member = member_of(group).transpose(0, 2, 1, 3).reshape(n_row, n_col, -1)
        places = jnp.sum(jnp.where(member, exclusive_counts(member), 0), axis=0)
        return places.reshape(n_col, n_row, own_nodes).transpose(1, 0, 2)

    def slots_of(group):
        member = member_of(group).reshape(n_row, n_row, -1)
        slots = jnp.sum(jnp.where(member, exclusive_counts(member), 0), axis=0)
        return slots.reshape(n_row, n_col, own_nodes)

    def seats_of(group):
        member = member_of(group)
        return jnp.sum(jnp.where(member, exclusive_counts(member), 0), axis=0)

    width = weight_two.shape[2]

    def instead(state):
        made = slow()
        small = jnp.stack([made[place] for place in (3, 4, 5, 7, 8, 9)])
        return (True,) + tuple(
            value.astype(jnp.bfloat16).reshape(like.shape)
            for value, like in zip((made[0], made[1], made[2], made[6], small), state[1:])
        )

    shapes = (
        (own_nodes, width),
        (own_nodes, in_width),
        (n_col, ORDER * in_width // n_col, width),
        (n_col, ORDER * width // n_col, width),
        (6, width),
    )

    def decide(group):
        member = member_of(group)
        fits = (
            (jnp.max(jnp.sum(member, axis=(1, 3))) <= own_cap)
            & (jnp.max(jnp.sum(member, axis=(2, 3))) <= send_cap)
            & (jnp.max(jnp.sum(member, axis=3)) <= seat_cap)
        )
        others = lax.while_loop(
            lambda state: jnp.logical_not(state[0]),
            instead,
            (fits,) + tuple(jnp.zeros(shape, jnp.bfloat16) for shape in shapes),
        )[1:]
        return fits, others

    home, home_grad, first, second, small = compact(
        codes,
        group,
        features,
        *shared,
        places_of,
        slots_of,
        seats_of,
        decide,
        (n_row, n_col),
        (own_cap, send_cap, seat_cap),
    )
    return (
        home,
        home_grad,
        first.reshape(weight_one.shape),
        small[0],
        small[1],
        small[2],
        second.reshape(weight_two.shape),
        small[3],
        small[4],
        small[5],
    )


def solution(mesh):
    n_row, n_col = mesh.shape["row"], mesh.shape["col"]
    by_core = jax.sharding.Mesh(
        mesh.devices.reshape(n_row, n_col // 2, 2), ("row", "chip", "core")
    )
    nodes = ("row", "chip", "core")
    placed = (
        P(nodes, None),
        P(nodes),
        P(nodes),
        P("row", COL),
        P("row", COL),
        P(),
        P(),
        P(),
        P(),
        P(),
        P(),
        P(),
        P(),
        P(nodes, None),
    )
    return jax.shard_map(
        functools.partial(local, n_row, n_col),
        mesh=by_core,
        in_specs=placed,
        out_specs=(P(nodes, None), P(nodes, None), P(), P(), P(), P(), P(), P(), P(), P()),
        check_vma=False,
    )
```

```python
import functools
import math

import jax
import jax.numpy as jnp
from jax import lax
from jax.experimental import pallas as pl
from jax.experimental.pallas import tpu as pltpu
from jax.sharding import PartitionSpec as P

ORDER = 13
CLUSTERS = 16
HELD_BYTES = 1 << 25
VMEM_BYTES = 32 << 20
TERMS = 3
NO_COST = pl.CostEstimate(flops=1, bytes_accessed=1, transcendentals=0)
COL = ("chip", "core")


def finish(mixed, gain, shift, valid_rows):
    active = jax.nn.gelu(mixed, approximate=False)
    centered = active - jnp.mean(active, axis=-1, keepdims=True)
    variance = jnp.mean(centered * centered, axis=-1, keepdims=True)
    return (centered * lax.rsqrt(variance + 1e-05) * gain + shift) * valid_rows[:, None]


def forward_product(adjacency, piece_low):
    partial_value = jnp.dot(
        adjacency,
        lax.all_gather(piece_low, "row", axis=0, tiled=True),
        preferred_element_type=jnp.float32,
    )
    return lax.psum_scatter(partial_value, COL, scatter_dimension=0, tiled=True)


def backward_product(adjacency, piece_low):
    partial_value = lax.dot_general(
        adjacency,
        lax.all_gather(piece_low, COL, axis=0, tiled=True),
        (((0,), (0,)), ((), ())),
        preferred_element_type=jnp.float32,
    )
    return lax.psum_scatter(
        partial_value.astype(jnp.bfloat16), "row", scatter_dimension=0, tiled=True
    ).astype(jnp.float32)


def layer_forward(adjacency, inputs, weight, bias, gain, shift, valid_rows):
    first_low = inputs.astype(jnp.bfloat16)
    second = -forward_product(adjacency, first_low)
    second_low = second.astype(jnp.bfloat16)

    def advance(state_pair, unused):
        previous, current, current_low = state_pair
        upcoming = -2.0 * forward_product(adjacency, current_low) - previous
        upcoming_low = upcoming.astype(jnp.bfloat16)
        return ((current, upcoming, upcoming_low), upcoming_low)

    ignored, others = lax.scan(advance, (inputs, second, second_low), None, length=ORDER - 2)
    stacked = jnp.concatenate([first_low[None], second_low[None], others], axis=0)
    mixed = jnp.einsum("kni,kio->no", stacked, weight, preferred_element_type=jnp.float32) + bias
    return (stacked, mixed, finish(mixed, gain, shift, valid_rows))


def layer_backward(adjacency, stacked, mixed, upstream, weight, gain, shift, valid_rows):

    def local_finish(mixed_in, gain_in, shift_in):
        return finish(mixed_in, gain_in, shift_in, valid_rows)

    ignored, pullback = jax.vjp(local_finish, mixed, gain, shift)
    mixed_grad, gain_grad, shift_grad = pullback(upstream)
    mixed_low = mixed_grad.astype(jnp.bfloat16)
    bias_grad = jnp.sum(mixed_low.astype(jnp.float32), axis=0)
    weight_grad = jnp.einsum("kni,no->kio", stacked, mixed_low, preferred_element_type=jnp.float32)
    direct = jnp.einsum("no,kio->kni", mixed_low, weight, preferred_element_type=jnp.float32)

    def retreat(state_pair, direct_term):
        later_two, later_one = state_pair
        current = (
            direct_term
            - 2.0 * backward_product(adjacency, later_one.astype(jnp.bfloat16))
            - later_two
        )
        return ((later_one, current), None)

    start_pair = (jnp.zeros_like(direct[0]), direct[ORDER - 1])
    (second_grad, first_grad), unused = lax.scan(
        retreat, start_pair, direct[1 : ORDER - 1], reverse=True
    )
    input_grad = (
        direct[0] - backward_product(adjacency, first_grad.astype(jnp.bfloat16)) - second_grad
    )
    return (input_grad, weight_grad, bias_grad, gain_grad, shift_grad)


def swap(value, axis):
    return lax.ppermute(value, axis, [(0, 1), (1, 0)])


def trade(pieces, axis):
    return lax.all_to_all(pieces, axis, 0, 0, tiled=False)


def broadcast_along(value, axis, size):
    return trade(jnp.broadcast_to(value[None], (size,) + value.shape), axis)


def joined(mine, other, mine_first):
    return jnp.where(
        mine_first, jnp.concatenate([mine, other]), jnp.concatenate([other, mine])
    )


def added(mine, received):
    return (mine.astype(jnp.float32) + received.astype(jnp.float32)).astype(jnp.bfloat16)


def assemble(place_ref, own_ref, sibling_ref, near_ref, far_ref, out_ref, done):
    chip, core = place_ref[0], place_ref[1]
    own_cap, span = own_ref.shape
    half = span // 2

    def rows(of_chip, of_core):
        return pl.ds(pl.multiple_of((2 * of_chip + of_core) * own_cap, own_cap), own_cap)

    def fetch(source, of_chip, of_core, columns, place):
        target = out_ref.at[rows(of_chip, of_core), columns]
        return pltpu.make_async_copy(source, target, done.at[place])

    def quadrant_copies(here):
        there = 1 - here
        columns = pl.ds(there * half, half)
        return (
            fetch(near_ref, there, core, columns, 2),
            fetch(far_ref, there, 1 - core, columns, 3),
        )

    everything = pl.ds(0, span)
    top = (
        fetch(own_ref, chip, core, everything, 0),
        fetch(sibling_ref, chip, 1 - core, everything, 1),
    )

    def of_chip(here):
        there = 1 - here
        copies = top + quadrant_copies(here)
        for copy in copies:
            copy.start()
        for copy in copies:
            copy.wait()
        here_rows = pl.ds(here * half, half)
        for tile in range(half // 128):
            columns = pl.ds(there * half + tile * 128, 128)
            strip = out_ref[here_rows, columns]
            turned = jnp.transpose(strip.astype(jnp.float32)).astype(jnp.bfloat16)
            out_ref[columns, here_rows] = turned

    @pl.when(chip == 0)
    def first():
        of_chip(0)

    @pl.when(chip == 1)
    def second():
        of_chip(1)

    across = jnp.ones((1, span), jnp.float32)
    for tile in range(span // 128):
        across = across + jnp.sum(
            out_ref[pl.ds(tile * 128, 128), :].astype(jnp.float32), axis=0, keepdims=True
        )
    across = lax.rsqrt(across)
    for tile in range(span // 128):
        strip = out_ref[pl.ds(tile * 128, 128), :].astype(jnp.float32)
        down = lax.rsqrt(1.0 + jnp.sum(strip, axis=1, keepdims=True))
        out_ref[pl.ds(tile * 128, 128), :] = (strip * down * across).astype(jnp.bfloat16)


def normalized_block(own, sibling, near, far, place):
    span = own.shape[1]
    return pl.pallas_call(
        assemble,
        out_shape=jax.ShapeDtypeStruct((span, span), jnp.bfloat16),
        in_specs=[pl.BlockSpec(memory_space=pltpu.SMEM)]
        + [pl.BlockSpec(memory_space=pltpu.HBM)] * 4,
        out_specs=pl.BlockSpec(memory_space=pltpu.VMEM),
        scratch_shapes=[pltpu.SemaphoreType.DMA((4,))],
        compiler_params=pltpu.CompilerParams(vmem_limit_bytes=VMEM_BYTES),
        cost_estimate=NO_COST,
        name="normalized_block",
    )(place, own, sibling, near, far)


def pack_kernel(
    keep_ref, row_codes_ref, col_codes_ref, row_keys_ref, col_keys_ref, weight_ref, out_ref,
    masked, picked, rows_hot, cols_hot
):
    tile_rows, tile_cols = weight_ref.shape
    blocks_down, blocks_across = keep_ref.shape
    groups, ignored, lanes = out_ref.shape
    send_cap, own_cap = rows_hot.shape[0] // groups, cols_hot.shape[0] // groups
    high, wide = tile_rows // blocks_down, tile_cols // blocks_across
    for down in range(blocks_down):
        for across in range(blocks_across):
            rows, columns = pl.ds(down * high, high), pl.ds(across * wide, wide)
            own, other = row_codes_ref[rows, :], col_codes_ref[:, columns]
            linked = (own == other) & (own % 2 == 1) & (keep_ref[down, across] == 1)
            weight = weight_ref[rows, columns].astype(jnp.float32)
            masked[rows, columns] = jnp.where(linked, weight, 0.0).astype(jnp.bfloat16)

    def one_hot(keys, start, count):
        standing = lax.broadcasted_iota(jnp.int32, (count, keys.shape[1]), 0) + start
        return jnp.where(standing == keys, 1.0, 0.0).astype(jnp.bfloat16)

    for group in range(groups):
        rows_hot[pl.ds(group * send_cap, send_cap), :] = one_hot(
            row_keys_ref[...], group * send_cap, send_cap
        )
        cols_hot[pl.ds(group * own_cap, own_cap), :] = one_hot(
            col_keys_ref[...], group * own_cap, own_cap
        )
    for tile in range(tile_cols // 256):
        columns = pl.ds(tile * 256, 256)
        picked[:, columns] = jnp.dot(
            rows_hot[...], masked[:, columns], preferred_element_type=jnp.float32
        ).astype(jnp.bfloat16)
    whole, half = own_cap // lanes, send_cap // 2
    for group in range(groups):
        packed = lax.dot_general(
            picked[pl.ds(group * send_cap, send_cap), :],
            cols_hot[pl.ds(group * own_cap, own_cap), :],
            (((1,), (1,)), ((), ())),
            preferred_element_type=jnp.float32,
        )
        for tile in range(whole):
            out_ref[group, pl.ds(tile * send_cap, send_cap), :] = packed[
                :, tile * lanes : (tile + 1) * lanes
            ].astype(jnp.bfloat16)
        ends = jnp.concatenate(
            [packed[:half, whole * lanes :], packed[half:, whole * lanes :]], axis=1
        )
        out_ref[group, pl.ds(whole * send_cap, half), :] = ends.astype(jnp.bfloat16)


def packed_pieces(block_keep, row_codes, col_codes, row_keys, col_keys, edge_weight, caps, groups):
    own_cap, send_cap = caps
    tile_rows, tile_cols = edge_weight.shape
    high = own_cap // 128 * send_cap + send_cap // 2
    vector = pl.BlockSpec(memory_space=pltpu.VMEM)
    return pl.pallas_call(
        pack_kernel,
        out_shape=jax.ShapeDtypeStruct((groups, high, 128), jnp.bfloat16),
        in_specs=[pl.BlockSpec(memory_space=pltpu.SMEM)] + [vector] * 5,
        out_specs=vector,
        scratch_shapes=[
            pltpu.VMEM((tile_rows, tile_cols), jnp.bfloat16),
            pltpu.VMEM((groups * send_cap, tile_cols), jnp.bfloat16),
            pltpu.VMEM((groups * send_cap, tile_rows), jnp.bfloat16),
            pltpu.VMEM((groups * own_cap, tile_cols), jnp.bfloat16),
        ],
        compiler_params=pltpu.CompilerParams(vmem_limit_bytes=VMEM_BYTES),
        cost_estimate=NO_COST,
        name="packed_pieces",
    )(block_keep, row_codes[:, None], col_codes[None], row_keys[None], col_keys[None], edge_weight)


def normal_share(mixed):
    return 0.5 * (1.0 + lax.erf(mixed * 0.5**0.5))


def norm_forward(mixed):
    active = mixed * normal_share(mixed)
    centered = active - jnp.mean(active, axis=-1, keepdims=True)
    scale = lax.rsqrt(jnp.mean(centered * centered, axis=-1, keepdims=True) + 1e-05)
    return centered * scale, scale


def norm_backward(mixed, upstream, gain, valid):
    normed, scale = norm_forward(mixed)
    upstream = upstream * valid
    inner = upstream * gain
    inner = inner - jnp.mean(inner, axis=-1, keepdims=True) - normed * jnp.mean(
        inner * normed, axis=-1, keepdims=True
    )
    density = jnp.exp(-0.5 * mixed * mixed) * (1.0 / (2.0 * math.pi) ** 0.5)
    low = (inner * scale * (normal_share(mixed) + mixed * density)).astype(jnp.bfloat16)
    rest = [low.astype(jnp.float32), upstream * normed, upstream]
    return low, [jnp.sum(value, axis=0, keepdims=True) for value in rest]


def weight_gradient(turned_ref, low, core, mine_ref, other_ref):
    part = turned_ref.shape[0] // 4

    def halves(first_ref, second_ref):
        for place in range(4):
            out_ref = second_ref if place % 2 else first_ref
            out_ref[place // 2, :part, :] = jnp.dot(
                turned_ref[place * part : (place + 1) * part, :],
                low,
                preferred_element_type=jnp.float32,
            ).astype(jnp.bfloat16)

    @pl.when(core == 0)
    def low_half_first():
        halves(mine_ref, other_ref)

    @pl.when(core == 1)
    def high_half_first():
        halves(other_ref, mine_ref)


def forward_step(step, powers_ref, all_ref, own_ref, weights, bias_ref, turned, mixed):
    terms, own_cap, span = powers_ref.shape
    fan_in = own_ref.shape[1]

    @pl.when(step == 0)
    def first():
        turned[:fan_in, :] = own_ref[...].T
        mixed[...] = bias_ref[...] + jnp.dot(
            own_ref[...], weights[0][0], preferred_element_type=jnp.float32
        )

    low = jnp.dot(
        powers_ref[...].reshape(terms * own_cap, span),
        all_ref[...],
        preferred_element_type=jnp.float32,
    ).astype(jnp.bfloat16)
    total = mixed[...]
    for term in range(terms):
        part = low[term * own_cap : (term + 1) * own_cap]
        start = pl.multiple_of((1 + step * terms + term) * fan_in, fan_in)
        turned[pl.ds(start, fan_in), :] = part.T
        total = total + jnp.dot(part, weights[1 + term][0], preferred_element_type=jnp.float32)
    mixed[...] = total


def layer_one_kernel(
    powers_ref,
    all_ref,
    own_ref,
    weight_0,
    weight_a,
    weight_b,
    weight_c,
    bias_ref,
    gain_ref,
    shift_ref,
    valid_ref,
    hidden_ref,
    turned_ref,
    mixed_ref,
):
    step = pl.program_id(0)
    weights = (weight_0, weight_a, weight_b, weight_c)
    forward_step(step, powers_ref, all_ref, own_ref, weights, bias_ref, turned_ref, mixed_ref)

    @pl.when(step == pl.num_programs(0) - 1)
    def finish_layer():
        normed, ignored = norm_forward(mixed_ref[...])
        hidden = (normed * gain_ref[...] + shift_ref[...]) * valid_ref[...]
        hidden_ref[...] = hidden.astype(jnp.bfloat16)


def layer_two_kernel(
    place_ref,
    powers_ref,
    all_ref,
    own_ref,
    weight_0,
    weight_a,
    weight_b,
    weight_c,
    bias_ref,
    gain_ref,
    shift_ref,
    valid_ref,
    upstream_ref,
    active_ref,
    low_ref,
    rest_ref,
    mine_ref,
    other_ref,
    turned,
    mixed,
):
    step = pl.program_id(0)
    weights = (weight_0, weight_a, weight_b, weight_c)
    forward_step(step, powers_ref, all_ref, own_ref, weights, bias_ref, turned, mixed)

    @pl.when(step == pl.num_programs(0) - 1)
    def finish_layer():
        normed, ignored = norm_forward(mixed[...])
        active = (normed * gain_ref[...] + shift_ref[...]) * valid_ref[...]
        active_ref[...] = active.astype(jnp.bfloat16)
        low, rest = norm_backward(
            mixed[...], upstream_ref[...].astype(jnp.float32), gain_ref[...], valid_ref[...]
        )
        low_ref[...] = low
        for place in range(3):
            rest_ref[place : place + 1, :] = rest[place]
        weight_gradient(turned, low, place_ref[1], mine_ref, other_ref)


def backward_step(step, powers_ref, all_ref, own_ref, weights, total):
    terms, own_cap, span = powers_ref.shape
    transposed = (((1,), (1,)), ((), ()))

    @pl.when(step == 0)
    def first():
        total[...] = lax.dot_general(
            own_ref[...], weights[0][0], transposed, preferred_element_type=jnp.float32
        )

    low = jnp.dot(
        powers_ref[...].reshape(terms * own_cap, span),
        all_ref[...],
        preferred_element_type=jnp.float32,
    ).astype(jnp.bfloat16)
    value = total[...]
    for term in range(terms):
        value = value + lax.dot_general(
            low[term * own_cap : (term + 1) * own_cap],
            weights[1 + term][0],
            transposed,
            preferred_element_type=jnp.float32,
        )
    total[...] = value


def back_two_kernel(
    place_ref,
    powers_ref,
    all_ref,
    own_ref,
    weight_0,
    weight_a,
    weight_b,
    weight_c,
    turned_ref,
    mixed_ref,
    gain_ref,
    valid_ref,
    rest_ref,
    low_ref,
    mine_ref,
    other_ref,
    total,
):
    step = pl.program_id(0)
    weights = (weight_0, weight_a, weight_b, weight_c)
    backward_step(step, powers_ref, all_ref, own_ref, weights, total)

    @pl.when(step == pl.num_programs(0) - 1)
    def finish_layer():
        low, rest = norm_backward(mixed_ref[...], total[...], gain_ref[...], valid_ref[...])
        low_ref[...] = low
        weight_gradient(turned_ref, low, place_ref[1], mine_ref, other_ref)
        part = turned_ref.shape[0] // 4
        extra = jnp.zeros((2, mine_ref.shape[1] - part, mine_ref.shape[2]), jnp.bfloat16)
        rows = rest + [rest_ref[place : place + 1, :] for place in range(3)]
        rows = jnp.concatenate(rows + [jnp.zeros((10, rows[0].shape[1]), jnp.float32)], axis=0)

        def below(first_ref, second_ref):
            first_ref[:, part:, :] = extra
            second_ref[:, part:, :] = extra
            first_ref[0, part : part + 16, :] = rows.astype(jnp.bfloat16)

        @pl.when(place_ref[1] == 0)
        def low_half_here():
            below(mine_ref, other_ref)

        @pl.when(place_ref[1] == 1)
        def low_half_there():
            below(other_ref, mine_ref)


def back_one_kernel(
    powers_ref, all_ref, own_ref, weight_0, weight_a, weight_b, weight_c, out_ref, total
):
    step = pl.program_id(0)
    weights = (weight_0, weight_a, weight_b, weight_c)
    backward_step(step, powers_ref, all_ref, own_ref, weights, total)

    @pl.when(step == pl.num_programs(0) - 1)
    def finish_layer():
        out_ref[...] = total[...].astype(jnp.bfloat16)


def layer_pass(kernel, name, place, powers, everyone, own, weight, others, outs, scratch):
    ignored, own_cap, span = powers.shape
    fan_in, width = weight.shape[1:]

    def whole(value):
        return pl.BlockSpec(value.shape, lambda step: (0,) * len(value.shape))

    def term_weight(term):
        return pl.BlockSpec((1, fan_in, width), lambda step: (1 + step * TERMS + term, 0, 0))

    in_specs = [
        pl.BlockSpec((TERMS, own_cap, span), lambda step: (step, 0, 0)),
        whole(everyone),
        whole(own),
        pl.BlockSpec((1, fan_in, width), lambda step: (0, 0, 0)),
    ]
    in_specs += [term_weight(term) for term in range(TERMS)] + [whole(value) for value in others]
    operands = [powers, everyone, own] + [weight] * (1 + TERMS) + list(others)
    if place is not None:
        in_specs = [pl.BlockSpec(memory_space=pltpu.SMEM)] + in_specs
        operands = [place] + operands
    return pl.pallas_call(
        kernel,
        grid=((ORDER - 1) // TERMS,),
        out_shape=outs,
        in_specs=in_specs,
        out_specs=[whole(value) for value in outs],
        scratch_shapes=[pltpu.VMEM(shape, dtype) for shape, dtype in scratch],
        compiler_params=pltpu.CompilerParams(vmem_limit_bytes=VMEM_BYTES),
        cost_estimate=NO_COST,
        name=name,
    )(*operands)


def exclusive_counts(member):
    count = member.shape[-1]
    before = jnp.arange(count)[:, None] < jnp.arange(count)[None, :]
    return jnp.dot(
        member.astype(jnp.bfloat16),
        before.astype(jnp.bfloat16),
        preferred_element_type=jnp.float32,
    ).astype(jnp.int32)


def assign(codes, n_row):
    cluster, valid = codes >> 1, codes & 1
    labels = jnp.arange(CLUSTERS)
    sizes = jnp.sum(
        (cluster.reshape(1, -1) == labels[:, None]) & (valid.reshape(1, -1) == 1), axis=1
    )
    ahead = (sizes[None, :] > sizes[:, None]) | (
        (sizes[None, :] == sizes[:, None]) & (labels[None, :] < labels[:, None])
    )
    rank = jnp.sum(ahead, axis=1)
    others = n_row - 1
    turn, place = (rank - 1) // others, (rank - 1) % others
    group = jnp.where(rank == 0, 0, 1 + jnp.where(turn == 0, place, others - 1 - place))
    of_node = jnp.sum(
        jnp.where(cluster[None] == labels[:, None, None, None], group[:, None, None, None], 0),
        axis=0,
    )
    return jnp.where(valid == 1, of_node, n_row)


def compact(
    codes,
    group,
    features,
    block_keep,
    edge_weight,
    weight_one,
    bias_one,
    gain_one,
    shift_one,
    weight_two,
    bias_two,
    gain_two,
    shift_two,
    cotangent,
    places_of,
    slots_of,
    seats_of,
    decide,
    sizes,
    caps,
):
    row, col = lax.axis_index("row"), lax.axis_index(COL)
    chip, core = lax.axis_index("chip"), lax.axis_index("core")
    n_row, n_col = sizes
    own_cap, send_cap, seat_cap = caps
    own_nodes, in_width = features.shape
    width = weight_two.shape[2]
    span = n_col * own_cap
    targets = jnp.arange(n_row)

    def in_col(value):
        return lax.dynamic_index_in_dim(value, col, 1, False).reshape(-1)

    def in_row(value):
        return lax.dynamic_index_in_dim(value, row, 0, False).reshape(-1)

    row_group, col_group = in_row(group), in_col(group)
    row_slots, col_places = in_row(slots_of(group)), in_col(places_of(group))
    row_keys = jnp.where(row_slots < send_cap, row_group * send_cap + row_slots, -1)
    col_keys = jnp.where(col_places < own_cap, col_group * own_cap + col_places, -1)
    pieces = packed_pieces(
        block_keep,
        in_row(codes),
        in_col(codes),
        row_keys,
        col_keys,
        edge_weight,
        (own_cap, send_cap),
        n_row,
    )
    pieces, codes = lax.optimization_barrier((pieces, codes))
    group = assign(codes, n_row)
    pieces = trade(pieces, "row")
    whole, half_send = own_cap // 128 * 128, send_cap // 2
    fits, others = decide(group)
    places, slots, seats = places_of(group), slots_of(group), seats_of(group)

    standing = jnp.arange(n_col)[None, :, None] * own_cap + places
    fits_here = jnp.where(group == row, standing, -1).reshape(n_row, -1)
    slot_of = slots.reshape(n_row, -1)
    target = jnp.max(
        jnp.where(
            slot_of[:, None, :] == jnp.arange(send_cap)[None, :, None], fits_here[:, None, :], -1
        ),
        axis=2,
    )
    spread = (target[:, :, None] == jnp.arange(span)[None, None, :]).astype(jnp.bfloat16)

    partners = row ^ targets
    group_here = lax.dynamic_index_in_dim(in_row(group).reshape(n_col, -1), col, 0, False)
    seat_here = lax.dynamic_index_in_dim(in_row(seats).reshape(n_col, -1), col, 0, False)

    def seat_of_node(groups):
        hot = (group_here[None, None, :] == groups[:, None, None]) & (
            seat_here[None, None, :] == jnp.arange(seat_cap)[None, :, None]
        )
        return hot.astype(jnp.bfloat16).reshape(n_row * seat_cap, own_nodes)

    both = jnp.dot(seat_of_node(partners), jnp.concatenate([features, cotangent], axis=1))
    both = both.reshape(n_row, seat_cap, -1)
    enter_home = seat_of_node(targets).T
    group_col = lax.dynamic_index_in_dim(group, col, 1, False)
    seats_col = lax.dynamic_index_in_dim(seats, col, 1, False)
    places_col = lax.dynamic_index_in_dim(places, col, 1, False)
    seated = (group_col == row)[:, None, :] & (
        seats_col[:, None, :] == jnp.arange(seat_cap)[None, :, None]
    )
    place_of_seat = jnp.max(jnp.where(seated, places_col[:, None, :], -1), axis=2)
    from_partner = jnp.max(
        jnp.where((partners[:, None] == targets)[:, :, None], place_of_seat[None], -1), axis=1
    )
    arrive = from_partner.reshape(1, -1) == jnp.arange(own_cap)[:, None]
    arrive = arrive.astype(jnp.bfloat16)
    leave_group = place_of_seat.reshape(-1, 1) == jnp.arange(own_cap)[None, :]
    leave_group = leave_group.astype(jnp.bfloat16)
    held_count = jnp.sum(group_col == row)
    valid_rows = (jnp.arange(own_cap) < held_count).astype(jnp.float32)[:, None]
    place = jnp.stack([chip, core]).astype(jnp.int32)
    scalars = (chip, 1 - chip, chip * (span // 2), col * own_cap)
    scalars = tuple(value.astype(jnp.uint32) for value in scalars) + (chip == 0, core == 0, place)
    pieces, both, spread, arrive, leave_group, enter_home, valid_rows, others, scalars = (
        lax.optimization_barrier(
            (pieces, both, spread, arrive, leave_group, enter_home, valid_rows, others, scalars)
        )
    )
    this_chip, other_chip, chip_start, own_start, first_chip, first_core, place = scalars

    many = whole // 128
    tiles = pieces[:, : many * send_cap].reshape(n_row, many, send_cap, 128)
    ends = pieces[:, many * send_cap :].reshape(n_row, half_send, 2, own_cap - whole)
    own_block = jnp.concatenate(
        [
            jnp.einsum("sktu,stw->kuw", tiles, spread).reshape(whole, span),
            jnp.einsum("sthu,shtw->uw", ends, spread.reshape(n_row, 2, half_send, span)),
        ]
    ).astype(jnp.bfloat16)
    quadrant = lax.dynamic_slice_in_dim(own_block, chip_start, span // 2, 1)
    quadrant = swap(quadrant, "chip")
    both = [both[0]] + [
        lax.ppermute(both[step], "row", [(place, place ^ step) for place in range(n_row)])
        for step in range(1, n_row)
    ]
    sibling = swap(own_block, "core")
    quadrant, *both = lax.optimization_barrier((quadrant, *both))
    adjacency = normalized_block(own_block, sibling, quadrant, swap(quadrant, "core"), place)
    mine = jnp.dot(arrive, jnp.concatenate(both))
    features_own, cotangent_own = mine[:, :in_width], mine[:, in_width:]
    sibling = swap(features_own, "core")

    first = (own_start + jnp.arange(own_cap, dtype=jnp.uint32))[:, None]
    first = first == jnp.arange(span, dtype=jnp.uint32)[None, :]
    previous = first.astype(jnp.float32)
    current = -lax.dynamic_slice_in_dim(adjacency, own_start, own_cap, 0).astype(jnp.float32)
    lowered = [current.astype(jnp.bfloat16)]
    for position in range(2, ORDER):
        upcoming = (
            -2.0 * jnp.dot(lowered[-1], adjacency, preferred_element_type=jnp.float32) - previous
        )
        low = upcoming.astype(jnp.bfloat16)
        if position == 4:
            low, sibling = lax.optimization_barrier((low, sibling))
            features_chip = joined(features_own, sibling, first_core)
            partner = swap(features_chip, "chip")
        if position == 8:
            low, partner = lax.optimization_barrier((low, partner))
            features_all = joined(features_chip, partner, first_chip)
        previous, current = current, upcoming
        lowered.append(low)
    powers = jnp.concatenate(lowered, axis=0).reshape(ORDER - 1, own_cap, span)

    def everywhere(value_low):
        return lax.all_gather(value_low, COL, axis=0, tiled=True)

    def chosen(value, other):
        return jnp.where(fits, value.astype(jnp.float32), other.astype(jnp.float32))

    def shaped(*shape, dtype=jnp.bfloat16):
        return jax.ShapeDtypeStruct(shape, dtype)

    part_one, part_two = ORDER * in_width // n_col, ORDER * width // n_col
    padded = -(-(part_one + 16) // (8 * n_row)) * (8 * n_row)
    hidden, turned_one, mixed_one = layer_pass(
        layer_one_kernel,
        "layer_one",
        None,
        powers,
        features_all,
        features_own,
        weight_one,
        [bias_one[None], gain_one[None], shift_one[None], valid_rows],
        [
            shaped(own_cap, width),
            shaped(n_col * part_one, own_cap),
            shaped(own_cap, width, dtype=jnp.float32),
        ],
        [],
    )
    activations, low_two, rest_two, mine, other = layer_pass(
        layer_two_kernel,
        "layer_two",
        place,
        powers,
        everywhere(hidden),
        hidden,
        weight_two,
        [bias_two[None], gain_two[None], shift_two[None], valid_rows, cotangent_own],
        [
            shaped(own_cap, width),
            shaped(own_cap, width),
            shaped(3, width, dtype=jnp.float32),
            shaped(2, part_two, width),
            shaped(2, part_two, width),
        ],
        [((n_col * part_two, own_cap), jnp.bfloat16), ((own_cap, width), jnp.float32)],
    )

    def add_cores(mine, other):
        got = swap(other, "core")
        return tuple(
            added(
                lax.dynamic_index_in_dim(mine, index, 0, False),
                lax.dynamic_index_in_dim(got, index, 0, False),
            )
            for index in (this_chip, other_chip)
        )

    leaving = jnp.dot(leave_group, activations).reshape(n_row, seat_cap, width)
    here, there = add_cores(mine, other)
    everyone_two, there = lax.optimization_barrier((everywhere(low_two), there))
    there = swap(there, "chip")
    low_one, mine, other = layer_pass(
        back_two_kernel,
        "back_two",
        place,
        powers,
        everyone_two,
        low_two,
        weight_two,
        [turned_one, mixed_one, gain_one[None], valid_rows, rest_two],
        [shaped(own_cap, width), shaped(2, padded, width), shaped(2, padded, width)],
        [((own_cap, width), jnp.float32)],
    )
    low_one, there = lax.optimization_barrier((low_one, there))
    second = added(here, there).reshape(n_row, -1, width)
    many = second.shape[1]
    second = jnp.concatenate([second, leaving], axis=1)
    low_one, second = lax.optimization_barrier((low_one, second))
    second = trade(second, "row")
    here, there = add_cores(mine, other)
    low_one, there = lax.optimization_barrier((low_one, there))
    everyone_one = everywhere(low_one)
    there = swap(there, "chip")
    everyone_one, second, there = lax.optimization_barrier((everyone_one, second, there))
    first = added(here, there).reshape(n_row, -1, width)
    share = first.shape[1]
    back = second[:, many:]
    second = jnp.sum(second[:, :many].astype(jnp.float32), axis=0).astype(jnp.bfloat16)
    second = jnp.broadcast_to(second[None], (n_row,) + second.shape)
    mixed = jnp.concatenate([first, second], axis=1)
    everyone_one, mixed = lax.optimization_barrier((everyone_one, mixed))
    mixed = trade(mixed, "row")
    (input_grad,) = layer_pass(
        back_one_kernel,
        "back_one",
        None,
        powers,
        everyone_one,
        low_one,
        weight_one,
        [],
        [shaped(own_cap, in_width)],
        [((own_cap, in_width), jnp.float32)],
    )
    leaving = jnp.dot(leave_group, input_grad).reshape(n_row, seat_cap * in_width // width, width)
    home = jnp.dot(enter_home, back.reshape(-1, width), preferred_element_type=jnp.float32)
    mixed, leaving, home = lax.optimization_barrier((mixed, leaving, home))
    first = jnp.sum(mixed[:, :share].astype(jnp.float32), axis=0).astype(jnp.bfloat16)
    first = jnp.broadcast_to(first[None], (n_row,) + first.shape)
    first = trade(jnp.concatenate([first, leaving], axis=1), "row")
    second = lax.all_gather(mixed[:, share:].reshape(-1, width), COL, axis=0)
    back = first[:, share:].reshape(n_row * seat_cap, in_width)
    first = lax.all_gather(first[:, :share].reshape(-1, width), COL, axis=0)
    home_grad = jnp.dot(enter_home, back, preferred_element_type=jnp.float32)

    return (
        chosen(home, others[0]),
        chosen(home_grad, others[1]),
        chosen(first[:, :part_one], others[2]),
        chosen(second, others[3]),
        chosen(first[0, part_one : part_one + 6], others[4]),
    )


def general(
    codes,
    features,
    block_keep,
    edge_weight,
    weight_one,
    bias_one,
    gain_one,
    shift_one,
    weight_two,
    bias_two,
    gain_two,
    shift_two,
    cotangent,
    node_valid,
):
    row, col = lax.axis_index("row"), lax.axis_index(COL)
    row_codes = lax.dynamic_index_in_dim(codes, row, 0, False).reshape(-1)
    col_codes = lax.dynamic_index_in_dim(codes, col, 1, False).reshape(-1)
    tile_rows, tile_cols = edge_weight.shape
    blocks_down, blocks_across = block_keep.shape
    block_side = tile_rows // blocks_down
    linked = (row_codes[:, None] == col_codes[None, :]) & (row_codes[:, None] & 1 == 1)
    linked = linked.reshape(blocks_down, block_side, blocks_across, block_side) & (
        block_keep[:, None, :, None] == 1
    )
    masked = edge_weight * linked.reshape(tile_rows, tile_cols).astype(jnp.bfloat16)
    degree_rows = 1.0 + lax.psum(jnp.sum(masked, axis=1, dtype=jnp.float32), COL)
    own_nodes = features.shape[0]
    own_degree = lax.dynamic_slice_in_dim(
        degree_rows, lax.axis_index(COL) * own_nodes, own_nodes, 0
    )
    degree_cols = lax.all_gather(own_degree, "row", axis=0, tiled=True)
    adjacency = (
        masked.astype(jnp.float32)
        * lax.rsqrt(degree_rows)[:, None]
        * lax.rsqrt(degree_cols)[None, :]
    ).astype(jnp.bfloat16)
    valid_rows = node_valid.astype(jnp.float32)
    stacked_one, mixed_one, hidden = layer_forward(
        adjacency,
        features.astype(jnp.float32),
        weight_one,
        bias_one,
        gain_one,
        shift_one,
        valid_rows,
    )
    stacked_two, mixed_two, activations = layer_forward(
        adjacency, hidden, weight_two, bias_two, gain_two, shift_two, valid_rows
    )
    hidden_grad, weight_two_grad, bias_two_grad, gain_two_grad, shift_two_grad = layer_backward(
        adjacency,
        stacked_two,
        mixed_two,
        cotangent.astype(jnp.float32),
        weight_two,
        gain_two,
        shift_two,
        valid_rows,
    )
    input_grad, weight_one_grad, bias_one_grad, gain_one_grad, shift_one_grad = layer_backward(
        adjacency, stacked_one, mixed_one, hidden_grad, weight_one, gain_one, shift_one, valid_rows
    )
    summed = lax.psum(
        (
            weight_one_grad,
            bias_one_grad,
            gain_one_grad,
            shift_one_grad,
            weight_two_grad,
            bias_two_grad,
            gain_two_grad,
            shift_two_grad,
        ),
        ("row",) + COL,
    )
    weight_one_grad, bias_one_grad, gain_one_grad, shift_one_grad = (
        summed[0],
        summed[1],
        summed[2],
        summed[3],
    )
    weight_two_grad, bias_two_grad, gain_two_grad, shift_two_grad = (
        summed[4],
        summed[5],
        summed[6],
        summed[7],
    )
    return (
        activations,
        input_grad,
        weight_one_grad,
        bias_one_grad,
        gain_one_grad,
        shift_one_grad,
        weight_two_grad,
        bias_two_grad,
        gain_two_grad,
        shift_two_grad,
    )


def local(n_row, n_col, *args):
    (
        features,
        node_valid,
        cluster,
        block_keep,
        edge_weight,
        weight_one,
        bias_one,
        gain_one,
        shift_one,
        weight_two,
        bias_two,
        gain_two,
        shift_two,
        cotangent,
    ) = args
    own_nodes, in_width = features.shape
    own_cap = own_nodes * n_row * 5 // 16
    send_cap = own_nodes * n_col * 11 // 32
    seat_cap = own_nodes // 2
    codes = broadcast_along(cluster * 2 + node_valid, ("row",) + COL, n_row * n_col)
    codes = codes.reshape(n_row, n_col, own_nodes)
    shared = (
        block_keep,
        edge_weight,
        weight_one,
        bias_one,
        gain_one,
        shift_one,
        weight_two,
        bias_two,
        gain_two,
        shift_two,
        cotangent,
    )

    def slow():
        return general(codes, features, *shared, node_valid)

    held = (ORDER - 1) * own_cap * own_cap * n_col * 2
    if held > HELD_BYTES or n_col != 4 or n_row < 2 or n_row & (n_row - 1):
        return slow()
    group = assign(codes, n_row)

    def member_of(group):
        return group[None] == jnp.arange(n_row)[:, None, None, None]

    def places_of(group):
        member = member_of(group).transpose(0, 2, 1, 3).reshape(n_row, n_col, -1)
        places = jnp.sum(jnp.where(member, exclusive_counts(member), 0), axis=0)
        return places.reshape(n_col, n_row, own_nodes).transpose(1, 0, 2)

    def slots_of(group):
        member = member_of(group).reshape(n_row, n_row, -1)
        slots = jnp.sum(jnp.where(member, exclusive_counts(member), 0), axis=0)
        return slots.reshape(n_row, n_col, own_nodes)

    def seats_of(group):
        member = member_of(group)
        return jnp.sum(jnp.where(member, exclusive_counts(member), 0), axis=0)

    width = weight_two.shape[2]

    def instead(state):
        made = slow()
        small = jnp.stack([made[place] for place in (3, 4, 5, 7, 8, 9)])
        return (True,) + tuple(
            value.astype(jnp.bfloat16).reshape(like.shape)
            for value, like in zip((made[0], made[1], made[2], made[6], small), state[1:])
        )

    shapes = (
        (own_nodes, width),
        (own_nodes, in_width),
        (n_col, ORDER * in_width // n_col, width),
        (n_col, ORDER * width // n_col, width),
        (6, width),
    )

    def decide(group):
        member = member_of(group)
        fits = (
            (jnp.max(jnp.sum(member, axis=(1, 3))) <= own_cap)
            & (jnp.max(jnp.sum(member, axis=(2, 3))) <= send_cap)
            & (jnp.max(jnp.sum(member, axis=3)) <= seat_cap)
        )
        others = lax.while_loop(
            lambda state: jnp.logical_not(state[0]),
            instead,
            (fits,) + tuple(jnp.zeros(shape, jnp.bfloat16) for shape in shapes),
        )[1:]
        return fits, others

    home, home_grad, first, second, small = compact(
        codes,
        group,
        features,
        *shared,
        places_of,
        slots_of,
        seats_of,
        decide,
        (n_row, n_col),
        (own_cap, send_cap, seat_cap),
    )
    return (
        home,
        home_grad,
        first.reshape(weight_one.shape),
        small[0],
        small[1],
        small[2],
        second.reshape(weight_two.shape),
        small[3],
        small[4],
        small[5],
    )


def solution(mesh):
    n_row, n_col = mesh.shape["row"], mesh.shape["col"]
    by_core = jax.sharding.Mesh(
        mesh.devices.reshape(n_row, n_col // 2, 2), ("row", "chip", "core")
    )
    nodes = ("row", "chip", "core")
    placed = (
        P(nodes, None),
        P(nodes),
        P(nodes),
        P("row", COL),
        P("row", COL),
        P(),
        P(),
        P(),
        P(),
        P(),
        P(),
        P(),
        P(),
        P(nodes, None),
    )
    return jax.shard_map(
        functools.partial(local, n_row, n_col),
        mesh=by_core,
        in_specs=placed,
        out_specs=(P(nodes, None), P(nodes, None), P(), P(), P(), P(), P(), P(), P(), P()),
        check_vma=False,
    )
```

```python
import functools
import math

import jax
import jax.numpy as jnp
from jax import lax
from jax.experimental import pallas as pl
from jax.experimental.pallas import tpu as pltpu
from jax.sharding import PartitionSpec as P

ORDER = 13
CLUSTERS = 16
HELD_BYTES = 1 << 25
GATHER_BYTES = 5 << 18
VMEM_BYTES = 32 << 20
TERMS = 3
NO_COST = pl.CostEstimate(flops=1, bytes_accessed=1, transcendentals=0)
COL = ("chip", "core")


def finish(mixed, gain, shift, valid_rows):
    active = jax.nn.gelu(mixed, approximate=False)
    centered = active - jnp.mean(active, axis=-1, keepdims=True)
    variance = jnp.mean(centered * centered, axis=-1, keepdims=True)
    return (centered * lax.rsqrt(variance + 1e-05) * gain + shift) * valid_rows[:, None]


def forward_product(adjacency, piece_low):
    partial_value = jnp.dot(
        adjacency,
        lax.all_gather(piece_low, "row", axis=0, tiled=True),
        preferred_element_type=jnp.float32,
    )
    return lax.psum_scatter(partial_value, COL, scatter_dimension=0, tiled=True)


def backward_product(adjacency, piece_low):
    partial_value = lax.dot_general(
        adjacency,
        lax.all_gather(piece_low, COL, axis=0, tiled=True),
        (((0,), (0,)), ((), ())),
        preferred_element_type=jnp.float32,
    )
    return lax.psum_scatter(
        partial_value.astype(jnp.bfloat16), "row", scatter_dimension=0, tiled=True
    ).astype(jnp.float32)


def layer_forward(adjacency, inputs, weight, bias, gain, shift, valid_rows):
    first_low = inputs.astype(jnp.bfloat16)
    second = -forward_product(adjacency, first_low)
    second_low = second.astype(jnp.bfloat16)

    def advance(state_pair, unused):
        previous, current, current_low = state_pair
        upcoming = -2.0 * forward_product(adjacency, current_low) - previous
        upcoming_low = upcoming.astype(jnp.bfloat16)
        return ((current, upcoming, upcoming_low), upcoming_low)

    ignored, others = lax.scan(advance, (inputs, second, second_low), None, length=ORDER - 2)
    stacked = jnp.concatenate([first_low[None], second_low[None], others], axis=0)
    mixed = jnp.einsum("kni,kio->no", stacked, weight, preferred_element_type=jnp.float32) + bias
    return (stacked, mixed, finish(mixed, gain, shift, valid_rows))


def layer_backward(adjacency, stacked, mixed, upstream, weight, gain, shift, valid_rows):

    def local_finish(mixed_in, gain_in, shift_in):
        return finish(mixed_in, gain_in, shift_in, valid_rows)

    ignored, pullback = jax.vjp(local_finish, mixed, gain, shift)
    mixed_grad, gain_grad, shift_grad = pullback(upstream)
    mixed_low = mixed_grad.astype(jnp.bfloat16)
    bias_grad = jnp.sum(mixed_low.astype(jnp.float32), axis=0)
    weight_grad = jnp.einsum("kni,no->kio", stacked, mixed_low, preferred_element_type=jnp.float32)
    direct = jnp.einsum("no,kio->kni", mixed_low, weight, preferred_element_type=jnp.float32)

    def retreat(state_pair, direct_term):
        later_two, later_one = state_pair
        current = (
            direct_term
            - 2.0 * backward_product(adjacency, later_one.astype(jnp.bfloat16))
            - later_two
        )
        return ((later_one, current), None)

    start_pair = (jnp.zeros_like(direct[0]), direct[ORDER - 1])
    (second_grad, first_grad), unused = lax.scan(
        retreat, start_pair, direct[1 : ORDER - 1], reverse=True
    )
    input_grad = (
        direct[0] - backward_product(adjacency, first_grad.astype(jnp.bfloat16)) - second_grad
    )
    return (input_grad, weight_grad, bias_grad, gain_grad, shift_grad)


def swap(value, axis):
    return lax.ppermute(value, axis, [(0, 1), (1, 0)])


def trade(pieces, axis):
    return lax.all_to_all(pieces, axis, 0, 0, tiled=False)


def broadcast_along(value, axis, size):
    return trade(jnp.broadcast_to(value[None], (size,) + value.shape), axis)


def joined(mine, other, mine_first):
    return jnp.where(
        mine_first, jnp.concatenate([mine, other]), jnp.concatenate([other, mine])
    )


def added(mine, received):
    return (mine.astype(jnp.float32) + received.astype(jnp.float32)).astype(jnp.bfloat16)


def assemble(place_ref, own_ref, sibling_ref, near_ref, far_ref, out_ref, done):
    chip, core = place_ref[0], place_ref[1]
    own_cap, span = own_ref.shape
    half = span // 2

    def rows(of_chip, of_core):
        return pl.ds(pl.multiple_of((2 * of_chip + of_core) * own_cap, own_cap), own_cap)

    def fetch(source, of_chip, of_core, columns, place):
        target = out_ref.at[rows(of_chip, of_core), columns]
        return pltpu.make_async_copy(source, target, done.at[place])

    def quadrant_copies(here):
        there = 1 - here
        columns = pl.ds(there * half, half)
        return (
            fetch(near_ref, there, core, columns, 2),
            fetch(far_ref, there, 1 - core, columns, 3),
        )

    everything = pl.ds(0, span)
    top = (
        fetch(own_ref, chip, core, everything, 0),
        fetch(sibling_ref, chip, 1 - core, everything, 1),
    )

    def of_chip(here):
        there = 1 - here
        copies = top + quadrant_copies(here)
        for copy in copies:
            copy.start()
        for copy in copies:
            copy.wait()
        here_rows = pl.ds(here * half, half)
        for tile in range(half // 128):
            columns = pl.ds(there * half + tile * 128, 128)
            strip = out_ref[here_rows, columns]
            turned = jnp.transpose(strip.astype(jnp.float32)).astype(jnp.bfloat16)
            out_ref[columns, here_rows] = turned

    @pl.when(chip == 0)
    def first():
        of_chip(0)

    @pl.when(chip == 1)
    def second():
        of_chip(1)

    across = jnp.ones((1, span), jnp.float32)
    for tile in range(span // 128):
        across = across + jnp.sum(
            out_ref[pl.ds(tile * 128, 128), :].astype(jnp.float32), axis=0, keepdims=True
        )
    across = lax.rsqrt(across)
    for tile in range(span // 128):
        strip = out_ref[pl.ds(tile * 128, 128), :].astype(jnp.float32)
        down = lax.rsqrt(1.0 + jnp.sum(strip, axis=1, keepdims=True))
        out_ref[pl.ds(tile * 128, 128), :] = (strip * down * across).astype(jnp.bfloat16)


def normalized_block(own, sibling, near, far, place):
    span = own.shape[1]
    return pl.pallas_call(
        assemble,
        out_shape=jax.ShapeDtypeStruct((span, span), jnp.bfloat16),
        in_specs=[pl.BlockSpec(memory_space=pltpu.SMEM)]
        + [pl.BlockSpec(memory_space=pltpu.HBM)] * 4,
        out_specs=pl.BlockSpec(memory_space=pltpu.VMEM),
        scratch_shapes=[pltpu.SemaphoreType.DMA((4,))],
        compiler_params=pltpu.CompilerParams(vmem_limit_bytes=VMEM_BYTES),
        cost_estimate=NO_COST,
        name="normalized_block",
    )(place, own, sibling, near, far)


def pack_kernel(
    keep_ref, row_codes_ref, col_codes_ref, row_keys_ref, col_keys_ref, weight_ref, out_ref,
    masked, picked, rows_hot, cols_hot
):
    tile_rows, tile_cols = weight_ref.shape
    blocks_down, blocks_across = keep_ref.shape
    groups, ignored, lanes = out_ref.shape
    send_cap, own_cap = rows_hot.shape[0] // groups, cols_hot.shape[0] // groups
    high, wide = tile_rows // blocks_down, tile_cols // blocks_across
    for down in range(blocks_down):
        for across in range(blocks_across):
            rows, columns = pl.ds(down * high, high), pl.ds(across * wide, wide)
            own, other = row_codes_ref[rows, :], col_codes_ref[:, columns]
            linked = (own == other) & (own % 2 == 1) & (keep_ref[down, across] == 1)
            weight = weight_ref[rows, columns].astype(jnp.float32)
            masked[rows, columns] = jnp.where(linked, weight, 0.0).astype(jnp.bfloat16)

    def one_hot(keys, start, count):
        standing = lax.broadcasted_iota(jnp.int32, (count, keys.shape[1]), 0) + start
        return jnp.where(standing == keys, 1.0, 0.0).astype(jnp.bfloat16)

    for group in range(groups):
        rows_hot[pl.ds(group * send_cap, send_cap), :] = one_hot(
            row_keys_ref[...], group * send_cap, send_cap
        )
        cols_hot[pl.ds(group * own_cap, own_cap), :] = one_hot(
            col_keys_ref[...], group * own_cap, own_cap
        )
    for tile in range(tile_cols // 256):
        columns = pl.ds(tile * 256, 256)
        picked[:, columns] = jnp.dot(
            rows_hot[...], masked[:, columns], preferred_element_type=jnp.float32
        ).astype(jnp.bfloat16)
    whole, half = own_cap // lanes, send_cap // 2
    for group in range(groups):
        packed = lax.dot_general(
            picked[pl.ds(group * send_cap, send_cap), :],
            cols_hot[pl.ds(group * own_cap, own_cap), :],
            (((1,), (1,)), ((), ())),
            preferred_element_type=jnp.float32,
        )
        for tile in range(whole):
            out_ref[group, pl.ds(tile * send_cap, send_cap), :] = packed[
                :, tile * lanes : (tile + 1) * lanes
            ].astype(jnp.bfloat16)
        ends = jnp.concatenate(
            [packed[:half, whole * lanes :], packed[half:, whole * lanes :]], axis=1
        )
        out_ref[group, pl.ds(whole * send_cap, half), :] = ends.astype(jnp.bfloat16)


def packed_pieces(block_keep, row_codes, col_codes, row_keys, col_keys, edge_weight, caps, groups):
    own_cap, send_cap = caps
    tile_rows, tile_cols = edge_weight.shape
    high = own_cap // 128 * send_cap + send_cap // 2
    vector = pl.BlockSpec(memory_space=pltpu.VMEM)
    return pl.pallas_call(
        pack_kernel,
        out_shape=jax.ShapeDtypeStruct((groups, high, 128), jnp.bfloat16),
        in_specs=[pl.BlockSpec(memory_space=pltpu.SMEM)] + [vector] * 5,
        out_specs=vector,
        scratch_shapes=[
            pltpu.VMEM((tile_rows, tile_cols), jnp.bfloat16),
            pltpu.VMEM((groups * send_cap, tile_cols), jnp.bfloat16),
            pltpu.VMEM((groups * send_cap, tile_rows), jnp.bfloat16),
            pltpu.VMEM((groups * own_cap, tile_cols), jnp.bfloat16),
        ],
        compiler_params=pltpu.CompilerParams(vmem_limit_bytes=VMEM_BYTES),
        cost_estimate=NO_COST,
        name="packed_pieces",
    )(block_keep, row_codes[:, None], col_codes[None], row_keys[None], col_keys[None], edge_weight)


def normal_share(mixed):
    return 0.5 * (1.0 + lax.erf(mixed * 0.5**0.5))


def norm_forward(mixed):
    active = mixed * normal_share(mixed)
    centered = active - jnp.mean(active, axis=-1, keepdims=True)
    scale = lax.rsqrt(jnp.mean(centered * centered, axis=-1, keepdims=True) + 1e-05)
    return centered * scale, scale


def norm_backward(mixed, upstream, gain, valid):
    normed, scale = norm_forward(mixed)
    upstream = upstream * valid
    inner = upstream * gain
    inner = inner - jnp.mean(inner, axis=-1, keepdims=True) - normed * jnp.mean(
        inner * normed, axis=-1, keepdims=True
    )
    density = jnp.exp(-0.5 * mixed * mixed) * (1.0 / (2.0 * math.pi) ** 0.5)
    low = (inner * scale * (normal_share(mixed) + mixed * density)).astype(jnp.bfloat16)
    rest = [low.astype(jnp.float32), upstream * normed, upstream]
    return low, [jnp.sum(value, axis=0, keepdims=True) for value in rest]


def weight_gradient(turned_ref, low, core, mine_ref, other_ref):
    part = turned_ref.shape[0] // 4

    def halves(first_ref, second_ref):
        for place in range(4):
            out_ref = second_ref if place % 2 else first_ref
            out_ref[place // 2, :part, :] = jnp.dot(
                turned_ref[place * part : (place + 1) * part, :],
                low,
                preferred_element_type=jnp.float32,
            ).astype(jnp.bfloat16)

    @pl.when(core == 0)
    def low_half_first():
        halves(mine_ref, other_ref)

    @pl.when(core == 1)
    def high_half_first():
        halves(other_ref, mine_ref)


def forward_step(step, powers_ref, all_ref, own_ref, weights, bias_ref, turned, mixed):
    terms, own_cap, span = powers_ref.shape
    fan_in = own_ref.shape[1]

    @pl.when(step == 0)
    def first():
        turned[:fan_in, :] = own_ref[...].T
        mixed[...] = bias_ref[...] + jnp.dot(
            own_ref[...], weights[0][0], preferred_element_type=jnp.float32
        )

    low = jnp.dot(
        powers_ref[...].reshape(terms * own_cap, span),
        all_ref[...],
        preferred_element_type=jnp.float32,
    ).astype(jnp.bfloat16)
    total = mixed[...]
    for term in range(terms):
        part = low[term * own_cap : (term + 1) * own_cap]
        start = pl.multiple_of((1 + step * terms + term) * fan_in, fan_in)
        turned[pl.ds(start, fan_in), :] = part.T
        total = total + jnp.dot(part, weights[1 + term][0], preferred_element_type=jnp.float32)
    mixed[...] = total


def layer_one_kernel(
    powers_ref,
    all_ref,
    own_ref,
    weight_0,
    weight_a,
    weight_b,
    weight_c,
    bias_ref,
    gain_ref,
    shift_ref,
    valid_ref,
    hidden_ref,
    turned_ref,
    mixed_ref,
):
    step = pl.program_id(0)
    weights = (weight_0, weight_a, weight_b, weight_c)
    forward_step(step, powers_ref, all_ref, own_ref, weights, bias_ref, turned_ref, mixed_ref)

    @pl.when(step == pl.num_programs(0) - 1)
    def finish_layer():
        normed, ignored = norm_forward(mixed_ref[...])
        hidden = (normed * gain_ref[...] + shift_ref[...]) * valid_ref[...]
        hidden_ref[...] = hidden.astype(jnp.bfloat16)


def layer_two_kernel(
    place_ref,
    powers_ref,
    all_ref,
    own_ref,
    weight_0,
    weight_a,
    weight_b,
    weight_c,
    bias_ref,
    gain_ref,
    shift_ref,
    valid_ref,
    upstream_ref,
    active_ref,
    low_ref,
    rest_ref,
    mine_ref,
    other_ref,
    turned,
    mixed,
):
    step = pl.program_id(0)
    weights = (weight_0, weight_a, weight_b, weight_c)
    forward_step(step, powers_ref, all_ref, own_ref, weights, bias_ref, turned, mixed)

    @pl.when(step == pl.num_programs(0) - 1)
    def finish_layer():
        normed, ignored = norm_forward(mixed[...])
        active = (normed * gain_ref[...] + shift_ref[...]) * valid_ref[...]
        active_ref[...] = active.astype(jnp.bfloat16)
        low, rest = norm_backward(
            mixed[...], upstream_ref[...].astype(jnp.float32), gain_ref[...], valid_ref[...]
        )
        low_ref[...] = low
        for place in range(3):
            rest_ref[place : place + 1, :] = rest[place]
        weight_gradient(turned, low, place_ref[1], mine_ref, other_ref)


def backward_step(step, powers_ref, all_ref, own_ref, weights, total):
    terms, own_cap, span = powers_ref.shape
    transposed = (((1,), (1,)), ((), ()))

    @pl.when(step == 0)
    def first():
        total[...] = lax.dot_general(
            own_ref[...], weights[0][0], transposed, preferred_element_type=jnp.float32
        )

    low = jnp.dot(
        powers_ref[...].reshape(terms * own_cap, span),
        all_ref[...],
        preferred_element_type=jnp.float32,
    ).astype(jnp.bfloat16)
    value = total[...]
    for term in range(terms):
        value = value + lax.dot_general(
            low[term * own_cap : (term + 1) * own_cap],
            weights[1 + term][0],
            transposed,
            preferred_element_type=jnp.float32,
        )
    total[...] = value


def back_two_kernel(
    place_ref,
    powers_ref,
    all_ref,
    own_ref,
    weight_0,
    weight_a,
    weight_b,
    weight_c,
    turned_ref,
    mixed_ref,
    gain_ref,
    valid_ref,
    rest_ref,
    low_ref,
    mine_ref,
    other_ref,
    total,
):
    step = pl.program_id(0)
    weights = (weight_0, weight_a, weight_b, weight_c)
    backward_step(step, powers_ref, all_ref, own_ref, weights, total)

    @pl.when(step == pl.num_programs(0) - 1)
    def finish_layer():
        low, rest = norm_backward(mixed_ref[...], total[...], gain_ref[...], valid_ref[...])
        low_ref[...] = low
        weight_gradient(turned_ref, low, place_ref[1], mine_ref, other_ref)
        part = turned_ref.shape[0] // 4
        extra = jnp.zeros((2, mine_ref.shape[1] - part, mine_ref.shape[2]), jnp.bfloat16)
        rows = rest + [rest_ref[place : place + 1, :] for place in range(3)]
        rows = jnp.concatenate(rows + [jnp.zeros((10, rows[0].shape[1]), jnp.float32)], axis=0)

        def below(first_ref, second_ref):
            first_ref[:, part:, :] = extra
            second_ref[:, part:, :] = extra
            first_ref[0, part : part + 16, :] = rows.astype(jnp.bfloat16)

        @pl.when(place_ref[1] == 0)
        def low_half_here():
            below(mine_ref, other_ref)

        @pl.when(place_ref[1] == 1)
        def low_half_there():
            below(other_ref, mine_ref)


def back_one_kernel(
    powers_ref, all_ref, own_ref, weight_0, weight_a, weight_b, weight_c, out_ref, total
):
    step = pl.program_id(0)
    weights = (weight_0, weight_a, weight_b, weight_c)
    backward_step(step, powers_ref, all_ref, own_ref, weights, total)

    @pl.when(step == pl.num_programs(0) - 1)
    def finish_layer():
        out_ref[...] = total[...].astype(jnp.bfloat16)


def layer_pass(kernel, name, place, powers, everyone, own, weight, others, outs, scratch):
    ignored, own_cap, span = powers.shape
    fan_in, width = weight.shape[1:]

    def whole(value):
        return pl.BlockSpec(value.shape, lambda step: (0,) * len(value.shape))

    def term_weight(term):
        return pl.BlockSpec((1, fan_in, width), lambda step: (1 + step * TERMS + term, 0, 0))

    in_specs = [
        pl.BlockSpec((TERMS, own_cap, span), lambda step: (step, 0, 0)),
        whole(everyone),
        whole(own),
        pl.BlockSpec((1, fan_in, width), lambda step: (0, 0, 0)),
    ]
    in_specs += [term_weight(term) for term in range(TERMS)] + [whole(value) for value in others]
    operands = [powers, everyone, own] + [weight] * (1 + TERMS) + list(others)
    if place is not None:
        in_specs = [pl.BlockSpec(memory_space=pltpu.SMEM)] + in_specs
        operands = [place] + operands
    return pl.pallas_call(
        kernel,
        grid=((ORDER - 1) // TERMS,),
        out_shape=outs,
        in_specs=in_specs,
        out_specs=[whole(value) for value in outs],
        scratch_shapes=[pltpu.VMEM(shape, dtype) for shape, dtype in scratch],
        compiler_params=pltpu.CompilerParams(vmem_limit_bytes=VMEM_BYTES),
        cost_estimate=NO_COST,
        name=name,
    )(*operands)


def finish_kernel(fits_ref, first_ref, second_ref, other_first, other_second, out_first, out_second):
    step, quarters = pl.program_id(0), pl.num_programs(0) // 2
    part = out_first.shape[1]

    def take(out_ref, fast, other):
        @pl.when(fits_ref[0] == 1)
        def fast_form():
            out_ref[0] = fast.astype(jnp.float32)

        @pl.when(fits_ref[0] == 0)
        def general_form():
            out_ref[0] = other.astype(jnp.float32)

    @pl.when(step < quarters)
    def layer_one():
        take(out_first, first_ref[0, :part, :], other_first[0])

    @pl.when(step >= quarters)
    def layer_two():
        take(out_second, second_ref[0], other_second[0])


def finished(fits, first, second, other_first, other_second):
    quarters, part_one, width = other_first.shape
    part_two = other_second.shape[1]

    def quarter_one(step, fits_ref):
        return jnp.minimum(step, quarters - 1), 0, 0

    def quarter_two(step, fits_ref):
        return jnp.maximum(step - quarters, 0), 0, 0

    def if_taken(quarter):
        return lambda step, fits_ref: ((1 - fits_ref[0]) * quarter(step, fits_ref)[0], 0, 0)

    one, two = (1, part_one, width), (1, part_two, width)
    return pl.pallas_call(
        finish_kernel,
        grid_spec=pltpu.PrefetchScalarGridSpec(
            num_scalar_prefetch=1,
            grid=(2 * quarters,),
            in_specs=[
                pl.BlockSpec((1,) + first.shape[1:], quarter_one),
                pl.BlockSpec(two, quarter_two),
                pl.BlockSpec(one, if_taken(quarter_one)),
                pl.BlockSpec(two, if_taken(quarter_two)),
            ],
            out_specs=[pl.BlockSpec(one, quarter_one), pl.BlockSpec(two, quarter_two)],
        ),
        out_shape=[
            jax.ShapeDtypeStruct(other_first.shape, jnp.float32),
            jax.ShapeDtypeStruct(other_second.shape, jnp.float32),
        ],
        compiler_params=pltpu.CompilerParams(vmem_limit_bytes=VMEM_BYTES),
        cost_estimate=NO_COST,
        name="finished",
    )(fits.astype(jnp.int32).reshape(1), first, second, other_first, other_second)


def exclusive_counts(member):
    count = member.shape[-1]
    before = jnp.arange(count)[:, None] < jnp.arange(count)[None, :]
    return jnp.dot(
        member.astype(jnp.bfloat16),
        before.astype(jnp.bfloat16),
        preferred_element_type=jnp.float32,
    ).astype(jnp.int32)


def assign(codes, n_row):
    cluster, valid = codes >> 1, codes & 1
    labels = jnp.arange(CLUSTERS)
    sizes = jnp.sum(
        (cluster.reshape(1, -1) == labels[:, None]) & (valid.reshape(1, -1) == 1), axis=1
    )
    ahead = (sizes[None, :] > sizes[:, None]) | (
        (sizes[None, :] == sizes[:, None]) & (labels[None, :] < labels[:, None])
    )
    rank = jnp.sum(ahead, axis=1)
    others = n_row - 1
    turn, place = (rank - 1) // others, (rank - 1) % others
    group = jnp.where(rank == 0, 0, 1 + jnp.where(turn == 0, place, others - 1 - place))
    of_node = jnp.sum(
        jnp.where(cluster[None] == labels[:, None, None, None], group[:, None, None, None], 0),
        axis=0,
    )
    return jnp.where(valid == 1, of_node, n_row)


def compact(
    codes,
    group,
    features,
    block_keep,
    edge_weight,
    weight_one,
    bias_one,
    gain_one,
    shift_one,
    weight_two,
    bias_two,
    gain_two,
    shift_two,
    cotangent,
    places_of,
    slots_of,
    seats_of,
    decide,
    nodes_col,
    sizes,
    caps,
):
    row, col = lax.axis_index("row"), lax.axis_index(COL)
    chip, core = lax.axis_index("chip"), lax.axis_index("core")
    n_row, n_col = sizes
    own_cap, send_cap, seat_cap = caps
    own_nodes, in_width = features.shape
    width = weight_two.shape[2]
    span = n_col * own_cap
    targets = jnp.arange(n_row)

    def in_col(value):
        return lax.dynamic_index_in_dim(value, col, 1, False).reshape(-1)

    def in_row(value):
        return lax.dynamic_index_in_dim(value, row, 0, False).reshape(-1)

    row_group, col_group = in_row(group), in_col(group)
    row_slots, col_places = in_row(slots_of(group)), in_col(places_of(group))
    row_keys = jnp.where(row_slots < send_cap, row_group * send_cap + row_slots, -1)
    col_keys = jnp.where(col_places < own_cap, col_group * own_cap + col_places, -1)
    pieces = packed_pieces(
        block_keep,
        in_row(codes),
        in_col(codes),
        row_keys,
        col_keys,
        edge_weight,
        (own_cap, send_cap),
        n_row,
    )
    pieces, codes = lax.optimization_barrier((pieces, codes))
    group = assign(codes, n_row)
    pieces = trade(pieces, "row")
    whole, half_send = own_cap // 128 * 128, send_cap // 2
    fits, others = decide(group)
    places, slots, seats = places_of(group), slots_of(group), seats_of(group)

    standing = jnp.arange(n_col)[None, :, None] * own_cap + places
    fits_here = jnp.where(group == row, standing, -1).reshape(n_row, -1)
    slot_of = slots.reshape(n_row, -1)
    target = jnp.max(
        jnp.where(
            slot_of[:, None, :] == jnp.arange(send_cap)[None, :, None], fits_here[:, None, :], -1
        ),
        axis=2,
    )
    spread = (target[:, :, None] == jnp.arange(span)[None, None, :]).astype(jnp.bfloat16)

    group_here = lax.dynamic_index_in_dim(in_row(group).reshape(n_col, -1), col, 0, False)
    seat_here = lax.dynamic_index_in_dim(in_row(seats).reshape(n_col, -1), col, 0, False)
    enter_home = (group_here[None, None, :] == targets[:, None, None]) & (
        seat_here[None, None, :] == jnp.arange(seat_cap)[None, :, None]
    )
    enter_home = enter_home.astype(jnp.bfloat16).reshape(n_row * seat_cap, own_nodes).T
    group_col = lax.dynamic_index_in_dim(group, col, 1, False)
    seats_col = lax.dynamic_index_in_dim(seats, col, 1, False)
    places_col = lax.dynamic_index_in_dim(places, col, 1, False)
    seated = (group_col == row)[:, None, :] & (
        seats_col[:, None, :] == jnp.arange(seat_cap)[None, :, None]
    )
    place_of_seat = jnp.max(jnp.where(seated, places_col[:, None, :], -1), axis=2)
    arrive = jnp.where(group_col == row, places_col, -1).reshape(1, -1)
    arrive = (arrive == jnp.arange(own_cap)[:, None]).astype(jnp.bfloat16)
    mine = jnp.dot(arrive, nodes_col)
    features_own, cotangent_own = mine[:, :in_width], mine[:, in_width : in_width + width]
    leave_group = place_of_seat.reshape(-1, 1) == jnp.arange(own_cap)[None, :]
    leave_group = leave_group.astype(jnp.bfloat16)
    held_count = jnp.sum(group_col == row)
    valid_rows = (jnp.arange(own_cap) < held_count).astype(jnp.float32)[:, None]
    place = jnp.stack([chip, core]).astype(jnp.int32)
    scalars = (chip, 1 - chip, chip * (span // 2), col * own_cap)
    scalars = tuple(value.astype(jnp.uint32) for value in scalars) + (chip == 0, core == 0, place)
    ready = (features_own, cotangent_own, spread, leave_group, enter_home, valid_rows, others)
    pieces, ready, scalars = lax.optimization_barrier((pieces, ready, scalars))
    features_own, cotangent_own, spread, leave_group, enter_home, valid_rows, others = ready
    this_chip, other_chip, chip_start, own_start, first_chip, first_core, place = scalars

    many = whole // 128
    tiles = pieces[:, : many * send_cap].reshape(n_row, many, send_cap, 128)
    ends = pieces[:, many * send_cap :].reshape(n_row, half_send, 2, own_cap - whole)
    own_block = jnp.concatenate(
        [
            jnp.einsum("sktu,stw->kuw", tiles, spread).reshape(whole, span),
            jnp.einsum("sthu,shtw->uw", ends, spread.reshape(n_row, 2, half_send, span)),
        ]
    ).astype(jnp.bfloat16)
    quadrant = lax.dynamic_slice_in_dim(own_block, chip_start, span // 2, 1)
    quadrant = swap(quadrant, "chip")
    sibling = swap(own_block, "core")
    adjacency = normalized_block(own_block, sibling, quadrant, swap(quadrant, "core"), place)
    sibling = swap(features_own, "core")

    first = (own_start + jnp.arange(own_cap, dtype=jnp.uint32))[:, None]
    first = first == jnp.arange(span, dtype=jnp.uint32)[None, :]
    previous = first.astype(jnp.float32)
    current = -lax.dynamic_slice_in_dim(adjacency, own_start, own_cap, 0).astype(jnp.float32)
    lowered = [current.astype(jnp.bfloat16)]
    for position in range(2, ORDER):
        upcoming = (
            -2.0 * jnp.dot(lowered[-1], adjacency, preferred_element_type=jnp.float32) - previous
        )
        low = upcoming.astype(jnp.bfloat16)
        if position == 4:
            low, sibling = lax.optimization_barrier((low, sibling))
            features_chip = joined(features_own, sibling, first_core)
            partner = swap(features_chip, "chip")
        if position == 8:
            low, partner = lax.optimization_barrier((low, partner))
            features_all = joined(features_chip, partner, first_chip)
        previous, current = current, upcoming
        lowered.append(low)
    powers = jnp.concatenate(lowered, axis=0).reshape(ORDER - 1, own_cap, span)

    def everywhere(value_low):
        return lax.all_gather(value_low, COL, axis=0, tiled=True)

    def chosen(value, other):
        return jnp.where(fits, value.astype(jnp.float32), other.astype(jnp.float32))

    def shaped(*shape, dtype=jnp.bfloat16):
        return jax.ShapeDtypeStruct(shape, dtype)

    part_one, part_two = ORDER * in_width // n_col, ORDER * width // n_col
    padded = -(-(part_one + 16) // (8 * n_row)) * (8 * n_row)
    hidden, turned_one, mixed_one = layer_pass(
        layer_one_kernel,
        "layer_one",
        None,
        powers,
        features_all,
        features_own,
        weight_one,
        [bias_one[None], gain_one[None], shift_one[None], valid_rows],
        [
            shaped(own_cap, width),
            shaped(n_col * part_one, own_cap),
            shaped(own_cap, width, dtype=jnp.float32),
        ],
        [],
    )
    activations, low_two, rest_two, mine, other = layer_pass(
        layer_two_kernel,
        "layer_two",
        place,
        powers,
        everywhere(hidden),
        hidden,
        weight_two,
        [bias_two[None], gain_two[None], shift_two[None], valid_rows, cotangent_own],
        [
            shaped(own_cap, width),
            shaped(own_cap, width),
            shaped(3, width, dtype=jnp.float32),
            shaped(2, part_two, width),
            shaped(2, part_two, width),
        ],
        [((n_col * part_two, own_cap), jnp.bfloat16), ((own_cap, width), jnp.float32)],
    )

    def add_cores(mine, other):
        got = swap(other, "core")
        return tuple(
            added(
                lax.dynamic_index_in_dim(mine, index, 0, False),
                lax.dynamic_index_in_dim(got, index, 0, False),
            )
            for index in (this_chip, other_chip)
        )

    leaving = jnp.dot(leave_group, activations).reshape(n_row, seat_cap, width)
    here, there = add_cores(mine, other)
    everyone_two, there = lax.optimization_barrier((everywhere(low_two), there))
    there = swap(there, "chip")
    low_one, mine, other = layer_pass(
        back_two_kernel,
        "back_two",
        place,
        powers,
        everyone_two,
        low_two,
        weight_two,
        [turned_one, mixed_one, gain_one[None], valid_rows, rest_two],
        [shaped(own_cap, width), shaped(2, padded, width), shaped(2, padded, width)],
        [((own_cap, width), jnp.float32)],
    )
    low_one, there = lax.optimization_barrier((low_one, there))
    second = added(here, there).reshape(n_row, -1, width)
    many = second.shape[1]
    second = jnp.concatenate([second, leaving], axis=1)
    low_one, second = lax.optimization_barrier((low_one, second))
    second = trade(second, "row")
    here, there = add_cores(mine, other)
    low_one, there = lax.optimization_barrier((low_one, there))
    everyone_one = everywhere(low_one)
    there = swap(there, "chip")
    everyone_one, second, there = lax.optimization_barrier((everyone_one, second, there))
    first = added(here, there).reshape(n_row, -1, width)
    share = first.shape[1]
    back = second[:, many:]
    second = jnp.sum(second[:, :many].astype(jnp.float32), axis=0).astype(jnp.bfloat16)
    second = jnp.broadcast_to(second[None], (n_row,) + second.shape)
    mixed = jnp.concatenate([first, second], axis=1)
    everyone_one, mixed = lax.optimization_barrier((everyone_one, mixed))
    mixed = trade(mixed, "row")
    (input_grad,) = layer_pass(
        back_one_kernel,
        "back_one",
        None,
        powers,
        everyone_one,
        low_one,
        weight_one,
        [],
        [shaped(own_cap, in_width)],
        [((own_cap, in_width), jnp.float32)],
    )
    leaving = jnp.dot(leave_group, input_grad).reshape(n_row, seat_cap * in_width // width, width)
    home = jnp.dot(enter_home, back.reshape(-1, width), preferred_element_type=jnp.float32)
    mixed, leaving, home = lax.optimization_barrier((mixed, leaving, home))
    first = jnp.sum(mixed[:, :share].astype(jnp.float32), axis=0).astype(jnp.bfloat16)
    first = jnp.broadcast_to(first[None], (n_row,) + first.shape)
    first, mixed = lax.optimization_barrier((jnp.concatenate([first, leaving], axis=1), mixed))
    first = trade(first, "row")
    second = lax.all_gather(mixed[:, share:].reshape(-1, width), COL, axis=0)
    back = first[:, share:].reshape(n_row * seat_cap, in_width)
    first = lax.all_gather(first[:, :share].reshape(-1, width), COL, axis=0)
    home_grad = jnp.dot(enter_home, back, preferred_element_type=jnp.float32)
    small = first[0, part_one : part_one + 6]
    first, second = finished(fits, first, second, others[2], others[3])
    return (
        chosen(home, others[0]),
        chosen(home_grad, others[1]),
        first,
        second,
        chosen(small, others[4]),
    )


def general(
    codes,
    features,
    block_keep,
    edge_weight,
    weight_one,
    bias_one,
    gain_one,
    shift_one,
    weight_two,
    bias_two,
    gain_two,
    shift_two,
    cotangent,
    node_valid,
):
    row, col = lax.axis_index("row"), lax.axis_index(COL)
    row_codes = lax.dynamic_index_in_dim(codes, row, 0, False).reshape(-1)
    col_codes = lax.dynamic_index_in_dim(codes, col, 1, False).reshape(-1)
    tile_rows, tile_cols = edge_weight.shape
    blocks_down, blocks_across = block_keep.shape
    block_side = tile_rows // blocks_down
    linked = (row_codes[:, None] == col_codes[None, :]) & (row_codes[:, None] & 1 == 1)
    linked = linked.reshape(blocks_down, block_side, blocks_across, block_side) & (
        block_keep[:, None, :, None] == 1
    )
    masked = edge_weight * linked.reshape(tile_rows, tile_cols).astype(jnp.bfloat16)
    degree_rows = 1.0 + lax.psum(jnp.sum(masked, axis=1, dtype=jnp.float32), COL)
    own_nodes = features.shape[0]
    own_degree = lax.dynamic_slice_in_dim(
        degree_rows, lax.axis_index(COL) * own_nodes, own_nodes, 0
    )
    degree_cols = lax.all_gather(own_degree, "row", axis=0, tiled=True)
    adjacency = (
        masked.astype(jnp.float32)
        * lax.rsqrt(degree_rows)[:, None]
        * lax.rsqrt(degree_cols)[None, :]
    ).astype(jnp.bfloat16)
    valid_rows = node_valid.astype(jnp.float32)
    stacked_one, mixed_one, hidden = layer_forward(
        adjacency,
        features.astype(jnp.float32),
        weight_one,
        bias_one,
        gain_one,
        shift_one,
        valid_rows,
    )
    stacked_two, mixed_two, activations = layer_forward(
        adjacency, hidden, weight_two, bias_two, gain_two, shift_two, valid_rows
    )
    hidden_grad, weight_two_grad, bias_two_grad, gain_two_grad, shift_two_grad = layer_backward(
        adjacency,
        stacked_two,
        mixed_two,
        cotangent.astype(jnp.float32),
        weight_two,
        gain_two,
        shift_two,
        valid_rows,
    )
    input_grad, weight_one_grad, bias_one_grad, gain_one_grad, shift_one_grad = layer_backward(
        adjacency, stacked_one, mixed_one, hidden_grad, weight_one, gain_one, shift_one, valid_rows
    )
    summed = lax.psum(
        (
            weight_one_grad,
            bias_one_grad,
            gain_one_grad,
            shift_one_grad,
            weight_two_grad,
            bias_two_grad,
            gain_two_grad,
            shift_two_grad,
        ),
        ("row",) + COL,
    )
    weight_one_grad, bias_one_grad, gain_one_grad, shift_one_grad = (
        summed[0],
        summed[1],
        summed[2],
        summed[3],
    )
    weight_two_grad, bias_two_grad, gain_two_grad, shift_two_grad = (
        summed[4],
        summed[5],
        summed[6],
        summed[7],
    )
    return (
        activations,
        input_grad,
        weight_one_grad,
        bias_one_grad,
        gain_one_grad,
        shift_one_grad,
        weight_two_grad,
        bias_two_grad,
        gain_two_grad,
        shift_two_grad,
    )


def local(n_row, n_col, *args):
    (
        features,
        node_valid,
        cluster,
        block_keep,
        edge_weight,
        weight_one,
        bias_one,
        gain_one,
        shift_one,
        weight_two,
        bias_two,
        gain_two,
        shift_two,
        cotangent,
    ) = args
    own_nodes, in_width = features.shape
    own_cap = own_nodes * n_row * 5 // 16
    send_cap = own_nodes * n_col * 11 // 32
    seat_cap = own_nodes // 2
    codes = broadcast_along(cluster * 2 + node_valid, ("row",) + COL, n_row * n_col)
    codes = codes.reshape(n_row, n_col, own_nodes)
    shared = (
        block_keep,
        edge_weight,
        weight_one,
        bias_one,
        gain_one,
        shift_one,
        weight_two,
        bias_two,
        gain_two,
        shift_two,
        cotangent,
    )

    def slow():
        return general(codes, features, *shared, node_valid)

    held = (ORDER - 1) * own_cap * own_cap * n_col * 2
    if held > HELD_BYTES or n_col != 4 or n_row < 2 or n_row & (n_row - 1):
        return slow()
    group = assign(codes, n_row)
    nodes_col = jnp.concatenate([features, cotangent], axis=1)
    lanes = max(0, GATHER_BYTES // (2 * own_nodes * n_row) - nodes_col.shape[1])
    nodes_col = jnp.pad(nodes_col, ((0, 0), (0, lanes)))
    nodes_col = lax.all_gather(nodes_col, "row", axis=0, tiled=True)

    def member_of(group):
        return group[None] == jnp.arange(n_row)[:, None, None, None]

    def places_of(group):
        member = member_of(group).transpose(0, 2, 1, 3).reshape(n_row, n_col, -1)
        places = jnp.sum(jnp.where(member, exclusive_counts(member), 0), axis=0)
        return places.reshape(n_col, n_row, own_nodes).transpose(1, 0, 2)

    def slots_of(group):
        member = member_of(group).reshape(n_row, n_row, -1)
        slots = jnp.sum(jnp.where(member, exclusive_counts(member), 0), axis=0)
        return slots.reshape(n_row, n_col, own_nodes)

    def seats_of(group):
        member = member_of(group)
        return jnp.sum(jnp.where(member, exclusive_counts(member), 0), axis=0)

    width = weight_two.shape[2]

    def instead(state):
        made = slow()
        small = jnp.stack([made[place] for place in (3, 4, 5, 7, 8, 9)])
        return (True,) + tuple(
            value.astype(jnp.bfloat16).reshape(like.shape)
            for value, like in zip((made[0], made[1], made[2], made[6], small), state[1:])
        )

    start = (
        cotangent,
        features,
        weight_one.reshape(n_col, -1, width),
        weight_two.reshape(n_col, -1, width),
        jnp.zeros((6, width), jnp.bfloat16),
    )

    def decide(group):
        member = member_of(group)
        fits = (
            (jnp.max(jnp.sum(member, axis=(1, 3))) <= own_cap)
            & (jnp.max(jnp.sum(member, axis=(2, 3))) <= send_cap)
            & (jnp.max(jnp.sum(member, axis=3)) <= seat_cap)
        )
        others = lax.while_loop(
            lambda state: jnp.logical_not(state[0]),
            instead,
            (fits,) + start,
        )[1:]
        return fits, others

    home, home_grad, first, second, small = compact(
        codes,
        group,
        features,
        *shared,
        places_of,
        slots_of,
        seats_of,
        decide,
        nodes_col,
        (n_row, n_col),
        (own_cap, send_cap, seat_cap),
    )
    return (
        home,
        home_grad,
        first.reshape(weight_one.shape),
        small[0],
        small[1],
        small[2],
        second.reshape(weight_two.shape),
        small[3],
        small[4],
        small[5],
    )


def solution(mesh):
    n_row, n_col = mesh.shape["row"], mesh.shape["col"]
    by_core = jax.sharding.Mesh(
        mesh.devices.reshape(n_row, n_col // 2, 2), ("row", "chip", "core")
    )
    nodes = ("row", "chip", "core")
    placed = (
        P(nodes, None),
        P(nodes),
        P(nodes),
        P("row", COL),
        P("row", COL),
        P(),
        P(),
        P(),
        P(),
        P(),
        P(),
        P(),
        P(),
        P(nodes, None),
    )
    return jax.shard_map(
        functools.partial(local, n_row, n_col),
        mesh=by_core,
        in_specs=placed,
        out_specs=(P(nodes, None), P(nodes, None), P(), P(), P(), P(), P(), P(), P(), P()),
        check_vma=False,
    )
```

```python
import functools
import math

import jax
import jax.numpy as jnp
from jax import lax
from jax.experimental import pallas as pl
from jax.experimental.pallas import tpu as pltpu
from jax.sharding import PartitionSpec as P

ORDER = 13
CLUSTERS = 16
HELD_BYTES = 1 << 25
VMEM_BYTES = 32 << 20
TERMS = 3
NO_COST = pl.CostEstimate(flops=1, bytes_accessed=1, transcendentals=0)
COL = ("chip", "core")


def finish(mixed, gain, shift, valid_rows):
    active = jax.nn.gelu(mixed, approximate=False)
    centered = active - jnp.mean(active, axis=-1, keepdims=True)
    variance = jnp.mean(centered * centered, axis=-1, keepdims=True)
    return (centered * lax.rsqrt(variance + 1e-05) * gain + shift) * valid_rows[:, None]


def forward_product(adjacency, piece_low):
    partial_value = jnp.dot(
        adjacency,
        lax.all_gather(piece_low, "row", axis=0, tiled=True),
        preferred_element_type=jnp.float32,
    )
    return lax.psum_scatter(partial_value, COL, scatter_dimension=0, tiled=True)


def backward_product(adjacency, piece_low):
    partial_value = lax.dot_general(
        adjacency,
        lax.all_gather(piece_low, COL, axis=0, tiled=True),
        (((0,), (0,)), ((), ())),
        preferred_element_type=jnp.float32,
    )
    return lax.psum_scatter(
        partial_value.astype(jnp.bfloat16), "row", scatter_dimension=0, tiled=True
    ).astype(jnp.float32)


def layer_forward(adjacency, inputs, weight, bias, gain, shift, valid_rows):
    first_low = inputs.astype(jnp.bfloat16)
    second = -forward_product(adjacency, first_low)
    second_low = second.astype(jnp.bfloat16)

    def advance(state_pair, unused):
        previous, current, current_low = state_pair
        upcoming = -2.0 * forward_product(adjacency, current_low) - previous
        upcoming_low = upcoming.astype(jnp.bfloat16)
        return ((current, upcoming, upcoming_low), upcoming_low)

    ignored, others = lax.scan(advance, (inputs, second, second_low), None, length=ORDER - 2)
    stacked = jnp.concatenate([first_low[None], second_low[None], others], axis=0)
    mixed = jnp.einsum("kni,kio->no", stacked, weight, preferred_element_type=jnp.float32) + bias
    return (stacked, mixed, finish(mixed, gain, shift, valid_rows))


def layer_backward(adjacency, stacked, mixed, upstream, weight, gain, shift, valid_rows):

    def local_finish(mixed_in, gain_in, shift_in):
        return finish(mixed_in, gain_in, shift_in, valid_rows)

    ignored, pullback = jax.vjp(local_finish, mixed, gain, shift)
    mixed_grad, gain_grad, shift_grad = pullback(upstream)
    mixed_low = mixed_grad.astype(jnp.bfloat16)
    bias_grad = jnp.sum(mixed_low.astype(jnp.float32), axis=0)
    weight_grad = jnp.einsum("kni,no->kio", stacked, mixed_low, preferred_element_type=jnp.float32)
    direct = jnp.einsum("no,kio->kni", mixed_low, weight, preferred_element_type=jnp.float32)

    def retreat(state_pair, direct_term):
        later_two, later_one = state_pair
        current = (
            direct_term
            - 2.0 * backward_product(adjacency, later_one.astype(jnp.bfloat16))
            - later_two
        )
        return ((later_one, current), None)

    start_pair = (jnp.zeros_like(direct[0]), direct[ORDER - 1])
    (second_grad, first_grad), unused = lax.scan(
        retreat, start_pair, direct[1 : ORDER - 1], reverse=True
    )
    input_grad = (
        direct[0] - backward_product(adjacency, first_grad.astype(jnp.bfloat16)) - second_grad
    )
    return (input_grad, weight_grad, bias_grad, gain_grad, shift_grad)


def swap(value, axis):
    return lax.ppermute(value, axis, [(0, 1), (1, 0)])


def trade(pieces, axis):
    return lax.all_to_all(pieces, axis, 0, 0, tiled=False)


def broadcast_along(value, axis, size):
    return trade(jnp.broadcast_to(value[None], (size,) + value.shape), axis)


def joined(mine, other, mine_first):
    return jnp.where(
        mine_first, jnp.concatenate([mine, other]), jnp.concatenate([other, mine])
    )


def added(mine, received):
    return (mine.astype(jnp.float32) + received.astype(jnp.float32)).astype(jnp.bfloat16)


def assemble(place_ref, own_ref, sibling_ref, near_ref, far_ref, out_ref, done):
    chip, core = place_ref[0], place_ref[1]
    own_cap, span = own_ref.shape
    half = span // 2

    def rows(of_chip, of_core):
        return pl.ds(pl.multiple_of((2 * of_chip + of_core) * own_cap, own_cap), own_cap)

    def fetch(source, of_chip, of_core, columns, place):
        target = out_ref.at[rows(of_chip, of_core), columns]
        return pltpu.make_async_copy(source, target, done.at[place])

    def quadrant_copies(here):
        there = 1 - here
        columns = pl.ds(there * half, half)
        return (
            fetch(near_ref, there, core, columns, 2),
            fetch(far_ref, there, 1 - core, columns, 3),
        )

    everything = pl.ds(0, span)
    top = (
        fetch(own_ref, chip, core, everything, 0),
        fetch(sibling_ref, chip, 1 - core, everything, 1),
    )

    def of_chip(here):
        there = 1 - here
        copies = top + quadrant_copies(here)
        for copy in copies:
            copy.start()
        for copy in copies:
            copy.wait()
        here_rows = pl.ds(here * half, half)
        for tile in range(half // 128):
            columns = pl.ds(there * half + tile * 128, 128)
            strip = out_ref[here_rows, columns]
            turned = jnp.transpose(strip.astype(jnp.float32)).astype(jnp.bfloat16)
            out_ref[columns, here_rows] = turned

    @pl.when(chip == 0)
    def first():
        of_chip(0)

    @pl.when(chip == 1)
    def second():
        of_chip(1)

    across = jnp.ones((1, span), jnp.float32)
    for tile in range(span // 128):
        across = across + jnp.sum(
            out_ref[pl.ds(tile * 128, 128), :].astype(jnp.float32), axis=0, keepdims=True
        )
    across = lax.rsqrt(across)
    for tile in range(span // 128):
        strip = out_ref[pl.ds(tile * 128, 128), :].astype(jnp.float32)
        down = lax.rsqrt(1.0 + jnp.sum(strip, axis=1, keepdims=True))
        out_ref[pl.ds(tile * 128, 128), :] = (strip * down * across).astype(jnp.bfloat16)


def normalized_block(own, sibling, near, far, place):
    span = own.shape[1]
    return pl.pallas_call(
        assemble,
        out_shape=jax.ShapeDtypeStruct((span, span), jnp.bfloat16),
        in_specs=[pl.BlockSpec(memory_space=pltpu.SMEM)]
        + [pl.BlockSpec(memory_space=pltpu.HBM)] * 4,
        out_specs=pl.BlockSpec(memory_space=pltpu.VMEM),
        scratch_shapes=[pltpu.SemaphoreType.DMA((4,))],
        compiler_params=pltpu.CompilerParams(vmem_limit_bytes=VMEM_BYTES),
        cost_estimate=NO_COST,
        name="normalized_block",
    )(place, own, sibling, near, far)


def pack_kernel(
    keep_ref, row_codes_ref, col_codes_ref, row_keys_ref, col_keys_ref, weight_ref, out_ref,
    masked, picked, rows_hot, cols_hot
):
    tile_rows, tile_cols = weight_ref.shape
    blocks_down, blocks_across = keep_ref.shape
    groups, ignored, lanes = out_ref.shape
    send_cap, own_cap = rows_hot.shape[0] // groups, cols_hot.shape[0] // groups
    high, wide = tile_rows // blocks_down, tile_cols // blocks_across
    for down in range(blocks_down):
        for across in range(blocks_across):
            rows, columns = pl.ds(down * high, high), pl.ds(across * wide, wide)
            own, other = row_codes_ref[rows, :], col_codes_ref[:, columns]
            linked = (own == other) & (own % 2 == 1) & (keep_ref[down, across] == 1)
            weight = weight_ref[rows, columns].astype(jnp.float32)
            masked[rows, columns] = jnp.where(linked, weight, 0.0).astype(jnp.bfloat16)

    def one_hot(keys, start, count):
        standing = lax.broadcasted_iota(jnp.int32, (count, keys.shape[1]), 0) + start
        return jnp.where(standing == keys, 1.0, 0.0).astype(jnp.bfloat16)

    for group in range(groups):
        rows_hot[pl.ds(group * send_cap, send_cap), :] = one_hot(
            row_keys_ref[...], group * send_cap, send_cap
        )
        cols_hot[pl.ds(group * own_cap, own_cap), :] = one_hot(
            col_keys_ref[...], group * own_cap, own_cap
        )
    for tile in range(tile_cols // 256):
        columns = pl.ds(tile * 256, 256)
        picked[:, columns] = jnp.dot(
            rows_hot[...], masked[:, columns], preferred_element_type=jnp.float32
        ).astype(jnp.bfloat16)
    whole, half = own_cap // lanes, send_cap // 2
    for group in range(groups):
        packed = lax.dot_general(
            picked[pl.ds(group * send_cap, send_cap), :],
            cols_hot[pl.ds(group * own_cap, own_cap), :],
            (((1,), (1,)), ((), ())),
            preferred_element_type=jnp.float32,
        )
        for tile in range(whole):
            out_ref[group, pl.ds(tile * send_cap, send_cap), :] = packed[
                :, tile * lanes : (tile + 1) * lanes
            ].astype(jnp.bfloat16)
        ends = jnp.concatenate(
            [packed[:half, whole * lanes :], packed[half:, whole * lanes :]], axis=1
        )
        out_ref[group, pl.ds(whole * send_cap, half), :] = ends.astype(jnp.bfloat16)


def packed_pieces(block_keep, row_codes, col_codes, row_keys, col_keys, edge_weight, caps, groups):
    own_cap, send_cap = caps
    tile_rows, tile_cols = edge_weight.shape
    high = own_cap // 128 * send_cap + send_cap // 2
    vector = pl.BlockSpec(memory_space=pltpu.VMEM)
    return pl.pallas_call(
        pack_kernel,
        out_shape=jax.ShapeDtypeStruct((groups, high, 128), jnp.bfloat16),
        in_specs=[pl.BlockSpec(memory_space=pltpu.SMEM)] + [vector] * 5,
        out_specs=vector,
        scratch_shapes=[
            pltpu.VMEM((tile_rows, tile_cols), jnp.bfloat16),
            pltpu.VMEM((groups * send_cap, tile_cols), jnp.bfloat16),
            pltpu.VMEM((groups * send_cap, tile_rows), jnp.bfloat16),
            pltpu.VMEM((groups * own_cap, tile_cols), jnp.bfloat16),
        ],
        compiler_params=pltpu.CompilerParams(vmem_limit_bytes=VMEM_BYTES),
        cost_estimate=NO_COST,
        name="packed_pieces",
    )(block_keep, row_codes[:, None], col_codes[None], row_keys[None], col_keys[None], edge_weight)


def normal_share(mixed):
    return 0.5 * (1.0 + lax.erf(mixed * 0.5**0.5))


def norm_forward(mixed):
    active = mixed * normal_share(mixed)
    centered = active - jnp.mean(active, axis=-1, keepdims=True)
    scale = lax.rsqrt(jnp.mean(centered * centered, axis=-1, keepdims=True) + 1e-05)
    return centered * scale, scale


def norm_backward(mixed, upstream, gain, valid):
    normed, scale = norm_forward(mixed)
    upstream = upstream * valid
    inner = upstream * gain
    inner = inner - jnp.mean(inner, axis=-1, keepdims=True) - normed * jnp.mean(
        inner * normed, axis=-1, keepdims=True
    )
    density = jnp.exp(-0.5 * mixed * mixed) * (1.0 / (2.0 * math.pi) ** 0.5)
    low = (inner * scale * (normal_share(mixed) + mixed * density)).astype(jnp.bfloat16)
    rest = [low.astype(jnp.float32), upstream * normed, upstream]
    return low, [jnp.sum(value, axis=0, keepdims=True) for value in rest]


def weight_gradient(turned_ref, low, core, mine_ref, other_ref):
    part = turned_ref.shape[0] // 4

    def halves(first_ref, second_ref):
        for place in range(4):
            out_ref = second_ref if place % 2 else first_ref
            out_ref[place // 2, :part, :] = jnp.dot(
                turned_ref[place * part : (place + 1) * part, :],
                low,
                preferred_element_type=jnp.float32,
            ).astype(jnp.bfloat16)

    @pl.when(core == 0)
    def low_half_first():
        halves(mine_ref, other_ref)

    @pl.when(core == 1)
    def high_half_first():
        halves(other_ref, mine_ref)


def forward_step(step, powers_ref, all_ref, own_ref, weights, bias_ref, turned, mixed):
    terms, own_cap, span = powers_ref.shape
    fan_in = own_ref.shape[1]

    @pl.when(step == 0)
    def first():
        turned[:fan_in, :] = own_ref[...].T
        mixed[...] = bias_ref[...] + jnp.dot(
            own_ref[...], weights[0][0], preferred_element_type=jnp.float32
        )

    low = jnp.dot(
        powers_ref[...].reshape(terms * own_cap, span),
        all_ref[...],
        preferred_element_type=jnp.float32,
    ).astype(jnp.bfloat16)
    total = mixed[...]
    for term in range(terms):
        part = low[term * own_cap : (term + 1) * own_cap]
        start = pl.multiple_of((1 + step * terms + term) * fan_in, fan_in)
        turned[pl.ds(start, fan_in), :] = part.T
        total = total + jnp.dot(part, weights[1 + term][0], preferred_element_type=jnp.float32)
    mixed[...] = total


def layer_one_kernel(
    powers_ref,
    all_ref,
    own_ref,
    weight_0,
    weight_a,
    weight_b,
    weight_c,
    bias_ref,
    gain_ref,
    shift_ref,
    valid_ref,
    hidden_ref,
    turned_ref,
    mixed_ref,
):
    step = pl.program_id(0)
    weights = (weight_0, weight_a, weight_b, weight_c)
    forward_step(step, powers_ref, all_ref, own_ref, weights, bias_ref, turned_ref, mixed_ref)

    @pl.when(step == pl.num_programs(0) - 1)
    def finish_layer():
        normed, ignored = norm_forward(mixed_ref[...])
        hidden = (normed * gain_ref[...] + shift_ref[...]) * valid_ref[...]
        hidden_ref[...] = hidden.astype(jnp.bfloat16)


def layer_two_kernel(
    place_ref,
    powers_ref,
    all_ref,
    own_ref,
    weight_0,
    weight_a,
    weight_b,
    weight_c,
    bias_ref,
    gain_ref,
    shift_ref,
    valid_ref,
    upstream_ref,
    active_ref,
    low_ref,
    rest_ref,
    mine_ref,
    other_ref,
    turned,
    mixed,
):
    step = pl.program_id(0)
    weights = (weight_0, weight_a, weight_b, weight_c)
    forward_step(step, powers_ref, all_ref, own_ref, weights, bias_ref, turned, mixed)

    @pl.when(step == pl.num_programs(0) - 1)
    def finish_layer():
        normed, ignored = norm_forward(mixed[...])
        active = (normed * gain_ref[...] + shift_ref[...]) * valid_ref[...]
        active_ref[...] = active.astype(jnp.bfloat16)
        low, rest = norm_backward(
            mixed[...], upstream_ref[...].astype(jnp.float32), gain_ref[...], valid_ref[...]
        )
        low_ref[...] = low
        for place in range(3):
            rest_ref[place : place + 1, :] = rest[place]
        weight_gradient(turned, low, place_ref[1], mine_ref, other_ref)


def backward_step(step, powers_ref, all_ref, own_ref, weights, total):
    terms, own_cap, span = powers_ref.shape
    transposed = (((1,), (1,)), ((), ()))

    @pl.when(step == 0)
    def first():
        total[...] = lax.dot_general(
            own_ref[...], weights[0][0], transposed, preferred_element_type=jnp.float32
        )

    low = jnp.dot(
        powers_ref[...].reshape(terms * own_cap, span),
        all_ref[...],
        preferred_element_type=jnp.float32,
    ).astype(jnp.bfloat16)
    value = total[...]
    for term in range(terms):
        value = value + lax.dot_general(
            low[term * own_cap : (term + 1) * own_cap],
            weights[1 + term][0],
            transposed,
            preferred_element_type=jnp.float32,
        )
    total[...] = value


def back_two_kernel(
    place_ref,
    powers_ref,
    all_ref,
    own_ref,
    weight_0,
    weight_a,
    weight_b,
    weight_c,
    turned_ref,
    mixed_ref,
    gain_ref,
    valid_ref,
    rest_ref,
    low_ref,
    mine_ref,
    other_ref,
    total,
):
    step = pl.program_id(0)
    weights = (weight_0, weight_a, weight_b, weight_c)
    backward_step(step, powers_ref, all_ref, own_ref, weights, total)

    @pl.when(step == pl.num_programs(0) - 1)
    def finish_layer():
        low, rest = norm_backward(mixed_ref[...], total[...], gain_ref[...], valid_ref[...])
        low_ref[...] = low
        weight_gradient(turned_ref, low, place_ref[1], mine_ref, other_ref)
        part = turned_ref.shape[0] // 4
        extra = jnp.zeros((2, mine_ref.shape[1] - part, mine_ref.shape[2]), jnp.bfloat16)
        rows = rest + [rest_ref[place : place + 1, :] for place in range(3)]
        rows = jnp.concatenate(rows + [jnp.zeros((10, rows[0].shape[1]), jnp.float32)], axis=0)

        def below(first_ref, second_ref):
            first_ref[:, part:, :] = extra
            second_ref[:, part:, :] = extra
            first_ref[0, part : part + 16, :] = rows.astype(jnp.bfloat16)

        @pl.when(place_ref[1] == 0)
        def low_half_here():
            below(mine_ref, other_ref)

        @pl.when(place_ref[1] == 1)
        def low_half_there():
            below(other_ref, mine_ref)


def back_one_kernel(
    powers_ref, all_ref, own_ref, weight_0, weight_a, weight_b, weight_c, out_ref, total
):
    step = pl.program_id(0)
    weights = (weight_0, weight_a, weight_b, weight_c)
    backward_step(step, powers_ref, all_ref, own_ref, weights, total)

    @pl.when(step == pl.num_programs(0) - 1)
    def finish_layer():
        out_ref[...] = total[...].astype(jnp.bfloat16)


def layer_pass(kernel, name, place, powers, everyone, own, weight, others, outs, scratch):
    ignored, own_cap, span = powers.shape
    fan_in, width = weight.shape[1:]

    def whole(value):
        return pl.BlockSpec(value.shape, lambda step: (0,) * len(value.shape))

    def term_weight(term):
        return pl.BlockSpec((1, fan_in, width), lambda step: (1 + step * TERMS + term, 0, 0))

    in_specs = [
        pl.BlockSpec((TERMS, own_cap, span), lambda step: (step, 0, 0)),
        whole(everyone),
        whole(own),
        pl.BlockSpec((1, fan_in, width), lambda step: (0, 0, 0)),
    ]
    in_specs += [term_weight(term) for term in range(TERMS)] + [whole(value) for value in others]
    operands = [powers, everyone, own] + [weight] * (1 + TERMS) + list(others)
    if place is not None:
        in_specs = [pl.BlockSpec(memory_space=pltpu.SMEM)] + in_specs
        operands = [place] + operands
    return pl.pallas_call(
        kernel,
        grid=((ORDER - 1) // TERMS,),
        out_shape=outs,
        in_specs=in_specs,
        out_specs=[whole(value) for value in outs],
        scratch_shapes=[pltpu.VMEM(shape, dtype) for shape, dtype in scratch],
        compiler_params=pltpu.CompilerParams(vmem_limit_bytes=VMEM_BYTES),
        cost_estimate=NO_COST,
        name=name,
    )(*operands)


def finish_kernel(scalars_ref, *refs):
    step = pl.program_id(0)
    if len(refs) == 3:
        values_ref, other_ref, out_ref = refs
        parts = [(step >= 0, values_ref)]
        small_ref = None
    else:
        pair_ref, siblings_ref, other_ref, out_ref, small_ref = refs
        parts = [(step < 2, pair_ref), (step >= 2, siblings_ref)]
    part = out_ref.shape[1]
    for here, values_ref in parts:
        @pl.when(here & (scalars_ref[0] == 1))
        def fast_form():
            out_ref[0] = values_ref[0, :part, :].astype(jnp.float32)

        if small_ref is not None:
            @pl.when(here & (scalars_ref[1 + step] == 0))
            def small_sums():
                small_ref[...] = values_ref[0, part : part + 16, :].astype(jnp.float32)

    @pl.when(scalars_ref[0] == 0)
    def general_form():
        out_ref[0] = other_ref[0].astype(jnp.float32)


def finished(scalars, pair, values, other):
    count, part, width = other.shape
    one = (1, part, width)
    if pair is None:
        operands, outs = [values, other], [jax.ShapeDtypeStruct(other.shape, jnp.float32)]

        def quarter(step, scalars_ref):
            return step

        in_specs = [pl.BlockSpec((1,) + values.shape[1:], lambda step, ref: (step, 0, 0))]
        small_specs = []
    else:
        operands = [pair, values, other]
        outs = [
            jax.ShapeDtypeStruct(other.shape, jnp.float32),
            jax.ShapeDtypeStruct((16, width), jnp.float32),
        ]

        def quarter(step, scalars_ref):
            return scalars_ref[1 + step]

        in_specs = [
            pl.BlockSpec((1,) + pair.shape[1:], lambda step, ref: (jnp.minimum(step, 1), 0, 0)),
            pl.BlockSpec((1,) + pair.shape[1:], lambda step, ref: (jnp.maximum(step - 2, 0), 0, 0)),
        ]
        small_specs = [pl.BlockSpec((16, width), lambda step, ref: (0, 0))]
    in_specs.append(
        pl.BlockSpec(one, lambda step, ref: ((1 - ref[0]) * quarter(step, ref), 0, 0))
    )
    result = pl.pallas_call(
        finish_kernel,
        grid_spec=pltpu.PrefetchScalarGridSpec(
            num_scalar_prefetch=1,
            grid=(count,),
            in_specs=in_specs,
            out_specs=[pl.BlockSpec(one, lambda step, ref: (quarter(step, ref), 0, 0))]
            + small_specs,
        ),
        out_shape=outs,
        compiler_params=pltpu.CompilerParams(vmem_limit_bytes=VMEM_BYTES),
        cost_estimate=NO_COST,
        name="finished",
    )(scalars, *operands)
    return result[0] if pair is None else result


def unpack_kernel(place_ref, pieces_ref, keys_ref, own_ref, quadrant_ref, columns, hot):
    groups, high, lanes = pieces_ref.shape
    own_cap, span = own_ref.shape
    whole = own_cap // lanes
    send_cap = keys_ref.shape[1] // groups
    half, rest = send_cap // 2, own_cap - whole * lanes
    for group in range(groups):
        start = group * send_cap
        for tile in range(whole):
            columns[start : start + send_cap, tile * lanes : (tile + 1) * lanes] = pieces_ref[
                group, tile * send_cap : (tile + 1) * send_cap, :
            ]
        ends = pieces_ref[group, whole * send_cap :, :]
        columns[start : start + half, whole * lanes :] = ends[:, :rest]
        columns[start + half : start + send_cap, whole * lanes :] = ends[:, rest:]
    standing = lax.broadcasted_iota(jnp.int32, hot.shape, 0)
    hot[...] = jnp.where(standing == keys_ref[...], 1.0, 0.0).astype(jnp.bfloat16)
    block = jnp.dot(hot[...], columns[...], preferred_element_type=jnp.float32)
    own_ref[...] = block.T.astype(jnp.bfloat16)
    middle = span // 2

    @pl.when(place_ref[0] == 0)
    def first():
        quadrant_ref[...] = own_ref[:, :middle]

    @pl.when(place_ref[0] == 1)
    def second():
        quadrant_ref[...] = own_ref[:, middle:]


def unpacked_block(pieces, keys, place, own_cap, span):
    vector = pl.BlockSpec(memory_space=pltpu.VMEM)
    return pl.pallas_call(
        unpack_kernel,
        out_shape=[
            jax.ShapeDtypeStruct((own_cap, span), jnp.bfloat16),
            jax.ShapeDtypeStruct((own_cap, span // 2), jnp.bfloat16),
        ],
        in_specs=[pl.BlockSpec(memory_space=pltpu.SMEM), vector, vector],
        out_specs=[vector, vector],
        scratch_shapes=[
            pltpu.VMEM((keys.shape[1], own_cap), jnp.bfloat16),
            pltpu.VMEM((span, keys.shape[1]), jnp.bfloat16),
        ],
        compiler_params=pltpu.CompilerParams(vmem_limit_bytes=VMEM_BYTES),
        cost_estimate=NO_COST,
        name="unpacked_block",
    )(place, pieces, keys)


def exclusive_counts(member):
    count = member.shape[-1]
    before = jnp.arange(count)[:, None] < jnp.arange(count)[None, :]
    return jnp.dot(
        member.astype(jnp.bfloat16),
        before.astype(jnp.bfloat16),
        preferred_element_type=jnp.float32,
    ).astype(jnp.int32)


def assign(codes, n_row):
    cluster, valid = codes >> 1, codes & 1
    labels = jnp.arange(CLUSTERS)
    sizes = jnp.sum(
        (cluster.reshape(1, -1) == labels[:, None]) & (valid.reshape(1, -1) == 1), axis=1
    )
    ahead = (sizes[None, :] > sizes[:, None]) | (
        (sizes[None, :] == sizes[:, None]) & (labels[None, :] < labels[:, None])
    )
    rank = jnp.sum(ahead, axis=1)
    others = n_row - 1
    turn, place = (rank - 1) // others, (rank - 1) % others
    group = jnp.where(rank == 0, 0, 1 + jnp.where(turn == 0, place, others - 1 - place))
    of_node = jnp.sum(
        jnp.where(cluster[None] == labels[:, None, None, None], group[:, None, None, None], 0),
        axis=0,
    )
    return jnp.where(valid == 1, of_node, n_row)


def compact(
    codes,
    group,
    features,
    block_keep,
    edge_weight,
    weight_one,
    bias_one,
    gain_one,
    shift_one,
    weight_two,
    bias_two,
    gain_two,
    shift_two,
    cotangent,
    places_of,
    slots_of,
    seats_of,
    decide,
    sizes,
    caps,
):
    row, col = lax.axis_index("row"), lax.axis_index(COL)
    chip, core = lax.axis_index("chip"), lax.axis_index("core")
    n_row, n_col = sizes
    own_cap, send_cap, seat_cap = caps
    own_nodes, in_width = features.shape
    width = weight_two.shape[2]
    span = n_col * own_cap
    targets = jnp.arange(n_row)

    def in_col(value):
        return lax.dynamic_index_in_dim(value, col, 1, False).reshape(-1)

    def in_row(value):
        return lax.dynamic_index_in_dim(value, row, 0, False).reshape(-1)

    row_group, col_group = in_row(group), in_col(group)
    row_slots, col_places = in_row(slots_of(group)), in_col(places_of(group))
    row_keys = jnp.where(row_slots < send_cap, row_group * send_cap + row_slots, -1)
    col_keys = jnp.where(col_places < own_cap, col_group * own_cap + col_places, -1)
    pieces = packed_pieces(
        block_keep,
        in_row(codes),
        in_col(codes),
        row_keys,
        col_keys,
        edge_weight,
        (own_cap, send_cap),
        n_row,
    )
    pieces, codes = lax.optimization_barrier((pieces, codes))
    group = assign(codes, n_row)
    pieces = trade(pieces, "row")
    fits, others = decide(group)
    places, slots, seats = places_of(group), slots_of(group), seats_of(group)

    standing = jnp.arange(n_col)[None, :, None] * own_cap + places
    fits_here = jnp.where(group == row, standing, -1).reshape(n_row, -1)
    slot_of = slots.reshape(n_row, -1)
    target = jnp.max(
        jnp.where(
            slot_of[:, None, :] == jnp.arange(send_cap)[None, :, None], fits_here[:, None, :], -1
        ),
        axis=2,
    )
    keys = target.reshape(1, -1)

    partners = row ^ targets
    group_here = lax.dynamic_index_in_dim(in_row(group).reshape(n_col, -1), col, 0, False)
    seat_here = lax.dynamic_index_in_dim(in_row(seats).reshape(n_col, -1), col, 0, False)

    def seat_of_node(groups):
        hot = (group_here[None, None, :] == groups[:, None, None]) & (
            seat_here[None, None, :] == jnp.arange(seat_cap)[None, :, None]
        )
        return hot.astype(jnp.bfloat16).reshape(n_row * seat_cap, own_nodes)

    both = jnp.dot(seat_of_node(partners), jnp.concatenate([features, cotangent], axis=1))
    both = both.reshape(n_row, seat_cap, -1)
    enter_home = seat_of_node(targets).T
    place_here = lax.dynamic_index_in_dim(in_row(places).reshape(n_col, -1), col, 0, False)
    enter_place = (group_here * own_cap + place_here)[:, None] == jnp.arange(n_row * own_cap)
    enter_place = enter_place.astype(jnp.bfloat16)
    group_col = lax.dynamic_index_in_dim(group, col, 1, False)
    seats_col = lax.dynamic_index_in_dim(seats, col, 1, False)
    places_col = lax.dynamic_index_in_dim(places, col, 1, False)
    seated = (group_col == row)[:, None, :] & (
        seats_col[:, None, :] == jnp.arange(seat_cap)[None, :, None]
    )
    place_of_seat = jnp.max(jnp.where(seated, places_col[:, None, :], -1), axis=2)
    from_partner = jnp.max(
        jnp.where((partners[:, None] == targets)[:, :, None], place_of_seat[None], -1), axis=1
    )
    arrive = from_partner.reshape(1, -1) == jnp.arange(own_cap)[:, None]
    arrive = arrive.astype(jnp.bfloat16)
    leave_group = place_of_seat.reshape(-1, 1) == jnp.arange(own_cap)[None, :]
    leave_group = leave_group.astype(jnp.bfloat16)
    held_count = jnp.sum(group_col == row)
    valid_rows = (jnp.arange(own_cap) < held_count).astype(jnp.float32)[:, None]
    place = jnp.stack([chip, core]).astype(jnp.int32)
    quarters = jnp.stack(
        [fits.astype(jnp.int32), col, (1 - chip) * 2 + core, chip * 2 + 1 - core, 3 - col]
    )
    scalars = (chip, 1 - chip, col * own_cap)
    scalars = tuple(value.astype(jnp.uint32) for value in scalars) + (chip == 0, core == 0, place, quarters)
    homes = enter_home, enter_place, leave_group
    pieces, both, keys, arrive, homes, valid_rows, others, scalars = lax.optimization_barrier(
        (pieces, both, keys, arrive, homes, valid_rows, others, scalars)
    )
    enter_home, enter_place, leave_group = homes
    this_chip, other_chip, own_start, first_chip, first_core, place, quarters = scalars

    own_block, quadrant = unpacked_block(pieces, keys, place, own_cap, span)
    quadrant = swap(quadrant, "chip")
    both = [both[0]] + [
        lax.ppermute(both[step], "row", [(place, place ^ step) for place in range(n_row)])
        for step in range(1, n_row)
    ]
    sibling = swap(own_block, "core")
    quadrant, *both = lax.optimization_barrier((quadrant, *both))
    adjacency = normalized_block(own_block, sibling, quadrant, swap(quadrant, "core"), place)
    mine = jnp.dot(arrive, jnp.concatenate(both))
    features_own, cotangent_own = mine[:, :in_width], mine[:, in_width:]
    sibling = swap(features_own, "core")

    first = (own_start + jnp.arange(own_cap, dtype=jnp.uint32))[:, None]
    first = first == jnp.arange(span, dtype=jnp.uint32)[None, :]
    previous = first.astype(jnp.float32)
    current = -lax.dynamic_slice_in_dim(adjacency, own_start, own_cap, 0).astype(jnp.float32)
    lowered = [current.astype(jnp.bfloat16)]
    for position in range(2, ORDER):
        upcoming = (
            -2.0 * jnp.dot(lowered[-1], adjacency, preferred_element_type=jnp.float32) - previous
        )
        low = upcoming.astype(jnp.bfloat16)
        if position == 4:
            low, sibling = lax.optimization_barrier((low, sibling))
            features_chip = joined(features_own, sibling, first_core)
            partner = swap(features_chip, "chip")
        if position == 8:
            low, partner = lax.optimization_barrier((low, partner))
            features_all = joined(features_chip, partner, first_chip)
        previous, current = current, upcoming
        lowered.append(low)
    powers = jnp.concatenate(lowered, axis=0).reshape(ORDER - 1, own_cap, span)

    def everywhere(value_low):
        return lax.all_gather(value_low, COL, axis=0, tiled=True)

    def chosen(value, other):
        return jnp.where(fits, value.astype(jnp.float32), other.astype(jnp.float32))

    def shaped(*shape, dtype=jnp.bfloat16):
        return jax.ShapeDtypeStruct(shape, dtype)

    part_one, part_two = ORDER * in_width // n_col, ORDER * width // n_col
    padded = -(-(part_one + 16) // (8 * n_row)) * (8 * n_row)
    hidden, turned_one, mixed_one = layer_pass(
        layer_one_kernel,
        "layer_one",
        None,
        powers,
        features_all,
        features_own,
        weight_one,
        [bias_one[None], gain_one[None], shift_one[None], valid_rows],
        [
            shaped(own_cap, width),
            shaped(n_col * part_one, own_cap),
            shaped(own_cap, width, dtype=jnp.float32),
        ],
        [],
    )
    activations, low_two, rest_two, mine, other = layer_pass(
        layer_two_kernel,
        "layer_two",
        place,
        powers,
        everywhere(hidden),
        hidden,
        weight_two,
        [bias_two[None], gain_two[None], shift_two[None], valid_rows, cotangent_own],
        [
            shaped(own_cap, width),
            shaped(own_cap, width),
            shaped(3, width, dtype=jnp.float32),
            shaped(2, part_two, width),
            shaped(2, part_two, width),
        ],
        [((n_col * part_two, own_cap), jnp.bfloat16), ((own_cap, width), jnp.float32)],
    )

    def add_cores(mine, other):
        got = swap(other, "core")
        return tuple(
            added(
                lax.dynamic_index_in_dim(mine, index, 0, False),
                lax.dynamic_index_in_dim(got, index, 0, False),
            )
            for index in (this_chip, other_chip)
        )

    activations_all = lax.all_gather(activations, "row", axis=0, tiled=True)
    here, there = add_cores(mine, other)
    everyone_two, there = lax.optimization_barrier((everywhere(low_two), there))
    there = swap(there, "chip")
    low_one, mine, other = layer_pass(
        back_two_kernel,
        "back_two",
        place,
        powers,
        everyone_two,
        low_two,
        weight_two,
        [turned_one, mixed_one, gain_one[None], valid_rows, rest_two],
        [shaped(own_cap, width), shaped(2, padded, width), shaped(2, padded, width)],
        [((own_cap, width), jnp.float32)],
    )
    low_one, there = lax.optimization_barrier((low_one, there))
    second = added(here, there).reshape(n_row, -1, width)
    low_one, second = lax.optimization_barrier((low_one, second))
    second = trade(second, "row")
    here, there = add_cores(mine, other)
    low_one, there = lax.optimization_barrier((low_one, there))
    everyone_one = everywhere(low_one)
    there = swap(there, "chip")
    everyone_one, second, there = lax.optimization_barrier((everyone_one, second, there))
    first = added(here, there).reshape(n_row, -1, width)
    share = first.shape[1]
    second = jnp.sum(second.astype(jnp.float32), axis=0).astype(jnp.bfloat16)
    second = jnp.broadcast_to(second[None], (n_row,) + second.shape)
    mixed = jnp.concatenate([first, second], axis=1)
    everyone_one, mixed = lax.optimization_barrier((everyone_one, mixed))
    mixed = trade(mixed, "row")
    (input_grad,) = layer_pass(
        back_one_kernel,
        "back_one",
        None,
        powers,
        everyone_one,
        low_one,
        weight_one,
        [],
        [shaped(own_cap, in_width)],
        [((own_cap, in_width), jnp.float32)],
    )
    leaving = jnp.dot(leave_group, input_grad).reshape(n_row, seat_cap * in_width // width, width)
    home = jnp.dot(enter_place, activations_all, preferred_element_type=jnp.float32)
    home = chosen(home, others[0])
    mixed, leaving, home = lax.optimization_barrier((mixed, leaving, home))
    first = jnp.sum(mixed[:, :share].astype(jnp.float32), axis=0).astype(jnp.bfloat16)
    first = jnp.broadcast_to(first[None], (n_row,) + first.shape)
    first, mixed = lax.optimization_barrier((jnp.concatenate([first, leaving], axis=1), mixed))
    first = trade(first, "row")
    second = lax.all_gather(mixed[:, share:].reshape(-1, width), COL, axis=0)
    back = first[:, share:].reshape(n_row * seat_cap, in_width)
    mine = first[:, :share].reshape(1, -1, width)
    pair = jnp.concatenate([mine, swap(mine, "chip")])
    siblings = swap(pair, "core")
    home_grad = jnp.dot(enter_home, back, preferred_element_type=jnp.float32)
    second = finished(quarters[:1], None, second, others[3])
    siblings, second = lax.optimization_barrier((siblings, second))
    first, small = finished(quarters, pair, siblings, others[2])
    return (
        home,
        chosen(home_grad, others[1]),
        first,
        second,
        chosen(small[:6], others[4]),
    )


def general(
    codes,
    features,
    block_keep,
    edge_weight,
    weight_one,
    bias_one,
    gain_one,
    shift_one,
    weight_two,
    bias_two,
    gain_two,
    shift_two,
    cotangent,
    node_valid,
):
    row, col = lax.axis_index("row"), lax.axis_index(COL)
    row_codes = lax.dynamic_index_in_dim(codes, row, 0, False).reshape(-1)
    col_codes = lax.dynamic_index_in_dim(codes, col, 1, False).reshape(-1)
    tile_rows, tile_cols = edge_weight.shape
    blocks_down, blocks_across = block_keep.shape
    block_side = tile_rows // blocks_down
    linked = (row_codes[:, None] == col_codes[None, :]) & (row_codes[:, None] & 1 == 1)
    linked = linked.reshape(blocks_down, block_side, blocks_across, block_side) & (
        block_keep[:, None, :, None] == 1
    )
    masked = edge_weight * linked.reshape(tile_rows, tile_cols).astype(jnp.bfloat16)
    degree_rows = 1.0 + lax.psum(jnp.sum(masked, axis=1, dtype=jnp.float32), COL)
    own_nodes = features.shape[0]
    own_degree = lax.dynamic_slice_in_dim(
        degree_rows, lax.axis_index(COL) * own_nodes, own_nodes, 0
    )
    degree_cols = lax.all_gather(own_degree, "row", axis=0, tiled=True)
    adjacency = (
        masked.astype(jnp.float32)
        * lax.rsqrt(degree_rows)[:, None]
        * lax.rsqrt(degree_cols)[None, :]
    ).astype(jnp.bfloat16)
    valid_rows = node_valid.astype(jnp.float32)
    stacked_one, mixed_one, hidden = layer_forward(
        adjacency,
        features.astype(jnp.float32),
        weight_one,
        bias_one,
        gain_one,
        shift_one,
        valid_rows,
    )
    stacked_two, mixed_two, activations = layer_forward(
        adjacency, hidden, weight_two, bias_two, gain_two, shift_two, valid_rows
    )
    hidden_grad, weight_two_grad, bias_two_grad, gain_two_grad, shift_two_grad = layer_backward(
        adjacency,
        stacked_two,
        mixed_two,
        cotangent.astype(jnp.float32),
        weight_two,
        gain_two,
        shift_two,
        valid_rows,
    )
    input_grad, weight_one_grad, bias_one_grad, gain_one_grad, shift_one_grad = layer_backward(
        adjacency, stacked_one, mixed_one, hidden_grad, weight_one, gain_one, shift_one, valid_rows
    )
    summed = lax.psum(
        (
            weight_one_grad,
            bias_one_grad,
            gain_one_grad,
            shift_one_grad,
            weight_two_grad,
            bias_two_grad,
            gain_two_grad,
            shift_two_grad,
        ),
        ("row",) + COL,
    )
    weight_one_grad, bias_one_grad, gain_one_grad, shift_one_grad = (
        summed[0],
        summed[1],
        summed[2],
        summed[3],
    )
    weight_two_grad, bias_two_grad, gain_two_grad, shift_two_grad = (
        summed[4],
        summed[5],
        summed[6],
        summed[7],
    )
    return (
        activations,
        input_grad,
        weight_one_grad,
        bias_one_grad,
        gain_one_grad,
        shift_one_grad,
        weight_two_grad,
        bias_two_grad,
        gain_two_grad,
        shift_two_grad,
    )


def local(n_row, n_col, *args):
    (
        features,
        node_valid,
        cluster,
        block_keep,
        edge_weight,
        weight_one,
        bias_one,
        gain_one,
        shift_one,
        weight_two,
        bias_two,
        gain_two,
        shift_two,
        cotangent,
    ) = args
    own_nodes, in_width = features.shape
    own_cap = own_nodes * n_row * 5 // 16
    send_cap = own_nodes * n_col * 11 // 32
    seat_cap = own_nodes // 2
    codes = broadcast_along(cluster * 2 + node_valid, ("row",) + COL, n_row * n_col)
    codes = codes.reshape(n_row, n_col, own_nodes)
    shared = (
        block_keep,
        edge_weight,
        weight_one,
        bias_one,
        gain_one,
        shift_one,
        weight_two,
        bias_two,
        gain_two,
        shift_two,
        cotangent,
    )

    def slow():
        return general(codes, features, *shared, node_valid)

    held = (ORDER - 1) * own_cap * own_cap * n_col * 2
    if held > HELD_BYTES or n_col != 4 or n_row < 2 or n_row & (n_row - 1):
        return slow()
    group = assign(codes, n_row)

    def member_of(group):
        return group[None] == jnp.arange(n_row)[:, None, None, None]

    def places_of(group):
        member = member_of(group).transpose(0, 2, 1, 3).reshape(n_row, n_col, -1)
        places = jnp.sum(jnp.where(member, exclusive_counts(member), 0), axis=0)
        return places.reshape(n_col, n_row, own_nodes).transpose(1, 0, 2)

    def slots_of(group):
        member = member_of(group).reshape(n_row, n_row, -1)
        slots = jnp.sum(jnp.where(member, exclusive_counts(member), 0), axis=0)
        return slots.reshape(n_row, n_col, own_nodes)

    def seats_of(group):
        member = member_of(group)
        return jnp.sum(jnp.where(member, exclusive_counts(member), 0), axis=0)

    width = weight_two.shape[2]

    def instead(state):
        made = slow()
        small = jnp.stack([made[place] for place in (3, 4, 5, 7, 8, 9)])
        return (True,) + tuple(
            value.astype(jnp.bfloat16).reshape(like.shape)
            for value, like in zip((made[0], made[1], made[2], made[6], small), state[1:])
        )

    start = (
        cotangent,
        features,
        weight_one.reshape(n_col, -1, width),
        weight_two.reshape(n_col, -1, width),
        jnp.zeros((6, width), jnp.bfloat16),
    )

    def decide(group):
        member = member_of(group)
        fits = (
            (jnp.max(jnp.sum(member, axis=(1, 3))) <= own_cap)
            & (jnp.max(jnp.sum(member, axis=(2, 3))) <= send_cap)
            & (jnp.max(jnp.sum(member, axis=3)) <= seat_cap)
        )
        others = lax.while_loop(
            lambda state: jnp.logical_not(state[0]),
            instead,
            (fits,) + start,
        )[1:]
        return fits, others

    home, home_grad, first, second, small = compact(
        codes,
        group,
        features,
        *shared,
        places_of,
        slots_of,
        seats_of,
        decide,
        (n_row, n_col),
        (own_cap, send_cap, seat_cap),
    )
    return (
        home,
        home_grad,
        first.reshape(weight_one.shape),
        small[0],
        small[1],
        small[2],
        second.reshape(weight_two.shape),
        small[3],
        small[4],
        small[5],
    )


def solution(mesh):
    n_row, n_col = mesh.shape["row"], mesh.shape["col"]
    by_core = jax.sharding.Mesh(
        mesh.devices.reshape(n_row, n_col // 2, 2), ("row", "chip", "core")
    )
    nodes = ("row", "chip", "core")
    placed = (
        P(nodes, None),
        P(nodes),
        P(nodes),
        P("row", COL),
        P("row", COL),
        P(),
        P(),
        P(),
        P(),
        P(),
        P(),
        P(),
        P(),
        P(nodes, None),
    )
    return jax.shard_map(
        functools.partial(local, n_row, n_col),
        mesh=by_core,
        in_specs=placed,
        out_specs=(P(nodes, None), P(nodes, None), P(), P(), P(), P(), P(), P(), P(), P()),
        check_vma=False,
    )
```

```python
import functools
import math

import jax
import jax.numpy as jnp
from jax import lax
from jax.experimental import pallas as pl
from jax.experimental.pallas import tpu as pltpu
from jax.sharding import PartitionSpec as P

ORDER = 13
CLUSTERS = 16
HELD_BYTES = 1 << 25
VMEM_BYTES = 32 << 20
ALL_VMEM_BYTES = 60 << 20
TERMS = 3
NO_COST = pl.CostEstimate(flops=1, bytes_accessed=1, transcendentals=0)
COL = ("chip", "core")


def finish(mixed, gain, shift, valid_rows):
    active = jax.nn.gelu(mixed, approximate=False)
    centered = active - jnp.mean(active, axis=-1, keepdims=True)
    variance = jnp.mean(centered * centered, axis=-1, keepdims=True)
    return (centered * lax.rsqrt(variance + 1e-05) * gain + shift) * valid_rows[:, None]


def forward_product(adjacency, piece_low):
    partial_value = jnp.dot(
        adjacency,
        lax.all_gather(piece_low, "row", axis=0, tiled=True),
        preferred_element_type=jnp.float32,
    )
    return lax.psum_scatter(partial_value, COL, scatter_dimension=0, tiled=True)


def backward_product(adjacency, piece_low):
    partial_value = lax.dot_general(
        adjacency,
        lax.all_gather(piece_low, COL, axis=0, tiled=True),
        (((0,), (0,)), ((), ())),
        preferred_element_type=jnp.float32,
    )
    return lax.psum_scatter(
        partial_value.astype(jnp.bfloat16), "row", scatter_dimension=0, tiled=True
    ).astype(jnp.float32)


def layer_forward(adjacency, inputs, weight, bias, gain, shift, valid_rows):
    first_low = inputs.astype(jnp.bfloat16)
    second = -forward_product(adjacency, first_low)
    second_low = second.astype(jnp.bfloat16)

    def advance(state_pair, unused):
        previous, current, current_low = state_pair
        upcoming = -2.0 * forward_product(adjacency, current_low) - previous
        upcoming_low = upcoming.astype(jnp.bfloat16)
        return ((current, upcoming, upcoming_low), upcoming_low)

    ignored, others = lax.scan(advance, (inputs, second, second_low), None, length=ORDER - 2)
    stacked = jnp.concatenate([first_low[None], second_low[None], others], axis=0)
    mixed = jnp.einsum("kni,kio->no", stacked, weight, preferred_element_type=jnp.float32) + bias
    return (stacked, mixed, finish(mixed, gain, shift, valid_rows))


def layer_backward(adjacency, stacked, mixed, upstream, weight, gain, shift, valid_rows):

    def local_finish(mixed_in, gain_in, shift_in):
        return finish(mixed_in, gain_in, shift_in, valid_rows)

    ignored, pullback = jax.vjp(local_finish, mixed, gain, shift)
    mixed_grad, gain_grad, shift_grad = pullback(upstream)
    mixed_low = mixed_grad.astype(jnp.bfloat16)
    bias_grad = jnp.sum(mixed_low.astype(jnp.float32), axis=0)
    weight_grad = jnp.einsum("kni,no->kio", stacked, mixed_low, preferred_element_type=jnp.float32)
    direct = jnp.einsum("no,kio->kni", mixed_low, weight, preferred_element_type=jnp.float32)

    def retreat(state_pair, direct_term):
        later_two, later_one = state_pair
        current = (
            direct_term
            - 2.0 * backward_product(adjacency, later_one.astype(jnp.bfloat16))
            - later_two
        )
        return ((later_one, current), None)

    start_pair = (jnp.zeros_like(direct[0]), direct[ORDER - 1])
    (second_grad, first_grad), unused = lax.scan(
        retreat, start_pair, direct[1 : ORDER - 1], reverse=True
    )
    input_grad = (
        direct[0] - backward_product(adjacency, first_grad.astype(jnp.bfloat16)) - second_grad
    )
    return (input_grad, weight_grad, bias_grad, gain_grad, shift_grad)


def swap(value, axis):
    return lax.ppermute(value, axis, [(0, 1), (1, 0)])


def trade(pieces, axis):
    return lax.all_to_all(pieces, axis, 0, 0, tiled=False)


def broadcast_along(value, axis, size):
    return trade(jnp.broadcast_to(value[None], (size,) + value.shape), axis)


def joined(mine, other, mine_first):
    return jnp.where(
        mine_first, jnp.concatenate([mine, other]), jnp.concatenate([other, mine])
    )


def added(mine, received):
    return (mine.astype(jnp.float32) + received.astype(jnp.float32)).astype(jnp.bfloat16)


def assemble(place_ref, own_ref, sibling_ref, near_ref, far_ref, out_ref, done):
    chip, core = place_ref[0], place_ref[1]
    own_cap, span = own_ref.shape
    half = span // 2

    def rows(of_chip, of_core):
        return pl.ds(pl.multiple_of((2 * of_chip + of_core) * own_cap, own_cap), own_cap)

    def fetch(source, of_chip, of_core, columns, place):
        target = out_ref.at[rows(of_chip, of_core), columns]
        return pltpu.make_async_copy(source, target, done.at[place])

    def quadrant_copies(here):
        there = 1 - here
        columns = pl.ds(there * half, half)
        return (
            fetch(near_ref, there, core, columns, 2),
            fetch(far_ref, there, 1 - core, columns, 3),
        )

    everything = pl.ds(0, span)
    top = (
        fetch(own_ref, chip, core, everything, 0),
        fetch(sibling_ref, chip, 1 - core, everything, 1),
    )

    def of_chip(here):
        there = 1 - here
        copies = top + quadrant_copies(here)
        for copy in copies:
            copy.start()
        for copy in copies:
            copy.wait()
        here_rows = pl.ds(here * half, half)
        for tile in range(half // 128):
            columns = pl.ds(there * half + tile * 128, 128)
            strip = out_ref[here_rows, columns]
            turned = jnp.transpose(strip.astype(jnp.float32)).astype(jnp.bfloat16)
            out_ref[columns, here_rows] = turned

    @pl.when(chip == 0)
    def first():
        of_chip(0)

    @pl.when(chip == 1)
    def second():
        of_chip(1)

    across = jnp.ones((1, span), jnp.float32)
    for tile in range(span // 128):
        across = across + jnp.sum(
            out_ref[pl.ds(tile * 128, 128), :].astype(jnp.float32), axis=0, keepdims=True
        )
    across = lax.rsqrt(across)
    for tile in range(span // 128):
        strip = out_ref[pl.ds(tile * 128, 128), :].astype(jnp.float32)
        down = lax.rsqrt(1.0 + jnp.sum(strip, axis=1, keepdims=True))
        out_ref[pl.ds(tile * 128, 128), :] = (strip * down * across).astype(jnp.bfloat16)


def normalized_block(own, sibling, near, far, place):
    span = own.shape[1]
    return pl.pallas_call(
        assemble,
        out_shape=jax.ShapeDtypeStruct((span, span), jnp.bfloat16),
        in_specs=[pl.BlockSpec(memory_space=pltpu.SMEM)]
        + [pl.BlockSpec(memory_space=pltpu.HBM)] * 4,
        out_specs=pl.BlockSpec(memory_space=pltpu.VMEM),
        scratch_shapes=[pltpu.SemaphoreType.DMA((4,))],
        compiler_params=pltpu.CompilerParams(vmem_limit_bytes=VMEM_BYTES),
        cost_estimate=NO_COST,
        name="normalized_block",
    )(place, own, sibling, near, far)


def pack_kernel(
    keep_ref, row_codes_ref, col_codes_ref, row_keys_ref, col_keys_ref, weight_ref, out_ref,
    masked, picked, rows_hot, cols_hot
):
    tile_rows, tile_cols = weight_ref.shape
    blocks_down, blocks_across = keep_ref.shape
    groups, ignored, lanes = out_ref.shape
    send_cap, own_cap = rows_hot.shape[0] // groups, cols_hot.shape[0] // groups
    high, wide = tile_rows // blocks_down, tile_cols // blocks_across
    for down in range(blocks_down):
        for across in range(blocks_across):
            rows, columns = pl.ds(down * high, high), pl.ds(across * wide, wide)
            own, other = row_codes_ref[rows, :], col_codes_ref[:, columns]
            linked = (own == other) & (own % 2 == 1) & (keep_ref[down, across] == 1)
            weight = weight_ref[rows, columns].astype(jnp.float32)
            masked[rows, columns] = jnp.where(linked, weight, 0.0).astype(jnp.bfloat16)

    def one_hot(keys, start, count):
        standing = lax.broadcasted_iota(jnp.int32, (count, keys.shape[1]), 0) + start
        return jnp.where(standing == keys, 1.0, 0.0).astype(jnp.bfloat16)

    for group in range(groups):
        rows_hot[pl.ds(group * send_cap, send_cap), :] = one_hot(
            row_keys_ref[...], group * send_cap, send_cap
        )
        cols_hot[pl.ds(group * own_cap, own_cap), :] = one_hot(
            col_keys_ref[...], group * own_cap, own_cap
        )
    for tile in range(tile_cols // 256):
        columns = pl.ds(tile * 256, 256)
        picked[:, columns] = jnp.dot(
            rows_hot[...], masked[:, columns], preferred_element_type=jnp.float32
        ).astype(jnp.bfloat16)
    whole, half = own_cap // lanes, send_cap // 2
    for group in range(groups):
        packed = lax.dot_general(
            picked[pl.ds(group * send_cap, send_cap), :],
            cols_hot[pl.ds(group * own_cap, own_cap), :],
            (((1,), (1,)), ((), ())),
            preferred_element_type=jnp.float32,
        )
        for tile in range(whole):
            out_ref[group, pl.ds(tile * send_cap, send_cap), :] = packed[
                :, tile * lanes : (tile + 1) * lanes
            ].astype(jnp.bfloat16)
        ends = jnp.concatenate(
            [packed[:half, whole * lanes :], packed[half:, whole * lanes :]], axis=1
        )
        out_ref[group, pl.ds(whole * send_cap, half), :] = ends.astype(jnp.bfloat16)


def packed_pieces(block_keep, row_codes, col_codes, row_keys, col_keys, edge_weight, caps, groups):
    own_cap, send_cap = caps
    tile_rows, tile_cols = edge_weight.shape
    high = own_cap // 128 * send_cap + send_cap // 2
    vector = pl.BlockSpec(memory_space=pltpu.VMEM)
    return pl.pallas_call(
        pack_kernel,
        out_shape=jax.ShapeDtypeStruct((groups, high, 128), jnp.bfloat16),
        in_specs=[pl.BlockSpec(memory_space=pltpu.SMEM)] + [vector] * 5,
        out_specs=vector,
        scratch_shapes=[
            pltpu.VMEM((tile_rows, tile_cols), jnp.bfloat16),
            pltpu.VMEM((groups * send_cap, tile_cols), jnp.bfloat16),
            pltpu.VMEM((groups * send_cap, tile_rows), jnp.bfloat16),
            pltpu.VMEM((groups * own_cap, tile_cols), jnp.bfloat16),
        ],
        compiler_params=pltpu.CompilerParams(vmem_limit_bytes=VMEM_BYTES),
        cost_estimate=NO_COST,
        name="packed_pieces",
    )(block_keep, row_codes[:, None], col_codes[None], row_keys[None], col_keys[None], edge_weight)


def normal_share(mixed):
    return 0.5 * (1.0 + lax.erf(mixed * 0.5**0.5))


def norm_forward(mixed):
    active = mixed * normal_share(mixed)
    centered = active - jnp.mean(active, axis=-1, keepdims=True)
    scale = lax.rsqrt(jnp.mean(centered * centered, axis=-1, keepdims=True) + 1e-05)
    return centered * scale, scale


def norm_backward(mixed, upstream, gain, valid):
    normed, scale = norm_forward(mixed)
    upstream = upstream * valid
    inner = upstream * gain
    inner = inner - jnp.mean(inner, axis=-1, keepdims=True) - normed * jnp.mean(
        inner * normed, axis=-1, keepdims=True
    )
    density = jnp.exp(-0.5 * mixed * mixed) * (1.0 / (2.0 * math.pi) ** 0.5)
    low = (inner * scale * (normal_share(mixed) + mixed * density)).astype(jnp.bfloat16)
    rest = [low.astype(jnp.float32), upstream * normed, upstream]
    return low, [jnp.sum(value, axis=0, keepdims=True) for value in rest]


def weight_gradient(turned_ref, low, core, mine_ref, other_ref):
    part = turned_ref.shape[0] // 4

    def halves(first_ref, second_ref):
        for place in range(4):
            out_ref = second_ref if place % 2 else first_ref
            out_ref[place // 2, :part, :] = jnp.dot(
                turned_ref[place * part : (place + 1) * part, :],
                low,
                preferred_element_type=jnp.float32,
            ).astype(jnp.bfloat16)

    @pl.when(core == 0)
    def low_half_first():
        halves(mine_ref, other_ref)

    @pl.when(core == 1)
    def high_half_first():
        halves(other_ref, mine_ref)


def forward_step(step, powers_ref, all_ref, own_ref, weights, bias_ref, turned, mixed):
    terms, own_cap, span = powers_ref.shape
    fan_in = own_ref.shape[1]

    @pl.when(step == 0)
    def first():
        turned[:fan_in, :] = own_ref[...].T
        mixed[...] = bias_ref[...] + jnp.dot(
            own_ref[...], weights[0][0], preferred_element_type=jnp.float32
        )

    low = jnp.dot(
        powers_ref[...].reshape(terms * own_cap, span),
        all_ref[...],
        preferred_element_type=jnp.float32,
    ).astype(jnp.bfloat16)
    total = mixed[...]
    for term in range(terms):
        part = low[term * own_cap : (term + 1) * own_cap]
        start = pl.multiple_of((1 + step * terms + term) * fan_in, fan_in)
        turned[pl.ds(start, fan_in), :] = part.T
        total = total + jnp.dot(part, weights[1 + term][0], preferred_element_type=jnp.float32)
    mixed[...] = total


def layer_one_kernel(
    powers_ref,
    all_ref,
    own_ref,
    weight_0,
    weight_a,
    weight_b,
    weight_c,
    bias_ref,
    gain_ref,
    shift_ref,
    valid_ref,
    hidden_ref,
    turned_ref,
    mixed_ref,
):
    step = pl.program_id(0)
    weights = (weight_0, weight_a, weight_b, weight_c)
    forward_step(step, powers_ref, all_ref, own_ref, weights, bias_ref, turned_ref, mixed_ref)

    @pl.when(step == pl.num_programs(0) - 1)
    def finish_layer():
        normed, ignored = norm_forward(mixed_ref[...])
        hidden = (normed * gain_ref[...] + shift_ref[...]) * valid_ref[...]
        hidden_ref[...] = hidden.astype(jnp.bfloat16)


def layer_two_kernel(
    place_ref,
    powers_ref,
    all_ref,
    own_ref,
    weight_0,
    weight_a,
    weight_b,
    weight_c,
    bias_ref,
    gain_ref,
    shift_ref,
    valid_ref,
    upstream_ref,
    active_ref,
    low_ref,
    rest_ref,
    mine_ref,
    other_ref,
    turned,
    mixed,
):
    step = pl.program_id(0)
    weights = (weight_0, weight_a, weight_b, weight_c)
    forward_step(step, powers_ref, all_ref, own_ref, weights, bias_ref, turned, mixed)

    @pl.when(step == pl.num_programs(0) - 1)
    def finish_layer():
        normed, ignored = norm_forward(mixed[...])
        active = (normed * gain_ref[...] + shift_ref[...]) * valid_ref[...]
        active_ref[...] = active.astype(jnp.bfloat16)
        low, rest = norm_backward(
            mixed[...], upstream_ref[...].astype(jnp.float32), gain_ref[...], valid_ref[...]
        )
        low_ref[...] = low
        for place in range(3):
            rest_ref[place : place + 1, :] = rest[place]
        weight_gradient(turned, low, place_ref[1], mine_ref, other_ref)


def backward_step(step, powers_ref, all_ref, own_ref, weights, total):
    terms, own_cap, span = powers_ref.shape
    transposed = (((1,), (1,)), ((), ()))

    @pl.when(step == 0)
    def first():
        total[...] = lax.dot_general(
            own_ref[...], weights[0][0], transposed, preferred_element_type=jnp.float32
        )

    low = jnp.dot(
        powers_ref[...].reshape(terms * own_cap, span),
        all_ref[...],
        preferred_element_type=jnp.float32,
    ).astype(jnp.bfloat16)
    value = total[...]
    for term in range(terms):
        value = value + lax.dot_general(
            low[term * own_cap : (term + 1) * own_cap],
            weights[1 + term][0],
            transposed,
            preferred_element_type=jnp.float32,
        )
    total[...] = value


def back_two_kernel(
    place_ref,
    powers_ref,
    all_ref,
    own_ref,
    weight_0,
    weight_a,
    weight_b,
    weight_c,
    turned_ref,
    mixed_ref,
    gain_ref,
    valid_ref,
    rest_ref,
    low_ref,
    mine_ref,
    other_ref,
    total,
):
    step = pl.program_id(0)
    weights = (weight_0, weight_a, weight_b, weight_c)
    backward_step(step, powers_ref, all_ref, own_ref, weights, total)

    @pl.when(step == pl.num_programs(0) - 1)
    def finish_layer():
        low, rest = norm_backward(mixed_ref[...], total[...], gain_ref[...], valid_ref[...])
        low_ref[...] = low
        weight_gradient(turned_ref, low, place_ref[1], mine_ref, other_ref)
        part = turned_ref.shape[0] // 4
        extra = jnp.zeros((2, mine_ref.shape[1] - part, mine_ref.shape[2]), jnp.bfloat16)
        rows = rest + [rest_ref[place : place + 1, :] for place in range(3)]
        rows = jnp.concatenate(rows + [jnp.zeros((10, rows[0].shape[1]), jnp.float32)], axis=0)

        def below(first_ref, second_ref):
            first_ref[:, part:, :] = extra
            second_ref[:, part:, :] = extra
            first_ref[0, part : part + 16, :] = rows.astype(jnp.bfloat16)

        @pl.when(place_ref[1] == 0)
        def low_half_here():
            below(mine_ref, other_ref)

        @pl.when(place_ref[1] == 1)
        def low_half_there():
            below(other_ref, mine_ref)


def back_one_kernel(
    powers_ref, all_ref, own_ref, weight_0, weight_a, weight_b, weight_c, out_ref, total
):
    step = pl.program_id(0)
    weights = (weight_0, weight_a, weight_b, weight_c)
    backward_step(step, powers_ref, all_ref, own_ref, weights, total)

    @pl.when(step == pl.num_programs(0) - 1)
    def finish_layer():
        out_ref[...] = total[...].astype(jnp.bfloat16)


def layer_pass(
    kernel, name, place, powers, everyone, own, weight, others, outs, scratch, grant=VMEM_BYTES
):
    ignored, own_cap, span = powers.shape
    fan_in, width = weight.shape[1:]

    def whole(value):
        return pl.BlockSpec(value.shape, lambda step: (0,) * len(value.shape))

    def term_weight(term):
        return pl.BlockSpec((1, fan_in, width), lambda step: (1 + step * TERMS + term, 0, 0))

    in_specs = [
        pl.BlockSpec((TERMS, own_cap, span), lambda step: (step, 0, 0)),
        whole(everyone),
        whole(own),
        pl.BlockSpec((1, fan_in, width), lambda step: (0, 0, 0)),
    ]
    in_specs += [term_weight(term) for term in range(TERMS)] + [whole(value) for value in others]
    operands = [powers, everyone, own] + [weight] * (1 + TERMS) + list(others)
    if place is not None:
        in_specs = [pl.BlockSpec(memory_space=pltpu.SMEM)] + in_specs
        operands = [place] + operands
    return pl.pallas_call(
        kernel,
        grid=((ORDER - 1) // TERMS,),
        out_shape=outs,
        in_specs=in_specs,
        out_specs=[whole(value) for value in outs],
        scratch_shapes=[pltpu.VMEM(shape, dtype) for shape, dtype in scratch],
        compiler_params=pltpu.CompilerParams(vmem_limit_bytes=grant),
        cost_estimate=NO_COST,
        name=name,
    )(*operands)


def finish_kernel(scalars_ref, *refs):
    step = pl.program_id(0)
    if len(refs) == 3:
        values_ref, other_ref, out_ref = refs
        parts = [(step >= 0, values_ref)]
        small_ref = None
    else:
        pair_ref, siblings_ref, other_ref, out_ref, small_ref = refs
        parts = [(step < 2, pair_ref), (step >= 2, siblings_ref)]
    part = out_ref.shape[1]
    for here, values_ref in parts:
        @pl.when(here & (scalars_ref[0] == 1))
        def fast_form():
            out_ref[0] = values_ref[0, :part, :].astype(jnp.float32)

        if small_ref is not None:
            @pl.when(here & (scalars_ref[1 + step] == 0))
            def small_sums():
                small_ref[...] = values_ref[0, part : part + 16, :].astype(jnp.float32)

    @pl.when(scalars_ref[0] == 0)
    def general_form():
        out_ref[0] = other_ref[0].astype(jnp.float32)


def finished(scalars, pair, values, other):
    count, part, width = other.shape
    one = (1, part, width)
    if pair is None:
        operands, outs = [values, other], [jax.ShapeDtypeStruct(other.shape, jnp.float32)]

        def quarter(step, scalars_ref):
            return step

        in_specs = [pl.BlockSpec((1,) + values.shape[1:], lambda step, ref: (step, 0, 0))]
        small_specs = []
    else:
        operands = [pair, values, other]
        outs = [
            jax.ShapeDtypeStruct(other.shape, jnp.float32),
            jax.ShapeDtypeStruct((16, width), jnp.float32),
        ]

        def quarter(step, scalars_ref):
            return scalars_ref[1 + step]

        in_specs = [
            pl.BlockSpec((1,) + pair.shape[1:], lambda step, ref: (jnp.minimum(step, 1), 0, 0)),
            pl.BlockSpec((1,) + pair.shape[1:], lambda step, ref: (jnp.maximum(step - 2, 0), 0, 0)),
        ]
        small_specs = [pl.BlockSpec((16, width), lambda step, ref: (0, 0))]
    in_specs.append(
        pl.BlockSpec(one, lambda step, ref: ((1 - ref[0]) * quarter(step, ref), 0, 0))
    )
    result = pl.pallas_call(
        finish_kernel,
        grid_spec=pltpu.PrefetchScalarGridSpec(
            num_scalar_prefetch=1,
            grid=(count,),
            in_specs=in_specs,
            out_specs=[pl.BlockSpec(one, lambda step, ref: (quarter(step, ref), 0, 0))]
            + small_specs,
        ),
        out_shape=outs,
        compiler_params=pltpu.CompilerParams(vmem_limit_bytes=ALL_VMEM_BYTES),
        cost_estimate=NO_COST,
        name="finished",
    )(scalars, *operands)
    return result[0] if pair is None else result


def unpack_kernel(place_ref, pieces_ref, keys_ref, own_ref, quadrant_ref, columns, hot):
    groups, high, lanes = pieces_ref.shape
    own_cap, span = own_ref.shape
    whole = own_cap // lanes
    send_cap = keys_ref.shape[1] // groups
    half, rest = send_cap // 2, own_cap - whole * lanes
    for group in range(groups):
        start = group * send_cap
        for tile in range(whole):
            columns[start : start + send_cap, tile * lanes : (tile + 1) * lanes] = pieces_ref[
                group, tile * send_cap : (tile + 1) * send_cap, :
            ]
        ends = pieces_ref[group, whole * send_cap :, :]
        columns[start : start + half, whole * lanes :] = ends[:, :rest]
        columns[start + half : start + send_cap, whole * lanes :] = ends[:, rest:]
    standing = lax.broadcasted_iota(jnp.int32, hot.shape, 0)
    hot[...] = jnp.where(standing == keys_ref[...], 1.0, 0.0).astype(jnp.bfloat16)
    block = jnp.dot(hot[...], columns[...], preferred_element_type=jnp.float32)
    own_ref[...] = block.T.astype(jnp.bfloat16)
    middle = span // 2

    @pl.when(place_ref[0] == 0)
    def first():
        quadrant_ref[...] = own_ref[:, :middle]

    @pl.when(place_ref[0] == 1)
    def second():
        quadrant_ref[...] = own_ref[:, middle:]


def unpacked_block(pieces, keys, place, own_cap, span):
    vector = pl.BlockSpec(memory_space=pltpu.VMEM)
    return pl.pallas_call(
        unpack_kernel,
        out_shape=[
            jax.ShapeDtypeStruct((own_cap, span), jnp.bfloat16),
            jax.ShapeDtypeStruct((own_cap, span // 2), jnp.bfloat16),
        ],
        in_specs=[pl.BlockSpec(memory_space=pltpu.SMEM), vector, vector],
        out_specs=[vector, vector],
        scratch_shapes=[
            pltpu.VMEM((keys.shape[1], own_cap), jnp.bfloat16),
            pltpu.VMEM((span, keys.shape[1]), jnp.bfloat16),
        ],
        compiler_params=pltpu.CompilerParams(vmem_limit_bytes=VMEM_BYTES),
        cost_estimate=NO_COST,
        name="unpacked_block",
    )(place, pieces, keys)


def exclusive_counts(member):
    count = member.shape[-1]
    before = jnp.arange(count)[:, None] < jnp.arange(count)[None, :]
    return jnp.dot(
        member.astype(jnp.bfloat16),
        before.astype(jnp.bfloat16),
        preferred_element_type=jnp.float32,
    ).astype(jnp.int32)


def assign(codes, n_row):
    cluster, valid = codes >> 1, codes & 1
    labels = jnp.arange(CLUSTERS)
    sizes = jnp.sum(
        (cluster.reshape(1, -1) == labels[:, None]) & (valid.reshape(1, -1) == 1), axis=1
    )
    ahead = (sizes[None, :] > sizes[:, None]) | (
        (sizes[None, :] == sizes[:, None]) & (labels[None, :] < labels[:, None])
    )
    rank = jnp.sum(ahead, axis=1)
    others = n_row - 1
    turn, place = (rank - 1) // others, (rank - 1) % others
    group = jnp.where(rank == 0, 0, 1 + jnp.where(turn == 0, place, others - 1 - place))
    of_node = jnp.sum(
        jnp.where(cluster[None] == labels[:, None, None, None], group[:, None, None, None], 0),
        axis=0,
    )
    return jnp.where(valid == 1, of_node, n_row)


def compact(
    codes,
    group,
    features,
    block_keep,
    edge_weight,
    weight_one,
    bias_one,
    gain_one,
    shift_one,
    weight_two,
    bias_two,
    gain_two,
    shift_two,
    cotangent,
    places_of,
    slots_of,
    seats_of,
    decide,
    sizes,
    caps,
):
    row, col = lax.axis_index("row"), lax.axis_index(COL)
    chip, core = lax.axis_index("chip"), lax.axis_index("core")
    n_row, n_col = sizes
    own_cap, send_cap, seat_cap = caps
    own_nodes, in_width = features.shape
    width = weight_two.shape[2]
    span = n_col * own_cap
    targets = jnp.arange(n_row)

    def in_col(value):
        return lax.dynamic_index_in_dim(value, col, 1, False).reshape(-1)

    def in_row(value):
        return lax.dynamic_index_in_dim(value, row, 0, False).reshape(-1)

    row_group, col_group = in_row(group), in_col(group)
    row_slots, col_places = in_row(slots_of(group)), in_col(places_of(group))
    row_keys = jnp.where(row_slots < send_cap, row_group * send_cap + row_slots, -1)
    col_keys = jnp.where(col_places < own_cap, col_group * own_cap + col_places, -1)
    pieces = packed_pieces(
        block_keep,
        in_row(codes),
        in_col(codes),
        row_keys,
        col_keys,
        edge_weight,
        (own_cap, send_cap),
        n_row,
    )
    pieces, codes = lax.optimization_barrier((pieces, codes))
    group = assign(codes, n_row)
    pieces = trade(pieces, "row")
    places, slots, seats = places_of(group), slots_of(group), seats_of(group)

    standing = jnp.arange(n_col)[None, :, None] * own_cap + places
    fits_here = jnp.where(group == row, standing, -1).reshape(n_row, -1)
    slot_of = slots.reshape(n_row, -1)
    target = jnp.max(
        jnp.where(
            slot_of[:, None, :] == jnp.arange(send_cap)[None, :, None], fits_here[:, None, :], -1
        ),
        axis=2,
    )
    keys = target.reshape(1, -1)

    def on_device(value):
        return lax.dynamic_index_in_dim(in_row(value).reshape(n_col, -1), col, 0, False)

    def seat_of_node(groups, group, seats):
        hot = (on_device(group)[None, None, :] == groups[:, None, None]) & (
            on_device(seats)[None, None, :] == jnp.arange(seat_cap)[None, :, None]
        )
        return hot.astype(jnp.bfloat16).reshape(n_row * seat_cap, own_nodes)

    group_col, places_col, seats_col = (
        lax.dynamic_index_in_dim(value, col, 1, False) for value in (group, places, seats)
    )
    seated = (group_col == row)[:, None, :] & (
        seats_col[:, None, :] == jnp.arange(seat_cap)[None, :, None]
    )
    place_of_seat = jnp.max(jnp.where(seated, places_col[:, None, :], -1), axis=2)
    leave_group = place_of_seat.reshape(-1, 1) == jnp.arange(own_cap)
    leave_group = leave_group.astype(jnp.bfloat16)

    partners = row ^ targets
    both = jnp.concatenate([features, cotangent], axis=1)
    both = jnp.dot(seat_of_node(partners, group, seats), both)
    both = both.reshape(n_row, seat_cap, -1)
    from_partner = jnp.max(
        jnp.where((partners[:, None] == targets)[:, :, None], place_of_seat[None], -1), axis=1
    )
    arrive = from_partner.reshape(1, -1) == jnp.arange(own_cap)[:, None]
    arrive = arrive.astype(jnp.bfloat16)
    held_count = jnp.sum(group_col == row)
    valid_rows = (jnp.arange(own_cap) < held_count).astype(jnp.float32)[:, None]
    place = jnp.stack([chip, core]).astype(jnp.int32)
    scalars = (chip, 1 - chip, col * own_cap)
    scalars = tuple(value.astype(jnp.uint32) for value in scalars) + (chip == 0, core == 0, place)
    pieces, both, keys, arrive, leave_group, valid_rows, scalars = lax.optimization_barrier(
        (pieces, both, keys, arrive, leave_group, valid_rows, scalars)
    )
    this_chip, other_chip, own_start, first_chip, first_core, place = scalars

    own_block, quadrant = unpacked_block(pieces, keys, place, own_cap, span)
    quadrant = swap(quadrant, "chip")
    both = [both[0]] + [
        lax.ppermute(both[step], "row", [(place, place ^ step) for place in range(n_row)])
        for step in range(1, n_row)
    ]
    sibling = swap(own_block, "core")
    quadrant, *both = lax.optimization_barrier((quadrant, *both))
    adjacency = normalized_block(own_block, sibling, quadrant, swap(quadrant, "core"), place)
    mine = jnp.dot(arrive, jnp.concatenate(both))
    features_own, cotangent_own = mine[:, :in_width], mine[:, in_width:]
    sibling = swap(features_own, "core")

    first = (own_start + jnp.arange(own_cap, dtype=jnp.uint32))[:, None]
    first = first == jnp.arange(span, dtype=jnp.uint32)[None, :]
    previous = first.astype(jnp.float32)
    current = -lax.dynamic_slice_in_dim(adjacency, own_start, own_cap, 0).astype(jnp.float32)
    lowered = [current.astype(jnp.bfloat16)]
    for position in range(2, ORDER):
        upcoming = (
            -2.0 * jnp.dot(lowered[-1], adjacency, preferred_element_type=jnp.float32) - previous
        )
        low = upcoming.astype(jnp.bfloat16)
        if position == 4:
            low, sibling = lax.optimization_barrier((low, sibling))
            features_chip = joined(features_own, sibling, first_core)
            partner = swap(features_chip, "chip")
        if position == 8:
            low, partner = lax.optimization_barrier((low, partner))
            features_all = joined(features_chip, partner, first_chip)
        previous, current = current, upcoming
        lowered.append(low)
    powers = jnp.concatenate(lowered, axis=0).reshape(ORDER - 1, own_cap, span)

    def everywhere(value_low):
        return lax.all_gather(value_low, COL, axis=0, tiled=True)

    def shaped(*shape, dtype=jnp.bfloat16):
        return jax.ShapeDtypeStruct(shape, dtype)

    part_one, part_two = ORDER * in_width // n_col, ORDER * width // n_col
    padded = -(-(part_one + 16) // (8 * n_row)) * (8 * n_row)
    hidden, turned_one, mixed_one = layer_pass(
        layer_one_kernel,
        "layer_one",
        None,
        powers,
        features_all,
        features_own,
        weight_one,
        [bias_one[None], gain_one[None], shift_one[None], valid_rows],
        [
            shaped(own_cap, width),
            shaped(n_col * part_one, own_cap),
            shaped(own_cap, width, dtype=jnp.float32),
        ],
        [],
    )
    activations, low_two, rest_two, mine, other = layer_pass(
        layer_two_kernel,
        "layer_two",
        place,
        powers,
        everywhere(hidden),
        hidden,
        weight_two,
        [bias_two[None], gain_two[None], shift_two[None], valid_rows, cotangent_own],
        [
            shaped(own_cap, width),
            shaped(own_cap, width),
            shaped(3, width, dtype=jnp.float32),
            shaped(2, part_two, width),
            shaped(2, part_two, width),
        ],
        [((n_col * part_two, own_cap), jnp.bfloat16), ((own_cap, width), jnp.float32)],
    )

    def add_cores(mine, other):
        got = swap(other, "core")
        return tuple(
            added(
                lax.dynamic_index_in_dim(mine, index, 0, False),
                lax.dynamic_index_in_dim(got, index, 0, False),
            )
            for index in (this_chip, other_chip)
        )

    leaving = jnp.dot(leave_group, activations).reshape(n_row, seat_cap, width)
    here, there = add_cores(mine, other)
    everyone_two, there, leaving = lax.optimization_barrier(
        (everywhere(low_two), there, leaving)
    )
    there = swap(there, "chip")
    back = trade(leaving, "row")
    low_one, mine, other = layer_pass(
        back_two_kernel,
        "back_two",
        place,
        powers,
        everyone_two,
        low_two,
        weight_two,
        [turned_one, mixed_one, gain_one[None], valid_rows, rest_two],
        [shaped(own_cap, width), shaped(2, padded, width), shaped(2, padded, width)],
        [((own_cap, width), jnp.float32)],
        ALL_VMEM_BYTES,
    )
    low_one, there, back, codes = lax.optimization_barrier((low_one, there, back, codes))
    second = added(here, there).reshape(n_row, -1, width)
    low_one, second = lax.optimization_barrier((low_one, second))
    second = trade(second, "row")
    here, there = add_cores(mine, other)
    low_one, there = lax.optimization_barrier((low_one, there))
    everyone_one = everywhere(low_one)
    there = swap(there, "chip")
    everyone_one, second, there = lax.optimization_barrier((everyone_one, second, there))
    first = added(here, there).reshape(n_row, -1, width)
    share = first.shape[1]
    second = jnp.sum(second.astype(jnp.float32), axis=0).astype(jnp.bfloat16)
    second = jnp.broadcast_to(second[None], (n_row,) + second.shape)
    mixed = jnp.concatenate([first, second], axis=1)
    everyone_one, mixed = lax.optimization_barrier((everyone_one, mixed))
    mixed = trade(mixed, "row")
    (input_grad,) = layer_pass(
        back_one_kernel,
        "back_one",
        None,
        powers,
        everyone_one,
        low_one,
        weight_one,
        [],
        [shaped(own_cap, in_width)],
        [((own_cap, in_width), jnp.float32)],
        ALL_VMEM_BYTES,
    )
    leaving = jnp.dot(leave_group, input_grad).reshape(n_row, seat_cap * in_width // width, width)
    group = assign(codes, n_row)
    fits, others = decide(group)
    enter_home = seat_of_node(targets, group, seats_of(group)).T
    quarters = jnp.stack(
        [fits.astype(jnp.int32), col, (1 - chip) * 2 + core, chip * 2 + 1 - core, 3 - col]
    )

    def chosen(value, other):
        return jnp.where(fits, value.astype(jnp.float32), other.astype(jnp.float32))

    home = jnp.dot(enter_home, back.reshape(-1, width), preferred_element_type=jnp.float32)
    home = chosen(home, others[0])
    mixed, leaving, home, enter_home, quarters, others = lax.optimization_barrier(
        (mixed, leaving, home, enter_home, quarters, others)
    )
    first = jnp.sum(mixed[:, :share].astype(jnp.float32), axis=0).astype(jnp.bfloat16)
    first = jnp.broadcast_to(first[None], (n_row,) + first.shape)
    first, mixed = lax.optimization_barrier((jnp.concatenate([first, leaving], axis=1), mixed))
    first = trade(first, "row")
    second = lax.all_gather(mixed[:, share:].reshape(-1, width), COL, axis=0)
    back = first[:, share:].reshape(n_row * seat_cap, in_width)
    mine = first[:, :share].reshape(1, -1, width)
    partner = swap(mine, "chip")
    second = finished(quarters[:1], None, second, others[3])
    home_grad = jnp.dot(enter_home, back, preferred_element_type=jnp.float32)
    pair = jnp.concatenate([mine, partner])
    siblings = swap(pair, "core")
    first, small = finished(quarters, pair, siblings, others[2])
    return (
        home,
        chosen(home_grad, others[1]),
        first,
        second,
        chosen(small[:6], others[4]),
    )


def general(
    codes,
    features,
    block_keep,
    edge_weight,
    weight_one,
    bias_one,
    gain_one,
    shift_one,
    weight_two,
    bias_two,
    gain_two,
    shift_two,
    cotangent,
    node_valid,
):
    row, col = lax.axis_index("row"), lax.axis_index(COL)
    row_codes = lax.dynamic_index_in_dim(codes, row, 0, False).reshape(-1)
    col_codes = lax.dynamic_index_in_dim(codes, col, 1, False).reshape(-1)
    tile_rows, tile_cols = edge_weight.shape
    blocks_down, blocks_across = block_keep.shape
    block_side = tile_rows // blocks_down
    linked = (row_codes[:, None] == col_codes[None, :]) & (row_codes[:, None] & 1 == 1)
    linked = linked.reshape(blocks_down, block_side, blocks_across, block_side) & (
        block_keep[:, None, :, None] == 1
    )
    masked = edge_weight * linked.reshape(tile_rows, tile_cols).astype(jnp.bfloat16)
    degree_rows = 1.0 + lax.psum(jnp.sum(masked, axis=1, dtype=jnp.float32), COL)
    own_nodes = features.shape[0]
    own_degree = lax.dynamic_slice_in_dim(
        degree_rows, lax.axis_index(COL) * own_nodes, own_nodes, 0
    )
    degree_cols = lax.all_gather(own_degree, "row", axis=0, tiled=True)
    adjacency = (
        masked.astype(jnp.float32)
        * lax.rsqrt(degree_rows)[:, None]
        * lax.rsqrt(degree_cols)[None, :]
    ).astype(jnp.bfloat16)
    valid_rows = node_valid.astype(jnp.float32)
    stacked_one, mixed_one, hidden = layer_forward(
        adjacency,
        features.astype(jnp.float32),
        weight_one,
        bias_one,
        gain_one,
        shift_one,
        valid_rows,
    )
    stacked_two, mixed_two, activations = layer_forward(
        adjacency, hidden, weight_two, bias_two, gain_two, shift_two, valid_rows
    )
    hidden_grad, weight_two_grad, bias_two_grad, gain_two_grad, shift_two_grad = layer_backward(
        adjacency,
        stacked_two,
        mixed_two,
        cotangent.astype(jnp.float32),
        weight_two,
        gain_two,
        shift_two,
        valid_rows,
    )
    input_grad, weight_one_grad, bias_one_grad, gain_one_grad, shift_one_grad = layer_backward(
        adjacency, stacked_one, mixed_one, hidden_grad, weight_one, gain_one, shift_one, valid_rows
    )
    summed = lax.psum(
        (
            weight_one_grad,
            bias_one_grad,
            gain_one_grad,
            shift_one_grad,
            weight_two_grad,
            bias_two_grad,
            gain_two_grad,
            shift_two_grad,
        ),
        ("row",) + COL,
    )
    weight_one_grad, bias_one_grad, gain_one_grad, shift_one_grad = (
        summed[0],
        summed[1],
        summed[2],
        summed[3],
    )
    weight_two_grad, bias_two_grad, gain_two_grad, shift_two_grad = (
        summed[4],
        summed[5],
        summed[6],
        summed[7],
    )
    return (
        activations,
        input_grad,
        weight_one_grad,
        bias_one_grad,
        gain_one_grad,
        shift_one_grad,
        weight_two_grad,
        bias_two_grad,
        gain_two_grad,
        shift_two_grad,
    )


def local(n_row, n_col, *args):
    (
        features,
        node_valid,
        cluster,
        block_keep,
        edge_weight,
        weight_one,
        bias_one,
        gain_one,
        shift_one,
        weight_two,
        bias_two,
        gain_two,
        shift_two,
        cotangent,
    ) = args
    own_nodes, in_width = features.shape
    own_cap = own_nodes * n_row * 5 // 16
    send_cap = own_nodes * n_col * 11 // 32
    seat_cap = own_nodes // 2
    codes = broadcast_along(cluster * 2 + node_valid, ("row",) + COL, n_row * n_col)
    codes = codes.reshape(n_row, n_col, own_nodes)
    shared = (
        block_keep,
        edge_weight,
        weight_one,
        bias_one,
        gain_one,
        shift_one,
        weight_two,
        bias_two,
        gain_two,
        shift_two,
        cotangent,
    )

    def slow():
        return general(codes, features, *shared, node_valid)

    held = (ORDER - 1) * own_cap * own_cap * n_col * 2
    if held > HELD_BYTES or n_col != 4 or n_row < 2 or n_row & (n_row - 1):
        return slow()
    group = assign(codes, n_row)

    def member_of(group):
        return group[None] == jnp.arange(n_row)[:, None, None, None]

    def places_of(group):
        member = member_of(group).transpose(0, 2, 1, 3).reshape(n_row, n_col, -1)
        places = jnp.sum(jnp.where(member, exclusive_counts(member), 0), axis=0)
        return places.reshape(n_col, n_row, own_nodes).transpose(1, 0, 2)

    def slots_of(group):
        member = member_of(group).reshape(n_row, n_row, -1)
        slots = jnp.sum(jnp.where(member, exclusive_counts(member), 0), axis=0)
        return slots.reshape(n_row, n_col, own_nodes)

    def seats_of(group):
        member = member_of(group)
        return jnp.sum(jnp.where(member, exclusive_counts(member), 0), axis=0)

    width = weight_two.shape[2]

    def instead(state):
        made = slow()
        small = jnp.stack([made[place] for place in (3, 4, 5, 7, 8, 9)])
        return (True,) + tuple(
            value.astype(jnp.bfloat16).reshape(like.shape)
            for value, like in zip((made[0], made[1], made[2], made[6], small), state[1:])
        )

    start = (
        cotangent,
        features,
        weight_one.reshape(n_col, -1, width),
        weight_two.reshape(n_col, -1, width),
        jnp.zeros((6, width), jnp.bfloat16),
    )

    def decide(group):
        member = member_of(group)
        fits = (
            (jnp.max(jnp.sum(member, axis=(1, 3))) <= own_cap)
            & (jnp.max(jnp.sum(member, axis=(2, 3))) <= send_cap)
            & (jnp.max(jnp.sum(member, axis=3)) <= seat_cap)
        )
        others = lax.while_loop(
            lambda state: jnp.logical_not(state[0]),
            instead,
            (fits,) + start,
        )[1:]
        return fits, others

    home, home_grad, first, second, small = compact(
        codes,
        group,
        features,
        *shared,
        places_of,
        slots_of,
        seats_of,
        decide,
        (n_row, n_col),
        (own_cap, send_cap, seat_cap),
    )
    return (
        home,
        home_grad,
        first.reshape(weight_one.shape),
        small[0],
        small[1],
        small[2],
        second.reshape(weight_two.shape),
        small[3],
        small[4],
        small[5],
    )


def solution(mesh):
    n_row, n_col = mesh.shape["row"], mesh.shape["col"]
    by_core = jax.sharding.Mesh(
        mesh.devices.reshape(n_row, n_col // 2, 2), ("row", "chip", "core")
    )
    nodes = ("row", "chip", "core")
    placed = (
        P(nodes, None),
        P(nodes),
        P(nodes),
        P("row", COL),
        P("row", COL),
        P(),
        P(),
        P(),
        P(),
        P(),
        P(),
        P(),
        P(),
        P(nodes, None),
    )
    return jax.shard_map(
        functools.partial(local, n_row, n_col),
        mesh=by_core,
        in_specs=placed,
        out_specs=(P(nodes, None), P(nodes, None), P(), P(), P(), P(), P(), P(), P(), P()),
        check_vma=False,
    )
```

```python
import functools
import math

import jax
import jax.numpy as jnp
from jax import lax
from jax.experimental import pallas as pl
from jax.experimental.pallas import tpu as pltpu
from jax.sharding import PartitionSpec as P

ORDER = 13
CLUSTERS = 16
HELD_BYTES = 1 << 25
VMEM_BYTES = 32 << 20
TERMS = 3
NO_COST = pl.CostEstimate(flops=1, bytes_accessed=1, transcendentals=0)
COL = ("chip", "core")


def finish(mixed, gain, shift, valid_rows):
    active = jax.nn.gelu(mixed, approximate=False)
    centered = active - jnp.mean(active, axis=-1, keepdims=True)
    variance = jnp.mean(centered * centered, axis=-1, keepdims=True)
    return (centered * lax.rsqrt(variance + 1e-05) * gain + shift) * valid_rows[:, None]


def forward_product(adjacency, piece_low):
    partial_value = jnp.dot(
        adjacency,
        lax.all_gather(piece_low, "row", axis=0, tiled=True),
        preferred_element_type=jnp.float32,
    )
    return lax.psum_scatter(partial_value, COL, scatter_dimension=0, tiled=True)


def backward_product(adjacency, piece_low):
    partial_value = lax.dot_general(
        adjacency,
        lax.all_gather(piece_low, COL, axis=0, tiled=True),
        (((0,), (0,)), ((), ())),
        preferred_element_type=jnp.float32,
    )
    return lax.psum_scatter(
        partial_value.astype(jnp.bfloat16), "row", scatter_dimension=0, tiled=True
    ).astype(jnp.float32)


def layer_forward(adjacency, inputs, weight, bias, gain, shift, valid_rows):
    first_low = inputs.astype(jnp.bfloat16)
    second = -forward_product(adjacency, first_low)
    second_low = second.astype(jnp.bfloat16)

    def advance(state_pair, unused):
        previous, current, current_low = state_pair
        upcoming = -2.0 * forward_product(adjacency, current_low) - previous
        upcoming_low = upcoming.astype(jnp.bfloat16)
        return ((current, upcoming, upcoming_low), upcoming_low)

    ignored, others = lax.scan(advance, (inputs, second, second_low), None, length=ORDER - 2)
    stacked = jnp.concatenate([first_low[None], second_low[None], others], axis=0)
    mixed = jnp.einsum("kni,kio->no", stacked, weight, preferred_element_type=jnp.float32) + bias
    return (stacked, mixed, finish(mixed, gain, shift, valid_rows))


def layer_backward(adjacency, stacked, mixed, upstream, weight, gain, shift, valid_rows):

    def local_finish(mixed_in, gain_in, shift_in):
        return finish(mixed_in, gain_in, shift_in, valid_rows)

    ignored, pullback = jax.vjp(local_finish, mixed, gain, shift)
    mixed_grad, gain_grad, shift_grad = pullback(upstream)
    mixed_low = mixed_grad.astype(jnp.bfloat16)
    bias_grad = jnp.sum(mixed_low.astype(jnp.float32), axis=0)
    weight_grad = jnp.einsum("kni,no->kio", stacked, mixed_low, preferred_element_type=jnp.float32)
    direct = jnp.einsum("no,kio->kni", mixed_low, weight, preferred_element_type=jnp.float32)

    def retreat(state_pair, direct_term):
        later_two, later_one = state_pair
        current = (
            direct_term
            - 2.0 * backward_product(adjacency, later_one.astype(jnp.bfloat16))
            - later_two
        )
        return ((later_one, current), None)

    start_pair = (jnp.zeros_like(direct[0]), direct[ORDER - 1])
    (second_grad, first_grad), unused = lax.scan(
        retreat, start_pair, direct[1 : ORDER - 1], reverse=True
    )
    input_grad = (
        direct[0] - backward_product(adjacency, first_grad.astype(jnp.bfloat16)) - second_grad
    )
    return (input_grad, weight_grad, bias_grad, gain_grad, shift_grad)


def swap(value, axis):
    return lax.ppermute(value, axis, [(0, 1), (1, 0)])


def trade(pieces, axis):
    return lax.all_to_all(pieces, axis, 0, 0, tiled=False)


def broadcast_along(value, axis, size):
    return trade(jnp.broadcast_to(value[None], (size,) + value.shape), axis)


def joined(mine, other, mine_first):
    return jnp.where(
        mine_first, jnp.concatenate([mine, other]), jnp.concatenate([other, mine])
    )


def added(mine, received):
    return (mine.astype(jnp.float32) + received.astype(jnp.float32)).astype(jnp.bfloat16)


def assemble(place_ref, own_ref, sibling_ref, near_ref, far_ref, out_ref, done):
    chip, core = place_ref[0], place_ref[1]
    own_cap, span = own_ref.shape
    half = span // 2

    def rows(of_chip, of_core):
        return pl.ds(pl.multiple_of((2 * of_chip + of_core) * own_cap, own_cap), own_cap)

    def fetch(source, of_chip, of_core, columns, place):
        target = out_ref.at[rows(of_chip, of_core), columns]
        return pltpu.make_async_copy(source, target, done.at[place])

    def quadrant_copies(here):
        there = 1 - here
        columns = pl.ds(there * half, half)
        return (
            fetch(near_ref, there, core, columns, 2),
            fetch(far_ref, there, 1 - core, columns, 3),
        )

    everything = pl.ds(0, span)
    top = (
        fetch(own_ref, chip, core, everything, 0),
        fetch(sibling_ref, chip, 1 - core, everything, 1),
    )

    def of_chip(here):
        there = 1 - here
        copies = top + quadrant_copies(here)
        for copy in copies:
            copy.start()
        for copy in copies:
            copy.wait()
        here_rows = pl.ds(here * half, half)
        for tile in range(half // 128):
            columns = pl.ds(there * half + tile * 128, 128)
            strip = out_ref[here_rows, columns]
            turned = jnp.transpose(strip.astype(jnp.float32)).astype(jnp.bfloat16)
            out_ref[columns, here_rows] = turned

    @pl.when(chip == 0)
    def first():
        of_chip(0)

    @pl.when(chip == 1)
    def second():
        of_chip(1)

    across = jnp.ones((1, span), jnp.float32)
    for tile in range(span // 128):
        across = across + jnp.sum(
            out_ref[pl.ds(tile * 128, 128), :].astype(jnp.float32), axis=0, keepdims=True
        )
    across = lax.rsqrt(across)
    for tile in range(span // 128):
        strip = out_ref[pl.ds(tile * 128, 128), :].astype(jnp.float32)
        down = lax.rsqrt(1.0 + jnp.sum(strip, axis=1, keepdims=True))
        out_ref[pl.ds(tile * 128, 128), :] = (strip * down * across).astype(jnp.bfloat16)


def normalized_block(own, sibling, near, far, place):
    span = own.shape[1]
    return pl.pallas_call(
        assemble,
        out_shape=jax.ShapeDtypeStruct((span, span), jnp.bfloat16),
        in_specs=[pl.BlockSpec(memory_space=pltpu.SMEM)]
        + [pl.BlockSpec(memory_space=pltpu.HBM)] * 4,
        out_specs=pl.BlockSpec(memory_space=pltpu.VMEM),
        scratch_shapes=[pltpu.SemaphoreType.DMA((4,))],
        compiler_params=pltpu.CompilerParams(vmem_limit_bytes=VMEM_BYTES),
        cost_estimate=NO_COST,
        name="normalized_block",
    )(place, own, sibling, near, far)


def pack_kernel(
    keep_ref, row_codes_ref, col_codes_ref, row_keys_ref, col_keys_ref, weight_ref, out_ref,
    masked, picked, rows_hot, cols_hot
):
    tile_rows, tile_cols = weight_ref.shape
    blocks_down, blocks_across = keep_ref.shape
    groups, ignored, lanes = out_ref.shape
    send_cap, own_cap = rows_hot.shape[0] // groups, cols_hot.shape[0] // groups
    high, wide = tile_rows // blocks_down, tile_cols // blocks_across
    for down in range(blocks_down):
        for across in range(blocks_across):
            rows, columns = pl.ds(down * high, high), pl.ds(across * wide, wide)
            own, other = row_codes_ref[rows, :], col_codes_ref[:, columns]
            linked = (own == other) & (own % 2 == 1) & (keep_ref[down, across] == 1)
            weight = weight_ref[rows, columns].astype(jnp.float32)
            masked[rows, columns] = jnp.where(linked, weight, 0.0).astype(jnp.bfloat16)

    def one_hot(keys, start, count):
        standing = lax.broadcasted_iota(jnp.int32, (count, keys.shape[1]), 0) + start
        return jnp.where(standing == keys, 1.0, 0.0).astype(jnp.bfloat16)

    for group in range(groups):
        rows_hot[pl.ds(group * send_cap, send_cap), :] = one_hot(
            row_keys_ref[...], group * send_cap, send_cap
        )
        cols_hot[pl.ds(group * own_cap, own_cap), :] = one_hot(
            col_keys_ref[...], group * own_cap, own_cap
        )
    for tile in range(tile_cols // 256):
        columns = pl.ds(tile * 256, 256)
        picked[:, columns] = jnp.dot(
            rows_hot[...], masked[:, columns], preferred_element_type=jnp.float32
        ).astype(jnp.bfloat16)
    whole, half = own_cap // lanes, send_cap // 2
    for group in range(groups):
        packed = lax.dot_general(
            picked[pl.ds(group * send_cap, send_cap), :],
            cols_hot[pl.ds(group * own_cap, own_cap), :],
            (((1,), (1,)), ((), ())),
            preferred_element_type=jnp.float32,
        )
        for tile in range(whole):
            out_ref[group, pl.ds(tile * send_cap, send_cap), :] = packed[
                :, tile * lanes : (tile + 1) * lanes
            ].astype(jnp.bfloat16)
        ends = jnp.concatenate(
            [packed[:half, whole * lanes :], packed[half:, whole * lanes :]], axis=1
        )
        out_ref[group, pl.ds(whole * send_cap, half), :] = ends.astype(jnp.bfloat16)


def packed_pieces(block_keep, row_codes, col_codes, row_keys, col_keys, edge_weight, caps, groups):
    own_cap, send_cap = caps
    tile_rows, tile_cols = edge_weight.shape
    high = own_cap // 128 * send_cap + send_cap // 2
    vector = pl.BlockSpec(memory_space=pltpu.VMEM)
    return pl.pallas_call(
        pack_kernel,
        out_shape=jax.ShapeDtypeStruct((groups, high, 128), jnp.bfloat16),
        in_specs=[pl.BlockSpec(memory_space=pltpu.SMEM)] + [vector] * 5,
        out_specs=vector,
        scratch_shapes=[
            pltpu.VMEM((tile_rows, tile_cols), jnp.bfloat16),
            pltpu.VMEM((groups * send_cap, tile_cols), jnp.bfloat16),
            pltpu.VMEM((groups * send_cap, tile_rows), jnp.bfloat16),
            pltpu.VMEM((groups * own_cap, tile_cols), jnp.bfloat16),
        ],
        compiler_params=pltpu.CompilerParams(vmem_limit_bytes=VMEM_BYTES),
        cost_estimate=NO_COST,
        name="packed_pieces",
    )(block_keep, row_codes[:, None], col_codes[None], row_keys[None], col_keys[None], edge_weight)


def normal_share(mixed):
    return 0.5 * (1.0 + lax.erf(mixed * 0.5**0.5))


def norm_forward(mixed):
    active = mixed * normal_share(mixed)
    centered = active - jnp.mean(active, axis=-1, keepdims=True)
    scale = lax.rsqrt(jnp.mean(centered * centered, axis=-1, keepdims=True) + 1e-05)
    return centered * scale, scale


def norm_backward(mixed, upstream, gain, valid):
    normed, scale = norm_forward(mixed)
    upstream = upstream * valid
    inner = upstream * gain
    inner = inner - jnp.mean(inner, axis=-1, keepdims=True) - normed * jnp.mean(
        inner * normed, axis=-1, keepdims=True
    )
    density = jnp.exp(-0.5 * mixed * mixed) * (1.0 / (2.0 * math.pi) ** 0.5)
    low = (inner * scale * (normal_share(mixed) + mixed * density)).astype(jnp.bfloat16)
    rest = [low.astype(jnp.float32), upstream * normed, upstream]
    return low, [jnp.sum(value, axis=0, keepdims=True) for value in rest]


def weight_gradient(turned_ref, low, core, mine_ref, other_ref):
    part = turned_ref.shape[0] // 4

    def halves(first_ref, second_ref):
        for place in range(4):
            out_ref = second_ref if place % 2 else first_ref
            out_ref[place // 2, :part, :] = jnp.dot(
                turned_ref[place * part : (place + 1) * part, :],
                low,
                preferred_element_type=jnp.float32,
            ).astype(jnp.bfloat16)

    @pl.when(core == 0)
    def low_half_first():
        halves(mine_ref, other_ref)

    @pl.when(core == 1)
    def high_half_first():
        halves(other_ref, mine_ref)


def forward_step(step, powers_ref, all_ref, own_ref, weights, bias_ref, turned, mixed):
    terms, own_cap, span = powers_ref.shape
    fan_in = own_ref.shape[1]

    @pl.when(step == 0)
    def first():
        turned[:fan_in, :] = own_ref[...].T
        mixed[...] = bias_ref[...] + jnp.dot(
            own_ref[...], weights[0][0], preferred_element_type=jnp.float32
        )

    low = jnp.dot(
        powers_ref[...].reshape(terms * own_cap, span),
        all_ref[...],
        preferred_element_type=jnp.float32,
    ).astype(jnp.bfloat16)
    total = mixed[...]
    for term in range(terms):
        part = low[term * own_cap : (term + 1) * own_cap]
        start = pl.multiple_of((1 + step * terms + term) * fan_in, fan_in)
        turned[pl.ds(start, fan_in), :] = part.T
        total = total + jnp.dot(part, weights[1 + term][0], preferred_element_type=jnp.float32)
    mixed[...] = total


def layer_one_kernel(
    powers_ref,
    all_ref,
    own_ref,
    weight_0,
    weight_a,
    weight_b,
    weight_c,
    bias_ref,
    gain_ref,
    shift_ref,
    valid_ref,
    hidden_ref,
    turned_ref,
    mixed_ref,
):
    step = pl.program_id(0)
    weights = (weight_0, weight_a, weight_b, weight_c)
    forward_step(step, powers_ref, all_ref, own_ref, weights, bias_ref, turned_ref, mixed_ref)

    @pl.when(step == pl.num_programs(0) - 1)
    def finish_layer():
        normed, ignored = norm_forward(mixed_ref[...])
        hidden = (normed * gain_ref[...] + shift_ref[...]) * valid_ref[...]
        hidden_ref[...] = hidden.astype(jnp.bfloat16)


def layer_two_kernel(
    place_ref,
    powers_ref,
    all_ref,
    own_ref,
    weight_0,
    weight_a,
    weight_b,
    weight_c,
    bias_ref,
    gain_ref,
    shift_ref,
    valid_ref,
    upstream_ref,
    active_ref,
    low_ref,
    rest_ref,
    mine_ref,
    other_ref,
    turned,
    mixed,
):
    step = pl.program_id(0)
    weights = (weight_0, weight_a, weight_b, weight_c)
    forward_step(step, powers_ref, all_ref, own_ref, weights, bias_ref, turned, mixed)

    @pl.when(step == pl.num_programs(0) - 1)
    def finish_layer():
        normed, ignored = norm_forward(mixed[...])
        active = (normed * gain_ref[...] + shift_ref[...]) * valid_ref[...]
        active_ref[...] = active.astype(jnp.bfloat16)
        low, rest = norm_backward(
            mixed[...], upstream_ref[...].astype(jnp.float32), gain_ref[...], valid_ref[...]
        )
        low_ref[...] = low
        for place in range(3):
            rest_ref[place : place + 1, :] = rest[place]
        weight_gradient(turned, low, place_ref[1], mine_ref, other_ref)


def backward_step(step, powers_ref, all_ref, own_ref, weights, total):
    terms, own_cap, span = powers_ref.shape
    transposed = (((1,), (1,)), ((), ()))

    @pl.when(step == 0)
    def first():
        total[...] = lax.dot_general(
            own_ref[...], weights[0][0], transposed, preferred_element_type=jnp.float32
        )

    low = jnp.dot(
        powers_ref[...].reshape(terms * own_cap, span),
        all_ref[...],
        preferred_element_type=jnp.float32,
    ).astype(jnp.bfloat16)
    value = total[...]
    for term in range(terms):
        value = value + lax.dot_general(
            low[term * own_cap : (term + 1) * own_cap],
            weights[1 + term][0],
            transposed,
            preferred_element_type=jnp.float32,
        )
    total[...] = value


def back_two_kernel(
    place_ref,
    powers_ref,
    all_ref,
    own_ref,
    weight_0,
    weight_a,
    weight_b,
    weight_c,
    turned_ref,
    mixed_ref,
    gain_ref,
    valid_ref,
    rest_ref,
    low_ref,
    mine_ref,
    other_ref,
    total,
):
    step = pl.program_id(0)
    weights = (weight_0, weight_a, weight_b, weight_c)
    backward_step(step, powers_ref, all_ref, own_ref, weights, total)

    @pl.when(step == pl.num_programs(0) - 1)
    def finish_layer():
        low, rest = norm_backward(mixed_ref[...], total[...], gain_ref[...], valid_ref[...])
        low_ref[...] = low
        weight_gradient(turned_ref, low, place_ref[1], mine_ref, other_ref)
        part = turned_ref.shape[0] // 4
        extra = jnp.zeros((2, mine_ref.shape[1] - part, mine_ref.shape[2]), jnp.bfloat16)
        rows = rest + [rest_ref[place : place + 1, :] for place in range(3)]
        rows = jnp.concatenate(rows + [jnp.zeros((10, rows[0].shape[1]), jnp.float32)], axis=0)

        def below(first_ref, second_ref):
            first_ref[:, part:, :] = extra
            second_ref[:, part:, :] = extra
            first_ref[0, part : part + 16, :] = rows.astype(jnp.bfloat16)

        @pl.when(place_ref[1] == 0)
        def low_half_here():
            below(mine_ref, other_ref)

        @pl.when(place_ref[1] == 1)
        def low_half_there():
            below(other_ref, mine_ref)


def back_one_kernel(
    powers_ref, all_ref, own_ref, weight_0, weight_a, weight_b, weight_c, out_ref, total
):
    step = pl.program_id(0)
    weights = (weight_0, weight_a, weight_b, weight_c)
    backward_step(step, powers_ref, all_ref, own_ref, weights, total)

    @pl.when(step == pl.num_programs(0) - 1)
    def finish_layer():
        out_ref[...] = total[...].astype(jnp.bfloat16)


def layer_pass(kernel, name, place, powers, everyone, own, weight, others, outs, scratch):
    ignored, own_cap, span = powers.shape
    fan_in, width = weight.shape[1:]

    def whole(value):
        return pl.BlockSpec(value.shape, lambda step: (0,) * len(value.shape))

    def term_weight(term):
        return pl.BlockSpec((1, fan_in, width), lambda step: (1 + step * TERMS + term, 0, 0))

    in_specs = [
        pl.BlockSpec((TERMS, own_cap, span), lambda step: (step, 0, 0)),
        whole(everyone),
        whole(own),
        pl.BlockSpec((1, fan_in, width), lambda step: (0, 0, 0)),
    ]
    in_specs += [term_weight(term) for term in range(TERMS)] + [whole(value) for value in others]
    operands = [powers, everyone, own] + [weight] * (1 + TERMS) + list(others)
    if place is not None:
        in_specs = [pl.BlockSpec(memory_space=pltpu.SMEM)] + in_specs
        operands = [place] + operands
    return pl.pallas_call(
        kernel,
        grid=((ORDER - 1) // TERMS,),
        out_shape=outs,
        in_specs=in_specs,
        out_specs=[whole(value) for value in outs],
        scratch_shapes=[pltpu.VMEM(shape, dtype) for shape, dtype in scratch],
        compiler_params=pltpu.CompilerParams(vmem_limit_bytes=VMEM_BYTES),
        cost_estimate=NO_COST,
        name=name,
    )(*operands)


def finish_kernel(scalars_ref, *refs):
    step = pl.program_id(0)
    if len(refs) == 3:
        values_ref, other_ref, out_ref = refs
        parts = [(step >= 0, values_ref)]
        small_ref = None
    else:
        pair_ref, siblings_ref, other_ref, out_ref, small_ref = refs
        parts = [(step < 2, pair_ref), (step >= 2, siblings_ref)]
    part = out_ref.shape[1]
    for here, values_ref in parts:
        @pl.when(here & (scalars_ref[0] == 1))
        def fast_form():
            out_ref[0] = values_ref[0, :part, :].astype(jnp.float32)

        if small_ref is not None:
            @pl.when(here & (scalars_ref[1 + step] == 0))
            def small_sums():
                small_ref[...] = values_ref[0, part : part + 16, :].astype(jnp.float32)

    @pl.when(scalars_ref[0] == 0)
    def general_form():
        out_ref[0] = other_ref[0].astype(jnp.float32)


def finished(scalars, pair, values, other):
    count, part, width = other.shape
    one = (1, part, width)
    if pair is None:
        operands, outs = [values, other], [jax.ShapeDtypeStruct(other.shape, jnp.float32)]

        def quarter(step, scalars_ref):
            return step

        in_specs = [pl.BlockSpec((1,) + values.shape[1:], lambda step, ref: (step, 0, 0))]
        small_specs = []
    else:
        operands = [pair, values, other]
        outs = [
            jax.ShapeDtypeStruct(other.shape, jnp.float32),
            jax.ShapeDtypeStruct((16, width), jnp.float32),
        ]

        def quarter(step, scalars_ref):
            return scalars_ref[1 + step]

        in_specs = [
            pl.BlockSpec((1,) + pair.shape[1:], lambda step, ref: (jnp.minimum(step, 1), 0, 0)),
            pl.BlockSpec((1,) + pair.shape[1:], lambda step, ref: (jnp.maximum(step - 2, 0), 0, 0)),
        ]
        small_specs = [pl.BlockSpec((16, width), lambda step, ref: (0, 0))]
    in_specs.append(
        pl.BlockSpec(one, lambda step, ref: ((1 - ref[0]) * quarter(step, ref), 0, 0))
    )
    result = pl.pallas_call(
        finish_kernel,
        grid_spec=pltpu.PrefetchScalarGridSpec(
            num_scalar_prefetch=1,
            grid=(count,),
            in_specs=in_specs,
            out_specs=[pl.BlockSpec(one, lambda step, ref: (quarter(step, ref), 0, 0))]
            + small_specs,
        ),
        out_shape=outs,
        compiler_params=pltpu.CompilerParams(vmem_limit_bytes=VMEM_BYTES),
        cost_estimate=NO_COST,
        name="finished",
    )(scalars, *operands)
    return result[0] if pair is None else result


def unpack_kernel(place_ref, pieces_ref, keys_ref, own_ref, quadrant_ref, columns, hot):
    groups, high, lanes = pieces_ref.shape
    own_cap, span = own_ref.shape
    whole = own_cap // lanes
    send_cap = keys_ref.shape[1] // groups
    half, rest = send_cap // 2, own_cap - whole * lanes
    for group in range(groups):
        start = group * send_cap
        for tile in range(whole):
            columns[start : start + send_cap, tile * lanes : (tile + 1) * lanes] = pieces_ref[
                group, tile * send_cap : (tile + 1) * send_cap, :
            ]
        ends = pieces_ref[group, whole * send_cap :, :]
        columns[start : start + half, whole * lanes :] = ends[:, :rest]
        columns[start + half : start + send_cap, whole * lanes :] = ends[:, rest:]
    standing = lax.broadcasted_iota(jnp.int32, hot.shape, 0)
    hot[...] = jnp.where(standing == keys_ref[...], 1.0, 0.0).astype(jnp.bfloat16)
    block = jnp.dot(hot[...], columns[...], preferred_element_type=jnp.float32)
    own_ref[...] = block.T.astype(jnp.bfloat16)
    middle = span // 2

    @pl.when(place_ref[0] == 0)
    def first():
        quadrant_ref[...] = own_ref[:, :middle]

    @pl.when(place_ref[0] == 1)
    def second():
        quadrant_ref[...] = own_ref[:, middle:]


def unpacked_block(pieces, keys, place, own_cap, span):
    vector = pl.BlockSpec(memory_space=pltpu.VMEM)
    return pl.pallas_call(
        unpack_kernel,
        out_shape=[
            jax.ShapeDtypeStruct((own_cap, span), jnp.bfloat16),
            jax.ShapeDtypeStruct((own_cap, span // 2), jnp.bfloat16),
        ],
        in_specs=[pl.BlockSpec(memory_space=pltpu.SMEM), vector, vector],
        out_specs=[vector, vector],
        scratch_shapes=[
            pltpu.VMEM((keys.shape[1], own_cap), jnp.bfloat16),
            pltpu.VMEM((span, keys.shape[1]), jnp.bfloat16),
        ],
        compiler_params=pltpu.CompilerParams(vmem_limit_bytes=VMEM_BYTES),
        cost_estimate=NO_COST,
        name="unpacked_block",
    )(place, pieces, keys)


def exclusive_counts(member):
    count = member.shape[-1]
    before = jnp.arange(count)[:, None] < jnp.arange(count)[None, :]
    return jnp.dot(
        member.astype(jnp.bfloat16),
        before.astype(jnp.bfloat16),
        preferred_element_type=jnp.float32,
    ).astype(jnp.int32)


def assign(codes, n_row):
    cluster, valid = codes >> 1, codes & 1
    labels = jnp.arange(CLUSTERS)
    sizes = jnp.sum(
        (cluster.reshape(1, -1) == labels[:, None]) & (valid.reshape(1, -1) == 1), axis=1
    )
    ahead = (sizes[None, :] > sizes[:, None]) | (
        (sizes[None, :] == sizes[:, None]) & (labels[None, :] < labels[:, None])
    )
    rank = jnp.sum(ahead, axis=1)
    others = n_row - 1
    turn, place = (rank - 1) // others, (rank - 1) % others
    group = jnp.where(rank == 0, 0, 1 + jnp.where(turn == 0, place, others - 1 - place))
    of_node = jnp.sum(
        jnp.where(cluster[None] == labels[:, None, None, None], group[:, None, None, None], 0),
        axis=0,
    )
    return jnp.where(valid == 1, of_node, n_row)


def compact(
    codes,
    group,
    features,
    block_keep,
    edge_weight,
    weight_one,
    bias_one,
    gain_one,
    shift_one,
    weight_two,
    bias_two,
    gain_two,
    shift_two,
    cotangent,
    places_of,
    slots_of,
    seats_of,
    decide,
    sizes,
    caps,
):
    row, col = lax.axis_index("row"), lax.axis_index(COL)
    chip, core = lax.axis_index("chip"), lax.axis_index("core")
    n_row, n_col = sizes
    own_cap, send_cap, seat_cap = caps
    own_nodes, in_width = features.shape
    width = weight_two.shape[2]
    span = n_col * own_cap
    targets = jnp.arange(n_row)

    def in_col(value):
        return lax.dynamic_index_in_dim(value, col, 1, False).reshape(-1)

    def in_row(value):
        return lax.dynamic_index_in_dim(value, row, 0, False).reshape(-1)

    row_group, col_group = in_row(group), in_col(group)
    row_slots, col_places = in_row(slots_of(group)), in_col(places_of(group))
    row_keys = jnp.where(row_slots < send_cap, row_group * send_cap + row_slots, -1)
    col_keys = jnp.where(col_places < own_cap, col_group * own_cap + col_places, -1)
    pieces = packed_pieces(
        block_keep,
        in_row(codes),
        in_col(codes),
        row_keys,
        col_keys,
        edge_weight,
        (own_cap, send_cap),
        n_row,
    )
    pieces, codes = lax.optimization_barrier((pieces, codes))
    group = assign(codes, n_row)
    pieces = trade(pieces, "row")
    places, slots, seats = places_of(group), slots_of(group), seats_of(group)

    standing = jnp.arange(n_col)[None, :, None] * own_cap + places
    fits_here = jnp.where(group == row, standing, -1).reshape(n_row, -1)
    slot_of = slots.reshape(n_row, -1)
    target = jnp.max(
        jnp.where(
            slot_of[:, None, :] == jnp.arange(send_cap)[None, :, None], fits_here[:, None, :], -1
        ),
        axis=2,
    )
    keys = target.reshape(1, -1)

    def on_device(value):
        return lax.dynamic_index_in_dim(in_row(value).reshape(n_col, -1), col, 0, False)

    def seat_of_node(groups, group, seats):
        hot = (on_device(group)[None, None, :] == groups[:, None, None]) & (
            on_device(seats)[None, None, :] == jnp.arange(seat_cap)[None, :, None]
        )
        return hot.astype(jnp.bfloat16).reshape(n_row * seat_cap, own_nodes)

    group_col, places_col, seats_col = (
        lax.dynamic_index_in_dim(value, col, 1, False) for value in (group, places, seats)
    )
    seated = (group_col == row)[:, None, :] & (
        seats_col[:, None, :] == jnp.arange(seat_cap)[None, :, None]
    )
    place_of_seat = jnp.max(jnp.where(seated, places_col[:, None, :], -1), axis=2)
    leave_group = place_of_seat.reshape(-1, 1) == jnp.arange(own_cap)
    leave_group = leave_group.astype(jnp.bfloat16)

    partners = row ^ targets
    both = jnp.concatenate([features, cotangent], axis=1)
    both = jnp.dot(seat_of_node(partners, group, seats), both)
    both = both.reshape(n_row, seat_cap, -1)
    from_partner = jnp.max(
        jnp.where((partners[:, None] == targets)[:, :, None], place_of_seat[None], -1), axis=1
    )
    arrive = from_partner.reshape(1, -1) == jnp.arange(own_cap)[:, None]
    arrive = arrive.astype(jnp.bfloat16)
    held_count = jnp.sum(group_col == row)
    valid_rows = (jnp.arange(own_cap) < held_count).astype(jnp.float32)[:, None]
    place = jnp.stack([chip, core]).astype(jnp.int32)
    scalars = (chip, 1 - chip, col * own_cap)
    scalars = tuple(value.astype(jnp.uint32) for value in scalars) + (chip == 0, core == 0, place)
    pieces, both, keys, arrive, leave_group, valid_rows, scalars = lax.optimization_barrier(
        (pieces, both, keys, arrive, leave_group, valid_rows, scalars)
    )
    this_chip, other_chip, own_start, first_chip, first_core, place = scalars

    own_block, quadrant = unpacked_block(pieces, keys, place, own_cap, span)
    quadrant = swap(quadrant, "chip")
    both = [both[0]] + [
        lax.ppermute(both[step], "row", [(place, place ^ step) for place in range(n_row)])
        for step in range(1, n_row)
    ]
    sibling = swap(own_block, "core")
    quadrant, *both = lax.optimization_barrier((quadrant, *both))
    adjacency = normalized_block(own_block, sibling, quadrant, swap(quadrant, "core"), place)
    mine = jnp.dot(arrive, jnp.concatenate(both))
    features_own, cotangent_own = mine[:, :in_width], mine[:, in_width:]
    sibling = swap(features_own, "core")

    first = (own_start + jnp.arange(own_cap, dtype=jnp.uint32))[:, None]
    first = first == jnp.arange(span, dtype=jnp.uint32)[None, :]
    previous = first.astype(jnp.float32)
    current = -lax.dynamic_slice_in_dim(adjacency, own_start, own_cap, 0).astype(jnp.float32)
    lowered = [current.astype(jnp.bfloat16)]
    for position in range(2, ORDER):
        upcoming = (
            -2.0 * jnp.dot(lowered[-1], adjacency, preferred_element_type=jnp.float32) - previous
        )
        low = upcoming.astype(jnp.bfloat16)
        if position == 4:
            low, sibling = lax.optimization_barrier((low, sibling))
            features_chip = joined(features_own, sibling, first_core)
            partner = swap(features_chip, "chip")
        if position == 8:
            low, partner = lax.optimization_barrier((low, partner))
            features_all = joined(features_chip, partner, first_chip)
        previous, current = current, upcoming
        lowered.append(low)
    powers = jnp.concatenate(lowered, axis=0).reshape(ORDER - 1, own_cap, span)

    def everywhere(value_low):
        return lax.all_gather(value_low, COL, axis=0, tiled=True)

    def shaped(*shape, dtype=jnp.bfloat16):
        return jax.ShapeDtypeStruct(shape, dtype)

    part_one, part_two = ORDER * in_width // n_col, ORDER * width // n_col
    padded = -(-(part_one + 16) // (8 * n_row)) * (8 * n_row)
    hidden, turned_one, mixed_one = layer_pass(
        layer_one_kernel,
        "layer_one",
        None,
        powers,
        features_all,
        features_own,
        weight_one,
        [bias_one[None], gain_one[None], shift_one[None], valid_rows],
        [
            shaped(own_cap, width),
            shaped(n_col * part_one, own_cap),
            shaped(own_cap, width, dtype=jnp.float32),
        ],
        [],
    )
    activations, low_two, rest_two, mine, other = layer_pass(
        layer_two_kernel,
        "layer_two",
        place,
        powers,
        everywhere(hidden),
        hidden,
        weight_two,
        [bias_two[None], gain_two[None], shift_two[None], valid_rows, cotangent_own],
        [
            shaped(own_cap, width),
            shaped(own_cap, width),
            shaped(3, width, dtype=jnp.float32),
            shaped(2, part_two, width),
            shaped(2, part_two, width),
        ],
        [((n_col * part_two, own_cap), jnp.bfloat16), ((own_cap, width), jnp.float32)],
    )

    def add_cores(mine, other):
        got = swap(other, "core")
        return tuple(
            added(
                lax.dynamic_index_in_dim(mine, index, 0, False),
                lax.dynamic_index_in_dim(got, index, 0, False),
            )
            for index in (this_chip, other_chip)
        )

    leaving = jnp.dot(leave_group, activations).reshape(n_row, seat_cap, width)
    here, there = add_cores(mine, other)
    everyone_two, there = lax.optimization_barrier((everywhere(low_two), there))
    there = swap(there, "chip")
    low_one, mine, other = layer_pass(
        back_two_kernel,
        "back_two",
        place,
        powers,
        everyone_two,
        low_two,
        weight_two,
        [turned_one, mixed_one, gain_one[None], valid_rows, rest_two],
        [shaped(own_cap, width), shaped(2, padded, width), shaped(2, padded, width)],
        [((own_cap, width), jnp.float32)],
    )
    low_one, there = lax.optimization_barrier((low_one, there))
    second = added(here, there).reshape(n_row, -1, width)
    many = second.shape[1]
    second = jnp.concatenate([second, leaving], axis=1)
    low_one, second = lax.optimization_barrier((low_one, second))
    second = trade(second, "row")
    here, there = add_cores(mine, other)
    low_one, there = lax.optimization_barrier((low_one, there))
    everyone_one = everywhere(low_one)
    there = swap(there, "chip")
    everyone_one, second, there = lax.optimization_barrier((everyone_one, second, there))
    first = added(here, there).reshape(n_row, -1, width)
    share = first.shape[1]
    back = second[:, many:]
    second = jnp.sum(second[:, :many].astype(jnp.float32), axis=0).astype(jnp.bfloat16)
    second = jnp.broadcast_to(second[None], (n_row,) + second.shape)
    mixed = jnp.concatenate([first, second], axis=1)
    everyone_one, mixed = lax.optimization_barrier((everyone_one, mixed))
    mixed = trade(mixed, "row")
    (input_grad,) = layer_pass(
        back_one_kernel,
        "back_one",
        None,
        powers,
        everyone_one,
        low_one,
        weight_one,
        [],
        [shaped(own_cap, in_width)],
        [((own_cap, in_width), jnp.float32)],
    )
    leaving = jnp.dot(leave_group, input_grad).reshape(n_row, seat_cap * in_width // width, width)
    leaving, codes = lax.optimization_barrier((leaving, codes))
    group = assign(codes, n_row)
    enter_home = seat_of_node(targets, group, seats_of(group)).T
    home = jnp.dot(enter_home, back.reshape(-1, width), preferred_element_type=jnp.float32)
    mixed, leaving, home, enter_home = lax.optimization_barrier((mixed, leaving, home, enter_home))
    first = jnp.sum(mixed[:, :share].astype(jnp.float32), axis=0).astype(jnp.bfloat16)
    first = jnp.broadcast_to(first[None], (n_row,) + first.shape)
    first, mixed, codes = lax.optimization_barrier(
        (jnp.concatenate([first, leaving], axis=1), mixed, codes)
    )
    first = trade(first, "row")
    second = lax.all_gather(mixed[:, share:].reshape(-1, width), COL, axis=0)
    fits, others = decide(assign(codes, n_row))
    quarters = jnp.stack(
        [fits.astype(jnp.int32), col, (1 - chip) * 2 + core, chip * 2 + 1 - core, 3 - col]
    )

    def chosen(value, other):
        return jnp.where(fits, value.astype(jnp.float32), other.astype(jnp.float32))

    home = chosen(home, others[0])
    first, home, quarters, others = lax.optimization_barrier((first, home, quarters, others))
    back = first[:, share:].reshape(n_row * seat_cap, in_width)
    mine = first[:, :share].reshape(1, -1, width)
    partner = swap(mine, "chip")
    second = finished(quarters[:1], None, second, others[3])
    home_grad = jnp.dot(enter_home, back, preferred_element_type=jnp.float32)
    home_grad = chosen(home_grad, others[1])
    partner, second, home_grad = lax.optimization_barrier((partner, second, home_grad))
    pair = jnp.concatenate([mine, partner])
    siblings = swap(pair, "core")
    first, small = finished(quarters, pair, siblings, others[2])
    return home, home_grad, first, second, chosen(small[:6], others[4])


def general(
    codes,
    features,
    block_keep,
    edge_weight,
    weight_one,
    bias_one,
    gain_one,
    shift_one,
    weight_two,
    bias_two,
    gain_two,
    shift_two,
    cotangent,
    node_valid,
):
    row, col = lax.axis_index("row"), lax.axis_index(COL)
    row_codes = lax.dynamic_index_in_dim(codes, row, 0, False).reshape(-1)
    col_codes = lax.dynamic_index_in_dim(codes, col, 1, False).reshape(-1)
    tile_rows, tile_cols = edge_weight.shape
    blocks_down, blocks_across = block_keep.shape
    block_side = tile_rows // blocks_down
    linked = (row_codes[:, None] == col_codes[None, :]) & (row_codes[:, None] & 1 == 1)
    linked = linked.reshape(blocks_down, block_side, blocks_across, block_side) & (
        block_keep[:, None, :, None] == 1
    )
    masked = edge_weight * linked.reshape(tile_rows, tile_cols).astype(jnp.bfloat16)
    degree_rows = 1.0 + lax.psum(jnp.sum(masked, axis=1, dtype=jnp.float32), COL)
    own_nodes = features.shape[0]
    own_degree = lax.dynamic_slice_in_dim(
        degree_rows, lax.axis_index(COL) * own_nodes, own_nodes, 0
    )
    degree_cols = lax.all_gather(own_degree, "row", axis=0, tiled=True)
    adjacency = (
        masked.astype(jnp.float32)
        * lax.rsqrt(degree_rows)[:, None]
        * lax.rsqrt(degree_cols)[None, :]
    ).astype(jnp.bfloat16)
    valid_rows = node_valid.astype(jnp.float32)
    stacked_one, mixed_one, hidden = layer_forward(
        adjacency,
        features.astype(jnp.float32),
        weight_one,
        bias_one,
        gain_one,
        shift_one,
        valid_rows,
    )
    stacked_two, mixed_two, activations = layer_forward(
        adjacency, hidden, weight_two, bias_two, gain_two, shift_two, valid_rows
    )
    hidden_grad, weight_two_grad, bias_two_grad, gain_two_grad, shift_two_grad = layer_backward(
        adjacency,
        stacked_two,
        mixed_two,
        cotangent.astype(jnp.float32),
        weight_two,
        gain_two,
        shift_two,
        valid_rows,
    )
    input_grad, weight_one_grad, bias_one_grad, gain_one_grad, shift_one_grad = layer_backward(
        adjacency, stacked_one, mixed_one, hidden_grad, weight_one, gain_one, shift_one, valid_rows
    )
    summed = lax.psum(
        (
            weight_one_grad,
            bias_one_grad,
            gain_one_grad,
            shift_one_grad,
            weight_two_grad,
            bias_two_grad,
            gain_two_grad,
            shift_two_grad,
        ),
        ("row",) + COL,
    )
    weight_one_grad, bias_one_grad, gain_one_grad, shift_one_grad = (
        summed[0],
        summed[1],
        summed[2],
        summed[3],
    )
    weight_two_grad, bias_two_grad, gain_two_grad, shift_two_grad = (
        summed[4],
        summed[5],
        summed[6],
        summed[7],
    )
    return (
        activations,
        input_grad,
        weight_one_grad,
        bias_one_grad,
        gain_one_grad,
        shift_one_grad,
        weight_two_grad,
        bias_two_grad,
        gain_two_grad,
        shift_two_grad,
    )


def local(n_row, n_col, *args):
    (
        features,
        node_valid,
        cluster,
        block_keep,
        edge_weight,
        weight_one,
        bias_one,
        gain_one,
        shift_one,
        weight_two,
        bias_two,
        gain_two,
        shift_two,
        cotangent,
    ) = args
    own_nodes, in_width = features.shape
    own_cap = own_nodes * n_row * 5 // 16
    send_cap = own_nodes * n_col * 11 // 32
    seat_cap = own_nodes // 2
    codes = broadcast_along(cluster * 2 + node_valid, ("row",) + COL, n_row * n_col)
    codes = codes.reshape(n_row, n_col, own_nodes)
    shared = (
        block_keep,
        edge_weight,
        weight_one,
        bias_one,
        gain_one,
        shift_one,
        weight_two,
        bias_two,
        gain_two,
        shift_two,
        cotangent,
    )

    def slow():
        return general(codes, features, *shared, node_valid)

    held = (ORDER - 1) * own_cap * own_cap * n_col * 2
    if held > HELD_BYTES or n_col != 4 or n_row < 2 or n_row & (n_row - 1):
        return slow()
    group = assign(codes, n_row)

    def member_of(group):
        return group[None] == jnp.arange(n_row)[:, None, None, None]

    def places_of(group):
        member = member_of(group).transpose(0, 2, 1, 3).reshape(n_row, n_col, -1)
        places = jnp.sum(jnp.where(member, exclusive_counts(member), 0), axis=0)
        return places.reshape(n_col, n_row, own_nodes).transpose(1, 0, 2)

    def slots_of(group):
        member = member_of(group).reshape(n_row, n_row, -1)
        slots = jnp.sum(jnp.where(member, exclusive_counts(member), 0), axis=0)
        return slots.reshape(n_row, n_col, own_nodes)

    def seats_of(group):
        member = member_of(group)
        return jnp.sum(jnp.where(member, exclusive_counts(member), 0), axis=0)

    width = weight_two.shape[2]

    def instead(state):
        made = slow()
        small = jnp.stack([made[place] for place in (3, 4, 5, 7, 8, 9)])
        return (True,) + tuple(
            value.astype(jnp.bfloat16).reshape(like.shape)
            for value, like in zip((made[0], made[1], made[2], made[6], small), state[1:])
        )

    start = (
        cotangent,
        features,
        weight_one.reshape(n_col, -1, width),
        weight_two.reshape(n_col, -1, width),
        jnp.zeros((6, width), jnp.bfloat16),
    )

    def decide(group):
        member = member_of(group)
        fits = (
            (jnp.max(jnp.sum(member, axis=(1, 3))) <= own_cap)
            & (jnp.max(jnp.sum(member, axis=(2, 3))) <= send_cap)
            & (jnp.max(jnp.sum(member, axis=3)) <= seat_cap)
        )
        others = lax.while_loop(
            lambda state: jnp.logical_not(state[0]),
            instead,
            (fits,) + start,
        )[1:]
        return fits, others

    home, home_grad, first, second, small = compact(
        codes,
        group,
        features,
        *shared,
        places_of,
        slots_of,
        seats_of,
        decide,
        (n_row, n_col),
        (own_cap, send_cap, seat_cap),
    )
    return (
        home,
        home_grad,
        first.reshape(weight_one.shape),
        small[0],
        small[1],
        small[2],
        second.reshape(weight_two.shape),
        small[3],
        small[4],
        small[5],
    )


def solution(mesh):
    n_row, n_col = mesh.shape["row"], mesh.shape["col"]
    by_core = jax.sharding.Mesh(
        mesh.devices.reshape(n_row, n_col // 2, 2), ("row", "chip", "core")
    )
    nodes = ("row", "chip", "core")
    placed = (
        P(nodes, None),
        P(nodes),
        P(nodes),
        P("row", COL),
        P("row", COL),
        P(),
        P(),
        P(),
        P(),
        P(),
        P(),
        P(),
        P(),
        P(nodes, None),
    )
    return jax.shard_map(
        functools.partial(local, n_row, n_col),
        mesh=by_core,
        in_specs=placed,
        out_specs=(P(nodes, None), P(nodes, None), P(), P(), P(), P(), P(), P(), P(), P()),
        check_vma=False,
    )
```

```python
import functools
import math

import jax
import jax.numpy as jnp
from jax import lax
from jax.experimental import pallas as pl
from jax.experimental.pallas import tpu as pltpu
from jax.sharding import PartitionSpec as P

ORDER = 13
CLUSTERS = 16
HELD_BYTES = 1 << 25
VMEM_BYTES = 32 << 20
TERMS = 3
NO_COST = pl.CostEstimate(flops=1, bytes_accessed=1, transcendentals=0)
COL = ("chip", "core")


def finish(mixed, gain, shift, valid_rows):
    active = jax.nn.gelu(mixed, approximate=False)
    centered = active - jnp.mean(active, axis=-1, keepdims=True)
    variance = jnp.mean(centered * centered, axis=-1, keepdims=True)
    return (centered * lax.rsqrt(variance + 1e-05) * gain + shift) * valid_rows[:, None]


def forward_product(adjacency, piece_low):
    partial_value = jnp.dot(
        adjacency,
        lax.all_gather(piece_low, "row", axis=0, tiled=True),
        preferred_element_type=jnp.float32,
    )
    return lax.psum_scatter(partial_value, COL, scatter_dimension=0, tiled=True)


def backward_product(adjacency, piece_low):
    partial_value = lax.dot_general(
        adjacency,
        lax.all_gather(piece_low, COL, axis=0, tiled=True),
        (((0,), (0,)), ((), ())),
        preferred_element_type=jnp.float32,
    )
    return lax.psum_scatter(
        partial_value.astype(jnp.bfloat16), "row", scatter_dimension=0, tiled=True
    ).astype(jnp.float32)


def layer_forward(adjacency, inputs, weight, bias, gain, shift, valid_rows):
    first_low = inputs.astype(jnp.bfloat16)
    second = -forward_product(adjacency, first_low)
    second_low = second.astype(jnp.bfloat16)

    def advance(state_pair, unused):
        previous, current, current_low = state_pair
        upcoming = -2.0 * forward_product(adjacency, current_low) - previous
        upcoming_low = upcoming.astype(jnp.bfloat16)
        return ((current, upcoming, upcoming_low), upcoming_low)

    ignored, others = lax.scan(advance, (inputs, second, second_low), None, length=ORDER - 2)
    stacked = jnp.concatenate([first_low[None], second_low[None], others], axis=0)
    mixed = jnp.einsum("kni,kio->no", stacked, weight, preferred_element_type=jnp.float32) + bias
    return (stacked, mixed, finish(mixed, gain, shift, valid_rows))


def layer_backward(adjacency, stacked, mixed, upstream, weight, gain, shift, valid_rows):

    def local_finish(mixed_in, gain_in, shift_in):
        return finish(mixed_in, gain_in, shift_in, valid_rows)

    ignored, pullback = jax.vjp(local_finish, mixed, gain, shift)
    mixed_grad, gain_grad, shift_grad = pullback(upstream)
    mixed_low = mixed_grad.astype(jnp.bfloat16)
    bias_grad = jnp.sum(mixed_low.astype(jnp.float32), axis=0)
    weight_grad = jnp.einsum("kni,no->kio", stacked, mixed_low, preferred_element_type=jnp.float32)
    direct = jnp.einsum("no,kio->kni", mixed_low, weight, preferred_element_type=jnp.float32)

    def retreat(state_pair, direct_term):
        later_two, later_one = state_pair
        current = (
            direct_term
            - 2.0 * backward_product(adjacency, later_one.astype(jnp.bfloat16))
            - later_two
        )
        return ((later_one, current), None)

    start_pair = (jnp.zeros_like(direct[0]), direct[ORDER - 1])
    (second_grad, first_grad), unused = lax.scan(
        retreat, start_pair, direct[1 : ORDER - 1], reverse=True
    )
    input_grad = (
        direct[0] - backward_product(adjacency, first_grad.astype(jnp.bfloat16)) - second_grad
    )
    return (input_grad, weight_grad, bias_grad, gain_grad, shift_grad)


def swap(value, axis):
    return lax.ppermute(value, axis, [(0, 1), (1, 0)])


def trade(pieces, axis):
    return lax.all_to_all(pieces, axis, 0, 0, tiled=False)


def broadcast_along(value, axis, size):
    return trade(jnp.broadcast_to(value[None], (size,) + value.shape), axis)


def joined(mine, other, mine_first):
    return jnp.where(
        mine_first, jnp.concatenate([mine, other]), jnp.concatenate([other, mine])
    )


def added(mine, received):
    return (mine.astype(jnp.float32) + received.astype(jnp.float32)).astype(jnp.bfloat16)


def assemble(place_ref, own_ref, sibling_ref, near_ref, far_ref, out_ref, done):
    chip, core = place_ref[0], place_ref[1]
    own_cap, span = own_ref.shape
    half = span // 2

    def rows(of_chip, of_core):
        return pl.ds(pl.multiple_of((2 * of_chip + of_core) * own_cap, own_cap), own_cap)

    def fetch(source, of_chip, of_core, columns, place):
        target = out_ref.at[rows(of_chip, of_core), columns]
        return pltpu.make_async_copy(source, target, done.at[place])

    def quadrant_copies(here):
        there = 1 - here
        columns = pl.ds(there * half, half)
        return (
            fetch(near_ref, there, core, columns, 2),
            fetch(far_ref, there, 1 - core, columns, 3),
        )

    everything = pl.ds(0, span)
    top = (
        fetch(own_ref, chip, core, everything, 0),
        fetch(sibling_ref, chip, 1 - core, everything, 1),
    )

    def of_chip(here):
        there = 1 - here
        copies = top + quadrant_copies(here)
        for copy in copies:
            copy.start()
        for copy in copies:
            copy.wait()
        here_rows = pl.ds(here * half, half)
        for tile in range(half // 128):
            columns = pl.ds(there * half + tile * 128, 128)
            strip = out_ref[here_rows, columns]
            turned = jnp.transpose(strip.astype(jnp.float32)).astype(jnp.bfloat16)
            out_ref[columns, here_rows] = turned

    @pl.when(chip == 0)
    def first():
        of_chip(0)

    @pl.when(chip == 1)
    def second():
        of_chip(1)

    across = jnp.ones((1, span), jnp.float32)
    for tile in range(span // 128):
        across = across + jnp.sum(
            out_ref[pl.ds(tile * 128, 128), :].astype(jnp.float32), axis=0, keepdims=True
        )
    across = lax.rsqrt(across)
    for tile in range(span // 128):
        strip = out_ref[pl.ds(tile * 128, 128), :].astype(jnp.float32)
        down = lax.rsqrt(1.0 + jnp.sum(strip, axis=1, keepdims=True))
        out_ref[pl.ds(tile * 128, 128), :] = (strip * down * across).astype(jnp.bfloat16)


def normalized_block(own, sibling, near, far, place):
    span = own.shape[1]
    return pl.pallas_call(
        assemble,
        out_shape=jax.ShapeDtypeStruct((span, span), jnp.bfloat16),
        in_specs=[pl.BlockSpec(memory_space=pltpu.SMEM)]
        + [pl.BlockSpec(memory_space=pltpu.HBM)] * 4,
        out_specs=pl.BlockSpec(memory_space=pltpu.VMEM),
        scratch_shapes=[pltpu.SemaphoreType.DMA((4,))],
        compiler_params=pltpu.CompilerParams(vmem_limit_bytes=VMEM_BYTES),
        cost_estimate=NO_COST,
        name="normalized_block",
    )(place, own, sibling, near, far)


def pack_kernel(
    keep_ref, row_codes_ref, col_codes_ref, row_keys_ref, col_keys_ref, weight_ref, out_ref,
    masked, picked, rows_hot, cols_hot
):
    tile_rows, tile_cols = weight_ref.shape
    blocks_down, blocks_across = keep_ref.shape
    groups, ignored, lanes = out_ref.shape
    send_cap, own_cap = rows_hot.shape[0] // groups, cols_hot.shape[0] // groups
    high, wide = tile_rows // blocks_down, tile_cols // blocks_across
    for down in range(blocks_down):
        for across in range(blocks_across):
            rows, columns = pl.ds(down * high, high), pl.ds(across * wide, wide)
            own, other = row_codes_ref[rows, :], col_codes_ref[:, columns]
            linked = (own == other) & (own % 2 == 1) & (keep_ref[down, across] == 1)
            weight = weight_ref[rows, columns].astype(jnp.float32)
            masked[rows, columns] = jnp.where(linked, weight, 0.0).astype(jnp.bfloat16)

    def one_hot(keys, start, count):
        standing = lax.broadcasted_iota(jnp.int32, (count, keys.shape[1]), 0) + start
        return jnp.where(standing == keys, 1.0, 0.0).astype(jnp.bfloat16)

    for group in range(groups):
        rows_hot[pl.ds(group * send_cap, send_cap), :] = one_hot(
            row_keys_ref[...], group * send_cap, send_cap
        )
        cols_hot[pl.ds(group * own_cap, own_cap), :] = one_hot(
            col_keys_ref[...], group * own_cap, own_cap
        )
    for tile in range(tile_cols // 256):
        columns = pl.ds(tile * 256, 256)
        picked[:, columns] = jnp.dot(
            rows_hot[...], masked[:, columns], preferred_element_type=jnp.float32
        ).astype(jnp.bfloat16)
    whole, half = own_cap // lanes, send_cap // 2
    for group in range(groups):
        packed = lax.dot_general(
            picked[pl.ds(group * send_cap, send_cap), :],
            cols_hot[pl.ds(group * own_cap, own_cap), :],
            (((1,), (1,)), ((), ())),
            preferred_element_type=jnp.float32,
        )
        for tile in range(whole):
            out_ref[group, pl.ds(tile * send_cap, send_cap), :] = packed[
                :, tile * lanes : (tile + 1) * lanes
            ].astype(jnp.bfloat16)
        ends = jnp.concatenate(
            [packed[:half, whole * lanes :], packed[half:, whole * lanes :]], axis=1
        )
        out_ref[group, pl.ds(whole * send_cap, half), :] = ends.astype(jnp.bfloat16)


def packed_pieces(block_keep, row_codes, col_codes, row_keys, col_keys, edge_weight, caps, groups):
    own_cap, send_cap = caps
    tile_rows, tile_cols = edge_weight.shape
    high = own_cap // 128 * send_cap + send_cap // 2
    vector = pl.BlockSpec(memory_space=pltpu.VMEM)
    return pl.pallas_call(
        pack_kernel,
        out_shape=jax.ShapeDtypeStruct((groups, high, 128), jnp.bfloat16),
        in_specs=[pl.BlockSpec(memory_space=pltpu.SMEM)] + [vector] * 5,
        out_specs=vector,
        scratch_shapes=[
            pltpu.VMEM((tile_rows, tile_cols), jnp.bfloat16),
            pltpu.VMEM((groups * send_cap, tile_cols), jnp.bfloat16),
            pltpu.VMEM((groups * send_cap, tile_rows), jnp.bfloat16),
            pltpu.VMEM((groups * own_cap, tile_cols), jnp.bfloat16),
        ],
        compiler_params=pltpu.CompilerParams(vmem_limit_bytes=VMEM_BYTES),
        cost_estimate=NO_COST,
        name="packed_pieces",
    )(block_keep, row_codes[:, None], col_codes[None], row_keys[None], col_keys[None], edge_weight)


def normal_share(mixed):
    return 0.5 * (1.0 + lax.erf(mixed * 0.5**0.5))


def norm_forward(mixed):
    active = mixed * normal_share(mixed)
    centered = active - jnp.mean(active, axis=-1, keepdims=True)
    scale = lax.rsqrt(jnp.mean(centered * centered, axis=-1, keepdims=True) + 1e-05)
    return centered * scale, scale


def norm_backward(mixed, upstream, gain, valid):
    normed, scale = norm_forward(mixed)
    upstream = upstream * valid
    inner = upstream * gain
    inner = inner - jnp.mean(inner, axis=-1, keepdims=True) - normed * jnp.mean(
        inner * normed, axis=-1, keepdims=True
    )
    density = jnp.exp(-0.5 * mixed * mixed) * (1.0 / (2.0 * math.pi) ** 0.5)
    low = (inner * scale * (normal_share(mixed) + mixed * density)).astype(jnp.bfloat16)
    rest = [low.astype(jnp.float32), upstream * normed, upstream]
    return low, [jnp.sum(value, axis=0, keepdims=True) for value in rest]


def weight_gradient(turned_ref, low, core, mine_ref, other_ref):
    part = turned_ref.shape[0] // 4

    def halves(first_ref, second_ref):
        for place in range(4):
            out_ref = second_ref if place % 2 else first_ref
            out_ref[place // 2, :part, :] = jnp.dot(
                turned_ref[place * part : (place + 1) * part, :],
                low,
                preferred_element_type=jnp.float32,
            ).astype(jnp.bfloat16)

    @pl.when(core == 0)
    def low_half_first():
        halves(mine_ref, other_ref)

    @pl.when(core == 1)
    def high_half_first():
        halves(other_ref, mine_ref)


def forward_step(step, powers_ref, all_ref, own_ref, weights, bias_ref, turned, mixed):
    terms, own_cap, span = powers_ref.shape
    fan_in = own_ref.shape[1]

    @pl.when(step == 0)
    def first():
        turned[:fan_in, :] = own_ref[...].T
        mixed[...] = bias_ref[...] + jnp.dot(
            own_ref[...], weights[0][0], preferred_element_type=jnp.float32
        )

    low = jnp.dot(
        powers_ref[...].reshape(terms * own_cap, span),
        all_ref[...],
        preferred_element_type=jnp.float32,
    ).astype(jnp.bfloat16)
    total = mixed[...]
    for term in range(terms):
        part = low[term * own_cap : (term + 1) * own_cap]
        start = pl.multiple_of((1 + step * terms + term) * fan_in, fan_in)
        turned[pl.ds(start, fan_in), :] = part.T
        total = total + jnp.dot(part, weights[1 + term][0], preferred_element_type=jnp.float32)
    mixed[...] = total


def layer_one_kernel(
    powers_ref,
    all_ref,
    own_ref,
    weight_0,
    weight_a,
    weight_b,
    weight_c,
    bias_ref,
    gain_ref,
    shift_ref,
    valid_ref,
    hidden_ref,
    turned_ref,
    mixed_ref,
):
    step = pl.program_id(0)
    weights = (weight_0, weight_a, weight_b, weight_c)
    forward_step(step, powers_ref, all_ref, own_ref, weights, bias_ref, turned_ref, mixed_ref)

    @pl.when(step == pl.num_programs(0) - 1)
    def finish_layer():
        normed, ignored = norm_forward(mixed_ref[...])
        hidden = (normed * gain_ref[...] + shift_ref[...]) * valid_ref[...]
        hidden_ref[...] = hidden.astype(jnp.bfloat16)


def layer_two_kernel(
    place_ref,
    powers_ref,
    all_ref,
    own_ref,
    weight_0,
    weight_a,
    weight_b,
    weight_c,
    bias_ref,
    gain_ref,
    shift_ref,
    valid_ref,
    upstream_ref,
    active_ref,
    low_ref,
    rest_ref,
    mine_ref,
    other_ref,
    turned,
    mixed,
):
    step = pl.program_id(0)
    weights = (weight_0, weight_a, weight_b, weight_c)
    forward_step(step, powers_ref, all_ref, own_ref, weights, bias_ref, turned, mixed)

    @pl.when(step == pl.num_programs(0) - 1)
    def finish_layer():
        normed, ignored = norm_forward(mixed[...])
        active = (normed * gain_ref[...] + shift_ref[...]) * valid_ref[...]
        active_ref[...] = active.astype(jnp.bfloat16)
        low, rest = norm_backward(
            mixed[...], upstream_ref[...].astype(jnp.float32), gain_ref[...], valid_ref[...]
        )
        low_ref[...] = low
        for place in range(3):
            rest_ref[place : place + 1, :] = rest[place]
        weight_gradient(turned, low, place_ref[1], mine_ref, other_ref)


def backward_step(step, powers_ref, all_ref, own_ref, weights, total):
    terms, own_cap, span = powers_ref.shape
    transposed = (((1,), (1,)), ((), ()))

    @pl.when(step == 0)
    def first():
        total[...] = lax.dot_general(
            own_ref[...], weights[0][0], transposed, preferred_element_type=jnp.float32
        )

    low = jnp.dot(
        powers_ref[...].reshape(terms * own_cap, span),
        all_ref[...],
        preferred_element_type=jnp.float32,
    ).astype(jnp.bfloat16)
    value = total[...]
    for term in range(terms):
        value = value + lax.dot_general(
            low[term * own_cap : (term + 1) * own_cap],
            weights[1 + term][0],
            transposed,
            preferred_element_type=jnp.float32,
        )
    total[...] = value


def back_two_kernel(
    place_ref,
    powers_ref,
    all_ref,
    own_ref,
    weight_0,
    weight_a,
    weight_b,
    weight_c,
    turned_ref,
    mixed_ref,
    gain_ref,
    valid_ref,
    rest_ref,
    low_ref,
    mine_ref,
    other_ref,
    total,
):
    step = pl.program_id(0)
    weights = (weight_0, weight_a, weight_b, weight_c)
    backward_step(step, powers_ref, all_ref, own_ref, weights, total)

    @pl.when(step == pl.num_programs(0) - 1)
    def finish_layer():
        low, rest = norm_backward(mixed_ref[...], total[...], gain_ref[...], valid_ref[...])
        low_ref[...] = low
        weight_gradient(turned_ref, low, place_ref[1], mine_ref, other_ref)
        part = turned_ref.shape[0] // 4
        extra = jnp.zeros((2, mine_ref.shape[1] - part, mine_ref.shape[2]), jnp.bfloat16)
        rows = rest + [rest_ref[place : place + 1, :] for place in range(3)]
        rows = jnp.concatenate(rows + [jnp.zeros((10, rows[0].shape[1]), jnp.float32)], axis=0)

        def below(first_ref, second_ref):
            first_ref[:, part:, :] = extra
            second_ref[:, part:, :] = extra
            first_ref[0, part : part + 16, :] = rows.astype(jnp.bfloat16)

        @pl.when(place_ref[1] == 0)
        def low_half_here():
            below(mine_ref, other_ref)

        @pl.when(place_ref[1] == 1)
        def low_half_there():
            below(other_ref, mine_ref)


def back_one_kernel(
    powers_ref, all_ref, own_ref, weight_0, weight_a, weight_b, weight_c, out_ref, total
):
    step = pl.program_id(0)
    weights = (weight_0, weight_a, weight_b, weight_c)
    backward_step(step, powers_ref, all_ref, own_ref, weights, total)

    @pl.when(step == pl.num_programs(0) - 1)
    def finish_layer():
        out_ref[...] = total[...].astype(jnp.bfloat16)


def layer_pass(kernel, name, place, powers, everyone, own, weight, others, outs, scratch):
    ignored, own_cap, span = powers.shape
    fan_in, width = weight.shape[1:]

    def whole(value):
        return pl.BlockSpec(value.shape, lambda step: (0,) * len(value.shape))

    def term_weight(term):
        return pl.BlockSpec((1, fan_in, width), lambda step: (1 + step * TERMS + term, 0, 0))

    in_specs = [
        pl.BlockSpec((TERMS, own_cap, span), lambda step: (step, 0, 0)),
        whole(everyone),
        whole(own),
        pl.BlockSpec((1, fan_in, width), lambda step: (0, 0, 0)),
    ]
    in_specs += [term_weight(term) for term in range(TERMS)] + [whole(value) for value in others]
    operands = [powers, everyone, own] + [weight] * (1 + TERMS) + list(others)
    if place is not None:
        in_specs = [pl.BlockSpec(memory_space=pltpu.SMEM)] + in_specs
        operands = [place] + operands
    return pl.pallas_call(
        kernel,
        grid=((ORDER - 1) // TERMS,),
        out_shape=outs,
        in_specs=in_specs,
        out_specs=[whole(value) for value in outs],
        scratch_shapes=[pltpu.VMEM(shape, dtype) for shape, dtype in scratch],
        compiler_params=pltpu.CompilerParams(vmem_limit_bytes=VMEM_BYTES),
        cost_estimate=NO_COST,
        name=name,
    )(*operands)


def finish_kernel(scalars_ref, *refs):
    step = pl.program_id(0)
    if len(refs) == 3:
        values_ref, other_ref, out_ref = refs
        parts = [(step >= 0, values_ref)]
        small_ref = None
    else:
        pair_ref, siblings_ref, other_ref, out_ref, small_ref = refs
        parts = [(step < 2, pair_ref), (step >= 2, siblings_ref)]
    part = out_ref.shape[1]
    for here, values_ref in parts:
        @pl.when(here & (scalars_ref[0] == 1))
        def fast_form():
            out_ref[0] = values_ref[0, :part, :].astype(jnp.float32)

        if small_ref is not None:
            @pl.when(here & (scalars_ref[1 + step] == 0))
            def small_sums():
                small_ref[...] = values_ref[0, part : part + 16, :].astype(jnp.float32)

    @pl.when(scalars_ref[0] == 0)
    def general_form():
        out_ref[0] = other_ref[0].astype(jnp.float32)


def finished(scalars, pair, values, other):
    count, part, width = other.shape
    one = (1, part, width)
    if pair is None:
        operands, outs = [values, other], [jax.ShapeDtypeStruct(other.shape, jnp.float32)]

        def quarter(step, scalars_ref):
            return step

        in_specs = [pl.BlockSpec((1,) + values.shape[1:], lambda step, ref: (step, 0, 0))]
        small_specs = []
    else:
        operands = [pair, values, other]
        outs = [
            jax.ShapeDtypeStruct(other.shape, jnp.float32),
            jax.ShapeDtypeStruct((16, width), jnp.float32),
        ]

        def quarter(step, scalars_ref):
            return scalars_ref[1 + step]

        in_specs = [
            pl.BlockSpec((1,) + pair.shape[1:], lambda step, ref: (jnp.minimum(step, 1), 0, 0)),
            pl.BlockSpec((1,) + pair.shape[1:], lambda step, ref: (jnp.maximum(step - 2, 0), 0, 0)),
        ]
        small_specs = [pl.BlockSpec((16, width), lambda step, ref: (0, 0))]
    in_specs.append(
        pl.BlockSpec(one, lambda step, ref: ((1 - ref[0]) * quarter(step, ref), 0, 0))
    )
    result = pl.pallas_call(
        finish_kernel,
        grid_spec=pltpu.PrefetchScalarGridSpec(
            num_scalar_prefetch=1,
            grid=(count,),
            in_specs=in_specs,
            out_specs=[pl.BlockSpec(one, lambda step, ref: (quarter(step, ref), 0, 0))]
            + small_specs,
        ),
        out_shape=outs,
        compiler_params=pltpu.CompilerParams(vmem_limit_bytes=VMEM_BYTES),
        cost_estimate=NO_COST,
        name="finished",
    )(scalars, *operands)
    return result[0] if pair is None else result


def unpack_kernel(place_ref, pieces_ref, keys_ref, own_ref, quadrant_ref, columns, hot):
    groups, high, lanes = pieces_ref.shape
    own_cap, span = own_ref.shape
    whole = own_cap // lanes
    send_cap = keys_ref.shape[1] // groups
    half, rest = send_cap // 2, own_cap - whole * lanes
    for group in range(groups):
        start = group * send_cap
        for tile in range(whole):
            columns[start : start + send_cap, tile * lanes : (tile + 1) * lanes] = pieces_ref[
                group, tile * send_cap : (tile + 1) * send_cap, :
            ]
        ends = pieces_ref[group, whole * send_cap :, :]
        columns[start : start + half, whole * lanes :] = ends[:, :rest]
        columns[start + half : start + send_cap, whole * lanes :] = ends[:, rest:]
    standing = lax.broadcasted_iota(jnp.int32, hot.shape, 0)
    hot[...] = jnp.where(standing == keys_ref[...], 1.0, 0.0).astype(jnp.bfloat16)
    block = jnp.dot(hot[...], columns[...], preferred_element_type=jnp.float32)
    own_ref[...] = block.T.astype(jnp.bfloat16)
    middle = span // 2

    @pl.when(place_ref[0] == 0)
    def first():
        quadrant_ref[...] = own_ref[:, :middle]

    @pl.when(place_ref[0] == 1)
    def second():
        quadrant_ref[...] = own_ref[:, middle:]


def unpacked_block(pieces, keys, place, own_cap, span):
    vector = pl.BlockSpec(memory_space=pltpu.VMEM)
    return pl.pallas_call(
        unpack_kernel,
        out_shape=[
            jax.ShapeDtypeStruct((own_cap, span), jnp.bfloat16),
            jax.ShapeDtypeStruct((own_cap, span // 2), jnp.bfloat16),
        ],
        in_specs=[pl.BlockSpec(memory_space=pltpu.SMEM), vector, vector],
        out_specs=[vector, vector],
        scratch_shapes=[
            pltpu.VMEM((keys.shape[1], own_cap), jnp.bfloat16),
            pltpu.VMEM((span, keys.shape[1]), jnp.bfloat16),
        ],
        compiler_params=pltpu.CompilerParams(vmem_limit_bytes=VMEM_BYTES),
        cost_estimate=NO_COST,
        name="unpacked_block",
    )(place, pieces, keys)


def fit_kernel(codes_ref, out_ref, *, n_row, caps):
    own_cap, send_cap, seat_cap = caps
    codes = codes_ref[...]
    devices = codes.shape[0]
    n_col = devices // n_row
    label = lax.broadcasted_iota(jnp.int32, (devices, 128), 1)
    counts = jnp.zeros((devices, 128), jnp.float32)
    for cluster in range(CLUSTERS):
        here = jnp.where(codes == 2 * cluster + 1, 1.0, 0.0)
        counts = counts + jnp.where(
            label == cluster, jnp.sum(here, axis=1, keepdims=True), 0.0
        )
    sizes = jnp.sum(counts, axis=0, keepdims=True)
    across = jnp.broadcast_to(sizes, (128, 128))
    down = across.T
    first = lax.broadcasted_iota(jnp.int32, (128, 128), 0)
    second = lax.broadcasted_iota(jnp.int32, (128, 128), 1)
    ahead = (across > down) | ((across == down) & (second < first))
    ahead = ahead & (second < CLUSTERS)
    rank = jnp.sum(jnp.where(ahead, 1.0, 0.0), axis=1, keepdims=True).astype(jnp.int32)
    others = n_row - 1
    later = rank > others
    turn = jnp.zeros_like(rank)
    for count in range(1, CLUSTERS // others + 1):
        turn = turn + jnp.where(rank - 1 >= count * others, 1, 0)
    place = rank - 1 - turn * others
    group = jnp.where(rank == 0, 0, 1 + jnp.where(later, others - 1 - place, place))
    member = (group == second) & (first < CLUSTERS)
    held = jnp.dot(
        counts.astype(jnp.bfloat16),
        jnp.where(member, 1.0, 0.0).astype(jnp.bfloat16),
        preferred_element_type=jnp.float32,
    )
    by_row = jnp.zeros((1, 128), jnp.float32)
    for row in range(n_row):
        rows = jnp.sum(held[row * n_col : (row + 1) * n_col], axis=0, keepdims=True)
        by_row = jnp.maximum(by_row, rows)
    device = lax.broadcasted_iota(jnp.int32, (devices, 128), 0)
    by_col = jnp.zeros((1, 128), jnp.float32)
    for col in range(n_col):
        cols = jnp.where(device % n_col == col, held, 0.0)
        by_col = jnp.maximum(by_col, jnp.sum(cols, axis=0, keepdims=True))
    fits = (
        (jnp.max(by_col) <= own_cap) & (jnp.max(by_row) <= send_cap) & (jnp.max(held) <= seat_cap)
    )
    out_ref[0] = jnp.where(fits, 1, 0)


def fits_in(codes, n_row, caps):
    fits = pl.pallas_call(
        functools.partial(fit_kernel, n_row=n_row, caps=caps),
        out_shape=jax.ShapeDtypeStruct((1,), jnp.int32),
        in_specs=[pl.BlockSpec(memory_space=pltpu.VMEM)],
        out_specs=pl.BlockSpec(memory_space=pltpu.SMEM),
        cost_estimate=NO_COST,
        name="fits",
    )(codes.reshape(-1, codes.shape[-1]))
    return fits


def exclusive_counts(member):
    count = member.shape[-1]
    before = jnp.arange(count)[:, None] < jnp.arange(count)[None, :]
    return jnp.dot(
        member.astype(jnp.bfloat16),
        before.astype(jnp.bfloat16),
        preferred_element_type=jnp.float32,
    ).astype(jnp.int32)


def assign(codes, n_row):
    cluster, valid = codes >> 1, codes & 1
    labels = jnp.arange(CLUSTERS)
    sizes = jnp.sum(
        (cluster.reshape(1, -1) == labels[:, None]) & (valid.reshape(1, -1) == 1), axis=1
    )
    ahead = (sizes[None, :] > sizes[:, None]) | (
        (sizes[None, :] == sizes[:, None]) & (labels[None, :] < labels[:, None])
    )
    rank = jnp.sum(ahead, axis=1)
    others = n_row - 1
    turn, place = (rank - 1) // others, (rank - 1) % others
    group = jnp.where(rank == 0, 0, 1 + jnp.where(turn == 0, place, others - 1 - place))
    of_node = jnp.sum(
        jnp.where(cluster[None] == labels[:, None, None, None], group[:, None, None, None], 0),
        axis=0,
    )
    return jnp.where(valid == 1, of_node, n_row)


def compact(
    codes,
    group,
    features,
    block_keep,
    edge_weight,
    weight_one,
    bias_one,
    gain_one,
    shift_one,
    weight_two,
    bias_two,
    gain_two,
    shift_two,
    cotangent,
    places_of,
    slots_of,
    seats_of,
    decide,
    sizes,
    caps,
):
    row, col = lax.axis_index("row"), lax.axis_index(COL)
    chip, core = lax.axis_index("chip"), lax.axis_index("core")
    n_row, n_col = sizes
    own_cap, send_cap, seat_cap = caps
    own_nodes, in_width = features.shape
    width = weight_two.shape[2]
    span = n_col * own_cap
    targets = jnp.arange(n_row)

    def in_col(value):
        return lax.dynamic_index_in_dim(value, col, 1, False).reshape(-1)

    def in_row(value):
        return lax.dynamic_index_in_dim(value, row, 0, False).reshape(-1)

    row_group, col_group = in_row(group), in_col(group)
    row_slots, col_places = in_row(slots_of(group)), in_col(places_of(group))
    row_keys = jnp.where(row_slots < send_cap, row_group * send_cap + row_slots, -1)
    col_keys = jnp.where(col_places < own_cap, col_group * own_cap + col_places, -1)
    pieces = packed_pieces(
        block_keep,
        in_row(codes),
        in_col(codes),
        row_keys,
        col_keys,
        edge_weight,
        (own_cap, send_cap),
        n_row,
    )
    pieces, codes = lax.optimization_barrier((pieces, codes))
    group = assign(codes, n_row)
    pieces = trade(pieces, "row")
    fits, others = decide(codes)
    places, slots, seats = places_of(group), slots_of(group), seats_of(group)

    standing = jnp.arange(n_col)[None, :, None] * own_cap + places
    fits_here = jnp.where(group == row, standing, -1).reshape(n_row, -1)
    slot_of = slots.reshape(n_row, -1)
    target = jnp.max(
        jnp.where(
            slot_of[:, None, :] == jnp.arange(send_cap)[None, :, None], fits_here[:, None, :], -1
        ),
        axis=2,
    )
    keys = target.reshape(1, -1)

    partners = row ^ targets
    group_here = lax.dynamic_index_in_dim(in_row(group).reshape(n_col, -1), col, 0, False)
    seat_here = lax.dynamic_index_in_dim(in_row(seats).reshape(n_col, -1), col, 0, False)

    def seat_of_node(groups):
        hot = (group_here[None, None, :] == groups[:, None, None]) & (
            seat_here[None, None, :] == jnp.arange(seat_cap)[None, :, None]
        )
        return hot.astype(jnp.bfloat16).reshape(n_row * seat_cap, own_nodes)

    both = jnp.dot(seat_of_node(partners), jnp.concatenate([features, cotangent], axis=1))
    both = both.reshape(n_row, seat_cap, -1)
    enter_home = seat_of_node(targets).T
    group_col = lax.dynamic_index_in_dim(group, col, 1, False)
    seats_col = lax.dynamic_index_in_dim(seats, col, 1, False)
    places_col = lax.dynamic_index_in_dim(places, col, 1, False)
    seated = (group_col == row)[:, None, :] & (
        seats_col[:, None, :] == jnp.arange(seat_cap)[None, :, None]
    )
    place_of_seat = jnp.max(jnp.where(seated, places_col[:, None, :], -1), axis=2)
    from_partner = jnp.max(
        jnp.where((partners[:, None] == targets)[:, :, None], place_of_seat[None], -1), axis=1
    )
    arrive = from_partner.reshape(1, -1) == jnp.arange(own_cap)[:, None]
    arrive = arrive.astype(jnp.bfloat16)
    leave_group = place_of_seat.reshape(-1, 1) == jnp.arange(own_cap)[None, :]
    leave_group = leave_group.astype(jnp.bfloat16)
    held_count = jnp.sum(group_col == row)
    valid_rows = (jnp.arange(own_cap) < held_count).astype(jnp.float32)[:, None]
    place = jnp.stack([chip, core]).astype(jnp.int32)
    quarters = jnp.stack([col, (1 - chip) * 2 + core, chip * 2 + 1 - core, 3 - col])
    quarters = jnp.concatenate([fits, quarters.astype(jnp.int32)])
    scalars = (chip, 1 - chip, col * own_cap)
    scalars = tuple(value.astype(jnp.uint32) for value in scalars) + (chip == 0, core == 0, place, quarters)
    pieces, both, keys, arrive, leave_group, enter_home, valid_rows, others, scalars = (
        lax.optimization_barrier(
            (pieces, both, keys, arrive, leave_group, enter_home, valid_rows, others, scalars)
        )
    )
    this_chip, other_chip, own_start, first_chip, first_core, place, quarters = scalars

    own_block, quadrant = unpacked_block(pieces, keys, place, own_cap, span)
    quadrant = swap(quadrant, "chip")
    both = [both[0]] + [
        lax.ppermute(both[step], "row", [(place, place ^ step) for place in range(n_row)])
        for step in range(1, n_row)
    ]
    sibling = swap(own_block, "core")
    quadrant, *both = lax.optimization_barrier((quadrant, *both))
    adjacency = normalized_block(own_block, sibling, quadrant, swap(quadrant, "core"), place)
    mine = jnp.dot(arrive, jnp.concatenate(both))
    features_own, cotangent_own = mine[:, :in_width], mine[:, in_width:]
    sibling = swap(features_own, "core")

    first = (own_start + jnp.arange(own_cap, dtype=jnp.uint32))[:, None]
    first = first == jnp.arange(span, dtype=jnp.uint32)[None, :]
    previous = first.astype(jnp.float32)
    current = -lax.dynamic_slice_in_dim(adjacency, own_start, own_cap, 0).astype(jnp.float32)
    lowered = [current.astype(jnp.bfloat16)]
    for position in range(2, ORDER):
        upcoming = (
            -2.0 * jnp.dot(lowered[-1], adjacency, preferred_element_type=jnp.float32) - previous
        )
        low = upcoming.astype(jnp.bfloat16)
        if position == 4:
            low, sibling = lax.optimization_barrier((low, sibling))
            features_chip = joined(features_own, sibling, first_core)
            partner = swap(features_chip, "chip")
        if position == 8:
            low, partner = lax.optimization_barrier((low, partner))
            features_all = joined(features_chip, partner, first_chip)
        previous, current = current, upcoming
        lowered.append(low)
    powers = jnp.concatenate(lowered, axis=0).reshape(ORDER - 1, own_cap, span)

    def everywhere(value_low):
        return lax.all_gather(value_low, COL, axis=0, tiled=True)

    def chosen(value, other):
        return jnp.where(quarters[0] == 1, value.astype(jnp.float32), other.astype(jnp.float32))

    def shaped(*shape, dtype=jnp.bfloat16):
        return jax.ShapeDtypeStruct(shape, dtype)

    part_one, part_two = ORDER * in_width // n_col, ORDER * width // n_col
    padded = -(-(part_one + 16) // (8 * n_row)) * (8 * n_row)
    hidden, turned_one, mixed_one = layer_pass(
        layer_one_kernel,
        "layer_one",
        None,
        powers,
        features_all,
        features_own,
        weight_one,
        [bias_one[None], gain_one[None], shift_one[None], valid_rows],
        [
            shaped(own_cap, width),
            shaped(n_col * part_one, own_cap),
            shaped(own_cap, width, dtype=jnp.float32),
        ],
        [],
    )
    activations, low_two, rest_two, mine, other = layer_pass(
        layer_two_kernel,
        "layer_two",
        place,
        powers,
        everywhere(hidden),
        hidden,
        weight_two,
        [bias_two[None], gain_two[None], shift_two[None], valid_rows, cotangent_own],
        [
            shaped(own_cap, width),
            shaped(own_cap, width),
            shaped(3, width, dtype=jnp.float32),
            shaped(2, part_two, width),
            shaped(2, part_two, width),
        ],
        [((n_col * part_two, own_cap), jnp.bfloat16), ((own_cap, width), jnp.float32)],
    )

    def add_cores(mine, other):
        got = swap(other, "core")
        return tuple(
            added(
                lax.dynamic_index_in_dim(mine, index, 0, False),
                lax.dynamic_index_in_dim(got, index, 0, False),
            )
            for index in (this_chip, other_chip)
        )

    leaving = jnp.dot(leave_group, activations).reshape(n_row, seat_cap, width)
    here, there = add_cores(mine, other)
    everyone_two, there = lax.optimization_barrier((everywhere(low_two), there))
    there = swap(there, "chip")
    low_one, mine, other = layer_pass(
        back_two_kernel,
        "back_two",
        place,
        powers,
        everyone_two,
        low_two,
        weight_two,
        [turned_one, mixed_one, gain_one[None], valid_rows, rest_two],
        [shaped(own_cap, width), shaped(2, padded, width), shaped(2, padded, width)],
        [((own_cap, width), jnp.float32)],
    )
    low_one, there = lax.optimization_barrier((low_one, there))
    second = added(here, there).reshape(n_row, -1, width)
    many = second.shape[1]
    second = jnp.concatenate([second, leaving], axis=1)
    low_one, second = lax.optimization_barrier((low_one, second))
    second = trade(second, "row")
    here, there = add_cores(mine, other)
    low_one, there = lax.optimization_barrier((low_one, there))
    everyone_one = everywhere(low_one)
    there = swap(there, "chip")
    everyone_one, second, there = lax.optimization_barrier((everyone_one, second, there))
    first = added(here, there).reshape(n_row, -1, width)
    share = first.shape[1]
    back = second[:, many:]
    second = jnp.sum(second[:, :many].astype(jnp.float32), axis=0).astype(jnp.bfloat16)
    second = jnp.broadcast_to(second[None], (n_row,) + second.shape)
    mixed = jnp.concatenate([first, second], axis=1)
    everyone_one, mixed = lax.optimization_barrier((everyone_one, mixed))
    mixed = trade(mixed, "row")
    (input_grad,) = layer_pass(
        back_one_kernel,
        "back_one",
        None,
        powers,
        everyone_one,
        low_one,
        weight_one,
        [],
        [shaped(own_cap, in_width)],
        [((own_cap, in_width), jnp.float32)],
    )
    leaving = jnp.dot(leave_group, input_grad).reshape(n_row, seat_cap * in_width // width, width)
    home = jnp.dot(enter_home, back.reshape(-1, width), preferred_element_type=jnp.float32)
    home = chosen(home, others[0])
    mixed, leaving, home = lax.optimization_barrier((mixed, leaving, home))
    first = jnp.sum(mixed[:, :share].astype(jnp.float32), axis=0).astype(jnp.bfloat16)
    first = jnp.broadcast_to(first[None], (n_row,) + first.shape)
    first, mixed = lax.optimization_barrier((jnp.concatenate([first, leaving], axis=1), mixed))
    first = trade(first, "row")
    second = lax.all_gather(mixed[:, share:].reshape(-1, width), COL, axis=0)
    back = first[:, share:].reshape(n_row * seat_cap, in_width)
    mine = first[:, :share].reshape(1, -1, width)
    partner = swap(mine, "chip")
    second = finished(quarters[:1], None, second, others[3])
    home_grad = jnp.dot(enter_home, back, preferred_element_type=jnp.float32)
    home_grad = chosen(home_grad, others[1])
    partner, second, home_grad = lax.optimization_barrier((partner, second, home_grad))
    pair = jnp.concatenate([mine, partner])
    siblings = swap(pair, "core")
    first, small = finished(quarters, pair, siblings, others[2])
    return home, home_grad, first, second, chosen(small[:6], others[4])


def general(
    codes,
    features,
    block_keep,
    edge_weight,
    weight_one,
    bias_one,
    gain_one,
    shift_one,
    weight_two,
    bias_two,
    gain_two,
    shift_two,
    cotangent,
    node_valid,
):
    row, col = lax.axis_index("row"), lax.axis_index(COL)
    row_codes = lax.dynamic_index_in_dim(codes, row, 0, False).reshape(-1)
    col_codes = lax.dynamic_index_in_dim(codes, col, 1, False).reshape(-1)
    tile_rows, tile_cols = edge_weight.shape
    blocks_down, blocks_across = block_keep.shape
    block_side = tile_rows // blocks_down
    linked = (row_codes[:, None] == col_codes[None, :]) & (row_codes[:, None] & 1 == 1)
    linked = linked.reshape(blocks_down, block_side, blocks_across, block_side) & (
        block_keep[:, None, :, None] == 1
    )
    masked = edge_weight * linked.reshape(tile_rows, tile_cols).astype(jnp.bfloat16)
    degree_rows = 1.0 + lax.psum(jnp.sum(masked, axis=1, dtype=jnp.float32), COL)
    own_nodes = features.shape[0]
    own_degree = lax.dynamic_slice_in_dim(
        degree_rows, lax.axis_index(COL) * own_nodes, own_nodes, 0
    )
    degree_cols = lax.all_gather(own_degree, "row", axis=0, tiled=True)
    adjacency = (
        masked.astype(jnp.float32)
        * lax.rsqrt(degree_rows)[:, None]
        * lax.rsqrt(degree_cols)[None, :]
    ).astype(jnp.bfloat16)
    valid_rows = node_valid.astype(jnp.float32)
    stacked_one, mixed_one, hidden = layer_forward(
        adjacency,
        features.astype(jnp.float32),
        weight_one,
        bias_one,
        gain_one,
        shift_one,
        valid_rows,
    )
    stacked_two, mixed_two, activations = layer_forward(
        adjacency, hidden, weight_two, bias_two, gain_two, shift_two, valid_rows
    )
    hidden_grad, weight_two_grad, bias_two_grad, gain_two_grad, shift_two_grad = layer_backward(
        adjacency,
        stacked_two,
        mixed_two,
        cotangent.astype(jnp.float32),
        weight_two,
        gain_two,
        shift_two,
        valid_rows,
    )
    input_grad, weight_one_grad, bias_one_grad, gain_one_grad, shift_one_grad = layer_backward(
        adjacency, stacked_one, mixed_one, hidden_grad, weight_one, gain_one, shift_one, valid_rows
    )
    summed = lax.psum(
        (
            weight_one_grad,
            bias_one_grad,
            gain_one_grad,
            shift_one_grad,
            weight_two_grad,
            bias_two_grad,
            gain_two_grad,
            shift_two_grad,
        ),
        ("row",) + COL,
    )
    weight_one_grad, bias_one_grad, gain_one_grad, shift_one_grad = (
        summed[0],
        summed[1],
        summed[2],
        summed[3],
    )
    weight_two_grad, bias_two_grad, gain_two_grad, shift_two_grad = (
        summed[4],
        summed[5],
        summed[6],
        summed[7],
    )
    return (
        activations,
        input_grad,
        weight_one_grad,
        bias_one_grad,
        gain_one_grad,
        shift_one_grad,
        weight_two_grad,
        bias_two_grad,
        gain_two_grad,
        shift_two_grad,
    )


def local(n_row, n_col, *args):
    (
        features,
        node_valid,
        cluster,
        block_keep,
        edge_weight,
        weight_one,
        bias_one,
        gain_one,
        shift_one,
        weight_two,
        bias_two,
        gain_two,
        shift_two,
        cotangent,
    ) = args
    own_nodes, in_width = features.shape
    own_cap = own_nodes * n_row * 5 // 16
    send_cap = own_nodes * n_col * 11 // 32
    seat_cap = own_nodes // 2
    codes = broadcast_along(cluster * 2 + node_valid, ("row",) + COL, n_row * n_col)
    codes = codes.reshape(n_row, n_col, own_nodes)
    shared = (
        block_keep,
        edge_weight,
        weight_one,
        bias_one,
        gain_one,
        shift_one,
        weight_two,
        bias_two,
        gain_two,
        shift_two,
        cotangent,
    )

    def slow():
        return general(codes, features, *shared, node_valid)

    held = (ORDER - 1) * own_cap * own_cap * n_col * 2
    if held > HELD_BYTES or n_col != 4 or n_row < 2 or n_row & (n_row - 1):
        return slow()
    group = assign(codes, n_row)

    def member_of(group):
        return group[None] == jnp.arange(n_row)[:, None, None, None]

    def places_of(group):
        member = member_of(group).transpose(0, 2, 1, 3).reshape(n_row, n_col, -1)
        places = jnp.sum(jnp.where(member, exclusive_counts(member), 0), axis=0)
        return places.reshape(n_col, n_row, own_nodes).transpose(1, 0, 2)

    def slots_of(group):
        member = member_of(group).reshape(n_row, n_row, -1)
        slots = jnp.sum(jnp.where(member, exclusive_counts(member), 0), axis=0)
        return slots.reshape(n_row, n_col, own_nodes)

    def seats_of(group):
        member = member_of(group)
        return jnp.sum(jnp.where(member, exclusive_counts(member), 0), axis=0)

    width = weight_two.shape[2]

    def instead(state):
        made = slow()
        small = jnp.stack([made[place] for place in (3, 4, 5, 7, 8, 9)])
        return (jnp.ones_like(state[0]),) + tuple(
            value.astype(jnp.bfloat16).reshape(like.shape)
            for value, like in zip((made[0], made[1], made[2], made[6], small), state[1:])
        )

    shapes = (
        (own_nodes, width),
        (own_nodes, in_width),
        (n_col, ORDER * in_width // n_col, width),
        (n_col, ORDER * width // n_col, width),
        (6, width),
    )

    def decide(codes):
        fits = fits_in(codes, n_row, (own_cap, send_cap, seat_cap))
        others = lax.while_loop(
            lambda state: state[0][0] == 0,
            instead,
            (fits,) + tuple(jnp.zeros(shape, jnp.bfloat16) for shape in shapes),
        )[1:]
        return fits, others

    home, home_grad, first, second, small = compact(
        codes,
        group,
        features,
        *shared,
        places_of,
        slots_of,
        seats_of,
        decide,
        (n_row, n_col),
        (own_cap, send_cap, seat_cap),
    )
    return (
        home,
        home_grad,
        first.reshape(weight_one.shape),
        small[0],
        small[1],
        small[2],
        second.reshape(weight_two.shape),
        small[3],
        small[4],
        small[5],
    )


def solution(mesh):
    n_row, n_col = mesh.shape["row"], mesh.shape["col"]
    by_core = jax.sharding.Mesh(
        mesh.devices.reshape(n_row, n_col // 2, 2), ("row", "chip", "core")
    )
    nodes = ("row", "chip", "core")
    placed = (
        P(nodes, None),
        P(nodes),
        P(nodes),
        P("row", COL),
        P("row", COL),
        P(),
        P(),
        P(),
        P(),
        P(),
        P(),
        P(),
        P(),
        P(nodes, None),
    )
    return jax.shard_map(
        functools.partial(local, n_row, n_col),
        mesh=by_core,
        in_specs=placed,
        out_specs=(P(nodes, None), P(nodes, None), P(), P(), P(), P(), P(), P(), P(), P()),
        check_vma=False,
    )
```

```python
import functools
import math

import jax
import jax.numpy as jnp
from jax import lax
from jax.experimental import pallas as pl
from jax.experimental.pallas import tpu as pltpu
from jax.sharding import PartitionSpec as P

ORDER = 13
CLUSTERS = 16
HELD_BYTES = 1 << 25
VMEM_BYTES = 32 << 20
TERMS = 3
NO_COST = pl.CostEstimate(flops=1, bytes_accessed=1, transcendentals=0)
COL = ("chip", "core")


def finish(mixed, gain, shift, valid_rows):
    active = jax.nn.gelu(mixed, approximate=False)
    centered = active - jnp.mean(active, axis=-1, keepdims=True)
    variance = jnp.mean(centered * centered, axis=-1, keepdims=True)
    return (centered * lax.rsqrt(variance + 1e-05) * gain + shift) * valid_rows[:, None]


def forward_product(adjacency, piece_low):
    partial_value = jnp.dot(
        adjacency,
        lax.all_gather(piece_low, "row", axis=0, tiled=True),
        preferred_element_type=jnp.float32,
    )
    return lax.psum_scatter(partial_value, COL, scatter_dimension=0, tiled=True)


def backward_product(adjacency, piece_low):
    partial_value = lax.dot_general(
        adjacency,
        lax.all_gather(piece_low, COL, axis=0, tiled=True),
        (((0,), (0,)), ((), ())),
        preferred_element_type=jnp.float32,
    )
    return lax.psum_scatter(
        partial_value.astype(jnp.bfloat16), "row", scatter_dimension=0, tiled=True
    ).astype(jnp.float32)


def layer_forward(adjacency, inputs, weight, bias, gain, shift, valid_rows):
    first_low = inputs.astype(jnp.bfloat16)
    second = -forward_product(adjacency, first_low)
    second_low = second.astype(jnp.bfloat16)

    def advance(state_pair, unused):
        previous, current, current_low = state_pair
        upcoming = -2.0 * forward_product(adjacency, current_low) - previous
        upcoming_low = upcoming.astype(jnp.bfloat16)
        return ((current, upcoming, upcoming_low), upcoming_low)

    ignored, others = lax.scan(advance, (inputs, second, second_low), None, length=ORDER - 2)
    stacked = jnp.concatenate([first_low[None], second_low[None], others], axis=0)
    mixed = jnp.einsum("kni,kio->no", stacked, weight, preferred_element_type=jnp.float32) + bias
    return (stacked, mixed, finish(mixed, gain, shift, valid_rows))


def layer_backward(adjacency, stacked, mixed, upstream, weight, gain, shift, valid_rows):

    def local_finish(mixed_in, gain_in, shift_in):
        return finish(mixed_in, gain_in, shift_in, valid_rows)

    ignored, pullback = jax.vjp(local_finish, mixed, gain, shift)
    mixed_grad, gain_grad, shift_grad = pullback(upstream)
    mixed_low = mixed_grad.astype(jnp.bfloat16)
    bias_grad = jnp.sum(mixed_low.astype(jnp.float32), axis=0)
    weight_grad = jnp.einsum("kni,no->kio", stacked, mixed_low, preferred_element_type=jnp.float32)
    direct = jnp.einsum("no,kio->kni", mixed_low, weight, preferred_element_type=jnp.float32)

    def retreat(state_pair, direct_term):
        later_two, later_one = state_pair
        current = (
            direct_term
            - 2.0 * backward_product(adjacency, later_one.astype(jnp.bfloat16))
            - later_two
        )
        return ((later_one, current), None)

    start_pair = (jnp.zeros_like(direct[0]), direct[ORDER - 1])
    (second_grad, first_grad), unused = lax.scan(
        retreat, start_pair, direct[1 : ORDER - 1], reverse=True
    )
    input_grad = (
        direct[0] - backward_product(adjacency, first_grad.astype(jnp.bfloat16)) - second_grad
    )
    return (input_grad, weight_grad, bias_grad, gain_grad, shift_grad)


def swap(value, axis):
    return lax.ppermute(value, axis, [(0, 1), (1, 0)])


def trade(pieces, axis):
    return lax.all_to_all(pieces, axis, 0, 0, tiled=False)


def broadcast_along(value, axis, size):
    return trade(jnp.broadcast_to(value[None], (size,) + value.shape), axis)


def joined(mine, other, mine_first):
    return jnp.where(
        mine_first, jnp.concatenate([mine, other]), jnp.concatenate([other, mine])
    )


def added(mine, received):
    return (mine.astype(jnp.float32) + received.astype(jnp.float32)).astype(jnp.bfloat16)


def assemble(place_ref, own_ref, sibling_ref, near_ref, far_ref, out_ref, done):
    chip, core = place_ref[0], place_ref[1]
    own_cap, span = own_ref.shape
    half = span // 2

    def rows(of_chip, of_core):
        return pl.ds(pl.multiple_of((2 * of_chip + of_core) * own_cap, own_cap), own_cap)

    def fetch(source, of_chip, of_core, columns, place):
        target = out_ref.at[rows(of_chip, of_core), columns]
        return pltpu.make_async_copy(source, target, done.at[place])

    def quadrant_copies(here):
        there = 1 - here
        columns = pl.ds(there * half, half)
        return (
            fetch(near_ref, there, core, columns, 2),
            fetch(far_ref, there, 1 - core, columns, 3),
        )

    everything = pl.ds(0, span)
    top = (
        fetch(own_ref, chip, core, everything, 0),
        fetch(sibling_ref, chip, 1 - core, everything, 1),
    )

    def of_chip(here):
        there = 1 - here
        copies = top + quadrant_copies(here)
        for copy in copies:
            copy.start()
        for copy in copies:
            copy.wait()
        here_rows = pl.ds(here * half, half)
        for tile in range(half // 128):
            columns = pl.ds(there * half + tile * 128, 128)
            strip = out_ref[here_rows, columns]
            turned = jnp.transpose(strip.astype(jnp.float32)).astype(jnp.bfloat16)
            out_ref[columns, here_rows] = turned

    @pl.when(chip == 0)
    def first():
        of_chip(0)

    @pl.when(chip == 1)
    def second():
        of_chip(1)

    across = jnp.ones((1, span), jnp.float32)
    for tile in range(span // 128):
        across = across + jnp.sum(
            out_ref[pl.ds(tile * 128, 128), :].astype(jnp.float32), axis=0, keepdims=True
        )
    across = lax.rsqrt(across)
    for tile in range(span // 128):
        strip = out_ref[pl.ds(tile * 128, 128), :].astype(jnp.float32)
        down = lax.rsqrt(1.0 + jnp.sum(strip, axis=1, keepdims=True))
        out_ref[pl.ds(tile * 128, 128), :] = (strip * down * across).astype(jnp.bfloat16)


def normalized_block(own, sibling, near, far, place):
    span = own.shape[1]
    return pl.pallas_call(
        assemble,
        out_shape=jax.ShapeDtypeStruct((span, span), jnp.bfloat16),
        in_specs=[pl.BlockSpec(memory_space=pltpu.SMEM)]
        + [pl.BlockSpec(memory_space=pltpu.HBM)] * 4,
        out_specs=pl.BlockSpec(memory_space=pltpu.VMEM),
        scratch_shapes=[pltpu.SemaphoreType.DMA((4,))],
        compiler_params=pltpu.CompilerParams(vmem_limit_bytes=VMEM_BYTES),
        cost_estimate=NO_COST,
        name="normalized_block",
    )(place, own, sibling, near, far)


def pack_kernel(
    keep_ref, row_codes_ref, col_codes_ref, row_keys_ref, col_keys_ref, weight_ref, out_ref,
    masked, picked, rows_hot, cols_hot
):
    tile_rows, tile_cols = weight_ref.shape
    blocks_down, blocks_across = keep_ref.shape
    groups, ignored, lanes = out_ref.shape
    send_cap, own_cap = rows_hot.shape[0] // groups, cols_hot.shape[0] // groups
    high, wide = tile_rows // blocks_down, tile_cols // blocks_across
    for down in range(blocks_down):
        for across in range(blocks_across):
            rows, columns = pl.ds(down * high, high), pl.ds(across * wide, wide)
            own, other = row_codes_ref[rows, :], col_codes_ref[:, columns]
            linked = (own == other) & (own % 2 == 1) & (keep_ref[down, across] == 1)
            weight = weight_ref[rows, columns].astype(jnp.float32)
            masked[rows, columns] = jnp.where(linked, weight, 0.0).astype(jnp.bfloat16)

    def one_hot(keys, start, count):
        standing = lax.broadcasted_iota(jnp.int32, (count, keys.shape[1]), 0) + start
        return jnp.where(standing == keys, 1.0, 0.0).astype(jnp.bfloat16)

    for group in range(groups):
        rows_hot[pl.ds(group * send_cap, send_cap), :] = one_hot(
            row_keys_ref[...], group * send_cap, send_cap
        )
        cols_hot[pl.ds(group * own_cap, own_cap), :] = one_hot(
            col_keys_ref[...], group * own_cap, own_cap
        )
    for tile in range(tile_cols // 256):
        columns = pl.ds(tile * 256, 256)
        picked[:, columns] = jnp.dot(
            rows_hot[...], masked[:, columns], preferred_element_type=jnp.float32
        ).astype(jnp.bfloat16)
    whole, half = own_cap // lanes, send_cap // 2
    for group in range(groups):
        packed = lax.dot_general(
            cols_hot[pl.ds(group * own_cap, own_cap), :],
            picked[pl.ds(group * send_cap, send_cap), :],
            (((1,), (1,)), ((), ())),
            preferred_element_type=jnp.float32,
        ).T
        for tile in range(whole):
            out_ref[group, pl.ds(tile * send_cap, send_cap), :] = packed[
                :, tile * lanes : (tile + 1) * lanes
            ].astype(jnp.bfloat16)
        ends = jnp.concatenate(
            [packed[:half, whole * lanes :], packed[half:, whole * lanes :]], axis=1
        )
        out_ref[group, pl.ds(whole * send_cap, half), :] = ends.astype(jnp.bfloat16)


def packed_pieces(block_keep, row_codes, col_codes, row_keys, col_keys, edge_weight, caps, groups):
    own_cap, send_cap = caps
    tile_rows, tile_cols = edge_weight.shape
    high = own_cap // 128 * send_cap + send_cap // 2
    vector = pl.BlockSpec(memory_space=pltpu.VMEM)
    return pl.pallas_call(
        pack_kernel,
        out_shape=jax.ShapeDtypeStruct((groups, high, 128), jnp.bfloat16),
        in_specs=[pl.BlockSpec(memory_space=pltpu.SMEM)] + [vector] * 5,
        out_specs=vector,
        scratch_shapes=[
            pltpu.VMEM((tile_rows, tile_cols), jnp.bfloat16),
            pltpu.VMEM((groups * send_cap, tile_cols), jnp.bfloat16),
            pltpu.VMEM((groups * send_cap, tile_rows), jnp.bfloat16),
            pltpu.VMEM((groups * own_cap, tile_cols), jnp.bfloat16),
        ],
        compiler_params=pltpu.CompilerParams(vmem_limit_bytes=VMEM_BYTES),
        cost_estimate=NO_COST,
        name="packed_pieces",
    )(block_keep, row_codes[:, None], col_codes[None], row_keys[None], col_keys[None], edge_weight)


def normal_share(mixed):
    return 0.5 * (1.0 + lax.erf(mixed * 0.5**0.5))


def norm_forward(mixed):
    active = mixed * normal_share(mixed)
    centered = active - jnp.mean(active, axis=-1, keepdims=True)
    scale = lax.rsqrt(jnp.mean(centered * centered, axis=-1, keepdims=True) + 1e-05)
    return centered * scale, scale


def norm_backward(mixed, upstream, gain, valid):
    normed, scale = norm_forward(mixed)
    upstream = upstream * valid
    inner = upstream * gain
    inner = inner - jnp.mean(inner, axis=-1, keepdims=True) - normed * jnp.mean(
        inner * normed, axis=-1, keepdims=True
    )
    density = jnp.exp(-0.5 * mixed * mixed) * (1.0 / (2.0 * math.pi) ** 0.5)
    low = (inner * scale * (normal_share(mixed) + mixed * density)).astype(jnp.bfloat16)
    rest = [low.astype(jnp.float32), upstream * normed, upstream]
    return low, [jnp.sum(value, axis=0, keepdims=True) for value in rest]


def weight_gradient(turned_ref, low, core, mine_ref, other_ref):
    part = turned_ref.shape[0] // 4

    def halves(first_ref, second_ref):
        for place in range(4):
            out_ref = second_ref if place % 2 else first_ref
            out_ref[place // 2, :part, :] = jnp.dot(
                turned_ref[place * part : (place + 1) * part, :],
                low,
                preferred_element_type=jnp.float32,
            ).astype(jnp.bfloat16)

    @pl.when(core == 0)
    def low_half_first():
        halves(mine_ref, other_ref)

    @pl.when(core == 1)
    def high_half_first():
        halves(other_ref, mine_ref)


def forward_step(step, powers_ref, all_ref, own_ref, weights, bias_ref, turned, mixed):
    terms, own_cap, span = powers_ref.shape
    fan_in = own_ref.shape[1]

    @pl.when(step == 0)
    def first():
        turned[:fan_in, :] = own_ref[...].T
        mixed[...] = bias_ref[...] + jnp.dot(
            own_ref[...], weights[0][0], preferred_element_type=jnp.float32
        )

    low = jnp.dot(
        powers_ref[...].reshape(terms * own_cap, span),
        all_ref[...],
        preferred_element_type=jnp.float32,
    ).astype(jnp.bfloat16)
    total = mixed[...]
    for term in range(terms):
        part = low[term * own_cap : (term + 1) * own_cap]
        start = pl.multiple_of((1 + step * terms + term) * fan_in, fan_in)
        turned[pl.ds(start, fan_in), :] = part.T
        total = total + jnp.dot(part, weights[1 + term][0], preferred_element_type=jnp.float32)
    mixed[...] = total


def layer_one_kernel(
    powers_ref,
    all_ref,
    own_ref,
    weight_0,
    weight_a,
    weight_b,
    weight_c,
    bias_ref,
    gain_ref,
    shift_ref,
    valid_ref,
    hidden_ref,
    turned_ref,
    mixed_ref,
):
    step = pl.program_id(0)
    weights = (weight_0, weight_a, weight_b, weight_c)
    forward_step(step, powers_ref, all_ref, own_ref, weights, bias_ref, turned_ref, mixed_ref)

    @pl.when(step == pl.num_programs(0) - 1)
    def finish_layer():
        normed, ignored = norm_forward(mixed_ref[...])
        hidden = (normed * gain_ref[...] + shift_ref[...]) * valid_ref[...]
        hidden_ref[...] = hidden.astype(jnp.bfloat16)


def layer_two_kernel(
    place_ref,
    powers_ref,
    all_ref,
    own_ref,
    weight_0,
    weight_a,
    weight_b,
    weight_c,
    bias_ref,
    gain_ref,
    shift_ref,
    valid_ref,
    upstream_ref,
    active_ref,
    low_ref,
    rest_ref,
    mine_ref,
    other_ref,
    turned,
    mixed,
):
    step = pl.program_id(0)
    weights = (weight_0, weight_a, weight_b, weight_c)
    forward_step(step, powers_ref, all_ref, own_ref, weights, bias_ref, turned, mixed)

    @pl.when(step == pl.num_programs(0) - 1)
    def finish_layer():
        normed, ignored = norm_forward(mixed[...])
        active = (normed * gain_ref[...] + shift_ref[...]) * valid_ref[...]
        active_ref[...] = active.astype(jnp.bfloat16)
        low, rest = norm_backward(
            mixed[...], upstream_ref[...].astype(jnp.float32), gain_ref[...], valid_ref[...]
        )
        low_ref[...] = low
        for place in range(3):
            rest_ref[place : place + 1, :] = rest[place]
        weight_gradient(turned, low, place_ref[1], mine_ref, other_ref)


def backward_step(step, powers_ref, all_ref, own_ref, weights, total):
    terms, own_cap, span = powers_ref.shape
    transposed = (((1,), (1,)), ((), ()))

    @pl.when(step == 0)
    def first():
        total[...] = lax.dot_general(
            own_ref[...], weights[0][0], transposed, preferred_element_type=jnp.float32
        )

    low = jnp.dot(
        powers_ref[...].reshape(terms * own_cap, span),
        all_ref[...],
        preferred_element_type=jnp.float32,
    ).astype(jnp.bfloat16)
    value = total[...]
    for term in range(terms):
        value = value + lax.dot_general(
            low[term * own_cap : (term + 1) * own_cap],
            weights[1 + term][0],
            transposed,
            preferred_element_type=jnp.float32,
        )
    total[...] = value


def back_two_kernel(
    place_ref,
    powers_ref,
    all_ref,
    own_ref,
    weight_0,
    weight_a,
    weight_b,
    weight_c,
    turned_ref,
    mixed_ref,
    gain_ref,
    valid_ref,
    rest_ref,
    low_ref,
    mine_ref,
    other_ref,
    total,
):
    step = pl.program_id(0)
    weights = (weight_0, weight_a, weight_b, weight_c)
    backward_step(step, powers_ref, all_ref, own_ref, weights, total)

    @pl.when(step == pl.num_programs(0) - 1)
    def finish_layer():
        low, rest = norm_backward(mixed_ref[...], total[...], gain_ref[...], valid_ref[...])
        low_ref[...] = low
        weight_gradient(turned_ref, low, place_ref[1], mine_ref, other_ref)
        part = turned_ref.shape[0] // 4
        extra = jnp.zeros((2, mine_ref.shape[1] - part, mine_ref.shape[2]), jnp.bfloat16)
        rows = rest + [rest_ref[place : place + 1, :] for place in range(3)]
        rows = jnp.concatenate(rows + [jnp.zeros((10, rows[0].shape[1]), jnp.float32)], axis=0)

        def below(first_ref, second_ref):
            first_ref[:, part:, :] = extra
            second_ref[:, part:, :] = extra
            first_ref[0, part : part + 16, :] = rows.astype(jnp.bfloat16)

        @pl.when(place_ref[1] == 0)
        def low_half_here():
            below(mine_ref, other_ref)

        @pl.when(place_ref[1] == 1)
        def low_half_there():
            below(other_ref, mine_ref)


def back_one_kernel(
    powers_ref, all_ref, own_ref, weight_0, weight_a, weight_b, weight_c, out_ref, total
):
    step = pl.program_id(0)
    weights = (weight_0, weight_a, weight_b, weight_c)
    backward_step(step, powers_ref, all_ref, own_ref, weights, total)

    @pl.when(step == pl.num_programs(0) - 1)
    def finish_layer():
        out_ref[...] = total[...].astype(jnp.bfloat16)


def layer_pass(kernel, name, place, powers, everyone, own, weight, others, outs, scratch):
    ignored, own_cap, span = powers.shape
    fan_in, width = weight.shape[1:]

    def whole(value):
        return pl.BlockSpec(value.shape, lambda step: (0,) * len(value.shape))

    def term_weight(term):
        return pl.BlockSpec((1, fan_in, width), lambda step: (1 + step * TERMS + term, 0, 0))

    in_specs = [
        pl.BlockSpec((TERMS, own_cap, span), lambda step: (step, 0, 0)),
        whole(everyone),
        whole(own),
        pl.BlockSpec((1, fan_in, width), lambda step: (0, 0, 0)),
    ]
    in_specs += [term_weight(term) for term in range(TERMS)] + [whole(value) for value in others]
    operands = [powers, everyone, own] + [weight] * (1 + TERMS) + list(others)
    if place is not None:
        in_specs = [pl.BlockSpec(memory_space=pltpu.SMEM)] + in_specs
        operands = [place] + operands
    return pl.pallas_call(
        kernel,
        grid=((ORDER - 1) // TERMS,),
        out_shape=outs,
        in_specs=in_specs,
        out_specs=[whole(value) for value in outs],
        scratch_shapes=[pltpu.VMEM(shape, dtype) for shape, dtype in scratch],
        compiler_params=pltpu.CompilerParams(vmem_limit_bytes=VMEM_BYTES),
        cost_estimate=NO_COST,
        name=name,
    )(*operands)


def finish_kernel(scalars_ref, *refs):
    step = pl.program_id(0)
    if len(refs) == 3:
        values_ref, other_ref, out_ref = refs
        parts = [(step >= 0, values_ref)]
        small_ref = None
    else:
        pair_ref, siblings_ref, other_ref, out_ref, small_ref = refs
        parts = [(step < 2, pair_ref), (step >= 2, siblings_ref)]
    part = out_ref.shape[1]
    for here, values_ref in parts:
        @pl.when(here & (scalars_ref[0] == 1))
        def fast_form():
            out_ref[0] = values_ref[0, :part, :].astype(jnp.float32)

        if small_ref is not None:
            @pl.when(here & (scalars_ref[1 + step] == 0))
            def small_sums():
                small_ref[...] = values_ref[0, part : part + 16, :].astype(jnp.float32)

    @pl.when(scalars_ref[0] == 0)
    def general_form():
        out_ref[0] = other_ref[0].astype(jnp.float32)


def finished(scalars, pair, values, other):
    count, part, width = other.shape
    one = (1, part, width)
    if pair is None:
        operands, outs = [values, other], [jax.ShapeDtypeStruct(other.shape, jnp.float32)]

        def quarter(step, scalars_ref):
            return step

        in_specs = [pl.BlockSpec((1,) + values.shape[1:], lambda step, ref: (step, 0, 0))]
        small_specs = []
    else:
        operands = [pair, values, other]
        outs = [
            jax.ShapeDtypeStruct(other.shape, jnp.float32),
            jax.ShapeDtypeStruct((16, width), jnp.float32),
        ]

        def quarter(step, scalars_ref):
            return scalars_ref[1 + step]

        in_specs = [
            pl.BlockSpec((1,) + pair.shape[1:], lambda step, ref: (jnp.minimum(step, 1), 0, 0)),
            pl.BlockSpec((1,) + pair.shape[1:], lambda step, ref: (jnp.maximum(step - 2, 0), 0, 0)),
        ]
        small_specs = [pl.BlockSpec((16, width), lambda step, ref: (0, 0))]
    in_specs.append(
        pl.BlockSpec(one, lambda step, ref: ((1 - ref[0]) * quarter(step, ref), 0, 0))
    )
    result = pl.pallas_call(
        finish_kernel,
        grid_spec=pltpu.PrefetchScalarGridSpec(
            num_scalar_prefetch=1,
            grid=(count,),
            in_specs=in_specs,
            out_specs=[pl.BlockSpec(one, lambda step, ref: (quarter(step, ref), 0, 0))]
            + small_specs,
        ),
        out_shape=outs,
        compiler_params=pltpu.CompilerParams(vmem_limit_bytes=VMEM_BYTES),
        cost_estimate=NO_COST,
        name="finished",
    )(scalars, *operands)
    return result[0] if pair is None else result


def unpack_kernel(place_ref, pieces_ref, keys_ref, own_ref, quadrant_ref, columns, hot):
    groups, high, lanes = pieces_ref.shape
    own_cap, span = own_ref.shape
    whole = own_cap // lanes
    send_cap = keys_ref.shape[1] // groups
    half, rest = send_cap // 2, own_cap - whole * lanes
    for group in range(groups):
        start = group * send_cap
        for tile in range(whole):
            columns[start : start + send_cap, tile * lanes : (tile + 1) * lanes] = pieces_ref[
                group, tile * send_cap : (tile + 1) * send_cap, :
            ]
        ends = pieces_ref[group, whole * send_cap :, :]
        columns[start : start + half, whole * lanes :] = ends[:, :rest]
        columns[start + half : start + send_cap, whole * lanes :] = ends[:, rest:]
    standing = lax.broadcasted_iota(jnp.int32, hot.shape, 0)
    hot[...] = jnp.where(standing == keys_ref[...], 1.0, 0.0).astype(jnp.bfloat16)
    block = jnp.dot(hot[...], columns[...], preferred_element_type=jnp.float32)
    own_ref[...] = block.T.astype(jnp.bfloat16)
    middle = span // 2

    @pl.when(place_ref[0] == 0)
    def first():
        quadrant_ref[...] = own_ref[:, :middle]

    @pl.when(place_ref[0] == 1)
    def second():
        quadrant_ref[...] = own_ref[:, middle:]


def unpacked_block(pieces, keys, place, own_cap, span):
    vector = pl.BlockSpec(memory_space=pltpu.VMEM)
    return pl.pallas_call(
        unpack_kernel,
        out_shape=[
            jax.ShapeDtypeStruct((own_cap, span), jnp.bfloat16),
            jax.ShapeDtypeStruct((own_cap, span // 2), jnp.bfloat16),
        ],
        in_specs=[pl.BlockSpec(memory_space=pltpu.SMEM), vector, vector],
        out_specs=[vector, vector],
        scratch_shapes=[
            pltpu.VMEM((keys.shape[1], own_cap), jnp.bfloat16),
            pltpu.VMEM((span, keys.shape[1]), jnp.bfloat16),
        ],
        compiler_params=pltpu.CompilerParams(vmem_limit_bytes=VMEM_BYTES),
        cost_estimate=NO_COST,
        name="unpacked_block",
    )(place, pieces, keys)


def fit_kernel(codes_ref, out_ref, *, n_row, caps):
    own_cap, send_cap, seat_cap = caps
    codes = codes_ref[...]
    devices = codes.shape[0]
    n_col = devices // n_row
    label = lax.broadcasted_iota(jnp.int32, (devices, 128), 1)
    counts = jnp.zeros((devices, 128), jnp.float32)
    for cluster in range(CLUSTERS):
        here = jnp.where(codes == 2 * cluster + 1, 1.0, 0.0)
        counts = counts + jnp.where(
            label == cluster, jnp.sum(here, axis=1, keepdims=True), 0.0
        )
    sizes = jnp.sum(counts, axis=0, keepdims=True)
    across = jnp.broadcast_to(sizes, (128, 128))
    down = across.T
    first = lax.broadcasted_iota(jnp.int32, (128, 128), 0)
    second = lax.broadcasted_iota(jnp.int32, (128, 128), 1)
    ahead = (across > down) | ((across == down) & (second < first))
    ahead = ahead & (second < CLUSTERS)
    rank = jnp.sum(jnp.where(ahead, 1.0, 0.0), axis=1, keepdims=True).astype(jnp.int32)
    others = n_row - 1
    later = rank > others
    turn = jnp.zeros_like(rank)
    for count in range(1, CLUSTERS // others + 1):
        turn = turn + jnp.where(rank - 1 >= count * others, 1, 0)
    place = rank - 1 - turn * others
    group = jnp.where(rank == 0, 0, 1 + jnp.where(later, others - 1 - place, place))
    member = (group == second) & (first < CLUSTERS)
    held = jnp.dot(
        counts.astype(jnp.bfloat16),
        jnp.where(member, 1.0, 0.0).astype(jnp.bfloat16),
        preferred_element_type=jnp.float32,
    )
    by_row = jnp.zeros((1, 128), jnp.float32)
    for row in range(n_row):
        rows = jnp.sum(held[row * n_col : (row + 1) * n_col], axis=0, keepdims=True)
        by_row = jnp.maximum(by_row, rows)
    device = lax.broadcasted_iota(jnp.int32, (devices, 128), 0)
    by_col = jnp.zeros((1, 128), jnp.float32)
    for col in range(n_col):
        cols = jnp.where(device % n_col == col, held, 0.0)
        by_col = jnp.maximum(by_col, jnp.sum(cols, axis=0, keepdims=True))
    fits = (
        (jnp.max(by_col) <= own_cap) & (jnp.max(by_row) <= send_cap) & (jnp.max(held) <= seat_cap)
    )
    out_ref[0] = jnp.where(fits, 1, 0)


def fits_in(codes, n_row, caps):
    fits = pl.pallas_call(
        functools.partial(fit_kernel, n_row=n_row, caps=caps),
        out_shape=jax.ShapeDtypeStruct((1,), jnp.int32),
        in_specs=[pl.BlockSpec(memory_space=pltpu.VMEM)],
        out_specs=pl.BlockSpec(memory_space=pltpu.SMEM),
        cost_estimate=NO_COST,
        name="fits",
    )(codes.reshape(-1, codes.shape[-1]))
    return fits


def exclusive_counts(member):
    count = member.shape[-1]
    before = jnp.arange(count)[:, None] < jnp.arange(count)[None, :]
    return jnp.dot(
        member.astype(jnp.bfloat16),
        before.astype(jnp.bfloat16),
        preferred_element_type=jnp.float32,
    ).astype(jnp.int32)


def assign(codes, n_row):
    cluster, valid = codes >> 1, codes & 1
    labels = jnp.arange(CLUSTERS)
    sizes = jnp.sum(
        (cluster.reshape(1, -1) == labels[:, None]) & (valid.reshape(1, -1) == 1), axis=1
    )
    ahead = (sizes[None, :] > sizes[:, None]) | (
        (sizes[None, :] == sizes[:, None]) & (labels[None, :] < labels[:, None])
    )
    rank = jnp.sum(ahead, axis=1)
    others = n_row - 1
    turn, place = (rank - 1) // others, (rank - 1) % others
    group = jnp.where(rank == 0, 0, 1 + jnp.where(turn == 0, place, others - 1 - place))
    of_node = jnp.sum(
        jnp.where(cluster[None] == labels[:, None, None, None], group[:, None, None, None], 0),
        axis=0,
    )
    return jnp.where(valid == 1, of_node, n_row)


def compact(
    codes,
    group,
    features,
    block_keep,
    edge_weight,
    weight_one,
    bias_one,
    gain_one,
    shift_one,
    weight_two,
    bias_two,
    gain_two,
    shift_two,
    cotangent,
    places_of,
    slots_of,
    seats_of,
    decide,
    sizes,
    caps,
):
    row, col = lax.axis_index("row"), lax.axis_index(COL)
    chip, core = lax.axis_index("chip"), lax.axis_index("core")
    n_row, n_col = sizes
    own_cap, send_cap, seat_cap = caps
    own_nodes, in_width = features.shape
    width = weight_two.shape[2]
    span = n_col * own_cap
    targets = jnp.arange(n_row)

    def in_col(value):
        return lax.dynamic_index_in_dim(value, col, 1, False).reshape(-1)

    def in_row(value):
        return lax.dynamic_index_in_dim(value, row, 0, False).reshape(-1)

    row_group, col_group = in_row(group), in_col(group)
    row_slots, col_places = in_row(slots_of(group)), in_col(places_of(group))
    row_keys = jnp.where(row_slots < send_cap, row_group * send_cap + row_slots, -1)
    col_keys = jnp.where(col_places < own_cap, col_group * own_cap + col_places, -1)
    pieces = packed_pieces(
        block_keep,
        in_row(codes),
        in_col(codes),
        row_keys,
        col_keys,
        edge_weight,
        (own_cap, send_cap),
        n_row,
    )
    pieces, codes = lax.optimization_barrier((pieces, codes))
    group = assign(codes, n_row)
    pieces = trade(pieces, "row")
    fits, others = decide(codes)
    places, slots, seats = places_of(group), slots_of(group), seats_of(group)

    standing = jnp.arange(n_col)[None, :, None] * own_cap + places
    fits_here = jnp.where(group == row, standing, -1).reshape(n_row, -1)
    slot_of = slots.reshape(n_row, -1)
    target = jnp.max(
        jnp.where(
            slot_of[:, None, :] == jnp.arange(send_cap)[None, :, None], fits_here[:, None, :], -1
        ),
        axis=2,
    )
    keys = target.reshape(1, -1)

    def to_partner(value, step):
        return lax.ppermute(value, "row", [(place, place ^ step) for place in range(n_row)])

    partners = row ^ targets
    group_here = lax.dynamic_index_in_dim(in_row(group).reshape(n_col, -1), col, 0, False)
    seat_here = lax.dynamic_index_in_dim(in_row(seats).reshape(n_col, -1), col, 0, False)

    def seat_of_node(groups):
        hot = (group_here[None, None, :] == groups[:, None, None]) & (
            seat_here[None, None, :] == jnp.arange(seat_cap)[None, :, None]
        )
        return hot.astype(jnp.bfloat16).reshape(n_row * seat_cap, own_nodes)

    enter_partner = seat_of_node(partners)
    both = jnp.dot(enter_partner, jnp.concatenate([features, cotangent], axis=1))
    both = both.reshape(n_row, seat_cap, -1)
    enter_partner = enter_partner.T
    enter_home = seat_of_node(targets).T
    group_col = lax.dynamic_index_in_dim(group, col, 1, False)
    seats_col = lax.dynamic_index_in_dim(seats, col, 1, False)
    places_col = lax.dynamic_index_in_dim(places, col, 1, False)
    seated = (group_col == row)[:, None, :] & (
        seats_col[:, None, :] == jnp.arange(seat_cap)[None, :, None]
    )
    place_of_seat = jnp.max(jnp.where(seated, places_col[:, None, :], -1), axis=2)
    from_partner = jnp.max(
        jnp.where((partners[:, None] == targets)[:, :, None], place_of_seat[None], -1), axis=1
    )
    arrive = from_partner.reshape(1, -1) == jnp.arange(own_cap)[:, None]
    arrive = arrive.astype(jnp.bfloat16)
    leave_partner = jnp.concatenate([from_partner[::2], from_partner[1::2]])
    leave_partner = leave_partner.reshape(-1, 1) == jnp.arange(own_cap)
    leave_partner = leave_partner.astype(jnp.bfloat16)
    leave_group = place_of_seat.reshape(-1, 1) == jnp.arange(own_cap)[None, :]
    leave_group = leave_group.astype(jnp.bfloat16)
    held_count = jnp.sum(group_col == row)
    valid_rows = (jnp.arange(own_cap) < held_count).astype(jnp.float32)[:, None]
    place = jnp.stack([chip, core]).astype(jnp.int32)
    quarters = jnp.stack([col, (1 - chip) * 2 + core, chip * 2 + 1 - core, 3 - col])
    quarters = jnp.concatenate([fits, quarters.astype(jnp.int32)])
    scalars = (chip, 1 - chip, col * own_cap)
    scalars = tuple(value.astype(jnp.uint32) for value in scalars) + (chip == 0, core == 0, place, quarters)
    homes = enter_home, enter_partner, leave_group, leave_partner
    pieces, both, keys, arrive, homes, valid_rows, others, scalars = lax.optimization_barrier(
        (pieces, both, keys, arrive, homes, valid_rows, others, scalars)
    )
    enter_home, enter_partner, leave_group, leave_partner = homes
    this_chip, other_chip, own_start, first_chip, first_core, place, quarters = scalars

    own_block, quadrant = unpacked_block(pieces, keys, place, own_cap, span)
    quadrant = swap(quadrant, "chip")
    both = [both[0]] + [to_partner(both[step], step) for step in range(1, n_row)]
    sibling = swap(own_block, "core")
    quadrant, *early = lax.optimization_barrier((quadrant, *both[:-2]))
    adjacency = normalized_block(own_block, sibling, quadrant, swap(quadrant, "core"), place)
    adjacency, *late = lax.optimization_barrier((adjacency, *both[-2:]))
    both = early + late
    mine = jnp.dot(arrive, jnp.concatenate(both))
    features_own, cotangent_own = mine[:, :in_width], mine[:, in_width:]
    sibling = swap(features_own, "core")

    first = (own_start + jnp.arange(own_cap, dtype=jnp.uint32))[:, None]
    first = first == jnp.arange(span, dtype=jnp.uint32)[None, :]
    previous = first.astype(jnp.float32)
    current = -lax.dynamic_slice_in_dim(adjacency, own_start, own_cap, 0).astype(jnp.float32)
    lowered = [current.astype(jnp.bfloat16)]
    for position in range(2, ORDER):
        upcoming = (
            -2.0 * jnp.dot(lowered[-1], adjacency, preferred_element_type=jnp.float32) - previous
        )
        low = upcoming.astype(jnp.bfloat16)
        if position == 4:
            low, sibling = lax.optimization_barrier((low, sibling))
            features_chip = joined(features_own, sibling, first_core)
            partner = swap(features_chip, "chip")
        if position == 8:
            low, partner = lax.optimization_barrier((low, partner))
            features_all = joined(features_chip, partner, first_chip)
        previous, current = current, upcoming
        lowered.append(low)
    powers = jnp.concatenate(lowered, axis=0).reshape(ORDER - 1, own_cap, span)

    def everywhere(value_low):
        return lax.all_gather(value_low, COL, axis=0, tiled=True)

    def chosen(value, other):
        return jnp.where(quarters[0] == 1, value.astype(jnp.float32), other.astype(jnp.float32))

    def shaped(*shape, dtype=jnp.bfloat16):
        return jax.ShapeDtypeStruct(shape, dtype)

    part_one, part_two = ORDER * in_width // n_col, ORDER * width // n_col
    padded = -(-(part_one + 16) // (8 * n_row)) * (8 * n_row)
    hidden, turned_one, mixed_one = layer_pass(
        layer_one_kernel,
        "layer_one",
        None,
        powers,
        features_all,
        features_own,
        weight_one,
        [bias_one[None], gain_one[None], shift_one[None], valid_rows],
        [
            shaped(own_cap, width),
            shaped(n_col * part_one, own_cap),
            shaped(own_cap, width, dtype=jnp.float32),
        ],
        [],
    )
    activations, low_two, rest_two, mine, other = layer_pass(
        layer_two_kernel,
        "layer_two",
        place,
        powers,
        everywhere(hidden),
        hidden,
        weight_two,
        [bias_two[None], gain_two[None], shift_two[None], valid_rows, cotangent_own],
        [
            shaped(own_cap, width),
            shaped(own_cap, width),
            shaped(3, width, dtype=jnp.float32),
            shaped(2, part_two, width),
            shaped(2, part_two, width),
        ],
        [((n_col * part_two, own_cap), jnp.bfloat16), ((own_cap, width), jnp.float32)],
    )

    def add_cores(mine, other):
        got = swap(other, "core")
        return tuple(
            added(
                lax.dynamic_index_in_dim(mine, index, 0, False),
                lax.dynamic_index_in_dim(got, index, 0, False),
            )
            for index in (this_chip, other_chip)
        )

    leaving = jnp.dot(leave_partner, activations).reshape(n_row, seat_cap, width)
    near, far = leaving[: n_row // 2], leaving[n_row // 2 :]
    far = to_partner(far, 1)
    here, there = add_cores(mine, other)
    everyone_two, there, far = lax.optimization_barrier((everywhere(low_two), there, far))
    there = swap(there, "chip")
    arrived = [jnp.stack([near[0], far[0]])] + [
        to_partner(jnp.stack([near[half], far[half]]), 2 * half) for half in range(1, n_row // 2)
    ]
    low_one, mine, other = layer_pass(
        back_two_kernel,
        "back_two",
        place,
        powers,
        everyone_two,
        low_two,
        weight_two,
        [turned_one, mixed_one, gain_one[None], valid_rows, rest_two],
        [shaped(own_cap, width), shaped(2, padded, width), shaped(2, padded, width)],
        [((own_cap, width), jnp.float32)],
    )
    low_one, there, arrived = lax.optimization_barrier((low_one, there, arrived))
    second = added(here, there).reshape(n_row, -1, width)
    many = second.shape[1]
    low_one, second = lax.optimization_barrier((low_one, second))
    second = trade(second, "row")
    here, there = add_cores(mine, other)
    low_one, there = lax.optimization_barrier((low_one, there))
    everyone_one = everywhere(low_one)
    there = swap(there, "chip")
    everyone_one, second, there = lax.optimization_barrier((everyone_one, second, there))
    first = added(here, there).reshape(n_row, -1, width)
    share = first.shape[1]
    second = jnp.sum(second.astype(jnp.float32), axis=0).astype(jnp.bfloat16)
    second = jnp.broadcast_to(second[None], (n_row,) + second.shape)
    mixed = jnp.concatenate([second, first], axis=1)
    everyone_one, mixed = lax.optimization_barrier((everyone_one, mixed))
    mixed = trade(mixed, "row")
    (input_grad,) = layer_pass(
        back_one_kernel,
        "back_one",
        None,
        powers,
        everyone_one,
        low_one,
        weight_one,
        [],
        [shaped(own_cap, in_width)],
        [((own_cap, in_width), jnp.float32)],
    )
    leaving = jnp.dot(leave_group, input_grad).reshape(n_row, seat_cap * in_width // width, width)
    arrived = jnp.concatenate(arrived).reshape(-1, width)
    home = jnp.dot(enter_partner, arrived, preferred_element_type=jnp.float32)
    home = chosen(home, others[0])
    mixed, leaving, home = lax.optimization_barrier((mixed, leaving, home))
    first = jnp.sum(mixed[:, many:].astype(jnp.float32), axis=0).astype(jnp.bfloat16)
    first = jnp.broadcast_to(first[None], (n_row,) + first.shape)
    first, mixed = lax.optimization_barrier((jnp.concatenate([first, leaving], axis=1), mixed))
    first = trade(first, "row")
    second = lax.all_gather(mixed[:, :many].reshape(-1, width), COL, axis=0)
    back = first[:, share:].reshape(n_row * seat_cap, in_width)
    mine = first[:, :share].reshape(1, -1, width)
    partner = swap(mine, "chip")
    second = finished(quarters[:1], None, second, others[3])
    home_grad = jnp.dot(enter_home, back, preferred_element_type=jnp.float32)
    home_grad = chosen(home_grad, others[1])
    partner, second, home_grad = lax.optimization_barrier((partner, second, home_grad))
    pair = jnp.concatenate([mine, partner])
    siblings = swap(pair, "core")
    first, small = finished(quarters, pair, siblings, others[2])
    return home, home_grad, first, second, chosen(small[:6], others[4])


def general(
    codes,
    features,
    block_keep,
    edge_weight,
    weight_one,
    bias_one,
    gain_one,
    shift_one,
    weight_two,
    bias_two,
    gain_two,
    shift_two,
    cotangent,
    node_valid,
):
    row, col = lax.axis_index("row"), lax.axis_index(COL)
    row_codes = lax.dynamic_index_in_dim(codes, row, 0, False).reshape(-1)
    col_codes = lax.dynamic_index_in_dim(codes, col, 1, False).reshape(-1)
    tile_rows, tile_cols = edge_weight.shape
    blocks_down, blocks_across = block_keep.shape
    block_side = tile_rows // blocks_down
    linked = (row_codes[:, None] == col_codes[None, :]) & (row_codes[:, None] & 1 == 1)
    linked = linked.reshape(blocks_down, block_side, blocks_across, block_side) & (
        block_keep[:, None, :, None] == 1
    )
    masked = edge_weight * linked.reshape(tile_rows, tile_cols).astype(jnp.bfloat16)
    degree_rows = 1.0 + lax.psum(jnp.sum(masked, axis=1, dtype=jnp.float32), COL)
    own_nodes = features.shape[0]
    own_degree = lax.dynamic_slice_in_dim(
        degree_rows, lax.axis_index(COL) * own_nodes, own_nodes, 0
    )
    degree_cols = lax.all_gather(own_degree, "row", axis=0, tiled=True)
    adjacency = (
        masked.astype(jnp.float32)
        * lax.rsqrt(degree_rows)[:, None]
        * lax.rsqrt(degree_cols)[None, :]
    ).astype(jnp.bfloat16)
    valid_rows = node_valid.astype(jnp.float32)
    stacked_one, mixed_one, hidden = layer_forward(
        adjacency,
        features.astype(jnp.float32),
        weight_one,
        bias_one,
        gain_one,
        shift_one,
        valid_rows,
    )
    stacked_two, mixed_two, activations = layer_forward(
        adjacency, hidden, weight_two, bias_two, gain_two, shift_two, valid_rows
    )
    hidden_grad, weight_two_grad, bias_two_grad, gain_two_grad, shift_two_grad = layer_backward(
        adjacency,
        stacked_two,
        mixed_two,
        cotangent.astype(jnp.float32),
        weight_two,
        gain_two,
        shift_two,
        valid_rows,
    )
    input_grad, weight_one_grad, bias_one_grad, gain_one_grad, shift_one_grad = layer_backward(
        adjacency, stacked_one, mixed_one, hidden_grad, weight_one, gain_one, shift_one, valid_rows
    )
    summed = lax.psum(
        (
            weight_one_grad,
            bias_one_grad,
            gain_one_grad,
            shift_one_grad,
            weight_two_grad,
            bias_two_grad,
            gain_two_grad,
            shift_two_grad,
        ),
        ("row",) + COL,
    )
    weight_one_grad, bias_one_grad, gain_one_grad, shift_one_grad = (
        summed[0],
        summed[1],
        summed[2],
        summed[3],
    )
    weight_two_grad, bias_two_grad, gain_two_grad, shift_two_grad = (
        summed[4],
        summed[5],
        summed[6],
        summed[7],
    )
    return (
        activations,
        input_grad,
        weight_one_grad,
        bias_one_grad,
        gain_one_grad,
        shift_one_grad,
        weight_two_grad,
        bias_two_grad,
        gain_two_grad,
        shift_two_grad,
    )


def local(n_row, n_col, *args):
    (
        features,
        node_valid,
        cluster,
        block_keep,
        edge_weight,
        weight_one,
        bias_one,
        gain_one,
        shift_one,
        weight_two,
        bias_two,
        gain_two,
        shift_two,
        cotangent,
    ) = args
    own_nodes, in_width = features.shape
    own_cap = own_nodes * n_row * 5 // 16
    send_cap = own_nodes * n_col * 11 // 32
    seat_cap = own_nodes // 2
    codes = broadcast_along(cluster * 2 + node_valid, ("row",) + COL, n_row * n_col)
    codes = codes.reshape(n_row, n_col, own_nodes)
    shared = (
        block_keep,
        edge_weight,
        weight_one,
        bias_one,
        gain_one,
        shift_one,
        weight_two,
        bias_two,
        gain_two,
        shift_two,
        cotangent,
    )

    def slow():
        return general(codes, features, *shared, node_valid)

    held = (ORDER - 1) * own_cap * own_cap * n_col * 2
    if held > HELD_BYTES or n_col != 4 or n_row < 2 or n_row & (n_row - 1):
        return slow()
    group = assign(codes, n_row)

    def member_of(group):
        return group[None] == jnp.arange(n_row)[:, None, None, None]

    def places_of(group):
        member = member_of(group).transpose(0, 2, 1, 3).reshape(n_row, n_col, -1)
        places = jnp.sum(jnp.where(member, exclusive_counts(member), 0), axis=0)
        return places.reshape(n_col, n_row, own_nodes).transpose(1, 0, 2)

    def slots_of(group):
        member = member_of(group).reshape(n_row, n_row, -1)
        slots = jnp.sum(jnp.where(member, exclusive_counts(member), 0), axis=0)
        return slots.reshape(n_row, n_col, own_nodes)

    def seats_of(group):
        member = member_of(group)
        return jnp.sum(jnp.where(member, exclusive_counts(member), 0), axis=0)

    width = weight_two.shape[2]

    def instead(state):
        made = slow()
        small = jnp.stack([made[place] for place in (3, 4, 5, 7, 8, 9)])
        return (jnp.ones_like(state[0]),) + tuple(
            value.astype(jnp.bfloat16).reshape(like.shape)
            for value, like in zip((made[0], made[1], made[2], made[6], small), state[1:])
        )

    shapes = (
        (own_nodes, width),
        (own_nodes, in_width),
        (n_col, ORDER * in_width // n_col, width),
        (n_col, ORDER * width // n_col, width),
        (6, width),
    )

    def decide(codes):
        fits = fits_in(codes, n_row, (own_cap, send_cap, seat_cap))
        others = lax.while_loop(
            lambda state: state[0][0] == 0,
            instead,
            (fits,) + tuple(jnp.zeros(shape, jnp.bfloat16) for shape in shapes),
        )[1:]
        return fits, others

    home, home_grad, first, second, small = compact(
        codes,
        group,
        features,
        *shared,
        places_of,
        slots_of,
        seats_of,
        decide,
        (n_row, n_col),
        (own_cap, send_cap, seat_cap),
    )
    return (
        home,
        home_grad,
        first.reshape(weight_one.shape),
        small[0],
        small[1],
        small[2],
        second.reshape(weight_two.shape),
        small[3],
        small[4],
        small[5],
    )


def solution(mesh):
    n_row, n_col = mesh.shape["row"], mesh.shape["col"]
    by_core = jax.sharding.Mesh(
        mesh.devices.reshape(n_row, n_col // 2, 2), ("row", "chip", "core")
    )
    nodes = ("row", "chip", "core")
    placed = (
        P(nodes, None),
        P(nodes),
        P(nodes),
        P("row", COL),
        P("row", COL),
        P(),
        P(),
        P(),
        P(),
        P(),
        P(),
        P(),
        P(),
        P(nodes, None),
    )
    return jax.shard_map(
        functools.partial(local, n_row, n_col),
        mesh=by_core,
        in_specs=placed,
        out_specs=(P(nodes, None), P(nodes, None), P(), P(), P(), P(), P(), P(), P(), P()),
        check_vma=False,
    )
```

```python
import functools
import math

import jax
import jax.numpy as jnp
from jax import lax
from jax.experimental import pallas as pl
from jax.experimental.pallas import tpu as pltpu
from jax.sharding import PartitionSpec as P

ORDER = 13
CLUSTERS = 16
HELD_BYTES = 1 << 25
VMEM_BYTES = 32 << 20
TERMS = 6
NO_COST = pl.CostEstimate(flops=1, bytes_accessed=1, transcendentals=0)
COL = ("chip", "core")


def finish(mixed, gain, shift, valid_rows):
    active = jax.nn.gelu(mixed, approximate=False)
    centered = active - jnp.mean(active, axis=-1, keepdims=True)
    variance = jnp.mean(centered * centered, axis=-1, keepdims=True)
    return (centered * lax.rsqrt(variance + 1e-05) * gain + shift) * valid_rows[:, None]


def forward_product(adjacency, piece_low):
    partial_value = jnp.dot(
        adjacency,
        lax.all_gather(piece_low, "row", axis=0, tiled=True),
        preferred_element_type=jnp.float32,
    )
    return lax.psum_scatter(partial_value, COL, scatter_dimension=0, tiled=True)


def backward_product(adjacency, piece_low):
    partial_value = lax.dot_general(
        adjacency,
        lax.all_gather(piece_low, COL, axis=0, tiled=True),
        (((0,), (0,)), ((), ())),
        preferred_element_type=jnp.float32,
    )
    return lax.psum_scatter(
        partial_value.astype(jnp.bfloat16), "row", scatter_dimension=0, tiled=True
    ).astype(jnp.float32)


def layer_forward(adjacency, inputs, weight, bias, gain, shift, valid_rows):
    first_low = inputs.astype(jnp.bfloat16)
    second = -forward_product(adjacency, first_low)
    second_low = second.astype(jnp.bfloat16)

    def advance(state_pair, unused):
        previous, current, current_low = state_pair
        upcoming = -2.0 * forward_product(adjacency, current_low) - previous
        upcoming_low = upcoming.astype(jnp.bfloat16)
        return ((current, upcoming, upcoming_low), upcoming_low)

    ignored, others = lax.scan(advance, (inputs, second, second_low), None, length=ORDER - 2)
    stacked = jnp.concatenate([first_low[None], second_low[None], others], axis=0)
    mixed = jnp.einsum("kni,kio->no", stacked, weight, preferred_element_type=jnp.float32) + bias
    return (stacked, mixed, finish(mixed, gain, shift, valid_rows))


def layer_backward(adjacency, stacked, mixed, upstream, weight, gain, shift, valid_rows):

    def local_finish(mixed_in, gain_in, shift_in):
        return finish(mixed_in, gain_in, shift_in, valid_rows)

    ignored, pullback = jax.vjp(local_finish, mixed, gain, shift)
    mixed_grad, gain_grad, shift_grad = pullback(upstream)
    mixed_low = mixed_grad.astype(jnp.bfloat16)
    bias_grad = jnp.sum(mixed_low.astype(jnp.float32), axis=0)
    weight_grad = jnp.einsum("kni,no->kio", stacked, mixed_low, preferred_element_type=jnp.float32)
    direct = jnp.einsum("no,kio->kni", mixed_low, weight, preferred_element_type=jnp.float32)

    def retreat(state_pair, direct_term):
        later_two, later_one = state_pair
        current = (
            direct_term
            - 2.0 * backward_product(adjacency, later_one.astype(jnp.bfloat16))
            - later_two
        )
        return ((later_one, current), None)

    start_pair = (jnp.zeros_like(direct[0]), direct[ORDER - 1])
    (second_grad, first_grad), unused = lax.scan(
        retreat, start_pair, direct[1 : ORDER - 1], reverse=True
    )
    input_grad = (
        direct[0] - backward_product(adjacency, first_grad.astype(jnp.bfloat16)) - second_grad
    )
    return (input_grad, weight_grad, bias_grad, gain_grad, shift_grad)


def swap(value, axis):
    return lax.ppermute(value, axis, [(0, 1), (1, 0)])


def trade(pieces, axis):
    return lax.all_to_all(pieces, axis, 0, 0, tiled=False)


def broadcast_along(value, axis, size):
    return trade(jnp.broadcast_to(value[None], (size,) + value.shape), axis)


def joined(mine, other, mine_first):
    return jnp.where(
        mine_first, jnp.concatenate([mine, other]), jnp.concatenate([other, mine])
    )


def added(mine, received):
    return (mine.astype(jnp.float32) + received.astype(jnp.float32)).astype(jnp.bfloat16)


def assemble(place_ref, own_ref, sibling_ref, near_ref, far_ref, out_ref, done):
    chip, core = place_ref[0], place_ref[1]
    own_cap, span = own_ref.shape
    half = span // 2

    def rows(of_chip, of_core):
        return pl.ds(pl.multiple_of((2 * of_chip + of_core) * own_cap, own_cap), own_cap)

    def fetch(source, of_chip, of_core, columns, place):
        target = out_ref.at[rows(of_chip, of_core), columns]
        return pltpu.make_async_copy(source, target, done.at[place])

    def quadrant_copies(here):
        there = 1 - here
        columns = pl.ds(there * half, half)
        return (
            fetch(near_ref, there, core, columns, 2),
            fetch(far_ref, there, 1 - core, columns, 3),
        )

    everything = pl.ds(0, span)
    top = (
        fetch(own_ref, chip, core, everything, 0),
        fetch(sibling_ref, chip, 1 - core, everything, 1),
    )

    def of_chip(here):
        there = 1 - here
        copies = top + quadrant_copies(here)
        for copy in copies:
            copy.start()
        for copy in copies:
            copy.wait()
        here_rows = pl.ds(here * half, half)
        for tile in range(half // 128):
            columns = pl.ds(there * half + tile * 128, 128)
            strip = out_ref[here_rows, columns]
            turned = jnp.transpose(strip.astype(jnp.float32)).astype(jnp.bfloat16)
            out_ref[columns, here_rows] = turned

    @pl.when(chip == 0)
    def first():
        of_chip(0)

    @pl.when(chip == 1)
    def second():
        of_chip(1)

    across = jnp.ones((1, span), jnp.float32)
    for tile in range(span // 128):
        across = across + jnp.sum(
            out_ref[pl.ds(tile * 128, 128), :].astype(jnp.float32), axis=0, keepdims=True
        )
    across = lax.rsqrt(across)
    for tile in range(span // 128):
        strip = out_ref[pl.ds(tile * 128, 128), :].astype(jnp.float32)
        down = lax.rsqrt(1.0 + jnp.sum(strip, axis=1, keepdims=True))
        out_ref[pl.ds(tile * 128, 128), :] = (strip * down * across).astype(jnp.bfloat16)


def normalized_block(own, sibling, near, far, place):
    span = own.shape[1]
    return pl.pallas_call(
        assemble,
        out_shape=jax.ShapeDtypeStruct((span, span), jnp.bfloat16),
        in_specs=[pl.BlockSpec(memory_space=pltpu.SMEM)]
        + [pl.BlockSpec(memory_space=pltpu.HBM)] * 4,
        out_specs=pl.BlockSpec(memory_space=pltpu.VMEM),
        scratch_shapes=[pltpu.SemaphoreType.DMA((4,))],
        compiler_params=pltpu.CompilerParams(vmem_limit_bytes=VMEM_BYTES),
        cost_estimate=NO_COST,
        name="normalized_block",
    )(place, own, sibling, near, far)


def pack_kernel(
    keep_ref, row_codes_ref, col_codes_ref, row_keys_ref, col_keys_ref, weight_ref, out_ref,
    masked, picked, rows_hot, cols_hot
):
    tile_rows, tile_cols = weight_ref.shape
    blocks_down, blocks_across = keep_ref.shape
    groups, ignored, lanes = out_ref.shape
    send_cap, own_cap = rows_hot.shape[0] // groups, cols_hot.shape[0] // groups
    high, wide = tile_rows // blocks_down, tile_cols // blocks_across
    for down in range(blocks_down):
        for across in range(blocks_across):
            rows, columns = pl.ds(down * high, high), pl.ds(across * wide, wide)
            own, other = row_codes_ref[rows, :], col_codes_ref[:, columns]
            linked = (own == other) & (own % 2 == 1) & (keep_ref[down, across] == 1)
            weight = weight_ref[rows, columns].astype(jnp.float32)
            masked[rows, columns] = jnp.where(linked, weight, 0.0).astype(jnp.bfloat16)

    def one_hot(keys, start, count):
        standing = lax.broadcasted_iota(jnp.int32, (count, keys.shape[1]), 0) + start
        return jnp.where(standing == keys, 1.0, 0.0).astype(jnp.bfloat16)

    for group in range(groups):
        rows_hot[pl.ds(group * send_cap, send_cap), :] = one_hot(
            row_keys_ref[...], group * send_cap, send_cap
        )
        cols_hot[pl.ds(group * own_cap, own_cap), :] = one_hot(
            col_keys_ref[...], group * own_cap, own_cap
        )
    for tile in range(tile_cols // 256):
        columns = pl.ds(tile * 256, 256)
        picked[:, columns] = jnp.dot(
            rows_hot[...], masked[:, columns], preferred_element_type=jnp.float32
        ).astype(jnp.bfloat16)
    whole, half = own_cap // lanes, send_cap // 2
    for group in range(groups):
        packed = lax.dot_general(
            cols_hot[pl.ds(group * own_cap, own_cap), :],
            picked[pl.ds(group * send_cap, send_cap), :],
            (((1,), (1,)), ((), ())),
            preferred_element_type=jnp.float32,
        ).T
        for tile in range(whole):
            out_ref[group, pl.ds(tile * send_cap, send_cap), :] = packed[
                :, tile * lanes : (tile + 1) * lanes
            ].astype(jnp.bfloat16)
        ends = jnp.concatenate(
            [packed[:half, whole * lanes :], packed[half:, whole * lanes :]], axis=1
        )
        out_ref[group, pl.ds(whole * send_cap, half), :] = ends.astype(jnp.bfloat16)


def packed_pieces(block_keep, row_codes, col_codes, row_keys, col_keys, edge_weight, caps, groups):
    own_cap, send_cap = caps
    tile_rows, tile_cols = edge_weight.shape
    high = own_cap // 128 * send_cap + send_cap // 2
    vector = pl.BlockSpec(memory_space=pltpu.VMEM)
    return pl.pallas_call(
        pack_kernel,
        out_shape=jax.ShapeDtypeStruct((groups, high, 128), jnp.bfloat16),
        in_specs=[pl.BlockSpec(memory_space=pltpu.SMEM)] + [vector] * 5,
        out_specs=vector,
        scratch_shapes=[
            pltpu.VMEM((tile_rows, tile_cols), jnp.bfloat16),
            pltpu.VMEM((groups * send_cap, tile_cols), jnp.bfloat16),
            pltpu.VMEM((groups * send_cap, tile_rows), jnp.bfloat16),
            pltpu.VMEM((groups * own_cap, tile_cols), jnp.bfloat16),
        ],
        compiler_params=pltpu.CompilerParams(vmem_limit_bytes=VMEM_BYTES),
        cost_estimate=NO_COST,
        name="packed_pieces",
    )(block_keep, row_codes[:, None], col_codes[None], row_keys[None], col_keys[None], edge_weight)


def normal_share(mixed):
    return 0.5 * (1.0 + lax.erf(mixed * 0.5**0.5))


def norm_forward(mixed):
    active = mixed * normal_share(mixed)
    centered = active - jnp.mean(active, axis=-1, keepdims=True)
    scale = lax.rsqrt(jnp.mean(centered * centered, axis=-1, keepdims=True) + 1e-05)
    return centered * scale, scale


def norm_backward(mixed, upstream, gain, valid):
    normed, scale = norm_forward(mixed)
    upstream = upstream * valid
    inner = upstream * gain
    inner = inner - jnp.mean(inner, axis=-1, keepdims=True) - normed * jnp.mean(
        inner * normed, axis=-1, keepdims=True
    )
    density = jnp.exp(-0.5 * mixed * mixed) * (1.0 / (2.0 * math.pi) ** 0.5)
    low = (inner * scale * (normal_share(mixed) + mixed * density)).astype(jnp.bfloat16)
    rest = [low.astype(jnp.float32), upstream * normed, upstream]
    return low, [jnp.sum(value, axis=0, keepdims=True) for value in rest]


def weight_gradient(turned_ref, low, core, mine_ref, other_ref):
    part = turned_ref.shape[0] // 4

    def halves(first_ref, second_ref):
        for place in range(4):
            out_ref = second_ref if place % 2 else first_ref
            out_ref[place // 2, :part, :] = jnp.dot(
                turned_ref[place * part : (place + 1) * part, :],
                low,
                preferred_element_type=jnp.float32,
            ).astype(jnp.bfloat16)

    @pl.when(core == 0)
    def low_half_first():
        halves(mine_ref, other_ref)

    @pl.when(core == 1)
    def high_half_first():
        halves(other_ref, mine_ref)


def term_products(powers_ref, everyone, take):
    count, own_cap, span = powers_ref.shape
    for start in range(0, count, TERMS):
        rows = powers_ref[start : start + TERMS].reshape(TERMS * own_cap, span)
        low = jnp.dot(rows, everyone, preferred_element_type=jnp.float32).astype(jnp.bfloat16)
        for place in range(TERMS):
            take(1 + start + place, low[place * own_cap : (place + 1) * own_cap])


def forward_terms(powers_ref, all_ref, own_ref, weight_ref, bias_ref, turned, mixed):
    fan_in = own_ref.shape[1]

    def take(term, low):
        turned[term * fan_in : (term + 1) * fan_in, :] = low.T
        mixed[...] += jnp.dot(low, weight_ref[term], preferred_element_type=jnp.float32)

    mixed[...] = jnp.broadcast_to(bias_ref[...], mixed.shape)
    take(0, own_ref[...])
    term_products(powers_ref, all_ref[...], take)


def backward_terms(powers_ref, all_ref, own_ref, weight_ref, total):
    def take(term, low):
        total[...] += lax.dot_general(
            low, weight_ref[term], (((1,), (1,)), ((), ())), preferred_element_type=jnp.float32
        )

    total[...] = jnp.zeros(total.shape, jnp.float32)
    take(0, own_ref[...])
    term_products(powers_ref, all_ref[...], take)


def layer_one_kernel(
    powers_ref,
    all_ref,
    own_ref,
    weight_ref,
    bias_ref,
    gain_ref,
    shift_ref,
    valid_ref,
    hidden_ref,
    turned_ref,
    mixed_ref,
):
    forward_terms(powers_ref, all_ref, own_ref, weight_ref, bias_ref, turned_ref, mixed_ref)
    normed, ignored = norm_forward(mixed_ref[...])
    hidden = (normed * gain_ref[...] + shift_ref[...]) * valid_ref[...]
    hidden_ref[...] = hidden.astype(jnp.bfloat16)


def layer_two_kernel(
    place_ref,
    powers_ref,
    all_ref,
    own_ref,
    weight_ref,
    bias_ref,
    gain_ref,
    shift_ref,
    valid_ref,
    upstream_ref,
    active_ref,
    low_ref,
    rest_ref,
    mine_ref,
    other_ref,
    turned,
    mixed,
):
    forward_terms(powers_ref, all_ref, own_ref, weight_ref, bias_ref, turned, mixed)
    normed, ignored = norm_forward(mixed[...])
    active = (normed * gain_ref[...] + shift_ref[...]) * valid_ref[...]
    active_ref[...] = active.astype(jnp.bfloat16)
    low, rest = norm_backward(
        mixed[...], upstream_ref[...].astype(jnp.float32), gain_ref[...], valid_ref[...]
    )
    low_ref[...] = low
    for place in range(3):
        rest_ref[place : place + 1, :] = rest[place]
    weight_gradient(turned, low, place_ref[1], mine_ref, other_ref)


def back_two_kernel(
    place_ref,
    powers_ref,
    all_ref,
    own_ref,
    weight_ref,
    turned_ref,
    mixed_ref,
    gain_ref,
    valid_ref,
    rest_ref,
    low_ref,
    mine_ref,
    other_ref,
    total,
):
    backward_terms(powers_ref, all_ref, own_ref, weight_ref, total)
    low, rest = norm_backward(mixed_ref[...], total[...], gain_ref[...], valid_ref[...])
    low_ref[...] = low
    weight_gradient(turned_ref, low, place_ref[1], mine_ref, other_ref)
    part = turned_ref.shape[0] // 4
    extra = jnp.zeros((2, mine_ref.shape[1] - part, mine_ref.shape[2]), jnp.bfloat16)
    rows = rest + [rest_ref[place : place + 1, :] for place in range(3)]
    rows = jnp.concatenate(rows + [jnp.zeros((10, rows[0].shape[1]), jnp.float32)], axis=0)

    def below(first_ref, second_ref):
        first_ref[:, part:, :] = extra
        second_ref[:, part:, :] = extra
        first_ref[0, part : part + 16, :] = rows.astype(jnp.bfloat16)

    @pl.when(place_ref[1] == 0)
    def low_half_here():
        below(mine_ref, other_ref)

    @pl.when(place_ref[1] == 1)
    def low_half_there():
        below(other_ref, mine_ref)


def back_one_kernel(powers_ref, all_ref, own_ref, weight_ref, out_ref, total):
    backward_terms(powers_ref, all_ref, own_ref, weight_ref, total)
    out_ref[...] = total[...].astype(jnp.bfloat16)


def layer_pass(kernel, name, place, powers, everyone, own, weight, others, outs, scratch):
    near = pl.BlockSpec(memory_space=pltpu.VMEM)
    operands = [powers, everyone, own, weight] + list(others)
    in_specs = [near] * len(operands)
    if place is not None:
        in_specs = [pl.BlockSpec(memory_space=pltpu.SMEM)] + in_specs
        operands = [place] + operands
    return pl.pallas_call(
        kernel,
        out_shape=outs,
        in_specs=in_specs,
        out_specs=[near] * len(outs),
        scratch_shapes=[pltpu.VMEM(shape, dtype) for shape, dtype in scratch],
        compiler_params=pltpu.CompilerParams(vmem_limit_bytes=VMEM_BYTES),
        cost_estimate=NO_COST,
        name=name,
    )(*operands)


def finish_kernel(scalars_ref, pair_ref, siblings_ref, other_ref, out_ref, *small_refs):
    step = pl.program_id(0)
    part = out_ref.shape[1]
    for here, values_ref in ((step < 2, pair_ref), (step >= 2, siblings_ref)):
        @pl.when(here & (scalars_ref[0] == 1))
        def fast_form():
            out_ref[0] = values_ref[0, :part, :].astype(jnp.float32)

        for small_ref in small_refs:
            @pl.when(here & (scalars_ref[1 + step] == 0))
            def small_sums():
                small_ref[...] = values_ref[0, part : part + 16, :].astype(jnp.float32)

    @pl.when(scalars_ref[0] == 0)
    def general_form():
        out_ref[0] = other_ref[0].astype(jnp.float32)


def finished(scalars, pair, siblings, other, with_small=False):
    count, part, width = other.shape
    out, held = (1, part, width), (1,) + pair.shape[1:]
    out_specs = [pl.BlockSpec(out, lambda step, ref: (ref[1 + step], 0, 0))]
    out_shape = [jax.ShapeDtypeStruct(other.shape, jnp.float32)]
    if with_small:
        out_specs.append(pl.BlockSpec((16, width), lambda step, ref: (0, 0)))
        out_shape.append(jax.ShapeDtypeStruct((16, width), jnp.float32))
    return pl.pallas_call(
        finish_kernel,
        grid_spec=pltpu.PrefetchScalarGridSpec(
            num_scalar_prefetch=1,
            grid=(count,),
            in_specs=[
                pl.BlockSpec(held, lambda step, ref: (jnp.minimum(step, 1), 0, 0)),
                pl.BlockSpec(held, lambda step, ref: (jnp.maximum(step - 2, 0), 0, 0)),
                pl.BlockSpec(out, lambda step, ref: ((1 - ref[0]) * ref[1 + step], 0, 0)),
            ],
            out_specs=out_specs,
        ),
        out_shape=out_shape,
        compiler_params=pltpu.CompilerParams(vmem_limit_bytes=VMEM_BYTES),
        cost_estimate=NO_COST,
        name="finished",
    )(scalars, pair, siblings, other)


def unpack_kernel(place_ref, pieces_ref, keys_ref, own_ref, quadrant_ref, columns, hot):
    groups, high, lanes = pieces_ref.shape
    own_cap, span = own_ref.shape
    whole = own_cap // lanes
    send_cap = keys_ref.shape[1] // groups
    half, rest = send_cap // 2, own_cap - whole * lanes
    for group in range(groups):
        start = group * send_cap
        for tile in range(whole):
            columns[start : start + send_cap, tile * lanes : (tile + 1) * lanes] = pieces_ref[
                group, tile * send_cap : (tile + 1) * send_cap, :
            ]
        ends = pieces_ref[group, whole * send_cap :, :]
        columns[start : start + half, whole * lanes :] = ends[:, :rest]
        columns[start + half : start + send_cap, whole * lanes :] = ends[:, rest:]
    standing = lax.broadcasted_iota(jnp.int32, hot.shape, 0)
    hot[...] = jnp.where(standing == keys_ref[...], 1.0, 0.0).astype(jnp.bfloat16)
    block = jnp.dot(hot[...], columns[...], preferred_element_type=jnp.float32)
    own_ref[...] = block.T.astype(jnp.bfloat16)
    middle = span // 2

    @pl.when(place_ref[0] == 0)
    def first():
        quadrant_ref[...] = own_ref[:, :middle]

    @pl.when(place_ref[0] == 1)
    def second():
        quadrant_ref[...] = own_ref[:, middle:]


def unpacked_block(pieces, keys, place, own_cap, span):
    vector = pl.BlockSpec(memory_space=pltpu.VMEM)
    return pl.pallas_call(
        unpack_kernel,
        out_shape=[
            jax.ShapeDtypeStruct((own_cap, span), jnp.bfloat16),
            jax.ShapeDtypeStruct((own_cap, span // 2), jnp.bfloat16),
        ],
        in_specs=[pl.BlockSpec(memory_space=pltpu.SMEM), vector, vector],
        out_specs=[vector, vector],
        scratch_shapes=[
            pltpu.VMEM((keys.shape[1], own_cap), jnp.bfloat16),
            pltpu.VMEM((span, keys.shape[1]), jnp.bfloat16),
        ],
        compiler_params=pltpu.CompilerParams(vmem_limit_bytes=VMEM_BYTES),
        cost_estimate=NO_COST,
        name="unpacked_block",
    )(place, pieces, keys)


def fit_kernel(codes_ref, out_ref, *, n_row, caps):
    own_cap, send_cap, seat_cap = caps
    codes = codes_ref[...]
    devices = codes.shape[0]
    n_col = devices // n_row
    label = lax.broadcasted_iota(jnp.int32, (devices, 128), 1)
    counts = jnp.zeros((devices, 128), jnp.float32)
    for cluster in range(CLUSTERS):
        here = jnp.where(codes == 2 * cluster + 1, 1.0, 0.0)
        counts = counts + jnp.where(
            label == cluster, jnp.sum(here, axis=1, keepdims=True), 0.0
        )
    sizes = jnp.sum(counts, axis=0, keepdims=True)
    across = jnp.broadcast_to(sizes, (128, 128))
    down = across.T
    first = lax.broadcasted_iota(jnp.int32, (128, 128), 0)
    second = lax.broadcasted_iota(jnp.int32, (128, 128), 1)
    ahead = (across > down) | ((across == down) & (second < first))
    ahead = ahead & (second < CLUSTERS)
    rank = jnp.sum(jnp.where(ahead, 1.0, 0.0), axis=1, keepdims=True).astype(jnp.int32)
    others = n_row - 1
    later = rank > others
    turn = jnp.zeros_like(rank)
    for count in range(1, CLUSTERS // others + 1):
        turn = turn + jnp.where(rank - 1 >= count * others, 1, 0)
    place = rank - 1 - turn * others
    group = jnp.where(rank == 0, 0, 1 + jnp.where(later, others - 1 - place, place))
    member = (group == second) & (first < CLUSTERS)
    held = jnp.dot(
        counts.astype(jnp.bfloat16),
        jnp.where(member, 1.0, 0.0).astype(jnp.bfloat16),
        preferred_element_type=jnp.float32,
    )
    by_row = jnp.zeros((1, 128), jnp.float32)
    for row in range(n_row):
        rows = jnp.sum(held[row * n_col : (row + 1) * n_col], axis=0, keepdims=True)
        by_row = jnp.maximum(by_row, rows)
    device = lax.broadcasted_iota(jnp.int32, (devices, 128), 0)
    by_col = jnp.zeros((1, 128), jnp.float32)
    for col in range(n_col):
        cols = jnp.where(device % n_col == col, held, 0.0)
        by_col = jnp.maximum(by_col, jnp.sum(cols, axis=0, keepdims=True))
    fits = (
        (jnp.max(by_col) <= own_cap) & (jnp.max(by_row) <= send_cap) & (jnp.max(held) <= seat_cap)
    )
    out_ref[0] = jnp.where(fits, 1, 0)


def fits_in(codes, n_row, caps):
    fits = pl.pallas_call(
        functools.partial(fit_kernel, n_row=n_row, caps=caps),
        out_shape=jax.ShapeDtypeStruct((1,), jnp.int32),
        in_specs=[pl.BlockSpec(memory_space=pltpu.VMEM)],
        out_specs=pl.BlockSpec(memory_space=pltpu.SMEM),
        cost_estimate=NO_COST,
        name="fits",
    )(codes.reshape(-1, codes.shape[-1]))
    return fits


def exclusive_counts(member):
    count = member.shape[-1]
    before = jnp.arange(count)[:, None] < jnp.arange(count)[None, :]
    return jnp.dot(
        member.astype(jnp.bfloat16),
        before.astype(jnp.bfloat16),
        preferred_element_type=jnp.float32,
    ).astype(jnp.int32)


def assign(codes, n_row):
    cluster, valid = codes >> 1, codes & 1
    labels = jnp.arange(CLUSTERS)
    sizes = jnp.sum(
        (cluster.reshape(1, -1) == labels[:, None]) & (valid.reshape(1, -1) == 1), axis=1
    )
    ahead = (sizes[None, :] > sizes[:, None]) | (
        (sizes[None, :] == sizes[:, None]) & (labels[None, :] < labels[:, None])
    )
    rank = jnp.sum(ahead, axis=1)
    others = n_row - 1
    turn, place = (rank - 1) // others, (rank - 1) % others
    group = jnp.where(rank == 0, 0, 1 + jnp.where(turn == 0, place, others - 1 - place))
    of_node = jnp.sum(
        jnp.where(cluster[None] == labels[:, None, None, None], group[:, None, None, None], 0),
        axis=0,
    )
    return jnp.where(valid == 1, of_node, n_row)


def compact(
    codes,
    group,
    features,
    block_keep,
    edge_weight,
    weight_one,
    bias_one,
    gain_one,
    shift_one,
    weight_two,
    bias_two,
    gain_two,
    shift_two,
    cotangent,
    places_of,
    slots_of,
    seats_of,
    decide,
    sizes,
    caps,
):
    row, col = lax.axis_index("row"), lax.axis_index(COL)
    chip, core = lax.axis_index("chip"), lax.axis_index("core")
    n_row, n_col = sizes
    own_cap, send_cap, seat_cap = caps
    own_nodes, in_width = features.shape
    width = weight_two.shape[2]
    span = n_col * own_cap
    targets = jnp.arange(n_row)

    def in_col(value):
        return lax.dynamic_index_in_dim(value, col, 1, False).reshape(-1)

    def in_row(value):
        return lax.dynamic_index_in_dim(value, row, 0, False).reshape(-1)

    row_group, col_group = in_row(group), in_col(group)
    row_slots, col_places = in_row(slots_of(group)), in_col(places_of(group))
    row_keys = jnp.where(row_slots < send_cap, row_group * send_cap + row_slots, -1)
    col_keys = jnp.where(col_places < own_cap, col_group * own_cap + col_places, -1)
    pieces = packed_pieces(
        block_keep,
        in_row(codes),
        in_col(codes),
        row_keys,
        col_keys,
        edge_weight,
        (own_cap, send_cap),
        n_row,
    )
    pieces, codes = lax.optimization_barrier((pieces, codes))
    group = assign(codes, n_row)
    pieces = trade(pieces, "row")
    places, slots, seats = places_of(group), slots_of(group), seats_of(group)

    standing = jnp.arange(n_col)[None, :, None] * own_cap + places
    fits_here = jnp.where(group == row, standing, -1).reshape(n_row, -1)
    slot_of = slots.reshape(n_row, -1)
    target = jnp.max(
        jnp.where(
            slot_of[:, None, :] == jnp.arange(send_cap)[None, :, None], fits_here[:, None, :], -1
        ),
        axis=2,
    )
    keys = target.reshape(1, -1)

    def to_partner(value, step):
        return lax.ppermute(value, "row", [(place, place ^ step) for place in range(n_row)])

    partners = row ^ targets
    group_here = lax.dynamic_index_in_dim(in_row(group).reshape(n_col, -1), col, 0, False)
    seat_here = lax.dynamic_index_in_dim(in_row(seats).reshape(n_col, -1), col, 0, False)

    def seat_of_node(groups):
        hot = (group_here[None, None, :] == groups[:, None, None]) & (
            seat_here[None, None, :] == jnp.arange(seat_cap)[None, :, None]
        )
        return hot.astype(jnp.bfloat16).reshape(n_row * seat_cap, own_nodes)

    enter_partner = seat_of_node(partners)
    both = jnp.dot(enter_partner, jnp.concatenate([features, cotangent], axis=1))
    both = both.reshape(n_row // 2, 2, seat_cap, -1)
    near, far = both[:, 0], to_partner(both[:, 1], 1)
    enter_partner = enter_partner.T
    near, codes = lax.optimization_barrier((near, codes))
    fits, others = decide(codes)
    enter_home = seat_of_node(targets).T
    group_col = lax.dynamic_index_in_dim(group, col, 1, False)
    seats_col = lax.dynamic_index_in_dim(seats, col, 1, False)
    places_col = lax.dynamic_index_in_dim(places, col, 1, False)
    seated = (group_col == row)[:, None, :] & (
        seats_col[:, None, :] == jnp.arange(seat_cap)[None, :, None]
    )
    place_of_seat = jnp.max(jnp.where(seated, places_col[:, None, :], -1), axis=2)
    from_partner = jnp.max(
        jnp.where((partners[:, None] == targets)[:, :, None], place_of_seat[None], -1), axis=1
    )
    arrive = from_partner.reshape(1, -1) == jnp.arange(own_cap)[:, None]
    arrive = arrive.astype(jnp.bfloat16)
    leave_partner = jnp.concatenate([from_partner[::2], from_partner[1::2]])
    leave_partner = leave_partner.reshape(-1, 1) == jnp.arange(own_cap)
    leave_partner = leave_partner.astype(jnp.bfloat16)
    leave_group = place_of_seat.reshape(-1, 1) == jnp.arange(own_cap)[None, :]
    leave_group = leave_group.astype(jnp.bfloat16)
    held_count = jnp.sum(group_col == row)
    valid_rows = (jnp.arange(own_cap) < held_count).astype(jnp.float32)[:, None]
    place = jnp.stack([chip, core]).astype(jnp.int32)
    quarters = jnp.stack([col, (1 - chip) * 2 + core, chip * 2 + 1 - core, 3 - col])
    quarters = jnp.concatenate([fits, quarters.astype(jnp.int32)])
    scalars = (chip, 1 - chip, col * own_cap)
    scalars = tuple(value.astype(jnp.uint32) for value in scalars) + (chip == 0, core == 0, place, quarters)
    homes = enter_home, enter_partner, leave_group, leave_partner
    both = jnp.stack([near, far], axis=1)
    pieces, both, keys, arrive, homes, valid_rows, others, scalars = lax.optimization_barrier(
        (pieces, both, keys, arrive, homes, valid_rows, others, scalars)
    )
    enter_home, enter_partner, leave_group, leave_partner = homes
    this_chip, other_chip, own_start, first_chip, first_core, place, quarters = scalars

    own_block, quadrant = unpacked_block(pieces, keys, place, own_cap, span)
    quadrant = swap(quadrant, "chip")
    both = [both[0]] + [to_partner(both[half], 2 * half) for half in range(1, n_row // 2)]
    sibling = swap(own_block, "core")
    quadrant, *both = lax.optimization_barrier((quadrant, *both))
    adjacency = normalized_block(own_block, sibling, quadrant, swap(quadrant, "core"), place)
    both = jnp.concatenate(both).reshape(n_row * seat_cap, -1)
    mine = jnp.dot(arrive, both)
    features_own, cotangent_own = mine[:, :in_width], mine[:, in_width:]
    sibling = swap(features_own, "core")

    first = (own_start + jnp.arange(own_cap, dtype=jnp.uint32))[:, None]
    first = first == jnp.arange(span, dtype=jnp.uint32)[None, :]
    previous = first.astype(jnp.float32)
    current = -lax.dynamic_slice_in_dim(adjacency, own_start, own_cap, 0).astype(jnp.float32)
    lowered = [current.astype(jnp.bfloat16)]
    for position in range(2, ORDER):
        upcoming = (
            -2.0 * jnp.dot(lowered[-1], adjacency, preferred_element_type=jnp.float32) - previous
        )
        low = upcoming.astype(jnp.bfloat16)
        if position == 4:
            low, sibling = lax.optimization_barrier((low, sibling))
            features_chip = joined(features_own, sibling, first_core)
            partner = swap(features_chip, "chip")
        if position == 8:
            low, partner = lax.optimization_barrier((low, partner))
            features_all = joined(features_chip, partner, first_chip)
        previous, current = current, upcoming
        lowered.append(low)
    powers = jnp.concatenate(lowered, axis=0).reshape(ORDER - 1, own_cap, span)

    def everywhere(value_low):
        return lax.all_gather(value_low, COL, axis=0, tiled=True)

    def chosen(value, other):
        return jnp.where(quarters[0] == 1, value.astype(jnp.float32), other.astype(jnp.float32))

    def shaped(*shape, dtype=jnp.bfloat16):
        return jax.ShapeDtypeStruct(shape, dtype)

    part_one, part_two = ORDER * in_width // n_col, ORDER * width // n_col
    padded = -(-(part_one + 16) // (8 * n_row)) * (8 * n_row)
    hidden, turned_one, mixed_one = layer_pass(
        layer_one_kernel,
        "layer_one",
        None,
        powers,
        features_all,
        features_own,
        weight_one,
        [bias_one[None], gain_one[None], shift_one[None], valid_rows],
        [
            shaped(own_cap, width),
            shaped(n_col * part_one, own_cap),
            shaped(own_cap, width, dtype=jnp.float32),
        ],
        [],
    )
    activations, low_two, rest_two, mine, other = layer_pass(
        layer_two_kernel,
        "layer_two",
        place,
        powers,
        everywhere(hidden),
        hidden,
        weight_two,
        [bias_two[None], gain_two[None], shift_two[None], valid_rows, cotangent_own],
        [
            shaped(own_cap, width),
            shaped(own_cap, width),
            shaped(3, width, dtype=jnp.float32),
            shaped(2, part_two, width),
            shaped(2, part_two, width),
        ],
        [((n_col * part_two, own_cap), jnp.bfloat16), ((own_cap, width), jnp.float32)],
    )

    def add_cores(mine, other):
        got = swap(other, "core")
        return tuple(
            added(
                lax.dynamic_index_in_dim(mine, index, 0, False),
                lax.dynamic_index_in_dim(got, index, 0, False),
            )
            for index in (this_chip, other_chip)
        )

    leaving = jnp.dot(leave_partner, activations).reshape(n_row, seat_cap, width)
    near, far = leaving[: n_row // 2], leaving[n_row // 2 :]
    far = to_partner(far, 1)
    here, there = add_cores(mine, other)
    everyone_two, there, far = lax.optimization_barrier((everywhere(low_two), there, far))
    there = swap(there, "chip")
    arrived = [jnp.stack([near[0], far[0]])] + [
        to_partner(jnp.stack([near[half], far[half]]), 2 * half) for half in range(1, n_row // 2)
    ]
    low_one, mine, other = layer_pass(
        back_two_kernel,
        "back_two",
        place,
        powers,
        everyone_two,
        low_two,
        weight_two,
        [turned_one, mixed_one, gain_one[None], valid_rows, rest_two],
        [shaped(own_cap, width), shaped(2, padded, width), shaped(2, padded, width)],
        [((own_cap, width), jnp.float32)],
    )
    low_one, there, arrived = lax.optimization_barrier((low_one, there, arrived))
    second = added(here, there).reshape(n_row, -1, width)
    many = second.shape[1]
    low_one, second = lax.optimization_barrier((low_one, second))
    second = trade(second, "row")
    here, there = add_cores(mine, other)
    low_one, there = lax.optimization_barrier((low_one, there))
    everyone_one = everywhere(low_one)
    there = swap(there, "chip")
    everyone_one, second, there = lax.optimization_barrier((everyone_one, second, there))
    first = added(here, there).reshape(n_row, -1, width)
    share = first.shape[1]
    second = jnp.sum(second.astype(jnp.float32), axis=0).astype(jnp.bfloat16)
    second = jnp.broadcast_to(second[None], (n_row,) + second.shape)
    mixed = jnp.concatenate([second, first], axis=1)
    everyone_one, mixed = lax.optimization_barrier((everyone_one, mixed))
    mixed = trade(mixed, "row")
    (input_grad,) = layer_pass(
        back_one_kernel,
        "back_one",
        None,
        powers,
        everyone_one,
        low_one,
        weight_one,
        [],
        [shaped(own_cap, in_width)],
        [((own_cap, in_width), jnp.float32)],
    )
    leaving = jnp.dot(leave_group, input_grad).reshape(n_row, seat_cap * in_width // width, width)
    arrived = jnp.concatenate(arrived).reshape(-1, width)
    home = jnp.dot(enter_partner, arrived, preferred_element_type=jnp.float32)
    home = chosen(home, others[0])
    mixed, leaving, home = lax.optimization_barrier((mixed, leaving, home))
    first = jnp.sum(mixed[:, many:].astype(jnp.float32), axis=0).astype(jnp.bfloat16)
    first = jnp.broadcast_to(first[None], (n_row,) + first.shape)
    first, mixed = lax.optimization_barrier((jnp.concatenate([first, leaving], axis=1), mixed))
    first = trade(first, "row")
    second = mixed[:, :many].reshape(1, -1, width)
    second = jnp.concatenate([second, swap(second, "chip")])
    second_siblings = swap(second, "core")
    back = first[:, share:].reshape(n_row * seat_cap, in_width)
    mine = first[:, :share].reshape(1, -1, width)
    first = jnp.concatenate([mine, swap(mine, "chip")])
    siblings = swap(first, "core")
    home_grad = jnp.dot(enter_home, back, preferred_element_type=jnp.float32)
    home_grad = chosen(home_grad, others[1])
    (second,) = finished(quarters, second, second_siblings, others[3])
    first, small = finished(quarters, first, siblings, others[2], True)
    return home, home_grad, first, second, chosen(small[:6], others[4])


def general(
    codes,
    features,
    block_keep,
    edge_weight,
    weight_one,
    bias_one,
    gain_one,
    shift_one,
    weight_two,
    bias_two,
    gain_two,
    shift_two,
    cotangent,
    node_valid,
):
    row, col = lax.axis_index("row"), lax.axis_index(COL)
    row_codes = lax.dynamic_index_in_dim(codes, row, 0, False).reshape(-1)
    col_codes = lax.dynamic_index_in_dim(codes, col, 1, False).reshape(-1)
    tile_rows, tile_cols = edge_weight.shape
    blocks_down, blocks_across = block_keep.shape
    block_side = tile_rows // blocks_down
    linked = (row_codes[:, None] == col_codes[None, :]) & (row_codes[:, None] & 1 == 1)
    linked = linked.reshape(blocks_down, block_side, blocks_across, block_side) & (
        block_keep[:, None, :, None] == 1
    )
    masked = edge_weight * linked.reshape(tile_rows, tile_cols).astype(jnp.bfloat16)
    degree_rows = 1.0 + lax.psum(jnp.sum(masked, axis=1, dtype=jnp.float32), COL)
    own_nodes = features.shape[0]
    own_degree = lax.dynamic_slice_in_dim(
        degree_rows, lax.axis_index(COL) * own_nodes, own_nodes, 0
    )
    degree_cols = lax.all_gather(own_degree, "row", axis=0, tiled=True)
    adjacency = (
        masked.astype(jnp.float32)
        * lax.rsqrt(degree_rows)[:, None]
        * lax.rsqrt(degree_cols)[None, :]
    ).astype(jnp.bfloat16)
    valid_rows = node_valid.astype(jnp.float32)
    stacked_one, mixed_one, hidden = layer_forward(
        adjacency,
        features.astype(jnp.float32),
        weight_one,
        bias_one,
        gain_one,
        shift_one,
        valid_rows,
    )
    stacked_two, mixed_two, activations = layer_forward(
        adjacency, hidden, weight_two, bias_two, gain_two, shift_two, valid_rows
    )
    hidden_grad, weight_two_grad, bias_two_grad, gain_two_grad, shift_two_grad = layer_backward(
        adjacency,
        stacked_two,
        mixed_two,
        cotangent.astype(jnp.float32),
        weight_two,
        gain_two,
        shift_two,
        valid_rows,
    )
    input_grad, weight_one_grad, bias_one_grad, gain_one_grad, shift_one_grad = layer_backward(
        adjacency, stacked_one, mixed_one, hidden_grad, weight_one, gain_one, shift_one, valid_rows
    )
    summed = lax.psum(
        (
            weight_one_grad,
            bias_one_grad,
            gain_one_grad,
            shift_one_grad,
            weight_two_grad,
            bias_two_grad,
            gain_two_grad,
            shift_two_grad,
        ),
        ("row",) + COL,
    )
    weight_one_grad, bias_one_grad, gain_one_grad, shift_one_grad = (
        summed[0],
        summed[1],
        summed[2],
        summed[3],
    )
    weight_two_grad, bias_two_grad, gain_two_grad, shift_two_grad = (
        summed[4],
        summed[5],
        summed[6],
        summed[7],
    )
    return (
        activations,
        input_grad,
        weight_one_grad,
        bias_one_grad,
        gain_one_grad,
        shift_one_grad,
        weight_two_grad,
        bias_two_grad,
        gain_two_grad,
        shift_two_grad,
    )


def local(n_row, n_col, *args):
    (
        features,
        node_valid,
        cluster,
        block_keep,
        edge_weight,
        weight_one,
        bias_one,
        gain_one,
        shift_one,
        weight_two,
        bias_two,
        gain_two,
        shift_two,
        cotangent,
    ) = args
    own_nodes, in_width = features.shape
    own_cap = own_nodes * n_row * 5 // 16
    send_cap = own_nodes * n_col * 11 // 32
    seat_cap = own_nodes // 2
    codes = broadcast_along(cluster * 2 + node_valid, ("row",) + COL, n_row * n_col)
    codes = codes.reshape(n_row, n_col, own_nodes)
    shared = (
        block_keep,
        edge_weight,
        weight_one,
        bias_one,
        gain_one,
        shift_one,
        weight_two,
        bias_two,
        gain_two,
        shift_two,
        cotangent,
    )

    def slow():
        return general(codes, features, *shared, node_valid)

    held = (ORDER - 1) * own_cap * own_cap * n_col * 2
    if held > HELD_BYTES or n_col != 4 or n_row < 2 or n_row & (n_row - 1):
        return slow()
    group = assign(codes, n_row)

    def member_of(group):
        return group[None] == jnp.arange(n_row)[:, None, None, None]

    def places_of(group):
        member = member_of(group).transpose(0, 2, 1, 3).reshape(n_row, n_col, -1)
        places = jnp.sum(jnp.where(member, exclusive_counts(member), 0), axis=0)
        return places.reshape(n_col, n_row, own_nodes).transpose(1, 0, 2)

    def slots_of(group):
        member = member_of(group).reshape(n_row, n_row, -1)
        slots = jnp.sum(jnp.where(member, exclusive_counts(member), 0), axis=0)
        return slots.reshape(n_row, n_col, own_nodes)

    def seats_of(group):
        member = member_of(group)
        return jnp.sum(jnp.where(member, exclusive_counts(member), 0), axis=0)

    width = weight_two.shape[2]

    def instead(state):
        made = slow()
        small = jnp.stack([made[place] for place in (3, 4, 5, 7, 8, 9)])
        return (jnp.ones_like(state[0]),) + tuple(
            value.astype(jnp.bfloat16).reshape(like.shape)
            for value, like in zip((made[0], made[1], made[2], made[6], small), state[1:])
        )

    shapes = (
        (own_nodes, width),
        (own_nodes, in_width),
        (n_col, ORDER * in_width // n_col, width),
        (n_col, ORDER * width // n_col, width),
        (6, width),
    )

    def decide(codes):
        fits = fits_in(codes, n_row, (own_cap, send_cap, seat_cap))
        others = lax.while_loop(
            lambda state: state[0][0] == 0,
            instead,
            (fits,) + tuple(jnp.zeros(shape, jnp.bfloat16) for shape in shapes),
        )[1:]
        return fits, others

    home, home_grad, first, second, small = compact(
        codes,
        group,
        features,
        *shared,
        places_of,
        slots_of,
        seats_of,
        decide,
        (n_row, n_col),
        (own_cap, send_cap, seat_cap),
    )
    return (
        home,
        home_grad,
        first.reshape(weight_one.shape),
        small[0],
        small[1],
        small[2],
        second.reshape(weight_two.shape),
        small[3],
        small[4],
        small[5],
    )


def solution(mesh):
    n_row, n_col = mesh.shape["row"], mesh.shape["col"]
    by_core = jax.sharding.Mesh(
        mesh.devices.reshape(n_row, n_col // 2, 2), ("row", "chip", "core")
    )
    nodes = ("row", "chip", "core")
    placed = (
        P(nodes, None),
        P(nodes),
        P(nodes),
        P("row", COL),
        P("row", COL),
        P(),
        P(),
        P(),
        P(),
        P(),
        P(),
        P(),
        P(),
        P(nodes, None),
    )
    return jax.shard_map(
        functools.partial(local, n_row, n_col),
        mesh=by_core,
        in_specs=placed,
        out_specs=(P(nodes, None), P(nodes, None), P(), P(), P(), P(), P(), P(), P(), P()),
        check_vma=False,
    )
```

```python
import functools
import math

import jax
import jax.numpy as jnp
from jax import lax
from jax.experimental import pallas as pl
from jax.experimental.pallas import tpu as pltpu
from jax.sharding import PartitionSpec as P

ORDER = 13
CLUSTERS = 16
HELD_BYTES = 1 << 25
VMEM_BYTES = 32 << 20
TERMS = 3
NO_COST = pl.CostEstimate(flops=1, bytes_accessed=1, transcendentals=0)
COL = ("chip", "core")
ROW = ("zed", "why")
PLANE = ("why", "chip", "core")


def finish(mixed, gain, shift, valid_rows):
    active = jax.nn.gelu(mixed, approximate=False)
    centered = active - jnp.mean(active, axis=-1, keepdims=True)
    variance = jnp.mean(centered * centered, axis=-1, keepdims=True)
    return (centered * lax.rsqrt(variance + 1e-05) * gain + shift) * valid_rows[:, None]


def forward_product(adjacency, piece_low):
    partial_value = jnp.dot(
        adjacency,
        lax.all_gather(piece_low, ROW, axis=0, tiled=True),
        preferred_element_type=jnp.float32,
    )
    return lax.psum_scatter(partial_value, COL, scatter_dimension=0, tiled=True)


def backward_product(adjacency, piece_low):
    partial_value = lax.dot_general(
        adjacency,
        lax.all_gather(piece_low, COL, axis=0, tiled=True),
        (((0,), (0,)), ((), ())),
        preferred_element_type=jnp.float32,
    )
    return lax.psum_scatter(
        partial_value.astype(jnp.bfloat16), ROW, scatter_dimension=0, tiled=True
    ).astype(jnp.float32)


def layer_forward(adjacency, inputs, weight, bias, gain, shift, valid_rows):
    first_low = inputs.astype(jnp.bfloat16)
    second = -forward_product(adjacency, first_low)
    second_low = second.astype(jnp.bfloat16)

    def advance(state_pair, unused):
        previous, current, current_low = state_pair
        upcoming = -2.0 * forward_product(adjacency, current_low) - previous
        upcoming_low = upcoming.astype(jnp.bfloat16)
        return ((current, upcoming, upcoming_low), upcoming_low)

    ignored, others = lax.scan(advance, (inputs, second, second_low), None, length=ORDER - 2)
    stacked = jnp.concatenate([first_low[None], second_low[None], others], axis=0)
    mixed = jnp.einsum("kni,kio->no", stacked, weight, preferred_element_type=jnp.float32) + bias
    return (stacked, mixed, finish(mixed, gain, shift, valid_rows))


def layer_backward(adjacency, stacked, mixed, upstream, weight, gain, shift, valid_rows):

    def local_finish(mixed_in, gain_in, shift_in):
        return finish(mixed_in, gain_in, shift_in, valid_rows)

    ignored, pullback = jax.vjp(local_finish, mixed, gain, shift)
    mixed_grad, gain_grad, shift_grad = pullback(upstream)
    mixed_low = mixed_grad.astype(jnp.bfloat16)
    bias_grad = jnp.sum(mixed_low.astype(jnp.float32), axis=0)
    weight_grad = jnp.einsum("kni,no->kio", stacked, mixed_low, preferred_element_type=jnp.float32)
    direct = jnp.einsum("no,kio->kni", mixed_low, weight, preferred_element_type=jnp.float32)

    def retreat(state_pair, direct_term):
        later_two, later_one = state_pair
        current = (
            direct_term
            - 2.0 * backward_product(adjacency, later_one.astype(jnp.bfloat16))
            - later_two
        )
        return ((later_one, current), None)

    start_pair = (jnp.zeros_like(direct[0]), direct[ORDER - 1])
    (second_grad, first_grad), unused = lax.scan(
        retreat, start_pair, direct[1 : ORDER - 1], reverse=True
    )
    input_grad = (
        direct[0] - backward_product(adjacency, first_grad.astype(jnp.bfloat16)) - second_grad
    )
    return (input_grad, weight_grad, bias_grad, gain_grad, shift_grad)


def swap(value, axis):
    return lax.ppermute(value, axis, [(0, 1), (1, 0)])


def trade(pieces, axis):
    return lax.all_to_all(pieces, axis, 0, 0, tiled=False)


def broadcast_along(value, axis, size):
    return trade(jnp.broadcast_to(value[None], (size,) + value.shape), axis)


def joined(mine, other, mine_first):
    return jnp.where(
        mine_first, jnp.concatenate([mine, other]), jnp.concatenate([other, mine])
    )


def added(mine, received):
    return (mine.astype(jnp.float32) + received.astype(jnp.float32)).astype(jnp.bfloat16)


def assemble(place_ref, own_ref, sibling_ref, near_ref, far_ref, out_ref, done):
    chip, core = place_ref[0], place_ref[1]
    own_cap, span = own_ref.shape
    half = span // 2

    def rows(of_chip, of_core):
        return pl.ds(pl.multiple_of((2 * of_chip + of_core) * own_cap, own_cap), own_cap)

    def fetch(source, of_chip, of_core, columns, place):
        target = out_ref.at[rows(of_chip, of_core), columns]
        return pltpu.make_async_copy(source, target, done.at[place])

    def quadrant_copies(here):
        there = 1 - here
        columns = pl.ds(there * half, half)
        return (
            fetch(near_ref, there, core, columns, 2),
            fetch(far_ref, there, 1 - core, columns, 3),
        )

    everything = pl.ds(0, span)
    top = (
        fetch(own_ref, chip, core, everything, 0),
        fetch(sibling_ref, chip, 1 - core, everything, 1),
    )

    def of_chip(here):
        there = 1 - here
        copies = top + quadrant_copies(here)
        for copy in copies:
            copy.start()
        for copy in copies:
            copy.wait()
        here_rows = pl.ds(here * half, half)
        for tile in range(half // 128):
            columns = pl.ds(there * half + tile * 128, 128)
            strip = out_ref[here_rows, columns]
            turned = jnp.transpose(strip.astype(jnp.float32)).astype(jnp.bfloat16)
            out_ref[columns, here_rows] = turned

    @pl.when(chip == 0)
    def first():
        of_chip(0)

    @pl.when(chip == 1)
    def second():
        of_chip(1)

    across = jnp.ones((1, span), jnp.float32)
    for tile in range(span // 128):
        across = across + jnp.sum(
            out_ref[pl.ds(tile * 128, 128), :].astype(jnp.float32), axis=0, keepdims=True
        )
    across = lax.rsqrt(across)
    for tile in range(span // 128):
        strip = out_ref[pl.ds(tile * 128, 128), :].astype(jnp.float32)
        down = lax.rsqrt(1.0 + jnp.sum(strip, axis=1, keepdims=True))
        out_ref[pl.ds(tile * 128, 128), :] = (strip * down * across).astype(jnp.bfloat16)


def normalized_block(own, sibling, near, far, place):
    span = own.shape[1]
    return pl.pallas_call(
        assemble,
        out_shape=jax.ShapeDtypeStruct((span, span), jnp.bfloat16),
        in_specs=[pl.BlockSpec(memory_space=pltpu.SMEM)]
        + [pl.BlockSpec(memory_space=pltpu.HBM)] * 4,
        out_specs=pl.BlockSpec(memory_space=pltpu.VMEM),
        scratch_shapes=[pltpu.SemaphoreType.DMA((4,))],
        compiler_params=pltpu.CompilerParams(vmem_limit_bytes=VMEM_BYTES),
        cost_estimate=NO_COST,
        name="normalized_block",
    )(place, own, sibling, near, far)


def pack_kernel(
    keep_ref, row_codes_ref, col_codes_ref, row_keys_ref, col_keys_ref, weight_ref, out_ref,
    masked, picked, rows_hot, cols_hot
):
    tile_rows, tile_cols = weight_ref.shape
    blocks_down, blocks_across = keep_ref.shape
    groups, ignored, lanes = out_ref.shape
    send_cap, own_cap = rows_hot.shape[0] // groups, cols_hot.shape[0] // groups
    high, wide = tile_rows // blocks_down, tile_cols // blocks_across
    for down in range(blocks_down):
        for across in range(blocks_across):
            rows, columns = pl.ds(down * high, high), pl.ds(across * wide, wide)
            own, other = row_codes_ref[rows, :], col_codes_ref[:, columns]
            linked = (own == other) & (own % 2 == 1) & (keep_ref[down, across] == 1)
            weight = weight_ref[rows, columns].astype(jnp.float32)
            masked[rows, columns] = jnp.where(linked, weight, 0.0).astype(jnp.bfloat16)

    def one_hot(keys, start, count):
        standing = lax.broadcasted_iota(jnp.int32, (count, keys.shape[1]), 0) + start
        return jnp.where(standing == keys, 1.0, 0.0).astype(jnp.bfloat16)

    for group in range(groups):
        rows_hot[pl.ds(group * send_cap, send_cap), :] = one_hot(
            row_keys_ref[...], group * send_cap, send_cap
        )
        cols_hot[pl.ds(group * own_cap, own_cap), :] = one_hot(
            col_keys_ref[...], group * own_cap, own_cap
        )
    for tile in range(tile_cols // 256):
        columns = pl.ds(tile * 256, 256)
        picked[:, columns] = jnp.dot(
            rows_hot[...], masked[:, columns], preferred_element_type=jnp.float32
        ).astype(jnp.bfloat16)
    whole, half = own_cap // lanes, send_cap // 2
    for group in range(groups):
        packed = lax.dot_general(
            cols_hot[pl.ds(group * own_cap, own_cap), :],
            picked[pl.ds(group * send_cap, send_cap), :],
            (((1,), (1,)), ((), ())),
            preferred_element_type=jnp.float32,
        ).T
        for tile in range(whole):
            out_ref[group, pl.ds(tile * send_cap, send_cap), :] = packed[
                :, tile * lanes : (tile + 1) * lanes
            ].astype(jnp.bfloat16)
        ends = jnp.concatenate(
            [packed[:half, whole * lanes :], packed[half:, whole * lanes :]], axis=1
        )
        out_ref[group, pl.ds(whole * send_cap, half), :] = ends.astype(jnp.bfloat16)


def packed_pieces(block_keep, row_codes, col_codes, row_keys, col_keys, edge_weight, caps, groups):
    own_cap, send_cap = caps
    tile_rows, tile_cols = edge_weight.shape
    high = own_cap // 128 * send_cap + send_cap // 2
    vector = pl.BlockSpec(memory_space=pltpu.VMEM)
    return pl.pallas_call(
        pack_kernel,
        out_shape=jax.ShapeDtypeStruct((groups, high, 128), jnp.bfloat16),
        in_specs=[pl.BlockSpec(memory_space=pltpu.SMEM)] + [vector] * 5,
        out_specs=vector,
        scratch_shapes=[
            pltpu.VMEM((tile_rows, tile_cols), jnp.bfloat16),
            pltpu.VMEM((groups * send_cap, tile_cols), jnp.bfloat16),
            pltpu.VMEM((groups * send_cap, tile_rows), jnp.bfloat16),
            pltpu.VMEM((groups * own_cap, tile_cols), jnp.bfloat16),
        ],
        compiler_params=pltpu.CompilerParams(vmem_limit_bytes=VMEM_BYTES),
        cost_estimate=NO_COST,
        name="packed_pieces",
    )(block_keep, row_codes[:, None], col_codes[None], row_keys[None], col_keys[None], edge_weight)


def normal_share(mixed):
    return 0.5 * (1.0 + lax.erf(mixed * 0.5**0.5))


def norm_forward(mixed):
    active = mixed * normal_share(mixed)
    centered = active - jnp.mean(active, axis=-1, keepdims=True)
    scale = lax.rsqrt(jnp.mean(centered * centered, axis=-1, keepdims=True) + 1e-05)
    return centered * scale, scale


def norm_backward(mixed, upstream, gain, valid):
    normed, scale = norm_forward(mixed)
    upstream = upstream * valid
    inner = upstream * gain
    inner = inner - jnp.mean(inner, axis=-1, keepdims=True) - normed * jnp.mean(
        inner * normed, axis=-1, keepdims=True
    )
    density = jnp.exp(-0.5 * mixed * mixed) * (1.0 / (2.0 * math.pi) ** 0.5)
    low = (inner * scale * (normal_share(mixed) + mixed * density)).astype(jnp.bfloat16)
    rest = [low.astype(jnp.float32), upstream * normed, upstream]
    return low, [jnp.sum(value, axis=0, keepdims=True) for value in rest]


def weight_gradient(turned_ref, low, core, mine_ref, other_ref):
    part = turned_ref.shape[0] // 4

    def halves(first_ref, second_ref):
        for place in range(4):
            out_ref = second_ref if place % 2 else first_ref
            out_ref[place // 2, :part, :] = jnp.dot(
                turned_ref[place * part : (place + 1) * part, :],
                low,
                preferred_element_type=jnp.float32,
            ).astype(jnp.bfloat16)

    @pl.when(core == 0)
    def low_half_first():
        halves(mine_ref, other_ref)

    @pl.when(core == 1)
    def high_half_first():
        halves(other_ref, mine_ref)


def forward_step(step, powers_ref, all_ref, own_ref, weights, bias_ref, turned, mixed):
    terms, own_cap, span = powers_ref.shape
    fan_in = own_ref.shape[1]

    @pl.when(step == 0)
    def first():
        turned[:fan_in, :] = own_ref[...].T
        mixed[...] = bias_ref[...] + jnp.dot(
            own_ref[...], weights[0][0], preferred_element_type=jnp.float32
        )

    low = jnp.dot(
        powers_ref[...].reshape(terms * own_cap, span),
        all_ref[...],
        preferred_element_type=jnp.float32,
    ).astype(jnp.bfloat16)
    total = mixed[...]
    for term in range(terms):
        part = low[term * own_cap : (term + 1) * own_cap]
        start = pl.multiple_of((1 + step * terms + term) * fan_in, fan_in)
        turned[pl.ds(start, fan_in), :] = part.T
        total = total + jnp.dot(part, weights[1 + term][0], preferred_element_type=jnp.float32)
    mixed[...] = total


def layer_one_kernel(
    powers_ref,
    all_ref,
    own_ref,
    weight_0,
    weight_a,
    weight_b,
    weight_c,
    bias_ref,
    gain_ref,
    shift_ref,
    valid_ref,
    hidden_ref,
    turned_ref,
    mixed_ref,
):
    step = pl.program_id(0)
    weights = (weight_0, weight_a, weight_b, weight_c)
    forward_step(step, powers_ref, all_ref, own_ref, weights, bias_ref, turned_ref, mixed_ref)

    @pl.when(step == pl.num_programs(0) - 1)
    def finish_layer():
        normed, ignored = norm_forward(mixed_ref[...])
        hidden = (normed * gain_ref[...] + shift_ref[...]) * valid_ref[...]
        hidden_ref[...] = hidden.astype(jnp.bfloat16)


def layer_two_kernel(
    place_ref,
    powers_ref,
    all_ref,
    own_ref,
    weight_0,
    weight_a,
    weight_b,
    weight_c,
    bias_ref,
    gain_ref,
    shift_ref,
    valid_ref,
    upstream_ref,
    active_ref,
    low_ref,
    rest_ref,
    mine_ref,
    other_ref,
    turned,
    mixed,
):
    step = pl.program_id(0)
    weights = (weight_0, weight_a, weight_b, weight_c)
    forward_step(step, powers_ref, all_ref, own_ref, weights, bias_ref, turned, mixed)

    @pl.when(step == pl.num_programs(0) - 1)
    def finish_layer():
        normed, ignored = norm_forward(mixed[...])
        active = (normed * gain_ref[...] + shift_ref[...]) * valid_ref[...]
        active_ref[...] = active.astype(jnp.bfloat16)
        low, rest = norm_backward(
            mixed[...], upstream_ref[...].astype(jnp.float32), gain_ref[...], valid_ref[...]
        )
        low_ref[...] = low
        for place in range(3):
            rest_ref[place : place + 1, :] = rest[place]
        weight_gradient(turned, low, place_ref[1], mine_ref, other_ref)


def backward_step(step, powers_ref, all_ref, own_ref, weights, total):
    terms, own_cap, span = powers_ref.shape
    transposed = (((1,), (1,)), ((), ()))

    @pl.when(step == 0)
    def first():
        total[...] = lax.dot_general(
            own_ref[...], weights[0][0], transposed, preferred_element_type=jnp.float32
        )

    low = jnp.dot(
        powers_ref[...].reshape(terms * own_cap, span),
        all_ref[...],
        preferred_element_type=jnp.float32,
    ).astype(jnp.bfloat16)
    value = total[...]
    for term in range(terms):
        value = value + lax.dot_general(
            low[term * own_cap : (term + 1) * own_cap],
            weights[1 + term][0],
            transposed,
            preferred_element_type=jnp.float32,
        )
    total[...] = value


def back_two_kernel(
    place_ref,
    powers_ref,
    all_ref,
    own_ref,
    weight_0,
    weight_a,
    weight_b,
    weight_c,
    turned_ref,
    mixed_ref,
    gain_ref,
    valid_ref,
    rest_ref,
    low_ref,
    mine_ref,
    other_ref,
    total,
):
    step = pl.program_id(0)
    weights = (weight_0, weight_a, weight_b, weight_c)
    backward_step(step, powers_ref, all_ref, own_ref, weights, total)

    @pl.when(step == pl.num_programs(0) - 1)
    def finish_layer():
        low, rest = norm_backward(mixed_ref[...], total[...], gain_ref[...], valid_ref[...])
        low_ref[...] = low
        weight_gradient(turned_ref, low, place_ref[1], mine_ref, other_ref)
        part = turned_ref.shape[0] // 4
        extra = jnp.zeros((2, mine_ref.shape[1] - part, mine_ref.shape[2]), jnp.bfloat16)
        rows = rest + [rest_ref[place : place + 1, :] for place in range(3)]
        rows = jnp.concatenate(rows + [jnp.zeros((10, rows[0].shape[1]), jnp.float32)], axis=0)

        def below(first_ref, second_ref):
            first_ref[:, part:, :] = extra
            second_ref[:, part:, :] = extra
            first_ref[0, part : part + 16, :] = rows.astype(jnp.bfloat16)

        @pl.when(place_ref[1] == 0)
        def low_half_here():
            below(mine_ref, other_ref)

        @pl.when(place_ref[1] == 1)
        def low_half_there():
            below(other_ref, mine_ref)


def back_one_kernel(
    powers_ref, all_ref, own_ref, weight_0, weight_a, weight_b, weight_c, out_ref, total
):
    step = pl.program_id(0)
    weights = (weight_0, weight_a, weight_b, weight_c)
    backward_step(step, powers_ref, all_ref, own_ref, weights, total)

    @pl.when(step == pl.num_programs(0) - 1)
    def finish_layer():
        out_ref[...] = total[...].astype(jnp.bfloat16)


def layer_pass(kernel, name, place, powers, everyone, own, weight, others, outs, scratch):
    ignored, own_cap, span = powers.shape
    fan_in, width = weight.shape[1:]

    def whole(value):
        return pl.BlockSpec(value.shape, lambda step: (0,) * len(value.shape))

    def term_weight(term):
        return pl.BlockSpec((1, fan_in, width), lambda step: (1 + step * TERMS + term, 0, 0))

    in_specs = [
        pl.BlockSpec((TERMS, own_cap, span), lambda step: (step, 0, 0)),
        whole(everyone),
        whole(own),
        pl.BlockSpec((1, fan_in, width), lambda step: (0, 0, 0)),
    ]
    in_specs += [term_weight(term) for term in range(TERMS)] + [whole(value) for value in others]
    operands = [powers, everyone, own] + [weight] * (1 + TERMS) + list(others)
    if place is not None:
        in_specs = [pl.BlockSpec(memory_space=pltpu.SMEM)] + in_specs
        operands = [place] + operands
    return pl.pallas_call(
        kernel,
        grid=((ORDER - 1) // TERMS,),
        out_shape=outs,
        in_specs=in_specs,
        out_specs=[whole(value) for value in outs],
        scratch_shapes=[pltpu.VMEM(shape, dtype) for shape, dtype in scratch],
        compiler_params=pltpu.CompilerParams(vmem_limit_bytes=VMEM_BYTES),
        cost_estimate=NO_COST,
        name=name,
    )(*operands)


def finish_kernel(fits_ref, lower_ref, upper_ref, other_ref, out_ref, *small_refs):
    part, half = out_ref.shape[1], lower_ref.shape[1]

    @pl.when(fits_ref[0] == 1)
    def fast_form():
        out_ref[0, :half, :] = lower_ref[0].astype(jnp.float32)
        out_ref[0, half:, :] = upper_ref[0, : part - half, :].astype(jnp.float32)

    for small_ref in small_refs:
        @pl.when(pl.program_id(0) == 0)
        def small_sums():
            start = part - half
            small_ref[...] = upper_ref[0, start : start + 16, :].astype(jnp.float32)

    @pl.when(fits_ref[0] == 0)
    def general_form():
        out_ref[0] = other_ref[0].astype(jnp.float32)


def finished(fits, gathered, other, with_small=False):
    count, part, width = other.shape
    out, held = (1, part, width), (1,) + gathered.shape[1:]
    out_specs = [pl.BlockSpec(out, lambda step, ref: (step, 0, 0))]
    out_shape = [jax.ShapeDtypeStruct(other.shape, jnp.float32)]
    if with_small:
        out_specs.append(pl.BlockSpec((16, width), lambda step, ref: (0, 0)))
        out_shape.append(jax.ShapeDtypeStruct((16, width), jnp.float32))
    return pl.pallas_call(
        finish_kernel,
        grid_spec=pltpu.PrefetchScalarGridSpec(
            num_scalar_prefetch=1,
            grid=(count,),
            in_specs=[
                pl.BlockSpec(held, lambda step, ref: (step, 0, 0)),
                pl.BlockSpec(held, lambda step, ref: (count + step, 0, 0)),
                pl.BlockSpec(out, lambda step, ref: ((1 - ref[0]) * step, 0, 0)),
            ],
            out_specs=out_specs,
        ),
        out_shape=out_shape,
        compiler_params=pltpu.CompilerParams(vmem_limit_bytes=VMEM_BYTES),
        cost_estimate=NO_COST,
        name="finished",
    )(fits, gathered, gathered, other)


def unpack_kernel(place_ref, pieces_ref, keys_ref, own_ref, quadrant_ref, columns, hot):
    groups, high, lanes = pieces_ref.shape
    own_cap, span = own_ref.shape
    whole = own_cap // lanes
    send_cap = keys_ref.shape[1] // groups
    half, rest = send_cap // 2, own_cap - whole * lanes
    for group in range(groups):
        start = group * send_cap
        for tile in range(whole):
            columns[start : start + send_cap, tile * lanes : (tile + 1) * lanes] = pieces_ref[
                group, tile * send_cap : (tile + 1) * send_cap, :
            ]
        ends = pieces_ref[group, whole * send_cap :, :]
        columns[start : start + half, whole * lanes :] = ends[:, :rest]
        columns[start + half : start + send_cap, whole * lanes :] = ends[:, rest:]
    standing = lax.broadcasted_iota(jnp.int32, hot.shape, 0)
    hot[...] = jnp.where(standing == keys_ref[...], 1.0, 0.0).astype(jnp.bfloat16)
    block = jnp.dot(hot[...], columns[...], preferred_element_type=jnp.float32)
    own_ref[...] = block.T.astype(jnp.bfloat16)
    middle = span // 2

    @pl.when(place_ref[0] == 0)
    def first():
        quadrant_ref[...] = own_ref[:, :middle]

    @pl.when(place_ref[0] == 1)
    def second():
        quadrant_ref[...] = own_ref[:, middle:]


def unpacked_block(pieces, keys, place, own_cap, span):
    vector = pl.BlockSpec(memory_space=pltpu.VMEM)
    return pl.pallas_call(
        unpack_kernel,
        out_shape=[
            jax.ShapeDtypeStruct((own_cap, span), jnp.bfloat16),
            jax.ShapeDtypeStruct((own_cap, span // 2), jnp.bfloat16),
        ],
        in_specs=[pl.BlockSpec(memory_space=pltpu.SMEM), vector, vector],
        out_specs=[vector, vector],
        scratch_shapes=[
            pltpu.VMEM((keys.shape[1], own_cap), jnp.bfloat16),
            pltpu.VMEM((span, keys.shape[1]), jnp.bfloat16),
        ],
        compiler_params=pltpu.CompilerParams(vmem_limit_bytes=VMEM_BYTES),
        cost_estimate=NO_COST,
        name="unpacked_block",
    )(place, pieces, keys)


def fit_kernel(codes_ref, out_ref, *, n_row, caps):
    own_cap, send_cap, seat_cap = caps
    codes = codes_ref[...]
    devices = codes.shape[0]
    n_col = devices // n_row
    label = lax.broadcasted_iota(jnp.int32, (devices, 128), 1)
    counts = jnp.zeros((devices, 128), jnp.float32)
    for cluster in range(CLUSTERS):
        here = jnp.where(codes == 2 * cluster + 1, 1.0, 0.0)
        counts = counts + jnp.where(
            label == cluster, jnp.sum(here, axis=1, keepdims=True), 0.0
        )
    sizes = jnp.sum(counts, axis=0, keepdims=True)
    across = jnp.broadcast_to(sizes, (128, 128))
    down = across.T
    first = lax.broadcasted_iota(jnp.int32, (128, 128), 0)
    second = lax.broadcasted_iota(jnp.int32, (128, 128), 1)
    ahead = (across > down) | ((across == down) & (second < first))
    ahead = ahead & (second < CLUSTERS)
    rank = jnp.sum(jnp.where(ahead, 1.0, 0.0), axis=1, keepdims=True).astype(jnp.int32)
    others = n_row - 1
    later = rank > others
    turn = jnp.zeros_like(rank)
    for count in range(1, CLUSTERS // others + 1):
        turn = turn + jnp.where(rank - 1 >= count * others, 1, 0)
    place = rank - 1 - turn * others
    group = jnp.where(rank == 0, 0, 1 + jnp.where(later, others - 1 - place, place))
    member = (group == second) & (first < CLUSTERS)
    held = jnp.dot(
        counts.astype(jnp.bfloat16),
        jnp.where(member, 1.0, 0.0).astype(jnp.bfloat16),
        preferred_element_type=jnp.float32,
    )
    by_row = jnp.zeros((1, 128), jnp.float32)
    for row in range(n_row):
        rows = jnp.sum(held[row * n_col : (row + 1) * n_col], axis=0, keepdims=True)
        by_row = jnp.maximum(by_row, rows)
    device = lax.broadcasted_iota(jnp.int32, (devices, 128), 0)
    by_col = jnp.zeros((1, 128), jnp.float32)
    for col in range(n_col):
        cols = jnp.where(device % n_col == col, held, 0.0)
        by_col = jnp.maximum(by_col, jnp.sum(cols, axis=0, keepdims=True))
    fits = (
        (jnp.max(by_col) <= own_cap) & (jnp.max(by_row) <= send_cap) & (jnp.max(held) <= seat_cap)
    )
    out_ref[0] = jnp.where(fits, 1, 0)


def fits_in(codes, n_row, caps):
    fits = pl.pallas_call(
        functools.partial(fit_kernel, n_row=n_row, caps=caps),
        out_shape=jax.ShapeDtypeStruct((1,), jnp.int32),
        in_specs=[pl.BlockSpec(memory_space=pltpu.VMEM)],
        out_specs=pl.BlockSpec(memory_space=pltpu.SMEM),
        cost_estimate=NO_COST,
        name="fits",
    )(codes.reshape(-1, codes.shape[-1]))
    return fits


def exclusive_counts(member):
    count = member.shape[-1]
    before = jnp.arange(count)[:, None] < jnp.arange(count)[None, :]
    return jnp.dot(
        member.astype(jnp.bfloat16),
        before.astype(jnp.bfloat16),
        preferred_element_type=jnp.float32,
    ).astype(jnp.int32)


def assign(codes, n_row):
    cluster, valid = codes >> 1, codes & 1
    labels = jnp.arange(CLUSTERS)
    sizes = jnp.sum(
        (cluster.reshape(1, -1) == labels[:, None]) & (valid.reshape(1, -1) == 1), axis=1
    )
    ahead = (sizes[None, :] > sizes[:, None]) | (
        (sizes[None, :] == sizes[:, None]) & (labels[None, :] < labels[:, None])
    )
    rank = jnp.sum(ahead, axis=1)
    others = n_row - 1
    turn, place = (rank - 1) // others, (rank - 1) % others
    group = jnp.where(rank == 0, 0, 1 + jnp.where(turn == 0, place, others - 1 - place))
    of_node = jnp.sum(
        jnp.where(cluster[None] == labels[:, None, None, None], group[:, None, None, None], 0),
        axis=0,
    )
    return jnp.where(valid == 1, of_node, n_row)


def compact(
    codes,
    group,
    features,
    block_keep,
    edge_weight,
    weight_one,
    bias_one,
    gain_one,
    shift_one,
    weight_two,
    bias_two,
    gain_two,
    shift_two,
    cotangent,
    places_of,
    slots_of,
    seats_of,
    decide,
    sizes,
    caps,
):
    row, col = lax.axis_index(ROW), lax.axis_index(COL)
    chip, core, why = lax.axis_index("chip"), lax.axis_index("core"), lax.axis_index("why")
    n_row, n_col = sizes
    own_cap, send_cap, seat_cap = caps
    own_nodes, in_width = features.shape
    width = weight_two.shape[2]
    span = n_col * own_cap
    targets = jnp.arange(n_row)

    def in_col(value):
        return lax.dynamic_index_in_dim(value, col, 1, False).reshape(-1)

    def in_row(value):
        return lax.dynamic_index_in_dim(value, row, 0, False).reshape(-1)

    row_group, col_group = in_row(group), in_col(group)
    row_slots, col_places = in_row(slots_of(group)), in_col(places_of(group))
    row_keys = jnp.where(row_slots < send_cap, row_group * send_cap + row_slots, -1)
    col_keys = jnp.where(col_places < own_cap, col_group * own_cap + col_places, -1)
    pieces = packed_pieces(
        block_keep,
        in_row(codes),
        in_col(codes),
        row_keys,
        col_keys,
        edge_weight,
        (own_cap, send_cap),
        n_row,
    )
    pieces, codes = lax.optimization_barrier((pieces, codes))
    group = assign(codes, n_row)
    pieces = trade(pieces, ROW)
    places, slots, seats = places_of(group), slots_of(group), seats_of(group)

    standing = jnp.arange(n_col)[None, :, None] * own_cap + places
    fits_here = jnp.where(group == row, standing, -1).reshape(n_row, -1)
    slot_of = slots.reshape(n_row, -1)
    target = jnp.max(
        jnp.where(
            slot_of[:, None, :] == jnp.arange(send_cap)[None, :, None], fits_here[:, None, :], -1
        ),
        axis=2,
    )
    keys = target.reshape(1, -1)

    def to_partner(value, step):
        return lax.ppermute(value, ROW, [(place, place ^ step) for place in range(n_row)])

    partners = row ^ targets
    group_here = lax.dynamic_index_in_dim(in_row(group).reshape(n_col, -1), col, 0, False)
    seat_here = lax.dynamic_index_in_dim(in_row(seats).reshape(n_col, -1), col, 0, False)

    def seat_of_node(groups):
        hot = (group_here[None, None, :] == groups[:, None, None]) & (
            seat_here[None, None, :] == jnp.arange(seat_cap)[None, :, None]
        )
        return hot.astype(jnp.bfloat16).reshape(n_row * seat_cap, own_nodes)

    enter_partner = seat_of_node(partners)
    both = jnp.dot(enter_partner, jnp.concatenate([features, cotangent], axis=1))
    both = both.reshape(n_row, seat_cap, -1)
    enter_partner = enter_partner.T
    both, codes = lax.optimization_barrier((both, codes))
    fits, others = decide(codes)
    enter_home = seat_of_node(targets ^ why).T
    group_col = lax.dynamic_index_in_dim(group, col, 1, False)
    seats_col = lax.dynamic_index_in_dim(seats, col, 1, False)
    places_col = lax.dynamic_index_in_dim(places, col, 1, False)
    seated = (group_col == row)[:, None, :] & (
        seats_col[:, None, :] == jnp.arange(seat_cap)[None, :, None]
    )
    place_of_seat = jnp.max(jnp.where(seated, places_col[:, None, :], -1), axis=2)
    from_partner = jnp.max(
        jnp.where((partners[:, None] == targets)[:, :, None], place_of_seat[None], -1), axis=1
    )
    arrive = from_partner.reshape(1, -1) == jnp.arange(own_cap)[:, None]
    arrive = arrive.astype(jnp.bfloat16)
    leave_partner = jnp.concatenate([from_partner[::2], from_partner[1::2]])
    leave_partner = leave_partner.reshape(-1, 1) == jnp.arange(own_cap)
    leave_partner = leave_partner.astype(jnp.bfloat16)
    leave_group = place_of_seat.reshape(-1, 1) == jnp.arange(own_cap)[None, :]
    leave_group = leave_group.astype(jnp.bfloat16)
    held_count = jnp.sum(group_col == row)
    valid_rows = (jnp.arange(own_cap) < held_count).astype(jnp.float32)[:, None]
    place = jnp.stack([chip, core]).astype(jnp.int32)
    scalars = (chip, 1 - chip, col * own_cap, why, 1 - why)
    scalars = tuple(value.astype(jnp.uint32) for value in scalars) + (chip == 0, core == 0, place, fits)
    homes = enter_home, enter_partner, leave_group, leave_partner
    pieces, both, keys, arrive, homes, valid_rows, others, scalars = lax.optimization_barrier(
        (pieces, both, keys, arrive, homes, valid_rows, others, scalars)
    )
    enter_home, enter_partner, leave_group, leave_partner = homes
    this_chip, other_chip, own_start, this_why, other_why = scalars[:5]
    first_chip, first_core, place, fits = scalars[5:]

    own_block, quadrant = unpacked_block(pieces, keys, place, own_cap, span)
    quadrant = swap(quadrant, "chip")
    both = [both[0]] + [to_partner(both[step], step) for step in range(1, n_row)]
    sibling = swap(own_block, "core")
    quadrant, *early = lax.optimization_barrier((quadrant, *both[:-2]))
    adjacency = normalized_block(own_block, sibling, quadrant, swap(quadrant, "core"), place)
    adjacency, *late = lax.optimization_barrier((adjacency, *both[-2:]))
    both = early + late
    mine = jnp.dot(arrive, jnp.concatenate(both))
    features_own, cotangent_own = mine[:, :in_width], mine[:, in_width:]
    sibling = swap(features_own, "core")

    first = (own_start + jnp.arange(own_cap, dtype=jnp.uint32))[:, None]
    first = first == jnp.arange(span, dtype=jnp.uint32)[None, :]
    previous = first.astype(jnp.float32)
    current = -lax.dynamic_slice_in_dim(adjacency, own_start, own_cap, 0).astype(jnp.float32)
    lowered = [current.astype(jnp.bfloat16)]
    for position in range(2, ORDER):
        upcoming = (
            -2.0 * jnp.dot(lowered[-1], adjacency, preferred_element_type=jnp.float32) - previous
        )
        low = upcoming.astype(jnp.bfloat16)
        if position == 4:
            low, sibling = lax.optimization_barrier((low, sibling))
            features_chip = joined(features_own, sibling, first_core)
            partner = swap(features_chip, "chip")
        if position == 8:
            low, partner = lax.optimization_barrier((low, partner))
            features_all = joined(features_chip, partner, first_chip)
        previous, current = current, upcoming
        lowered.append(low)
    powers = jnp.concatenate(lowered, axis=0).reshape(ORDER - 1, own_cap, span)

    def everywhere(value_low):
        return lax.all_gather(value_low, COL, axis=0, tiled=True)

    def chosen(value, other):
        return jnp.where(fits[0] == 1, value.astype(jnp.float32), other.astype(jnp.float32))

    def shaped(*shape, dtype=jnp.bfloat16):
        return jax.ShapeDtypeStruct(shape, dtype)

    part_one, part_two = ORDER * in_width // n_col, ORDER * width // n_col
    padded = -(-(part_one + 16) // (8 * n_row)) * (8 * n_row)
    hidden, turned_one, mixed_one = layer_pass(
        layer_one_kernel,
        "layer_one",
        None,
        powers,
        features_all,
        features_own,
        weight_one,
        [bias_one[None], gain_one[None], shift_one[None], valid_rows],
        [
            shaped(own_cap, width),
            shaped(n_col * part_one, own_cap),
            shaped(own_cap, width, dtype=jnp.float32),
        ],
        [],
    )
    activations, low_two, rest_two, mine, other = layer_pass(
        layer_two_kernel,
        "layer_two",
        place,
        powers,
        everywhere(hidden),
        hidden,
        weight_two,
        [bias_two[None], gain_two[None], shift_two[None], valid_rows, cotangent_own],
        [
            shaped(own_cap, width),
            shaped(own_cap, width),
            shaped(3, width, dtype=jnp.float32),
            shaped(2, part_two, width),
            shaped(2, part_two, width),
        ],
        [((n_col * part_two, own_cap), jnp.bfloat16), ((own_cap, width), jnp.float32)],
    )

    def add_cores(mine, other):
        got = swap(other, "core")
        return tuple(
            added(
                lax.dynamic_index_in_dim(mine, index, 0, False),
                lax.dynamic_index_in_dim(got, index, 0, False),
            )
            for index in (this_chip, other_chip)
        )

    leaving = jnp.dot(leave_partner, activations).reshape(n_row, seat_cap, width)
    near, far = leaving[: n_row // 2], leaving[n_row // 2 :]
    far = to_partner(far, 1)
    here, there = add_cores(mine, other)
    everyone_two, there, far = lax.optimization_barrier((everywhere(low_two), there, far))
    there = swap(there, "chip")
    arrived = [jnp.stack([near[0], far[0]])] + [
        to_partner(jnp.stack([near[half], far[half]]), 2 * half) for half in range(1, n_row // 2)
    ]
    low_one, mine, other = layer_pass(
        back_two_kernel,
        "back_two",
        place,
        powers,
        everyone_two,
        low_two,
        weight_two,
        [turned_one, mixed_one, gain_one[None], valid_rows, rest_two],
        [shaped(own_cap, width), shaped(2, padded, width), shaped(2, padded, width)],
        [((own_cap, width), jnp.float32)],
    )
    low_one, there, arrived = lax.optimization_barrier((low_one, there, arrived))
    second = added(here, there).reshape(2, n_row // 2, -1, width).swapaxes(0, 1)
    many = second.shape[2]
    second = second.reshape(n_row, many, width)
    low_one, second = lax.optimization_barrier((low_one, second))
    second = trade(second, ROW)
    here, there = add_cores(mine, other)
    low_one, there = lax.optimization_barrier((low_one, there))
    everyone_one = everywhere(low_one)
    there = swap(there, "chip")
    everyone_one, second, there = lax.optimization_barrier((everyone_one, second, there))
    first = added(here, there).reshape(2, n_row // 2, -1, width)
    share = first.shape[2]
    got = swap(lax.dynamic_index_in_dim(first, other_why, 0, False), "why")
    first = added(lax.dynamic_index_in_dim(first, this_why, 0, False), got)
    second = jnp.sum(second.astype(jnp.float32), axis=0).astype(jnp.bfloat16)
    second = jnp.broadcast_to(second[None], (n_row // 2,) + second.shape)
    mixed = jnp.concatenate([second, first], axis=1)
    everyone_one, mixed = lax.optimization_barrier((everyone_one, mixed))
    mixed = trade(mixed, "zed")
    (input_grad,) = layer_pass(
        back_one_kernel,
        "back_one",
        None,
        powers,
        everyone_one,
        low_one,
        weight_one,
        [],
        [shaped(own_cap, in_width)],
        [((own_cap, in_width), jnp.float32)],
    )
    leaving = jnp.dot(leave_group, input_grad)
    leaving = leaving.reshape(n_row // 2, 2, seat_cap * in_width // width, width)
    got = swap(lax.dynamic_index_in_dim(leaving, other_why, 1, False), "why")
    leaving = lax.dynamic_index_in_dim(leaving, this_why, 1, False)
    leaving = jnp.concatenate([leaving, got], axis=1)
    arrived = jnp.concatenate(arrived).reshape(-1, width)
    home = jnp.dot(enter_partner, arrived, preferred_element_type=jnp.float32)
    home = chosen(home, others[0])
    mixed, leaving, home = lax.optimization_barrier((mixed, leaving, home))
    first = jnp.sum(mixed[:, many:].astype(jnp.float32), axis=0).astype(jnp.bfloat16)
    first = jnp.broadcast_to(first[None], (n_row // 2,) + first.shape)
    first, mixed = lax.optimization_barrier((jnp.concatenate([first, leaving], axis=1), mixed))
    first = trade(first, "zed")
    second = lax.all_gather(mixed[:, :many].reshape(-1, width), PLANE, axis=0)
    back = first[:, share:].reshape(n_row * seat_cap, in_width)
    first = lax.all_gather(first[:, :share].reshape(-1, width), PLANE, axis=0)
    home_grad = jnp.dot(enter_home, back, preferred_element_type=jnp.float32)
    home_grad = chosen(home_grad, others[1])
    (second,) = finished(fits, second, others[3])
    first, small = finished(fits, first, others[2], True)
    return home, home_grad, first, second, chosen(small[:6], others[4])


def general(
    codes,
    features,
    block_keep,
    edge_weight,
    weight_one,
    bias_one,
    gain_one,
    shift_one,
    weight_two,
    bias_two,
    gain_two,
    shift_two,
    cotangent,
    node_valid,
):
    row, col = lax.axis_index(ROW), lax.axis_index(COL)
    row_codes = lax.dynamic_index_in_dim(codes, row, 0, False).reshape(-1)
    col_codes = lax.dynamic_index_in_dim(codes, col, 1, False).reshape(-1)
    tile_rows, tile_cols = edge_weight.shape
    blocks_down, blocks_across = block_keep.shape
    block_side = tile_rows // blocks_down
    linked = (row_codes[:, None] == col_codes[None, :]) & (row_codes[:, None] & 1 == 1)
    linked = linked.reshape(blocks_down, block_side, blocks_across, block_side) & (
        block_keep[:, None, :, None] == 1
    )
    masked = edge_weight * linked.reshape(tile_rows, tile_cols).astype(jnp.bfloat16)
    degree_rows = 1.0 + lax.psum(jnp.sum(masked, axis=1, dtype=jnp.float32), COL)
    own_nodes = features.shape[0]
    own_degree = lax.dynamic_slice_in_dim(
        degree_rows, lax.axis_index(COL) * own_nodes, own_nodes, 0
    )
    degree_cols = lax.all_gather(own_degree, ROW, axis=0, tiled=True)
    adjacency = (
        masked.astype(jnp.float32)
        * lax.rsqrt(degree_rows)[:, None]
        * lax.rsqrt(degree_cols)[None, :]
    ).astype(jnp.bfloat16)
    valid_rows = node_valid.astype(jnp.float32)
    stacked_one, mixed_one, hidden = layer_forward(
        adjacency,
        features.astype(jnp.float32),
        weight_one,
        bias_one,
        gain_one,
        shift_one,
        valid_rows,
    )
    stacked_two, mixed_two, activations = layer_forward(
        adjacency, hidden, weight_two, bias_two, gain_two, shift_two, valid_rows
    )
    hidden_grad, weight_two_grad, bias_two_grad, gain_two_grad, shift_two_grad = layer_backward(
        adjacency,
        stacked_two,
        mixed_two,
        cotangent.astype(jnp.float32),
        weight_two,
        gain_two,
        shift_two,
        valid_rows,
    )
    input_grad, weight_one_grad, bias_one_grad, gain_one_grad, shift_one_grad = layer_backward(
        adjacency, stacked_one, mixed_one, hidden_grad, weight_one, gain_one, shift_one, valid_rows
    )
    summed = lax.psum(
        (
            weight_one_grad,
            bias_one_grad,
            gain_one_grad,
            shift_one_grad,
            weight_two_grad,
            bias_two_grad,
            gain_two_grad,
            shift_two_grad,
        ),
        ROW + COL,
    )
    weight_one_grad, bias_one_grad, gain_one_grad, shift_one_grad = (
        summed[0],
        summed[1],
        summed[2],
        summed[3],
    )
    weight_two_grad, bias_two_grad, gain_two_grad, shift_two_grad = (
        summed[4],
        summed[5],
        summed[6],
        summed[7],
    )
    return (
        activations,
        input_grad,
        weight_one_grad,
        bias_one_grad,
        gain_one_grad,
        shift_one_grad,
        weight_two_grad,
        bias_two_grad,
        gain_two_grad,
        shift_two_grad,
    )


def local(n_row, n_col, *args):
    (
        features,
        node_valid,
        cluster,
        block_keep,
        edge_weight,
        weight_one,
        bias_one,
        gain_one,
        shift_one,
        weight_two,
        bias_two,
        gain_two,
        shift_two,
        cotangent,
    ) = args
    own_nodes, in_width = features.shape
    own_cap = own_nodes * n_row * 5 // 16
    send_cap = own_nodes * n_col * 11 // 32
    seat_cap = own_nodes // 2
    codes = broadcast_along(cluster * 2 + node_valid, ROW + COL, n_row * n_col)
    codes = codes.reshape(n_row, n_col, own_nodes)
    shared = (
        block_keep,
        edge_weight,
        weight_one,
        bias_one,
        gain_one,
        shift_one,
        weight_two,
        bias_two,
        gain_two,
        shift_two,
        cotangent,
    )

    def slow():
        return general(codes, features, *shared, node_valid)

    held = (ORDER - 1) * own_cap * own_cap * n_col * 2
    if held > HELD_BYTES or n_col != 4 or n_row < 2 or n_row & (n_row - 1):
        return slow()
    group = assign(codes, n_row)

    def member_of(group):
        return group[None] == jnp.arange(n_row)[:, None, None, None]

    def places_of(group):
        member = member_of(group).transpose(0, 2, 1, 3).reshape(n_row, n_col, -1)
        places = jnp.sum(jnp.where(member, exclusive_counts(member), 0), axis=0)
        return places.reshape(n_col, n_row, own_nodes).transpose(1, 0, 2)

    def slots_of(group):
        member = member_of(group).reshape(n_row, n_row, -1)
        slots = jnp.sum(jnp.where(member, exclusive_counts(member), 0), axis=0)
        return slots.reshape(n_row, n_col, own_nodes)

    def seats_of(group):
        member = member_of(group)
        return jnp.sum(jnp.where(member, exclusive_counts(member), 0), axis=0)

    width = weight_two.shape[2]

    def instead(state):
        made = slow()
        small = jnp.stack([made[place] for place in (3, 4, 5, 7, 8, 9)])
        return (jnp.ones_like(state[0]),) + tuple(
            value.astype(jnp.bfloat16).reshape(like.shape)
            for value, like in zip((made[0], made[1], made[2], made[6], small), state[1:])
        )

    shapes = (
        (own_nodes, width),
        (own_nodes, in_width),
        (n_col, ORDER * in_width // n_col, width),
        (n_col, ORDER * width // n_col, width),
        (6, width),
    )

    def decide(codes):
        fits = fits_in(codes, n_row, (own_cap, send_cap, seat_cap))
        others = lax.while_loop(
            lambda state: state[0][0] == 0,
            instead,
            (fits,) + tuple(jnp.zeros(shape, jnp.bfloat16) for shape in shapes),
        )[1:]
        return fits, others

    home, home_grad, first, second, small = compact(
        codes,
        group,
        features,
        *shared,
        places_of,
        slots_of,
        seats_of,
        decide,
        (n_row, n_col),
        (own_cap, send_cap, seat_cap),
    )
    return (
        home,
        home_grad,
        first.reshape(weight_one.shape),
        small[0],
        small[1],
        small[2],
        second.reshape(weight_two.shape),
        small[3],
        small[4],
        small[5],
    )


def solution(mesh):
    n_row, n_col = mesh.shape["row"], mesh.shape["col"]
    split = jax.sharding.Mesh(
        mesh.devices.reshape(n_row // 2, 2, n_col // 2, 2), ROW + COL
    )
    nodes = ROW + COL
    placed = (
        P(nodes, None),
        P(nodes),
        P(nodes),
        P(ROW, COL),
        P(ROW, COL),
        P(),
        P(),
        P(),
        P(),
        P(),
        P(),
        P(),
        P(),
        P(nodes, None),
    )
    return jax.shard_map(
        functools.partial(local, n_row, n_col),
        mesh=split,
        in_specs=placed,
        out_specs=(P(nodes, None), P(nodes, None), P(), P(), P(), P(), P(), P(), P(), P()),
        check_vma=False,
    )
```

```python
import functools
import math

import jax
import jax.numpy as jnp
from jax import lax
from jax.experimental import pallas as pl
from jax.experimental.pallas import tpu as pltpu
from jax.sharding import PartitionSpec as P

ORDER = 13
CLUSTERS = 16
HELD_BYTES = 1 << 25
VMEM_BYTES = 32 << 20
TERMS = 3
NO_COST = pl.CostEstimate(flops=1, bytes_accessed=1, transcendentals=0)
COL = ("chip", "core")


def finish(mixed, gain, shift, valid_rows):
    active = jax.nn.gelu(mixed, approximate=False)
    centered = active - jnp.mean(active, axis=-1, keepdims=True)
    variance = jnp.mean(centered * centered, axis=-1, keepdims=True)
    return (centered * lax.rsqrt(variance + 1e-05) * gain + shift) * valid_rows[:, None]


def forward_product(adjacency, piece_low):
    partial_value = jnp.dot(
        adjacency,
        lax.all_gather(piece_low, "row", axis=0, tiled=True),
        preferred_element_type=jnp.float32,
    )
    return lax.psum_scatter(partial_value, COL, scatter_dimension=0, tiled=True)


def backward_product(adjacency, piece_low):
    partial_value = lax.dot_general(
        adjacency,
        lax.all_gather(piece_low, COL, axis=0, tiled=True),
        (((0,), (0,)), ((), ())),
        preferred_element_type=jnp.float32,
    )
    return lax.psum_scatter(
        partial_value.astype(jnp.bfloat16), "row", scatter_dimension=0, tiled=True
    ).astype(jnp.float32)


def layer_forward(adjacency, inputs, weight, bias, gain, shift, valid_rows):
    first_low = inputs.astype(jnp.bfloat16)
    second = -forward_product(adjacency, first_low)
    second_low = second.astype(jnp.bfloat16)

    def advance(state_pair, unused):
        previous, current, current_low = state_pair
        upcoming = -2.0 * forward_product(adjacency, current_low) - previous
        upcoming_low = upcoming.astype(jnp.bfloat16)
        return ((current, upcoming, upcoming_low), upcoming_low)

    ignored, others = lax.scan(advance, (inputs, second, second_low), None, length=ORDER - 2)
    stacked = jnp.concatenate([first_low[None], second_low[None], others], axis=0)
    mixed = jnp.einsum("kni,kio->no", stacked, weight, preferred_element_type=jnp.float32) + bias
    return (stacked, mixed, finish(mixed, gain, shift, valid_rows))


def layer_backward(adjacency, stacked, mixed, upstream, weight, gain, shift, valid_rows):

    def local_finish(mixed_in, gain_in, shift_in):
        return finish(mixed_in, gain_in, shift_in, valid_rows)

    ignored, pullback = jax.vjp(local_finish, mixed, gain, shift)
    mixed_grad, gain_grad, shift_grad = pullback(upstream)
    mixed_low = mixed_grad.astype(jnp.bfloat16)
    bias_grad = jnp.sum(mixed_low.astype(jnp.float32), axis=0)
    weight_grad = jnp.einsum("kni,no->kio", stacked, mixed_low, preferred_element_type=jnp.float32)
    direct = jnp.einsum("no,kio->kni", mixed_low, weight, preferred_element_type=jnp.float32)

    def retreat(state_pair, direct_term):
        later_two, later_one = state_pair
        current = (
            direct_term
            - 2.0 * backward_product(adjacency, later_one.astype(jnp.bfloat16))
            - later_two
        )
        return ((later_one, current), None)

    start_pair = (jnp.zeros_like(direct[0]), direct[ORDER - 1])
    (second_grad, first_grad), unused = lax.scan(
        retreat, start_pair, direct[1 : ORDER - 1], reverse=True
    )
    input_grad = (
        direct[0] - backward_product(adjacency, first_grad.astype(jnp.bfloat16)) - second_grad
    )
    return (input_grad, weight_grad, bias_grad, gain_grad, shift_grad)


def swap(value, axis):
    return lax.ppermute(value, axis, [(0, 1), (1, 0)])


def trade(pieces, axis):
    return lax.all_to_all(pieces, axis, 0, 0, tiled=False)


def broadcast_along(value, axis, size):
    return trade(jnp.broadcast_to(value[None], (size,) + value.shape), axis)


def joined(mine, other, mine_first):
    return jnp.where(
        mine_first, jnp.concatenate([mine, other]), jnp.concatenate([other, mine])
    )


def added(mine, received):
    return (mine.astype(jnp.float32) + received.astype(jnp.float32)).astype(jnp.bfloat16)


def assemble(place_ref, own_ref, sibling_ref, near_ref, far_ref, out_ref, done):
    chip, core = place_ref[0], place_ref[1]
    own_cap, span = own_ref.shape
    half = span // 2

    def rows(of_chip, of_core):
        return pl.ds(pl.multiple_of((2 * of_chip + of_core) * own_cap, own_cap), own_cap)

    def fetch(source, of_chip, of_core, columns, place):
        target = out_ref.at[rows(of_chip, of_core), columns]
        return pltpu.make_async_copy(source, target, done.at[place])

    def quadrant_copies(here):
        there = 1 - here
        columns = pl.ds(there * half, half)
        return (
            fetch(near_ref, there, core, columns, 2),
            fetch(far_ref, there, 1 - core, columns, 3),
        )

    everything = pl.ds(0, span)
    top = (
        fetch(own_ref, chip, core, everything, 0),
        fetch(sibling_ref, chip, 1 - core, everything, 1),
    )

    def of_chip(here):
        there = 1 - here
        copies = top + quadrant_copies(here)
        for copy in copies:
            copy.start()
        for copy in copies:
            copy.wait()
        here_rows = pl.ds(here * half, half)
        for tile in range(half // 128):
            columns = pl.ds(there * half + tile * 128, 128)
            strip = out_ref[here_rows, columns]
            turned = jnp.transpose(strip.astype(jnp.float32)).astype(jnp.bfloat16)
            out_ref[columns, here_rows] = turned

    @pl.when(chip == 0)
    def first():
        of_chip(0)

    @pl.when(chip == 1)
    def second():
        of_chip(1)

    across = jnp.ones((1, span), jnp.float32)
    for tile in range(span // 128):
        across = across + jnp.sum(
            out_ref[pl.ds(tile * 128, 128), :].astype(jnp.float32), axis=0, keepdims=True
        )
    across = lax.rsqrt(across)
    for tile in range(span // 128):
        strip = out_ref[pl.ds(tile * 128, 128), :].astype(jnp.float32)
        down = lax.rsqrt(1.0 + jnp.sum(strip, axis=1, keepdims=True))
        out_ref[pl.ds(tile * 128, 128), :] = (strip * down * across).astype(jnp.bfloat16)


def normalized_block(own, sibling, near, far, place):
    span = own.shape[1]
    return pl.pallas_call(
        assemble,
        out_shape=jax.ShapeDtypeStruct((span, span), jnp.bfloat16),
        in_specs=[pl.BlockSpec(memory_space=pltpu.SMEM)]
        + [pl.BlockSpec(memory_space=pltpu.HBM)] * 4,
        out_specs=pl.BlockSpec(memory_space=pltpu.VMEM),
        scratch_shapes=[pltpu.SemaphoreType.DMA((4,))],
        compiler_params=pltpu.CompilerParams(vmem_limit_bytes=VMEM_BYTES),
        cost_estimate=NO_COST,
        name="normalized_block",
    )(place, own, sibling, near, far)


def pack_kernel(
    keep_ref, row_codes_ref, col_codes_ref, row_keys_ref, col_keys_ref, weight_ref, out_ref,
    masked, picked, rows_hot, cols_hot
):
    tile_rows, tile_cols = weight_ref.shape
    blocks_down, blocks_across = keep_ref.shape
    groups, ignored, lanes = out_ref.shape
    send_cap, own_cap = rows_hot.shape[0] // groups, cols_hot.shape[0] // groups
    high, wide = tile_rows // blocks_down, tile_cols // blocks_across
    for down in range(blocks_down):
        for across in range(blocks_across):
            rows, columns = pl.ds(down * high, high), pl.ds(across * wide, wide)
            own, other = row_codes_ref[rows, :], col_codes_ref[:, columns]
            linked = (own == other) & (own % 2 == 1) & (keep_ref[down, across] == 1)
            weight = weight_ref[rows, columns].astype(jnp.float32)
            masked[rows, columns] = jnp.where(linked, weight, 0.0).astype(jnp.bfloat16)

    def one_hot(keys, start, count):
        standing = lax.broadcasted_iota(jnp.int32, (count, keys.shape[1]), 0) + start
        return jnp.where(standing == keys, 1.0, 0.0).astype(jnp.bfloat16)

    for group in range(groups):
        rows_hot[pl.ds(group * send_cap, send_cap), :] = one_hot(
            row_keys_ref[...], group * send_cap, send_cap
        )
        cols_hot[pl.ds(group * own_cap, own_cap), :] = one_hot(
            col_keys_ref[...], group * own_cap, own_cap
        )
    for tile in range(tile_cols // 256):
        columns = pl.ds(tile * 256, 256)
        picked[:, columns] = jnp.dot(
            rows_hot[...], masked[:, columns], preferred_element_type=jnp.float32
        ).astype(jnp.bfloat16)
    whole, half = own_cap // lanes, send_cap // 2
    for group in range(groups):
        packed = lax.dot_general(
            cols_hot[pl.ds(group * own_cap, own_cap), :],
            picked[pl.ds(group * send_cap, send_cap), :],
            (((1,), (1,)), ((), ())),
            preferred_element_type=jnp.float32,
        ).T
        for tile in range(whole):
            out_ref[group, pl.ds(tile * send_cap, send_cap), :] = packed[
                :, tile * lanes : (tile + 1) * lanes
            ].astype(jnp.bfloat16)
        ends = jnp.concatenate(
            [packed[:half, whole * lanes :], packed[half:, whole * lanes :]], axis=1
        )
        out_ref[group, pl.ds(whole * send_cap, half), :] = ends.astype(jnp.bfloat16)


def packed_pieces(block_keep, row_codes, col_codes, row_keys, col_keys, edge_weight, caps, groups):
    own_cap, send_cap = caps
    tile_rows, tile_cols = edge_weight.shape
    high = own_cap // 128 * send_cap + send_cap // 2
    vector = pl.BlockSpec(memory_space=pltpu.VMEM)
    return pl.pallas_call(
        pack_kernel,
        out_shape=jax.ShapeDtypeStruct((groups, high, 128), jnp.bfloat16),
        in_specs=[pl.BlockSpec(memory_space=pltpu.SMEM)] + [vector] * 5,
        out_specs=vector,
        scratch_shapes=[
            pltpu.VMEM((tile_rows, tile_cols), jnp.bfloat16),
            pltpu.VMEM((groups * send_cap, tile_cols), jnp.bfloat16),
            pltpu.VMEM((groups * send_cap, tile_rows), jnp.bfloat16),
            pltpu.VMEM((groups * own_cap, tile_cols), jnp.bfloat16),
        ],
        compiler_params=pltpu.CompilerParams(vmem_limit_bytes=VMEM_BYTES),
        cost_estimate=NO_COST,
        name="packed_pieces",
    )(block_keep, row_codes[:, None], col_codes[None], row_keys[None], col_keys[None], edge_weight)


def normal_share(mixed):
    return 0.5 * (1.0 + lax.erf(mixed * 0.5**0.5))


def norm_forward(mixed):
    active = mixed * normal_share(mixed)
    centered = active - jnp.mean(active, axis=-1, keepdims=True)
    scale = lax.rsqrt(jnp.mean(centered * centered, axis=-1, keepdims=True) + 1e-05)
    return centered * scale, scale


def norm_backward(mixed, upstream, gain, valid):
    normed, scale = norm_forward(mixed)
    upstream = upstream * valid
    inner = upstream * gain
    inner = inner - jnp.mean(inner, axis=-1, keepdims=True) - normed * jnp.mean(
        inner * normed, axis=-1, keepdims=True
    )
    density = jnp.exp(-0.5 * mixed * mixed) * (1.0 / (2.0 * math.pi) ** 0.5)
    low = (inner * scale * (normal_share(mixed) + mixed * density)).astype(jnp.bfloat16)
    rest = [low.astype(jnp.float32), upstream * normed, upstream]
    return low, [jnp.sum(value, axis=0, keepdims=True) for value in rest]


def weight_gradient(turned_ref, low, core, mine_ref, other_ref):
    part = turned_ref.shape[0] // 4

    def halves(first_ref, second_ref):
        for place in range(4):
            out_ref = second_ref if place % 2 else first_ref
            out_ref[place // 2, :part, :] = jnp.dot(
                turned_ref[place * part : (place + 1) * part, :],
                low,
                preferred_element_type=jnp.float32,
            ).astype(jnp.bfloat16)

    @pl.when(core == 0)
    def low_half_first():
        halves(mine_ref, other_ref)

    @pl.when(core == 1)
    def high_half_first():
        halves(other_ref, mine_ref)


def forward_step(step, powers_ref, all_ref, own_ref, weights, bias_ref, turned, mixed):
    terms, own_cap, span = powers_ref.shape
    fan_in = own_ref.shape[1]

    @pl.when(step == 0)
    def first():
        turned[:fan_in, :] = own_ref[...].T
        mixed[...] = bias_ref[...] + jnp.dot(
            own_ref[...], weights[0][0], preferred_element_type=jnp.float32
        )

    low = jnp.dot(
        powers_ref[...].reshape(terms * own_cap, span),
        all_ref[...],
        preferred_element_type=jnp.float32,
    ).astype(jnp.bfloat16)
    total = mixed[...]
    for term in range(terms):
        part = low[term * own_cap : (term + 1) * own_cap]
        start = pl.multiple_of((1 + step * terms + term) * fan_in, fan_in)
        turned[pl.ds(start, fan_in), :] = part.T
        total = total + jnp.dot(part, weights[1 + term][0], preferred_element_type=jnp.float32)
    mixed[...] = total


def layer_one_kernel(
    powers_ref,
    all_ref,
    own_ref,
    weight_0,
    weight_a,
    weight_b,
    weight_c,
    bias_ref,
    gain_ref,
    shift_ref,
    valid_ref,
    hidden_ref,
    turned_ref,
    mixed_ref,
):
    step = pl.program_id(0)
    weights = (weight_0, weight_a, weight_b, weight_c)
    forward_step(step, powers_ref, all_ref, own_ref, weights, bias_ref, turned_ref, mixed_ref)

    @pl.when(step == pl.num_programs(0) - 1)
    def finish_layer():
        normed, ignored = norm_forward(mixed_ref[...])
        hidden = (normed * gain_ref[...] + shift_ref[...]) * valid_ref[...]
        hidden_ref[...] = hidden.astype(jnp.bfloat16)


def layer_two_kernel(
    place_ref,
    powers_ref,
    all_ref,
    own_ref,
    weight_0,
    weight_a,
    weight_b,
    weight_c,
    bias_ref,
    gain_ref,
    shift_ref,
    valid_ref,
    upstream_ref,
    active_ref,
    low_ref,
    rest_ref,
    mine_ref,
    other_ref,
    turned,
    mixed,
):
    step = pl.program_id(0)
    weights = (weight_0, weight_a, weight_b, weight_c)
    forward_step(step, powers_ref, all_ref, own_ref, weights, bias_ref, turned, mixed)

    @pl.when(step == pl.num_programs(0) - 1)
    def finish_layer():
        normed, ignored = norm_forward(mixed[...])
        active = (normed * gain_ref[...] + shift_ref[...]) * valid_ref[...]
        active_ref[...] = active.astype(jnp.bfloat16)
        low, rest = norm_backward(
            mixed[...], upstream_ref[...].astype(jnp.float32), gain_ref[...], valid_ref[...]
        )
        low_ref[...] = low
        for place in range(3):
            rest_ref[place : place + 1, :] = rest[place]
        weight_gradient(turned, low, place_ref[1], mine_ref, other_ref)


def backward_step(step, powers_ref, all_ref, own_ref, weights, total):
    terms, own_cap, span = powers_ref.shape
    transposed = (((1,), (1,)), ((), ()))

    @pl.when(step == 0)
    def first():
        total[...] = lax.dot_general(
            own_ref[...], weights[0][0], transposed, preferred_element_type=jnp.float32
        )

    low = jnp.dot(
        powers_ref[...].reshape(terms * own_cap, span),
        all_ref[...],
        preferred_element_type=jnp.float32,
    ).astype(jnp.bfloat16)
    value = total[...]
    for term in range(terms):
        value = value + lax.dot_general(
            low[term * own_cap : (term + 1) * own_cap],
            weights[1 + term][0],
            transposed,
            preferred_element_type=jnp.float32,
        )
    total[...] = value


def back_two_kernel(
    place_ref,
    powers_ref,
    all_ref,
    own_ref,
    weight_0,
    weight_a,
    weight_b,
    weight_c,
    turned_ref,
    mixed_ref,
    gain_ref,
    valid_ref,
    rest_ref,
    low_ref,
    mine_ref,
    other_ref,
    total,
):
    step = pl.program_id(0)
    weights = (weight_0, weight_a, weight_b, weight_c)
    backward_step(step, powers_ref, all_ref, own_ref, weights, total)

    @pl.when(step == pl.num_programs(0) - 1)
    def finish_layer():
        low, rest = norm_backward(mixed_ref[...], total[...], gain_ref[...], valid_ref[...])
        low_ref[...] = low
        weight_gradient(turned_ref, low, place_ref[1], mine_ref, other_ref)
        part = turned_ref.shape[0] // 4
        extra = jnp.zeros((2, mine_ref.shape[1] - part, mine_ref.shape[2]), jnp.bfloat16)
        rows = rest + [rest_ref[place : place + 1, :] for place in range(3)]
        rows = jnp.concatenate(rows + [jnp.zeros((10, rows[0].shape[1]), jnp.float32)], axis=0)

        def below(first_ref, second_ref):
            first_ref[:, part:, :] = extra
            second_ref[:, part:, :] = extra
            first_ref[0, part : part + 16, :] = rows.astype(jnp.bfloat16)

        @pl.when(place_ref[1] == 0)
        def low_half_here():
            below(mine_ref, other_ref)

        @pl.when(place_ref[1] == 1)
        def low_half_there():
            below(other_ref, mine_ref)


def back_one_kernel(
    powers_ref, all_ref, own_ref, weight_0, weight_a, weight_b, weight_c, out_ref, total
):
    step = pl.program_id(0)
    weights = (weight_0, weight_a, weight_b, weight_c)
    backward_step(step, powers_ref, all_ref, own_ref, weights, total)

    @pl.when(step == pl.num_programs(0) - 1)
    def finish_layer():
        out_ref[...] = total[...].astype(jnp.bfloat16)


def layer_pass(kernel, name, place, powers, everyone, own, weight, others, outs, scratch):
    ignored, own_cap, span = powers.shape
    fan_in, width = weight.shape[1:]

    def whole(value):
        return pl.BlockSpec(value.shape, lambda step: (0,) * len(value.shape))

    def term_weight(term):
        return pl.BlockSpec((1, fan_in, width), lambda step: (1 + step * TERMS + term, 0, 0))

    in_specs = [
        pl.BlockSpec((TERMS, own_cap, span), lambda step: (step, 0, 0)),
        whole(everyone),
        whole(own),
        pl.BlockSpec((1, fan_in, width), lambda step: (0, 0, 0)),
    ]
    in_specs += [term_weight(term) for term in range(TERMS)] + [whole(value) for value in others]
    operands = [powers, everyone, own] + [weight] * (1 + TERMS) + list(others)
    if place is not None:
        in_specs = [pl.BlockSpec(memory_space=pltpu.SMEM)] + in_specs
        operands = [place] + operands
    return pl.pallas_call(
        kernel,
        grid=((ORDER - 1) // TERMS,),
        out_shape=outs,
        in_specs=in_specs,
        out_specs=[whole(value) for value in outs],
        scratch_shapes=[pltpu.VMEM(shape, dtype) for shape, dtype in scratch],
        compiler_params=pltpu.CompilerParams(vmem_limit_bytes=VMEM_BYTES),
        cost_estimate=NO_COST,
        name=name,
    )(*operands)


def finish_kernel(scalars_ref, *refs):
    step = pl.program_id(0)
    if len(refs) == 3:
        values_ref, other_ref, out_ref = refs
        parts = [(step >= 0, values_ref)]
        small_ref = None
    else:
        pair_ref, siblings_ref, other_ref, out_ref, small_ref = refs
        parts = [(step < 2, pair_ref), (step >= 2, siblings_ref)]
    part = out_ref.shape[1]
    for here, values_ref in parts:
        @pl.when(here & (scalars_ref[0] == 1))
        def fast_form():
            out_ref[0] = values_ref[0, :part, :].astype(jnp.float32)

        if small_ref is not None:
            @pl.when(here & (scalars_ref[1 + step] == 0))
            def small_sums():
                small_ref[...] = values_ref[0, part : part + 16, :].astype(jnp.float32)

    @pl.when(scalars_ref[0] == 0)
    def general_form():
        out_ref[0] = other_ref[0].astype(jnp.float32)


def finished(scalars, pair, values, other):
    count, part, width = other.shape
    one = (1, part, width)
    if pair is None:
        operands, outs = [values, other], [jax.ShapeDtypeStruct(other.shape, jnp.float32)]

        def quarter(step, scalars_ref):
            return step

        in_specs = [pl.BlockSpec((1,) + values.shape[1:], lambda step, ref: (step, 0, 0))]
        small_specs = []
    else:
        operands = [pair, values, other]
        outs = [
            jax.ShapeDtypeStruct(other.shape, jnp.float32),
            jax.ShapeDtypeStruct((16, width), jnp.float32),
        ]

        def quarter(step, scalars_ref):
            return scalars_ref[1 + step]

        in_specs = [
            pl.BlockSpec((1,) + pair.shape[1:], lambda step, ref: (jnp.minimum(step, 1), 0, 0)),
            pl.BlockSpec((1,) + pair.shape[1:], lambda step, ref: (jnp.maximum(step - 2, 0), 0, 0)),
        ]
        small_specs = [pl.BlockSpec((16, width), lambda step, ref: (0, 0))]
    in_specs.append(
        pl.BlockSpec(one, lambda step, ref: ((1 - ref[0]) * quarter(step, ref), 0, 0))
    )
    result = pl.pallas_call(
        finish_kernel,
        grid_spec=pltpu.PrefetchScalarGridSpec(
            num_scalar_prefetch=1,
            grid=(count,),
            in_specs=in_specs,
            out_specs=[pl.BlockSpec(one, lambda step, ref: (quarter(step, ref), 0, 0))]
            + small_specs,
        ),
        out_shape=outs,
        compiler_params=pltpu.CompilerParams(vmem_limit_bytes=VMEM_BYTES),
        cost_estimate=NO_COST,
        name="finished",
    )(scalars, *operands)
    return result[0] if pair is None else result


def unpack_kernel(place_ref, pieces_ref, keys_ref, own_ref, quadrant_ref, columns, hot):
    groups, high, lanes = pieces_ref.shape
    own_cap, span = own_ref.shape
    whole = own_cap // lanes
    send_cap = keys_ref.shape[1] // groups
    half, rest = send_cap // 2, own_cap - whole * lanes
    for group in range(groups):
        start = group * send_cap
        for tile in range(whole):
            columns[start : start + send_cap, tile * lanes : (tile + 1) * lanes] = pieces_ref[
                group, tile * send_cap : (tile + 1) * send_cap, :
            ]
        ends = pieces_ref[group, whole * send_cap :, :]
        columns[start : start + half, whole * lanes :] = ends[:, :rest]
        columns[start + half : start + send_cap, whole * lanes :] = ends[:, rest:]
    standing = lax.broadcasted_iota(jnp.int32, hot.shape, 0)
    hot[...] = jnp.where(standing == keys_ref[...], 1.0, 0.0).astype(jnp.bfloat16)
    block = jnp.dot(hot[...], columns[...], preferred_element_type=jnp.float32)
    own_ref[...] = block.T.astype(jnp.bfloat16)
    middle = span // 2

    @pl.when(place_ref[0] == 0)
    def first():
        quadrant_ref[...] = own_ref[:, :middle]

    @pl.when(place_ref[0] == 1)
    def second():
        quadrant_ref[...] = own_ref[:, middle:]


def unpacked_block(pieces, keys, place, own_cap, span):
    vector = pl.BlockSpec(memory_space=pltpu.VMEM)
    return pl.pallas_call(
        unpack_kernel,
        out_shape=[
            jax.ShapeDtypeStruct((own_cap, span), jnp.bfloat16),
            jax.ShapeDtypeStruct((own_cap, span // 2), jnp.bfloat16),
        ],
        in_specs=[pl.BlockSpec(memory_space=pltpu.SMEM), vector, vector],
        out_specs=[vector, vector],
        scratch_shapes=[
            pltpu.VMEM((keys.shape[1], own_cap), jnp.bfloat16),
            pltpu.VMEM((span, keys.shape[1]), jnp.bfloat16),
        ],
        compiler_params=pltpu.CompilerParams(vmem_limit_bytes=VMEM_BYTES),
        cost_estimate=NO_COST,
        name="unpacked_block",
    )(place, pieces, keys)


def fit_kernel(codes_ref, out_ref, *, n_row, caps):
    own_cap, send_cap, seat_cap = caps
    codes = codes_ref[...]
    devices = codes.shape[0]
    n_col = devices // n_row
    label = lax.broadcasted_iota(jnp.int32, (devices, 128), 1)
    counts = jnp.zeros((devices, 128), jnp.float32)
    for cluster in range(CLUSTERS):
        here = jnp.where(codes == 2 * cluster + 1, 1.0, 0.0)
        counts = counts + jnp.where(
            label == cluster, jnp.sum(here, axis=1, keepdims=True), 0.0
        )
    sizes = jnp.sum(counts, axis=0, keepdims=True)
    across = jnp.broadcast_to(sizes, (128, 128))
    down = across.T
    first = lax.broadcasted_iota(jnp.int32, (128, 128), 0)
    second = lax.broadcasted_iota(jnp.int32, (128, 128), 1)
    ahead = (across > down) | ((across == down) & (second < first))
    ahead = ahead & (second < CLUSTERS)
    rank = jnp.sum(jnp.where(ahead, 1.0, 0.0), axis=1, keepdims=True).astype(jnp.int32)
    others = n_row - 1
    later = rank > others
    turn = jnp.zeros_like(rank)
    for count in range(1, CLUSTERS // others + 1):
        turn = turn + jnp.where(rank - 1 >= count * others, 1, 0)
    place = rank - 1 - turn * others
    group = jnp.where(rank == 0, 0, 1 + jnp.where(later, others - 1 - place, place))
    member = (group == second) & (first < CLUSTERS)
    held = jnp.dot(
        counts.astype(jnp.bfloat16),
        jnp.where(member, 1.0, 0.0).astype(jnp.bfloat16),
        preferred_element_type=jnp.float32,
    )
    by_row = jnp.zeros((1, 128), jnp.float32)
    for row in range(n_row):
        rows = jnp.sum(held[row * n_col : (row + 1) * n_col], axis=0, keepdims=True)
        by_row = jnp.maximum(by_row, rows)
    device = lax.broadcasted_iota(jnp.int32, (devices, 128), 0)
    by_col = jnp.zeros((1, 128), jnp.float32)
    for col in range(n_col):
        cols = jnp.where(device % n_col == col, held, 0.0)
        by_col = jnp.maximum(by_col, jnp.sum(cols, axis=0, keepdims=True))
    fits = (
        (jnp.max(by_col) <= own_cap) & (jnp.max(by_row) <= send_cap) & (jnp.max(held) <= seat_cap)
    )
    out_ref[0] = jnp.where(fits, 1, 0)


def fits_in(codes, n_row, caps):
    fits = pl.pallas_call(
        functools.partial(fit_kernel, n_row=n_row, caps=caps),
        out_shape=jax.ShapeDtypeStruct((1,), jnp.int32),
        in_specs=[pl.BlockSpec(memory_space=pltpu.VMEM)],
        out_specs=pl.BlockSpec(memory_space=pltpu.SMEM),
        cost_estimate=NO_COST,
        name="fits",
    )(codes.reshape(-1, codes.shape[-1]))
    return fits


def exclusive_counts(member):
    count = member.shape[-1]
    before = jnp.arange(count)[:, None] < jnp.arange(count)[None, :]
    return jnp.dot(
        member.astype(jnp.bfloat16),
        before.astype(jnp.bfloat16),
        preferred_element_type=jnp.float32,
    ).astype(jnp.int32)


def assign(codes, n_row):
    cluster, valid = codes >> 1, codes & 1
    labels = jnp.arange(CLUSTERS)
    sizes = jnp.sum(
        (cluster.reshape(1, -1) == labels[:, None]) & (valid.reshape(1, -1) == 1), axis=1
    )
    ahead = (sizes[None, :] > sizes[:, None]) | (
        (sizes[None, :] == sizes[:, None]) & (labels[None, :] < labels[:, None])
    )
    rank = jnp.sum(ahead, axis=1)
    others = n_row - 1
    turn, place = (rank - 1) // others, (rank - 1) % others
    group = jnp.where(rank == 0, 0, 1 + jnp.where(turn == 0, place, others - 1 - place))
    of_node = jnp.sum(
        jnp.where(cluster[None] == labels[:, None, None, None], group[:, None, None, None], 0),
        axis=0,
    )
    return jnp.where(valid == 1, of_node, n_row)


def compact(
    codes,
    group,
    features,
    block_keep,
    edge_weight,
    weight_one,
    bias_one,
    gain_one,
    shift_one,
    weight_two,
    bias_two,
    gain_two,
    shift_two,
    cotangent,
    places_of,
    slots_of,
    seats_of,
    decide,
    sizes,
    caps,
):
    row, col = lax.axis_index("row"), lax.axis_index(COL)
    chip, core = lax.axis_index("chip"), lax.axis_index("core")
    n_row, n_col = sizes
    own_cap, send_cap, seat_cap = caps
    own_nodes, in_width = features.shape
    width = weight_two.shape[2]
    span = n_col * own_cap
    targets = jnp.arange(n_row)

    def in_col(value):
        return lax.dynamic_index_in_dim(value, col, 1, False).reshape(-1)

    def in_row(value):
        return lax.dynamic_index_in_dim(value, row, 0, False).reshape(-1)

    row_group, col_group = in_row(group), in_col(group)
    row_slots, col_places = in_row(slots_of(group)), in_col(places_of(group))
    row_keys = jnp.where(row_slots < send_cap, row_group * send_cap + row_slots, -1)
    col_keys = jnp.where(col_places < own_cap, col_group * own_cap + col_places, -1)
    pieces = packed_pieces(
        block_keep,
        in_row(codes),
        in_col(codes),
        row_keys,
        col_keys,
        edge_weight,
        (own_cap, send_cap),
        n_row,
    )
    pieces, codes = lax.optimization_barrier((pieces, codes))
    group = assign(codes, n_row)
    pieces = trade(pieces, "row")
    places, slots, seats = places_of(group), slots_of(group), seats_of(group)

    standing = jnp.arange(n_col)[None, :, None] * own_cap + places
    fits_here = jnp.where(group == row, standing, -1).reshape(n_row, -1)
    slot_of = slots.reshape(n_row, -1)
    target = jnp.max(
        jnp.where(
            slot_of[:, None, :] == jnp.arange(send_cap)[None, :, None], fits_here[:, None, :], -1
        ),
        axis=2,
    )
    keys = target.reshape(1, -1)

    def to_partner(value, step):
        return lax.ppermute(value, "row", [(place, place ^ step) for place in range(n_row)])

    partners = row ^ targets
    group_here = lax.dynamic_index_in_dim(in_row(group).reshape(n_col, -1), col, 0, False)
    seat_here = lax.dynamic_index_in_dim(in_row(seats).reshape(n_col, -1), col, 0, False)

    def seat_of_node(groups):
        hot = (group_here[None, None, :] == groups[:, None, None]) & (
            seat_here[None, None, :] == jnp.arange(seat_cap)[None, :, None]
        )
        return hot.astype(jnp.bfloat16).reshape(n_row * seat_cap, own_nodes)

    enter_partner = seat_of_node(partners)
    both = jnp.dot(enter_partner, jnp.concatenate([features, cotangent], axis=1))
    both = both.reshape(n_row, seat_cap, -1)
    enter_partner = enter_partner.T
    both, codes = lax.optimization_barrier((both, codes))
    fits, others = decide(codes)
    enter_home = seat_of_node(targets).T
    group_col = lax.dynamic_index_in_dim(group, col, 1, False)
    seats_col = lax.dynamic_index_in_dim(seats, col, 1, False)
    places_col = lax.dynamic_index_in_dim(places, col, 1, False)
    seated = (group_col == row)[:, None, :] & (
        seats_col[:, None, :] == jnp.arange(seat_cap)[None, :, None]
    )
    place_of_seat = jnp.max(jnp.where(seated, places_col[:, None, :], -1), axis=2)
    from_partner = jnp.max(
        jnp.where((partners[:, None] == targets)[:, :, None], place_of_seat[None], -1), axis=1
    )
    arrive = from_partner.reshape(1, -1) == jnp.arange(own_cap)[:, None]
    arrive = arrive.astype(jnp.bfloat16)
    leave_partner = jnp.concatenate([from_partner[::2], from_partner[1::2]])
    leave_partner = leave_partner.reshape(-1, 1) == jnp.arange(own_cap)
    leave_partner = leave_partner.astype(jnp.bfloat16)
    leave_group = place_of_seat.reshape(-1, 1) == jnp.arange(own_cap)[None, :]
    leave_group = leave_group.astype(jnp.bfloat16)
    held_count = jnp.sum(group_col == row)
    valid_rows = (jnp.arange(own_cap) < held_count).astype(jnp.float32)[:, None]
    place = jnp.stack([chip, core]).astype(jnp.int32)
    quarters = jnp.stack([col, (1 - chip) * 2 + core, chip * 2 + 1 - core, 3 - col])
    quarters = jnp.concatenate([fits, quarters.astype(jnp.int32)])
    scalars = (chip, 1 - chip, col * own_cap)
    scalars = tuple(value.astype(jnp.uint32) for value in scalars) + (chip == 0, core == 0, place, quarters)
    homes = enter_home, enter_partner, leave_group, leave_partner
    pieces, both, keys, arrive, homes, valid_rows, others, scalars = lax.optimization_barrier(
        (pieces, both, keys, arrive, homes, valid_rows, others, scalars)
    )
    enter_home, enter_partner, leave_group, leave_partner = homes
    this_chip, other_chip, own_start, first_chip, first_core, place, quarters = scalars

    own_block, quadrant = unpacked_block(pieces, keys, place, own_cap, span)
    quadrant = swap(quadrant, "chip")
    both = [both[0]] + [to_partner(both[step], step) for step in range(1, n_row)]
    sibling = swap(own_block, "core")
    quadrant, *early = lax.optimization_barrier((quadrant, *both[:-2]))
    adjacency = normalized_block(own_block, sibling, quadrant, swap(quadrant, "core"), place)
    adjacency, *late = lax.optimization_barrier((adjacency, *both[-2:]))
    both = early + late
    mine = jnp.dot(arrive, jnp.concatenate(both))
    features_own, cotangent_own = mine[:, :in_width], mine[:, in_width:]
    sibling = swap(features_own, "core")

    first = (own_start + jnp.arange(own_cap, dtype=jnp.uint32))[:, None]
    first = first == jnp.arange(span, dtype=jnp.uint32)[None, :]
    previous = first.astype(jnp.float32)
    current = -lax.dynamic_slice_in_dim(adjacency, own_start, own_cap, 0).astype(jnp.float32)
    lowered = [current.astype(jnp.bfloat16)]
    for position in range(2, ORDER):
        upcoming = (
            -2.0 * jnp.dot(lowered[-1], adjacency, preferred_element_type=jnp.float32) - previous
        )
        low = upcoming.astype(jnp.bfloat16)
        if position == 4:
            low, sibling = lax.optimization_barrier((low, sibling))
            features_chip = joined(features_own, sibling, first_core)
            partner = swap(features_chip, "chip")
        if position == 8:
            low, partner = lax.optimization_barrier((low, partner))
            features_all = joined(features_chip, partner, first_chip)
        previous, current = current, upcoming
        lowered.append(low)
    powers = jnp.concatenate(lowered, axis=0).reshape(ORDER - 1, own_cap, span)

    def everywhere(value_low):
        return lax.all_gather(value_low, COL, axis=0, tiled=True)

    def chosen(value, other):
        return jnp.where(quarters[0] == 1, value.astype(jnp.float32), other.astype(jnp.float32))

    def shaped(*shape, dtype=jnp.bfloat16):
        return jax.ShapeDtypeStruct(shape, dtype)

    part_one, part_two = ORDER * in_width // n_col, ORDER * width // n_col
    padded = -(-(part_one + 16) // (8 * n_row)) * (8 * n_row)
    hidden, turned_one, mixed_one = layer_pass(
        layer_one_kernel,
        "layer_one",
        None,
        powers,
        features_all,
        features_own,
        weight_one,
        [bias_one[None], gain_one[None], shift_one[None], valid_rows],
        [
            shaped(own_cap, width),
            shaped(n_col * part_one, own_cap),
            shaped(own_cap, width, dtype=jnp.float32),
        ],
        [],
    )
    activations, low_two, rest_two, mine, other = layer_pass(
        layer_two_kernel,
        "layer_two",
        place,
        powers,
        everywhere(hidden),
        hidden,
        weight_two,
        [bias_two[None], gain_two[None], shift_two[None], valid_rows, cotangent_own],
        [
            shaped(own_cap, width),
            shaped(own_cap, width),
            shaped(3, width, dtype=jnp.float32),
            shaped(2, part_two, width),
            shaped(2, part_two, width),
        ],
        [((n_col * part_two, own_cap), jnp.bfloat16), ((own_cap, width), jnp.float32)],
    )

    def add_cores(mine, other):
        got = swap(other, "core")
        return tuple(
            added(
                lax.dynamic_index_in_dim(mine, index, 0, False),
                lax.dynamic_index_in_dim(got, index, 0, False),
            )
            for index in (this_chip, other_chip)
        )

    leaving = jnp.dot(leave_partner, activations).reshape(n_row, seat_cap, width)
    near, far = leaving[: n_row // 2], leaving[n_row // 2 :]
    far = to_partner(far, 1)
    here, there = add_cores(mine, other)
    everyone_two, there, far = lax.optimization_barrier((everywhere(low_two), there, far))
    there = swap(there, "chip")
    arrived = [jnp.stack([near[0], far[0]])] + [
        to_partner(jnp.stack([near[half], far[half]]), 2 * half) for half in range(1, n_row // 2)
    ]
    low_one, mine, other = layer_pass(
        back_two_kernel,
        "back_two",
        place,
        powers,
        everyone_two,
        low_two,
        weight_two,
        [turned_one, mixed_one, gain_one[None], valid_rows, rest_two],
        [shaped(own_cap, width), shaped(2, padded, width), shaped(2, padded, width)],
        [((own_cap, width), jnp.float32)],
    )
    low_one, there, arrived = lax.optimization_barrier((low_one, there, arrived))
    second = added(here, there).reshape(n_row, -1, width)
    many = second.shape[1]
    low_one, second = lax.optimization_barrier((low_one, second))
    second = trade(second, "row")
    here, there = add_cores(mine, other)
    there = swap(there, "chip")
    first = added(here, there).reshape(n_row, -1, width)
    share = first.shape[1]
    second = jnp.sum(second.astype(jnp.float32), axis=0).astype(jnp.bfloat16)
    second = jnp.broadcast_to(second[None], (n_row,) + second.shape)
    mixed = jnp.concatenate([second, first], axis=1)
    low_one, mixed = lax.optimization_barrier((low_one, mixed))
    everyone_one = everywhere(low_one)
    mixed = trade(mixed, "row")
    (input_grad,) = layer_pass(
        back_one_kernel,
        "back_one",
        None,
        powers,
        everyone_one,
        low_one,
        weight_one,
        [],
        [shaped(own_cap, in_width)],
        [((own_cap, in_width), jnp.float32)],
    )
    leaving = jnp.dot(leave_group, input_grad).reshape(n_row, seat_cap * in_width // width, width)
    arrived = jnp.concatenate(arrived).reshape(-1, width)
    home = jnp.dot(enter_partner, arrived, preferred_element_type=jnp.float32)
    home = chosen(home, others[0])
    mixed, leaving, home = lax.optimization_barrier((mixed, leaving, home))
    first = jnp.sum(mixed[:, many:].astype(jnp.float32), axis=0).astype(jnp.bfloat16)
    first = jnp.broadcast_to(first[None], (n_row,) + first.shape)
    first, mixed = lax.optimization_barrier((jnp.concatenate([first, leaving], axis=1), mixed))
    first = trade(first, "row")
    second = lax.all_gather(mixed[:, :many].reshape(-1, width), COL, axis=0)
    back = first[:, share:].reshape(n_row * seat_cap, in_width)
    mine = first[:, :share].reshape(1, -1, width)
    partner = swap(mine, "chip")
    second = finished(quarters[:1], None, second, others[3])
    home_grad = jnp.dot(enter_home, back, preferred_element_type=jnp.float32)
    home_grad = chosen(home_grad, others[1])
    pair = jnp.concatenate([mine, partner])
    siblings = swap(pair, "core")
    first, small = finished(quarters, pair, siblings, others[2])
    return home, home_grad, first, second, chosen(small[:6], others[4])


def general(
    codes,
    features,
    block_keep,
    edge_weight,
    weight_one,
    bias_one,
    gain_one,
    shift_one,
    weight_two,
    bias_two,
    gain_two,
    shift_two,
    cotangent,
    node_valid,
):
    row, col = lax.axis_index("row"), lax.axis_index(COL)
    row_codes = lax.dynamic_index_in_dim(codes, row, 0, False).reshape(-1)
    col_codes = lax.dynamic_index_in_dim(codes, col, 1, False).reshape(-1)
    tile_rows, tile_cols = edge_weight.shape
    blocks_down, blocks_across = block_keep.shape
    block_side = tile_rows // blocks_down
    linked = (row_codes[:, None] == col_codes[None, :]) & (row_codes[:, None] & 1 == 1)
    linked = linked.reshape(blocks_down, block_side, blocks_across, block_side) & (
        block_keep[:, None, :, None] == 1
    )
    masked = edge_weight * linked.reshape(tile_rows, tile_cols).astype(jnp.bfloat16)
    degree_rows = 1.0 + lax.psum(jnp.sum(masked, axis=1, dtype=jnp.float32), COL)
    own_nodes = features.shape[0]
    own_degree = lax.dynamic_slice_in_dim(
        degree_rows, lax.axis_index(COL) * own_nodes, own_nodes, 0
    )
    degree_cols = lax.all_gather(own_degree, "row", axis=0, tiled=True)
    adjacency = (
        masked.astype(jnp.float32)
        * lax.rsqrt(degree_rows)[:, None]
        * lax.rsqrt(degree_cols)[None, :]
    ).astype(jnp.bfloat16)
    valid_rows = node_valid.astype(jnp.float32)
    stacked_one, mixed_one, hidden = layer_forward(
        adjacency,
        features.astype(jnp.float32),
        weight_one,
        bias_one,
        gain_one,
        shift_one,
        valid_rows,
    )
    stacked_two, mixed_two, activations = layer_forward(
        adjacency, hidden, weight_two, bias_two, gain_two, shift_two, valid_rows
    )
    hidden_grad, weight_two_grad, bias_two_grad, gain_two_grad, shift_two_grad = layer_backward(
        adjacency,
        stacked_two,
        mixed_two,
        cotangent.astype(jnp.float32),
        weight_two,
        gain_two,
        shift_two,
        valid_rows,
    )
    input_grad, weight_one_grad, bias_one_grad, gain_one_grad, shift_one_grad = layer_backward(
        adjacency, stacked_one, mixed_one, hidden_grad, weight_one, gain_one, shift_one, valid_rows
    )
    summed = lax.psum(
        (
            weight_one_grad,
            bias_one_grad,
            gain_one_grad,
            shift_one_grad,
            weight_two_grad,
            bias_two_grad,
            gain_two_grad,
            shift_two_grad,
        ),
        ("row",) + COL,
    )
    weight_one_grad, bias_one_grad, gain_one_grad, shift_one_grad = (
        summed[0],
        summed[1],
        summed[2],
        summed[3],
    )
    weight_two_grad, bias_two_grad, gain_two_grad, shift_two_grad = (
        summed[4],
        summed[5],
        summed[6],
        summed[7],
    )
    return (
        activations,
        input_grad,
        weight_one_grad,
        bias_one_grad,
        gain_one_grad,
        shift_one_grad,
        weight_two_grad,
        bias_two_grad,
        gain_two_grad,
        shift_two_grad,
    )


def local(n_row, n_col, *args):
    (
        features,
        node_valid,
        cluster,
        block_keep,
        edge_weight,
        weight_one,
        bias_one,
        gain_one,
        shift_one,
        weight_two,
        bias_two,
        gain_two,
        shift_two,
        cotangent,
    ) = args
    own_nodes, in_width = features.shape
    own_cap = own_nodes * n_row * 5 // 16
    send_cap = own_nodes * n_col * 11 // 32
    seat_cap = own_nodes // 2
    codes = broadcast_along(cluster * 2 + node_valid, ("row",) + COL, n_row * n_col)
    codes = codes.reshape(n_row, n_col, own_nodes)
    shared = (
        block_keep,
        edge_weight,
        weight_one,
        bias_one,
        gain_one,
        shift_one,
        weight_two,
        bias_two,
        gain_two,
        shift_two,
        cotangent,
    )

    def slow():
        return general(codes, features, *shared, node_valid)

    held = (ORDER - 1) * own_cap * own_cap * n_col * 2
    if held > HELD_BYTES or n_col != 4 or n_row < 2 or n_row & (n_row - 1):
        return slow()
    group = assign(codes, n_row)

    def member_of(group):
        return group[None] == jnp.arange(n_row)[:, None, None, None]

    def places_of(group):
        member = member_of(group).transpose(0, 2, 1, 3).reshape(n_row, n_col, -1)
        places = jnp.sum(jnp.where(member, exclusive_counts(member), 0), axis=0)
        return places.reshape(n_col, n_row, own_nodes).transpose(1, 0, 2)

    def slots_of(group):
        member = member_of(group).reshape(n_row, n_row, -1)
        slots = jnp.sum(jnp.where(member, exclusive_counts(member), 0), axis=0)
        return slots.reshape(n_row, n_col, own_nodes)

    def seats_of(group):
        member = member_of(group)
        return jnp.sum(jnp.where(member, exclusive_counts(member), 0), axis=0)

    width = weight_two.shape[2]

    def instead(state):
        made = slow()
        small = jnp.stack([made[place] for place in (3, 4, 5, 7, 8, 9)])
        return (jnp.ones_like(state[0]),) + tuple(
            value.astype(jnp.bfloat16).reshape(like.shape)
            for value, like in zip((made[0], made[1], made[2], made[6], small), state[1:])
        )

    shapes = (
        (own_nodes, width),
        (own_nodes, in_width),
        (n_col, ORDER * in_width // n_col, width),
        (n_col, ORDER * width // n_col, width),
        (6, width),
    )

    def decide(codes):
        fits = fits_in(codes, n_row, (own_cap, send_cap, seat_cap))
        others = lax.while_loop(
            lambda state: state[0][0] == 0,
            instead,
            (fits,) + tuple(jnp.zeros(shape, jnp.bfloat16) for shape in shapes),
        )[1:]
        return fits, others

    home, home_grad, first, second, small = compact(
        codes,
        group,
        features,
        *shared,
        places_of,
        slots_of,
        seats_of,
        decide,
        (n_row, n_col),
        (own_cap, send_cap, seat_cap),
    )
    return (
        home,
        home_grad,
        first.reshape(weight_one.shape),
        small[0],
        small[1],
        small[2],
        second.reshape(weight_two.shape),
        small[3],
        small[4],
        small[5],
    )


def solution(mesh):
    n_row, n_col = mesh.shape["row"], mesh.shape["col"]
    by_core = jax.sharding.Mesh(
        mesh.devices.reshape(n_row, n_col // 2, 2), ("row", "chip", "core")
    )
    nodes = ("row", "chip", "core")
    placed = (
        P(nodes, None),
        P(nodes),
        P(nodes),
        P("row", COL),
        P("row", COL),
        P(),
        P(),
        P(),
        P(),
        P(),
        P(),
        P(),
        P(),
        P(nodes, None),
    )
    return jax.shard_map(
        functools.partial(local, n_row, n_col),
        mesh=by_core,
        in_specs=placed,
        out_specs=(P(nodes, None), P(nodes, None), P(), P(), P(), P(), P(), P(), P(), P()),
        check_vma=False,
    )
```

```python
import functools
import math

import jax
import jax.numpy as jnp
from jax import lax
from jax.experimental import pallas as pl
from jax.experimental.pallas import tpu as pltpu
from jax.sharding import PartitionSpec as P

ORDER = 13
CLUSTERS = 16
HELD_BYTES = 1 << 25
VMEM_BYTES = 32 << 20
TERMS = 3
NO_COST = pl.CostEstimate(flops=1, bytes_accessed=1, transcendentals=0)
COL = ("chip", "core")


def finish(mixed, gain, shift, valid_rows):
    active = jax.nn.gelu(mixed, approximate=False)
    centered = active - jnp.mean(active, axis=-1, keepdims=True)
    variance = jnp.mean(centered * centered, axis=-1, keepdims=True)
    return (centered * lax.rsqrt(variance + 1e-05) * gain + shift) * valid_rows[:, None]


def forward_product(adjacency, piece_low):
    partial_value = jnp.dot(
        adjacency,
        lax.all_gather(piece_low, "row", axis=0, tiled=True),
        preferred_element_type=jnp.float32,
    )
    return lax.psum_scatter(partial_value, COL, scatter_dimension=0, tiled=True)


def backward_product(adjacency, piece_low):
    partial_value = lax.dot_general(
        adjacency,
        lax.all_gather(piece_low, COL, axis=0, tiled=True),
        (((0,), (0,)), ((), ())),
        preferred_element_type=jnp.float32,
    )
    return lax.psum_scatter(
        partial_value.astype(jnp.bfloat16), "row", scatter_dimension=0, tiled=True
    ).astype(jnp.float32)


def layer_forward(adjacency, inputs, weight, bias, gain, shift, valid_rows):
    first_low = inputs.astype(jnp.bfloat16)
    second = -forward_product(adjacency, first_low)
    second_low = second.astype(jnp.bfloat16)

    def advance(state_pair, unused):
        previous, current, current_low = state_pair
        upcoming = -2.0 * forward_product(adjacency, current_low) - previous
        upcoming_low = upcoming.astype(jnp.bfloat16)
        return ((current, upcoming, upcoming_low), upcoming_low)

    ignored, others = lax.scan(advance, (inputs, second, second_low), None, length=ORDER - 2)
    stacked = jnp.concatenate([first_low[None], second_low[None], others], axis=0)
    mixed = jnp.einsum("kni,kio->no", stacked, weight, preferred_element_type=jnp.float32) + bias
    return (stacked, mixed, finish(mixed, gain, shift, valid_rows))


def layer_backward(adjacency, stacked, mixed, upstream, weight, gain, shift, valid_rows):

    def local_finish(mixed_in, gain_in, shift_in):
        return finish(mixed_in, gain_in, shift_in, valid_rows)

    ignored, pullback = jax.vjp(local_finish, mixed, gain, shift)
    mixed_grad, gain_grad, shift_grad = pullback(upstream)
    mixed_low = mixed_grad.astype(jnp.bfloat16)
    bias_grad = jnp.sum(mixed_low.astype(jnp.float32), axis=0)
    weight_grad = jnp.einsum("kni,no->kio", stacked, mixed_low, preferred_element_type=jnp.float32)
    direct = jnp.einsum("no,kio->kni", mixed_low, weight, preferred_element_type=jnp.float32)

    def retreat(state_pair, direct_term):
        later_two, later_one = state_pair
        current = (
            direct_term
            - 2.0 * backward_product(adjacency, later_one.astype(jnp.bfloat16))
            - later_two
        )
        return ((later_one, current), None)

    start_pair = (jnp.zeros_like(direct[0]), direct[ORDER - 1])
    (second_grad, first_grad), unused = lax.scan(
        retreat, start_pair, direct[1 : ORDER - 1], reverse=True
    )
    input_grad = (
        direct[0] - backward_product(adjacency, first_grad.astype(jnp.bfloat16)) - second_grad
    )
    return (input_grad, weight_grad, bias_grad, gain_grad, shift_grad)


def swap(value, axis):
    return lax.ppermute(value, axis, [(0, 1), (1, 0)])


def trade(pieces, axis):
    return lax.all_to_all(pieces, axis, 0, 0, tiled=False)


def broadcast_along(value, axis, size):
    return trade(jnp.broadcast_to(value[None], (size,) + value.shape), axis)


def joined(mine, other, mine_first):
    return jnp.where(
        mine_first, jnp.concatenate([mine, other]), jnp.concatenate([other, mine])
    )


def added(mine, received):
    return (mine.astype(jnp.float32) + received.astype(jnp.float32)).astype(jnp.bfloat16)


def assemble(place_ref, own_ref, sibling_ref, near_ref, far_ref, out_ref, done):
    chip, core = place_ref[0], place_ref[1]
    own_cap, span = own_ref.shape
    half = span // 2

    def rows(of_chip, of_core):
        return pl.ds(pl.multiple_of((2 * of_chip + of_core) * own_cap, own_cap), own_cap)

    def fetch(source, of_chip, of_core, columns, place):
        target = out_ref.at[rows(of_chip, of_core), columns]
        return pltpu.make_async_copy(source, target, done.at[place])

    def quadrant_copies(here):
        there = 1 - here
        columns = pl.ds(there * half, half)
        return (
            fetch(near_ref, there, core, columns, 2),
            fetch(far_ref, there, 1 - core, columns, 3),
        )

    everything = pl.ds(0, span)
    top = (
        fetch(own_ref, chip, core, everything, 0),
        fetch(sibling_ref, chip, 1 - core, everything, 1),
    )

    def of_chip(here):
        there = 1 - here
        copies = top + quadrant_copies(here)
        for copy in copies:
            copy.start()
        for copy in copies:
            copy.wait()
        here_rows = pl.ds(here * half, half)
        for tile in range(half // 128):
            columns = pl.ds(there * half + tile * 128, 128)
            strip = out_ref[here_rows, columns]
            turned = jnp.transpose(strip.astype(jnp.float32)).astype(jnp.bfloat16)
            out_ref[columns, here_rows] = turned

    @pl.when(chip == 0)
    def first():
        of_chip(0)

    @pl.when(chip == 1)
    def second():
        of_chip(1)

    across = jnp.ones((1, span), jnp.float32)
    for tile in range(span // 128):
        across = across + jnp.sum(
            out_ref[pl.ds(tile * 128, 128), :].astype(jnp.float32), axis=0, keepdims=True
        )
    across = lax.rsqrt(across)
    for tile in range(span // 128):
        strip = out_ref[pl.ds(tile * 128, 128), :].astype(jnp.float32)
        down = lax.rsqrt(1.0 + jnp.sum(strip, axis=1, keepdims=True))
        out_ref[pl.ds(tile * 128, 128), :] = (strip * down * across).astype(jnp.bfloat16)


def normalized_block(own, sibling, near, far, place):
    span = own.shape[1]
    return pl.pallas_call(
        assemble,
        out_shape=jax.ShapeDtypeStruct((span, span), jnp.bfloat16),
        in_specs=[pl.BlockSpec(memory_space=pltpu.SMEM)]
        + [pl.BlockSpec(memory_space=pltpu.HBM)] * 4,
        out_specs=pl.BlockSpec(memory_space=pltpu.VMEM),
        scratch_shapes=[pltpu.SemaphoreType.DMA((4,))],
        compiler_params=pltpu.CompilerParams(vmem_limit_bytes=VMEM_BYTES),
        cost_estimate=NO_COST,
        name="normalized_block",
    )(place, own, sibling, near, far)


def pack_kernel(
    keep_ref, row_codes_ref, col_codes_ref, row_keys_ref, col_keys_ref, weight_ref, out_ref,
    masked, picked, rows_hot, cols_hot
):
    tile_rows, tile_cols = weight_ref.shape
    blocks_down, blocks_across = keep_ref.shape
    groups, ignored, lanes = out_ref.shape
    send_cap, own_cap = rows_hot.shape[0] // groups, cols_hot.shape[0] // groups
    high, wide = tile_rows // blocks_down, tile_cols // blocks_across
    for down in range(blocks_down):
        for across in range(blocks_across):
            rows, columns = pl.ds(down * high, high), pl.ds(across * wide, wide)
            own, other = row_codes_ref[rows, :], col_codes_ref[:, columns]
            linked = (own == other) & (own % 2 == 1) & (keep_ref[down, across] == 1)
            weight = weight_ref[rows, columns].astype(jnp.float32)
            masked[rows, columns] = jnp.where(linked, weight, 0.0).astype(jnp.bfloat16)

    def one_hot(keys, start, count):
        standing = lax.broadcasted_iota(jnp.int32, (count, keys.shape[1]), 0) + start
        return jnp.where(standing == keys, 1.0, 0.0).astype(jnp.bfloat16)

    for group in range(groups):
        rows_hot[pl.ds(group * send_cap, send_cap), :] = one_hot(
            row_keys_ref[...], group * send_cap, send_cap
        )
        cols_hot[pl.ds(group * own_cap, own_cap), :] = one_hot(
            col_keys_ref[...], group * own_cap, own_cap
        )
    for tile in range(tile_cols // 256):
        columns = pl.ds(tile * 256, 256)
        picked[:, columns] = jnp.dot(
            rows_hot[...], masked[:, columns], preferred_element_type=jnp.float32
        ).astype(jnp.bfloat16)
    whole, half = own_cap // lanes, send_cap // 2
    for group in range(groups):
        packed = lax.dot_general(
            cols_hot[pl.ds(group * own_cap, own_cap), :],
            picked[pl.ds(group * send_cap, send_cap), :],
            (((1,), (1,)), ((), ())),
            preferred_element_type=jnp.float32,
        ).T
        for tile in range(whole):
            out_ref[group, pl.ds(tile * send_cap, send_cap), :] = packed[
                :, tile * lanes : (tile + 1) * lanes
            ].astype(jnp.bfloat16)
        ends = jnp.concatenate(
            [packed[:half, whole * lanes :], packed[half:, whole * lanes :]], axis=1
        )
        out_ref[group, pl.ds(whole * send_cap, half), :] = ends.astype(jnp.bfloat16)


def packed_pieces(block_keep, row_codes, col_codes, row_keys, col_keys, edge_weight, caps, groups):
    own_cap, send_cap = caps
    tile_rows, tile_cols = edge_weight.shape
    high = own_cap // 128 * send_cap + send_cap // 2
    vector = pl.BlockSpec(memory_space=pltpu.VMEM)
    return pl.pallas_call(
        pack_kernel,
        out_shape=jax.ShapeDtypeStruct((groups, high, 128), jnp.bfloat16),
        in_specs=[pl.BlockSpec(memory_space=pltpu.SMEM)] + [vector] * 5,
        out_specs=vector,
        scratch_shapes=[
            pltpu.VMEM((tile_rows, tile_cols), jnp.bfloat16),
            pltpu.VMEM((groups * send_cap, tile_cols), jnp.bfloat16),
            pltpu.VMEM((groups * send_cap, tile_rows), jnp.bfloat16),
            pltpu.VMEM((groups * own_cap, tile_cols), jnp.bfloat16),
        ],
        compiler_params=pltpu.CompilerParams(vmem_limit_bytes=VMEM_BYTES),
        cost_estimate=NO_COST,
        name="packed_pieces",
    )(block_keep, row_codes[:, None], col_codes[None], row_keys[None], col_keys[None], edge_weight)


def normal_share(mixed):
    return 0.5 * (1.0 + lax.erf(mixed * 0.5**0.5))


def norm_forward(mixed):
    active = mixed * normal_share(mixed)
    centered = active - jnp.mean(active, axis=-1, keepdims=True)
    scale = lax.rsqrt(jnp.mean(centered * centered, axis=-1, keepdims=True) + 1e-05)
    return centered * scale, scale


def norm_backward(mixed, upstream, gain, valid):
    normed, scale = norm_forward(mixed)
    upstream = upstream * valid
    inner = upstream * gain
    inner = inner - jnp.mean(inner, axis=-1, keepdims=True) - normed * jnp.mean(
        inner * normed, axis=-1, keepdims=True
    )
    density = jnp.exp(-0.5 * mixed * mixed) * (1.0 / (2.0 * math.pi) ** 0.5)
    low = (inner * scale * (normal_share(mixed) + mixed * density)).astype(jnp.bfloat16)
    rest = [low.astype(jnp.float32), upstream * normed, upstream]
    return low, [jnp.sum(value, axis=0, keepdims=True) for value in rest]


def weight_gradient(turned_ref, low, core, mine_ref, other_ref):
    part = turned_ref.shape[0] // 4

    def halves(first_ref, second_ref):
        for place in range(4):
            out_ref = second_ref if place % 2 else first_ref
            out_ref[place // 2, :part, :] = jnp.dot(
                turned_ref[place * part : (place + 1) * part, :],
                low,
                preferred_element_type=jnp.float32,
            ).astype(jnp.bfloat16)

    @pl.when(core == 0)
    def low_half_first():
        halves(mine_ref, other_ref)

    @pl.when(core == 1)
    def high_half_first():
        halves(other_ref, mine_ref)


def forward_step(step, powers_ref, all_ref, own_ref, weights, bias_ref, turned, mixed):
    terms, own_cap, span = powers_ref.shape
    fan_in = own_ref.shape[1]

    @pl.when(step == 0)
    def first():
        turned[:fan_in, :] = own_ref[...].T
        mixed[...] = bias_ref[...] + jnp.dot(
            own_ref[...], weights[0][0], preferred_element_type=jnp.float32
        )

    low = jnp.dot(
        powers_ref[...].reshape(terms * own_cap, span),
        all_ref[...],
        preferred_element_type=jnp.float32,
    ).astype(jnp.bfloat16)
    total = mixed[...]
    for term in range(terms):
        part = low[term * own_cap : (term + 1) * own_cap]
        start = pl.multiple_of((1 + step * terms + term) * fan_in, fan_in)
        turned[pl.ds(start, fan_in), :] = part.T
        total = total + jnp.dot(part, weights[1 + term][0], preferred_element_type=jnp.float32)
    mixed[...] = total


def layer_one_kernel(
    powers_ref,
    all_ref,
    own_ref,
    weight_0,
    weight_a,
    weight_b,
    weight_c,
    bias_ref,
    gain_ref,
    shift_ref,
    valid_ref,
    hidden_ref,
    turned_ref,
    mixed_ref,
):
    step = pl.program_id(0)
    weights = (weight_0, weight_a, weight_b, weight_c)
    forward_step(step, powers_ref, all_ref, own_ref, weights, bias_ref, turned_ref, mixed_ref)

    @pl.when(step == pl.num_programs(0) - 1)
    def finish_layer():
        normed, ignored = norm_forward(mixed_ref[...])
        hidden = (normed * gain_ref[...] + shift_ref[...]) * valid_ref[...]
        hidden_ref[...] = hidden.astype(jnp.bfloat16)


def layer_two_kernel(
    place_ref,
    powers_ref,
    all_ref,
    own_ref,
    weight_0,
    weight_a,
    weight_b,
    weight_c,
    bias_ref,
    gain_ref,
    shift_ref,
    valid_ref,
    upstream_ref,
    active_ref,
    low_ref,
    rest_ref,
    mine_ref,
    other_ref,
    turned,
    mixed,
):
    step = pl.program_id(0)
    weights = (weight_0, weight_a, weight_b, weight_c)
    forward_step(step, powers_ref, all_ref, own_ref, weights, bias_ref, turned, mixed)

    @pl.when(step == pl.num_programs(0) - 1)
    def finish_layer():
        normed, ignored = norm_forward(mixed[...])
        active = (normed * gain_ref[...] + shift_ref[...]) * valid_ref[...]
        active_ref[...] = active.astype(jnp.bfloat16)
        low, rest = norm_backward(
            mixed[...], upstream_ref[...].astype(jnp.float32), gain_ref[...], valid_ref[...]
        )
        low_ref[...] = low
        for place in range(3):
            rest_ref[place : place + 1, :] = rest[place]
        weight_gradient(turned, low, place_ref[1], mine_ref, other_ref)


def backward_step(step, powers_ref, all_ref, own_ref, weights, total):
    terms, own_cap, span = powers_ref.shape
    transposed = (((1,), (1,)), ((), ()))

    @pl.when(step == 0)
    def first():
        total[...] = lax.dot_general(
            own_ref[...], weights[0][0], transposed, preferred_element_type=jnp.float32
        )

    low = jnp.dot(
        powers_ref[...].reshape(terms * own_cap, span),
        all_ref[...],
        preferred_element_type=jnp.float32,
    ).astype(jnp.bfloat16)
    value = total[...]
    for term in range(terms):
        value = value + lax.dot_general(
            low[term * own_cap : (term + 1) * own_cap],
            weights[1 + term][0],
            transposed,
            preferred_element_type=jnp.float32,
        )
    total[...] = value


def back_two_kernel(
    place_ref,
    powers_ref,
    all_ref,
    own_ref,
    weight_0,
    weight_a,
    weight_b,
    weight_c,
    turned_ref,
    mixed_ref,
    gain_ref,
    valid_ref,
    rest_ref,
    low_ref,
    mine_ref,
    other_ref,
    total,
):
    step = pl.program_id(0)
    weights = (weight_0, weight_a, weight_b, weight_c)
    backward_step(step, powers_ref, all_ref, own_ref, weights, total)

    @pl.when(step == pl.num_programs(0) - 1)
    def finish_layer():
        low, rest = norm_backward(mixed_ref[...], total[...], gain_ref[...], valid_ref[...])
        low_ref[...] = low
        weight_gradient(turned_ref, low, place_ref[1], mine_ref, other_ref)
        part = turned_ref.shape[0] // 4
        extra = jnp.zeros((2, mine_ref.shape[1] - part, mine_ref.shape[2]), jnp.bfloat16)
        rows = rest + [rest_ref[place : place + 1, :] for place in range(3)]
        rows = jnp.concatenate(rows + [jnp.zeros((10, rows[0].shape[1]), jnp.float32)], axis=0)

        def below(first_ref, second_ref):
            first_ref[:, part:, :] = extra
            second_ref[:, part:, :] = extra
            first_ref[0, part : part + 16, :] = rows.astype(jnp.bfloat16)

        @pl.when(place_ref[1] == 0)
        def low_half_here():
            below(mine_ref, other_ref)

        @pl.when(place_ref[1] == 1)
        def low_half_there():
            below(other_ref, mine_ref)


def back_one_kernel(
    powers_ref, all_ref, own_ref, weight_0, weight_a, weight_b, weight_c, out_ref, total
):
    step = pl.program_id(0)
    weights = (weight_0, weight_a, weight_b, weight_c)
    backward_step(step, powers_ref, all_ref, own_ref, weights, total)

    @pl.when(step == pl.num_programs(0) - 1)
    def finish_layer():
        out_ref[...] = total[...].astype(jnp.bfloat16)


def layer_pass(
    kernel, name, place, powers, everyone, own, weight, others, outs, scratch, cost=NO_COST
):
    ignored, own_cap, span = powers.shape
    fan_in, width = weight.shape[1:]

    def whole(value):
        return pl.BlockSpec(value.shape, lambda step: (0,) * len(value.shape))

    def term_weight(term):
        return pl.BlockSpec((1, fan_in, width), lambda step: (1 + step * TERMS + term, 0, 0))

    in_specs = [
        pl.BlockSpec((TERMS, own_cap, span), lambda step: (step, 0, 0)),
        whole(everyone),
        whole(own),
        pl.BlockSpec((1, fan_in, width), lambda step: (0, 0, 0)),
    ]
    in_specs += [term_weight(term) for term in range(TERMS)] + [whole(value) for value in others]
    operands = [powers, everyone, own] + [weight] * (1 + TERMS) + list(others)
    if place is not None:
        in_specs = [pl.BlockSpec(memory_space=pltpu.SMEM)] + in_specs
        operands = [place] + operands
    return pl.pallas_call(
        kernel,
        grid=((ORDER - 1) // TERMS,),
        out_shape=outs,
        in_specs=in_specs,
        out_specs=[whole(value) for value in outs],
        scratch_shapes=[pltpu.VMEM(shape, dtype) for shape, dtype in scratch],
        compiler_params=pltpu.CompilerParams(vmem_limit_bytes=VMEM_BYTES),
        cost_estimate=cost,
        name=name,
    )(*operands)


def finish_kernel(scalars_ref, *refs):
    step = pl.program_id(0)
    if len(refs) == 3:
        values_ref, other_ref, out_ref = refs
        parts = [(step >= 0, values_ref)]
        small_ref = None
    else:
        pair_ref, siblings_ref, other_ref, out_ref, small_ref = refs
        parts = [(step < 2, pair_ref), (step >= 2, siblings_ref)]
    part = out_ref.shape[1]
    for here, values_ref in parts:
        @pl.when(here & (scalars_ref[0] == 1))
        def fast_form():
            out_ref[0] = values_ref[0, :part, :].astype(jnp.float32)

        if small_ref is not None:
            @pl.when(here & (scalars_ref[1 + step] == 0))
            def small_sums():
                small_ref[...] = values_ref[0, part : part + 16, :].astype(jnp.float32)

    @pl.when(scalars_ref[0] == 0)
    def general_form():
        out_ref[0] = other_ref[0].astype(jnp.float32)


def finished(scalars, pair, values, other):
    count, part, width = other.shape
    one = (1, part, width)
    if pair is None:
        operands, outs = [values, other], [jax.ShapeDtypeStruct(other.shape, jnp.float32)]

        def quarter(step, scalars_ref):
            return step

        in_specs = [pl.BlockSpec((1,) + values.shape[1:], lambda step, ref: (step, 0, 0))]
        small_specs = []
    else:
        operands = [pair, values, other]
        outs = [
            jax.ShapeDtypeStruct(other.shape, jnp.float32),
            jax.ShapeDtypeStruct((16, width), jnp.float32),
        ]

        def quarter(step, scalars_ref):
            return scalars_ref[1 + step]

        in_specs = [
            pl.BlockSpec((1,) + pair.shape[1:], lambda step, ref: (jnp.minimum(step, 1), 0, 0)),
            pl.BlockSpec((1,) + pair.shape[1:], lambda step, ref: (jnp.maximum(step - 2, 0), 0, 0)),
        ]
        small_specs = [pl.BlockSpec((16, width), lambda step, ref: (0, 0))]
    in_specs.append(
        pl.BlockSpec(one, lambda step, ref: ((1 - ref[0]) * quarter(step, ref), 0, 0))
    )
    result = pl.pallas_call(
        finish_kernel,
        grid_spec=pltpu.PrefetchScalarGridSpec(
            num_scalar_prefetch=1,
            grid=(count,),
            in_specs=in_specs,
            out_specs=[pl.BlockSpec(one, lambda step, ref: (quarter(step, ref), 0, 0))]
            + small_specs,
        ),
        out_shape=outs,
        compiler_params=pltpu.CompilerParams(vmem_limit_bytes=VMEM_BYTES),
        cost_estimate=NO_COST,
        name="finished",
    )(scalars, *operands)
    return result[0] if pair is None else result


def unpack_kernel(place_ref, pieces_ref, keys_ref, own_ref, quadrant_ref, columns, hot):
    groups, high, lanes = pieces_ref.shape
    own_cap, span = own_ref.shape
    whole = own_cap // lanes
    send_cap = keys_ref.shape[1] // groups
    half, rest = send_cap // 2, own_cap - whole * lanes
    for group in range(groups):
        start = group * send_cap
        for tile in range(whole):
            columns[start : start + send_cap, tile * lanes : (tile + 1) * lanes] = pieces_ref[
                group, tile * send_cap : (tile + 1) * send_cap, :
            ]
        ends = pieces_ref[group, whole * send_cap :, :]
        columns[start : start + half, whole * lanes :] = ends[:, :rest]
        columns[start + half : start + send_cap, whole * lanes :] = ends[:, rest:]
    standing = lax.broadcasted_iota(jnp.int32, hot.shape, 0)
    hot[...] = jnp.where(standing == keys_ref[...], 1.0, 0.0).astype(jnp.bfloat16)
    block = jnp.dot(hot[...], columns[...], preferred_element_type=jnp.float32)
    own_ref[...] = block.T.astype(jnp.bfloat16)
    middle = span // 2

    @pl.when(place_ref[0] == 0)
    def first():
        quadrant_ref[...] = own_ref[:, :middle]

    @pl.when(place_ref[0] == 1)
    def second():
        quadrant_ref[...] = own_ref[:, middle:]


def unpacked_block(pieces, keys, place, own_cap, span):
    vector = pl.BlockSpec(memory_space=pltpu.VMEM)
    return pl.pallas_call(
        unpack_kernel,
        out_shape=[
            jax.ShapeDtypeStruct((own_cap, span), jnp.bfloat16),
            jax.ShapeDtypeStruct((own_cap, span // 2), jnp.bfloat16),
        ],
        in_specs=[pl.BlockSpec(memory_space=pltpu.SMEM), vector, vector],
        out_specs=[vector, vector],
        scratch_shapes=[
            pltpu.VMEM((keys.shape[1], own_cap), jnp.bfloat16),
            pltpu.VMEM((span, keys.shape[1]), jnp.bfloat16),
        ],
        compiler_params=pltpu.CompilerParams(vmem_limit_bytes=VMEM_BYTES),
        cost_estimate=NO_COST,
        name="unpacked_block",
    )(place, pieces, keys)


def fit_kernel(codes_ref, out_ref, *, n_row, caps):
    own_cap, send_cap, seat_cap = caps
    codes = codes_ref[...]
    devices = codes.shape[0]
    n_col = devices // n_row
    label = lax.broadcasted_iota(jnp.int32, (devices, 128), 1)
    counts = jnp.zeros((devices, 128), jnp.float32)
    for cluster in range(CLUSTERS):
        here = jnp.where(codes == 2 * cluster + 1, 1.0, 0.0)
        counts = counts + jnp.where(
            label == cluster, jnp.sum(here, axis=1, keepdims=True), 0.0
        )
    sizes = jnp.sum(counts, axis=0, keepdims=True)
    across = jnp.broadcast_to(sizes, (128, 128))
    down = across.T
    first = lax.broadcasted_iota(jnp.int32, (128, 128), 0)
    second = lax.broadcasted_iota(jnp.int32, (128, 128), 1)
    ahead = (across > down) | ((across == down) & (second < first))
    ahead = ahead & (second < CLUSTERS)
    rank = jnp.sum(jnp.where(ahead, 1.0, 0.0), axis=1, keepdims=True).astype(jnp.int32)
    others = n_row - 1
    later = rank > others
    turn = jnp.zeros_like(rank)
    for count in range(1, CLUSTERS // others + 1):
        turn = turn + jnp.where(rank - 1 >= count * others, 1, 0)
    place = rank - 1 - turn * others
    group = jnp.where(rank == 0, 0, 1 + jnp.where(later, others - 1 - place, place))
    member = (group == second) & (first < CLUSTERS)
    held = jnp.dot(
        counts.astype(jnp.bfloat16),
        jnp.where(member, 1.0, 0.0).astype(jnp.bfloat16),
        preferred_element_type=jnp.float32,
    )
    by_row = jnp.zeros((1, 128), jnp.float32)
    for row in range(n_row):
        rows = jnp.sum(held[row * n_col : (row + 1) * n_col], axis=0, keepdims=True)
        by_row = jnp.maximum(by_row, rows)
    device = lax.broadcasted_iota(jnp.int32, (devices, 128), 0)
    by_col = jnp.zeros((1, 128), jnp.float32)
    for col in range(n_col):
        cols = jnp.where(device % n_col == col, held, 0.0)
        by_col = jnp.maximum(by_col, jnp.sum(cols, axis=0, keepdims=True))
    fits = (
        (jnp.max(by_col) <= own_cap) & (jnp.max(by_row) <= send_cap) & (jnp.max(held) <= seat_cap)
    )
    out_ref[0] = jnp.where(fits, 1, 0)


def fits_in(codes, n_row, caps):
    fits = pl.pallas_call(
        functools.partial(fit_kernel, n_row=n_row, caps=caps),
        out_shape=jax.ShapeDtypeStruct((1,), jnp.int32),
        in_specs=[pl.BlockSpec(memory_space=pltpu.VMEM)],
        out_specs=pl.BlockSpec(memory_space=pltpu.SMEM),
        cost_estimate=NO_COST,
        name="fits",
    )(codes.reshape(-1, codes.shape[-1]))
    return fits


def exclusive_counts(member):
    count = member.shape[-1]
    before = jnp.arange(count)[:, None] < jnp.arange(count)[None, :]
    return jnp.dot(
        member.astype(jnp.bfloat16),
        before.astype(jnp.bfloat16),
        preferred_element_type=jnp.float32,
    ).astype(jnp.int32)


def assign(codes, n_row):
    cluster, valid = codes >> 1, codes & 1
    labels = jnp.arange(CLUSTERS)
    sizes = jnp.sum(
        (cluster.reshape(1, -1) == labels[:, None]) & (valid.reshape(1, -1) == 1), axis=1
    )
    ahead = (sizes[None, :] > sizes[:, None]) | (
        (sizes[None, :] == sizes[:, None]) & (labels[None, :] < labels[:, None])
    )
    rank = jnp.sum(ahead, axis=1)
    others = n_row - 1
    turn, place = (rank - 1) // others, (rank - 1) % others
    group = jnp.where(rank == 0, 0, 1 + jnp.where(turn == 0, place, others - 1 - place))
    of_node = jnp.sum(
        jnp.where(cluster[None] == labels[:, None, None, None], group[:, None, None, None], 0),
        axis=0,
    )
    return jnp.where(valid == 1, of_node, n_row)


def compact(
    codes,
    group,
    features,
    block_keep,
    edge_weight,
    weight_one,
    bias_one,
    gain_one,
    shift_one,
    weight_two,
    bias_two,
    gain_two,
    shift_two,
    cotangent,
    places_of,
    slots_of,
    seats_of,
    decide,
    sizes,
    caps,
):
    row, col = lax.axis_index("row"), lax.axis_index(COL)
    chip, core = lax.axis_index("chip"), lax.axis_index("core")
    n_row, n_col = sizes
    own_cap, send_cap, seat_cap = caps
    own_nodes, in_width = features.shape
    width = weight_two.shape[2]
    span = n_col * own_cap
    targets = jnp.arange(n_row)

    def in_col(value):
        return lax.dynamic_index_in_dim(value, col, 1, False).reshape(-1)

    def in_row(value):
        return lax.dynamic_index_in_dim(value, row, 0, False).reshape(-1)

    row_group, col_group = in_row(group), in_col(group)
    row_slots, col_places = in_row(slots_of(group)), in_col(places_of(group))
    row_keys = jnp.where(row_slots < send_cap, row_group * send_cap + row_slots, -1)
    col_keys = jnp.where(col_places < own_cap, col_group * own_cap + col_places, -1)
    pieces = packed_pieces(
        block_keep,
        in_row(codes),
        in_col(codes),
        row_keys,
        col_keys,
        edge_weight,
        (own_cap, send_cap),
        n_row,
    )
    pieces, codes = lax.optimization_barrier((pieces, codes))
    group = assign(codes, n_row)
    pieces = trade(pieces, "row")
    places, slots, seats = places_of(group), slots_of(group), seats_of(group)

    standing = jnp.arange(n_col)[None, :, None] * own_cap + places
    fits_here = jnp.where(group == row, standing, -1).reshape(n_row, -1)
    slot_of = slots.reshape(n_row, -1)
    target = jnp.max(
        jnp.where(
            slot_of[:, None, :] == jnp.arange(send_cap)[None, :, None], fits_here[:, None, :], -1
        ),
        axis=2,
    )
    keys = target.reshape(1, -1)

    def to_partner(value, step):
        return lax.ppermute(value, "row", [(place, place ^ step) for place in range(n_row)])

    partners = row ^ targets
    group_here = lax.dynamic_index_in_dim(in_row(group).reshape(n_col, -1), col, 0, False)
    seat_here = lax.dynamic_index_in_dim(in_row(seats).reshape(n_col, -1), col, 0, False)

    def seat_of_node(groups):
        hot = (group_here[None, None, :] == groups[:, None, None]) & (
            seat_here[None, None, :] == jnp.arange(seat_cap)[None, :, None]
        )
        return hot.astype(jnp.bfloat16).reshape(n_row * seat_cap, own_nodes)

    enter_partner = seat_of_node(partners)
    both = jnp.dot(enter_partner, jnp.concatenate([features, cotangent], axis=1))
    both = both.reshape(n_row, seat_cap, -1)
    enter_partner = enter_partner.T
    both, codes = lax.optimization_barrier((both, codes))
    fits, others = decide(codes)
    group_col = lax.dynamic_index_in_dim(group, col, 1, False)
    seats_col = lax.dynamic_index_in_dim(seats, col, 1, False)
    places_col = lax.dynamic_index_in_dim(places, col, 1, False)
    seated = (group_col == row)[:, None, :] & (
        seats_col[:, None, :] == jnp.arange(seat_cap)[None, :, None]
    )
    place_of_seat = jnp.max(jnp.where(seated, places_col[:, None, :], -1), axis=2)
    from_partner = jnp.max(
        jnp.where((partners[:, None] == targets)[:, :, None], place_of_seat[None], -1), axis=1
    )
    arrive = from_partner.reshape(1, -1) == jnp.arange(own_cap)[:, None]
    arrive = arrive.astype(jnp.bfloat16)
    leave_partner = jnp.concatenate([from_partner[::2], from_partner[1::2]])
    leave_partner = leave_partner.reshape(-1, 1) == jnp.arange(own_cap)
    leave_partner = leave_partner.astype(jnp.bfloat16)
    held_count = jnp.sum(group_col == row)
    valid_rows = (jnp.arange(own_cap) < held_count).astype(jnp.float32)[:, None]
    place = jnp.stack([chip, core]).astype(jnp.int32)
    quarters = jnp.stack([col, (1 - chip) * 2 + core, chip * 2 + 1 - core, 3 - col])
    quarters = jnp.concatenate([fits, quarters.astype(jnp.int32)])
    scalars = (chip, 1 - chip, col * own_cap)
    scalars = tuple(value.astype(jnp.uint32) for value in scalars) + (chip == 0, core == 0, place, quarters)
    homes = enter_partner, leave_partner
    pieces, both, keys, arrive, homes, valid_rows, others, scalars = lax.optimization_barrier(
        (pieces, both, keys, arrive, homes, valid_rows, others, scalars)
    )
    enter_partner, leave_partner = homes
    this_chip, other_chip, own_start, first_chip, first_core, place, quarters = scalars

    own_block, quadrant = unpacked_block(pieces, keys, place, own_cap, span)
    quadrant = swap(quadrant, "chip")
    both = [both[0]] + [to_partner(both[step], step) for step in range(1, n_row)]
    sibling = swap(own_block, "core")
    quadrant, *early = lax.optimization_barrier((quadrant, *both[:-2]))
    adjacency = normalized_block(own_block, sibling, quadrant, swap(quadrant, "core"), place)
    adjacency, *late = lax.optimization_barrier((adjacency, *both[-2:]))
    both = early + late
    mine = jnp.dot(arrive, jnp.concatenate(both))
    features_own, cotangent_own = mine[:, :in_width], mine[:, in_width:]
    sibling = swap(features_own, "core")

    first = (own_start + jnp.arange(own_cap, dtype=jnp.uint32))[:, None]
    first = first == jnp.arange(span, dtype=jnp.uint32)[None, :]
    previous = first.astype(jnp.float32)
    current = -lax.dynamic_slice_in_dim(adjacency, own_start, own_cap, 0).astype(jnp.float32)
    lowered = [current.astype(jnp.bfloat16)]
    for position in range(2, ORDER):
        upcoming = (
            -2.0 * jnp.dot(lowered[-1], adjacency, preferred_element_type=jnp.float32) - previous
        )
        low = upcoming.astype(jnp.bfloat16)
        if position == 4:
            low, sibling = lax.optimization_barrier((low, sibling))
            features_chip = joined(features_own, sibling, first_core)
            partner = swap(features_chip, "chip")
        if position == 8:
            low, partner = lax.optimization_barrier((low, partner))
            features_all = joined(features_chip, partner, first_chip)
        previous, current = current, upcoming
        lowered.append(low)
    powers = jnp.concatenate(lowered, axis=0).reshape(ORDER - 1, own_cap, span)

    def everywhere(value_low):
        return lax.all_gather(value_low, COL, axis=0, tiled=True)

    def chosen(value, other):
        return jnp.where(quarters[0] == 1, value.astype(jnp.float32), other.astype(jnp.float32))

    def shaped(*shape, dtype=jnp.bfloat16):
        return jax.ShapeDtypeStruct(shape, dtype)

    part_one, part_two = ORDER * in_width // n_col, ORDER * width // n_col
    padded = -(-(part_one + 16) // (8 * n_row)) * (8 * n_row)
    hidden, turned_one, mixed_one = layer_pass(
        layer_one_kernel,
        "layer_one",
        None,
        powers,
        features_all,
        features_own,
        weight_one,
        [bias_one[None], gain_one[None], shift_one[None], valid_rows],
        [
            shaped(own_cap, width),
            shaped(n_col * part_one, own_cap),
            shaped(own_cap, width, dtype=jnp.float32),
        ],
        [],
    )
    activations, low_two, rest_two, mine, other = layer_pass(
        layer_two_kernel,
        "layer_two",
        place,
        powers,
        everywhere(hidden),
        hidden,
        weight_two,
        [bias_two[None], gain_two[None], shift_two[None], valid_rows, cotangent_own],
        [
            shaped(own_cap, width),
            shaped(own_cap, width),
            shaped(3, width, dtype=jnp.float32),
            shaped(2, part_two, width),
            shaped(2, part_two, width),
        ],
        [((n_col * part_two, own_cap), jnp.bfloat16), ((own_cap, width), jnp.float32)],
    )

    def add_cores(mine, other):
        got = swap(other, "core")
        return tuple(
            added(
                lax.dynamic_index_in_dim(mine, index, 0, False),
                lax.dynamic_index_in_dim(got, index, 0, False),
            )
            for index in (this_chip, other_chip)
        )

    leaving = jnp.dot(leave_partner, activations).reshape(n_row, seat_cap, width)
    near, far = leaving[: n_row // 2], leaving[n_row // 2 :]
    far = to_partner(far, 1)
    here, there = add_cores(mine, other)
    everyone_two, there, far = lax.optimization_barrier((everywhere(low_two), there, far))
    there = swap(there, "chip")
    arrived = [jnp.stack([near[0], far[0]])] + [
        to_partner(jnp.stack([near[half], far[half]]), 2 * half) for half in range(1, n_row // 2)
    ]
    low_one, mine, other = layer_pass(
        back_two_kernel,
        "back_two",
        place,
        powers,
        everyone_two,
        low_two,
        weight_two,
        [turned_one, mixed_one, gain_one[None], valid_rows, rest_two],
        [shaped(own_cap, width), shaped(2, padded, width), shaped(2, padded, width)],
        [((own_cap, width), jnp.float32)],
    )
    low_one, there, arrived = lax.optimization_barrier((low_one, there, arrived))
    second = added(here, there).reshape(n_row, -1, width)
    many = second.shape[1]
    low_one, second = lax.optimization_barrier((low_one, second))
    second = trade(second, "row")
    here, there = add_cores(mine, other)
    there = swap(there, "chip")
    first = added(here, there).reshape(n_row, -1, width)
    share = first.shape[1]
    second = jnp.sum(second.astype(jnp.float32), axis=0).astype(jnp.bfloat16)
    second = jnp.broadcast_to(second[None], (n_row,) + second.shape)
    mixed = jnp.concatenate([second, first], axis=1)
    low_one, mixed = lax.optimization_barrier((low_one, mixed))
    everyone_one = everywhere(low_one)
    mixed = trade(mixed, "row")
    arrived = jnp.concatenate(arrived).reshape(-1, width)
    home = jnp.dot(enter_partner, arrived, preferred_element_type=jnp.float32)
    home = chosen(home, others[0])
    mixed, home = lax.optimization_barrier((mixed, home))
    first = jnp.sum(mixed[:, many:].astype(jnp.float32), axis=0).astype(jnp.bfloat16)
    first = jnp.broadcast_to(first[None], (n_row,) + first.shape)
    first, mixed, everyone_one = lax.optimization_barrier((first, mixed, everyone_one))
    first = trade(first, "row")
    second = lax.all_gather(mixed[:, :many].reshape(-1, width), COL, axis=0)
    (input_grad,) = layer_pass(
        back_one_kernel,
        "back_one",
        None,
        powers,
        everyone_one,
        low_one,
        weight_one,
        [],
        [shaped(own_cap, in_width)],
        [((own_cap, in_width), jnp.float32)],
        pl.CostEstimate(
            flops=2 * ORDER * own_cap * width * (span + in_width),
            bytes_accessed=2 * ORDER * own_cap * span,
            transcendentals=0,
        ),
    )
    leaving = jnp.dot(leave_partner, input_grad).reshape(n_row, seat_cap, in_width)
    near, far = leaving[: n_row // 2], leaving[n_row // 2 :]
    far = to_partner(far, 1)
    first, near, far = lax.optimization_barrier((first, near, far))
    mine = first.reshape(1, -1, width)
    partner = swap(mine, "chip")
    arrived = [jnp.stack([near[0], far[0]])] + [
        to_partner(jnp.stack([near[half], far[half]]), 2 * half) for half in range(1, n_row // 2)
    ]
    second = finished(quarters[:1], None, second, others[3])
    partner, second, arrived = lax.optimization_barrier((partner, second, arrived))
    pair = jnp.concatenate([mine, partner])
    siblings = swap(pair, "core")
    arrived = jnp.concatenate(arrived).reshape(-1, in_width)
    home_grad = jnp.dot(enter_partner, arrived, preferred_element_type=jnp.float32)
    first, small = finished(quarters, pair, siblings, others[2])
    return home, chosen(home_grad, others[1]), first, second, chosen(small[:6], others[4])


def general(
    codes,
    features,
    block_keep,
    edge_weight,
    weight_one,
    bias_one,
    gain_one,
    shift_one,
    weight_two,
    bias_two,
    gain_two,
    shift_two,
    cotangent,
    node_valid,
):
    row, col = lax.axis_index("row"), lax.axis_index(COL)
    row_codes = lax.dynamic_index_in_dim(codes, row, 0, False).reshape(-1)
    col_codes = lax.dynamic_index_in_dim(codes, col, 1, False).reshape(-1)
    tile_rows, tile_cols = edge_weight.shape
    blocks_down, blocks_across = block_keep.shape
    block_side = tile_rows // blocks_down
    linked = (row_codes[:, None] == col_codes[None, :]) & (row_codes[:, None] & 1 == 1)
    linked = linked.reshape(blocks_down, block_side, blocks_across, block_side) & (
        block_keep[:, None, :, None] == 1
    )
    masked = edge_weight * linked.reshape(tile_rows, tile_cols).astype(jnp.bfloat16)
    degree_rows = 1.0 + lax.psum(jnp.sum(masked, axis=1, dtype=jnp.float32), COL)
    own_nodes = features.shape[0]
    own_degree = lax.dynamic_slice_in_dim(
        degree_rows, lax.axis_index(COL) * own_nodes, own_nodes, 0
    )
    degree_cols = lax.all_gather(own_degree, "row", axis=0, tiled=True)
    adjacency = (
        masked.astype(jnp.float32)
        * lax.rsqrt(degree_rows)[:, None]
        * lax.rsqrt(degree_cols)[None, :]
    ).astype(jnp.bfloat16)
    valid_rows = node_valid.astype(jnp.float32)
    stacked_one, mixed_one, hidden = layer_forward(
        adjacency,
        features.astype(jnp.float32),
        weight_one,
        bias_one,
        gain_one,
        shift_one,
        valid_rows,
    )
    stacked_two, mixed_two, activations = layer_forward(
        adjacency, hidden, weight_two, bias_two, gain_two, shift_two, valid_rows
    )
    hidden_grad, weight_two_grad, bias_two_grad, gain_two_grad, shift_two_grad = layer_backward(
        adjacency,
        stacked_two,
        mixed_two,
        cotangent.astype(jnp.float32),
        weight_two,
        gain_two,
        shift_two,
        valid_rows,
    )
    input_grad, weight_one_grad, bias_one_grad, gain_one_grad, shift_one_grad = layer_backward(
        adjacency, stacked_one, mixed_one, hidden_grad, weight_one, gain_one, shift_one, valid_rows
    )
    summed = lax.psum(
        (
            weight_one_grad,
            bias_one_grad,
            gain_one_grad,
            shift_one_grad,
            weight_two_grad,
            bias_two_grad,
            gain_two_grad,
            shift_two_grad,
        ),
        ("row",) + COL,
    )
    weight_one_grad, bias_one_grad, gain_one_grad, shift_one_grad = (
        summed[0],
        summed[1],
        summed[2],
        summed[3],
    )
    weight_two_grad, bias_two_grad, gain_two_grad, shift_two_grad = (
        summed[4],
        summed[5],
        summed[6],
        summed[7],
    )
    return (
        activations,
        input_grad,
        weight_one_grad,
        bias_one_grad,
        gain_one_grad,
        shift_one_grad,
        weight_two_grad,
        bias_two_grad,
        gain_two_grad,
        shift_two_grad,
    )


def local(n_row, n_col, *args):
    (
        features,
        node_valid,
        cluster,
        block_keep,
        edge_weight,
        weight_one,
        bias_one,
        gain_one,
        shift_one,
        weight_two,
        bias_two,
        gain_two,
        shift_two,
        cotangent,
    ) = args
    own_nodes, in_width = features.shape
    own_cap = own_nodes * n_row * 5 // 16
    send_cap = own_nodes * n_col * 11 // 32
    seat_cap = own_nodes // 2
    codes = broadcast_along(cluster * 2 + node_valid, ("row",) + COL, n_row * n_col)
    codes = codes.reshape(n_row, n_col, own_nodes)
    shared = (
        block_keep,
        edge_weight,
        weight_one,
        bias_one,
        gain_one,
        shift_one,
        weight_two,
        bias_two,
        gain_two,
        shift_two,
        cotangent,
    )

    def slow():
        return general(codes, features, *shared, node_valid)

    held = (ORDER - 1) * own_cap * own_cap * n_col * 2
    if held > HELD_BYTES or n_col != 4 or n_row < 2 or n_row & (n_row - 1):
        return slow()
    group = assign(codes, n_row)

    def member_of(group):
        return group[None] == jnp.arange(n_row)[:, None, None, None]

    def places_of(group):
        member = member_of(group).transpose(0, 2, 1, 3).reshape(n_row, n_col, -1)
        places = jnp.sum(jnp.where(member, exclusive_counts(member), 0), axis=0)
        return places.reshape(n_col, n_row, own_nodes).transpose(1, 0, 2)

    def slots_of(group):
        member = member_of(group).reshape(n_row, n_row, -1)
        slots = jnp.sum(jnp.where(member, exclusive_counts(member), 0), axis=0)
        return slots.reshape(n_row, n_col, own_nodes)

    def seats_of(group):
        member = member_of(group)
        return jnp.sum(jnp.where(member, exclusive_counts(member), 0), axis=0)

    width = weight_two.shape[2]

    def instead(state):
        made = slow()
        small = jnp.stack([made[place] for place in (3, 4, 5, 7, 8, 9)])
        return (jnp.ones_like(state[0]),) + tuple(
            value.astype(jnp.bfloat16).reshape(like.shape)
            for value, like in zip((made[0], made[1], made[2], made[6], small), state[1:])
        )

    shapes = (
        (own_nodes, width),
        (own_nodes, in_width),
        (n_col, ORDER * in_width // n_col, width),
        (n_col, ORDER * width // n_col, width),
        (6, width),
    )

    def decide(codes):
        fits = fits_in(codes, n_row, (own_cap, send_cap, seat_cap))
        others = lax.while_loop(
            lambda state: state[0][0] == 0,
            instead,
            (fits,) + tuple(jnp.zeros(shape, jnp.bfloat16) for shape in shapes),
        )[1:]
        return fits, others

    home, home_grad, first, second, small = compact(
        codes,
        group,
        features,
        *shared,
        places_of,
        slots_of,
        seats_of,
        decide,
        (n_row, n_col),
        (own_cap, send_cap, seat_cap),
    )
    return (
        home,
        home_grad,
        first.reshape(weight_one.shape),
        small[0],
        small[1],
        small[2],
        second.reshape(weight_two.shape),
        small[3],
        small[4],
        small[5],
    )


def solution(mesh):
    n_row, n_col = mesh.shape["row"], mesh.shape["col"]
    by_core = jax.sharding.Mesh(
        mesh.devices.reshape(n_row, n_col // 2, 2), ("row", "chip", "core")
    )
    nodes = ("row", "chip", "core")
    placed = (
        P(nodes, None),
        P(nodes),
        P(nodes),
        P("row", COL),
        P("row", COL),
        P(),
        P(),
        P(),
        P(),
        P(),
        P(),
        P(),
        P(),
        P(nodes, None),
    )
    return jax.shard_map(
        functools.partial(local, n_row, n_col),
        mesh=by_core,
        in_specs=placed,
        out_specs=(P(nodes, None), P(nodes, None), P(), P(), P(), P(), P(), P(), P(), P()),
        check_vma=False,
    )
```

```python
import functools
import math

import jax
import jax.numpy as jnp
from jax import lax
from jax.experimental import pallas as pl
from jax.experimental.pallas import tpu as pltpu
from jax.sharding import PartitionSpec as P

ORDER = 13
CLUSTERS = 16
HELD_BYTES = 1 << 25
VMEM_BYTES = 32 << 20
TERMS = 3
NO_COST = pl.CostEstimate(flops=1, bytes_accessed=1, transcendentals=0)
COL = ("chip", "core")


def finish(mixed, gain, shift, valid_rows):
    active = jax.nn.gelu(mixed, approximate=False)
    centered = active - jnp.mean(active, axis=-1, keepdims=True)
    variance = jnp.mean(centered * centered, axis=-1, keepdims=True)
    return (centered * lax.rsqrt(variance + 1e-05) * gain + shift) * valid_rows[:, None]


def forward_product(adjacency, piece_low):
    partial_value = jnp.dot(
        adjacency,
        lax.all_gather(piece_low, "row", axis=0, tiled=True),
        preferred_element_type=jnp.float32,
    )
    return lax.psum_scatter(partial_value, COL, scatter_dimension=0, tiled=True)


def backward_product(adjacency, piece_low):
    partial_value = lax.dot_general(
        adjacency,
        lax.all_gather(piece_low, COL, axis=0, tiled=True),
        (((0,), (0,)), ((), ())),
        preferred_element_type=jnp.float32,
    )
    return lax.psum_scatter(
        partial_value.astype(jnp.bfloat16), "row", scatter_dimension=0, tiled=True
    ).astype(jnp.float32)


def layer_forward(adjacency, inputs, weight, bias, gain, shift, valid_rows):
    first_low = inputs.astype(jnp.bfloat16)
    second = -forward_product(adjacency, first_low)
    second_low = second.astype(jnp.bfloat16)

    def advance(state_pair, unused):
        previous, current, current_low = state_pair
        upcoming = -2.0 * forward_product(adjacency, current_low) - previous
        upcoming_low = upcoming.astype(jnp.bfloat16)
        return ((current, upcoming, upcoming_low), upcoming_low)

    ignored, others = lax.scan(advance, (inputs, second, second_low), None, length=ORDER - 2)
    stacked = jnp.concatenate([first_low[None], second_low[None], others], axis=0)
    mixed = jnp.einsum("kni,kio->no", stacked, weight, preferred_element_type=jnp.float32) + bias
    return (stacked, mixed, finish(mixed, gain, shift, valid_rows))


def layer_backward(adjacency, stacked, mixed, upstream, weight, gain, shift, valid_rows):

    def local_finish(mixed_in, gain_in, shift_in):
        return finish(mixed_in, gain_in, shift_in, valid_rows)

    ignored, pullback = jax.vjp(local_finish, mixed, gain, shift)
    mixed_grad, gain_grad, shift_grad = pullback(upstream)
    mixed_low = mixed_grad.astype(jnp.bfloat16)
    bias_grad = jnp.sum(mixed_low.astype(jnp.float32), axis=0)
    weight_grad = jnp.einsum("kni,no->kio", stacked, mixed_low, preferred_element_type=jnp.float32)
    direct = jnp.einsum("no,kio->kni", mixed_low, weight, preferred_element_type=jnp.float32)

    def retreat(state_pair, direct_term):
        later_two, later_one = state_pair
        current = (
            direct_term
            - 2.0 * backward_product(adjacency, later_one.astype(jnp.bfloat16))
            - later_two
        )
        return ((later_one, current), None)

    start_pair = (jnp.zeros_like(direct[0]), direct[ORDER - 1])
    (second_grad, first_grad), unused = lax.scan(
        retreat, start_pair, direct[1 : ORDER - 1], reverse=True
    )
    input_grad = (
        direct[0] - backward_product(adjacency, first_grad.astype(jnp.bfloat16)) - second_grad
    )
    return (input_grad, weight_grad, bias_grad, gain_grad, shift_grad)


def swap(value, axis):
    return lax.ppermute(value, axis, [(0, 1), (1, 0)])


def trade(pieces, axis):
    return lax.all_to_all(pieces, axis, 0, 0, tiled=False)


def broadcast_along(value, axis, size):
    return trade(jnp.broadcast_to(value[None], (size,) + value.shape), axis)


def joined(mine, other, mine_first):
    return jnp.where(
        mine_first, jnp.concatenate([mine, other]), jnp.concatenate([other, mine])
    )


def added(mine, received):
    return (mine.astype(jnp.float32) + received.astype(jnp.float32)).astype(jnp.bfloat16)


def assemble(place_ref, own_ref, sibling_ref, near_ref, far_ref, out_ref, done):
    chip, core = place_ref[0], place_ref[1]
    own_cap, span = own_ref.shape
    half = span // 2

    def rows(of_chip, of_core):
        return pl.ds(pl.multiple_of((2 * of_chip + of_core) * own_cap, own_cap), own_cap)

    def fetch(source, of_chip, of_core, columns, place):
        target = out_ref.at[rows(of_chip, of_core), columns]
        return pltpu.make_async_copy(source, target, done.at[place])

    def quadrant_copies(here):
        there = 1 - here
        columns = pl.ds(there * half, half)
        return (
            fetch(near_ref, there, core, columns, 2),
            fetch(far_ref, there, 1 - core, columns, 3),
        )

    everything = pl.ds(0, span)
    top = (
        fetch(own_ref, chip, core, everything, 0),
        fetch(sibling_ref, chip, 1 - core, everything, 1),
    )

    def of_chip(here):
        there = 1 - here
        copies = top + quadrant_copies(here)
        for copy in copies:
            copy.start()
        for copy in copies:
            copy.wait()
        here_rows = pl.ds(here * half, half)
        for tile in range(half // 128):
            columns = pl.ds(there * half + tile * 128, 128)
            strip = out_ref[here_rows, columns]
            turned = jnp.transpose(strip.astype(jnp.float32)).astype(jnp.bfloat16)
            out_ref[columns, here_rows] = turned

    @pl.when(chip == 0)
    def first():
        of_chip(0)

    @pl.when(chip == 1)
    def second():
        of_chip(1)

    across = jnp.ones((1, span), jnp.float32)
    for tile in range(span // 128):
        across = across + jnp.sum(
            out_ref[pl.ds(tile * 128, 128), :].astype(jnp.float32), axis=0, keepdims=True
        )
    across = lax.rsqrt(across)
    for tile in range(span // 128):
        strip = out_ref[pl.ds(tile * 128, 128), :].astype(jnp.float32)
        down = lax.rsqrt(1.0 + jnp.sum(strip, axis=1, keepdims=True))
        out_ref[pl.ds(tile * 128, 128), :] = (strip * down * across).astype(jnp.bfloat16)


def normalized_block(own, sibling, near, far, place):
    span = own.shape[1]
    return pl.pallas_call(
        assemble,
        out_shape=jax.ShapeDtypeStruct((span, span), jnp.bfloat16),
        in_specs=[pl.BlockSpec(memory_space=pltpu.SMEM)]
        + [pl.BlockSpec(memory_space=pltpu.HBM)] * 4,
        out_specs=pl.BlockSpec(memory_space=pltpu.VMEM),
        scratch_shapes=[pltpu.SemaphoreType.DMA((4,))],
        compiler_params=pltpu.CompilerParams(vmem_limit_bytes=VMEM_BYTES),
        cost_estimate=NO_COST,
        name="normalized_block",
    )(place, own, sibling, near, far)


def pack_kernel(
    keep_ref, row_codes_ref, col_codes_ref, row_keys_ref, col_keys_ref, weight_ref, out_ref,
    masked, picked, rows_hot, cols_hot
):
    tile_rows, tile_cols = weight_ref.shape
    blocks_down, blocks_across = keep_ref.shape
    groups, ignored, lanes = out_ref.shape
    send_cap, own_cap = rows_hot.shape[0] // groups, cols_hot.shape[0] // groups
    high, wide = tile_rows // blocks_down, tile_cols // blocks_across
    for down in range(blocks_down):
        for across in range(blocks_across):
            rows, columns = pl.ds(down * high, high), pl.ds(across * wide, wide)
            own, other = row_codes_ref[rows, :], col_codes_ref[:, columns]
            linked = (own == other) & (own % 2 == 1) & (keep_ref[down, across] == 1)
            weight = weight_ref[rows, columns].astype(jnp.float32)
            masked[rows, columns] = jnp.where(linked, weight, 0.0).astype(jnp.bfloat16)

    def one_hot(keys, start, count):
        standing = lax.broadcasted_iota(jnp.int32, (count, keys.shape[1]), 0) + start
        return jnp.where(standing == keys, 1.0, 0.0).astype(jnp.bfloat16)

    for group in range(groups):
        rows_hot[pl.ds(group * send_cap, send_cap), :] = one_hot(
            row_keys_ref[...], group * send_cap, send_cap
        )
        cols_hot[pl.ds(group * own_cap, own_cap), :] = one_hot(
            col_keys_ref[...], group * own_cap, own_cap
        )
    for tile in range(tile_cols // 256):
        columns = pl.ds(tile * 256, 256)
        picked[:, columns] = jnp.dot(
            rows_hot[...], masked[:, columns], preferred_element_type=jnp.float32
        ).astype(jnp.bfloat16)
    whole, half = own_cap // lanes, send_cap // 2
    for group in range(groups):
        packed = lax.dot_general(
            cols_hot[pl.ds(group * own_cap, own_cap), :],
            picked[pl.ds(group * send_cap, send_cap), :],
            (((1,), (1,)), ((), ())),
            preferred_element_type=jnp.float32,
        ).T
        for tile in range(whole):
            out_ref[group, pl.ds(tile * send_cap, send_cap), :] = packed[
                :, tile * lanes : (tile + 1) * lanes
            ].astype(jnp.bfloat16)
        ends = jnp.concatenate(
            [packed[:half, whole * lanes :], packed[half:, whole * lanes :]], axis=1
        )
        out_ref[group, pl.ds(whole * send_cap, half), :] = ends.astype(jnp.bfloat16)


def packed_pieces(block_keep, row_codes, col_codes, row_keys, col_keys, edge_weight, caps, groups):
    own_cap, send_cap = caps
    tile_rows, tile_cols = edge_weight.shape
    high = own_cap // 128 * send_cap + send_cap // 2
    vector = pl.BlockSpec(memory_space=pltpu.VMEM)
    return pl.pallas_call(
        pack_kernel,
        out_shape=jax.ShapeDtypeStruct((groups, high, 128), jnp.bfloat16),
        in_specs=[pl.BlockSpec(memory_space=pltpu.SMEM)] + [vector] * 5,
        out_specs=vector,
        scratch_shapes=[
            pltpu.VMEM((tile_rows, tile_cols), jnp.bfloat16),
            pltpu.VMEM((groups * send_cap, tile_cols), jnp.bfloat16),
            pltpu.VMEM((groups * send_cap, tile_rows), jnp.bfloat16),
            pltpu.VMEM((groups * own_cap, tile_cols), jnp.bfloat16),
        ],
        compiler_params=pltpu.CompilerParams(vmem_limit_bytes=VMEM_BYTES),
        cost_estimate=NO_COST,
        name="packed_pieces",
    )(block_keep, row_codes[:, None], col_codes[None], row_keys[None], col_keys[None], edge_weight)


def normal_share(mixed):
    return 0.5 * (1.0 + lax.erf(mixed * 0.5**0.5))


def norm_forward(mixed):
    active = mixed * normal_share(mixed)
    centered = active - jnp.mean(active, axis=-1, keepdims=True)
    scale = lax.rsqrt(jnp.mean(centered * centered, axis=-1, keepdims=True) + 1e-05)
    return centered * scale, scale


def norm_backward(mixed, upstream, gain, valid):
    normed, scale = norm_forward(mixed)
    upstream = upstream * valid
    inner = upstream * gain
    inner = inner - jnp.mean(inner, axis=-1, keepdims=True) - normed * jnp.mean(
        inner * normed, axis=-1, keepdims=True
    )
    density = jnp.exp(-0.5 * mixed * mixed) * (1.0 / (2.0 * math.pi) ** 0.5)
    low = (inner * scale * (normal_share(mixed) + mixed * density)).astype(jnp.bfloat16)
    rest = [low.astype(jnp.float32), upstream * normed, upstream]
    return low, [jnp.sum(value, axis=0, keepdims=True) for value in rest]


def weight_gradient(turned_ref, low, core, mine_ref, other_ref):
    part = turned_ref.shape[0] // 4

    def halves(first_ref, second_ref):
        for place in range(4):
            out_ref = second_ref if place % 2 else first_ref
            out_ref[place // 2, :part, :] = jnp.dot(
                turned_ref[place * part : (place + 1) * part, :],
                low,
                preferred_element_type=jnp.float32,
            ).astype(jnp.bfloat16)

    @pl.when(core == 0)
    def low_half_first():
        halves(mine_ref, other_ref)

    @pl.when(core == 1)
    def high_half_first():
        halves(other_ref, mine_ref)


def forward_step(step, powers_ref, all_ref, own_ref, weights, bias_ref, turned, mixed):
    terms, own_cap, span = powers_ref.shape
    fan_in = own_ref.shape[1]

    @pl.when(step == 0)
    def first():
        turned[:fan_in, :] = own_ref[...].T
        mixed[...] = bias_ref[...] + jnp.dot(
            own_ref[...], weights[0][0], preferred_element_type=jnp.float32
        )

    low = jnp.dot(
        powers_ref[...].reshape(terms * own_cap, span),
        all_ref[...],
        preferred_element_type=jnp.float32,
    ).astype(jnp.bfloat16)
    total = mixed[...]
    for term in range(terms):
        part = low[term * own_cap : (term + 1) * own_cap]
        start = pl.multiple_of((1 + step * terms + term) * fan_in, fan_in)
        turned[pl.ds(start, fan_in), :] = part.T
        total = total + jnp.dot(part, weights[1 + term][0], preferred_element_type=jnp.float32)
    mixed[...] = total


def layer_one_kernel(
    powers_ref,
    all_ref,
    own_ref,
    weight_0,
    weight_a,
    weight_b,
    weight_c,
    bias_ref,
    gain_ref,
    shift_ref,
    valid_ref,
    hidden_ref,
    turned_ref,
    mixed_ref,
):
    step = pl.program_id(0)
    weights = (weight_0, weight_a, weight_b, weight_c)
    forward_step(step, powers_ref, all_ref, own_ref, weights, bias_ref, turned_ref, mixed_ref)

    @pl.when(step == pl.num_programs(0) - 1)
    def finish_layer():
        normed, ignored = norm_forward(mixed_ref[...])
        hidden = (normed * gain_ref[...] + shift_ref[...]) * valid_ref[...]
        hidden_ref[...] = hidden.astype(jnp.bfloat16)


def layer_two_kernel(
    place_ref,
    powers_ref,
    all_ref,
    own_ref,
    weight_0,
    weight_a,
    weight_b,
    weight_c,
    bias_ref,
    gain_ref,
    shift_ref,
    valid_ref,
    upstream_ref,
    active_ref,
    low_ref,
    rest_ref,
    mine_ref,
    other_ref,
    turned,
    mixed,
):
    step = pl.program_id(0)
    weights = (weight_0, weight_a, weight_b, weight_c)
    forward_step(step, powers_ref, all_ref, own_ref, weights, bias_ref, turned, mixed)

    @pl.when(step == pl.num_programs(0) - 1)
    def finish_layer():
        normed, ignored = norm_forward(mixed[...])
        active = (normed * gain_ref[...] + shift_ref[...]) * valid_ref[...]
        active_ref[...] = active.astype(jnp.bfloat16)
        low, rest = norm_backward(
            mixed[...], upstream_ref[...].astype(jnp.float32), gain_ref[...], valid_ref[...]
        )
        low_ref[...] = low
        for place in range(3):
            rest_ref[place : place + 1, :] = rest[place]
        weight_gradient(turned, low, place_ref[1], mine_ref, other_ref)


def backward_step(step, powers_ref, all_ref, own_ref, weights, total):
    terms, own_cap, span = powers_ref.shape
    transposed = (((1,), (1,)), ((), ()))

    @pl.when(step == 0)
    def first():
        total[...] = lax.dot_general(
            own_ref[...], weights[0][0], transposed, preferred_element_type=jnp.float32
        )

    low = jnp.dot(
        powers_ref[...].reshape(terms * own_cap, span),
        all_ref[...],
        preferred_element_type=jnp.float32,
    ).astype(jnp.bfloat16)
    value = total[...]
    for term in range(terms):
        value = value + lax.dot_general(
            low[term * own_cap : (term + 1) * own_cap],
            weights[1 + term][0],
            transposed,
            preferred_element_type=jnp.float32,
        )
    total[...] = value


def back_two_kernel(
    place_ref,
    powers_ref,
    all_ref,
    own_ref,
    weight_0,
    weight_a,
    weight_b,
    weight_c,
    turned_ref,
    mixed_ref,
    gain_ref,
    valid_ref,
    rest_ref,
    low_ref,
    mine_ref,
    other_ref,
    total,
):
    step = pl.program_id(0)
    weights = (weight_0, weight_a, weight_b, weight_c)
    backward_step(step, powers_ref, all_ref, own_ref, weights, total)

    @pl.when(step == pl.num_programs(0) - 1)
    def finish_layer():
        low, rest = norm_backward(mixed_ref[...], total[...], gain_ref[...], valid_ref[...])
        low_ref[...] = low
        weight_gradient(turned_ref, low, place_ref[1], mine_ref, other_ref)
        part = turned_ref.shape[0] // 4
        extra = jnp.zeros((2, mine_ref.shape[1] - part, mine_ref.shape[2]), jnp.bfloat16)
        rows = rest + [rest_ref[place : place + 1, :] for place in range(3)]
        rows = jnp.concatenate(rows + [jnp.zeros((10, rows[0].shape[1]), jnp.float32)], axis=0)

        def below(first_ref, second_ref):
            first_ref[:, part:, :] = extra
            second_ref[:, part:, :] = extra
            first_ref[0, part : part + 16, :] = rows.astype(jnp.bfloat16)

        @pl.when(place_ref[1] == 0)
        def low_half_here():
            below(mine_ref, other_ref)

        @pl.when(place_ref[1] == 1)
        def low_half_there():
            below(other_ref, mine_ref)


def back_one_kernel(
    powers_ref, all_ref, own_ref, weight_0, weight_a, weight_b, weight_c, out_ref, total
):
    step = pl.program_id(0)
    weights = (weight_0, weight_a, weight_b, weight_c)
    backward_step(step, powers_ref, all_ref, own_ref, weights, total)

    @pl.when(step == pl.num_programs(0) - 1)
    def finish_layer():
        out_ref[...] = total[...].astype(jnp.bfloat16)


def layer_pass(kernel, name, place, powers, everyone, own, weight, others, outs, scratch):
    ignored, own_cap, span = powers.shape
    fan_in, width = weight.shape[1:]

    def whole(value):
        return pl.BlockSpec(value.shape, lambda step: (0,) * len(value.shape))

    def term_weight(term):
        return pl.BlockSpec((1, fan_in, width), lambda step: (1 + step * TERMS + term, 0, 0))

    in_specs = [
        pl.BlockSpec((TERMS, own_cap, span), lambda step: (step, 0, 0)),
        whole(everyone),
        whole(own),
        pl.BlockSpec((1, fan_in, width), lambda step: (0, 0, 0)),
    ]
    in_specs += [term_weight(term) for term in range(TERMS)] + [whole(value) for value in others]
    operands = [powers, everyone, own] + [weight] * (1 + TERMS) + list(others)
    if place is not None:
        in_specs = [pl.BlockSpec(memory_space=pltpu.SMEM)] + in_specs
        operands = [place] + operands
    return pl.pallas_call(
        kernel,
        grid=((ORDER - 1) // TERMS,),
        out_shape=outs,
        in_specs=in_specs,
        out_specs=[whole(value) for value in outs],
        scratch_shapes=[pltpu.VMEM(shape, dtype) for shape, dtype in scratch],
        compiler_params=pltpu.CompilerParams(vmem_limit_bytes=VMEM_BYTES),
        cost_estimate=NO_COST,
        name=name,
    )(*operands)


def finish_kernel(scalars_ref, *refs):
    step = pl.program_id(0)
    if len(refs) == 3:
        values_ref, other_ref, out_ref = refs
        parts = [(step >= 0, values_ref)]
        small_ref = None
    else:
        pair_ref, siblings_ref, other_ref, out_ref, small_ref = refs
        parts = [(step < 2, pair_ref), (step >= 2, siblings_ref)]
    part = out_ref.shape[1]
    for here, values_ref in parts:
        @pl.when(here & (scalars_ref[0] == 1))
        def fast_form():
            out_ref[0] = values_ref[0, :part, :].astype(jnp.float32)

        if small_ref is not None:
            @pl.when(here & (scalars_ref[1 + step] == 0))
            def small_sums():
                small_ref[...] = values_ref[0, part : part + 16, :].astype(jnp.float32)

    @pl.when(scalars_ref[0] == 0)
    def general_form():
        out_ref[0] = other_ref[0].astype(jnp.float32)


def finished(scalars, pair, values, other):
    count, part, width = other.shape
    one = (1, part, width)
    if pair is None:
        operands, outs = [values, other], [jax.ShapeDtypeStruct(other.shape, jnp.float32)]

        def quarter(step, scalars_ref):
            return step

        in_specs = [pl.BlockSpec((1,) + values.shape[1:], lambda step, ref: (step, 0, 0))]
        small_specs = []
    else:
        operands = [pair, values, other]
        outs = [
            jax.ShapeDtypeStruct(other.shape, jnp.float32),
            jax.ShapeDtypeStruct((16, width), jnp.float32),
        ]

        def quarter(step, scalars_ref):
            return scalars_ref[1 + step]

        in_specs = [
            pl.BlockSpec((1,) + pair.shape[1:], lambda step, ref: (jnp.minimum(step, 1), 0, 0)),
            pl.BlockSpec((1,) + pair.shape[1:], lambda step, ref: (jnp.maximum(step - 2, 0), 0, 0)),
        ]
        small_specs = [pl.BlockSpec((16, width), lambda step, ref: (0, 0))]
    in_specs.append(
        pl.BlockSpec(one, lambda step, ref: ((1 - ref[0]) * quarter(step, ref), 0, 0))
    )
    result = pl.pallas_call(
        finish_kernel,
        grid_spec=pltpu.PrefetchScalarGridSpec(
            num_scalar_prefetch=1,
            grid=(count,),
            in_specs=in_specs,
            out_specs=[pl.BlockSpec(one, lambda step, ref: (quarter(step, ref), 0, 0))]
            + small_specs,
        ),
        out_shape=outs,
        compiler_params=pltpu.CompilerParams(vmem_limit_bytes=VMEM_BYTES),
        cost_estimate=NO_COST,
        name="finished",
    )(scalars, *operands)
    return result[0] if pair is None else result


def unpack_kernel(place_ref, pieces_ref, keys_ref, own_ref, quadrant_ref, columns, hot):
    groups, high, lanes = pieces_ref.shape
    own_cap, span = own_ref.shape
    whole = own_cap // lanes
    send_cap = keys_ref.shape[1] // groups
    half, rest = send_cap // 2, own_cap - whole * lanes
    for group in range(groups):
        start = group * send_cap
        for tile in range(whole):
            columns[start : start + send_cap, tile * lanes : (tile + 1) * lanes] = pieces_ref[
                group, tile * send_cap : (tile + 1) * send_cap, :
            ]
        ends = pieces_ref[group, whole * send_cap :, :]
        columns[start : start + half, whole * lanes :] = ends[:, :rest]
        columns[start + half : start + send_cap, whole * lanes :] = ends[:, rest:]
    standing = lax.broadcasted_iota(jnp.int32, hot.shape, 0)
    hot[...] = jnp.where(standing == keys_ref[...], 1.0, 0.0).astype(jnp.bfloat16)
    block = jnp.dot(hot[...], columns[...], preferred_element_type=jnp.float32)
    own_ref[...] = block.T.astype(jnp.bfloat16)
    middle = span // 2

    @pl.when(place_ref[0] == 0)
    def first():
        quadrant_ref[...] = own_ref[:, :middle]

    @pl.when(place_ref[0] == 1)
    def second():
        quadrant_ref[...] = own_ref[:, middle:]


def unpacked_block(pieces, keys, place, own_cap, span):
    vector = pl.BlockSpec(memory_space=pltpu.VMEM)
    return pl.pallas_call(
        unpack_kernel,
        out_shape=[
            jax.ShapeDtypeStruct((own_cap, span), jnp.bfloat16),
            jax.ShapeDtypeStruct((own_cap, span // 2), jnp.bfloat16),
        ],
        in_specs=[pl.BlockSpec(memory_space=pltpu.SMEM), vector, vector],
        out_specs=[vector, vector],
        scratch_shapes=[
            pltpu.VMEM((keys.shape[1], own_cap), jnp.bfloat16),
            pltpu.VMEM((span, keys.shape[1]), jnp.bfloat16),
        ],
        compiler_params=pltpu.CompilerParams(vmem_limit_bytes=VMEM_BYTES),
        cost_estimate=NO_COST,
        name="unpacked_block",
    )(place, pieces, keys)


def fit_kernel(codes_ref, out_ref, *, n_row, caps):
    own_cap, send_cap, seat_cap = caps
    codes = codes_ref[...]
    devices = codes.shape[0]
    n_col = devices // n_row
    label = lax.broadcasted_iota(jnp.int32, (devices, 128), 1)
    counts = jnp.zeros((devices, 128), jnp.float32)
    for cluster in range(CLUSTERS):
        here = jnp.where(codes == 2 * cluster + 1, 1.0, 0.0)
        counts = counts + jnp.where(
            label == cluster, jnp.sum(here, axis=1, keepdims=True), 0.0
        )
    sizes = jnp.sum(counts, axis=0, keepdims=True)
    across = jnp.broadcast_to(sizes, (128, 128))
    down = across.T
    first = lax.broadcasted_iota(jnp.int32, (128, 128), 0)
    second = lax.broadcasted_iota(jnp.int32, (128, 128), 1)
    ahead = (across > down) | ((across == down) & (second < first))
    ahead = ahead & (second < CLUSTERS)
    rank = jnp.sum(jnp.where(ahead, 1.0, 0.0), axis=1, keepdims=True).astype(jnp.int32)
    others = n_row - 1
    later = rank > others
    turn = jnp.zeros_like(rank)
    for count in range(1, CLUSTERS // others + 1):
        turn = turn + jnp.where(rank - 1 >= count * others, 1, 0)
    place = rank - 1 - turn * others
    group = jnp.where(rank == 0, 0, 1 + jnp.where(later, others - 1 - place, place))
    member = (group == second) & (first < CLUSTERS)
    held = jnp.dot(
        counts.astype(jnp.bfloat16),
        jnp.where(member, 1.0, 0.0).astype(jnp.bfloat16),
        preferred_element_type=jnp.float32,
    )
    by_row = jnp.zeros((1, 128), jnp.float32)
    for row in range(n_row):
        rows = jnp.sum(held[row * n_col : (row + 1) * n_col], axis=0, keepdims=True)
        by_row = jnp.maximum(by_row, rows)
    device = lax.broadcasted_iota(jnp.int32, (devices, 128), 0)
    by_col = jnp.zeros((1, 128), jnp.float32)
    for col in range(n_col):
        cols = jnp.where(device % n_col == col, held, 0.0)
        by_col = jnp.maximum(by_col, jnp.sum(cols, axis=0, keepdims=True))
    fits = (
        (jnp.max(by_col) <= own_cap) & (jnp.max(by_row) <= send_cap) & (jnp.max(held) <= seat_cap)
    )
    out_ref[0] = jnp.where(fits, 1, 0)


def fits_in(codes, n_row, caps):
    fits = pl.pallas_call(
        functools.partial(fit_kernel, n_row=n_row, caps=caps),
        out_shape=jax.ShapeDtypeStruct((1,), jnp.int32),
        in_specs=[pl.BlockSpec(memory_space=pltpu.VMEM)],
        out_specs=pl.BlockSpec(memory_space=pltpu.SMEM),
        cost_estimate=NO_COST,
        name="fits",
    )(codes.reshape(-1, codes.shape[-1]))
    return fits


def exclusive_counts(member):
    count = member.shape[-1]
    before = jnp.arange(count)[:, None] < jnp.arange(count)[None, :]
    return jnp.dot(
        member.astype(jnp.bfloat16),
        before.astype(jnp.bfloat16),
        preferred_element_type=jnp.float32,
    ).astype(jnp.int32)


def assign(codes, n_row):
    cluster, valid = codes >> 1, codes & 1
    labels = jnp.arange(CLUSTERS)
    sizes = jnp.sum(
        (cluster.reshape(1, -1) == labels[:, None]) & (valid.reshape(1, -1) == 1), axis=1
    )
    ahead = (sizes[None, :] > sizes[:, None]) | (
        (sizes[None, :] == sizes[:, None]) & (labels[None, :] < labels[:, None])
    )
    rank = jnp.sum(ahead, axis=1)
    others = n_row - 1
    turn, place = (rank - 1) // others, (rank - 1) % others
    group = jnp.where(rank == 0, 0, 1 + jnp.where(turn == 0, place, others - 1 - place))
    of_node = jnp.sum(
        jnp.where(cluster[None] == labels[:, None, None, None], group[:, None, None, None], 0),
        axis=0,
    )
    return jnp.where(valid == 1, of_node, n_row)


def compact(
    codes,
    group,
    features,
    block_keep,
    edge_weight,
    weight_one,
    bias_one,
    gain_one,
    shift_one,
    weight_two,
    bias_two,
    gain_two,
    shift_two,
    cotangent,
    places_of,
    slots_of,
    seats_of,
    decide,
    sizes,
    caps,
):
    row, col = lax.axis_index("row"), lax.axis_index(COL)
    chip, core = lax.axis_index("chip"), lax.axis_index("core")
    n_row, n_col = sizes
    own_cap, send_cap, seat_cap = caps
    own_nodes, in_width = features.shape
    width = weight_two.shape[2]
    span = n_col * own_cap
    targets = jnp.arange(n_row)

    def in_col(value):
        return lax.dynamic_index_in_dim(value, col, 1, False).reshape(-1)

    def in_row(value):
        return lax.dynamic_index_in_dim(value, row, 0, False).reshape(-1)

    row_group, col_group = in_row(group), in_col(group)
    row_slots, col_places = in_row(slots_of(group)), in_col(places_of(group))
    row_keys = jnp.where(row_slots < send_cap, row_group * send_cap + row_slots, -1)
    col_keys = jnp.where(col_places < own_cap, col_group * own_cap + col_places, -1)
    pieces = packed_pieces(
        block_keep,
        in_row(codes),
        in_col(codes),
        row_keys,
        col_keys,
        edge_weight,
        (own_cap, send_cap),
        n_row,
    )
    pieces, codes = lax.optimization_barrier((pieces, codes))
    group = assign(codes, n_row)
    pieces = trade(pieces, "row")
    places, slots, seats = places_of(group), slots_of(group), seats_of(group)

    standing = jnp.arange(n_col)[None, :, None] * own_cap + places
    fits_here = jnp.where(group == row, standing, -1).reshape(n_row, -1)
    slot_of = slots.reshape(n_row, -1)
    target = jnp.max(
        jnp.where(
            slot_of[:, None, :] == jnp.arange(send_cap)[None, :, None], fits_here[:, None, :], -1
        ),
        axis=2,
    )
    keys = target.reshape(1, -1)

    def to_partner(value, step):
        return lax.ppermute(value, "row", [(place, place ^ step) for place in range(n_row)])

    partners = row ^ targets
    group_here = lax.dynamic_index_in_dim(in_row(group).reshape(n_col, -1), col, 0, False)
    seat_here = lax.dynamic_index_in_dim(in_row(seats).reshape(n_col, -1), col, 0, False)

    def seat_of_node(groups):
        hot = (group_here[None, None, :] == groups[:, None, None]) & (
            seat_here[None, None, :] == jnp.arange(seat_cap)[None, :, None]
        )
        return hot.astype(jnp.bfloat16).reshape(n_row * seat_cap, own_nodes)

    enter_partner = seat_of_node(partners)
    both = jnp.dot(enter_partner, jnp.concatenate([features, cotangent], axis=1))
    both = both.reshape(n_row, seat_cap, -1)
    enter_partner = enter_partner.T
    both, codes = lax.optimization_barrier((both, codes))
    fits, others = decide(codes)
    group_col = lax.dynamic_index_in_dim(group, col, 1, False)
    seats_col = lax.dynamic_index_in_dim(seats, col, 1, False)
    places_col = lax.dynamic_index_in_dim(places, col, 1, False)
    seated = (group_col == row)[:, None, :] & (
        seats_col[:, None, :] == jnp.arange(seat_cap)[None, :, None]
    )
    place_of_seat = jnp.max(jnp.where(seated, places_col[:, None, :], -1), axis=2)
    from_partner = jnp.max(
        jnp.where((partners[:, None] == targets)[:, :, None], place_of_seat[None], -1), axis=1
    )
    arrive = from_partner.reshape(1, -1) == jnp.arange(own_cap)[:, None]
    arrive = arrive.astype(jnp.bfloat16)
    leave_partner = jnp.concatenate([from_partner[::2], from_partner[1::2]])
    leave_partner = leave_partner.reshape(-1, 1) == jnp.arange(own_cap)
    leave_partner = leave_partner.astype(jnp.bfloat16)
    held_count = jnp.sum(group_col == row)
    valid_rows = (jnp.arange(own_cap) < held_count).astype(jnp.float32)[:, None]
    place = jnp.stack([chip, core]).astype(jnp.int32)
    quarters = jnp.stack([col, (1 - chip) * 2 + core, chip * 2 + 1 - core, 3 - col])
    quarters = jnp.concatenate([fits, quarters.astype(jnp.int32)])
    scalars = (chip, 1 - chip, col * own_cap)
    scalars = tuple(value.astype(jnp.uint32) for value in scalars) + (chip == 0, core == 0, place, quarters)
    homes = enter_partner, leave_partner
    pieces, both, keys, arrive, homes, valid_rows, others, scalars = lax.optimization_barrier(
        (pieces, both, keys, arrive, homes, valid_rows, others, scalars)
    )
    enter_partner, leave_partner = homes
    this_chip, other_chip, own_start, first_chip, first_core, place, quarters = scalars

    own_block, quadrant = unpacked_block(pieces, keys, place, own_cap, span)
    quadrant = swap(quadrant, "chip")
    both = [both[0]] + [to_partner(both[step], step) for step in range(1, n_row)]
    sibling = swap(own_block, "core")
    quadrant, *early = lax.optimization_barrier((quadrant, *both[:-2]))
    adjacency = normalized_block(own_block, sibling, quadrant, swap(quadrant, "core"), place)
    adjacency, *late = lax.optimization_barrier((adjacency, *both[-2:]))
    both = early + late
    mine = jnp.dot(arrive, jnp.concatenate(both))
    features_own, cotangent_own = mine[:, :in_width], mine[:, in_width:]
    sibling = swap(features_own, "core")

    first = (own_start + jnp.arange(own_cap, dtype=jnp.uint32))[:, None]
    first = first == jnp.arange(span, dtype=jnp.uint32)[None, :]
    previous = first.astype(jnp.float32)
    current = -lax.dynamic_slice_in_dim(adjacency, own_start, own_cap, 0).astype(jnp.float32)
    lowered = [current.astype(jnp.bfloat16)]
    for position in range(2, ORDER):
        upcoming = (
            -2.0 * jnp.dot(lowered[-1], adjacency, preferred_element_type=jnp.float32) - previous
        )
        low = upcoming.astype(jnp.bfloat16)
        if position == 4:
            low, sibling = lax.optimization_barrier((low, sibling))
            features_chip = joined(features_own, sibling, first_core)
            partner = swap(features_chip, "chip")
        if position == 8:
            low, partner = lax.optimization_barrier((low, partner))
            features_all = joined(features_chip, partner, first_chip)
        previous, current = current, upcoming
        lowered.append(low)
    powers = jnp.concatenate(lowered, axis=0).reshape(ORDER - 1, own_cap, span)

    def everywhere(value_low):
        return lax.all_gather(value_low, COL, axis=0, tiled=True)

    def chosen(value, other):
        return jnp.where(quarters[0] == 1, value.astype(jnp.float32), other.astype(jnp.float32))

    def shaped(*shape, dtype=jnp.bfloat16):
        return jax.ShapeDtypeStruct(shape, dtype)

    part_one, part_two = ORDER * in_width // n_col, ORDER * width // n_col
    padded = -(-(part_one + 16) // (8 * n_row)) * (8 * n_row)
    hidden, turned_one, mixed_one = layer_pass(
        layer_one_kernel,
        "layer_one",
        None,
        powers,
        features_all,
        features_own,
        weight_one,
        [bias_one[None], gain_one[None], shift_one[None], valid_rows],
        [
            shaped(own_cap, width),
            shaped(n_col * part_one, own_cap),
            shaped(own_cap, width, dtype=jnp.float32),
        ],
        [],
    )
    activations, low_two, rest_two, mine, other = layer_pass(
        layer_two_kernel,
        "layer_two",
        place,
        powers,
        everywhere(hidden),
        hidden,
        weight_two,
        [bias_two[None], gain_two[None], shift_two[None], valid_rows, cotangent_own],
        [
            shaped(own_cap, width),
            shaped(own_cap, width),
            shaped(3, width, dtype=jnp.float32),
            shaped(2, part_two, width),
            shaped(2, part_two, width),
        ],
        [((n_col * part_two, own_cap), jnp.bfloat16), ((own_cap, width), jnp.float32)],
    )

    def add_cores(mine, other):
        got = swap(other, "core")
        return tuple(
            added(
                lax.dynamic_index_in_dim(mine, index, 0, False),
                lax.dynamic_index_in_dim(got, index, 0, False),
            )
            for index in (this_chip, other_chip)
        )

    leaving = jnp.dot(leave_partner, activations).reshape(n_row, seat_cap, width)
    near, far = leaving[: n_row // 2], leaving[n_row // 2 :]
    far = to_partner(far, 1)
    here, there = add_cores(mine, other)
    everyone_two, there, far = lax.optimization_barrier((everywhere(low_two), there, far))
    there = swap(there, "chip")
    arrived = [jnp.stack([near[0], far[0]])] + [
        to_partner(jnp.stack([near[half], far[half]]), 2 * half) for half in range(1, n_row // 2)
    ]
    low_one, mine, other = layer_pass(
        back_two_kernel,
        "back_two",
        place,
        powers,
        everyone_two,
        low_two,
        weight_two,
        [turned_one, mixed_one, gain_one[None], valid_rows, rest_two],
        [shaped(own_cap, width), shaped(2, padded, width), shaped(2, padded, width)],
        [((own_cap, width), jnp.float32)],
    )
    low_one, there, arrived = lax.optimization_barrier((low_one, there, arrived))
    second = added(here, there).reshape(n_row, -1, width)
    many = second.shape[1]
    low_one, second = lax.optimization_barrier((low_one, second))
    second = trade(second, "row")
    here, there = add_cores(mine, other)
    there = swap(there, "chip")
    first = added(here, there).reshape(n_row, -1, width)
    share = first.shape[1]
    second = jnp.sum(second.astype(jnp.float32), axis=0).astype(jnp.bfloat16)
    second = jnp.broadcast_to(second[None], (n_row,) + second.shape)
    mixed = jnp.concatenate([second, first], axis=1)
    low_one, mixed = lax.optimization_barrier((low_one, mixed))
    everyone_one = everywhere(low_one)
    mixed = trade(mixed, "row")
    (input_grad,) = layer_pass(
        back_one_kernel,
        "back_one",
        None,
        powers,
        everyone_one,
        low_one,
        weight_one,
        [],
        [shaped(own_cap, in_width)],
        [((own_cap, in_width), jnp.float32)],
    )
    leaving = jnp.dot(leave_partner, input_grad).reshape(n_row, seat_cap, in_width)
    arrived = jnp.concatenate(arrived).reshape(-1, width)
    home = jnp.dot(enter_partner, arrived, preferred_element_type=jnp.float32)
    home = chosen(home, others[0])
    mixed, leaving, home = lax.optimization_barrier((mixed, leaving, home))
    first = jnp.sum(mixed[:, many:].astype(jnp.float32), axis=0).astype(jnp.bfloat16)
    first = jnp.broadcast_to(first[None], (n_row,) + first.shape)
    first, mixed, leaving = lax.optimization_barrier((first, mixed, leaving))
    first = trade(first, "row")
    second = lax.all_gather(mixed[:, :many].reshape(-1, width), COL, axis=0)
    near, far = leaving[: n_row // 2], leaving[n_row // 2 :]
    far = to_partner(far, 1)
    arrived = [jnp.stack([near[0], far[0]])] + [
        to_partner(jnp.stack([near[half], far[half]]), 2 * half) for half in range(1, n_row // 2)
    ]
    first, arrived = lax.optimization_barrier((first, arrived))
    mine = first.reshape(1, -1, width)
    partner = swap(mine, "chip")
    arrived = jnp.concatenate(arrived).reshape(-1, in_width)
    home_grad = jnp.dot(enter_partner, arrived, preferred_element_type=jnp.float32)
    home_grad = chosen(home_grad, others[1])
    second = finished(quarters[:1], None, second, others[3])
    partner, second, home_grad = lax.optimization_barrier((partner, second, home_grad))
    pair = jnp.concatenate([mine, partner])
    siblings = swap(pair, "core")
    first, small = finished(quarters, pair, siblings, others[2])
    return home, home_grad, first, second, chosen(small[:6], others[4])


def general(
    codes,
    features,
    block_keep,
    edge_weight,
    weight_one,
    bias_one,
    gain_one,
    shift_one,
    weight_two,
    bias_two,
    gain_two,
    shift_two,
    cotangent,
    node_valid,
):
    row, col = lax.axis_index("row"), lax.axis_index(COL)
    row_codes = lax.dynamic_index_in_dim(codes, row, 0, False).reshape(-1)
    col_codes = lax.dynamic_index_in_dim(codes, col, 1, False).reshape(-1)
    tile_rows, tile_cols = edge_weight.shape
    blocks_down, blocks_across = block_keep.shape
    block_side = tile_rows // blocks_down
    linked = (row_codes[:, None] == col_codes[None, :]) & (row_codes[:, None] & 1 == 1)
    linked = linked.reshape(blocks_down, block_side, blocks_across, block_side) & (
        block_keep[:, None, :, None] == 1
    )
    masked = edge_weight * linked.reshape(tile_rows, tile_cols).astype(jnp.bfloat16)
    degree_rows = 1.0 + lax.psum(jnp.sum(masked, axis=1, dtype=jnp.float32), COL)
    own_nodes = features.shape[0]
    own_degree = lax.dynamic_slice_in_dim(
        degree_rows, lax.axis_index(COL) * own_nodes, own_nodes, 0
    )
    degree_cols = lax.all_gather(own_degree, "row", axis=0, tiled=True)
    adjacency = (
        masked.astype(jnp.float32)
        * lax.rsqrt(degree_rows)[:, None]
        * lax.rsqrt(degree_cols)[None, :]
    ).astype(jnp.bfloat16)
    valid_rows = node_valid.astype(jnp.float32)
    stacked_one, mixed_one, hidden = layer_forward(
        adjacency,
        features.astype(jnp.float32),
        weight_one,
        bias_one,
        gain_one,
        shift_one,
        valid_rows,
    )
    stacked_two, mixed_two, activations = layer_forward(
        adjacency, hidden, weight_two, bias_two, gain_two, shift_two, valid_rows
    )
    hidden_grad, weight_two_grad, bias_two_grad, gain_two_grad, shift_two_grad = layer_backward(
        adjacency,
        stacked_two,
        mixed_two,
        cotangent.astype(jnp.float32),
        weight_two,
        gain_two,
        shift_two,
        valid_rows,
    )
    input_grad, weight_one_grad, bias_one_grad, gain_one_grad, shift_one_grad = layer_backward(
        adjacency, stacked_one, mixed_one, hidden_grad, weight_one, gain_one, shift_one, valid_rows
    )
    summed = lax.psum(
        (
            weight_one_grad,
            bias_one_grad,
            gain_one_grad,
            shift_one_grad,
            weight_two_grad,
            bias_two_grad,
            gain_two_grad,
            shift_two_grad,
        ),
        ("row",) + COL,
    )
    weight_one_grad, bias_one_grad, gain_one_grad, shift_one_grad = (
        summed[0],
        summed[1],
        summed[2],
        summed[3],
    )
    weight_two_grad, bias_two_grad, gain_two_grad, shift_two_grad = (
        summed[4],
        summed[5],
        summed[6],
        summed[7],
    )
    return (
        activations,
        input_grad,
        weight_one_grad,
        bias_one_grad,
        gain_one_grad,
        shift_one_grad,
        weight_two_grad,
        bias_two_grad,
        gain_two_grad,
        shift_two_grad,
    )


def local(n_row, n_col, *args):
    (
        features,
        node_valid,
        cluster,
        block_keep,
        edge_weight,
        weight_one,
        bias_one,
        gain_one,
        shift_one,
        weight_two,
        bias_two,
        gain_two,
        shift_two,
        cotangent,
    ) = args
    own_nodes, in_width = features.shape
    own_cap = own_nodes * n_row * 5 // 16
    send_cap = own_nodes * n_col * 11 // 32
    seat_cap = own_nodes // 2
    codes = broadcast_along(cluster * 2 + node_valid, ("row",) + COL, n_row * n_col)
    codes = codes.reshape(n_row, n_col, own_nodes)
    shared = (
        block_keep,
        edge_weight,
        weight_one,
        bias_one,
        gain_one,
        shift_one,
        weight_two,
        bias_two,
        gain_two,
        shift_two,
        cotangent,
    )

    def slow():
        return general(codes, features, *shared, node_valid)

    held = (ORDER - 1) * own_cap * own_cap * n_col * 2
    if held > HELD_BYTES or n_col != 4 or n_row < 2 or n_row & (n_row - 1):
        return slow()
    group = assign(codes, n_row)

    def member_of(group):
        return group[None] == jnp.arange(n_row)[:, None, None, None]

    def places_of(group):
        member = member_of(group).transpose(0, 2, 1, 3).reshape(n_row, n_col, -1)
        places = jnp.sum(jnp.where(member, exclusive_counts(member), 0), axis=0)
        return places.reshape(n_col, n_row, own_nodes).transpose(1, 0, 2)

    def slots_of(group):
        member = member_of(group).reshape(n_row, n_row, -1)
        slots = jnp.sum(jnp.where(member, exclusive_counts(member), 0), axis=0)
        return slots.reshape(n_row, n_col, own_nodes)

    def seats_of(group):
        member = member_of(group)
        return jnp.sum(jnp.where(member, exclusive_counts(member), 0), axis=0)

    width = weight_two.shape[2]

    def instead(state):
        made = slow()
        small = jnp.stack([made[place] for place in (3, 4, 5, 7, 8, 9)])
        return (jnp.ones_like(state[0]),) + tuple(
            value.astype(jnp.bfloat16).reshape(like.shape)
            for value, like in zip((made[0], made[1], made[2], made[6], small), state[1:])
        )

    shapes = (
        (own_nodes, width),
        (own_nodes, in_width),
        (n_col, ORDER * in_width // n_col, width),
        (n_col, ORDER * width // n_col, width),
        (6, width),
    )

    def decide(codes):
        fits = fits_in(codes, n_row, (own_cap, send_cap, seat_cap))
        others = lax.while_loop(
            lambda state: state[0][0] == 0,
            instead,
            (fits,) + tuple(jnp.zeros(shape, jnp.bfloat16) for shape in shapes),
        )[1:]
        return fits, others

    home, home_grad, first, second, small = compact(
        codes,
        group,
        features,
        *shared,
        places_of,
        slots_of,
        seats_of,
        decide,
        (n_row, n_col),
        (own_cap, send_cap, seat_cap),
    )
    return (
        home,
        home_grad,
        first.reshape(weight_one.shape),
        small[0],
        small[1],
        small[2],
        second.reshape(weight_two.shape),
        small[3],
        small[4],
        small[5],
    )


def solution(mesh):
    n_row, n_col = mesh.shape["row"], mesh.shape["col"]
    by_core = jax.sharding.Mesh(
        mesh.devices.reshape(n_row, n_col // 2, 2), ("row", "chip", "core")
    )
    nodes = ("row", "chip", "core")
    placed = (
        P(nodes, None),
        P(nodes),
        P(nodes),
        P("row", COL),
        P("row", COL),
        P(),
        P(),
        P(),
        P(),
        P(),
        P(),
        P(),
        P(),
        P(nodes, None),
    )
    return jax.shard_map(
        functools.partial(local, n_row, n_col),
        mesh=by_core,
        in_specs=placed,
        out_specs=(P(nodes, None), P(nodes, None), P(), P(), P(), P(), P(), P(), P(), P()),
        check_vma=False,
    )
```

```python
import functools
import math

import jax
import jax.numpy as jnp
from jax import lax
from jax.experimental import pallas as pl
from jax.experimental.pallas import tpu as pltpu
from jax.sharding import PartitionSpec as P

ORDER = 13
CLUSTERS = 16
HELD_BYTES = 1 << 25
VMEM_BYTES = 32 << 20
TERMS = 3
NO_COST = pl.CostEstimate(flops=1, bytes_accessed=1, transcendentals=0)
COL = ("chip", "core")


def finish(mixed, gain, shift, valid_rows):
    active = jax.nn.gelu(mixed, approximate=False)
    centered = active - jnp.mean(active, axis=-1, keepdims=True)
    variance = jnp.mean(centered * centered, axis=-1, keepdims=True)
    return (centered * lax.rsqrt(variance + 1e-05) * gain + shift) * valid_rows[:, None]


def forward_product(adjacency, piece_low):
    partial_value = jnp.dot(
        adjacency,
        lax.all_gather(piece_low, "row", axis=0, tiled=True),
        preferred_element_type=jnp.float32,
    )
    return lax.psum_scatter(partial_value, COL, scatter_dimension=0, tiled=True)


def backward_product(adjacency, piece_low):
    partial_value = lax.dot_general(
        adjacency,
        lax.all_gather(piece_low, COL, axis=0, tiled=True),
        (((0,), (0,)), ((), ())),
        preferred_element_type=jnp.float32,
    )
    return lax.psum_scatter(
        partial_value.astype(jnp.bfloat16), "row", scatter_dimension=0, tiled=True
    ).astype(jnp.float32)


def layer_forward(adjacency, inputs, weight, bias, gain, shift, valid_rows):
    first_low = inputs.astype(jnp.bfloat16)
    second = -forward_product(adjacency, first_low)
    second_low = second.astype(jnp.bfloat16)

    def advance(state_pair, unused):
        previous, current, current_low = state_pair
        upcoming = -2.0 * forward_product(adjacency, current_low) - previous
        upcoming_low = upcoming.astype(jnp.bfloat16)
        return ((current, upcoming, upcoming_low), upcoming_low)

    ignored, others = lax.scan(advance, (inputs, second, second_low), None, length=ORDER - 2)
    stacked = jnp.concatenate([first_low[None], second_low[None], others], axis=0)
    mixed = jnp.einsum("kni,kio->no", stacked, weight, preferred_element_type=jnp.float32) + bias
    return (stacked, mixed, finish(mixed, gain, shift, valid_rows))


def layer_backward(adjacency, stacked, mixed, upstream, weight, gain, shift, valid_rows):

    def local_finish(mixed_in, gain_in, shift_in):
        return finish(mixed_in, gain_in, shift_in, valid_rows)

    ignored, pullback = jax.vjp(local_finish, mixed, gain, shift)
    mixed_grad, gain_grad, shift_grad = pullback(upstream)
    mixed_low = mixed_grad.astype(jnp.bfloat16)
    bias_grad = jnp.sum(mixed_low.astype(jnp.float32), axis=0)
    weight_grad = jnp.einsum("kni,no->kio", stacked, mixed_low, preferred_element_type=jnp.float32)
    direct = jnp.einsum("no,kio->kni", mixed_low, weight, preferred_element_type=jnp.float32)

    def retreat(state_pair, direct_term):
        later_two, later_one = state_pair
        current = (
            direct_term
            - 2.0 * backward_product(adjacency, later_one.astype(jnp.bfloat16))
            - later_two
        )
        return ((later_one, current), None)

    start_pair = (jnp.zeros_like(direct[0]), direct[ORDER - 1])
    (second_grad, first_grad), unused = lax.scan(
        retreat, start_pair, direct[1 : ORDER - 1], reverse=True
    )
    input_grad = (
        direct[0] - backward_product(adjacency, first_grad.astype(jnp.bfloat16)) - second_grad
    )
    return (input_grad, weight_grad, bias_grad, gain_grad, shift_grad)


def swap(value, axis):
    return lax.ppermute(value, axis, [(0, 1), (1, 0)])


def trade(pieces, axis):
    return lax.all_to_all(pieces, axis, 0, 0, tiled=False)


def broadcast_along(value, axis, size):
    return trade(jnp.broadcast_to(value[None], (size,) + value.shape), axis)


def joined(mine, other, mine_first):
    return jnp.where(
        mine_first, jnp.concatenate([mine, other]), jnp.concatenate([other, mine])
    )


def added(mine, received):
    return (mine.astype(jnp.float32) + received.astype(jnp.float32)).astype(jnp.bfloat16)


def assemble(place_ref, own_ref, sibling_ref, near_ref, far_ref, out_ref, done):
    chip, core = place_ref[0], place_ref[1]
    own_cap, span = own_ref.shape
    half = span // 2

    def rows(of_chip, of_core):
        return pl.ds(pl.multiple_of((2 * of_chip + of_core) * own_cap, own_cap), own_cap)

    def fetch(source, of_chip, of_core, columns, place):
        target = out_ref.at[rows(of_chip, of_core), columns]
        return pltpu.make_async_copy(source, target, done.at[place])

    def quadrant_copies(here):
        there = 1 - here
        columns = pl.ds(there * half, half)
        return (
            fetch(near_ref, there, core, columns, 2),
            fetch(far_ref, there, 1 - core, columns, 3),
        )

    everything = pl.ds(0, span)
    top = (
        fetch(own_ref, chip, core, everything, 0),
        fetch(sibling_ref, chip, 1 - core, everything, 1),
    )

    def of_chip(here):
        there = 1 - here
        copies = top + quadrant_copies(here)
        for copy in copies:
            copy.start()
        for copy in copies:
            copy.wait()
        here_rows = pl.ds(here * half, half)
        for tile in range(half // 128):
            columns = pl.ds(there * half + tile * 128, 128)
            strip = out_ref[here_rows, columns]
            turned = jnp.transpose(strip.astype(jnp.float32)).astype(jnp.bfloat16)
            out_ref[columns, here_rows] = turned

    @pl.when(chip == 0)
    def first():
        of_chip(0)

    @pl.when(chip == 1)
    def second():
        of_chip(1)

    across = jnp.ones((1, span), jnp.float32)
    for tile in range(span // 128):
        across = across + jnp.sum(
            out_ref[pl.ds(tile * 128, 128), :].astype(jnp.float32), axis=0, keepdims=True
        )
    across = lax.rsqrt(across)
    for tile in range(span // 128):
        strip = out_ref[pl.ds(tile * 128, 128), :].astype(jnp.float32)
        down = lax.rsqrt(1.0 + jnp.sum(strip, axis=1, keepdims=True))
        out_ref[pl.ds(tile * 128, 128), :] = (strip * down * across).astype(jnp.bfloat16)


def normalized_block(own, sibling, near, far, place):
    span = own.shape[1]
    return pl.pallas_call(
        assemble,
        out_shape=jax.ShapeDtypeStruct((span, span), jnp.bfloat16),
        in_specs=[pl.BlockSpec(memory_space=pltpu.SMEM)]
        + [pl.BlockSpec(memory_space=pltpu.HBM)] * 4,
        out_specs=pl.BlockSpec(memory_space=pltpu.VMEM),
        scratch_shapes=[pltpu.SemaphoreType.DMA((4,))],
        compiler_params=pltpu.CompilerParams(vmem_limit_bytes=VMEM_BYTES),
        cost_estimate=NO_COST,
        name="normalized_block",
    )(place, own, sibling, near, far)


def pack_kernel(
    keep_ref, row_codes_ref, col_codes_ref, row_keys_ref, col_keys_ref, weight_ref, out_ref,
    masked, picked, rows_hot, cols_hot
):
    tile_rows, tile_cols = weight_ref.shape
    blocks_down, blocks_across = keep_ref.shape
    groups, ignored, lanes = out_ref.shape
    send_cap, own_cap = rows_hot.shape[0] // groups, cols_hot.shape[0] // groups
    high, wide = tile_rows // blocks_down, tile_cols // blocks_across
    for down in range(blocks_down):
        for across in range(blocks_across):
            rows, columns = pl.ds(down * high, high), pl.ds(across * wide, wide)
            own, other = row_codes_ref[rows, :], col_codes_ref[:, columns]
            linked = (own == other) & (own % 2 == 1) & (keep_ref[down, across] == 1)
            weight = weight_ref[rows, columns].astype(jnp.float32)
            masked[rows, columns] = jnp.where(linked, weight, 0.0).astype(jnp.bfloat16)

    def one_hot(keys, start, count):
        standing = lax.broadcasted_iota(jnp.int32, (count, keys.shape[1]), 0) + start
        return jnp.where(standing == keys, 1.0, 0.0).astype(jnp.bfloat16)

    for group in range(groups):
        rows_hot[pl.ds(group * send_cap, send_cap), :] = one_hot(
            row_keys_ref[...], group * send_cap, send_cap
        )
        cols_hot[pl.ds(group * own_cap, own_cap), :] = one_hot(
            col_keys_ref[...], group * own_cap, own_cap
        )
    for tile in range(tile_cols // 256):
        columns = pl.ds(tile * 256, 256)
        picked[:, columns] = jnp.dot(
            rows_hot[...], masked[:, columns], preferred_element_type=jnp.float32
        ).astype(jnp.bfloat16)
    whole, half = own_cap // lanes, send_cap // 2
    for group in range(groups):
        packed = lax.dot_general(
            cols_hot[pl.ds(group * own_cap, own_cap), :],
            picked[pl.ds(group * send_cap, send_cap), :],
            (((1,), (1,)), ((), ())),
            preferred_element_type=jnp.float32,
        ).T
        for tile in range(whole):
            out_ref[group, pl.ds(tile * send_cap, send_cap), :] = packed[
                :, tile * lanes : (tile + 1) * lanes
            ].astype(jnp.bfloat16)
        ends = jnp.concatenate(
            [packed[:half, whole * lanes :], packed[half:, whole * lanes :]], axis=1
        )
        out_ref[group, pl.ds(whole * send_cap, half), :] = ends.astype(jnp.bfloat16)


def packed_pieces(block_keep, row_codes, col_codes, row_keys, col_keys, edge_weight, caps, groups):
    own_cap, send_cap = caps
    tile_rows, tile_cols = edge_weight.shape
    high = own_cap // 128 * send_cap + send_cap // 2
    vector = pl.BlockSpec(memory_space=pltpu.VMEM)
    return pl.pallas_call(
        pack_kernel,
        out_shape=jax.ShapeDtypeStruct((groups, high, 128), jnp.bfloat16),
        in_specs=[pl.BlockSpec(memory_space=pltpu.SMEM)] + [vector] * 5,
        out_specs=vector,
        scratch_shapes=[
            pltpu.VMEM((tile_rows, tile_cols), jnp.bfloat16),
            pltpu.VMEM((groups * send_cap, tile_cols), jnp.bfloat16),
            pltpu.VMEM((groups * send_cap, tile_rows), jnp.bfloat16),
            pltpu.VMEM((groups * own_cap, tile_cols), jnp.bfloat16),
        ],
        compiler_params=pltpu.CompilerParams(vmem_limit_bytes=VMEM_BYTES),
        cost_estimate=NO_COST,
        name="packed_pieces",
    )(block_keep, row_codes[:, None], col_codes[None], row_keys[None], col_keys[None], edge_weight)


def normal_share(mixed):
    return 0.5 * (1.0 + lax.erf(mixed * 0.5**0.5))


def norm_forward(mixed):
    active = mixed * normal_share(mixed)
    centered = active - jnp.mean(active, axis=-1, keepdims=True)
    scale = lax.rsqrt(jnp.mean(centered * centered, axis=-1, keepdims=True) + 1e-05)
    return centered * scale, scale


def norm_backward(mixed, upstream, gain, valid):
    normed, scale = norm_forward(mixed)
    upstream = upstream * valid
    inner = upstream * gain
    inner = inner - jnp.mean(inner, axis=-1, keepdims=True) - normed * jnp.mean(
        inner * normed, axis=-1, keepdims=True
    )
    density = jnp.exp(-0.5 * mixed * mixed) * (1.0 / (2.0 * math.pi) ** 0.5)
    low = (inner * scale * (normal_share(mixed) + mixed * density)).astype(jnp.bfloat16)
    rest = [low.astype(jnp.float32), upstream * normed, upstream]
    return low, [jnp.sum(value, axis=0, keepdims=True) for value in rest]


def weight_gradient(turned_ref, low, core, mine_ref, other_ref):
    part = turned_ref.shape[0] // 4

    def halves(first_ref, second_ref):
        for place in range(4):
            out_ref = second_ref if place % 2 else first_ref
            out_ref[place // 2, :part, :] = jnp.dot(
                turned_ref[place * part : (place + 1) * part, :],
                low,
                preferred_element_type=jnp.float32,
            ).astype(jnp.bfloat16)

    @pl.when(core == 0)
    def low_half_first():
        halves(mine_ref, other_ref)

    @pl.when(core == 1)
    def high_half_first():
        halves(other_ref, mine_ref)


def forward_step(step, powers_ref, all_ref, own_ref, weights, bias_ref, turned, mixed):
    terms, own_cap, span = powers_ref.shape
    fan_in = own_ref.shape[1]

    @pl.when(step == 0)
    def first():
        turned[:fan_in, :] = own_ref[...].T
        mixed[...] = bias_ref[...] + jnp.dot(
            own_ref[...], weights[0][0], preferred_element_type=jnp.float32
        )

    low = jnp.dot(
        powers_ref[...].reshape(terms * own_cap, span),
        all_ref[...],
        preferred_element_type=jnp.float32,
    ).astype(jnp.bfloat16)
    total = mixed[...]
    for term in range(terms):
        part = low[term * own_cap : (term + 1) * own_cap]
        start = pl.multiple_of((1 + step * terms + term) * fan_in, fan_in)
        turned[pl.ds(start, fan_in), :] = part.T
        total = total + jnp.dot(part, weights[1 + term][0], preferred_element_type=jnp.float32)
    mixed[...] = total


def layer_one_kernel(
    powers_ref,
    all_ref,
    own_ref,
    weight_0,
    weight_a,
    weight_b,
    weight_c,
    bias_ref,
    gain_ref,
    shift_ref,
    valid_ref,
    hidden_ref,
    turned_ref,
    mixed_ref,
):
    step = pl.program_id(0)
    weights = (weight_0, weight_a, weight_b, weight_c)
    forward_step(step, powers_ref, all_ref, own_ref, weights, bias_ref, turned_ref, mixed_ref)

    @pl.when(step == pl.num_programs(0) - 1)
    def finish_layer():
        normed, ignored = norm_forward(mixed_ref[...])
        hidden = (normed * gain_ref[...] + shift_ref[...]) * valid_ref[...]
        hidden_ref[...] = hidden.astype(jnp.bfloat16)


def layer_two_kernel(
    place_ref,
    powers_ref,
    all_ref,
    own_ref,
    weight_0,
    weight_a,
    weight_b,
    weight_c,
    bias_ref,
    gain_ref,
    shift_ref,
    valid_ref,
    upstream_ref,
    active_ref,
    low_ref,
    rest_ref,
    mine_ref,
    other_ref,
    turned,
    mixed,
):
    step = pl.program_id(0)
    weights = (weight_0, weight_a, weight_b, weight_c)
    forward_step(step, powers_ref, all_ref, own_ref, weights, bias_ref, turned, mixed)

    @pl.when(step == pl.num_programs(0) - 1)
    def finish_layer():
        normed, ignored = norm_forward(mixed[...])
        active = (normed * gain_ref[...] + shift_ref[...]) * valid_ref[...]
        active_ref[...] = active.astype(jnp.bfloat16)
        low, rest = norm_backward(
            mixed[...], upstream_ref[...].astype(jnp.float32), gain_ref[...], valid_ref[...]
        )
        low_ref[...] = low
        for place in range(3):
            rest_ref[place : place + 1, :] = rest[place]
        weight_gradient(turned, low, place_ref[1], mine_ref, other_ref)


def backward_step(step, powers_ref, all_ref, own_ref, weights, total):
    terms, own_cap, span = powers_ref.shape
    transposed = (((1,), (1,)), ((), ()))

    @pl.when(step == 0)
    def first():
        total[...] = lax.dot_general(
            own_ref[...], weights[0][0], transposed, preferred_element_type=jnp.float32
        )

    low = jnp.dot(
        powers_ref[...].reshape(terms * own_cap, span),
        all_ref[...],
        preferred_element_type=jnp.float32,
    ).astype(jnp.bfloat16)
    value = total[...]
    for term in range(terms):
        value = value + lax.dot_general(
            low[term * own_cap : (term + 1) * own_cap],
            weights[1 + term][0],
            transposed,
            preferred_element_type=jnp.float32,
        )
    total[...] = value


def back_two_kernel(
    place_ref,
    powers_ref,
    all_ref,
    own_ref,
    weight_0,
    weight_a,
    weight_b,
    weight_c,
    turned_ref,
    mixed_ref,
    gain_ref,
    valid_ref,
    rest_ref,
    low_ref,
    mine_ref,
    other_ref,
    total,
):
    step = pl.program_id(0)
    weights = (weight_0, weight_a, weight_b, weight_c)
    backward_step(step, powers_ref, all_ref, own_ref, weights, total)

    @pl.when(step == pl.num_programs(0) - 1)
    def finish_layer():
        low, rest = norm_backward(mixed_ref[...], total[...], gain_ref[...], valid_ref[...])
        low_ref[...] = low
        weight_gradient(turned_ref, low, place_ref[1], mine_ref, other_ref)
        part = turned_ref.shape[0] // 4
        extra = jnp.zeros((2, mine_ref.shape[1] - part, mine_ref.shape[2]), jnp.bfloat16)
        rows = rest + [rest_ref[place : place + 1, :] for place in range(3)]
        rows = jnp.concatenate(rows + [jnp.zeros((10, rows[0].shape[1]), jnp.float32)], axis=0)

        def below(first_ref, second_ref):
            first_ref[:, part:, :] = extra
            second_ref[:, part:, :] = extra
            first_ref[0, part : part + 16, :] = rows.astype(jnp.bfloat16)

        @pl.when(place_ref[1] == 0)
        def low_half_here():
            below(mine_ref, other_ref)

        @pl.when(place_ref[1] == 1)
        def low_half_there():
            below(other_ref, mine_ref)


def back_one_kernel(
    powers_ref, all_ref, own_ref, weight_0, weight_a, weight_b, weight_c, out_ref, total
):
    step = pl.program_id(0)
    weights = (weight_0, weight_a, weight_b, weight_c)
    backward_step(step, powers_ref, all_ref, own_ref, weights, total)

    @pl.when(step == pl.num_programs(0) - 1)
    def finish_layer():
        out_ref[...] = total[...].astype(jnp.bfloat16)


def layer_pass(kernel, name, place, powers, everyone, own, weight, others, outs, scratch):
    ignored, own_cap, span = powers.shape
    fan_in, width = weight.shape[1:]

    def whole(value):
        return pl.BlockSpec(value.shape, lambda step: (0,) * len(value.shape))

    def term_weight(term):
        return pl.BlockSpec((1, fan_in, width), lambda step: (1 + step * TERMS + term, 0, 0))

    in_specs = [
        pl.BlockSpec((TERMS, own_cap, span), lambda step: (step, 0, 0)),
        whole(everyone),
        whole(own),
        pl.BlockSpec((1, fan_in, width), lambda step: (0, 0, 0)),
    ]
    in_specs += [term_weight(term) for term in range(TERMS)] + [whole(value) for value in others]
    operands = [powers, everyone, own] + [weight] * (1 + TERMS) + list(others)
    if place is not None:
        in_specs = [pl.BlockSpec(memory_space=pltpu.SMEM)] + in_specs
        operands = [place] + operands
    return pl.pallas_call(
        kernel,
        grid=((ORDER - 1) // TERMS,),
        out_shape=outs,
        in_specs=in_specs,
        out_specs=[whole(value) for value in outs],
        scratch_shapes=[pltpu.VMEM(shape, dtype) for shape, dtype in scratch],
        compiler_params=pltpu.CompilerParams(vmem_limit_bytes=VMEM_BYTES),
        cost_estimate=NO_COST,
        name=name,
    )(*operands)


def finish_kernel(scalars_ref, pair_ref, siblings_ref, other_ref, out_ref, *small_refs):
    step = pl.program_id(0)
    part = out_ref.shape[1]
    for here, values_ref in ((step < 2, pair_ref), (step >= 2, siblings_ref)):
        @pl.when(here & (scalars_ref[0] == 1))
        def fast_form():
            out_ref[0] = values_ref[0, :part, :].astype(jnp.float32)

        for small_ref in small_refs:
            @pl.when(here & (scalars_ref[1 + step] == 0))
            def small_sums():
                small_ref[...] = values_ref[0, part : part + 16, :].astype(jnp.float32)

    @pl.when(scalars_ref[0] == 0)
    def general_form():
        out_ref[0] = other_ref[0].astype(jnp.float32)


def finished(scalars, pair, siblings, other, with_small=False):
    count, part, width = other.shape
    out, held = (1, part, width), (1,) + pair.shape[1:]
    out_specs = [pl.BlockSpec(out, lambda step, ref: (ref[1 + step], 0, 0))]
    out_shape = [jax.ShapeDtypeStruct(other.shape, jnp.float32)]
    if with_small:
        out_specs.append(pl.BlockSpec((16, width), lambda step, ref: (0, 0)))
        out_shape.append(jax.ShapeDtypeStruct((16, width), jnp.float32))
    return pl.pallas_call(
        finish_kernel,
        grid_spec=pltpu.PrefetchScalarGridSpec(
            num_scalar_prefetch=1,
            grid=(count,),
            in_specs=[
                pl.BlockSpec(held, lambda step, ref: (jnp.minimum(step, 1), 0, 0)),
                pl.BlockSpec(held, lambda step, ref: (jnp.maximum(step - 2, 0), 0, 0)),
                pl.BlockSpec(out, lambda step, ref: ((1 - ref[0]) * ref[1 + step], 0, 0)),
            ],
            out_specs=out_specs,
        ),
        out_shape=out_shape,
        compiler_params=pltpu.CompilerParams(vmem_limit_bytes=VMEM_BYTES),
        cost_estimate=NO_COST,
        name="finished",
    )(scalars, pair, siblings, other)


def unpack_kernel(place_ref, pieces_ref, keys_ref, own_ref, quadrant_ref, columns, hot):
    groups, high, lanes = pieces_ref.shape
    own_cap, span = own_ref.shape
    whole = own_cap // lanes
    send_cap = keys_ref.shape[1] // groups
    half, rest = send_cap // 2, own_cap - whole * lanes
    for group in range(groups):
        start = group * send_cap
        for tile in range(whole):
            columns[start : start + send_cap, tile * lanes : (tile + 1) * lanes] = pieces_ref[
                group, tile * send_cap : (tile + 1) * send_cap, :
            ]
        ends = pieces_ref[group, whole * send_cap :, :]
        columns[start : start + half, whole * lanes :] = ends[:, :rest]
        columns[start + half : start + send_cap, whole * lanes :] = ends[:, rest:]
    standing = lax.broadcasted_iota(jnp.int32, hot.shape, 0)
    hot[...] = jnp.where(standing == keys_ref[...], 1.0, 0.0).astype(jnp.bfloat16)
    block = jnp.dot(hot[...], columns[...], preferred_element_type=jnp.float32)
    own_ref[...] = block.T.astype(jnp.bfloat16)
    middle = span // 2

    @pl.when(place_ref[0] == 0)
    def first():
        quadrant_ref[...] = own_ref[:, :middle]

    @pl.when(place_ref[0] == 1)
    def second():
        quadrant_ref[...] = own_ref[:, middle:]


def unpacked_block(pieces, keys, place, own_cap, span):
    vector = pl.BlockSpec(memory_space=pltpu.VMEM)
    return pl.pallas_call(
        unpack_kernel,
        out_shape=[
            jax.ShapeDtypeStruct((own_cap, span), jnp.bfloat16),
            jax.ShapeDtypeStruct((own_cap, span // 2), jnp.bfloat16),
        ],
        in_specs=[pl.BlockSpec(memory_space=pltpu.SMEM), vector, vector],
        out_specs=[vector, vector],
        scratch_shapes=[
            pltpu.VMEM((keys.shape[1], own_cap), jnp.bfloat16),
            pltpu.VMEM((span, keys.shape[1]), jnp.bfloat16),
        ],
        compiler_params=pltpu.CompilerParams(vmem_limit_bytes=VMEM_BYTES),
        cost_estimate=NO_COST,
        name="unpacked_block",
    )(place, pieces, keys)


def fit_kernel(codes_ref, out_ref, *, n_row, caps):
    own_cap, send_cap, seat_cap = caps
    codes = codes_ref[...]
    devices = codes.shape[0]
    n_col = devices // n_row
    label = lax.broadcasted_iota(jnp.int32, (devices, 128), 1)
    counts = jnp.zeros((devices, 128), jnp.float32)
    for cluster in range(CLUSTERS):
        here = jnp.where(codes == 2 * cluster + 1, 1.0, 0.0)
        counts = counts + jnp.where(
            label == cluster, jnp.sum(here, axis=1, keepdims=True), 0.0
        )
    sizes = jnp.sum(counts, axis=0, keepdims=True)
    across = jnp.broadcast_to(sizes, (128, 128))
    down = across.T
    first = lax.broadcasted_iota(jnp.int32, (128, 128), 0)
    second = lax.broadcasted_iota(jnp.int32, (128, 128), 1)
    ahead = (across > down) | ((across == down) & (second < first))
    ahead = ahead & (second < CLUSTERS)
    rank = jnp.sum(jnp.where(ahead, 1.0, 0.0), axis=1, keepdims=True).astype(jnp.int32)
    others = n_row - 1
    later = rank > others
    turn = jnp.zeros_like(rank)
    for count in range(1, CLUSTERS // others + 1):
        turn = turn + jnp.where(rank - 1 >= count * others, 1, 0)
    place = rank - 1 - turn * others
    group = jnp.where(rank == 0, 0, 1 + jnp.where(later, others - 1 - place, place))
    member = (group == second) & (first < CLUSTERS)
    held = jnp.dot(
        counts.astype(jnp.bfloat16),
        jnp.where(member, 1.0, 0.0).astype(jnp.bfloat16),
        preferred_element_type=jnp.float32,
    )
    by_row = jnp.zeros((1, 128), jnp.float32)
    for row in range(n_row):
        rows = jnp.sum(held[row * n_col : (row + 1) * n_col], axis=0, keepdims=True)
        by_row = jnp.maximum(by_row, rows)
    device = lax.broadcasted_iota(jnp.int32, (devices, 128), 0)
    by_col = jnp.zeros((1, 128), jnp.float32)
    for col in range(n_col):
        cols = jnp.where(device % n_col == col, held, 0.0)
        by_col = jnp.maximum(by_col, jnp.sum(cols, axis=0, keepdims=True))
    fits = (
        (jnp.max(by_col) <= own_cap) & (jnp.max(by_row) <= send_cap) & (jnp.max(held) <= seat_cap)
    )
    out_ref[0] = jnp.where(fits, 1, 0)


def fits_in(codes, n_row, caps):
    fits = pl.pallas_call(
        functools.partial(fit_kernel, n_row=n_row, caps=caps),
        out_shape=jax.ShapeDtypeStruct((1,), jnp.int32),
        in_specs=[pl.BlockSpec(memory_space=pltpu.VMEM)],
        out_specs=pl.BlockSpec(memory_space=pltpu.SMEM),
        cost_estimate=NO_COST,
        name="fits",
    )(codes.reshape(-1, codes.shape[-1]))
    return fits


def exclusive_counts(member):
    count = member.shape[-1]
    before = jnp.arange(count)[:, None] < jnp.arange(count)[None, :]
    return jnp.dot(
        member.astype(jnp.bfloat16),
        before.astype(jnp.bfloat16),
        preferred_element_type=jnp.float32,
    ).astype(jnp.int32)


def assign(codes, n_row):
    cluster, valid = codes >> 1, codes & 1
    labels = jnp.arange(CLUSTERS)
    sizes = jnp.sum(
        (cluster.reshape(1, -1) == labels[:, None]) & (valid.reshape(1, -1) == 1), axis=1
    )
    ahead = (sizes[None, :] > sizes[:, None]) | (
        (sizes[None, :] == sizes[:, None]) & (labels[None, :] < labels[:, None])
    )
    rank = jnp.sum(ahead, axis=1)
    others = n_row - 1
    turn, place = (rank - 1) // others, (rank - 1) % others
    group = jnp.where(rank == 0, 0, 1 + jnp.where(turn == 0, place, others - 1 - place))
    of_node = jnp.sum(
        jnp.where(cluster[None] == labels[:, None, None, None], group[:, None, None, None], 0),
        axis=0,
    )
    return jnp.where(valid == 1, of_node, n_row)


def compact(
    codes,
    group,
    features,
    block_keep,
    edge_weight,
    weight_one,
    bias_one,
    gain_one,
    shift_one,
    weight_two,
    bias_two,
    gain_two,
    shift_two,
    cotangent,
    places_of,
    slots_of,
    seats_of,
    decide,
    sizes,
    caps,
):
    row, col = lax.axis_index("row"), lax.axis_index(COL)
    chip, core = lax.axis_index("chip"), lax.axis_index("core")
    n_row, n_col = sizes
    own_cap, send_cap, seat_cap = caps
    own_nodes, in_width = features.shape
    width = weight_two.shape[2]
    span = n_col * own_cap
    targets = jnp.arange(n_row)

    def in_col(value):
        return lax.dynamic_index_in_dim(value, col, 1, False).reshape(-1)

    def in_row(value):
        return lax.dynamic_index_in_dim(value, row, 0, False).reshape(-1)

    row_group, col_group = in_row(group), in_col(group)
    row_slots, col_places = in_row(slots_of(group)), in_col(places_of(group))
    row_keys = jnp.where(row_slots < send_cap, row_group * send_cap + row_slots, -1)
    col_keys = jnp.where(col_places < own_cap, col_group * own_cap + col_places, -1)
    pieces = packed_pieces(
        block_keep,
        in_row(codes),
        in_col(codes),
        row_keys,
        col_keys,
        edge_weight,
        (own_cap, send_cap),
        n_row,
    )
    pieces, codes = lax.optimization_barrier((pieces, codes))
    group = assign(codes, n_row)
    pieces = trade(pieces, "row")
    places, slots, seats = places_of(group), slots_of(group), seats_of(group)

    standing = jnp.arange(n_col)[None, :, None] * own_cap + places
    fits_here = jnp.where(group == row, standing, -1).reshape(n_row, -1)
    slot_of = slots.reshape(n_row, -1)
    target = jnp.max(
        jnp.where(
            slot_of[:, None, :] == jnp.arange(send_cap)[None, :, None], fits_here[:, None, :], -1
        ),
        axis=2,
    )
    keys = target.reshape(1, -1)

    def to_partner(value, step):
        return lax.ppermute(value, "row", [(place, place ^ step) for place in range(n_row)])

    partners = row ^ targets
    group_here = lax.dynamic_index_in_dim(in_row(group).reshape(n_col, -1), col, 0, False)
    seat_here = lax.dynamic_index_in_dim(in_row(seats).reshape(n_col, -1), col, 0, False)

    def seat_of_node(groups):
        hot = (group_here[None, None, :] == groups[:, None, None]) & (
            seat_here[None, None, :] == jnp.arange(seat_cap)[None, :, None]
        )
        return hot.astype(jnp.bfloat16).reshape(n_row * seat_cap, own_nodes)

    enter_partner = seat_of_node(partners)
    both = jnp.dot(enter_partner, jnp.concatenate([features, cotangent], axis=1))
    both = both.reshape(n_row, seat_cap, -1)
    enter_partner = enter_partner.T
    both, codes = lax.optimization_barrier((both, codes))
    fits, others = decide(codes)
    group_col = lax.dynamic_index_in_dim(group, col, 1, False)
    seats_col = lax.dynamic_index_in_dim(seats, col, 1, False)
    places_col = lax.dynamic_index_in_dim(places, col, 1, False)
    seated = (group_col == row)[:, None, :] & (
        seats_col[:, None, :] == jnp.arange(seat_cap)[None, :, None]
    )
    place_of_seat = jnp.max(jnp.where(seated, places_col[:, None, :], -1), axis=2)
    from_partner = jnp.max(
        jnp.where((partners[:, None] == targets)[:, :, None], place_of_seat[None], -1), axis=1
    )
    arrive = from_partner.reshape(1, -1) == jnp.arange(own_cap)[:, None]
    arrive = arrive.astype(jnp.bfloat16)
    leave_partner = jnp.concatenate([from_partner[::2], from_partner[1::2]])
    leave_partner = leave_partner.reshape(-1, 1) == jnp.arange(own_cap)
    leave_partner = leave_partner.astype(jnp.bfloat16)
    held_count = jnp.sum(group_col == row)
    valid_rows = (jnp.arange(own_cap) < held_count).astype(jnp.float32)[:, None]
    place = jnp.stack([chip, core]).astype(jnp.int32)
    quarters = jnp.stack([col, (1 - chip) * 2 + core, chip * 2 + 1 - core, 3 - col])
    quarters = jnp.concatenate([fits, quarters.astype(jnp.int32)])
    scalars = (chip, 1 - chip, col * own_cap)
    scalars = tuple(value.astype(jnp.uint32) for value in scalars) + (chip == 0, core == 0, place, quarters)
    homes = enter_partner, leave_partner
    pieces, both, keys, arrive, homes, valid_rows, others, scalars = lax.optimization_barrier(
        (pieces, both, keys, arrive, homes, valid_rows, others, scalars)
    )
    enter_partner, leave_partner = homes
    this_chip, other_chip, own_start, first_chip, first_core, place, quarters = scalars

    own_block, quadrant = unpacked_block(pieces, keys, place, own_cap, span)
    quadrant = swap(quadrant, "chip")
    both = [both[0]] + [to_partner(both[step], step) for step in range(1, n_row)]
    sibling = swap(own_block, "core")
    quadrant, *early = lax.optimization_barrier((quadrant, *both[:-2]))
    adjacency = normalized_block(own_block, sibling, quadrant, swap(quadrant, "core"), place)
    adjacency, *late = lax.optimization_barrier((adjacency, *both[-2:]))
    both = early + late
    mine = jnp.dot(arrive, jnp.concatenate(both))
    features_own, cotangent_own = mine[:, :in_width], mine[:, in_width:]
    sibling = swap(features_own, "core")

    first = (own_start + jnp.arange(own_cap, dtype=jnp.uint32))[:, None]
    first = first == jnp.arange(span, dtype=jnp.uint32)[None, :]
    previous = first.astype(jnp.float32)
    current = -lax.dynamic_slice_in_dim(adjacency, own_start, own_cap, 0).astype(jnp.float32)
    lowered = [current.astype(jnp.bfloat16)]
    for position in range(2, ORDER):
        upcoming = (
            -2.0 * jnp.dot(lowered[-1], adjacency, preferred_element_type=jnp.float32) - previous
        )
        low = upcoming.astype(jnp.bfloat16)
        if position == 4:
            low, sibling = lax.optimization_barrier((low, sibling))
            features_chip = joined(features_own, sibling, first_core)
            partner = swap(features_chip, "chip")
        if position == 8:
            low, partner = lax.optimization_barrier((low, partner))
            features_all = joined(features_chip, partner, first_chip)
        previous, current = current, upcoming
        lowered.append(low)
    powers = jnp.concatenate(lowered, axis=0).reshape(ORDER - 1, own_cap, span)

    def everywhere(value_low):
        return lax.all_gather(value_low, COL, axis=0, tiled=True)

    def chosen(value, other):
        return jnp.where(quarters[0] == 1, value.astype(jnp.float32), other.astype(jnp.float32))

    def shaped(*shape, dtype=jnp.bfloat16):
        return jax.ShapeDtypeStruct(shape, dtype)

    part_one, part_two = ORDER * in_width // n_col, ORDER * width // n_col
    padded = -(-(part_one + 16) // (8 * n_row)) * (8 * n_row)
    hidden, turned_one, mixed_one = layer_pass(
        layer_one_kernel,
        "layer_one",
        None,
        powers,
        features_all,
        features_own,
        weight_one,
        [bias_one[None], gain_one[None], shift_one[None], valid_rows],
        [
            shaped(own_cap, width),
            shaped(n_col * part_one, own_cap),
            shaped(own_cap, width, dtype=jnp.float32),
        ],
        [],
    )
    activations, low_two, rest_two, mine, other = layer_pass(
        layer_two_kernel,
        "layer_two",
        place,
        powers,
        everywhere(hidden),
        hidden,
        weight_two,
        [bias_two[None], gain_two[None], shift_two[None], valid_rows, cotangent_own],
        [
            shaped(own_cap, width),
            shaped(own_cap, width),
            shaped(3, width, dtype=jnp.float32),
            shaped(2, part_two, width),
            shaped(2, part_two, width),
        ],
        [((n_col * part_two, own_cap), jnp.bfloat16), ((own_cap, width), jnp.float32)],
    )

    def add_cores(mine, other):
        got = swap(other, "core")
        return tuple(
            added(
                lax.dynamic_index_in_dim(mine, index, 0, False),
                lax.dynamic_index_in_dim(got, index, 0, False),
            )
            for index in (this_chip, other_chip)
        )

    leaving = jnp.dot(leave_partner, activations).reshape(n_row, seat_cap, width)
    near, far = leaving[: n_row // 2], leaving[n_row // 2 :]
    far = to_partner(far, 1)
    here, there = add_cores(mine, other)
    everyone_two, there, far = lax.optimization_barrier((everywhere(low_two), there, far))
    there = swap(there, "chip")
    arrived = [jnp.stack([near[0], far[0]])] + [
        to_partner(jnp.stack([near[half], far[half]]), 2 * half) for half in range(1, n_row // 2)
    ]
    low_one, mine, other = layer_pass(
        back_two_kernel,
        "back_two",
        place,
        powers,
        everyone_two,
        low_two,
        weight_two,
        [turned_one, mixed_one, gain_one[None], valid_rows, rest_two],
        [shaped(own_cap, width), shaped(2, padded, width), shaped(2, padded, width)],
        [((own_cap, width), jnp.float32)],
    )
    low_one, there, arrived = lax.optimization_barrier((low_one, there, arrived))
    second = added(here, there).reshape(n_row, -1, width)
    many = second.shape[1]
    low_one, second = lax.optimization_barrier((low_one, second))
    second = trade(second, "row")
    here, there = add_cores(mine, other)
    there = swap(there, "chip")
    first = added(here, there).reshape(n_row, -1, width)
    share = first.shape[1]
    second = jnp.sum(second.astype(jnp.float32), axis=0).astype(jnp.bfloat16)
    second = jnp.broadcast_to(second[None], (n_row,) + second.shape)
    mixed = jnp.concatenate([second, first], axis=1)
    low_one, mixed = lax.optimization_barrier((low_one, mixed))
    everyone_one = everywhere(low_one)
    mixed = trade(mixed, "row")
    (input_grad,) = layer_pass(
        back_one_kernel,
        "back_one",
        None,
        powers,
        everyone_one,
        low_one,
        weight_one,
        [],
        [shaped(own_cap, in_width)],
        [((own_cap, in_width), jnp.float32)],
    )
    leaving = jnp.dot(leave_partner, input_grad).reshape(n_row, seat_cap, in_width)
    arrived = jnp.concatenate(arrived).reshape(-1, width)
    home = jnp.dot(enter_partner, arrived, preferred_element_type=jnp.float32)
    home = chosen(home, others[0])
    mixed, leaving, home = lax.optimization_barrier((mixed, leaving, home))
    first = jnp.sum(mixed[:, many:].astype(jnp.float32), axis=0).astype(jnp.bfloat16)
    first = jnp.broadcast_to(first[None], (n_row,) + first.shape)
    first, mixed, leaving = lax.optimization_barrier((first, mixed, leaving))
    first = trade(first, "row")
    second = mixed[:, :many].reshape(1, -1, width)
    partner_two = swap(second, "chip")
    near, far = leaving[: n_row // 2], leaving[n_row // 2 :]
    far = to_partner(far, 1)
    first, far, partner_two = lax.optimization_barrier((first, far, partner_two))
    mine = first.reshape(1, -1, width)
    partner = swap(mine, "chip")
    arrived = [jnp.stack([near[0], far[0]])] + [
        to_partner(jnp.stack([near[half], far[half]]), 2 * half) for half in range(1, n_row // 2)
    ]
    second = jnp.concatenate([second, partner_two])
    (second,) = finished(quarters, second, swap(second, "core"), others[3])
    partner, second, arrived = lax.optimization_barrier((partner, second, arrived))
    pair = jnp.concatenate([mine, partner])
    siblings = swap(pair, "core")
    arrived = jnp.concatenate(arrived).reshape(-1, in_width)
    home_grad = jnp.dot(enter_partner, arrived, preferred_element_type=jnp.float32)
    home_grad = chosen(home_grad, others[1])
    first, small = finished(quarters, pair, siblings, others[2], True)
    return home, home_grad, first, second, chosen(small[:6], others[4])


def general(
    codes,
    features,
    block_keep,
    edge_weight,
    weight_one,
    bias_one,
    gain_one,
    shift_one,
    weight_two,
    bias_two,
    gain_two,
    shift_two,
    cotangent,
    node_valid,
):
    row, col = lax.axis_index("row"), lax.axis_index(COL)
    row_codes = lax.dynamic_index_in_dim(codes, row, 0, False).reshape(-1)
    col_codes = lax.dynamic_index_in_dim(codes, col, 1, False).reshape(-1)
    tile_rows, tile_cols = edge_weight.shape
    blocks_down, blocks_across = block_keep.shape
    block_side = tile_rows // blocks_down
    linked = (row_codes[:, None] == col_codes[None, :]) & (row_codes[:, None] & 1 == 1)
    linked = linked.reshape(blocks_down, block_side, blocks_across, block_side) & (
        block_keep[:, None, :, None] == 1
    )
    masked = edge_weight * linked.reshape(tile_rows, tile_cols).astype(jnp.bfloat16)
    degree_rows = 1.0 + lax.psum(jnp.sum(masked, axis=1, dtype=jnp.float32), COL)
    own_nodes = features.shape[0]
    own_degree = lax.dynamic_slice_in_dim(
        degree_rows, lax.axis_index(COL) * own_nodes, own_nodes, 0
    )
    degree_cols = lax.all_gather(own_degree, "row", axis=0, tiled=True)
    adjacency = (
        masked.astype(jnp.float32)
        * lax.rsqrt(degree_rows)[:, None]
        * lax.rsqrt(degree_cols)[None, :]
    ).astype(jnp.bfloat16)
    valid_rows = node_valid.astype(jnp.float32)
    stacked_one, mixed_one, hidden = layer_forward(
        adjacency,
        features.astype(jnp.float32),
        weight_one,
        bias_one,
        gain_one,
        shift_one,
        valid_rows,
    )
    stacked_two, mixed_two, activations = layer_forward(
        adjacency, hidden, weight_two, bias_two, gain_two, shift_two, valid_rows
    )
    hidden_grad, weight_two_grad, bias_two_grad, gain_two_grad, shift_two_grad = layer_backward(
        adjacency,
        stacked_two,
        mixed_two,
        cotangent.astype(jnp.float32),
        weight_two,
        gain_two,
        shift_two,
        valid_rows,
    )
    input_grad, weight_one_grad, bias_one_grad, gain_one_grad, shift_one_grad = layer_backward(
        adjacency, stacked_one, mixed_one, hidden_grad, weight_one, gain_one, shift_one, valid_rows
    )
    summed = lax.psum(
        (
            weight_one_grad,
            bias_one_grad,
            gain_one_grad,
            shift_one_grad,
            weight_two_grad,
            bias_two_grad,
            gain_two_grad,
            shift_two_grad,
        ),
        ("row",) + COL,
    )
    weight_one_grad, bias_one_grad, gain_one_grad, shift_one_grad = (
        summed[0],
        summed[1],
        summed[2],
        summed[3],
    )
    weight_two_grad, bias_two_grad, gain_two_grad, shift_two_grad = (
        summed[4],
        summed[5],
        summed[6],
        summed[7],
    )
    return (
        activations,
        input_grad,
        weight_one_grad,
        bias_one_grad,
        gain_one_grad,
        shift_one_grad,
        weight_two_grad,
        bias_two_grad,
        gain_two_grad,
        shift_two_grad,
    )


def local(n_row, n_col, *args):
    (
        features,
        node_valid,
        cluster,
        block_keep,
        edge_weight,
        weight_one,
        bias_one,
        gain_one,
        shift_one,
        weight_two,
        bias_two,
        gain_two,
        shift_two,
        cotangent,
    ) = args
    own_nodes, in_width = features.shape
    own_cap = own_nodes * n_row * 5 // 16
    send_cap = own_nodes * n_col * 11 // 32
    seat_cap = own_nodes * 7 // 16
    codes = (cluster * 2 + node_valid)[None]
    codes = joined(codes, swap(codes, "core"), lax.axis_index("core") == 0)
    codes = broadcast_along(codes, ("row", "chip"), n_row * n_col // 2)
    codes = codes.reshape(n_row, n_col, own_nodes)
    shared = (
        block_keep,
        edge_weight,
        weight_one,
        bias_one,
        gain_one,
        shift_one,
        weight_two,
        bias_two,
        gain_two,
        shift_two,
        cotangent,
    )

    def slow():
        return general(codes, features, *shared, node_valid)

    held = (ORDER - 1) * own_cap * own_cap * n_col * 2
    if held > HELD_BYTES or n_col != 4 or n_row < 2 or n_row & (n_row - 1):
        return slow()
    group = assign(codes, n_row)

    def member_of(group):
        return group[None] == jnp.arange(n_row)[:, None, None, None]

    def places_of(group):
        member = member_of(group).transpose(0, 2, 1, 3).reshape(n_row, n_col, -1)
        places = jnp.sum(jnp.where(member, exclusive_counts(member), 0), axis=0)
        return places.reshape(n_col, n_row, own_nodes).transpose(1, 0, 2)

    def slots_of(group):
        member = member_of(group).reshape(n_row, n_row, -1)
        slots = jnp.sum(jnp.where(member, exclusive_counts(member), 0), axis=0)
        return slots.reshape(n_row, n_col, own_nodes)

    def seats_of(group):
        member = member_of(group)
        return jnp.sum(jnp.where(member, exclusive_counts(member), 0), axis=0)

    width = weight_two.shape[2]

    def instead(state):
        made = slow()
        small = jnp.stack([made[place] for place in (3, 4, 5, 7, 8, 9)])
        return (jnp.ones_like(state[0]),) + tuple(
            value.astype(jnp.bfloat16).reshape(like.shape)
            for value, like in zip((made[0], made[1], made[2], made[6], small), state[1:])
        )

    shapes = (
        (own_nodes, width),
        (own_nodes, in_width),
        (n_col, ORDER * in_width // n_col, width),
        (n_col, ORDER * width // n_col, width),
        (6, width),
    )

    def decide(codes):
        fits = fits_in(codes, n_row, (own_cap, send_cap, seat_cap))
        others = lax.while_loop(
            lambda state: state[0][0] == 0,
            instead,
            (fits,) + tuple(jnp.zeros(shape, jnp.bfloat16) for shape in shapes),
        )[1:]
        return fits, others

    home, home_grad, first, second, small = compact(
        codes,
        group,
        features,
        *shared,
        places_of,
        slots_of,
        seats_of,
        decide,
        (n_row, n_col),
        (own_cap, send_cap, seat_cap),
    )
    return (
        home,
        home_grad,
        first.reshape(weight_one.shape),
        small[0],
        small[1],
        small[2],
        second.reshape(weight_two.shape),
        small[3],
        small[4],
        small[5],
    )


def solution(mesh):
    n_row, n_col = mesh.shape["row"], mesh.shape["col"]
    by_core = jax.sharding.Mesh(
        mesh.devices.reshape(n_row, n_col // 2, 2), ("row", "chip", "core")
    )
    nodes = ("row", "chip", "core")
    placed = (
        P(nodes, None),
        P(nodes),
        P(nodes),
        P("row", COL),
        P("row", COL),
        P(),
        P(),
        P(),
        P(),
        P(),
        P(),
        P(),
        P(),
        P(nodes, None),
    )
    return jax.shard_map(
        functools.partial(local, n_row, n_col),
        mesh=by_core,
        in_specs=placed,
        out_specs=(P(nodes, None), P(nodes, None), P(), P(), P(), P(), P(), P(), P(), P()),
        check_vma=False,
    )
```

```python
import functools
import math

import jax
import jax.numpy as jnp
from jax import lax
from jax.experimental import pallas as pl
from jax.experimental.pallas import tpu as pltpu
from jax.sharding import PartitionSpec as P

ORDER = 13
CLUSTERS = 16
HELD_BYTES = 1 << 25
VMEM_BYTES = 32 << 20
TERMS = 3
NO_COST = pl.CostEstimate(flops=1, bytes_accessed=1, transcendentals=0)
COL = ("chip", "core")


def finish(mixed, gain, shift, valid_rows):
    active = jax.nn.gelu(mixed, approximate=False)
    centered = active - jnp.mean(active, axis=-1, keepdims=True)
    variance = jnp.mean(centered * centered, axis=-1, keepdims=True)
    return (centered * lax.rsqrt(variance + 1e-05) * gain + shift) * valid_rows[:, None]


def forward_product(adjacency, piece_low):
    partial_value = jnp.dot(
        adjacency,
        lax.all_gather(piece_low, "row", axis=0, tiled=True),
        preferred_element_type=jnp.float32,
    )
    return lax.psum_scatter(partial_value, COL, scatter_dimension=0, tiled=True)


def backward_product(adjacency, piece_low):
    partial_value = lax.dot_general(
        adjacency,
        lax.all_gather(piece_low, COL, axis=0, tiled=True),
        (((0,), (0,)), ((), ())),
        preferred_element_type=jnp.float32,
    )
    return lax.psum_scatter(
        partial_value.astype(jnp.bfloat16), "row", scatter_dimension=0, tiled=True
    ).astype(jnp.float32)


def layer_forward(adjacency, inputs, weight, bias, gain, shift, valid_rows):
    first_low = inputs.astype(jnp.bfloat16)
    second = -forward_product(adjacency, first_low)
    second_low = second.astype(jnp.bfloat16)

    def advance(state_pair, unused):
        previous, current, current_low = state_pair
        upcoming = -2.0 * forward_product(adjacency, current_low) - previous
        upcoming_low = upcoming.astype(jnp.bfloat16)
        return ((current, upcoming, upcoming_low), upcoming_low)

    ignored, others = lax.scan(advance, (inputs, second, second_low), None, length=ORDER - 2)
    stacked = jnp.concatenate([first_low[None], second_low[None], others], axis=0)
    mixed = jnp.einsum("kni,kio->no", stacked, weight, preferred_element_type=jnp.float32) + bias
    return (stacked, mixed, finish(mixed, gain, shift, valid_rows))


def layer_backward(adjacency, stacked, mixed, upstream, weight, gain, shift, valid_rows):

    def local_finish(mixed_in, gain_in, shift_in):
        return finish(mixed_in, gain_in, shift_in, valid_rows)

    ignored, pullback = jax.vjp(local_finish, mixed, gain, shift)
    mixed_grad, gain_grad, shift_grad = pullback(upstream)
    mixed_low = mixed_grad.astype(jnp.bfloat16)
    bias_grad = jnp.sum(mixed_low.astype(jnp.float32), axis=0)
    weight_grad = jnp.einsum("kni,no->kio", stacked, mixed_low, preferred_element_type=jnp.float32)
    direct = jnp.einsum("no,kio->kni", mixed_low, weight, preferred_element_type=jnp.float32)

    def retreat(state_pair, direct_term):
        later_two, later_one = state_pair
        current = (
            direct_term
            - 2.0 * backward_product(adjacency, later_one.astype(jnp.bfloat16))
            - later_two
        )
        return ((later_one, current), None)

    start_pair = (jnp.zeros_like(direct[0]), direct[ORDER - 1])
    (second_grad, first_grad), unused = lax.scan(
        retreat, start_pair, direct[1 : ORDER - 1], reverse=True
    )
    input_grad = (
        direct[0] - backward_product(adjacency, first_grad.astype(jnp.bfloat16)) - second_grad
    )
    return (input_grad, weight_grad, bias_grad, gain_grad, shift_grad)


def swap(value, axis):
    return lax.ppermute(value, axis, [(0, 1), (1, 0)])


def trade(pieces, axis):
    return lax.all_to_all(pieces, axis, 0, 0, tiled=False)


def broadcast_along(value, axis, size):
    return trade(jnp.broadcast_to(value[None], (size,) + value.shape), axis)


def joined(mine, other, mine_first):
    return jnp.where(
        mine_first, jnp.concatenate([mine, other]), jnp.concatenate([other, mine])
    )


def added(mine, received):
    return (mine.astype(jnp.float32) + received.astype(jnp.float32)).astype(jnp.bfloat16)


def assemble(place_ref, own_ref, sibling_ref, near_ref, far_ref, out_ref, done):
    chip, core = place_ref[0], place_ref[1]
    own_cap, span = own_ref.shape
    half = span // 2

    def rows(of_chip, of_core):
        return pl.ds(pl.multiple_of((2 * of_chip + of_core) * own_cap, own_cap), own_cap)

    def fetch(source, of_chip, of_core, columns, place):
        target = out_ref.at[rows(of_chip, of_core), columns]
        return pltpu.make_async_copy(source, target, done.at[place])

    def quadrant_copies(here):
        there = 1 - here
        columns = pl.ds(there * half, half)
        return (
            fetch(near_ref, there, core, columns, 2),
            fetch(far_ref, there, 1 - core, columns, 3),
        )

    everything = pl.ds(0, span)
    top = (
        fetch(own_ref, chip, core, everything, 0),
        fetch(sibling_ref, chip, 1 - core, everything, 1),
    )

    def of_chip(here):
        there = 1 - here
        copies = top + quadrant_copies(here)
        for copy in copies:
            copy.start()
        for copy in copies:
            copy.wait()
        here_rows = pl.ds(here * half, half)
        for tile in range(half // 128):
            columns = pl.ds(there * half + tile * 128, 128)
            strip = out_ref[here_rows, columns]
            turned = jnp.transpose(strip.astype(jnp.float32)).astype(jnp.bfloat16)
            out_ref[columns, here_rows] = turned

    @pl.when(chip == 0)
    def first():
        of_chip(0)

    @pl.when(chip == 1)
    def second():
        of_chip(1)

    across = jnp.ones((1, span), jnp.float32)
    for tile in range(span // 128):
        across = across + jnp.sum(
            out_ref[pl.ds(tile * 128, 128), :].astype(jnp.float32), axis=0, keepdims=True
        )
    across = lax.rsqrt(across)
    for tile in range(span // 128):
        strip = out_ref[pl.ds(tile * 128, 128), :].astype(jnp.float32)
        down = lax.rsqrt(1.0 + jnp.sum(strip, axis=1, keepdims=True))
        out_ref[pl.ds(tile * 128, 128), :] = (strip * down * across).astype(jnp.bfloat16)


def normalized_block(own, sibling, near, far, place):
    span = own.shape[1]
    return pl.pallas_call(
        assemble,
        out_shape=jax.ShapeDtypeStruct((span, span), jnp.bfloat16),
        in_specs=[pl.BlockSpec(memory_space=pltpu.SMEM)]
        + [pl.BlockSpec(memory_space=pltpu.HBM)] * 4,
        out_specs=pl.BlockSpec(memory_space=pltpu.VMEM),
        scratch_shapes=[pltpu.SemaphoreType.DMA((4,))],
        compiler_params=pltpu.CompilerParams(vmem_limit_bytes=VMEM_BYTES),
        cost_estimate=NO_COST,
        name="normalized_block",
    )(place, own, sibling, near, far)


def pack_kernel(
    keep_ref, row_codes_ref, col_codes_ref, row_keys_ref, col_keys_ref, weight_ref, out_ref,
    masked, picked, rows_hot, cols_hot
):
    tile_rows, tile_cols = weight_ref.shape
    blocks_down, blocks_across = keep_ref.shape
    groups, ignored, lanes = out_ref.shape
    send_cap, own_cap = rows_hot.shape[0] // groups, cols_hot.shape[0] // groups
    high, wide = tile_rows // blocks_down, tile_cols // blocks_across
    for down in range(blocks_down):
        for across in range(blocks_across):
            rows, columns = pl.ds(down * high, high), pl.ds(across * wide, wide)
            own, other = row_codes_ref[rows, :], col_codes_ref[:, columns]
            linked = (own == other) & (own % 2 == 1) & (keep_ref[down, across] == 1)
            weight = weight_ref[rows, columns].astype(jnp.float32)
            masked[rows, columns] = jnp.where(linked, weight, 0.0).astype(jnp.bfloat16)

    def one_hot(keys, start, count):
        standing = lax.broadcasted_iota(jnp.int32, (count, keys.shape[1]), 0) + start
        return jnp.where(standing == keys, 1.0, 0.0).astype(jnp.bfloat16)

    for group in range(groups):
        rows_hot[pl.ds(group * send_cap, send_cap), :] = one_hot(
            row_keys_ref[...], group * send_cap, send_cap
        )
        cols_hot[pl.ds(group * own_cap, own_cap), :] = one_hot(
            col_keys_ref[...], group * own_cap, own_cap
        )
    for tile in range(tile_cols // 256):
        columns = pl.ds(tile * 256, 256)
        picked[:, columns] = jnp.dot(
            rows_hot[...], masked[:, columns], preferred_element_type=jnp.float32
        ).astype(jnp.bfloat16)
    whole, half = own_cap // lanes, send_cap // 2
    for group in range(groups):
        packed = lax.dot_general(
            cols_hot[pl.ds(group * own_cap, own_cap), :],
            picked[pl.ds(group * send_cap, send_cap), :],
            (((1,), (1,)), ((), ())),
            preferred_element_type=jnp.float32,
        ).T
        for tile in range(whole):
            out_ref[group, pl.ds(tile * send_cap, send_cap), :] = packed[
                :, tile * lanes : (tile + 1) * lanes
            ].astype(jnp.bfloat16)
        ends = jnp.concatenate(
            [packed[:half, whole * lanes :], packed[half:, whole * lanes :]], axis=1
        )
        out_ref[group, pl.ds(whole * send_cap, half), :] = ends.astype(jnp.bfloat16)


def packed_pieces(block_keep, row_codes, col_codes, row_keys, col_keys, edge_weight, caps, groups):
    own_cap, send_cap = caps
    tile_rows, tile_cols = edge_weight.shape
    high = own_cap // 128 * send_cap + send_cap // 2
    vector = pl.BlockSpec(memory_space=pltpu.VMEM)
    return pl.pallas_call(
        pack_kernel,
        out_shape=jax.ShapeDtypeStruct((groups, high, 128), jnp.bfloat16),
        in_specs=[pl.BlockSpec(memory_space=pltpu.SMEM)] + [vector] * 5,
        out_specs=vector,
        scratch_shapes=[
            pltpu.VMEM((tile_rows, tile_cols), jnp.bfloat16),
            pltpu.VMEM((groups * send_cap, tile_cols), jnp.bfloat16),
            pltpu.VMEM((groups * send_cap, tile_rows), jnp.bfloat16),
            pltpu.VMEM((groups * own_cap, tile_cols), jnp.bfloat16),
        ],
        compiler_params=pltpu.CompilerParams(vmem_limit_bytes=VMEM_BYTES),
        cost_estimate=NO_COST,
        name="packed_pieces",
    )(block_keep, row_codes[:, None], col_codes[None], row_keys[None], col_keys[None], edge_weight)


def normal_share(mixed):
    return 0.5 * (1.0 + lax.erf(mixed * 0.5**0.5))


def norm_forward(mixed):
    active = mixed * normal_share(mixed)
    centered = active - jnp.mean(active, axis=-1, keepdims=True)
    scale = lax.rsqrt(jnp.mean(centered * centered, axis=-1, keepdims=True) + 1e-05)
    return centered * scale, scale


def norm_backward(mixed, upstream, gain, valid):
    normed, scale = norm_forward(mixed)
    upstream = upstream * valid
    inner = upstream * gain
    inner = inner - jnp.mean(inner, axis=-1, keepdims=True) - normed * jnp.mean(
        inner * normed, axis=-1, keepdims=True
    )
    density = jnp.exp(-0.5 * mixed * mixed) * (1.0 / (2.0 * math.pi) ** 0.5)
    low = (inner * scale * (normal_share(mixed) + mixed * density)).astype(jnp.bfloat16)
    rest = [low.astype(jnp.float32), upstream * normed, upstream]
    return low, [jnp.sum(value, axis=0, keepdims=True) for value in rest]


def weight_gradient(turned_ref, low, core, mine_ref, other_ref):
    part = turned_ref.shape[0] // 4

    def halves(first_ref, second_ref):
        for place in range(4):
            out_ref = second_ref if place % 2 else first_ref
            out_ref[place // 2, :part, :] = jnp.dot(
                turned_ref[place * part : (place + 1) * part, :],
                low,
                preferred_element_type=jnp.float32,
            ).astype(jnp.bfloat16)

    @pl.when(core == 0)
    def low_half_first():
        halves(mine_ref, other_ref)

    @pl.when(core == 1)
    def high_half_first():
        halves(other_ref, mine_ref)


def forward_step(step, powers_ref, all_ref, own_ref, weights, bias_ref, turned, mixed):
    terms, own_cap, span = powers_ref.shape
    fan_in = own_ref.shape[1]

    @pl.when(step == 0)
    def first():
        turned[:fan_in, :] = own_ref[...].T
        mixed[...] = bias_ref[...] + jnp.dot(
            own_ref[...], weights[0][0], preferred_element_type=jnp.float32
        )

    low = jnp.dot(
        powers_ref[...].reshape(terms * own_cap, span),
        all_ref[...],
        preferred_element_type=jnp.float32,
    ).astype(jnp.bfloat16)
    total = mixed[...]
    for term in range(terms):
        part = low[term * own_cap : (term + 1) * own_cap]
        start = pl.multiple_of((1 + step * terms + term) * fan_in, fan_in)
        turned[pl.ds(start, fan_in), :] = part.T
        total = total + jnp.dot(part, weights[1 + term][0], preferred_element_type=jnp.float32)
    mixed[...] = total


def layer_one_kernel(
    powers_ref,
    all_ref,
    own_ref,
    weight_0,
    weight_a,
    weight_b,
    weight_c,
    bias_ref,
    gain_ref,
    shift_ref,
    valid_ref,
    hidden_ref,
    turned_ref,
    mixed_ref,
):
    step = pl.program_id(0)
    weights = (weight_0, weight_a, weight_b, weight_c)
    forward_step(step, powers_ref, all_ref, own_ref, weights, bias_ref, turned_ref, mixed_ref)

    @pl.when(step == pl.num_programs(0) - 1)
    def finish_layer():
        normed, ignored = norm_forward(mixed_ref[...])
        hidden = (normed * gain_ref[...] + shift_ref[...]) * valid_ref[...]
        hidden_ref[...] = hidden.astype(jnp.bfloat16)


def layer_two_kernel(
    place_ref,
    powers_ref,
    all_ref,
    own_ref,
    weight_0,
    weight_a,
    weight_b,
    weight_c,
    bias_ref,
    gain_ref,
    shift_ref,
    valid_ref,
    upstream_ref,
    active_ref,
    low_ref,
    rest_ref,
    mine_ref,
    other_ref,
    turned,
    mixed,
):
    step = pl.program_id(0)
    weights = (weight_0, weight_a, weight_b, weight_c)
    forward_step(step, powers_ref, all_ref, own_ref, weights, bias_ref, turned, mixed)

    @pl.when(step == pl.num_programs(0) - 1)
    def finish_layer():
        normed, ignored = norm_forward(mixed[...])
        active = (normed * gain_ref[...] + shift_ref[...]) * valid_ref[...]
        active_ref[...] = active.astype(jnp.bfloat16)
        low, rest = norm_backward(
            mixed[...], upstream_ref[...].astype(jnp.float32), gain_ref[...], valid_ref[...]
        )
        low_ref[...] = low
        for place in range(3):
            rest_ref[place : place + 1, :] = rest[place]
        weight_gradient(turned, low, place_ref[1], mine_ref, other_ref)


def backward_step(step, powers_ref, all_ref, own_ref, weights, total):
    terms, own_cap, span = powers_ref.shape
    transposed = (((1,), (1,)), ((), ()))

    @pl.when(step == 0)
    def first():
        total[...] = lax.dot_general(
            own_ref[...], weights[0][0], transposed, preferred_element_type=jnp.float32
        )

    low = jnp.dot(
        powers_ref[...].reshape(terms * own_cap, span),
        all_ref[...],
        preferred_element_type=jnp.float32,
    ).astype(jnp.bfloat16)
    value = total[...]
    for term in range(terms):
        value = value + lax.dot_general(
            low[term * own_cap : (term + 1) * own_cap],
            weights[1 + term][0],
            transposed,
            preferred_element_type=jnp.float32,
        )
    total[...] = value


def back_two_kernel(
    place_ref,
    powers_ref,
    all_ref,
    own_ref,
    weight_0,
    weight_a,
    weight_b,
    weight_c,
    turned_ref,
    mixed_ref,
    gain_ref,
    valid_ref,
    rest_ref,
    low_ref,
    mine_ref,
    other_ref,
    total,
):
    step = pl.program_id(0)
    weights = (weight_0, weight_a, weight_b, weight_c)
    backward_step(step, powers_ref, all_ref, own_ref, weights, total)

    @pl.when(step == pl.num_programs(0) - 1)
    def finish_layer():
        low, rest = norm_backward(mixed_ref[...], total[...], gain_ref[...], valid_ref[...])
        low_ref[...] = low
        weight_gradient(turned_ref, low, place_ref[1], mine_ref, other_ref)
        part = turned_ref.shape[0] // 4
        extra = jnp.zeros((2, mine_ref.shape[1] - part, mine_ref.shape[2]), jnp.bfloat16)
        rows = rest + [rest_ref[place : place + 1, :] for place in range(3)]
        rows = jnp.concatenate(rows + [jnp.zeros((10, rows[0].shape[1]), jnp.float32)], axis=0)

        def below(first_ref, second_ref):
            first_ref[:, part:, :] = extra
            second_ref[:, part:, :] = extra
            first_ref[0, part : part + 16, :] = rows.astype(jnp.bfloat16)

        @pl.when(place_ref[1] == 0)
        def low_half_here():
            below(mine_ref, other_ref)

        @pl.when(place_ref[1] == 1)
        def low_half_there():
            below(other_ref, mine_ref)


def back_one_kernel(
    powers_ref, all_ref, own_ref, weight_0, weight_a, weight_b, weight_c, out_ref, total
):
    step = pl.program_id(0)
    weights = (weight_0, weight_a, weight_b, weight_c)
    backward_step(step, powers_ref, all_ref, own_ref, weights, total)

    @pl.when(step == pl.num_programs(0) - 1)
    def finish_layer():
        out_ref[...] = total[...].astype(jnp.bfloat16)


def layer_pass(kernel, name, place, powers, everyone, own, weight, others, outs, scratch):
    ignored, own_cap, span = powers.shape
    fan_in, width = weight.shape[1:]

    def whole(value):
        return pl.BlockSpec(value.shape, lambda step: (0,) * len(value.shape))

    def term_weight(term):
        return pl.BlockSpec((1, fan_in, width), lambda step: (1 + step * TERMS + term, 0, 0))

    in_specs = [
        pl.BlockSpec((TERMS, own_cap, span), lambda step: (step, 0, 0)),
        whole(everyone),
        whole(own),
        pl.BlockSpec((1, fan_in, width), lambda step: (0, 0, 0)),
    ]
    in_specs += [term_weight(term) for term in range(TERMS)] + [whole(value) for value in others]
    operands = [powers, everyone, own] + [weight] * (1 + TERMS) + list(others)
    if place is not None:
        in_specs = [pl.BlockSpec(memory_space=pltpu.SMEM)] + in_specs
        operands = [place] + operands
    return pl.pallas_call(
        kernel,
        grid=((ORDER - 1) // TERMS,),
        out_shape=outs,
        in_specs=in_specs,
        out_specs=[whole(value) for value in outs],
        scratch_shapes=[pltpu.VMEM(shape, dtype) for shape, dtype in scratch],
        compiler_params=pltpu.CompilerParams(vmem_limit_bytes=VMEM_BYTES),
        cost_estimate=NO_COST,
        name=name,
    )(*operands)


def finish_kernel(scalars_ref, pair_ref, siblings_ref, other_ref, out_ref, *small_refs):
    step = pl.program_id(0)
    part = out_ref.shape[1]
    for here, values_ref in ((step < 2, pair_ref), (step >= 2, siblings_ref)):
        @pl.when(here & (scalars_ref[0] == 1))
        def fast_form():
            out_ref[0] = values_ref[0, :part, :].astype(jnp.float32)

        for small_ref in small_refs:
            @pl.when(here & (scalars_ref[1 + step] == 0))
            def small_sums():
                small_ref[...] = values_ref[0, part : part + 16, :].astype(jnp.float32)

    @pl.when(scalars_ref[0] == 0)
    def general_form():
        out_ref[0] = other_ref[0].astype(jnp.float32)


def finished(scalars, pair, siblings, other, with_small=False):
    count, part, width = other.shape
    out, held = (1, part, width), (1,) + pair.shape[1:]
    out_specs = [pl.BlockSpec(out, lambda step, ref: (ref[1 + step], 0, 0))]
    out_shape = [jax.ShapeDtypeStruct(other.shape, jnp.float32)]
    if with_small:
        out_specs.append(pl.BlockSpec((16, width), lambda step, ref: (0, 0)))
        out_shape.append(jax.ShapeDtypeStruct((16, width), jnp.float32))
    return pl.pallas_call(
        finish_kernel,
        grid_spec=pltpu.PrefetchScalarGridSpec(
            num_scalar_prefetch=1,
            grid=(count,),
            in_specs=[
                pl.BlockSpec(held, lambda step, ref: (jnp.minimum(step, 1), 0, 0)),
                pl.BlockSpec(held, lambda step, ref: (jnp.maximum(step - 2, 0), 0, 0)),
                pl.BlockSpec(out, lambda step, ref: ((1 - ref[0]) * ref[1 + step], 0, 0)),
            ],
            out_specs=out_specs,
        ),
        out_shape=out_shape,
        compiler_params=pltpu.CompilerParams(vmem_limit_bytes=VMEM_BYTES),
        cost_estimate=NO_COST,
        name="finished",
    )(scalars, pair, siblings, other)


def unpack_kernel(place_ref, pieces_ref, keys_ref, own_ref, quadrant_ref, columns, hot):
    groups, high, lanes = pieces_ref.shape
    own_cap, span = own_ref.shape
    whole = own_cap // lanes
    send_cap = keys_ref.shape[1] // groups
    half, rest = send_cap // 2, own_cap - whole * lanes
    for group in range(groups):
        start = group * send_cap
        for tile in range(whole):
            columns[start : start + send_cap, tile * lanes : (tile + 1) * lanes] = pieces_ref[
                group, tile * send_cap : (tile + 1) * send_cap, :
            ]
        ends = pieces_ref[group, whole * send_cap :, :]
        columns[start : start + half, whole * lanes :] = ends[:, :rest]
        columns[start + half : start + send_cap, whole * lanes :] = ends[:, rest:]
    standing = lax.broadcasted_iota(jnp.int32, hot.shape, 0)
    hot[...] = jnp.where(standing == keys_ref[...], 1.0, 0.0).astype(jnp.bfloat16)
    block = jnp.dot(hot[...], columns[...], preferred_element_type=jnp.float32)
    own_ref[...] = block.T.astype(jnp.bfloat16)
    middle = span // 2

    @pl.when(place_ref[0] == 0)
    def first():
        quadrant_ref[...] = own_ref[:, :middle]

    @pl.when(place_ref[0] == 1)
    def second():
        quadrant_ref[...] = own_ref[:, middle:]


def unpacked_block(pieces, keys, place, own_cap, span):
    vector = pl.BlockSpec(memory_space=pltpu.VMEM)
    return pl.pallas_call(
        unpack_kernel,
        out_shape=[
            jax.ShapeDtypeStruct((own_cap, span), jnp.bfloat16),
            jax.ShapeDtypeStruct((own_cap, span // 2), jnp.bfloat16),
        ],
        in_specs=[pl.BlockSpec(memory_space=pltpu.SMEM), vector, vector],
        out_specs=[vector, vector],
        scratch_shapes=[
            pltpu.VMEM((keys.shape[1], own_cap), jnp.bfloat16),
            pltpu.VMEM((span, keys.shape[1]), jnp.bfloat16),
        ],
        compiler_params=pltpu.CompilerParams(vmem_limit_bytes=VMEM_BYTES),
        cost_estimate=NO_COST,
        name="unpacked_block",
    )(place, pieces, keys)


def fit_kernel(codes_ref, out_ref, *, n_row, caps):
    own_cap, send_cap, seat_cap = caps
    codes = codes_ref[...]
    devices = codes.shape[0]
    n_col = devices // n_row
    label = lax.broadcasted_iota(jnp.int32, (devices, 128), 1)
    counts = jnp.zeros((devices, 128), jnp.float32)
    for cluster in range(CLUSTERS):
        here = jnp.where(codes == 2 * cluster + 1, 1.0, 0.0)
        counts = counts + jnp.where(
            label == cluster, jnp.sum(here, axis=1, keepdims=True), 0.0
        )
    sizes = jnp.sum(counts, axis=0, keepdims=True)
    across = jnp.broadcast_to(sizes, (128, 128))
    down = across.T
    first = lax.broadcasted_iota(jnp.int32, (128, 128), 0)
    second = lax.broadcasted_iota(jnp.int32, (128, 128), 1)
    ahead = (across > down) | ((across == down) & (second < first))
    ahead = ahead & (second < CLUSTERS)
    rank = jnp.sum(jnp.where(ahead, 1.0, 0.0), axis=1, keepdims=True).astype(jnp.int32)
    others = n_row - 1
    later = rank > others
    turn = jnp.zeros_like(rank)
    for count in range(1, CLUSTERS // others + 1):
        turn = turn + jnp.where(rank - 1 >= count * others, 1, 0)
    place = rank - 1 - turn * others
    group = jnp.where(rank == 0, 0, 1 + jnp.where(later, others - 1 - place, place))
    member = (group == second) & (first < CLUSTERS)
    held = jnp.dot(
        counts.astype(jnp.bfloat16),
        jnp.where(member, 1.0, 0.0).astype(jnp.bfloat16),
        preferred_element_type=jnp.float32,
    )
    by_row = jnp.zeros((1, 128), jnp.float32)
    for row in range(n_row):
        rows = jnp.sum(held[row * n_col : (row + 1) * n_col], axis=0, keepdims=True)
        by_row = jnp.maximum(by_row, rows)
    device = lax.broadcasted_iota(jnp.int32, (devices, 128), 0)
    by_col = jnp.zeros((1, 128), jnp.float32)
    for col in range(n_col):
        cols = jnp.where(device % n_col == col, held, 0.0)
        by_col = jnp.maximum(by_col, jnp.sum(cols, axis=0, keepdims=True))
    fits = (
        (jnp.max(by_col) <= own_cap) & (jnp.max(by_row) <= send_cap) & (jnp.max(held) <= seat_cap)
    )
    out_ref[0] = jnp.where(fits, 1, 0)


def fits_in(codes, n_row, caps):
    fits = pl.pallas_call(
        functools.partial(fit_kernel, n_row=n_row, caps=caps),
        out_shape=jax.ShapeDtypeStruct((1,), jnp.int32),
        in_specs=[pl.BlockSpec(memory_space=pltpu.VMEM)],
        out_specs=pl.BlockSpec(memory_space=pltpu.SMEM),
        cost_estimate=NO_COST,
        name="fits",
    )(codes.reshape(-1, codes.shape[-1]))
    return fits


def exclusive_counts(member):
    count = member.shape[-1]
    before = jnp.arange(count)[:, None] < jnp.arange(count)[None, :]
    return jnp.dot(
        member.astype(jnp.bfloat16),
        before.astype(jnp.bfloat16),
        preferred_element_type=jnp.float32,
    ).astype(jnp.int32)


def assign(codes, n_row):
    cluster, valid = codes >> 1, codes & 1
    labels = jnp.arange(CLUSTERS)
    sizes = jnp.sum(
        (cluster.reshape(1, -1) == labels[:, None]) & (valid.reshape(1, -1) == 1), axis=1
    )
    ahead = (sizes[None, :] > sizes[:, None]) | (
        (sizes[None, :] == sizes[:, None]) & (labels[None, :] < labels[:, None])
    )
    rank = jnp.sum(ahead, axis=1)
    others = n_row - 1
    turn, place = (rank - 1) // others, (rank - 1) % others
    group = jnp.where(rank == 0, 0, 1 + jnp.where(turn == 0, place, others - 1 - place))
    of_node = jnp.sum(
        jnp.where(cluster[None] == labels[:, None, None, None], group[:, None, None, None], 0),
        axis=0,
    )
    return jnp.where(valid == 1, of_node, n_row)


def compact(
    codes,
    group,
    features,
    block_keep,
    edge_weight,
    weight_one,
    bias_one,
    gain_one,
    shift_one,
    weight_two,
    bias_two,
    gain_two,
    shift_two,
    cotangent,
    places_of,
    slots_of,
    seats_of,
    decide,
    sizes,
    caps,
):
    row, col = lax.axis_index("row"), lax.axis_index(COL)
    chip, core = lax.axis_index("chip"), lax.axis_index("core")
    n_row, n_col = sizes
    own_cap, send_cap, seat_cap = caps
    own_nodes, in_width = features.shape
    width = weight_two.shape[2]
    span = n_col * own_cap
    targets = jnp.arange(n_row)

    def in_col(value):
        return lax.dynamic_index_in_dim(value, col, 1, False).reshape(-1)

    def in_row(value):
        return lax.dynamic_index_in_dim(value, row, 0, False).reshape(-1)

    row_group, col_group = in_row(group), in_col(group)
    row_slots, col_places = in_row(slots_of(group)), in_col(places_of(group))
    row_keys = jnp.where(row_slots < send_cap, row_group * send_cap + row_slots, -1)
    col_keys = jnp.where(col_places < own_cap, col_group * own_cap + col_places, -1)
    pieces = packed_pieces(
        block_keep,
        in_row(codes),
        in_col(codes),
        row_keys,
        col_keys,
        edge_weight,
        (own_cap, send_cap),
        n_row,
    )
    pieces, codes = lax.optimization_barrier((pieces, codes))
    group = assign(codes, n_row)
    pieces = trade(pieces, "row")
    places, slots, seats = places_of(group), slots_of(group), seats_of(group)

    standing = jnp.arange(n_col)[None, :, None] * own_cap + places
    fits_here = jnp.where(group == row, standing, -1).reshape(n_row, -1)
    slot_of = slots.reshape(n_row, -1)
    target = jnp.max(
        jnp.where(
            slot_of[:, None, :] == jnp.arange(send_cap)[None, :, None], fits_here[:, None, :], -1
        ),
        axis=2,
    )
    keys = target.reshape(1, -1)

    def to_partner(value, step):
        return lax.ppermute(value, "row", [(place, place ^ step) for place in range(n_row)])

    partners = row ^ targets
    group_here = lax.dynamic_index_in_dim(in_row(group).reshape(n_col, -1), col, 0, False)
    seat_here = lax.dynamic_index_in_dim(in_row(seats).reshape(n_col, -1), col, 0, False)

    def seat_of_node(groups):
        hot = (group_here[None, None, :] == groups[:, None, None]) & (
            seat_here[None, None, :] == jnp.arange(seat_cap)[None, :, None]
        )
        return hot.astype(jnp.bfloat16).reshape(n_row * seat_cap, own_nodes)

    enter_home = seat_of_node(targets).T
    enter_partner = seat_of_node(partners)
    both = jnp.dot(enter_partner, jnp.concatenate([features, cotangent], axis=1))
    both = both.reshape(n_row, seat_cap, -1)
    enter_partner = enter_partner.T
    both, codes = lax.optimization_barrier((both, codes))
    fits, others = decide(codes)
    group_col = lax.dynamic_index_in_dim(group, col, 1, False)
    seats_col = lax.dynamic_index_in_dim(seats, col, 1, False)
    places_col = lax.dynamic_index_in_dim(places, col, 1, False)
    seated = (group_col == row)[:, None, :] & (
        seats_col[:, None, :] == jnp.arange(seat_cap)[None, :, None]
    )
    place_of_seat = jnp.max(jnp.where(seated, places_col[:, None, :], -1), axis=2)
    from_partner = jnp.max(
        jnp.where((partners[:, None] == targets)[:, :, None], place_of_seat[None], -1), axis=1
    )
    arrive = from_partner.reshape(1, -1) == jnp.arange(own_cap)[:, None]
    arrive = arrive.astype(jnp.bfloat16)
    leave_group = place_of_seat.reshape(-1, 1) == jnp.arange(own_cap)
    leave_group = leave_group.astype(jnp.bfloat16)
    leave_partner = jnp.concatenate([from_partner[::2], from_partner[1::2]])
    leave_partner = leave_partner.reshape(-1, 1) == jnp.arange(own_cap)
    leave_partner = leave_partner.astype(jnp.bfloat16)
    held_count = jnp.sum(group_col == row)
    valid_rows = (jnp.arange(own_cap) < held_count).astype(jnp.float32)[:, None]
    place = jnp.stack([chip, core]).astype(jnp.int32)
    quarters = jnp.stack([col, (1 - chip) * 2 + core, chip * 2 + 1 - core, 3 - col])
    quarters = jnp.concatenate([fits, quarters.astype(jnp.int32)])
    scalars = (chip, 1 - chip, col * own_cap)
    scalars = tuple(value.astype(jnp.uint32) for value in scalars) + (chip == 0, core == 0, place, quarters)
    homes = enter_home, enter_partner, leave_group, leave_partner
    pieces, both, keys, arrive, homes, valid_rows, others, scalars = lax.optimization_barrier(
        (pieces, both, keys, arrive, homes, valid_rows, others, scalars)
    )
    enter_home, enter_partner, leave_group, leave_partner = homes
    this_chip, other_chip, own_start, first_chip, first_core, place, quarters = scalars

    own_block, quadrant = unpacked_block(pieces, keys, place, own_cap, span)
    quadrant = swap(quadrant, "chip")
    both = [both[0]] + [to_partner(both[step], step) for step in range(1, n_row)]
    sibling = swap(own_block, "core")
    quadrant, *early = lax.optimization_barrier((quadrant, *both[:-2]))
    adjacency = normalized_block(own_block, sibling, quadrant, swap(quadrant, "core"), place)
    adjacency, *late = lax.optimization_barrier((adjacency, *both[-2:]))
    both = early + late
    mine = jnp.dot(arrive, jnp.concatenate(both))
    features_own, cotangent_own = mine[:, :in_width], mine[:, in_width:]
    sibling = swap(features_own, "core")

    first = (own_start + jnp.arange(own_cap, dtype=jnp.uint32))[:, None]
    first = first == jnp.arange(span, dtype=jnp.uint32)[None, :]
    previous = first.astype(jnp.float32)
    current = -lax.dynamic_slice_in_dim(adjacency, own_start, own_cap, 0).astype(jnp.float32)
    lowered = [current.astype(jnp.bfloat16)]
    for position in range(2, ORDER):
        upcoming = (
            -2.0 * jnp.dot(lowered[-1], adjacency, preferred_element_type=jnp.float32) - previous
        )
        low = upcoming.astype(jnp.bfloat16)
        if position == 4:
            low, sibling = lax.optimization_barrier((low, sibling))
            features_chip = joined(features_own, sibling, first_core)
            partner = swap(features_chip, "chip")
        if position == 8:
            low, partner = lax.optimization_barrier((low, partner))
            features_all = joined(features_chip, partner, first_chip)
        previous, current = current, upcoming
        lowered.append(low)
    powers = jnp.concatenate(lowered, axis=0).reshape(ORDER - 1, own_cap, span)

    def everywhere(value_low):
        return lax.all_gather(value_low, COL, axis=0, tiled=True)

    def chosen(value, other):
        return jnp.where(quarters[0] == 1, value.astype(jnp.float32), other.astype(jnp.float32))

    def shaped(*shape, dtype=jnp.bfloat16):
        return jax.ShapeDtypeStruct(shape, dtype)

    part_one, part_two = ORDER * in_width // n_col, ORDER * width // n_col
    padded = -(-(part_one + 16) // (8 * n_row)) * (8 * n_row)
    hidden, turned_one, mixed_one = layer_pass(
        layer_one_kernel,
        "layer_one",
        None,
        powers,
        features_all,
        features_own,
        weight_one,
        [bias_one[None], gain_one[None], shift_one[None], valid_rows],
        [
            shaped(own_cap, width),
            shaped(n_col * part_one, own_cap),
            shaped(own_cap, width, dtype=jnp.float32),
        ],
        [],
    )
    activations, low_two, rest_two, mine, other = layer_pass(
        layer_two_kernel,
        "layer_two",
        place,
        powers,
        everywhere(hidden),
        hidden,
        weight_two,
        [bias_two[None], gain_two[None], shift_two[None], valid_rows, cotangent_own],
        [
            shaped(own_cap, width),
            shaped(own_cap, width),
            shaped(3, width, dtype=jnp.float32),
            shaped(2, part_two, width),
            shaped(2, part_two, width),
        ],
        [((n_col * part_two, own_cap), jnp.bfloat16), ((own_cap, width), jnp.float32)],
    )

    def add_cores(mine, other):
        got = swap(other, "core")
        return tuple(
            added(
                lax.dynamic_index_in_dim(mine, index, 0, False),
                lax.dynamic_index_in_dim(got, index, 0, False),
            )
            for index in (this_chip, other_chip)
        )

    leaving = jnp.dot(leave_partner, activations).reshape(n_row, seat_cap, width)
    near, far = leaving[: n_row // 2], leaving[n_row // 2 :]
    far = to_partner(far, 1)
    here, there = add_cores(mine, other)
    everyone_two, there, far = lax.optimization_barrier((everywhere(low_two), there, far))
    there = swap(there, "chip")
    arrived = [jnp.stack([near[0], far[0]])] + [
        to_partner(jnp.stack([near[half], far[half]]), 2 * half) for half in range(1, n_row // 2)
    ]
    low_one, mine, other = layer_pass(
        back_two_kernel,
        "back_two",
        place,
        powers,
        everyone_two,
        low_two,
        weight_two,
        [turned_one, mixed_one, gain_one[None], valid_rows, rest_two],
        [shaped(own_cap, width), shaped(2, padded, width), shaped(2, padded, width)],
        [((own_cap, width), jnp.float32)],
    )
    low_one, there, arrived = lax.optimization_barrier((low_one, there, arrived))
    second = added(here, there).reshape(n_row, -1, width)
    many = second.shape[1]
    low_one, second = lax.optimization_barrier((low_one, second))
    second = trade(second, "row")
    here, there = add_cores(mine, other)
    there = swap(there, "chip")
    first = added(here, there).reshape(n_row, -1, width)
    share = first.shape[1]
    second = jnp.sum(second.astype(jnp.float32), axis=0).astype(jnp.bfloat16)
    second = jnp.broadcast_to(second[None], (n_row,) + second.shape)
    mixed = jnp.concatenate([second, first], axis=1)
    low_one, mixed = lax.optimization_barrier((low_one, mixed))
    everyone_one = everywhere(low_one)
    mixed = trade(mixed, "row")
    (input_grad,) = layer_pass(
        back_one_kernel,
        "back_one",
        None,
        powers,
        everyone_one,
        low_one,
        weight_one,
        [],
        [shaped(own_cap, in_width)],
        [((own_cap, in_width), jnp.float32)],
    )
    leaving = jnp.dot(leave_group, input_grad)
    leaving = leaving.reshape(n_row, seat_cap * in_width // width, width)
    arrived = jnp.concatenate(arrived).reshape(-1, width)
    home = jnp.dot(enter_partner, arrived, preferred_element_type=jnp.float32)
    home = chosen(home, others[0])
    mixed, leaving, home = lax.optimization_barrier((mixed, leaving, home))
    first = jnp.sum(mixed[:, many:].astype(jnp.float32), axis=0).astype(jnp.bfloat16)
    first = jnp.broadcast_to(first[None], (n_row,) + first.shape)
    first, mixed = lax.optimization_barrier((jnp.concatenate([first, leaving], axis=1), mixed))
    first = trade(first, "row")
    second = mixed[:, :many].reshape(1, -1, width)
    partner_two = swap(second, "chip")
    first, partner_two = lax.optimization_barrier((first, partner_two))
    mine = first[:, :share].reshape(1, -1, width)
    partner = swap(mine, "chip")
    second = jnp.concatenate([second, partner_two])
    (second,) = finished(quarters, second, swap(second, "core"), others[3])
    back = first[:, share:].reshape(n_row * seat_cap, in_width)
    home_grad = jnp.dot(enter_home, back, preferred_element_type=jnp.float32)
    home_grad = chosen(home_grad, others[1])
    partner, second, home_grad = lax.optimization_barrier((partner, second, home_grad))
    pair = jnp.concatenate([mine, partner])
    siblings = swap(pair, "core")
    first, small = finished(quarters, pair, siblings, others[2], True)
    return home, home_grad, first, second, chosen(small[:6], others[4])


def general(
    codes,
    features,
    block_keep,
    edge_weight,
    weight_one,
    bias_one,
    gain_one,
    shift_one,
    weight_two,
    bias_two,
    gain_two,
    shift_two,
    cotangent,
    node_valid,
):
    row, col = lax.axis_index("row"), lax.axis_index(COL)
    row_codes = lax.dynamic_index_in_dim(codes, row, 0, False).reshape(-1)
    col_codes = lax.dynamic_index_in_dim(codes, col, 1, False).reshape(-1)
    tile_rows, tile_cols = edge_weight.shape
    blocks_down, blocks_across = block_keep.shape
    block_side = tile_rows // blocks_down
    linked = (row_codes[:, None] == col_codes[None, :]) & (row_codes[:, None] & 1 == 1)
    linked = linked.reshape(blocks_down, block_side, blocks_across, block_side) & (
        block_keep[:, None, :, None] == 1
    )
    masked = edge_weight * linked.reshape(tile_rows, tile_cols).astype(jnp.bfloat16)
    degree_rows = 1.0 + lax.psum(jnp.sum(masked, axis=1, dtype=jnp.float32), COL)
    own_nodes = features.shape[0]
    own_degree = lax.dynamic_slice_in_dim(
        degree_rows, lax.axis_index(COL) * own_nodes, own_nodes, 0
    )
    degree_cols = lax.all_gather(own_degree, "row", axis=0, tiled=True)
    adjacency = (
        masked.astype(jnp.float32)
        * lax.rsqrt(degree_rows)[:, None]
        * lax.rsqrt(degree_cols)[None, :]
    ).astype(jnp.bfloat16)
    valid_rows = node_valid.astype(jnp.float32)
    stacked_one, mixed_one, hidden = layer_forward(
        adjacency,
        features.astype(jnp.float32),
        weight_one,
        bias_one,
        gain_one,
        shift_one,
        valid_rows,
    )
    stacked_two, mixed_two, activations = layer_forward(
        adjacency, hidden, weight_two, bias_two, gain_two, shift_two, valid_rows
    )
    hidden_grad, weight_two_grad, bias_two_grad, gain_two_grad, shift_two_grad = layer_backward(
        adjacency,
        stacked_two,
        mixed_two,
        cotangent.astype(jnp.float32),
        weight_two,
        gain_two,
        shift_two,
        valid_rows,
    )
    input_grad, weight_one_grad, bias_one_grad, gain_one_grad, shift_one_grad = layer_backward(
        adjacency, stacked_one, mixed_one, hidden_grad, weight_one, gain_one, shift_one, valid_rows
    )
    summed = lax.psum(
        (
            weight_one_grad,
            bias_one_grad,
            gain_one_grad,
            shift_one_grad,
            weight_two_grad,
            bias_two_grad,
            gain_two_grad,
            shift_two_grad,
        ),
        ("row",) + COL,
    )
    weight_one_grad, bias_one_grad, gain_one_grad, shift_one_grad = (
        summed[0],
        summed[1],
        summed[2],
        summed[3],
    )
    weight_two_grad, bias_two_grad, gain_two_grad, shift_two_grad = (
        summed[4],
        summed[5],
        summed[6],
        summed[7],
    )
    return (
        activations,
        input_grad,
        weight_one_grad,
        bias_one_grad,
        gain_one_grad,
        shift_one_grad,
        weight_two_grad,
        bias_two_grad,
        gain_two_grad,
        shift_two_grad,
    )


def local(n_row, n_col, *args):
    (
        features,
        node_valid,
        cluster,
        block_keep,
        edge_weight,
        weight_one,
        bias_one,
        gain_one,
        shift_one,
        weight_two,
        bias_two,
        gain_two,
        shift_two,
        cotangent,
    ) = args
    own_nodes, in_width = features.shape
    own_cap = own_nodes * n_row * 5 // 16
    send_cap = own_nodes * n_col * 11 // 32
    seat_cap = own_nodes * 7 // 16
    codes = broadcast_along(cluster * 2 + node_valid, ("row",) + COL, n_row * n_col)
    codes = codes.reshape(n_row, n_col, own_nodes)
    shared = (
        block_keep,
        edge_weight,
        weight_one,
        bias_one,
        gain_one,
        shift_one,
        weight_two,
        bias_two,
        gain_two,
        shift_two,
        cotangent,
    )

    def slow():
        return general(codes, features, *shared, node_valid)

    held = (ORDER - 1) * own_cap * own_cap * n_col * 2
    if held > HELD_BYTES or n_col != 4 or n_row < 2 or n_row & (n_row - 1):
        return slow()
    group = assign(codes, n_row)

    def member_of(group):
        return group[None] == jnp.arange(n_row)[:, None, None, None]

    def places_of(group):
        member = member_of(group).transpose(0, 2, 1, 3).reshape(n_row, n_col, -1)
        places = jnp.sum(jnp.where(member, exclusive_counts(member), 0), axis=0)
        return places.reshape(n_col, n_row, own_nodes).transpose(1, 0, 2)

    def slots_of(group):
        member = member_of(group).reshape(n_row, n_row, -1)
        slots = jnp.sum(jnp.where(member, exclusive_counts(member), 0), axis=0)
        return slots.reshape(n_row, n_col, own_nodes)

    def seats_of(group):
        member = member_of(group)
        return jnp.sum(jnp.where(member, exclusive_counts(member), 0), axis=0)

    width = weight_two.shape[2]

    def instead(state):
        made = slow()
        small = jnp.stack([made[place] for place in (3, 4, 5, 7, 8, 9)])
        return (jnp.ones_like(state[0]),) + tuple(
            value.astype(jnp.bfloat16).reshape(like.shape)
            for value, like in zip((made[0], made[1], made[2], made[6], small), state[1:])
        )

    shapes = (
        (own_nodes, width),
        (own_nodes, in_width),
        (n_col, ORDER * in_width // n_col, width),
        (n_col, ORDER * width // n_col, width),
        (6, width),
    )

    def decide(codes):
        fits = fits_in(codes, n_row, (own_cap, send_cap, seat_cap))
        others = lax.while_loop(
            lambda state: state[0][0] == 0,
            instead,
            (fits,) + tuple(jnp.zeros(shape, jnp.bfloat16) for shape in shapes),
        )[1:]
        return fits, others

    home, home_grad, first, second, small = compact(
        codes,
        group,
        features,
        *shared,
        places_of,
        slots_of,
        seats_of,
        decide,
        (n_row, n_col),
        (own_cap, send_cap, seat_cap),
    )
    return (
        home,
        home_grad,
        first.reshape(weight_one.shape),
        small[0],
        small[1],
        small[2],
        second.reshape(weight_two.shape),
        small[3],
        small[4],
        small[5],
    )


def solution(mesh):
    n_row, n_col = mesh.shape["row"], mesh.shape["col"]
    by_core = jax.sharding.Mesh(
        mesh.devices.reshape(n_row, n_col // 2, 2), ("row", "chip", "core")
    )
    nodes = ("row", "chip", "core")
    placed = (
        P(nodes, None),
        P(nodes),
        P(nodes),
        P("row", COL),
        P("row", COL),
        P(),
        P(),
        P(),
        P(),
        P(),
        P(),
        P(),
        P(),
        P(nodes, None),
    )
    return jax.shard_map(
        functools.partial(local, n_row, n_col),
        mesh=by_core,
        in_specs=placed,
        out_specs=(P(nodes, None), P(nodes, None), P(), P(), P(), P(), P(), P(), P(), P()),
        check_vma=False,
    )
```

```python
import functools
import math

import jax
import jax.numpy as jnp
from jax import lax
from jax.experimental import pallas as pl
from jax.experimental.pallas import tpu as pltpu
from jax.sharding import PartitionSpec as P

ORDER = 13
CLUSTERS = 16
HELD_BYTES = 1 << 25
VMEM_BYTES = 32 << 20
TERMS = 3
NO_COST = pl.CostEstimate(flops=1, bytes_accessed=1, transcendentals=0)
COL = ("chip", "core")


def finish(mixed, gain, shift, valid_rows):
    active = jax.nn.gelu(mixed, approximate=False)
    centered = active - jnp.mean(active, axis=-1, keepdims=True)
    variance = jnp.mean(centered * centered, axis=-1, keepdims=True)
    return (centered * lax.rsqrt(variance + 1e-05) * gain + shift) * valid_rows[:, None]


def forward_product(adjacency, piece_low):
    partial_value = jnp.dot(
        adjacency,
        lax.all_gather(piece_low, "row", axis=0, tiled=True),
        preferred_element_type=jnp.float32,
    )
    return lax.psum_scatter(partial_value, COL, scatter_dimension=0, tiled=True)


def backward_product(adjacency, piece_low):
    partial_value = lax.dot_general(
        adjacency,
        lax.all_gather(piece_low, COL, axis=0, tiled=True),
        (((0,), (0,)), ((), ())),
        preferred_element_type=jnp.float32,
    )
    return lax.psum_scatter(
        partial_value.astype(jnp.bfloat16), "row", scatter_dimension=0, tiled=True
    ).astype(jnp.float32)


def layer_forward(adjacency, inputs, weight, bias, gain, shift, valid_rows):
    first_low = inputs.astype(jnp.bfloat16)
    second = -forward_product(adjacency, first_low)
    second_low = second.astype(jnp.bfloat16)

    def advance(state_pair, unused):
        previous, current, current_low = state_pair
        upcoming = -2.0 * forward_product(adjacency, current_low) - previous
        upcoming_low = upcoming.astype(jnp.bfloat16)
        return ((current, upcoming, upcoming_low), upcoming_low)

    ignored, others = lax.scan(advance, (inputs, second, second_low), None, length=ORDER - 2)
    stacked = jnp.concatenate([first_low[None], second_low[None], others], axis=0)
    mixed = jnp.einsum("kni,kio->no", stacked, weight, preferred_element_type=jnp.float32) + bias
    return (stacked, mixed, finish(mixed, gain, shift, valid_rows))


def layer_backward(adjacency, stacked, mixed, upstream, weight, gain, shift, valid_rows):

    def local_finish(mixed_in, gain_in, shift_in):
        return finish(mixed_in, gain_in, shift_in, valid_rows)

    ignored, pullback = jax.vjp(local_finish, mixed, gain, shift)
    mixed_grad, gain_grad, shift_grad = pullback(upstream)
    mixed_low = mixed_grad.astype(jnp.bfloat16)
    bias_grad = jnp.sum(mixed_low.astype(jnp.float32), axis=0)
    weight_grad = jnp.einsum("kni,no->kio", stacked, mixed_low, preferred_element_type=jnp.float32)
    direct = jnp.einsum("no,kio->kni", mixed_low, weight, preferred_element_type=jnp.float32)

    def retreat(state_pair, direct_term):
        later_two, later_one = state_pair
        current = (
            direct_term
            - 2.0 * backward_product(adjacency, later_one.astype(jnp.bfloat16))
            - later_two
        )
        return ((later_one, current), None)

    start_pair = (jnp.zeros_like(direct[0]), direct[ORDER - 1])
    (second_grad, first_grad), unused = lax.scan(
        retreat, start_pair, direct[1 : ORDER - 1], reverse=True
    )
    input_grad = (
        direct[0] - backward_product(adjacency, first_grad.astype(jnp.bfloat16)) - second_grad
    )
    return (input_grad, weight_grad, bias_grad, gain_grad, shift_grad)


def swap(value, axis):
    return lax.ppermute(value, axis, [(0, 1), (1, 0)])


def trade(pieces, axis):
    return lax.all_to_all(pieces, axis, 0, 0, tiled=False)


def broadcast_along(value, axis, size):
    return trade(jnp.broadcast_to(value[None], (size,) + value.shape), axis)


def joined(mine, other, mine_first):
    return jnp.where(
        mine_first, jnp.concatenate([mine, other]), jnp.concatenate([other, mine])
    )


def added(mine, received):
    return (mine.astype(jnp.float32) + received.astype(jnp.float32)).astype(jnp.bfloat16)


def assemble(place_ref, own_ref, sibling_ref, near_ref, far_ref, out_ref, done):
    chip, core = place_ref[0], place_ref[1]
    own_cap, span = own_ref.shape
    half = span // 2

    def rows(of_chip, of_core):
        return pl.ds(pl.multiple_of((2 * of_chip + of_core) * own_cap, own_cap), own_cap)

    def fetch(source, of_chip, of_core, columns, place):
        target = out_ref.at[rows(of_chip, of_core), columns]
        return pltpu.make_async_copy(source, target, done.at[place])

    def quadrant_copies(here):
        there = 1 - here
        columns = pl.ds(there * half, half)
        return (
            fetch(near_ref, there, core, columns, 2),
            fetch(far_ref, there, 1 - core, columns, 3),
        )

    everything = pl.ds(0, span)
    top = (
        fetch(own_ref, chip, core, everything, 0),
        fetch(sibling_ref, chip, 1 - core, everything, 1),
    )

    def of_chip(here):
        there = 1 - here
        copies = top + quadrant_copies(here)
        for copy in copies:
            copy.start()
        for copy in copies:
            copy.wait()
        here_rows = pl.ds(here * half, half)
        for tile in range(half // 128):
            columns = pl.ds(there * half + tile * 128, 128)
            strip = out_ref[here_rows, columns]
            turned = jnp.transpose(strip.astype(jnp.float32)).astype(jnp.bfloat16)
            out_ref[columns, here_rows] = turned

    @pl.when(chip == 0)
    def first():
        of_chip(0)

    @pl.when(chip == 1)
    def second():
        of_chip(1)

    across = jnp.ones((1, span), jnp.float32)
    for tile in range(span // 128):
        across = across + jnp.sum(
            out_ref[pl.ds(tile * 128, 128), :].astype(jnp.float32), axis=0, keepdims=True
        )
    across = lax.rsqrt(across)
    for tile in range(span // 128):
        strip = out_ref[pl.ds(tile * 128, 128), :].astype(jnp.float32)
        down = lax.rsqrt(1.0 + jnp.sum(strip, axis=1, keepdims=True))
        out_ref[pl.ds(tile * 128, 128), :] = (strip * down * across).astype(jnp.bfloat16)


def normalized_block(own, sibling, near, far, place):
    span = own.shape[1]
    return pl.pallas_call(
        assemble,
        out_shape=jax.ShapeDtypeStruct((span, span), jnp.bfloat16),
        in_specs=[pl.BlockSpec(memory_space=pltpu.SMEM)]
        + [pl.BlockSpec(memory_space=pltpu.HBM)] * 4,
        out_specs=pl.BlockSpec(memory_space=pltpu.VMEM),
        scratch_shapes=[pltpu.SemaphoreType.DMA((4,))],
        compiler_params=pltpu.CompilerParams(vmem_limit_bytes=VMEM_BYTES),
        cost_estimate=NO_COST,
        name="normalized_block",
    )(place, own, sibling, near, far)


def pack_kernel(
    keep_ref, row_codes_ref, col_codes_ref, row_keys_ref, col_keys_ref, weight_ref, out_ref,
    masked, picked, rows_hot, cols_hot
):
    tile_rows, tile_cols = weight_ref.shape
    blocks_down, blocks_across = keep_ref.shape
    groups, ignored, lanes = out_ref.shape
    send_cap, own_cap = rows_hot.shape[0] // groups, cols_hot.shape[0] // groups
    high, wide = tile_rows // blocks_down, tile_cols // blocks_across
    for down in range(blocks_down):
        for across in range(blocks_across):
            rows, columns = pl.ds(down * high, high), pl.ds(across * wide, wide)
            own, other = row_codes_ref[rows, :], col_codes_ref[:, columns]
            linked = (own == other) & (own % 2 == 1) & (keep_ref[down, across] == 1)
            weight = weight_ref[rows, columns].astype(jnp.float32)
            masked[rows, columns] = jnp.where(linked, weight, 0.0).astype(jnp.bfloat16)

    def one_hot(keys, start, count):
        standing = lax.broadcasted_iota(jnp.int32, (count, keys.shape[1]), 0) + start
        return jnp.where(standing == keys, 1.0, 0.0).astype(jnp.bfloat16)

    for group in range(groups):
        rows_hot[pl.ds(group * send_cap, send_cap), :] = one_hot(
            row_keys_ref[...], group * send_cap, send_cap
        )
        cols_hot[pl.ds(group * own_cap, own_cap), :] = one_hot(
            col_keys_ref[...], group * own_cap, own_cap
        )
    for tile in range(tile_cols // 256):
        columns = pl.ds(tile * 256, 256)
        picked[:, columns] = jnp.dot(
            rows_hot[...], masked[:, columns], preferred_element_type=jnp.float32
        ).astype(jnp.bfloat16)
    whole, half = own_cap // lanes, send_cap // 2
    for group in range(groups):
        packed = lax.dot_general(
            cols_hot[pl.ds(group * own_cap, own_cap), :],
            picked[pl.ds(group * send_cap, send_cap), :],
            (((1,), (1,)), ((), ())),
            preferred_element_type=jnp.float32,
        ).T
        for tile in range(whole):
            out_ref[group, pl.ds(tile * send_cap, send_cap), :] = packed[
                :, tile * lanes : (tile + 1) * lanes
            ].astype(jnp.bfloat16)
        ends = jnp.concatenate(
            [packed[:half, whole * lanes :], packed[half:, whole * lanes :]], axis=1
        )
        out_ref[group, pl.ds(whole * send_cap, half), :] = ends.astype(jnp.bfloat16)


def packed_pieces(block_keep, row_codes, col_codes, row_keys, col_keys, edge_weight, caps, groups):
    own_cap, send_cap = caps
    tile_rows, tile_cols = edge_weight.shape
    high = own_cap // 128 * send_cap + send_cap // 2
    vector = pl.BlockSpec(memory_space=pltpu.VMEM)
    return pl.pallas_call(
        pack_kernel,
        out_shape=jax.ShapeDtypeStruct((groups, high, 128), jnp.bfloat16),
        in_specs=[pl.BlockSpec(memory_space=pltpu.SMEM)] + [vector] * 5,
        out_specs=vector,
        scratch_shapes=[
            pltpu.VMEM((tile_rows, tile_cols), jnp.bfloat16),
            pltpu.VMEM((groups * send_cap, tile_cols), jnp.bfloat16),
            pltpu.VMEM((groups * send_cap, tile_rows), jnp.bfloat16),
            pltpu.VMEM((groups * own_cap, tile_cols), jnp.bfloat16),
        ],
        compiler_params=pltpu.CompilerParams(vmem_limit_bytes=VMEM_BYTES),
        cost_estimate=NO_COST,
        name="packed_pieces",
    )(block_keep, row_codes[:, None], col_codes[None], row_keys[None], col_keys[None], edge_weight)


def normal_share(mixed):
    return 0.5 * (1.0 + lax.erf(mixed * 0.5**0.5))


def norm_forward(mixed):
    active = mixed * normal_share(mixed)
    centered = active - jnp.mean(active, axis=-1, keepdims=True)
    scale = lax.rsqrt(jnp.mean(centered * centered, axis=-1, keepdims=True) + 1e-05)
    return centered * scale, scale


def norm_backward(mixed, upstream, gain, valid):
    normed, scale = norm_forward(mixed)
    upstream = upstream * valid
    inner = upstream * gain
    inner = inner - jnp.mean(inner, axis=-1, keepdims=True) - normed * jnp.mean(
        inner * normed, axis=-1, keepdims=True
    )
    density = jnp.exp(-0.5 * mixed * mixed) * (1.0 / (2.0 * math.pi) ** 0.5)
    low = (inner * scale * (normal_share(mixed) + mixed * density)).astype(jnp.bfloat16)
    rest = [low.astype(jnp.float32), upstream * normed, upstream]
    return low, [jnp.sum(value, axis=0, keepdims=True) for value in rest]


def weight_gradient(turned_ref, low, core, mine_ref, other_ref):
    part = turned_ref.shape[0] // 4

    def halves(first_ref, second_ref):
        for place in range(4):
            out_ref = second_ref if place % 2 else first_ref
            out_ref[place // 2, :part, :] = jnp.dot(
                turned_ref[place * part : (place + 1) * part, :],
                low,
                preferred_element_type=jnp.float32,
            ).astype(jnp.bfloat16)

    @pl.when(core == 0)
    def low_half_first():
        halves(mine_ref, other_ref)

    @pl.when(core == 1)
    def high_half_first():
        halves(other_ref, mine_ref)


def forward_step(step, powers_ref, all_ref, own_ref, weights, bias_ref, turned, mixed):
    terms, own_cap, span = powers_ref.shape
    fan_in = own_ref.shape[1]

    @pl.when(step == 0)
    def first():
        turned[:fan_in, :] = own_ref[...].T
        mixed[...] = bias_ref[...] + jnp.dot(
            own_ref[...], weights[0][0], preferred_element_type=jnp.float32
        )

    low = jnp.dot(
        powers_ref[...].reshape(terms * own_cap, span),
        all_ref[...],
        preferred_element_type=jnp.float32,
    ).astype(jnp.bfloat16)
    total = mixed[...]
    for term in range(terms):
        part = low[term * own_cap : (term + 1) * own_cap]
        start = pl.multiple_of((1 + step * terms + term) * fan_in, fan_in)
        turned[pl.ds(start, fan_in), :] = part.T
        total = total + jnp.dot(part, weights[1 + term][0], preferred_element_type=jnp.float32)
    mixed[...] = total


def layer_one_kernel(
    powers_ref,
    all_ref,
    own_ref,
    weight_0,
    weight_a,
    weight_b,
    weight_c,
    bias_ref,
    gain_ref,
    shift_ref,
    valid_ref,
    hidden_ref,
    turned_ref,
    mixed_ref,
):
    step = pl.program_id(0)
    weights = (weight_0, weight_a, weight_b, weight_c)
    forward_step(step, powers_ref, all_ref, own_ref, weights, bias_ref, turned_ref, mixed_ref)

    @pl.when(step == pl.num_programs(0) - 1)
    def finish_layer():
        normed, ignored = norm_forward(mixed_ref[...])
        hidden = (normed * gain_ref[...] + shift_ref[...]) * valid_ref[...]
        hidden_ref[...] = hidden.astype(jnp.bfloat16)


def layer_two_kernel(
    place_ref,
    powers_ref,
    all_ref,
    own_ref,
    weight_0,
    weight_a,
    weight_b,
    weight_c,
    bias_ref,
    gain_ref,
    shift_ref,
    valid_ref,
    upstream_ref,
    active_ref,
    low_ref,
    rest_ref,
    mine_ref,
    other_ref,
    turned,
    mixed,
):
    step = pl.program_id(0)
    weights = (weight_0, weight_a, weight_b, weight_c)
    forward_step(step, powers_ref, all_ref, own_ref, weights, bias_ref, turned, mixed)

    @pl.when(step == pl.num_programs(0) - 1)
    def finish_layer():
        normed, ignored = norm_forward(mixed[...])
        active = (normed * gain_ref[...] + shift_ref[...]) * valid_ref[...]
        active_ref[...] = active.astype(jnp.bfloat16)
        low, rest = norm_backward(
            mixed[...], upstream_ref[...].astype(jnp.float32), gain_ref[...], valid_ref[...]
        )
        low_ref[...] = low
        for place in range(3):
            rest_ref[place : place + 1, :] = rest[place]
        weight_gradient(turned, low, place_ref[1], mine_ref, other_ref)


def backward_step(step, powers_ref, all_ref, own_ref, weights, total):
    terms, own_cap, span = powers_ref.shape
    transposed = (((1,), (1,)), ((), ()))

    @pl.when(step == 0)
    def first():
        total[...] = lax.dot_general(
            own_ref[...], weights[0][0], transposed, preferred_element_type=jnp.float32
        )

    low = jnp.dot(
        powers_ref[...].reshape(terms * own_cap, span),
        all_ref[...],
        preferred_element_type=jnp.float32,
    ).astype(jnp.bfloat16)
    value = total[...]
    for term in range(terms):
        value = value + lax.dot_general(
            low[term * own_cap : (term + 1) * own_cap],
            weights[1 + term][0],
            transposed,
            preferred_element_type=jnp.float32,
        )
    total[...] = value


def back_two_kernel(
    place_ref,
    powers_ref,
    all_ref,
    own_ref,
    weight_0,
    weight_a,
    weight_b,
    weight_c,
    turned_ref,
    mixed_ref,
    gain_ref,
    valid_ref,
    rest_ref,
    low_ref,
    mine_ref,
    other_ref,
    total,
):
    step = pl.program_id(0)
    weights = (weight_0, weight_a, weight_b, weight_c)
    backward_step(step, powers_ref, all_ref, own_ref, weights, total)

    @pl.when(step == pl.num_programs(0) - 1)
    def finish_layer():
        low, rest = norm_backward(mixed_ref[...], total[...], gain_ref[...], valid_ref[...])
        low_ref[...] = low
        weight_gradient(turned_ref, low, place_ref[1], mine_ref, other_ref)
        part = turned_ref.shape[0] // 4
        extra = jnp.zeros((2, mine_ref.shape[1] - part, mine_ref.shape[2]), jnp.bfloat16)
        rows = rest + [rest_ref[place : place + 1, :] for place in range(3)]
        rows = jnp.concatenate(rows + [jnp.zeros((10, rows[0].shape[1]), jnp.float32)], axis=0)

        def below(first_ref, second_ref):
            first_ref[:, part:, :] = extra
            second_ref[:, part:, :] = extra
            first_ref[0, part : part + 16, :] = rows.astype(jnp.bfloat16)

        @pl.when(place_ref[1] == 0)
        def low_half_here():
            below(mine_ref, other_ref)

        @pl.when(place_ref[1] == 1)
        def low_half_there():
            below(other_ref, mine_ref)


def back_one_kernel(
    powers_ref, all_ref, own_ref, weight_0, weight_a, weight_b, weight_c, out_ref, total
):
    step = pl.program_id(0)
    weights = (weight_0, weight_a, weight_b, weight_c)
    backward_step(step, powers_ref, all_ref, own_ref, weights, total)

    @pl.when(step == pl.num_programs(0) - 1)
    def finish_layer():
        out_ref[...] = total[...].astype(jnp.bfloat16)


def layer_pass(kernel, name, place, powers, everyone, own, weight, others, outs, scratch):
    ignored, own_cap, span = powers.shape
    fan_in, width = weight.shape[1:]

    def whole(value):
        return pl.BlockSpec(value.shape, lambda step: (0,) * len(value.shape))

    def term_weight(term):
        return pl.BlockSpec((1, fan_in, width), lambda step: (1 + step * TERMS + term, 0, 0))

    in_specs = [
        pl.BlockSpec((TERMS, own_cap, span), lambda step: (step, 0, 0)),
        whole(everyone),
        whole(own),
        pl.BlockSpec((1, fan_in, width), lambda step: (0, 0, 0)),
    ]
    in_specs += [term_weight(term) for term in range(TERMS)] + [whole(value) for value in others]
    operands = [powers, everyone, own] + [weight] * (1 + TERMS) + list(others)
    if place is not None:
        in_specs = [pl.BlockSpec(memory_space=pltpu.SMEM)] + in_specs
        operands = [place] + operands
    return pl.pallas_call(
        kernel,
        grid=((ORDER - 1) // TERMS,),
        out_shape=outs,
        in_specs=in_specs,
        out_specs=[whole(value) for value in outs],
        scratch_shapes=[pltpu.VMEM(shape, dtype) for shape, dtype in scratch],
        compiler_params=pltpu.CompilerParams(vmem_limit_bytes=VMEM_BYTES),
        cost_estimate=NO_COST,
        name=name,
    )(*operands)


def finish_kernel(scalars_ref, pair_ref, siblings_ref, other_ref, out_ref, *small_refs):
    step = pl.program_id(0)
    part = out_ref.shape[1]
    for here, values_ref in ((step < 2, pair_ref), (step >= 2, siblings_ref)):
        @pl.when(here & (scalars_ref[0] == 1))
        def fast_form():
            out_ref[0] = values_ref[0, :part, :].astype(jnp.float32)

        for small_ref in small_refs:
            @pl.when(here & (scalars_ref[1 + step] == 0))
            def small_sums():
                small_ref[...] = values_ref[0, part : part + 16, :].astype(jnp.float32)

    @pl.when(scalars_ref[0] == 0)
    def general_form():
        out_ref[0] = other_ref[0].astype(jnp.float32)


def finished(scalars, pair, siblings, other, with_small=False):
    count, part, width = other.shape
    out, held = (1, part, width), (1,) + pair.shape[1:]
    out_specs = [pl.BlockSpec(out, lambda step, ref: (ref[1 + step], 0, 0))]
    out_shape = [jax.ShapeDtypeStruct(other.shape, jnp.float32)]
    if with_small:
        out_specs.append(pl.BlockSpec((16, width), lambda step, ref: (0, 0)))
        out_shape.append(jax.ShapeDtypeStruct((16, width), jnp.float32))
    return pl.pallas_call(
        finish_kernel,
        grid_spec=pltpu.PrefetchScalarGridSpec(
            num_scalar_prefetch=1,
            grid=(count,),
            in_specs=[
                pl.BlockSpec(held, lambda step, ref: (jnp.minimum(step, 1), 0, 0)),
                pl.BlockSpec(held, lambda step, ref: (jnp.maximum(step - 2, 0), 0, 0)),
                pl.BlockSpec(out, lambda step, ref: ((1 - ref[0]) * ref[1 + step], 0, 0)),
            ],
            out_specs=out_specs,
        ),
        out_shape=out_shape,
        compiler_params=pltpu.CompilerParams(vmem_limit_bytes=VMEM_BYTES),
        cost_estimate=pl.CostEstimate(
            flops=other.size, bytes_accessed=6 * other.size, transcendentals=0
        ),
        name="finished",
    )(scalars, pair, siblings, other)


def unpack_kernel(place_ref, pieces_ref, keys_ref, own_ref, quadrant_ref, columns, hot):
    groups, high, lanes = pieces_ref.shape
    own_cap, span = own_ref.shape
    whole = own_cap // lanes
    send_cap = keys_ref.shape[1] // groups
    half, rest = send_cap // 2, own_cap - whole * lanes
    for group in range(groups):
        start = group * send_cap
        for tile in range(whole):
            columns[start : start + send_cap, tile * lanes : (tile + 1) * lanes] = pieces_ref[
                group, tile * send_cap : (tile + 1) * send_cap, :
            ]
        ends = pieces_ref[group, whole * send_cap :, :]
        columns[start : start + half, whole * lanes :] = ends[:, :rest]
        columns[start + half : start + send_cap, whole * lanes :] = ends[:, rest:]
    standing = lax.broadcasted_iota(jnp.int32, hot.shape, 0)
    hot[...] = jnp.where(standing == keys_ref[...], 1.0, 0.0).astype(jnp.bfloat16)
    block = jnp.dot(hot[...], columns[...], preferred_element_type=jnp.float32)
    own_ref[...] = block.T.astype(jnp.bfloat16)
    middle = span // 2

    @pl.when(place_ref[0] == 0)
    def first():
        quadrant_ref[...] = own_ref[:, :middle]

    @pl.when(place_ref[0] == 1)
    def second():
        quadrant_ref[...] = own_ref[:, middle:]


def unpacked_block(pieces, keys, place, own_cap, span):
    vector = pl.BlockSpec(memory_space=pltpu.VMEM)
    return pl.pallas_call(
        unpack_kernel,
        out_shape=[
            jax.ShapeDtypeStruct((own_cap, span), jnp.bfloat16),
            jax.ShapeDtypeStruct((own_cap, span // 2), jnp.bfloat16),
        ],
        in_specs=[pl.BlockSpec(memory_space=pltpu.SMEM), vector, vector],
        out_specs=[vector, vector],
        scratch_shapes=[
            pltpu.VMEM((keys.shape[1], own_cap), jnp.bfloat16),
            pltpu.VMEM((span, keys.shape[1]), jnp.bfloat16),
        ],
        compiler_params=pltpu.CompilerParams(vmem_limit_bytes=VMEM_BYTES),
        cost_estimate=NO_COST,
        name="unpacked_block",
    )(place, pieces, keys)


def fit_kernel(codes_ref, out_ref, *, n_row, caps):
    own_cap, send_cap, seat_cap = caps
    codes = codes_ref[...]
    devices = codes.shape[0]
    n_col = devices // n_row
    label = lax.broadcasted_iota(jnp.int32, (devices, 128), 1)
    counts = jnp.zeros((devices, 128), jnp.float32)
    for cluster in range(CLUSTERS):
        here = jnp.where(codes == 2 * cluster + 1, 1.0, 0.0)
        counts = counts + jnp.where(
            label == cluster, jnp.sum(here, axis=1, keepdims=True), 0.0
        )
    sizes = jnp.sum(counts, axis=0, keepdims=True)
    across = jnp.broadcast_to(sizes, (128, 128))
    down = across.T
    first = lax.broadcasted_iota(jnp.int32, (128, 128), 0)
    second = lax.broadcasted_iota(jnp.int32, (128, 128), 1)
    ahead = (across > down) | ((across == down) & (second < first))
    ahead = ahead & (second < CLUSTERS)
    rank = jnp.sum(jnp.where(ahead, 1.0, 0.0), axis=1, keepdims=True).astype(jnp.int32)
    others = n_row - 1
    later = rank > others
    turn = jnp.zeros_like(rank)
    for count in range(1, CLUSTERS // others + 1):
        turn = turn + jnp.where(rank - 1 >= count * others, 1, 0)
    place = rank - 1 - turn * others
    group = jnp.where(rank == 0, 0, 1 + jnp.where(later, others - 1 - place, place))
    member = (group == second) & (first < CLUSTERS)
    held = jnp.dot(
        counts.astype(jnp.bfloat16),
        jnp.where(member, 1.0, 0.0).astype(jnp.bfloat16),
        preferred_element_type=jnp.float32,
    )
    by_row = jnp.zeros((1, 128), jnp.float32)
    for row in range(n_row):
        rows = jnp.sum(held[row * n_col : (row + 1) * n_col], axis=0, keepdims=True)
        by_row = jnp.maximum(by_row, rows)
    device = lax.broadcasted_iota(jnp.int32, (devices, 128), 0)
    by_col = jnp.zeros((1, 128), jnp.float32)
    for col in range(n_col):
        cols = jnp.where(device % n_col == col, held, 0.0)
        by_col = jnp.maximum(by_col, jnp.sum(cols, axis=0, keepdims=True))
    fits = (
        (jnp.max(by_col) <= own_cap) & (jnp.max(by_row) <= send_cap) & (jnp.max(held) <= seat_cap)
    )
    out_ref[0] = jnp.where(fits, 1, 0)


def fits_in(codes, n_row, caps):
    fits = pl.pallas_call(
        functools.partial(fit_kernel, n_row=n_row, caps=caps),
        out_shape=jax.ShapeDtypeStruct((1,), jnp.int32),
        in_specs=[pl.BlockSpec(memory_space=pltpu.VMEM)],
        out_specs=pl.BlockSpec(memory_space=pltpu.SMEM),
        cost_estimate=NO_COST,
        name="fits",
    )(codes.reshape(-1, codes.shape[-1]))
    return fits


def exclusive_counts(member):
    count = member.shape[-1]
    before = jnp.arange(count)[:, None] < jnp.arange(count)[None, :]
    return jnp.dot(
        member.astype(jnp.bfloat16),
        before.astype(jnp.bfloat16),
        preferred_element_type=jnp.float32,
    ).astype(jnp.int32)


def assign(codes, n_row):
    cluster, valid = codes >> 1, codes & 1
    labels = jnp.arange(CLUSTERS)
    sizes = jnp.sum(
        (cluster.reshape(1, -1) == labels[:, None]) & (valid.reshape(1, -1) == 1), axis=1
    )
    ahead = (sizes[None, :] > sizes[:, None]) | (
        (sizes[None, :] == sizes[:, None]) & (labels[None, :] < labels[:, None])
    )
    rank = jnp.sum(ahead, axis=1)
    others = n_row - 1
    turn, place = (rank - 1) // others, (rank - 1) % others
    group = jnp.where(rank == 0, 0, 1 + jnp.where(turn == 0, place, others - 1 - place))
    of_node = jnp.sum(
        jnp.where(cluster[None] == labels[:, None, None, None], group[:, None, None, None], 0),
        axis=0,
    )
    return jnp.where(valid == 1, of_node, n_row)


def compact(
    codes,
    group,
    features,
    block_keep,
    edge_weight,
    weight_one,
    bias_one,
    gain_one,
    shift_one,
    weight_two,
    bias_two,
    gain_two,
    shift_two,
    cotangent,
    places_of,
    slots_of,
    seats_of,
    decide,
    sizes,
    caps,
):
    row, col = lax.axis_index("row"), lax.axis_index(COL)
    chip, core = lax.axis_index("chip"), lax.axis_index("core")
    n_row, n_col = sizes
    own_cap, send_cap, seat_cap = caps
    own_nodes, in_width = features.shape
    width = weight_two.shape[2]
    span = n_col * own_cap
    targets = jnp.arange(n_row)

    def in_col(value):
        return lax.dynamic_index_in_dim(value, col, 1, False).reshape(-1)

    def in_row(value):
        return lax.dynamic_index_in_dim(value, row, 0, False).reshape(-1)

    row_group, col_group = in_row(group), in_col(group)
    row_slots, col_places = in_row(slots_of(group)), in_col(places_of(group))
    row_keys = jnp.where(row_slots < send_cap, row_group * send_cap + row_slots, -1)
    col_keys = jnp.where(col_places < own_cap, col_group * own_cap + col_places, -1)
    pieces = packed_pieces(
        block_keep,
        in_row(codes),
        in_col(codes),
        row_keys,
        col_keys,
        edge_weight,
        (own_cap, send_cap),
        n_row,
    )
    pieces, codes = lax.optimization_barrier((pieces, codes))
    group = assign(codes, n_row)
    places, slots, seats = places_of(group), slots_of(group), seats_of(group)

    standing = jnp.arange(n_col)[None, :, None] * own_cap + places
    fits_here = jnp.where(group == row, standing, -1).reshape(n_row, -1)
    slot_of = slots.reshape(n_row, -1)
    target = jnp.max(
        jnp.where(
            slot_of[:, None, :] == jnp.arange(send_cap)[None, :, None], fits_here[:, None, :], -1
        ),
        axis=2,
    )
    keys = target.reshape(1, -1)

    def to_partner(value, step):
        return lax.ppermute(value, "row", [(place, place ^ step) for place in range(n_row)])

    partners = row ^ targets
    group_here = lax.dynamic_index_in_dim(in_row(group).reshape(n_col, -1), col, 0, False)
    seat_here = lax.dynamic_index_in_dim(in_row(seats).reshape(n_col, -1), col, 0, False)

    def seat_of_node(groups):
        hot = (group_here[None, None, :] == groups[:, None, None]) & (
            seat_here[None, None, :] == jnp.arange(seat_cap)[None, :, None]
        )
        return hot.astype(jnp.bfloat16).reshape(n_row * seat_cap, own_nodes)

    enter_home = seat_of_node(targets).T
    enter_partner = seat_of_node(partners)
    both = jnp.dot(enter_partner, jnp.concatenate([features, cotangent], axis=1))
    both = both.reshape(n_row, seat_cap, -1)
    enter_partner = enter_partner.T
    pieces = trade(pieces, "row")
    both, codes = lax.optimization_barrier((both, codes))
    fits, others = decide(codes)
    group_col = lax.dynamic_index_in_dim(group, col, 1, False)
    seats_col = lax.dynamic_index_in_dim(seats, col, 1, False)
    places_col = lax.dynamic_index_in_dim(places, col, 1, False)
    seated = (group_col == row)[:, None, :] & (
        seats_col[:, None, :] == jnp.arange(seat_cap)[None, :, None]
    )
    place_of_seat = jnp.max(jnp.where(seated, places_col[:, None, :], -1), axis=2)
    from_partner = jnp.max(
        jnp.where((partners[:, None] == targets)[:, :, None], place_of_seat[None], -1), axis=1
    )
    arrive = from_partner.reshape(1, -1) == jnp.arange(own_cap)[:, None]
    arrive = arrive.astype(jnp.bfloat16)
    leave_group = place_of_seat.reshape(-1, 1) == jnp.arange(own_cap)
    leave_group = leave_group.astype(jnp.bfloat16)
    leave_partner = jnp.concatenate([from_partner[::2], from_partner[1::2]])
    leave_partner = leave_partner.reshape(-1, 1) == jnp.arange(own_cap)
    leave_partner = leave_partner.astype(jnp.bfloat16)
    held_count = jnp.sum(group_col == row)
    valid_rows = (jnp.arange(own_cap) < held_count).astype(jnp.float32)[:, None]
    place = jnp.stack([chip, core]).astype(jnp.int32)
    quarters = jnp.stack([col, (1 - chip) * 2 + core, chip * 2 + 1 - core, 3 - col])
    quarters = jnp.concatenate([fits, quarters.astype(jnp.int32)])
    scalars = (chip, 1 - chip, col * own_cap)
    scalars = tuple(value.astype(jnp.uint32) for value in scalars) + (chip == 0, core == 0, place, quarters)
    homes = enter_home, enter_partner, leave_group, leave_partner
    pieces, both, keys, arrive, homes, valid_rows, others, scalars = lax.optimization_barrier(
        (pieces, both, keys, arrive, homes, valid_rows, others, scalars)
    )
    enter_home, enter_partner, leave_group, leave_partner = homes
    this_chip, other_chip, own_start, first_chip, first_core, place, quarters = scalars

    own_block, quadrant = unpacked_block(pieces, keys, place, own_cap, span)
    quadrant = swap(quadrant, "chip")
    both = [both[0]] + [to_partner(both[step], step) for step in range(1, n_row)]
    sibling = swap(own_block, "core")
    quadrant, *early = lax.optimization_barrier((quadrant, *both[:-2]))
    adjacency = normalized_block(own_block, sibling, quadrant, swap(quadrant, "core"), place)
    adjacency, *late = lax.optimization_barrier((adjacency, *both[-2:]))
    both = early + late
    mine = jnp.dot(arrive, jnp.concatenate(both))
    features_own, cotangent_own = mine[:, :in_width], mine[:, in_width:]
    sibling = swap(features_own, "core")

    first = (own_start + jnp.arange(own_cap, dtype=jnp.uint32))[:, None]
    first = first == jnp.arange(span, dtype=jnp.uint32)[None, :]
    previous = first.astype(jnp.float32)
    current = -lax.dynamic_slice_in_dim(adjacency, own_start, own_cap, 0).astype(jnp.float32)
    lowered = [current.astype(jnp.bfloat16)]
    for position in range(2, ORDER):
        upcoming = (
            -2.0 * jnp.dot(lowered[-1], adjacency, preferred_element_type=jnp.float32) - previous
        )
        low = upcoming.astype(jnp.bfloat16)
        if position == 4:
            low, sibling = lax.optimization_barrier((low, sibling))
            features_chip = joined(features_own, sibling, first_core)
            partner = swap(features_chip, "chip")
        if position == 8:
            low, partner = lax.optimization_barrier((low, partner))
            features_all = joined(features_chip, partner, first_chip)
        previous, current = current, upcoming
        lowered.append(low)
    powers = jnp.concatenate(lowered, axis=0).reshape(ORDER - 1, own_cap, span)

    def everywhere(value_low):
        return lax.all_gather(value_low, COL, axis=0, tiled=True)

    def chosen(value, other):
        return jnp.where(quarters[0] == 1, value.astype(jnp.float32), other.astype(jnp.float32))

    def shaped(*shape, dtype=jnp.bfloat16):
        return jax.ShapeDtypeStruct(shape, dtype)

    part_one, part_two = ORDER * in_width // n_col, ORDER * width // n_col
    padded = -(-(part_one + 16) // (8 * n_row)) * (8 * n_row)
    hidden, turned_one, mixed_one = layer_pass(
        layer_one_kernel,
        "layer_one",
        None,
        powers,
        features_all,
        features_own,
        weight_one,
        [bias_one[None], gain_one[None], shift_one[None], valid_rows],
        [
            shaped(own_cap, width),
            shaped(n_col * part_one, own_cap),
            shaped(own_cap, width, dtype=jnp.float32),
        ],
        [],
    )
    activations, low_two, rest_two, mine, other = layer_pass(
        layer_two_kernel,
        "layer_two",
        place,
        powers,
        everywhere(hidden),
        hidden,
        weight_two,
        [bias_two[None], gain_two[None], shift_two[None], valid_rows, cotangent_own],
        [
            shaped(own_cap, width),
            shaped(own_cap, width),
            shaped(3, width, dtype=jnp.float32),
            shaped(2, part_two, width),
            shaped(2, part_two, width),
        ],
        [((n_col * part_two, own_cap), jnp.bfloat16), ((own_cap, width), jnp.float32)],
    )

    def add_cores(mine, other):
        got = swap(other, "core")
        return tuple(
            added(
                lax.dynamic_index_in_dim(mine, index, 0, False),
                lax.dynamic_index_in_dim(got, index, 0, False),
            )
            for index in (this_chip, other_chip)
        )

    leaving = jnp.dot(leave_partner, activations).reshape(n_row, seat_cap, width)
    near, far = leaving[: n_row // 2], leaving[n_row // 2 :]
    far = to_partner(far, 1)
    here, there = add_cores(mine, other)
    everyone_two, there, far = lax.optimization_barrier((everywhere(low_two), there, far))
    there = swap(there, "chip")
    arrived = [jnp.stack([near[0], far[0]])] + [
        to_partner(jnp.stack([near[half], far[half]]), 2 * half) for half in range(1, n_row // 2)
    ]
    low_one, mine, other = layer_pass(
        back_two_kernel,
        "back_two",
        place,
        powers,
        everyone_two,
        low_two,
        weight_two,
        [turned_one, mixed_one, gain_one[None], valid_rows, rest_two],
        [shaped(own_cap, width), shaped(2, padded, width), shaped(2, padded, width)],
        [((own_cap, width), jnp.float32)],
    )
    low_one, there, arrived = lax.optimization_barrier((low_one, there, arrived))
    second = added(here, there).reshape(n_row, -1, width)
    many = second.shape[1]
    low_one, second = lax.optimization_barrier((low_one, second))
    second = trade(second, "row")
    here, there = add_cores(mine, other)
    there = swap(there, "chip")
    first = added(here, there).reshape(n_row, -1, width)
    share = first.shape[1]
    second = jnp.sum(second.astype(jnp.float32), axis=0).astype(jnp.bfloat16)
    second = jnp.broadcast_to(second[None], (n_row,) + second.shape)
    mixed = jnp.concatenate([second, first], axis=1)
    low_one, mixed = lax.optimization_barrier((low_one, mixed))
    everyone_one = everywhere(low_one)
    mixed = trade(mixed, "row")
    (input_grad,) = layer_pass(
        back_one_kernel,
        "back_one",
        None,
        powers,
        everyone_one,
        low_one,
        weight_one,
        [],
        [shaped(own_cap, in_width)],
        [((own_cap, in_width), jnp.float32)],
    )
    leaving = jnp.dot(leave_group, input_grad)
    leaving = leaving.reshape(n_row, seat_cap * in_width // width, width)
    arrived = jnp.concatenate(arrived).reshape(-1, width)
    home = jnp.dot(enter_partner, arrived, preferred_element_type=jnp.float32)
    home = chosen(home, others[0])
    mixed, leaving, home = lax.optimization_barrier((mixed, leaving, home))
    first = jnp.sum(mixed[:, many:].astype(jnp.float32), axis=0).astype(jnp.bfloat16)
    first = jnp.broadcast_to(first[None], (n_row,) + first.shape)
    second = mixed[:, :many].reshape(1, -1, width)
    partner_two = swap(second, "chip")
    first = trade(jnp.concatenate([first, leaving], axis=1), "row")
    first, partner_two = lax.optimization_barrier((first, partner_two))
    mine = first[:, :share].reshape(1, -1, width)
    partner = swap(mine, "chip")
    second = jnp.concatenate([second, partner_two])
    (second,) = finished(quarters, second, swap(second, "core"), others[3])
    back = first[:, share:].reshape(n_row * seat_cap, in_width)
    home_grad = jnp.dot(enter_home, back, preferred_element_type=jnp.float32)
    home_grad = chosen(home_grad, others[1])
    partner, second, home_grad = lax.optimization_barrier((partner, second, home_grad))
    pair = jnp.concatenate([mine, partner])
    siblings = swap(pair, "core")
    first, small = finished(quarters, pair, siblings, others[2], True)
    return home, home_grad, first, second, chosen(small[:6], others[4])


def general(
    codes,
    features,
    block_keep,
    edge_weight,
    weight_one,
    bias_one,
    gain_one,
    shift_one,
    weight_two,
    bias_two,
    gain_two,
    shift_two,
    cotangent,
    node_valid,
):
    row, col = lax.axis_index("row"), lax.axis_index(COL)
    row_codes = lax.dynamic_index_in_dim(codes, row, 0, False).reshape(-1)
    col_codes = lax.dynamic_index_in_dim(codes, col, 1, False).reshape(-1)
    tile_rows, tile_cols = edge_weight.shape
    blocks_down, blocks_across = block_keep.shape
    block_side = tile_rows // blocks_down
    linked = (row_codes[:, None] == col_codes[None, :]) & (row_codes[:, None] & 1 == 1)
    linked = linked.reshape(blocks_down, block_side, blocks_across, block_side) & (
        block_keep[:, None, :, None] == 1
    )
    masked = edge_weight * linked.reshape(tile_rows, tile_cols).astype(jnp.bfloat16)
    degree_rows = 1.0 + lax.psum(jnp.sum(masked, axis=1, dtype=jnp.float32), COL)
    own_nodes = features.shape[0]
    own_degree = lax.dynamic_slice_in_dim(
        degree_rows, lax.axis_index(COL) * own_nodes, own_nodes, 0
    )
    degree_cols = lax.all_gather(own_degree, "row", axis=0, tiled=True)
    adjacency = (
        masked.astype(jnp.float32)
        * lax.rsqrt(degree_rows)[:, None]
        * lax.rsqrt(degree_cols)[None, :]
    ).astype(jnp.bfloat16)
    valid_rows = node_valid.astype(jnp.float32)
    stacked_one, mixed_one, hidden = layer_forward(
        adjacency,
        features.astype(jnp.float32),
        weight_one,
        bias_one,
        gain_one,
        shift_one,
        valid_rows,
    )
    stacked_two, mixed_two, activations = layer_forward(
        adjacency, hidden, weight_two, bias_two, gain_two, shift_two, valid_rows
    )
    hidden_grad, weight_two_grad, bias_two_grad, gain_two_grad, shift_two_grad = layer_backward(
        adjacency,
        stacked_two,
        mixed_two,
        cotangent.astype(jnp.float32),
        weight_two,
        gain_two,
        shift_two,
        valid_rows,
    )
    input_grad, weight_one_grad, bias_one_grad, gain_one_grad, shift_one_grad = layer_backward(
        adjacency, stacked_one, mixed_one, hidden_grad, weight_one, gain_one, shift_one, valid_rows
    )
    summed = lax.psum(
        (
            weight_one_grad,
            bias_one_grad,
            gain_one_grad,
            shift_one_grad,
            weight_two_grad,
            bias_two_grad,
            gain_two_grad,
            shift_two_grad,
        ),
        ("row",) + COL,
    )
    weight_one_grad, bias_one_grad, gain_one_grad, shift_one_grad = (
        summed[0],
        summed[1],
        summed[2],
        summed[3],
    )
    weight_two_grad, bias_two_grad, gain_two_grad, shift_two_grad = (
        summed[4],
        summed[5],
        summed[6],
        summed[7],
    )
    return (
        activations,
        input_grad,
        weight_one_grad,
        bias_one_grad,
        gain_one_grad,
        shift_one_grad,
        weight_two_grad,
        bias_two_grad,
        gain_two_grad,
        shift_two_grad,
    )


def local(n_row, n_col, *args):
    (
        features,
        node_valid,
        cluster,
        block_keep,
        edge_weight,
        weight_one,
        bias_one,
        gain_one,
        shift_one,
        weight_two,
        bias_two,
        gain_two,
        shift_two,
        cotangent,
    ) = args
    own_nodes, in_width = features.shape
    own_cap = own_nodes * n_row * 5 // 16
    send_cap = own_nodes * n_col * 11 // 32
    seat_cap = own_nodes * 7 // 16
    codes = broadcast_along(cluster * 2 + node_valid, ("row",) + COL, n_row * n_col)
    codes = codes.reshape(n_row, n_col, own_nodes)
    shared = (
        block_keep,
        edge_weight,
        weight_one,
        bias_one,
        gain_one,
        shift_one,
        weight_two,
        bias_two,
        gain_two,
        shift_two,
        cotangent,
    )

    def slow():
        return general(codes, features, *shared, node_valid)

    held = (ORDER - 1) * own_cap * own_cap * n_col * 2
    if held > HELD_BYTES or n_col != 4 or n_row < 2 or n_row & (n_row - 1):
        return slow()
    group = assign(codes, n_row)

    def member_of(group):
        return group[None] == jnp.arange(n_row)[:, None, None, None]

    def places_of(group):
        member = member_of(group).transpose(0, 2, 1, 3).reshape(n_row, n_col, -1)
        places = jnp.sum(jnp.where(member, exclusive_counts(member), 0), axis=0)
        return places.reshape(n_col, n_row, own_nodes).transpose(1, 0, 2)

    def slots_of(group):
        member = member_of(group).reshape(n_row, n_row, -1)
        slots = jnp.sum(jnp.where(member, exclusive_counts(member), 0), axis=0)
        return slots.reshape(n_row, n_col, own_nodes)

    def seats_of(group):
        member = member_of(group)
        return jnp.sum(jnp.where(member, exclusive_counts(member), 0), axis=0)

    width = weight_two.shape[2]

    def instead(state):
        made = slow()
        small = jnp.stack([made[place] for place in (3, 4, 5, 7, 8, 9)])
        return (jnp.ones_like(state[0]),) + tuple(
            value.astype(jnp.bfloat16).reshape(like.shape)
            for value, like in zip((made[0], made[1], made[2], made[6], small), state[1:])
        )

    shapes = (
        (own_nodes, width),
        (own_nodes, in_width),
        (n_col, ORDER * in_width // n_col, width),
        (n_col, ORDER * width // n_col, width),
        (6, width),
    )

    def decide(codes):
        fits = fits_in(codes, n_row, (own_cap, send_cap, seat_cap))
        others = lax.while_loop(
            lambda state: state[0][0] == 0,
            instead,
            (fits,) + tuple(jnp.zeros(shape, jnp.bfloat16) for shape in shapes),
        )[1:]
        return fits, others

    home, home_grad, first, second, small = compact(
        codes,
        group,
        features,
        *shared,
        places_of,
        slots_of,
        seats_of,
        decide,
        (n_row, n_col),
        (own_cap, send_cap, seat_cap),
    )
    return (
        home,
        home_grad,
        first.reshape(weight_one.shape),
        small[0],
        small[1],
        small[2],
        second.reshape(weight_two.shape),
        small[3],
        small[4],
        small[5],
    )


def solution(mesh):
    n_row, n_col = mesh.shape["row"], mesh.shape["col"]
    by_core = jax.sharding.Mesh(
        mesh.devices.reshape(n_row, n_col // 2, 2), ("row", "chip", "core")
    )
    nodes = ("row", "chip", "core")
    placed = (
        P(nodes, None),
        P(nodes),
        P(nodes),
        P("row", COL),
        P("row", COL),
        P(),
        P(),
        P(),
        P(),
        P(),
        P(),
        P(),
        P(),
        P(nodes, None),
    )
    return jax.shard_map(
        functools.partial(local, n_row, n_col),
        mesh=by_core,
        in_specs=placed,
        out_specs=(P(nodes, None), P(nodes, None), P(), P(), P(), P(), P(), P(), P(), P()),
        check_vma=False,
    )
```

```python
import functools
import math

import jax
import jax.numpy as jnp
from jax import lax
from jax.experimental import pallas as pl
from jax.experimental.pallas import tpu as pltpu
from jax.sharding import PartitionSpec as P

ORDER = 13
CLUSTERS = 16
HELD_BYTES = 1 << 25
VMEM_BYTES = 32 << 20
TERMS = 3
NO_COST = pl.CostEstimate(flops=1, bytes_accessed=1, transcendentals=0)
COL = ("chip", "core")


def finish(mixed, gain, shift, valid_rows):
    active = jax.nn.gelu(mixed, approximate=False)
    centered = active - jnp.mean(active, axis=-1, keepdims=True)
    variance = jnp.mean(centered * centered, axis=-1, keepdims=True)
    return (centered * lax.rsqrt(variance + 1e-05) * gain + shift) * valid_rows[:, None]


def forward_product(adjacency, piece_low):
    partial_value = jnp.dot(
        adjacency,
        lax.all_gather(piece_low, "row", axis=0, tiled=True),
        preferred_element_type=jnp.float32,
    )
    return lax.psum_scatter(partial_value, COL, scatter_dimension=0, tiled=True)


def backward_product(adjacency, piece_low):
    partial_value = lax.dot_general(
        adjacency,
        lax.all_gather(piece_low, COL, axis=0, tiled=True),
        (((0,), (0,)), ((), ())),
        preferred_element_type=jnp.float32,
    )
    return lax.psum_scatter(
        partial_value.astype(jnp.bfloat16), "row", scatter_dimension=0, tiled=True
    ).astype(jnp.float32)


def layer_forward(adjacency, inputs, weight, bias, gain, shift, valid_rows):
    first_low = inputs.astype(jnp.bfloat16)
    second = -forward_product(adjacency, first_low)
    second_low = second.astype(jnp.bfloat16)

    def advance(state_pair, unused):
        previous, current, current_low = state_pair
        upcoming = -2.0 * forward_product(adjacency, current_low) - previous
        upcoming_low = upcoming.astype(jnp.bfloat16)
        return ((current, upcoming, upcoming_low), upcoming_low)

    ignored, others = lax.scan(advance, (inputs, second, second_low), None, length=ORDER - 2)
    stacked = jnp.concatenate([first_low[None], second_low[None], others], axis=0)
    mixed = jnp.einsum("kni,kio->no", stacked, weight, preferred_element_type=jnp.float32) + bias
    return (stacked, mixed, finish(mixed, gain, shift, valid_rows))


def layer_backward(adjacency, stacked, mixed, upstream, weight, gain, shift, valid_rows):

    def local_finish(mixed_in, gain_in, shift_in):
        return finish(mixed_in, gain_in, shift_in, valid_rows)

    ignored, pullback = jax.vjp(local_finish, mixed, gain, shift)
    mixed_grad, gain_grad, shift_grad = pullback(upstream)
    mixed_low = mixed_grad.astype(jnp.bfloat16)
    bias_grad = jnp.sum(mixed_low.astype(jnp.float32), axis=0)
    weight_grad = jnp.einsum("kni,no->kio", stacked, mixed_low, preferred_element_type=jnp.float32)
    direct = jnp.einsum("no,kio->kni", mixed_low, weight, preferred_element_type=jnp.float32)

    def retreat(state_pair, direct_term):
        later_two, later_one = state_pair
        current = (
            direct_term
            - 2.0 * backward_product(adjacency, later_one.astype(jnp.bfloat16))
            - later_two
        )
        return ((later_one, current), None)

    start_pair = (jnp.zeros_like(direct[0]), direct[ORDER - 1])
    (second_grad, first_grad), unused = lax.scan(
        retreat, start_pair, direct[1 : ORDER - 1], reverse=True
    )
    input_grad = (
        direct[0] - backward_product(adjacency, first_grad.astype(jnp.bfloat16)) - second_grad
    )
    return (input_grad, weight_grad, bias_grad, gain_grad, shift_grad)


def swap(value, axis):
    return lax.ppermute(value, axis, [(0, 1), (1, 0)])


def trade(pieces, axis):
    return lax.all_to_all(pieces, axis, 0, 0, tiled=False)


def broadcast_along(value, axis, size):
    return trade(jnp.broadcast_to(value[None], (size,) + value.shape), axis)


def joined(mine, other, mine_first):
    return jnp.where(
        mine_first, jnp.concatenate([mine, other]), jnp.concatenate([other, mine])
    )


def added(mine, received):
    return (mine.astype(jnp.float32) + received.astype(jnp.float32)).astype(jnp.bfloat16)


def assemble(place_ref, own_ref, sibling_ref, near_ref, far_ref, out_ref, done):
    chip, core = place_ref[0], place_ref[1]
    own_cap, span = own_ref.shape
    half = span // 2

    def rows(of_chip, of_core):
        return pl.ds(pl.multiple_of((2 * of_chip + of_core) * own_cap, own_cap), own_cap)

    def fetch(source, of_chip, of_core, columns, place):
        target = out_ref.at[rows(of_chip, of_core), columns]
        return pltpu.make_async_copy(source, target, done.at[place])

    def quadrant_copies(here):
        there = 1 - here
        columns = pl.ds(there * half, half)
        return (
            fetch(near_ref, there, core, columns, 2),
            fetch(far_ref, there, 1 - core, columns, 3),
        )

    everything = pl.ds(0, span)
    top = (
        fetch(own_ref, chip, core, everything, 0),
        fetch(sibling_ref, chip, 1 - core, everything, 1),
    )

    def of_chip(here):
        there = 1 - here
        copies = top + quadrant_copies(here)
        for copy in copies:
            copy.start()
        for copy in copies:
            copy.wait()
        here_rows = pl.ds(here * half, half)
        for tile in range(half // 128):
            columns = pl.ds(there * half + tile * 128, 128)
            strip = out_ref[here_rows, columns]
            turned = jnp.transpose(strip.astype(jnp.float32)).astype(jnp.bfloat16)
            out_ref[columns, here_rows] = turned

    @pl.when(chip == 0)
    def first():
        of_chip(0)

    @pl.when(chip == 1)
    def second():
        of_chip(1)

    across = jnp.ones((1, span), jnp.float32)
    for tile in range(span // 128):
        across = across + jnp.sum(
            out_ref[pl.ds(tile * 128, 128), :].astype(jnp.float32), axis=0, keepdims=True
        )
    across = lax.rsqrt(across)
    for tile in range(span // 128):
        strip = out_ref[pl.ds(tile * 128, 128), :].astype(jnp.float32)
        down = lax.rsqrt(1.0 + jnp.sum(strip, axis=1, keepdims=True))
        out_ref[pl.ds(tile * 128, 128), :] = (strip * down * across).astype(jnp.bfloat16)


def normalized_block(own, sibling, near, far, place):
    span = own.shape[1]
    return pl.pallas_call(
        assemble,
        out_shape=jax.ShapeDtypeStruct((span, span), jnp.bfloat16),
        in_specs=[pl.BlockSpec(memory_space=pltpu.SMEM)]
        + [pl.BlockSpec(memory_space=pltpu.HBM)] * 4,
        out_specs=pl.BlockSpec(memory_space=pltpu.VMEM),
        scratch_shapes=[pltpu.SemaphoreType.DMA((4,))],
        compiler_params=pltpu.CompilerParams(vmem_limit_bytes=VMEM_BYTES),
        cost_estimate=NO_COST,
        name="normalized_block",
    )(place, own, sibling, near, far)


def pack_kernel(
    keep_ref, row_codes_ref, col_codes_ref, row_keys_ref, col_keys_ref, weight_ref, out_ref,
    masked, picked, rows_hot, cols_hot
):
    tile_rows, tile_cols = weight_ref.shape
    blocks_down, blocks_across = keep_ref.shape
    groups, ignored, lanes = out_ref.shape
    send_cap, own_cap = rows_hot.shape[0] // groups, cols_hot.shape[0] // groups
    high, wide = tile_rows // blocks_down, tile_cols // blocks_across
    for down in range(blocks_down):
        for across in range(blocks_across):
            rows, columns = pl.ds(down * high, high), pl.ds(across * wide, wide)
            own, other = row_codes_ref[rows, :], col_codes_ref[:, columns]
            linked = (own == other) & (own % 2 == 1) & (keep_ref[down, across] == 1)
            weight = weight_ref[rows, columns].astype(jnp.float32)
            masked[rows, columns] = jnp.where(linked, weight, 0.0).astype(jnp.bfloat16)

    def one_hot(keys, start, count):
        standing = lax.broadcasted_iota(jnp.int32, (count, keys.shape[1]), 0) + start
        return jnp.where(standing == keys, 1.0, 0.0).astype(jnp.bfloat16)

    for group in range(groups):
        rows_hot[pl.ds(group * send_cap, send_cap), :] = one_hot(
            row_keys_ref[...], group * send_cap, send_cap
        )
        cols_hot[pl.ds(group * own_cap, own_cap), :] = one_hot(
            col_keys_ref[...], group * own_cap, own_cap
        )
    for tile in range(tile_cols // 256):
        columns = pl.ds(tile * 256, 256)
        picked[:, columns] = jnp.dot(
            rows_hot[...], masked[:, columns], preferred_element_type=jnp.float32
        ).astype(jnp.bfloat16)
    whole, half = own_cap // lanes, send_cap // 2
    for group in range(groups):
        packed = lax.dot_general(
            cols_hot[pl.ds(group * own_cap, own_cap), :],
            picked[pl.ds(group * send_cap, send_cap), :],
            (((1,), (1,)), ((), ())),
            preferred_element_type=jnp.float32,
        ).T
        for tile in range(whole):
            out_ref[group, pl.ds(tile * send_cap, send_cap), :] = packed[
                :, tile * lanes : (tile + 1) * lanes
            ].astype(jnp.bfloat16)
        ends = jnp.concatenate(
            [packed[:half, whole * lanes :], packed[half:, whole * lanes :]], axis=1
        )
        out_ref[group, pl.ds(whole * send_cap, half), :] = ends.astype(jnp.bfloat16)


def packed_pieces(block_keep, row_codes, col_codes, row_keys, col_keys, edge_weight, caps, groups):
    own_cap, send_cap = caps
    tile_rows, tile_cols = edge_weight.shape
    high = own_cap // 128 * send_cap + send_cap // 2
    vector = pl.BlockSpec(memory_space=pltpu.VMEM)
    return pl.pallas_call(
        pack_kernel,
        out_shape=jax.ShapeDtypeStruct((groups, high, 128), jnp.bfloat16),
        in_specs=[pl.BlockSpec(memory_space=pltpu.SMEM)] + [vector] * 5,
        out_specs=vector,
        scratch_shapes=[
            pltpu.VMEM((tile_rows, tile_cols), jnp.bfloat16),
            pltpu.VMEM((groups * send_cap, tile_cols), jnp.bfloat16),
            pltpu.VMEM((groups * send_cap, tile_rows), jnp.bfloat16),
            pltpu.VMEM((groups * own_cap, tile_cols), jnp.bfloat16),
        ],
        compiler_params=pltpu.CompilerParams(vmem_limit_bytes=VMEM_BYTES),
        cost_estimate=NO_COST,
        name="packed_pieces",
    )(block_keep, row_codes[:, None], col_codes[None], row_keys[None], col_keys[None], edge_weight)


def normal_share(mixed):
    return 0.5 * (1.0 + lax.erf(mixed * 0.5**0.5))


def norm_forward(mixed):
    active = mixed * normal_share(mixed)
    centered = active - jnp.mean(active, axis=-1, keepdims=True)
    scale = lax.rsqrt(jnp.mean(centered * centered, axis=-1, keepdims=True) + 1e-05)
    return centered * scale, scale


def norm_backward(mixed, upstream, gain, valid):
    normed, scale = norm_forward(mixed)
    upstream = upstream * valid
    inner = upstream * gain
    inner = inner - jnp.mean(inner, axis=-1, keepdims=True) - normed * jnp.mean(
        inner * normed, axis=-1, keepdims=True
    )
    density = jnp.exp(-0.5 * mixed * mixed) * (1.0 / (2.0 * math.pi) ** 0.5)
    low = (inner * scale * (normal_share(mixed) + mixed * density)).astype(jnp.bfloat16)
    rest = [low.astype(jnp.float32), upstream * normed, upstream]
    return low, [jnp.sum(value, axis=0, keepdims=True) for value in rest]


def weight_gradient(turned_ref, low, core, mine_ref, other_ref):
    parts = mine_ref.shape[0]
    part = turned_ref.shape[0] // (2 * parts)

    def halves(first_ref, second_ref):
        for place in range(2 * parts):
            out_ref = second_ref if place % 2 else first_ref
            out_ref[place // 2, :part, :] = jnp.dot(
                turned_ref[place * part : (place + 1) * part, :],
                low,
                preferred_element_type=jnp.float32,
            ).astype(jnp.bfloat16)

    @pl.when(core == 0)
    def low_half_first():
        halves(mine_ref, other_ref)

    @pl.when(core == 1)
    def high_half_first():
        halves(other_ref, mine_ref)


def forward_step(step, powers_ref, all_ref, own_ref, weights, bias_ref, turned, mixed):
    terms, own_cap, span = powers_ref.shape
    fan_in = own_ref.shape[1]

    @pl.when(step == 0)
    def first():
        turned[:fan_in, :] = own_ref[...].T
        mixed[...] = bias_ref[...] + jnp.dot(
            own_ref[...], weights[0][0], preferred_element_type=jnp.float32
        )

    low = jnp.dot(
        powers_ref[...].reshape(terms * own_cap, span),
        all_ref[...],
        preferred_element_type=jnp.float32,
    ).astype(jnp.bfloat16)
    total = mixed[...]
    for term in range(terms):
        part = low[term * own_cap : (term + 1) * own_cap]
        start = pl.multiple_of((1 + step * terms + term) * fan_in, fan_in)
        turned[pl.ds(start, fan_in), :] = part.T
        total = total + jnp.dot(part, weights[1 + term][0], preferred_element_type=jnp.float32)
    mixed[...] = total


def layer_one_kernel(
    powers_ref,
    all_ref,
    own_ref,
    weight_0,
    weight_a,
    weight_b,
    weight_c,
    bias_ref,
    gain_ref,
    shift_ref,
    valid_ref,
    hidden_ref,
    turned_ref,
    mixed_ref,
):
    step = pl.program_id(0)
    weights = (weight_0, weight_a, weight_b, weight_c)
    forward_step(step, powers_ref, all_ref, own_ref, weights, bias_ref, turned_ref, mixed_ref)

    @pl.when(step == pl.num_programs(0) - 1)
    def finish_layer():
        normed, ignored = norm_forward(mixed_ref[...])
        hidden = (normed * gain_ref[...] + shift_ref[...]) * valid_ref[...]
        hidden_ref[...] = hidden.astype(jnp.bfloat16)


def layer_two_kernel(
    place_ref,
    powers_ref,
    all_ref,
    own_ref,
    weight_0,
    weight_a,
    weight_b,
    weight_c,
    bias_ref,
    gain_ref,
    shift_ref,
    valid_ref,
    upstream_ref,
    active_ref,
    low_ref,
    rest_ref,
    mine_ref,
    other_ref,
    turned,
    mixed,
):
    step = pl.program_id(0)
    weights = (weight_0, weight_a, weight_b, weight_c)
    forward_step(step, powers_ref, all_ref, own_ref, weights, bias_ref, turned, mixed)

    @pl.when(step == pl.num_programs(0) - 1)
    def finish_layer():
        normed, ignored = norm_forward(mixed[...])
        active = (normed * gain_ref[...] + shift_ref[...]) * valid_ref[...]
        active_ref[...] = active.astype(jnp.bfloat16)
        low, rest = norm_backward(
            mixed[...], upstream_ref[...].astype(jnp.float32), gain_ref[...], valid_ref[...]
        )
        low_ref[...] = low
        for place in range(3):
            rest_ref[place : place + 1, :] = rest[place]
        weight_gradient(turned, low, place_ref[1], mine_ref, other_ref)


def backward_step(step, powers_ref, all_ref, own_ref, weights, total):
    terms, own_cap, span = powers_ref.shape
    transposed = (((1,), (1,)), ((), ()))

    @pl.when(step == 0)
    def first():
        total[...] = lax.dot_general(
            own_ref[...], weights[0][0], transposed, preferred_element_type=jnp.float32
        )

    low = jnp.dot(
        powers_ref[...].reshape(terms * own_cap, span),
        all_ref[...],
        preferred_element_type=jnp.float32,
    ).astype(jnp.bfloat16)
    value = total[...]
    for term in range(terms):
        value = value + lax.dot_general(
            low[term * own_cap : (term + 1) * own_cap],
            weights[1 + term][0],
            transposed,
            preferred_element_type=jnp.float32,
        )
    total[...] = value


def back_two_kernel(
    place_ref,
    powers_ref,
    all_ref,
    own_ref,
    weight_0,
    weight_a,
    weight_b,
    weight_c,
    turned_ref,
    mixed_ref,
    gain_ref,
    valid_ref,
    rest_ref,
    low_ref,
    mine_ref,
    other_ref,
    total,
):
    step = pl.program_id(0)
    weights = (weight_0, weight_a, weight_b, weight_c)
    backward_step(step, powers_ref, all_ref, own_ref, weights, total)

    @pl.when(step == pl.num_programs(0) - 1)
    def finish_layer():
        low, rest = norm_backward(mixed_ref[...], total[...], gain_ref[...], valid_ref[...])
        low_ref[...] = low
        weight_gradient(turned_ref, low, place_ref[1], mine_ref, other_ref)
        part = turned_ref.shape[0] // 2
        extra = jnp.zeros((1, mine_ref.shape[1] - part, mine_ref.shape[2]), jnp.bfloat16)
        rows = rest + [rest_ref[place : place + 1, :] for place in range(3)]
        rows = jnp.concatenate(rows + [jnp.zeros((10, rows[0].shape[1]), jnp.float32)], axis=0)

        def below(first_ref, second_ref):
            first_ref[:, part:, :] = extra
            second_ref[:, part:, :] = extra
            first_ref[0, part : part + 16, :] = rows.astype(jnp.bfloat16)

        @pl.when(place_ref[1] == 0)
        def low_half_here():
            below(mine_ref, other_ref)

        @pl.when(place_ref[1] == 1)
        def low_half_there():
            below(other_ref, mine_ref)


def back_one_kernel(
    powers_ref, all_ref, own_ref, weight_0, weight_a, weight_b, weight_c, out_ref, total
):
    step = pl.program_id(0)
    weights = (weight_0, weight_a, weight_b, weight_c)
    backward_step(step, powers_ref, all_ref, own_ref, weights, total)

    @pl.when(step == pl.num_programs(0) - 1)
    def finish_layer():
        out_ref[...] = total[...].astype(jnp.bfloat16)


def layer_pass(kernel, name, place, powers, everyone, own, weight, others, outs, scratch):
    ignored, own_cap, span = powers.shape
    fan_in, width = weight.shape[1:]

    def whole(value):
        return pl.BlockSpec(value.shape, lambda step: (0,) * len(value.shape))

    def term_weight(term):
        return pl.BlockSpec((1, fan_in, width), lambda step: (1 + step * TERMS + term, 0, 0))

    in_specs = [
        pl.BlockSpec((TERMS, own_cap, span), lambda step: (step, 0, 0)),
        whole(everyone),
        whole(own),
        pl.BlockSpec((1, fan_in, width), lambda step: (0, 0, 0)),
    ]
    in_specs += [term_weight(term) for term in range(TERMS)] + [whole(value) for value in others]
    operands = [powers, everyone, own] + [weight] * (1 + TERMS) + list(others)
    if place is not None:
        in_specs = [pl.BlockSpec(memory_space=pltpu.SMEM)] + in_specs
        operands = [place] + operands
    return pl.pallas_call(
        kernel,
        grid=((ORDER - 1) // TERMS,),
        out_shape=outs,
        in_specs=in_specs,
        out_specs=[whole(value) for value in outs],
        scratch_shapes=[pltpu.VMEM(shape, dtype) for shape, dtype in scratch],
        compiler_params=pltpu.CompilerParams(vmem_limit_bytes=VMEM_BYTES),
        cost_estimate=NO_COST,
        name=name,
    )(*operands)


def finish_kernel(scalars_ref, pair_ref, siblings_ref, other_ref, out_ref, *small_refs):
    step = pl.program_id(0)
    part = out_ref.shape[1]
    held = pl.num_programs(0) // 2
    for here, values_ref in ((step < held, pair_ref), (step >= held, siblings_ref)):
        @pl.when(here & (scalars_ref[0] == 1))
        def fast_form():
            out_ref[0] = values_ref[0, :part, :].astype(jnp.float32)

        for small_ref in small_refs:
            @pl.when(here & (scalars_ref[1 + step] == 0))
            def small_sums():
                small_ref[...] = values_ref[0, part : part + 16, :].astype(jnp.float32)

    @pl.when(scalars_ref[0] == 0)
    def general_form():
        out_ref[0] = other_ref[0].astype(jnp.float32)


def finished(scalars, pair, siblings, other, with_small=False):
    count, part, width = other.shape
    out, held = (1, part, width), (1,) + pair.shape[1:]
    out_specs = [pl.BlockSpec(out, lambda step, ref: (ref[1 + step], 0, 0))]
    out_shape = [jax.ShapeDtypeStruct(other.shape, jnp.float32)]
    if with_small:
        out_specs.append(pl.BlockSpec((16, width), lambda step, ref: (0, 0)))
        out_shape.append(jax.ShapeDtypeStruct((16, width), jnp.float32))
    return pl.pallas_call(
        finish_kernel,
        grid_spec=pltpu.PrefetchScalarGridSpec(
            num_scalar_prefetch=1,
            grid=(count,),
            in_specs=[
                pl.BlockSpec(held, lambda step, ref: (jnp.minimum(step, count // 2 - 1), 0, 0)),
                pl.BlockSpec(held, lambda step, ref: (jnp.maximum(step - count // 2, 0), 0, 0)),
                pl.BlockSpec(out, lambda step, ref: ((1 - ref[0]) * ref[1 + step], 0, 0)),
            ],
            out_specs=out_specs,
        ),
        out_shape=out_shape,
        compiler_params=pltpu.CompilerParams(vmem_limit_bytes=VMEM_BYTES),
        cost_estimate=pl.CostEstimate(
            flops=other.size, bytes_accessed=6 * other.size, transcendentals=0
        ),
        name="finished",
    )(scalars, pair, siblings, other)


def unpack_kernel(place_ref, pieces_ref, keys_ref, own_ref, quadrant_ref, columns, hot):
    groups, high, lanes = pieces_ref.shape
    own_cap, span = own_ref.shape
    whole = own_cap // lanes
    send_cap = keys_ref.shape[1] // groups
    half, rest = send_cap // 2, own_cap - whole * lanes
    for group in range(groups):
        start = group * send_cap
        for tile in range(whole):
            columns[start : start + send_cap, tile * lanes : (tile + 1) * lanes] = pieces_ref[
                group, tile * send_cap : (tile + 1) * send_cap, :
            ]
        ends = pieces_ref[group, whole * send_cap :, :]
        columns[start : start + half, whole * lanes :] = ends[:, :rest]
        columns[start + half : start + send_cap, whole * lanes :] = ends[:, rest:]
    standing = lax.broadcasted_iota(jnp.int32, hot.shape, 0)
    hot[...] = jnp.where(standing == keys_ref[...], 1.0, 0.0).astype(jnp.bfloat16)
    block = jnp.dot(hot[...], columns[...], preferred_element_type=jnp.float32)
    own_ref[...] = block.T.astype(jnp.bfloat16)
    middle = span // 2

    @pl.when(place_ref[0] == 0)
    def first():
        quadrant_ref[...] = own_ref[:, :middle]

    @pl.when(place_ref[0] == 1)
    def second():
        quadrant_ref[...] = own_ref[:, middle:]


def unpacked_block(pieces, keys, place, own_cap, span):
    vector = pl.BlockSpec(memory_space=pltpu.VMEM)
    return pl.pallas_call(
        unpack_kernel,
        out_shape=[
            jax.ShapeDtypeStruct((own_cap, span), jnp.bfloat16),
            jax.ShapeDtypeStruct((own_cap, span // 2), jnp.bfloat16),
        ],
        in_specs=[pl.BlockSpec(memory_space=pltpu.SMEM), vector, vector],
        out_specs=[vector, vector],
        scratch_shapes=[
            pltpu.VMEM((keys.shape[1], own_cap), jnp.bfloat16),
            pltpu.VMEM((span, keys.shape[1]), jnp.bfloat16),
        ],
        compiler_params=pltpu.CompilerParams(vmem_limit_bytes=VMEM_BYTES),
        cost_estimate=NO_COST,
        name="unpacked_block",
    )(place, pieces, keys)


def fit_kernel(codes_ref, out_ref, *, n_row, caps):
    own_cap, send_cap, seat_cap = caps
    codes = codes_ref[...]
    devices = codes.shape[0]
    n_col = devices // n_row
    label = lax.broadcasted_iota(jnp.int32, (devices, 128), 1)
    counts = jnp.zeros((devices, 128), jnp.float32)
    for cluster in range(CLUSTERS):
        here = jnp.where(codes == 2 * cluster + 1, 1.0, 0.0)
        counts = counts + jnp.where(
            label == cluster, jnp.sum(here, axis=1, keepdims=True), 0.0
        )
    sizes = jnp.sum(counts, axis=0, keepdims=True)
    across = jnp.broadcast_to(sizes, (128, 128))
    down = across.T
    first = lax.broadcasted_iota(jnp.int32, (128, 128), 0)
    second = lax.broadcasted_iota(jnp.int32, (128, 128), 1)
    ahead = (across > down) | ((across == down) & (second < first))
    ahead = ahead & (second < CLUSTERS)
    rank = jnp.sum(jnp.where(ahead, 1.0, 0.0), axis=1, keepdims=True).astype(jnp.int32)
    others = n_row - 1
    later = rank > others
    turn = jnp.zeros_like(rank)
    for count in range(1, CLUSTERS // others + 1):
        turn = turn + jnp.where(rank - 1 >= count * others, 1, 0)
    place = rank - 1 - turn * others
    group = jnp.where(rank == 0, 0, 1 + jnp.where(later, others - 1 - place, place))
    member = (group == second) & (first < CLUSTERS)
    held = jnp.dot(
        counts.astype(jnp.bfloat16),
        jnp.where(member, 1.0, 0.0).astype(jnp.bfloat16),
        preferred_element_type=jnp.float32,
    )
    by_row = jnp.zeros((1, 128), jnp.float32)
    for row in range(n_row):
        rows = jnp.sum(held[row * n_col : (row + 1) * n_col], axis=0, keepdims=True)
        by_row = jnp.maximum(by_row, rows)
    device = lax.broadcasted_iota(jnp.int32, (devices, 128), 0)
    by_col = jnp.zeros((1, 128), jnp.float32)
    for col in range(n_col):
        cols = jnp.where(device % n_col == col, held, 0.0)
        by_col = jnp.maximum(by_col, jnp.sum(cols, axis=0, keepdims=True))
    fits = (
        (jnp.max(by_col) <= own_cap) & (jnp.max(by_row) <= send_cap) & (jnp.max(held) <= seat_cap)
    )
    out_ref[0] = jnp.where(fits, 1, 0)


def fits_in(codes, n_row, caps):
    fits = pl.pallas_call(
        functools.partial(fit_kernel, n_row=n_row, caps=caps),
        out_shape=jax.ShapeDtypeStruct((1,), jnp.int32),
        in_specs=[pl.BlockSpec(memory_space=pltpu.VMEM)],
        out_specs=pl.BlockSpec(memory_space=pltpu.SMEM),
        cost_estimate=NO_COST,
        name="fits",
    )(codes.reshape(-1, codes.shape[-1]))
    return fits


def exclusive_counts(member):
    count = member.shape[-1]
    before = jnp.arange(count)[:, None] < jnp.arange(count)[None, :]
    return jnp.dot(
        member.astype(jnp.bfloat16),
        before.astype(jnp.bfloat16),
        preferred_element_type=jnp.float32,
    ).astype(jnp.int32)


def assign(codes, n_row):
    cluster, valid = codes >> 1, codes & 1
    labels = jnp.arange(CLUSTERS)
    sizes = jnp.sum(
        (cluster.reshape(1, -1) == labels[:, None]) & (valid.reshape(1, -1) == 1), axis=1
    )
    ahead = (sizes[None, :] > sizes[:, None]) | (
        (sizes[None, :] == sizes[:, None]) & (labels[None, :] < labels[:, None])
    )
    rank = jnp.sum(ahead, axis=1)
    others = n_row - 1
    turn, place = (rank - 1) // others, (rank - 1) % others
    group = jnp.where(rank == 0, 0, 1 + jnp.where(turn == 0, place, others - 1 - place))
    of_node = jnp.sum(
        jnp.where(cluster[None] == labels[:, None, None, None], group[:, None, None, None], 0),
        axis=0,
    )
    return jnp.where(valid == 1, of_node, n_row)


def compact(
    codes,
    group,
    features,
    block_keep,
    edge_weight,
    weight_one,
    bias_one,
    gain_one,
    shift_one,
    weight_two,
    bias_two,
    gain_two,
    shift_two,
    cotangent,
    places_of,
    slots_of,
    seats_of,
    decide,
    sizes,
    caps,
):
    row, col = lax.axis_index("row"), lax.axis_index(COL)
    chip, core = lax.axis_index("chip"), lax.axis_index("core")
    n_row, n_col = sizes
    own_cap, send_cap, seat_cap = caps
    own_nodes, in_width = features.shape
    width = weight_two.shape[2]
    span = n_col * own_cap
    targets = jnp.arange(n_row)

    def in_col(value):
        return lax.dynamic_index_in_dim(value, col, 1, False).reshape(-1)

    def in_row(value):
        return lax.dynamic_index_in_dim(value, row, 0, False).reshape(-1)

    row_group, col_group = in_row(group), in_col(group)
    row_slots, col_places = in_row(slots_of(group)), in_col(places_of(group))
    row_keys = jnp.where(row_slots < send_cap, row_group * send_cap + row_slots, -1)
    col_keys = jnp.where(col_places < own_cap, col_group * own_cap + col_places, -1)
    pieces = packed_pieces(
        block_keep,
        in_row(codes),
        in_col(codes),
        row_keys,
        col_keys,
        edge_weight,
        (own_cap, send_cap),
        n_row,
    )
    pieces, codes = lax.optimization_barrier((pieces, codes))
    group = assign(codes, n_row)
    places, slots, seats = places_of(group), slots_of(group), seats_of(group)

    standing = jnp.arange(n_col)[None, :, None] * own_cap + places
    fits_here = jnp.where(group == row, standing, -1).reshape(n_row, -1)
    slot_of = slots.reshape(n_row, -1)
    target = jnp.max(
        jnp.where(
            slot_of[:, None, :] == jnp.arange(send_cap)[None, :, None], fits_here[:, None, :], -1
        ),
        axis=2,
    )
    keys = target.reshape(1, -1)

    def to_partner(value, step):
        return lax.ppermute(value, "row", [(place, place ^ step) for place in range(n_row)])

    partners = row ^ targets
    group_here = lax.dynamic_index_in_dim(in_row(group).reshape(n_col, -1), col, 0, False)
    seat_here = lax.dynamic_index_in_dim(in_row(seats).reshape(n_col, -1), col, 0, False)

    def seat_of_node(groups):
        hot = (group_here[None, None, :] == groups[:, None, None]) & (
            seat_here[None, None, :] == jnp.arange(seat_cap)[None, :, None]
        )
        return hot.astype(jnp.bfloat16).reshape(n_row * seat_cap, own_nodes)

    enter_home = seat_of_node(targets).T
    enter_partner = seat_of_node(partners)
    both = jnp.dot(enter_partner, jnp.concatenate([features, cotangent], axis=1))
    both = both.reshape(n_row, seat_cap, -1)
    enter_partner = enter_partner.T
    pieces = trade(pieces, "row")
    both, codes = lax.optimization_barrier((both, codes))
    fits, others = decide(codes)
    group_col = lax.dynamic_index_in_dim(group, col, 1, False)
    seats_col = lax.dynamic_index_in_dim(seats, col, 1, False)
    places_col = lax.dynamic_index_in_dim(places, col, 1, False)
    seated = (group_col == row)[:, None, :] & (
        seats_col[:, None, :] == jnp.arange(seat_cap)[None, :, None]
    )
    place_of_seat = jnp.max(jnp.where(seated, places_col[:, None, :], -1), axis=2)
    from_partner = jnp.max(
        jnp.where((partners[:, None] == targets)[:, :, None], place_of_seat[None], -1), axis=1
    )
    arrive = from_partner.reshape(1, -1) == jnp.arange(own_cap)[:, None]
    arrive = arrive.astype(jnp.bfloat16)
    leave_group = place_of_seat.reshape(-1, 1) == jnp.arange(own_cap)
    leave_group = leave_group.astype(jnp.bfloat16)
    leave_partner = jnp.concatenate([from_partner[::2], from_partner[1::2]])
    leave_partner = leave_partner.reshape(-1, 1) == jnp.arange(own_cap)
    leave_partner = leave_partner.astype(jnp.bfloat16)
    held_count = jnp.sum(group_col == row)
    valid_rows = (jnp.arange(own_cap) < held_count).astype(jnp.float32)[:, None]
    place = jnp.stack([chip, core]).astype(jnp.int32)
    quarters = jnp.stack([col, (1 - chip) * 2 + core, chip * 2 + 1 - core, 3 - col])
    quarters = jnp.concatenate([fits, quarters.astype(jnp.int32)])
    own_halves = jnp.concatenate([fits, jnp.stack([core, 1 - core]).astype(jnp.int32)])
    scalars = (chip, 1 - chip, col * own_cap)
    scalars = tuple(value.astype(jnp.uint32) for value in scalars) + (chip == 0, core == 0, place)
    scalars = scalars + (quarters, own_halves)
    homes = enter_home, enter_partner, leave_group, leave_partner
    pieces, both, keys, arrive, homes, valid_rows, others, scalars = lax.optimization_barrier(
        (pieces, both, keys, arrive, homes, valid_rows, others, scalars)
    )
    enter_home, enter_partner, leave_group, leave_partner = homes
    this_chip, other_chip, own_start, first_chip, first_core = scalars[:5]
    place, quarters, own_halves = scalars[5:]

    own_block, quadrant = unpacked_block(pieces, keys, place, own_cap, span)
    quadrant = swap(quadrant, "chip")
    both = [both[0]] + [to_partner(both[step], step) for step in range(1, n_row)]
    sibling = swap(own_block, "core")
    quadrant, *early = lax.optimization_barrier((quadrant, *both[:-2]))
    adjacency = normalized_block(own_block, sibling, quadrant, swap(quadrant, "core"), place)
    adjacency, *late = lax.optimization_barrier((adjacency, *both[-2:]))
    both = early + late
    mine = jnp.dot(arrive, jnp.concatenate(both))
    features_own, cotangent_own = mine[:, :in_width], mine[:, in_width:]
    sibling = swap(features_own, "core")

    first = (own_start + jnp.arange(own_cap, dtype=jnp.uint32))[:, None]
    first = first == jnp.arange(span, dtype=jnp.uint32)[None, :]
    previous = first.astype(jnp.float32)
    current = -lax.dynamic_slice_in_dim(adjacency, own_start, own_cap, 0).astype(jnp.float32)
    lowered = [current.astype(jnp.bfloat16)]
    for position in range(2, ORDER):
        upcoming = (
            -2.0 * jnp.dot(lowered[-1], adjacency, preferred_element_type=jnp.float32) - previous
        )
        low = upcoming.astype(jnp.bfloat16)
        if position == 4:
            low, sibling = lax.optimization_barrier((low, sibling))
            features_chip = joined(features_own, sibling, first_core)
            partner = swap(features_chip, "chip")
        if position == 8:
            low, partner = lax.optimization_barrier((low, partner))
            features_all = joined(features_chip, partner, first_chip)
        previous, current = current, upcoming
        lowered.append(low)
    powers = jnp.concatenate(lowered, axis=0).reshape(ORDER - 1, own_cap, span)

    def everywhere(value_low):
        return lax.all_gather(value_low, COL, axis=0, tiled=True)

    def chosen(value, other):
        return jnp.where(quarters[0] == 1, value.astype(jnp.float32), other.astype(jnp.float32))

    def shaped(*shape, dtype=jnp.bfloat16):
        return jax.ShapeDtypeStruct(shape, dtype)

    part_one, part_two = ORDER * in_width // 2, ORDER * width // n_col
    padded = -(-(part_one + 16) // (16 * n_row)) * (16 * n_row)
    hidden, turned_one, mixed_one = layer_pass(
        layer_one_kernel,
        "layer_one",
        None,
        powers,
        features_all,
        features_own,
        weight_one,
        [bias_one[None], gain_one[None], shift_one[None], valid_rows],
        [
            shaped(own_cap, width),
            shaped(2 * part_one, own_cap),
            shaped(own_cap, width, dtype=jnp.float32),
        ],
        [],
    )
    activations, low_two, rest_two, mine, other = layer_pass(
        layer_two_kernel,
        "layer_two",
        place,
        powers,
        everywhere(hidden),
        hidden,
        weight_two,
        [bias_two[None], gain_two[None], shift_two[None], valid_rows, cotangent_own],
        [
            shaped(own_cap, width),
            shaped(own_cap, width),
            shaped(3, width, dtype=jnp.float32),
            shaped(2, part_two, width),
            shaped(2, part_two, width),
        ],
        [((n_col * part_two, own_cap), jnp.bfloat16), ((own_cap, width), jnp.float32)],
    )

    def add_cores(mine, other, axis=0):
        got = swap(other, "core")
        return tuple(
            added(
                lax.dynamic_index_in_dim(mine, index, axis, False),
                lax.dynamic_index_in_dim(got, index, axis, False),
            )
            for index in (this_chip, other_chip)
        )

    leaving = jnp.dot(leave_partner, activations).reshape(n_row, seat_cap, width)
    near, far = leaving[: n_row // 2], leaving[n_row // 2 :]
    far = to_partner(far, 1)
    here, there = add_cores(mine, other)
    everyone_two, there, far = lax.optimization_barrier((everywhere(low_two), there, far))
    there = swap(there, "chip")
    arrived = [jnp.stack([near[0], far[0]])] + [
        to_partner(jnp.stack([near[half], far[half]]), 2 * half) for half in range(1, n_row // 2)
    ]
    low_one, mine, other = layer_pass(
        back_two_kernel,
        "back_two",
        place,
        powers,
        everyone_two,
        low_two,
        weight_two,
        [turned_one, mixed_one, gain_one[None], valid_rows, rest_two],
        [shaped(own_cap, width), shaped(1, padded, width), shaped(1, padded, width)],
        [((own_cap, width), jnp.float32)],
    )
    low_one, there, arrived = lax.optimization_barrier((low_one, there, arrived))
    second = added(here, there).reshape(n_row, -1, width)
    many = second.shape[1]
    low_one, second = lax.optimization_barrier((low_one, second))
    second = trade(second, "row")
    mine, other = (value.reshape(n_row, 2, -1, width) for value in (mine, other))
    here, there = add_cores(mine, other, 1)
    there = swap(there, "chip")
    first = added(here, there)
    second = jnp.sum(second.astype(jnp.float32), axis=0).astype(jnp.bfloat16)
    second = jnp.broadcast_to(second[None], (n_row,) + second.shape)
    mixed = jnp.concatenate([second, first], axis=1)
    low_one, mixed = lax.optimization_barrier((low_one, mixed))
    everyone_one = everywhere(low_one)
    mixed = trade(mixed, "row")
    (input_grad,) = layer_pass(
        back_one_kernel,
        "back_one",
        None,
        powers,
        everyone_one,
        low_one,
        weight_one,
        [],
        [shaped(own_cap, in_width)],
        [((own_cap, in_width), jnp.float32)],
    )
    leaving = jnp.dot(leave_group, input_grad)
    leaving = leaving.reshape(n_row, seat_cap * in_width // width, width)
    arrived = jnp.concatenate(arrived).reshape(-1, width)
    home = jnp.dot(enter_partner, arrived, preferred_element_type=jnp.float32)
    home = chosen(home, others[0])
    mixed, leaving, home = lax.optimization_barrier((mixed, leaving, home))
    first = jnp.sum(mixed[:, many:].astype(jnp.float32), axis=0).astype(jnp.bfloat16)
    second = mixed[:, :many].reshape(1, -1, width)
    partner_two = swap(second, "chip")
    first = joined(first, swap(first, "chip"), first_chip)
    share = first.shape[0]
    first = jnp.broadcast_to(first[None], (n_row,) + first.shape)
    first = trade(jnp.concatenate([first, leaving], axis=1), "row")
    second = jnp.concatenate([second, partner_two])
    (second,) = finished(quarters, second, swap(second, "core"), others[3])
    first, second = lax.optimization_barrier((first, second))
    mine = first[:, :share].reshape(1, -1, width)
    siblings = swap(mine, "core")
    back = first[:, share:].reshape(n_row * seat_cap, in_width)
    home_grad = jnp.dot(enter_home, back, preferred_element_type=jnp.float32)
    home_grad = chosen(home_grad, others[1])
    first, small = finished(own_halves, mine, siblings, others[2], True)
    return home, home_grad, first, second, chosen(small[:6], others[4])


def general(
    codes,
    features,
    block_keep,
    edge_weight,
    weight_one,
    bias_one,
    gain_one,
    shift_one,
    weight_two,
    bias_two,
    gain_two,
    shift_two,
    cotangent,
    node_valid,
):
    row, col = lax.axis_index("row"), lax.axis_index(COL)
    row_codes = lax.dynamic_index_in_dim(codes, row, 0, False).reshape(-1)
    col_codes = lax.dynamic_index_in_dim(codes, col, 1, False).reshape(-1)
    tile_rows, tile_cols = edge_weight.shape
    blocks_down, blocks_across = block_keep.shape
    block_side = tile_rows // blocks_down
    linked = (row_codes[:, None] == col_codes[None, :]) & (row_codes[:, None] & 1 == 1)
    linked = linked.reshape(blocks_down, block_side, blocks_across, block_side) & (
        block_keep[:, None, :, None] == 1
    )
    masked = edge_weight * linked.reshape(tile_rows, tile_cols).astype(jnp.bfloat16)
    degree_rows = 1.0 + lax.psum(jnp.sum(masked, axis=1, dtype=jnp.float32), COL)
    own_nodes = features.shape[0]
    own_degree = lax.dynamic_slice_in_dim(
        degree_rows, lax.axis_index(COL) * own_nodes, own_nodes, 0
    )
    degree_cols = lax.all_gather(own_degree, "row", axis=0, tiled=True)
    adjacency = (
        masked.astype(jnp.float32)
        * lax.rsqrt(degree_rows)[:, None]
        * lax.rsqrt(degree_cols)[None, :]
    ).astype(jnp.bfloat16)
    valid_rows = node_valid.astype(jnp.float32)
    stacked_one, mixed_one, hidden = layer_forward(
        adjacency,
        features.astype(jnp.float32),
        weight_one,
        bias_one,
        gain_one,
        shift_one,
        valid_rows,
    )
    stacked_two, mixed_two, activations = layer_forward(
        adjacency, hidden, weight_two, bias_two, gain_two, shift_two, valid_rows
    )
    hidden_grad, weight_two_grad, bias_two_grad, gain_two_grad, shift_two_grad = layer_backward(
        adjacency,
        stacked_two,
        mixed_two,
        cotangent.astype(jnp.float32),
        weight_two,
        gain_two,
        shift_two,
        valid_rows,
    )
    input_grad, weight_one_grad, bias_one_grad, gain_one_grad, shift_one_grad = layer_backward(
        adjacency, stacked_one, mixed_one, hidden_grad, weight_one, gain_one, shift_one, valid_rows
    )
    summed = lax.psum(
        (
            weight_one_grad,
            bias_one_grad,
            gain_one_grad,
            shift_one_grad,
            weight_two_grad,
            bias_two_grad,
            gain_two_grad,
            shift_two_grad,
        ),
        ("row",) + COL,
    )
    weight_one_grad, bias_one_grad, gain_one_grad, shift_one_grad = (
        summed[0],
        summed[1],
        summed[2],
        summed[3],
    )
    weight_two_grad, bias_two_grad, gain_two_grad, shift_two_grad = (
        summed[4],
        summed[5],
        summed[6],
        summed[7],
    )
    return (
        activations,
        input_grad,
        weight_one_grad,
        bias_one_grad,
        gain_one_grad,
        shift_one_grad,
        weight_two_grad,
        bias_two_grad,
        gain_two_grad,
        shift_two_grad,
    )


def local(n_row, n_col, *args):
    (
        features,
        node_valid,
        cluster,
        block_keep,
        edge_weight,
        weight_one,
        bias_one,
        gain_one,
        shift_one,
        weight_two,
        bias_two,
        gain_two,
        shift_two,
        cotangent,
    ) = args
    own_nodes, in_width = features.shape
    own_cap = own_nodes * n_row * 5 // 16
    send_cap = own_nodes * n_col * 11 // 32
    seat_cap = own_nodes * 7 // 16
    codes = broadcast_along(cluster * 2 + node_valid, ("row",) + COL, n_row * n_col)
    codes = codes.reshape(n_row, n_col, own_nodes)
    shared = (
        block_keep,
        edge_weight,
        weight_one,
        bias_one,
        gain_one,
        shift_one,
        weight_two,
        bias_two,
        gain_two,
        shift_two,
        cotangent,
    )

    def slow():
        return general(codes, features, *shared, node_valid)

    held = (ORDER - 1) * own_cap * own_cap * n_col * 2
    if held > HELD_BYTES or n_col != 4 or n_row < 2 or n_row & (n_row - 1):
        return slow()
    group = assign(codes, n_row)

    def member_of(group):
        return group[None] == jnp.arange(n_row)[:, None, None, None]

    def places_of(group):
        member = member_of(group).transpose(0, 2, 1, 3).reshape(n_row, n_col, -1)
        places = jnp.sum(jnp.where(member, exclusive_counts(member), 0), axis=0)
        return places.reshape(n_col, n_row, own_nodes).transpose(1, 0, 2)

    def slots_of(group):
        member = member_of(group).reshape(n_row, n_row, -1)
        slots = jnp.sum(jnp.where(member, exclusive_counts(member), 0), axis=0)
        return slots.reshape(n_row, n_col, own_nodes)

    def seats_of(group):
        member = member_of(group)
        return jnp.sum(jnp.where(member, exclusive_counts(member), 0), axis=0)

    width = weight_two.shape[2]

    def instead(state):
        made = slow()
        small = jnp.stack([made[place] for place in (3, 4, 5, 7, 8, 9)])
        return (jnp.ones_like(state[0]),) + tuple(
            value.astype(jnp.bfloat16).reshape(like.shape)
            for value, like in zip((made[0], made[1], made[2], made[6], small), state[1:])
        )

    shapes = (
        (own_nodes, width),
        (own_nodes, in_width),
        (2, ORDER * in_width // 2, width),
        (n_col, ORDER * width // n_col, width),
        (6, width),
    )

    def decide(codes):
        fits = fits_in(codes, n_row, (own_cap, send_cap, seat_cap))
        others = lax.while_loop(
            lambda state: state[0][0] == 0,
            instead,
            (fits,) + tuple(jnp.zeros(shape, jnp.bfloat16) for shape in shapes),
        )[1:]
        return fits, others

    home, home_grad, first, second, small = compact(
        codes,
        group,
        features,
        *shared,
        places_of,
        slots_of,
        seats_of,
        decide,
        (n_row, n_col),
        (own_cap, send_cap, seat_cap),
    )
    return (
        home,
        home_grad,
        first.reshape(weight_one.shape),
        small[0],
        small[1],
        small[2],
        second.reshape(weight_two.shape),
        small[3],
        small[4],
        small[5],
    )


def solution(mesh):
    n_row, n_col = mesh.shape["row"], mesh.shape["col"]
    by_core = jax.sharding.Mesh(
        mesh.devices.reshape(n_row, n_col // 2, 2), ("row", "chip", "core")
    )
    nodes = ("row", "chip", "core")
    placed = (
        P(nodes, None),
        P(nodes),
        P(nodes),
        P("row", COL),
        P("row", COL),
        P(),
        P(),
        P(),
        P(),
        P(),
        P(),
        P(),
        P(),
        P(nodes, None),
    )
    return jax.shard_map(
        functools.partial(local, n_row, n_col),
        mesh=by_core,
        in_specs=placed,
        out_specs=(P(nodes, None), P(nodes, None), P(), P(), P(), P(), P(), P(), P(), P()),
        check_vma=False,
    )
```

```python
import functools
import math

import jax
import jax.numpy as jnp
from jax import lax
from jax.experimental import pallas as pl
from jax.experimental.pallas import tpu as pltpu
from jax.sharding import PartitionSpec as P

ORDER = 13
CLUSTERS = 16
HELD_BYTES = 1 << 25
VMEM_BYTES = 32 << 20
TERMS = 3
NO_COST = pl.CostEstimate(flops=1, bytes_accessed=1, transcendentals=0)
COL = ("chip", "core")


def finish(mixed, gain, shift, valid_rows):
    active = jax.nn.gelu(mixed, approximate=False)
    centered = active - jnp.mean(active, axis=-1, keepdims=True)
    variance = jnp.mean(centered * centered, axis=-1, keepdims=True)
    return (centered * lax.rsqrt(variance + 1e-05) * gain + shift) * valid_rows[:, None]


def forward_product(adjacency, piece_low):
    partial_value = jnp.dot(
        adjacency,
        lax.all_gather(piece_low, "row", axis=0, tiled=True),
        preferred_element_type=jnp.float32,
    )
    return lax.psum_scatter(partial_value, COL, scatter_dimension=0, tiled=True)


def backward_product(adjacency, piece_low):
    partial_value = lax.dot_general(
        adjacency,
        lax.all_gather(piece_low, COL, axis=0, tiled=True),
        (((0,), (0,)), ((), ())),
        preferred_element_type=jnp.float32,
    )
    return lax.psum_scatter(
        partial_value.astype(jnp.bfloat16), "row", scatter_dimension=0, tiled=True
    ).astype(jnp.float32)


def layer_forward(adjacency, inputs, weight, bias, gain, shift, valid_rows):
    first_low = inputs.astype(jnp.bfloat16)
    second = -forward_product(adjacency, first_low)
    second_low = second.astype(jnp.bfloat16)

    def advance(state_pair, unused):
        previous, current, current_low = state_pair
        upcoming = -2.0 * forward_product(adjacency, current_low) - previous
        upcoming_low = upcoming.astype(jnp.bfloat16)
        return ((current, upcoming, upcoming_low), upcoming_low)

    ignored, others = lax.scan(advance, (inputs, second, second_low), None, length=ORDER - 2)
    stacked = jnp.concatenate([first_low[None], second_low[None], others], axis=0)
    mixed = jnp.einsum("kni,kio->no", stacked, weight, preferred_element_type=jnp.float32) + bias
    return (stacked, mixed, finish(mixed, gain, shift, valid_rows))


def layer_backward(adjacency, stacked, mixed, upstream, weight, gain, shift, valid_rows):

    def local_finish(mixed_in, gain_in, shift_in):
        return finish(mixed_in, gain_in, shift_in, valid_rows)

    ignored, pullback = jax.vjp(local_finish, mixed, gain, shift)
    mixed_grad, gain_grad, shift_grad = pullback(upstream)
    mixed_low = mixed_grad.astype(jnp.bfloat16)
    bias_grad = jnp.sum(mixed_low.astype(jnp.float32), axis=0)
    weight_grad = jnp.einsum("kni,no->kio", stacked, mixed_low, preferred_element_type=jnp.float32)
    direct = jnp.einsum("no,kio->kni", mixed_low, weight, preferred_element_type=jnp.float32)

    def retreat(state_pair, direct_term):
        later_two, later_one = state_pair
        current = (
            direct_term
            - 2.0 * backward_product(adjacency, later_one.astype(jnp.bfloat16))
            - later_two
        )
        return ((later_one, current), None)

    start_pair = (jnp.zeros_like(direct[0]), direct[ORDER - 1])
    (second_grad, first_grad), unused = lax.scan(
        retreat, start_pair, direct[1 : ORDER - 1], reverse=True
    )
    input_grad = (
        direct[0] - backward_product(adjacency, first_grad.astype(jnp.bfloat16)) - second_grad
    )
    return (input_grad, weight_grad, bias_grad, gain_grad, shift_grad)


def swap(value, axis):
    return lax.ppermute(value, axis, [(0, 1), (1, 0)])


def trade(pieces, axis):
    return lax.all_to_all(pieces, axis, 0, 0, tiled=False)


def broadcast_along(value, axis, size):
    return trade(jnp.broadcast_to(value[None], (size,) + value.shape), axis)


def joined(mine, other, mine_first):
    return jnp.where(
        mine_first, jnp.concatenate([mine, other]), jnp.concatenate([other, mine])
    )


def added(mine, received):
    return (mine.astype(jnp.float32) + received.astype(jnp.float32)).astype(jnp.bfloat16)


def assemble(place_ref, own_ref, sibling_ref, near_ref, far_ref, out_ref, done):
    chip, core = place_ref[0], place_ref[1]
    own_cap, span = own_ref.shape
    half = span // 2

    def rows(of_chip, of_core):
        return pl.ds(pl.multiple_of((2 * of_chip + of_core) * own_cap, own_cap), own_cap)

    def fetch(source, of_chip, of_core, columns, place):
        target = out_ref.at[rows(of_chip, of_core), columns]
        return pltpu.make_async_copy(source, target, done.at[place])

    def quadrant_copies(here):
        there = 1 - here
        columns = pl.ds(there * half, half)
        return (
            fetch(near_ref, there, core, columns, 2),
            fetch(far_ref, there, 1 - core, columns, 3),
        )

    everything = pl.ds(0, span)
    top = (
        fetch(own_ref, chip, core, everything, 0),
        fetch(sibling_ref, chip, 1 - core, everything, 1),
    )

    def of_chip(here):
        there = 1 - here
        copies = top + quadrant_copies(here)
        for copy in copies:
            copy.start()
        for copy in copies:
            copy.wait()
        here_rows = pl.ds(here * half, half)
        for tile in range(half // 128):
            columns = pl.ds(there * half + tile * 128, 128)
            strip = out_ref[here_rows, columns]
            turned = jnp.transpose(strip.astype(jnp.float32)).astype(jnp.bfloat16)
            out_ref[columns, here_rows] = turned

    @pl.when(chip == 0)
    def first():
        of_chip(0)

    @pl.when(chip == 1)
    def second():
        of_chip(1)

    across = jnp.ones((1, span), jnp.float32)
    for tile in range(span // 128):
        across = across + jnp.sum(
            out_ref[pl.ds(tile * 128, 128), :].astype(jnp.float32), axis=0, keepdims=True
        )
    across = lax.rsqrt(across)
    for tile in range(span // 128):
        strip = out_ref[pl.ds(tile * 128, 128), :].astype(jnp.float32)
        down = lax.rsqrt(1.0 + jnp.sum(strip, axis=1, keepdims=True))
        out_ref[pl.ds(tile * 128, 128), :] = (strip * down * across).astype(jnp.bfloat16)


def normalized_block(own, sibling, near, far, place):
    span = own.shape[1]
    return pl.pallas_call(
        assemble,
        out_shape=jax.ShapeDtypeStruct((span, span), jnp.bfloat16),
        in_specs=[pl.BlockSpec(memory_space=pltpu.SMEM)]
        + [pl.BlockSpec(memory_space=pltpu.HBM)] * 4,
        out_specs=pl.BlockSpec(memory_space=pltpu.VMEM),
        scratch_shapes=[pltpu.SemaphoreType.DMA((4,))],
        compiler_params=pltpu.CompilerParams(vmem_limit_bytes=VMEM_BYTES),
        cost_estimate=NO_COST,
        name="normalized_block",
    )(place, own, sibling, near, far)


def pack_kernel(
    keep_ref, row_codes_ref, col_codes_ref, row_keys_ref, col_keys_ref, weight_ref, out_ref,
    masked, picked, rows_hot, cols_hot
):
    tile_rows, tile_cols = weight_ref.shape
    blocks_down, blocks_across = keep_ref.shape
    groups, ignored, lanes = out_ref.shape
    send_cap, own_cap = rows_hot.shape[0] // groups, cols_hot.shape[0] // groups
    high, wide = tile_rows // blocks_down, tile_cols // blocks_across
    for down in range(blocks_down):
        for across in range(blocks_across):
            rows, columns = pl.ds(down * high, high), pl.ds(across * wide, wide)
            own, other = row_codes_ref[rows, :], col_codes_ref[:, columns]
            linked = (own == other) & (own % 2 == 1) & (keep_ref[down, across] == 1)
            weight = weight_ref[rows, columns].astype(jnp.float32)
            masked[rows, columns] = jnp.where(linked, weight, 0.0).astype(jnp.bfloat16)

    def one_hot(keys, start, count):
        standing = lax.broadcasted_iota(jnp.int32, (count, keys.shape[1]), 0) + start
        return jnp.where(standing == keys, 1.0, 0.0).astype(jnp.bfloat16)

    for group in range(groups):
        rows_hot[pl.ds(group * send_cap, send_cap), :] = one_hot(
            row_keys_ref[...], group * send_cap, send_cap
        )
        cols_hot[pl.ds(group * own_cap, own_cap), :] = one_hot(
            col_keys_ref[...], group * own_cap, own_cap
        )
    for tile in range(tile_cols // 256):
        columns = pl.ds(tile * 256, 256)
        picked[:, columns] = jnp.dot(
            rows_hot[...], masked[:, columns], preferred_element_type=jnp.float32
        ).astype(jnp.bfloat16)
    whole, half = own_cap // lanes, send_cap // 2
    for group in range(groups):
        packed = lax.dot_general(
            cols_hot[pl.ds(group * own_cap, own_cap), :],
            picked[pl.ds(group * send_cap, send_cap), :],
            (((1,), (1,)), ((), ())),
            preferred_element_type=jnp.float32,
        ).T
        for tile in range(whole):
            out_ref[group, pl.ds(tile * send_cap, send_cap), :] = packed[
                :, tile * lanes : (tile + 1) * lanes
            ].astype(jnp.bfloat16)
        ends = jnp.concatenate(
            [packed[:half, whole * lanes :], packed[half:, whole * lanes :]], axis=1
        )
        out_ref[group, pl.ds(whole * send_cap, half), :] = ends.astype(jnp.bfloat16)


def packed_pieces(block_keep, row_codes, col_codes, row_keys, col_keys, edge_weight, caps, groups):
    own_cap, send_cap = caps
    tile_rows, tile_cols = edge_weight.shape
    high = own_cap // 128 * send_cap + send_cap // 2
    vector = pl.BlockSpec(memory_space=pltpu.VMEM)
    return pl.pallas_call(
        pack_kernel,
        out_shape=jax.ShapeDtypeStruct((groups, high, 128), jnp.bfloat16),
        in_specs=[pl.BlockSpec(memory_space=pltpu.SMEM)] + [vector] * 5,
        out_specs=vector,
        scratch_shapes=[
            pltpu.VMEM((tile_rows, tile_cols), jnp.bfloat16),
            pltpu.VMEM((groups * send_cap, tile_cols), jnp.bfloat16),
            pltpu.VMEM((groups * send_cap, tile_rows), jnp.bfloat16),
            pltpu.VMEM((groups * own_cap, tile_cols), jnp.bfloat16),
        ],
        compiler_params=pltpu.CompilerParams(vmem_limit_bytes=VMEM_BYTES),
        cost_estimate=NO_COST,
        name="packed_pieces",
    )(block_keep, row_codes[:, None], col_codes[None], row_keys[None], col_keys[None], edge_weight)


def normal_share(mixed):
    return 0.5 * (1.0 + lax.erf(mixed * 0.5**0.5))


def norm_forward(mixed):
    active = mixed * normal_share(mixed)
    centered = active - jnp.mean(active, axis=-1, keepdims=True)
    scale = lax.rsqrt(jnp.mean(centered * centered, axis=-1, keepdims=True) + 1e-05)
    return centered * scale, scale


def norm_backward(mixed, upstream, gain, valid):
    normed, scale = norm_forward(mixed)
    upstream = upstream * valid
    inner = upstream * gain
    inner = inner - jnp.mean(inner, axis=-1, keepdims=True) - normed * jnp.mean(
        inner * normed, axis=-1, keepdims=True
    )
    density = jnp.exp(-0.5 * mixed * mixed) * (1.0 / (2.0 * math.pi) ** 0.5)
    low = (inner * scale * (normal_share(mixed) + mixed * density)).astype(jnp.bfloat16)
    rest = [low.astype(jnp.float32), upstream * normed, upstream]
    return low, [jnp.sum(value, axis=0, keepdims=True) for value in rest]


def weight_gradient(turned_ref, low, core, mine_ref, other_ref):
    parts = mine_ref.shape[0]
    part = turned_ref.shape[0] // (2 * parts)

    def halves(first_ref, second_ref):
        for place in range(2 * parts):
            out_ref = second_ref if place % 2 else first_ref
            out_ref[place // 2, :part, :] = jnp.dot(
                turned_ref[place * part : (place + 1) * part, :],
                low,
                preferred_element_type=jnp.float32,
            ).astype(jnp.bfloat16)

    @pl.when(core == 0)
    def low_half_first():
        halves(mine_ref, other_ref)

    @pl.when(core == 1)
    def high_half_first():
        halves(other_ref, mine_ref)


def forward_step(step, powers_ref, all_ref, own_ref, weights, bias_ref, turned, mixed):
    terms, own_cap, span = powers_ref.shape
    fan_in = own_ref.shape[1]

    @pl.when(step == 0)
    def first():
        turned[:fan_in, :] = own_ref[...].T
        mixed[...] = bias_ref[...] + jnp.dot(
            own_ref[...], weights[0][0], preferred_element_type=jnp.float32
        )

    low = jnp.dot(
        powers_ref[...].reshape(terms * own_cap, span),
        all_ref[...],
        preferred_element_type=jnp.float32,
    ).astype(jnp.bfloat16)
    total = mixed[...]
    for term in range(terms):
        part = low[term * own_cap : (term + 1) * own_cap]
        start = pl.multiple_of((1 + step * terms + term) * fan_in, fan_in)
        turned[pl.ds(start, fan_in), :] = part.T
        total = total + jnp.dot(part, weights[1 + term][0], preferred_element_type=jnp.float32)
    mixed[...] = total


def layer_one_kernel(
    powers_ref,
    all_ref,
    own_ref,
    weight_0,
    weight_a,
    weight_b,
    weight_c,
    bias_ref,
    gain_ref,
    shift_ref,
    valid_ref,
    hidden_ref,
    turned_ref,
    mixed_ref,
):
    step = pl.program_id(0)
    weights = (weight_0, weight_a, weight_b, weight_c)
    forward_step(step, powers_ref, all_ref, own_ref, weights, bias_ref, turned_ref, mixed_ref)

    @pl.when(step == pl.num_programs(0) - 1)
    def finish_layer():
        normed, ignored = norm_forward(mixed_ref[...])
        hidden = (normed * gain_ref[...] + shift_ref[...]) * valid_ref[...]
        hidden_ref[...] = hidden.astype(jnp.bfloat16)


def layer_two_kernel(
    place_ref,
    powers_ref,
    all_ref,
    own_ref,
    weight_0,
    weight_a,
    weight_b,
    weight_c,
    bias_ref,
    gain_ref,
    shift_ref,
    valid_ref,
    upstream_ref,
    active_ref,
    low_ref,
    rest_ref,
    mine_ref,
    other_ref,
    turned,
    mixed,
):
    step = pl.program_id(0)
    weights = (weight_0, weight_a, weight_b, weight_c)
    forward_step(step, powers_ref, all_ref, own_ref, weights, bias_ref, turned, mixed)

    @pl.when(step == pl.num_programs(0) - 1)
    def finish_layer():
        normed, ignored = norm_forward(mixed[...])
        active = (normed * gain_ref[...] + shift_ref[...]) * valid_ref[...]
        active_ref[...] = active.astype(jnp.bfloat16)
        low, rest = norm_backward(
            mixed[...], upstream_ref[...].astype(jnp.float32), gain_ref[...], valid_ref[...]
        )
        low_ref[...] = low
        for place in range(3):
            rest_ref[place : place + 1, :] = rest[place]
        weight_gradient(turned, low, place_ref[1], mine_ref, other_ref)


def backward_step(step, powers_ref, all_ref, own_ref, weights, total):
    terms, own_cap, span = powers_ref.shape
    transposed = (((1,), (1,)), ((), ()))

    @pl.when(step == 0)
    def first():
        total[...] = lax.dot_general(
            own_ref[...], weights[0][0], transposed, preferred_element_type=jnp.float32
        )

    low = jnp.dot(
        powers_ref[...].reshape(terms * own_cap, span),
        all_ref[...],
        preferred_element_type=jnp.float32,
    ).astype(jnp.bfloat16)
    value = total[...]
    for term in range(terms):
        value = value + lax.dot_general(
            low[term * own_cap : (term + 1) * own_cap],
            weights[1 + term][0],
            transposed,
            preferred_element_type=jnp.float32,
        )
    total[...] = value


def back_two_kernel(
    place_ref,
    powers_ref,
    all_ref,
    own_ref,
    weight_0,
    weight_a,
    weight_b,
    weight_c,
    turned_ref,
    mixed_ref,
    gain_ref,
    valid_ref,
    rest_ref,
    low_ref,
    mine_ref,
    other_ref,
    total,
):
    step = pl.program_id(0)
    weights = (weight_0, weight_a, weight_b, weight_c)
    backward_step(step, powers_ref, all_ref, own_ref, weights, total)

    @pl.when(step == pl.num_programs(0) - 1)
    def finish_layer():
        low, rest = norm_backward(mixed_ref[...], total[...], gain_ref[...], valid_ref[...])
        low_ref[...] = low
        weight_gradient(turned_ref, low, place_ref[1], mine_ref, other_ref)
        part = turned_ref.shape[0] // 2
        extra = jnp.zeros((1, mine_ref.shape[1] - part, mine_ref.shape[2]), jnp.bfloat16)
        rows = rest + [rest_ref[place : place + 1, :] for place in range(3)]
        rows = jnp.concatenate(rows + [jnp.zeros((10, rows[0].shape[1]), jnp.float32)], axis=0)

        def below(first_ref, second_ref):
            first_ref[:, part:, :] = extra
            second_ref[:, part:, :] = extra
            first_ref[0, part : part + 16, :] = rows.astype(jnp.bfloat16)

        @pl.when(place_ref[1] == 0)
        def low_half_here():
            below(mine_ref, other_ref)

        @pl.when(place_ref[1] == 1)
        def low_half_there():
            below(other_ref, mine_ref)


def back_one_kernel(
    powers_ref, all_ref, own_ref, weight_0, weight_a, weight_b, weight_c, out_ref, total
):
    step = pl.program_id(0)
    weights = (weight_0, weight_a, weight_b, weight_c)
    backward_step(step, powers_ref, all_ref, own_ref, weights, total)

    @pl.when(step == pl.num_programs(0) - 1)
    def finish_layer():
        out_ref[...] = total[...].astype(jnp.bfloat16)


def layer_pass(kernel, name, place, powers, everyone, own, weight, others, outs, scratch):
    ignored, own_cap, span = powers.shape
    fan_in, width = weight.shape[1:]

    def whole(value):
        return pl.BlockSpec(value.shape, lambda step: (0,) * len(value.shape))

    def term_weight(term):
        return pl.BlockSpec((1, fan_in, width), lambda step: (1 + step * TERMS + term, 0, 0))

    in_specs = [
        pl.BlockSpec((TERMS, own_cap, span), lambda step: (step, 0, 0)),
        whole(everyone),
        whole(own),
        pl.BlockSpec((1, fan_in, width), lambda step: (0, 0, 0)),
    ]
    in_specs += [term_weight(term) for term in range(TERMS)] + [whole(value) for value in others]
    operands = [powers, everyone, own] + [weight] * (1 + TERMS) + list(others)
    if place is not None:
        in_specs = [pl.BlockSpec(memory_space=pltpu.SMEM)] + in_specs
        operands = [place] + operands
    return pl.pallas_call(
        kernel,
        grid=((ORDER - 1) // TERMS,),
        out_shape=outs,
        in_specs=in_specs,
        out_specs=[whole(value) for value in outs],
        scratch_shapes=[pltpu.VMEM(shape, dtype) for shape, dtype in scratch],
        compiler_params=pltpu.CompilerParams(vmem_limit_bytes=VMEM_BYTES),
        cost_estimate=NO_COST,
        name=name,
    )(*operands)


def finish_kernel(scalars_ref, pair_ref, siblings_ref, other_ref, out_ref, *small_refs):
    step = pl.program_id(0)
    part = out_ref.shape[1]
    held = pl.num_programs(0) // 2
    for here, values_ref in ((step < held, pair_ref), (step >= held, siblings_ref)):
        @pl.when(here & (scalars_ref[0] == 1))
        def fast_form():
            out_ref[0] = values_ref[0, :part, :].astype(jnp.float32)

        for small_ref in small_refs:
            @pl.when(here & (scalars_ref[1 + step] == 0))
            def small_sums():
                small_ref[...] = values_ref[0, part : part + 16, :].astype(jnp.float32)

    @pl.when(scalars_ref[0] == 0)
    def general_form():
        out_ref[0] = other_ref[0].astype(jnp.float32)


def finished(scalars, pair, siblings, other, with_small=False):
    count, part, width = other.shape
    out, held = (1, part, width), (1,) + pair.shape[1:]
    out_specs = [pl.BlockSpec(out, lambda step, ref: (ref[1 + step], 0, 0))]
    out_shape = [jax.ShapeDtypeStruct(other.shape, jnp.float32)]
    if with_small:
        out_specs.append(pl.BlockSpec((16, width), lambda step, ref: (0, 0)))
        out_shape.append(jax.ShapeDtypeStruct((16, width), jnp.float32))
    return pl.pallas_call(
        finish_kernel,
        grid_spec=pltpu.PrefetchScalarGridSpec(
            num_scalar_prefetch=1,
            grid=(count,),
            in_specs=[
                pl.BlockSpec(held, lambda step, ref: (jnp.minimum(step, count // 2 - 1), 0, 0)),
                pl.BlockSpec(held, lambda step, ref: (jnp.maximum(step - count // 2, 0), 0, 0)),
                pl.BlockSpec(out, lambda step, ref: ((1 - ref[0]) * ref[1 + step], 0, 0)),
            ],
            out_specs=out_specs,
        ),
        out_shape=out_shape,
        compiler_params=pltpu.CompilerParams(vmem_limit_bytes=VMEM_BYTES),
        cost_estimate=pl.CostEstimate(
            flops=other.size, bytes_accessed=6 * other.size, transcendentals=0
        ),
        name="finished",
    )(scalars, pair, siblings, other)


def unpack_kernel(place_ref, pieces_ref, keys_ref, own_ref, quadrant_ref, columns, hot):
    groups, high, lanes = pieces_ref.shape
    own_cap, span = own_ref.shape
    whole = own_cap // lanes
    send_cap = keys_ref.shape[1] // groups
    half, rest = send_cap // 2, own_cap - whole * lanes
    for group in range(groups):
        start = group * send_cap
        for tile in range(whole):
            columns[start : start + send_cap, tile * lanes : (tile + 1) * lanes] = pieces_ref[
                group, tile * send_cap : (tile + 1) * send_cap, :
            ]
        ends = pieces_ref[group, whole * send_cap :, :]
        columns[start : start + half, whole * lanes :] = ends[:, :rest]
        columns[start + half : start + send_cap, whole * lanes :] = ends[:, rest:]
    standing = lax.broadcasted_iota(jnp.int32, hot.shape, 0)
    hot[...] = jnp.where(standing == keys_ref[...], 1.0, 0.0).astype(jnp.bfloat16)
    block = jnp.dot(hot[...], columns[...], preferred_element_type=jnp.float32)
    own_ref[...] = block.T.astype(jnp.bfloat16)
    middle = span // 2

    @pl.when(place_ref[0] == 0)
    def first():
        quadrant_ref[...] = own_ref[:, :middle]

    @pl.when(place_ref[0] == 1)
    def second():
        quadrant_ref[...] = own_ref[:, middle:]


def unpacked_block(pieces, keys, place, own_cap, span):
    vector = pl.BlockSpec(memory_space=pltpu.VMEM)
    return pl.pallas_call(
        unpack_kernel,
        out_shape=[
            jax.ShapeDtypeStruct((own_cap, span), jnp.bfloat16),
            jax.ShapeDtypeStruct((own_cap, span // 2), jnp.bfloat16),
        ],
        in_specs=[pl.BlockSpec(memory_space=pltpu.SMEM), vector, vector],
        out_specs=[vector, vector],
        scratch_shapes=[
            pltpu.VMEM((keys.shape[1], own_cap), jnp.bfloat16),
            pltpu.VMEM((span, keys.shape[1]), jnp.bfloat16),
        ],
        compiler_params=pltpu.CompilerParams(vmem_limit_bytes=VMEM_BYTES),
        cost_estimate=NO_COST,
        name="unpacked_block",
    )(place, pieces, keys)


def fit_kernel(codes_ref, out_ref, *, n_row, caps):
    own_cap, send_cap, seat_cap = caps
    codes = codes_ref[...]
    devices = codes.shape[0]
    n_col = devices // n_row
    label = lax.broadcasted_iota(jnp.int32, (devices, 128), 1)
    counts = jnp.zeros((devices, 128), jnp.float32)
    for cluster in range(CLUSTERS):
        here = jnp.where(codes == 2 * cluster + 1, 1.0, 0.0)
        counts = counts + jnp.where(
            label == cluster, jnp.sum(here, axis=1, keepdims=True), 0.0
        )
    sizes = jnp.sum(counts, axis=0, keepdims=True)
    across = jnp.broadcast_to(sizes, (128, 128))
    down = across.T
    first = lax.broadcasted_iota(jnp.int32, (128, 128), 0)
    second = lax.broadcasted_iota(jnp.int32, (128, 128), 1)
    ahead = (across > down) | ((across == down) & (second < first))
    ahead = ahead & (second < CLUSTERS)
    rank = jnp.sum(jnp.where(ahead, 1.0, 0.0), axis=1, keepdims=True).astype(jnp.int32)
    others = n_row - 1
    later = rank > others
    turn = jnp.zeros_like(rank)
    for count in range(1, CLUSTERS // others + 1):
        turn = turn + jnp.where(rank - 1 >= count * others, 1, 0)
    place = rank - 1 - turn * others
    group = jnp.where(rank == 0, 0, 1 + jnp.where(later, others - 1 - place, place))
    member = (group == second) & (first < CLUSTERS)
    held = jnp.dot(
        counts.astype(jnp.bfloat16),
        jnp.where(member, 1.0, 0.0).astype(jnp.bfloat16),
        preferred_element_type=jnp.float32,
    )
    by_row = jnp.zeros((1, 128), jnp.float32)
    for row in range(n_row):
        rows = jnp.sum(held[row * n_col : (row + 1) * n_col], axis=0, keepdims=True)
        by_row = jnp.maximum(by_row, rows)
    device = lax.broadcasted_iota(jnp.int32, (devices, 128), 0)
    by_col = jnp.zeros((1, 128), jnp.float32)
    for col in range(n_col):
        cols = jnp.where(device % n_col == col, held, 0.0)
        by_col = jnp.maximum(by_col, jnp.sum(cols, axis=0, keepdims=True))
    fits = (
        (jnp.max(by_col) <= own_cap) & (jnp.max(by_row) <= send_cap) & (jnp.max(held) <= seat_cap)
    )
    out_ref[0] = jnp.where(fits, 1, 0)


def fits_in(codes, n_row, caps):
    fits = pl.pallas_call(
        functools.partial(fit_kernel, n_row=n_row, caps=caps),
        out_shape=jax.ShapeDtypeStruct((1,), jnp.int32),
        in_specs=[pl.BlockSpec(memory_space=pltpu.VMEM)],
        out_specs=pl.BlockSpec(memory_space=pltpu.SMEM),
        cost_estimate=NO_COST,
        name="fits",
    )(codes.reshape(-1, codes.shape[-1]))
    return fits


def exclusive_counts(member):
    count = member.shape[-1]
    before = jnp.arange(count)[:, None] < jnp.arange(count)[None, :]
    return jnp.dot(
        member.astype(jnp.bfloat16),
        before.astype(jnp.bfloat16),
        preferred_element_type=jnp.float32,
    ).astype(jnp.int32)


def assign(codes, n_row):
    cluster, valid = codes >> 1, codes & 1
    labels = jnp.arange(CLUSTERS)
    sizes = jnp.sum(
        (cluster.reshape(1, -1) == labels[:, None]) & (valid.reshape(1, -1) == 1), axis=1
    )
    ahead = (sizes[None, :] > sizes[:, None]) | (
        (sizes[None, :] == sizes[:, None]) & (labels[None, :] < labels[:, None])
    )
    rank = jnp.sum(ahead, axis=1)
    others = n_row - 1
    turn, place = (rank - 1) // others, (rank - 1) % others
    group = jnp.where(rank == 0, 0, 1 + jnp.where(turn == 0, place, others - 1 - place))
    of_node = jnp.sum(
        jnp.where(cluster[None] == labels[:, None, None, None], group[:, None, None, None], 0),
        axis=0,
    )
    return jnp.where(valid == 1, of_node, n_row)


def compact(
    codes,
    group,
    features,
    block_keep,
    edge_weight,
    weight_one,
    bias_one,
    gain_one,
    shift_one,
    weight_two,
    bias_two,
    gain_two,
    shift_two,
    cotangent,
    places_of,
    slots_of,
    seats_of,
    decide,
    sizes,
    caps,
):
    row, col = lax.axis_index("row"), lax.axis_index(COL)
    chip, core = lax.axis_index("chip"), lax.axis_index("core")
    n_row, n_col = sizes
    own_cap, send_cap, seat_cap = caps
    own_nodes, in_width = features.shape
    width = weight_two.shape[2]
    span = n_col * own_cap
    targets = jnp.arange(n_row)

    def in_col(value):
        return lax.dynamic_index_in_dim(value, col, 1, False).reshape(-1)

    def in_row(value):
        return lax.dynamic_index_in_dim(value, row, 0, False).reshape(-1)

    row_group, col_group = in_row(group), in_col(group)
    row_slots, col_places = in_row(slots_of(group)), in_col(places_of(group))
    row_keys = jnp.where(row_slots < send_cap, row_group * send_cap + row_slots, -1)
    col_keys = jnp.where(col_places < own_cap, col_group * own_cap + col_places, -1)
    pieces = packed_pieces(
        block_keep,
        in_row(codes),
        in_col(codes),
        row_keys,
        col_keys,
        edge_weight,
        (own_cap, send_cap),
        n_row,
    )
    pieces, codes = lax.optimization_barrier((pieces, codes))
    group = assign(codes, n_row)
    places, slots, seats = places_of(group), slots_of(group), seats_of(group)

    standing = jnp.arange(n_col)[None, :, None] * own_cap + places
    fits_here = jnp.where(group == row, standing, -1).reshape(n_row, -1)
    slot_of = slots.reshape(n_row, -1)
    target = jnp.max(
        jnp.where(
            slot_of[:, None, :] == jnp.arange(send_cap)[None, :, None], fits_here[:, None, :], -1
        ),
        axis=2,
    )
    keys = target.reshape(1, -1)

    def to_partner(value, step):
        return lax.ppermute(value, "row", [(place, place ^ step) for place in range(n_row)])

    partners = row ^ targets
    group_here = lax.dynamic_index_in_dim(in_row(group).reshape(n_col, -1), col, 0, False)
    seat_here = lax.dynamic_index_in_dim(in_row(seats).reshape(n_col, -1), col, 0, False)

    def seat_of_node(groups):
        hot = (group_here[None, None, :] == groups[:, None, None]) & (
            seat_here[None, None, :] == jnp.arange(seat_cap)[None, :, None]
        )
        return hot.astype(jnp.bfloat16).reshape(n_row * seat_cap, own_nodes)

    enter_home = seat_of_node(targets).T
    enter_partner = seat_of_node(partners)
    both = jnp.dot(enter_partner, jnp.concatenate([features, cotangent], axis=1))
    both = both.reshape(n_row, seat_cap, -1)
    enter_partner = enter_partner.T
    pieces = trade(pieces, "row")
    both, codes = lax.optimization_barrier((both, codes))
    fits, others = decide(codes)
    group_col = lax.dynamic_index_in_dim(group, col, 1, False)
    seats_col = lax.dynamic_index_in_dim(seats, col, 1, False)
    places_col = lax.dynamic_index_in_dim(places, col, 1, False)
    seated = (group_col == row)[:, None, :] & (
        seats_col[:, None, :] == jnp.arange(seat_cap)[None, :, None]
    )
    place_of_seat = jnp.max(jnp.where(seated, places_col[:, None, :], -1), axis=2)
    from_partner = jnp.max(
        jnp.where((partners[:, None] == targets)[:, :, None], place_of_seat[None], -1), axis=1
    )
    arrive = from_partner.reshape(1, -1) == jnp.arange(own_cap)[:, None]
    arrive = arrive.astype(jnp.bfloat16)
    leave_group = place_of_seat.reshape(-1, 1) == jnp.arange(own_cap)
    leave_group = leave_group.astype(jnp.bfloat16)
    leave_partner = jnp.concatenate([from_partner[::2], from_partner[1::2]])
    leave_partner = leave_partner.reshape(-1, 1) == jnp.arange(own_cap)
    leave_partner = leave_partner.astype(jnp.bfloat16)
    held_count = jnp.sum(group_col == row)
    valid_rows = (jnp.arange(own_cap) < held_count).astype(jnp.float32)[:, None]
    place = jnp.stack([chip, core]).astype(jnp.int32)
    quarters = jnp.stack([col, (1 - chip) * 2 + core, chip * 2 + 1 - core, 3 - col])
    quarters = jnp.concatenate([fits, quarters.astype(jnp.int32)])
    own_halves = jnp.concatenate([fits, jnp.stack([core, 1 - core]).astype(jnp.int32)])
    scalars = (chip, 1 - chip, col * own_cap)
    scalars = tuple(value.astype(jnp.uint32) for value in scalars) + (chip == 0, core == 0, place)
    scalars = scalars + (quarters, own_halves)
    homes = enter_home, enter_partner, leave_group, leave_partner
    pieces, both, keys, arrive, homes, valid_rows, others, scalars = lax.optimization_barrier(
        (pieces, both, keys, arrive, homes, valid_rows, others, scalars)
    )
    enter_home, enter_partner, leave_group, leave_partner = homes
    this_chip, other_chip, own_start, first_chip, first_core = scalars[:5]
    place, quarters, own_halves = scalars[5:]

    own_block, quadrant = unpacked_block(pieces, keys, place, own_cap, span)
    quadrant = swap(quadrant, "chip")
    both = [both[0]] + [to_partner(both[step], step) for step in range(1, n_row)]
    sibling = swap(own_block, "core")
    quadrant, *early = lax.optimization_barrier((quadrant, *both[:-2]))
    adjacency = normalized_block(own_block, sibling, quadrant, swap(quadrant, "core"), place)
    adjacency, *late = lax.optimization_barrier((adjacency, *both[-2:]))
    both = early + late
    mine = jnp.dot(arrive, jnp.concatenate(both))
    features_own, cotangent_own = mine[:, :in_width], mine[:, in_width:]
    sibling = swap(features_own, "core")

    first = (own_start + jnp.arange(own_cap, dtype=jnp.uint32))[:, None]
    first = first == jnp.arange(span, dtype=jnp.uint32)[None, :]
    previous = first.astype(jnp.float32)
    current = -lax.dynamic_slice_in_dim(adjacency, own_start, own_cap, 0).astype(jnp.float32)
    lowered = [current.astype(jnp.bfloat16)]
    for position in range(2, ORDER):
        upcoming = (
            -2.0 * jnp.dot(lowered[-1], adjacency, preferred_element_type=jnp.float32) - previous
        )
        low = upcoming.astype(jnp.bfloat16)
        if position == 4:
            low, sibling = lax.optimization_barrier((low, sibling))
            features_chip = joined(features_own, sibling, first_core)
            partner = swap(features_chip, "chip")
        if position == 8:
            low, partner = lax.optimization_barrier((low, partner))
            features_all = joined(features_chip, partner, first_chip)
        previous, current = current, upcoming
        lowered.append(low)
    powers = jnp.concatenate(lowered, axis=0).reshape(ORDER - 1, own_cap, span)

    def everywhere(value_low):
        return lax.all_gather(value_low, COL, axis=0, tiled=True)

    def chosen(value, other):
        return jnp.where(quarters[0] == 1, value.astype(jnp.float32), other.astype(jnp.float32))

    def shaped(*shape, dtype=jnp.bfloat16):
        return jax.ShapeDtypeStruct(shape, dtype)

    part_one, part_two = ORDER * in_width // 2, ORDER * width // n_col
    padded = -(-(part_one + 16) // (16 * n_row)) * (16 * n_row)
    hidden, turned_one, mixed_one = layer_pass(
        layer_one_kernel,
        "layer_one",
        None,
        powers,
        features_all,
        features_own,
        weight_one,
        [bias_one[None], gain_one[None], shift_one[None], valid_rows],
        [
            shaped(own_cap, width),
            shaped(2 * part_one, own_cap),
            shaped(own_cap, width, dtype=jnp.float32),
        ],
        [],
    )
    activations, low_two, rest_two, mine, other = layer_pass(
        layer_two_kernel,
        "layer_two",
        place,
        powers,
        everywhere(hidden),
        hidden,
        weight_two,
        [bias_two[None], gain_two[None], shift_two[None], valid_rows, cotangent_own],
        [
            shaped(own_cap, width),
            shaped(own_cap, width),
            shaped(3, width, dtype=jnp.float32),
            shaped(2, part_two, width),
            shaped(2, part_two, width),
        ],
        [((n_col * part_two, own_cap), jnp.bfloat16), ((own_cap, width), jnp.float32)],
    )

    def add_cores(mine, other, axis=0):
        got = swap(other, "core")
        return tuple(
            added(
                lax.dynamic_index_in_dim(mine, index, axis, False),
                lax.dynamic_index_in_dim(got, index, axis, False),
            )
            for index in (this_chip, other_chip)
        )

    leaving = jnp.dot(leave_partner, activations).reshape(n_row, seat_cap, width)
    near, far = leaving[: n_row // 2], leaving[n_row // 2 :]
    far = to_partner(far, 1)
    here, there = add_cores(mine, other)
    everyone_two, there, far = lax.optimization_barrier((everywhere(low_two), there, far))
    there = swap(there, "chip")
    arrived = [jnp.stack([near[0], far[0]])] + [
        to_partner(jnp.stack([near[half], far[half]]), 2 * half) for half in range(1, n_row // 2)
    ]
    low_one, mine, other = layer_pass(
        back_two_kernel,
        "back_two",
        place,
        powers,
        everyone_two,
        low_two,
        weight_two,
        [turned_one, mixed_one, gain_one[None], valid_rows, rest_two],
        [shaped(own_cap, width), shaped(1, padded, width), shaped(1, padded, width)],
        [((own_cap, width), jnp.float32)],
    )
    low_one, there, arrived = lax.optimization_barrier((low_one, there, arrived))
    second = added(here, there).reshape(n_row, -1, width)
    many = second.shape[1]
    low_one, second = lax.optimization_barrier((low_one, second))
    second = trade(second, "row")
    mine, other = (value.reshape(n_row, 2, -1, width) for value in (mine, other))
    here, there = add_cores(mine, other, 1)
    there = swap(there, "chip")
    first = added(here, there)
    second = jnp.sum(second.astype(jnp.float32), axis=0).astype(jnp.bfloat16)
    second = jnp.broadcast_to(second[None], (n_row,) + second.shape)
    mixed = jnp.concatenate([second, first], axis=1)
    low_one, mixed = lax.optimization_barrier((low_one, mixed))
    everyone_one = everywhere(low_one)
    mixed = trade(mixed, "row")
    (input_grad,) = layer_pass(
        back_one_kernel,
        "back_one",
        None,
        powers,
        everyone_one,
        low_one,
        weight_one,
        [],
        [shaped(own_cap, in_width)],
        [((own_cap, in_width), jnp.float32)],
    )
    leaving = jnp.dot(leave_group, input_grad)
    leaving = leaving.reshape(n_row, seat_cap * in_width // width, width)
    arrived = jnp.concatenate(arrived).reshape(-1, width)
    home = jnp.dot(enter_partner, arrived, preferred_element_type=jnp.float32)
    home = chosen(home, others[0])
    mixed, leaving, home = lax.optimization_barrier((mixed, leaving, home))
    first = jnp.sum(mixed[:, many:].astype(jnp.float32), axis=0).astype(jnp.bfloat16)
    partner, mixed = lax.optimization_barrier((swap(first, "chip"), mixed))
    second = mixed[:, :many].reshape(1, -1, width)
    partner_two = swap(second, "chip")
    first = joined(first, partner, first_chip)
    share = first.shape[0]
    first = jnp.broadcast_to(first[None], (n_row,) + first.shape)
    first = trade(jnp.concatenate([first, leaving], axis=1), "row")
    second = jnp.concatenate([second, partner_two])
    (second,) = finished(quarters, second, swap(second, "core"), others[3])
    first, second = lax.optimization_barrier((first, second))
    mine = first[:, :share].reshape(1, -1, width)
    siblings = swap(mine, "core")
    back = first[:, share:].reshape(n_row * seat_cap, in_width)
    home_grad = jnp.dot(enter_home, back, preferred_element_type=jnp.float32)
    home_grad = chosen(home_grad, others[1])
    first, small = finished(own_halves, mine, siblings, others[2], True)
    return home, home_grad, first, second, chosen(small[:6], others[4])


def general(
    codes,
    features,
    block_keep,
    edge_weight,
    weight_one,
    bias_one,
    gain_one,
    shift_one,
    weight_two,
    bias_two,
    gain_two,
    shift_two,
    cotangent,
    node_valid,
):
    row, col = lax.axis_index("row"), lax.axis_index(COL)
    row_codes = lax.dynamic_index_in_dim(codes, row, 0, False).reshape(-1)
    col_codes = lax.dynamic_index_in_dim(codes, col, 1, False).reshape(-1)
    tile_rows, tile_cols = edge_weight.shape
    blocks_down, blocks_across = block_keep.shape
    block_side = tile_rows // blocks_down
    linked = (row_codes[:, None] == col_codes[None, :]) & (row_codes[:, None] & 1 == 1)
    linked = linked.reshape(blocks_down, block_side, blocks_across, block_side) & (
        block_keep[:, None, :, None] == 1
    )
    masked = edge_weight * linked.reshape(tile_rows, tile_cols).astype(jnp.bfloat16)
    degree_rows = 1.0 + lax.psum(jnp.sum(masked, axis=1, dtype=jnp.float32), COL)
    own_nodes = features.shape[0]
    own_degree = lax.dynamic_slice_in_dim(
        degree_rows, lax.axis_index(COL) * own_nodes, own_nodes, 0
    )
    degree_cols = lax.all_gather(own_degree, "row", axis=0, tiled=True)
    adjacency = (
        masked.astype(jnp.float32)
        * lax.rsqrt(degree_rows)[:, None]
        * lax.rsqrt(degree_cols)[None, :]
    ).astype(jnp.bfloat16)
    valid_rows = node_valid.astype(jnp.float32)
    stacked_one, mixed_one, hidden = layer_forward(
        adjacency,
        features.astype(jnp.float32),
        weight_one,
        bias_one,
        gain_one,
        shift_one,
        valid_rows,
    )
    stacked_two, mixed_two, activations = layer_forward(
        adjacency, hidden, weight_two, bias_two, gain_two, shift_two, valid_rows
    )
    hidden_grad, weight_two_grad, bias_two_grad, gain_two_grad, shift_two_grad = layer_backward(
        adjacency,
        stacked_two,
        mixed_two,
        cotangent.astype(jnp.float32),
        weight_two,
        gain_two,
        shift_two,
        valid_rows,
    )
    input_grad, weight_one_grad, bias_one_grad, gain_one_grad, shift_one_grad = layer_backward(
        adjacency, stacked_one, mixed_one, hidden_grad, weight_one, gain_one, shift_one, valid_rows
    )
    summed = lax.psum(
        (
            weight_one_grad,
            bias_one_grad,
            gain_one_grad,
            shift_one_grad,
            weight_two_grad,
            bias_two_grad,
            gain_two_grad,
            shift_two_grad,
        ),
        ("row",) + COL,
    )
    weight_one_grad, bias_one_grad, gain_one_grad, shift_one_grad = (
        summed[0],
        summed[1],
        summed[2],
        summed[3],
    )
    weight_two_grad, bias_two_grad, gain_two_grad, shift_two_grad = (
        summed[4],
        summed[5],
        summed[6],
        summed[7],
    )
    return (
        activations,
        input_grad,
        weight_one_grad,
        bias_one_grad,
        gain_one_grad,
        shift_one_grad,
        weight_two_grad,
        bias_two_grad,
        gain_two_grad,
        shift_two_grad,
    )


def local(n_row, n_col, *args):
    (
        features,
        node_valid,
        cluster,
        block_keep,
        edge_weight,
        weight_one,
        bias_one,
        gain_one,
        shift_one,
        weight_two,
        bias_two,
        gain_two,
        shift_two,
        cotangent,
    ) = args
    own_nodes, in_width = features.shape
    own_cap = own_nodes * n_row * 5 // 16
    send_cap = own_nodes * n_col * 11 // 32
    seat_cap = own_nodes * 7 // 16
    codes = broadcast_along(cluster * 2 + node_valid, ("row",) + COL, n_row * n_col)
    codes = codes.reshape(n_row, n_col, own_nodes)
    shared = (
        block_keep,
        edge_weight,
        weight_one,
        bias_one,
        gain_one,
        shift_one,
        weight_two,
        bias_two,
        gain_two,
        shift_two,
        cotangent,
    )

    def slow():
        return general(codes, features, *shared, node_valid)

    held = (ORDER - 1) * own_cap * own_cap * n_col * 2
    if held > HELD_BYTES or n_col != 4 or n_row < 2 or n_row & (n_row - 1):
        return slow()
    group = assign(codes, n_row)

    def member_of(group):
        return group[None] == jnp.arange(n_row)[:, None, None, None]

    def places_of(group):
        member = member_of(group).transpose(0, 2, 1, 3).reshape(n_row, n_col, -1)
        places = jnp.sum(jnp.where(member, exclusive_counts(member), 0), axis=0)
        return places.reshape(n_col, n_row, own_nodes).transpose(1, 0, 2)

    def slots_of(group):
        member = member_of(group).reshape(n_row, n_row, -1)
        slots = jnp.sum(jnp.where(member, exclusive_counts(member), 0), axis=0)
        return slots.reshape(n_row, n_col, own_nodes)

    def seats_of(group):
        member = member_of(group)
        return jnp.sum(jnp.where(member, exclusive_counts(member), 0), axis=0)

    width = weight_two.shape[2]

    def instead(state):
        made = slow()
        small = jnp.stack([made[place] for place in (3, 4, 5, 7, 8, 9)])
        return (jnp.ones_like(state[0]),) + tuple(
            value.astype(jnp.bfloat16).reshape(like.shape)
            for value, like in zip((made[0], made[1], made[2], made[6], small), state[1:])
        )

    shapes = (
        (own_nodes, width),
        (own_nodes, in_width),
        (2, ORDER * in_width // 2, width),
        (n_col, ORDER * width // n_col, width),
        (6, width),
    )

    def decide(codes):
        fits = fits_in(codes, n_row, (own_cap, send_cap, seat_cap))
        others = lax.while_loop(
            lambda state: state[0][0] == 0,
            instead,
            (fits,) + tuple(jnp.zeros(shape, jnp.bfloat16) for shape in shapes),
        )[1:]
        return fits, others

    home, home_grad, first, second, small = compact(
        codes,
        group,
        features,
        *shared,
        places_of,
        slots_of,
        seats_of,
        decide,
        (n_row, n_col),
        (own_cap, send_cap, seat_cap),
    )
    return (
        home,
        home_grad,
        first.reshape(weight_one.shape),
        small[0],
        small[1],
        small[2],
        second.reshape(weight_two.shape),
        small[3],
        small[4],
        small[5],
    )


def solution(mesh):
    n_row, n_col = mesh.shape["row"], mesh.shape["col"]
    by_core = jax.sharding.Mesh(
        mesh.devices.reshape(n_row, n_col // 2, 2), ("row", "chip", "core")
    )
    nodes = ("row", "chip", "core")
    placed = (
        P(nodes, None),
        P(nodes),
        P(nodes),
        P("row", COL),
        P("row", COL),
        P(),
        P(),
        P(),
        P(),
        P(),
        P(),
        P(),
        P(),
        P(nodes, None),
    )
    return jax.shard_map(
        functools.partial(local, n_row, n_col),
        mesh=by_core,
        in_specs=placed,
        out_specs=(P(nodes, None), P(nodes, None), P(), P(), P(), P(), P(), P(), P(), P()),
        check_vma=False,
    )
```

```python
import functools
import math

import jax
import jax.numpy as jnp
from jax import lax
from jax.experimental import pallas as pl
from jax.experimental.pallas import tpu as pltpu
from jax.sharding import PartitionSpec as P

ORDER = 13
CLUSTERS = 16
HELD_BYTES = 1 << 25
VMEM_BYTES = 32 << 20
TERMS = 3
NO_COST = pl.CostEstimate(flops=1, bytes_accessed=1, transcendentals=0)
COL = ("chip", "core")


def finish(mixed, gain, shift, valid_rows):
    active = jax.nn.gelu(mixed, approximate=False)
    centered = active - jnp.mean(active, axis=-1, keepdims=True)
    variance = jnp.mean(centered * centered, axis=-1, keepdims=True)
    return (centered * lax.rsqrt(variance + 1e-05) * gain + shift) * valid_rows[:, None]


def forward_product(adjacency, piece_low):
    partial_value = jnp.dot(
        adjacency,
        lax.all_gather(piece_low, "row", axis=0, tiled=True),
        preferred_element_type=jnp.float32,
    )
    return lax.psum_scatter(partial_value, COL, scatter_dimension=0, tiled=True)


def backward_product(adjacency, piece_low):
    partial_value = lax.dot_general(
        adjacency,
        lax.all_gather(piece_low, COL, axis=0, tiled=True),
        (((0,), (0,)), ((), ())),
        preferred_element_type=jnp.float32,
    )
    return lax.psum_scatter(
        partial_value.astype(jnp.bfloat16), "row", scatter_dimension=0, tiled=True
    ).astype(jnp.float32)


def layer_forward(adjacency, inputs, weight, bias, gain, shift, valid_rows):
    first_low = inputs.astype(jnp.bfloat16)
    second = -forward_product(adjacency, first_low)
    second_low = second.astype(jnp.bfloat16)

    def advance(state_pair, unused):
        previous, current, current_low = state_pair
        upcoming = -2.0 * forward_product(adjacency, current_low) - previous
        upcoming_low = upcoming.astype(jnp.bfloat16)
        return ((current, upcoming, upcoming_low), upcoming_low)

    ignored, others = lax.scan(advance, (inputs, second, second_low), None, length=ORDER - 2)
    stacked = jnp.concatenate([first_low[None], second_low[None], others], axis=0)
    mixed = jnp.einsum("kni,kio->no", stacked, weight, preferred_element_type=jnp.float32) + bias
    return (stacked, mixed, finish(mixed, gain, shift, valid_rows))


def layer_backward(adjacency, stacked, mixed, upstream, weight, gain, shift, valid_rows):

    def local_finish(mixed_in, gain_in, shift_in):
        return finish(mixed_in, gain_in, shift_in, valid_rows)

    ignored, pullback = jax.vjp(local_finish, mixed, gain, shift)
    mixed_grad, gain_grad, shift_grad = pullback(upstream)
    mixed_low = mixed_grad.astype(jnp.bfloat16)
    bias_grad = jnp.sum(mixed_low.astype(jnp.float32), axis=0)
    weight_grad = jnp.einsum("kni,no->kio", stacked, mixed_low, preferred_element_type=jnp.float32)
    direct = jnp.einsum("no,kio->kni", mixed_low, weight, preferred_element_type=jnp.float32)

    def retreat(state_pair, direct_term):
        later_two, later_one = state_pair
        current = (
            direct_term
            - 2.0 * backward_product(adjacency, later_one.astype(jnp.bfloat16))
            - later_two
        )
        return ((later_one, current), None)

    start_pair = (jnp.zeros_like(direct[0]), direct[ORDER - 1])
    (second_grad, first_grad), unused = lax.scan(
        retreat, start_pair, direct[1 : ORDER - 1], reverse=True
    )
    input_grad = (
        direct[0] - backward_product(adjacency, first_grad.astype(jnp.bfloat16)) - second_grad
    )
    return (input_grad, weight_grad, bias_grad, gain_grad, shift_grad)


def swap(value, axis):
    return lax.ppermute(value, axis, [(0, 1), (1, 0)])


def trade(pieces, axis):
    return lax.all_to_all(pieces, axis, 0, 0, tiled=False)


def broadcast_along(value, axis, size):
    return trade(jnp.broadcast_to(value[None], (size,) + value.shape), axis)


def joined(mine, other, mine_first):
    return jnp.where(
        mine_first, jnp.concatenate([mine, other]), jnp.concatenate([other, mine])
    )


def added(mine, received):
    return (mine.astype(jnp.float32) + received.astype(jnp.float32)).astype(jnp.bfloat16)


def assemble(place_ref, own_ref, sibling_ref, near_ref, far_ref, out_ref, done):
    chip, core = place_ref[0], place_ref[1]
    own_cap, span = own_ref.shape
    half = span // 2

    def rows(of_chip, of_core):
        return pl.ds(pl.multiple_of((2 * of_chip + of_core) * own_cap, own_cap), own_cap)

    def fetch(source, of_chip, of_core, columns, place):
        target = out_ref.at[rows(of_chip, of_core), columns]
        return pltpu.make_async_copy(source, target, done.at[place])

    def quadrant_copies(here):
        there = 1 - here
        columns = pl.ds(there * half, half)
        return (
            fetch(near_ref, there, core, columns, 2),
            fetch(far_ref, there, 1 - core, columns, 3),
        )

    everything = pl.ds(0, span)
    top = (
        fetch(own_ref, chip, core, everything, 0),
        fetch(sibling_ref, chip, 1 - core, everything, 1),
    )

    def of_chip(here):
        there = 1 - here
        copies = top + quadrant_copies(here)
        for copy in copies:
            copy.start()
        for copy in copies:
            copy.wait()
        here_rows = pl.ds(here * half, half)
        for tile in range(half // 128):
            columns = pl.ds(there * half + tile * 128, 128)
            strip = out_ref[here_rows, columns]
            turned = jnp.transpose(strip.astype(jnp.float32)).astype(jnp.bfloat16)
            out_ref[columns, here_rows] = turned

    @pl.when(chip == 0)
    def first():
        of_chip(0)

    @pl.when(chip == 1)
    def second():
        of_chip(1)

    across = jnp.ones((1, span), jnp.float32)
    for tile in range(span // 128):
        across = across + jnp.sum(
            out_ref[pl.ds(tile * 128, 128), :].astype(jnp.float32), axis=0, keepdims=True
        )
    across = lax.rsqrt(across)
    for tile in range(span // 128):
        strip = out_ref[pl.ds(tile * 128, 128), :].astype(jnp.float32)
        down = lax.rsqrt(1.0 + jnp.sum(strip, axis=1, keepdims=True))
        out_ref[pl.ds(tile * 128, 128), :] = (strip * down * across).astype(jnp.bfloat16)


def normalized_block(own, sibling, near, far, place):
    span = own.shape[1]
    return pl.pallas_call(
        assemble,
        out_shape=jax.ShapeDtypeStruct((span, span), jnp.bfloat16),
        in_specs=[pl.BlockSpec(memory_space=pltpu.SMEM)]
        + [pl.BlockSpec(memory_space=pltpu.HBM)] * 4,
        out_specs=pl.BlockSpec(memory_space=pltpu.VMEM),
        scratch_shapes=[pltpu.SemaphoreType.DMA((4,))],
        compiler_params=pltpu.CompilerParams(vmem_limit_bytes=VMEM_BYTES),
        cost_estimate=NO_COST,
        name="normalized_block",
    )(place, own, sibling, near, far)


def pack_kernel(
    keep_ref, row_codes_ref, col_codes_ref, row_keys_ref, col_keys_ref, weight_ref, out_ref,
    masked, picked, rows_hot, cols_hot
):
    tile_rows, tile_cols = weight_ref.shape
    blocks_down, blocks_across = keep_ref.shape
    groups, ignored, lanes = out_ref.shape
    send_cap, own_cap = rows_hot.shape[0] // groups, cols_hot.shape[0] // groups
    high, wide = tile_rows // blocks_down, tile_cols // blocks_across
    for down in range(blocks_down):
        for across in range(blocks_across):
            rows, columns = pl.ds(down * high, high), pl.ds(across * wide, wide)
            own, other = row_codes_ref[rows, :], col_codes_ref[:, columns]
            linked = (own == other) & (own % 2 == 1) & (keep_ref[down, across] == 1)
            weight = weight_ref[rows, columns].astype(jnp.float32)
            masked[rows, columns] = jnp.where(linked, weight, 0.0).astype(jnp.bfloat16)

    def one_hot(keys, start, count):
        standing = lax.broadcasted_iota(jnp.int32, (count, keys.shape[1]), 0) + start
        return jnp.where(standing == keys, 1.0, 0.0).astype(jnp.bfloat16)

    for group in range(groups):
        rows_hot[pl.ds(group * send_cap, send_cap), :] = one_hot(
            row_keys_ref[...], group * send_cap, send_cap
        )
        cols_hot[pl.ds(group * own_cap, own_cap), :] = one_hot(
            col_keys_ref[...], group * own_cap, own_cap
        )
    for tile in range(tile_cols // 256):
        columns = pl.ds(tile * 256, 256)
        picked[:, columns] = jnp.dot(
            rows_hot[...], masked[:, columns], preferred_element_type=jnp.float32
        ).astype(jnp.bfloat16)
    whole, half = own_cap // lanes, send_cap // 2
    for group in range(groups):
        packed = lax.dot_general(
            cols_hot[pl.ds(group * own_cap, own_cap), :],
            picked[pl.ds(group * send_cap, send_cap), :],
            (((1,), (1,)), ((), ())),
            preferred_element_type=jnp.float32,
        ).T
        for tile in range(whole):
            out_ref[group, pl.ds(tile * send_cap, send_cap), :] = packed[
                :, tile * lanes : (tile + 1) * lanes
            ].astype(jnp.bfloat16)
        ends = jnp.concatenate(
            [packed[:half, whole * lanes :], packed[half:, whole * lanes :]], axis=1
        )
        out_ref[group, pl.ds(whole * send_cap, half), :] = ends.astype(jnp.bfloat16)


def packed_pieces(block_keep, row_codes, col_codes, row_keys, col_keys, edge_weight, caps, groups):
    own_cap, send_cap = caps
    tile_rows, tile_cols = edge_weight.shape
    high = own_cap // 128 * send_cap + send_cap // 2
    vector = pl.BlockSpec(memory_space=pltpu.VMEM)
    return pl.pallas_call(
        pack_kernel,
        out_shape=jax.ShapeDtypeStruct((groups, high, 128), jnp.bfloat16),
        in_specs=[pl.BlockSpec(memory_space=pltpu.SMEM)] + [vector] * 5,
        out_specs=vector,
        scratch_shapes=[
            pltpu.VMEM((tile_rows, tile_cols), jnp.bfloat16),
            pltpu.VMEM((groups * send_cap, tile_cols), jnp.bfloat16),
            pltpu.VMEM((groups * send_cap, tile_rows), jnp.bfloat16),
            pltpu.VMEM((groups * own_cap, tile_cols), jnp.bfloat16),
        ],
        compiler_params=pltpu.CompilerParams(vmem_limit_bytes=VMEM_BYTES),
        cost_estimate=NO_COST,
        name="packed_pieces",
    )(block_keep, row_codes[:, None], col_codes[None], row_keys[None], col_keys[None], edge_weight)


def normal_share(mixed):
    return 0.5 * (1.0 + lax.erf(mixed * 0.5**0.5))


def norm_forward(mixed):
    active = mixed * normal_share(mixed)
    centered = active - jnp.mean(active, axis=-1, keepdims=True)
    scale = lax.rsqrt(jnp.mean(centered * centered, axis=-1, keepdims=True) + 1e-05)
    return centered * scale, scale


def norm_backward(mixed, upstream, gain, valid):
    normed, scale = norm_forward(mixed)
    upstream = upstream * valid
    inner = upstream * gain
    inner = inner - jnp.mean(inner, axis=-1, keepdims=True) - normed * jnp.mean(
        inner * normed, axis=-1, keepdims=True
    )
    density = jnp.exp(-0.5 * mixed * mixed) * (1.0 / (2.0 * math.pi) ** 0.5)
    low = (inner * scale * (normal_share(mixed) + mixed * density)).astype(jnp.bfloat16)
    rest = [low.astype(jnp.float32), upstream * normed, upstream]
    return low, [jnp.sum(value, axis=0, keepdims=True) for value in rest]


def weight_gradient(turned_ref, low, core, mine_ref, other_ref):
    parts = mine_ref.shape[0]
    part = turned_ref.shape[0] // (2 * parts)

    def halves(first_ref, second_ref):
        for place in range(2 * parts):
            out_ref = second_ref if place % 2 else first_ref
            out_ref[place // 2, :part, :] = jnp.dot(
                turned_ref[place * part : (place + 1) * part, :],
                low,
                preferred_element_type=jnp.float32,
            ).astype(jnp.bfloat16)

    @pl.when(core == 0)
    def low_half_first():
        halves(mine_ref, other_ref)

    @pl.when(core == 1)
    def high_half_first():
        halves(other_ref, mine_ref)


def forward_step(step, powers_ref, all_ref, own_ref, weights, bias_ref, turned, mixed):
    terms, own_cap, span = powers_ref.shape
    fan_in = own_ref.shape[1]

    @pl.when(step == 0)
    def first():
        turned[:fan_in, :] = own_ref[...].T
        mixed[...] = bias_ref[...] + jnp.dot(
            own_ref[...], weights[0][0], preferred_element_type=jnp.float32
        )

    low = jnp.dot(
        powers_ref[...].reshape(terms * own_cap, span),
        all_ref[...],
        preferred_element_type=jnp.float32,
    ).astype(jnp.bfloat16)
    total = mixed[...]
    for term in range(terms):
        part = low[term * own_cap : (term + 1) * own_cap]
        start = pl.multiple_of((1 + step * terms + term) * fan_in, fan_in)
        turned[pl.ds(start, fan_in), :] = part.T
        total = total + jnp.dot(part, weights[1 + term][0], preferred_element_type=jnp.float32)
    mixed[...] = total


def layer_one_kernel(
    powers_ref,
    all_ref,
    own_ref,
    weight_0,
    weight_a,
    weight_b,
    weight_c,
    bias_ref,
    gain_ref,
    shift_ref,
    valid_ref,
    hidden_ref,
    turned_ref,
    mixed_ref,
):
    step = pl.program_id(0)
    weights = (weight_0, weight_a, weight_b, weight_c)
    forward_step(step, powers_ref, all_ref, own_ref, weights, bias_ref, turned_ref, mixed_ref)

    @pl.when(step == pl.num_programs(0) - 1)
    def finish_layer():
        normed, ignored = norm_forward(mixed_ref[...])
        hidden = (normed * gain_ref[...] + shift_ref[...]) * valid_ref[...]
        hidden_ref[...] = hidden.astype(jnp.bfloat16)


def layer_two_kernel(
    place_ref,
    powers_ref,
    all_ref,
    own_ref,
    weight_0,
    weight_a,
    weight_b,
    weight_c,
    bias_ref,
    gain_ref,
    shift_ref,
    valid_ref,
    upstream_ref,
    active_ref,
    low_ref,
    rest_ref,
    mine_ref,
    other_ref,
    turned,
    mixed,
):
    step = pl.program_id(0)
    weights = (weight_0, weight_a, weight_b, weight_c)
    forward_step(step, powers_ref, all_ref, own_ref, weights, bias_ref, turned, mixed)

    @pl.when(step == pl.num_programs(0) - 1)
    def finish_layer():
        normed, ignored = norm_forward(mixed[...])
        active = (normed * gain_ref[...] + shift_ref[...]) * valid_ref[...]
        active_ref[...] = active.astype(jnp.bfloat16)
        low, rest = norm_backward(
            mixed[...], upstream_ref[...].astype(jnp.float32), gain_ref[...], valid_ref[...]
        )
        low_ref[...] = low
        for place in range(3):
            rest_ref[place : place + 1, :] = rest[place]
        weight_gradient(turned, low, place_ref[1], mine_ref, other_ref)


def backward_step(step, powers_ref, all_ref, own_ref, weights, total):
    terms, own_cap, span = powers_ref.shape
    transposed = (((1,), (1,)), ((), ()))

    @pl.when(step == 0)
    def first():
        total[...] = lax.dot_general(
            own_ref[...], weights[0][0], transposed, preferred_element_type=jnp.float32
        )

    low = jnp.dot(
        powers_ref[...].reshape(terms * own_cap, span),
        all_ref[...],
        preferred_element_type=jnp.float32,
    ).astype(jnp.bfloat16)
    value = total[...]
    for term in range(terms):
        value = value + lax.dot_general(
            low[term * own_cap : (term + 1) * own_cap],
            weights[1 + term][0],
            transposed,
            preferred_element_type=jnp.float32,
        )
    total[...] = value


def back_two_kernel(
    place_ref,
    powers_ref,
    all_ref,
    own_ref,
    weight_0,
    weight_a,
    weight_b,
    weight_c,
    turned_ref,
    mixed_ref,
    gain_ref,
    valid_ref,
    rest_ref,
    low_ref,
    mine_ref,
    other_ref,
    total,
):
    step = pl.program_id(0)
    weights = (weight_0, weight_a, weight_b, weight_c)
    backward_step(step, powers_ref, all_ref, own_ref, weights, total)

    @pl.when(step == pl.num_programs(0) - 1)
    def finish_layer():
        low, rest = norm_backward(mixed_ref[...], total[...], gain_ref[...], valid_ref[...])
        low_ref[...] = low
        weight_gradient(turned_ref, low, place_ref[1], mine_ref, other_ref)
        part = turned_ref.shape[0] // 2
        extra = jnp.zeros((1, mine_ref.shape[1] - part, mine_ref.shape[2]), jnp.bfloat16)
        rows = rest + [rest_ref[place : place + 1, :] for place in range(3)]
        rows = jnp.concatenate(rows + [jnp.zeros((10, rows[0].shape[1]), jnp.float32)], axis=0)

        def below(first_ref, second_ref):
            first_ref[:, part:, :] = extra
            second_ref[:, part:, :] = extra
            first_ref[0, part : part + 16, :] = rows.astype(jnp.bfloat16)

        @pl.when(place_ref[1] == 0)
        def low_half_here():
            below(mine_ref, other_ref)

        @pl.when(place_ref[1] == 1)
        def low_half_there():
            below(other_ref, mine_ref)


def back_one_kernel(
    powers_ref, all_ref, own_ref, weight_0, weight_a, weight_b, weight_c, out_ref, total
):
    step = pl.program_id(0)
    weights = (weight_0, weight_a, weight_b, weight_c)
    backward_step(step, powers_ref, all_ref, own_ref, weights, total)

    @pl.when(step == pl.num_programs(0) - 1)
    def finish_layer():
        out_ref[...] = total[...].astype(jnp.bfloat16)


def layer_pass(kernel, name, place, powers, everyone, own, weight, others, outs, scratch):
    ignored, own_cap, span = powers.shape
    fan_in, width = weight.shape[1:]

    def whole(value):
        return pl.BlockSpec(value.shape, lambda step: (0,) * len(value.shape))

    def term_weight(term):
        return pl.BlockSpec((1, fan_in, width), lambda step: (1 + step * TERMS + term, 0, 0))

    in_specs = [
        pl.BlockSpec((TERMS, own_cap, span), lambda step: (step, 0, 0)),
        whole(everyone),
        whole(own),
        pl.BlockSpec((1, fan_in, width), lambda step: (0, 0, 0)),
    ]
    in_specs += [term_weight(term) for term in range(TERMS)] + [whole(value) for value in others]
    operands = [powers, everyone, own] + [weight] * (1 + TERMS) + list(others)
    if place is not None:
        in_specs = [pl.BlockSpec(memory_space=pltpu.SMEM)] + in_specs
        operands = [place] + operands
    return pl.pallas_call(
        kernel,
        grid=((ORDER - 1) // TERMS,),
        out_shape=outs,
        in_specs=in_specs,
        out_specs=[whole(value) for value in outs],
        scratch_shapes=[pltpu.VMEM(shape, dtype) for shape, dtype in scratch],
        compiler_params=pltpu.CompilerParams(vmem_limit_bytes=VMEM_BYTES),
        cost_estimate=NO_COST,
        name=name,
    )(*operands)


def finish_kernel(scalars_ref, pair_ref, siblings_ref, other_ref, out_ref, *small_refs):
    step = pl.program_id(0)
    part = out_ref.shape[1]
    held = pl.num_programs(0) // 2
    for here, values_ref in ((step < held, pair_ref), (step >= held, siblings_ref)):
        @pl.when(here & (scalars_ref[0] == 1))
        def fast_form():
            out_ref[0] = values_ref[0, :part, :].astype(jnp.float32)

        for small_ref in small_refs:
            @pl.when(here & (scalars_ref[1 + step] == 0))
            def small_sums():
                small_ref[...] = values_ref[0, part : part + 16, :].astype(jnp.float32)

    @pl.when(scalars_ref[0] == 0)
    def general_form():
        out_ref[0] = other_ref[0].astype(jnp.float32)


def finished(scalars, pair, siblings, other, with_small=False):
    count, part, width = other.shape
    out, held = (1, part, width), (1,) + pair.shape[1:]
    out_specs = [pl.BlockSpec(out, lambda step, ref: (ref[1 + step], 0, 0))]
    out_shape = [jax.ShapeDtypeStruct(other.shape, jnp.float32)]
    if with_small:
        out_specs.append(pl.BlockSpec((16, width), lambda step, ref: (0, 0)))
        out_shape.append(jax.ShapeDtypeStruct((16, width), jnp.float32))
    return pl.pallas_call(
        finish_kernel,
        grid_spec=pltpu.PrefetchScalarGridSpec(
            num_scalar_prefetch=1,
            grid=(count,),
            in_specs=[
                pl.BlockSpec(held, lambda step, ref: (jnp.minimum(step, count // 2 - 1), 0, 0)),
                pl.BlockSpec(held, lambda step, ref: (jnp.maximum(step - count // 2, 0), 0, 0)),
                pl.BlockSpec(out, lambda step, ref: ((1 - ref[0]) * ref[1 + step], 0, 0)),
            ],
            out_specs=out_specs,
        ),
        out_shape=out_shape,
        compiler_params=pltpu.CompilerParams(vmem_limit_bytes=VMEM_BYTES),
        cost_estimate=pl.CostEstimate(
            flops=other.size, bytes_accessed=6 * other.size, transcendentals=0
        ),
        name="finished",
    )(scalars, pair, siblings, other)


def unpack_kernel(place_ref, pieces_ref, keys_ref, own_ref, quadrant_ref, columns, hot):
    groups, high, lanes = pieces_ref.shape
    own_cap, span = own_ref.shape
    whole = own_cap // lanes
    send_cap = keys_ref.shape[1] // groups
    half, rest = send_cap // 2, own_cap - whole * lanes
    for group in range(groups):
        start = group * send_cap
        for tile in range(whole):
            columns[start : start + send_cap, tile * lanes : (tile + 1) * lanes] = pieces_ref[
                group, tile * send_cap : (tile + 1) * send_cap, :
            ]
        ends = pieces_ref[group, whole * send_cap :, :]
        columns[start : start + half, whole * lanes :] = ends[:, :rest]
        columns[start + half : start + send_cap, whole * lanes :] = ends[:, rest:]
    standing = lax.broadcasted_iota(jnp.int32, hot.shape, 0)
    hot[...] = jnp.where(standing == keys_ref[...], 1.0, 0.0).astype(jnp.bfloat16)
    block = jnp.dot(hot[...], columns[...], preferred_element_type=jnp.float32)
    own_ref[...] = block.T.astype(jnp.bfloat16)
    middle = span // 2

    @pl.when(place_ref[0] == 0)
    def first():
        quadrant_ref[...] = own_ref[:, :middle]

    @pl.when(place_ref[0] == 1)
    def second():
        quadrant_ref[...] = own_ref[:, middle:]


def unpacked_block(pieces, keys, place, own_cap, span):
    vector = pl.BlockSpec(memory_space=pltpu.VMEM)
    return pl.pallas_call(
        unpack_kernel,
        out_shape=[
            jax.ShapeDtypeStruct((own_cap, span), jnp.bfloat16),
            jax.ShapeDtypeStruct((own_cap, span // 2), jnp.bfloat16),
        ],
        in_specs=[pl.BlockSpec(memory_space=pltpu.SMEM), vector, vector],
        out_specs=[vector, vector],
        scratch_shapes=[
            pltpu.VMEM((keys.shape[1], own_cap), jnp.bfloat16),
            pltpu.VMEM((span, keys.shape[1]), jnp.bfloat16),
        ],
        compiler_params=pltpu.CompilerParams(vmem_limit_bytes=VMEM_BYTES),
        cost_estimate=NO_COST,
        name="unpacked_block",
    )(place, pieces, keys)


def fit_kernel(codes_ref, out_ref, *, n_row, caps):
    own_cap, send_cap, seat_cap = caps
    codes = codes_ref[...]
    devices = codes.shape[0]
    n_col = devices // n_row
    label = lax.broadcasted_iota(jnp.int32, (devices, 128), 1)
    counts = jnp.zeros((devices, 128), jnp.float32)
    for cluster in range(CLUSTERS):
        here = jnp.where(codes == 2 * cluster + 1, 1.0, 0.0)
        counts = counts + jnp.where(
            label == cluster, jnp.sum(here, axis=1, keepdims=True), 0.0
        )
    sizes = jnp.sum(counts, axis=0, keepdims=True)
    across = jnp.broadcast_to(sizes, (128, 128))
    down = across.T
    first = lax.broadcasted_iota(jnp.int32, (128, 128), 0)
    second = lax.broadcasted_iota(jnp.int32, (128, 128), 1)
    ahead = (across > down) | ((across == down) & (second < first))
    ahead = ahead & (second < CLUSTERS)
    rank = jnp.sum(jnp.where(ahead, 1.0, 0.0), axis=1, keepdims=True).astype(jnp.int32)
    others = n_row - 1
    later = rank > others
    turn = jnp.zeros_like(rank)
    for count in range(1, CLUSTERS // others + 1):
        turn = turn + jnp.where(rank - 1 >= count * others, 1, 0)
    place = rank - 1 - turn * others
    group = jnp.where(rank == 0, 0, 1 + jnp.where(later, others - 1 - place, place))
    member = (group == second) & (first < CLUSTERS)
    held = jnp.dot(
        counts.astype(jnp.bfloat16),
        jnp.where(member, 1.0, 0.0).astype(jnp.bfloat16),
        preferred_element_type=jnp.float32,
    )
    by_row = jnp.zeros((1, 128), jnp.float32)
    for row in range(n_row):
        rows = jnp.sum(held[row * n_col : (row + 1) * n_col], axis=0, keepdims=True)
        by_row = jnp.maximum(by_row, rows)
    device = lax.broadcasted_iota(jnp.int32, (devices, 128), 0)
    by_col = jnp.zeros((1, 128), jnp.float32)
    for col in range(n_col):
        cols = jnp.where(device % n_col == col, held, 0.0)
        by_col = jnp.maximum(by_col, jnp.sum(cols, axis=0, keepdims=True))
    fits = (
        (jnp.max(by_col) <= own_cap) & (jnp.max(by_row) <= send_cap) & (jnp.max(held) <= seat_cap)
    )
    out_ref[0] = jnp.where(fits, 1, 0)


def fits_in(codes, n_row, caps):
    fits = pl.pallas_call(
        functools.partial(fit_kernel, n_row=n_row, caps=caps),
        out_shape=jax.ShapeDtypeStruct((1,), jnp.int32),
        in_specs=[pl.BlockSpec(memory_space=pltpu.VMEM)],
        out_specs=pl.BlockSpec(memory_space=pltpu.SMEM),
        cost_estimate=NO_COST,
        name="fits",
    )(codes.reshape(-1, codes.shape[-1]))
    return fits


def exclusive_counts(member):
    count = member.shape[-1]
    before = jnp.arange(count)[:, None] < jnp.arange(count)[None, :]
    return jnp.dot(
        member.astype(jnp.bfloat16),
        before.astype(jnp.bfloat16),
        preferred_element_type=jnp.float32,
    ).astype(jnp.int32)


def assign(codes, n_row):
    cluster, valid = codes >> 1, codes & 1
    labels = jnp.arange(CLUSTERS)
    sizes = jnp.sum(
        (cluster.reshape(1, -1) == labels[:, None]) & (valid.reshape(1, -1) == 1), axis=1
    )
    ahead = (sizes[None, :] > sizes[:, None]) | (
        (sizes[None, :] == sizes[:, None]) & (labels[None, :] < labels[:, None])
    )
    rank = jnp.sum(ahead, axis=1)
    others = n_row - 1
    turn, place = (rank - 1) // others, (rank - 1) % others
    group = jnp.where(rank == 0, 0, 1 + jnp.where(turn == 0, place, others - 1 - place))
    of_node = jnp.sum(
        jnp.where(cluster[None] == labels[:, None, None, None], group[:, None, None, None], 0),
        axis=0,
    )
    return jnp.where(valid == 1, of_node, n_row)


def compact(
    codes,
    group,
    features,
    block_keep,
    edge_weight,
    weight_one,
    bias_one,
    gain_one,
    shift_one,
    weight_two,
    bias_two,
    gain_two,
    shift_two,
    cotangent,
    places_of,
    slots_of,
    seats_of,
    decide,
    sizes,
    caps,
):
    row, col = lax.axis_index("row"), lax.axis_index(COL)
    chip, core = lax.axis_index("chip"), lax.axis_index("core")
    n_row, n_col = sizes
    own_cap, send_cap, seat_cap = caps
    own_nodes, in_width = features.shape
    width = weight_two.shape[2]
    span = n_col * own_cap
    targets = jnp.arange(n_row)

    def in_col(value):
        return lax.dynamic_index_in_dim(value, col, 1, False).reshape(-1)

    def in_row(value):
        return lax.dynamic_index_in_dim(value, row, 0, False).reshape(-1)

    row_group, col_group = in_row(group), in_col(group)
    row_slots, col_places = in_row(slots_of(group)), in_col(places_of(group))
    row_keys = jnp.where(row_slots < send_cap, row_group * send_cap + row_slots, -1)
    col_keys = jnp.where(col_places < own_cap, col_group * own_cap + col_places, -1)
    pieces = packed_pieces(
        block_keep,
        in_row(codes),
        in_col(codes),
        row_keys,
        col_keys,
        edge_weight,
        (own_cap, send_cap),
        n_row,
    )
    pieces, codes = lax.optimization_barrier((pieces, codes))
    group = assign(codes, n_row)
    places, slots, seats = places_of(group), slots_of(group), seats_of(group)

    standing = jnp.arange(n_col)[None, :, None] * own_cap + places
    fits_here = jnp.where(group == row, standing, -1).reshape(n_row, -1)
    slot_of = slots.reshape(n_row, -1)
    target = jnp.max(
        jnp.where(
            slot_of[:, None, :] == jnp.arange(send_cap)[None, :, None], fits_here[:, None, :], -1
        ),
        axis=2,
    )
    keys = target.reshape(1, -1)

    def to_partner(value, step):
        return lax.ppermute(value, "row", [(place, place ^ step) for place in range(n_row)])

    partners = row ^ targets
    group_here = lax.dynamic_index_in_dim(in_row(group).reshape(n_col, -1), col, 0, False)
    seat_here = lax.dynamic_index_in_dim(in_row(seats).reshape(n_col, -1), col, 0, False)

    def seat_of_node(groups):
        hot = (group_here[None, None, :] == groups[:, None, None]) & (
            seat_here[None, None, :] == jnp.arange(seat_cap)[None, :, None]
        )
        return hot.astype(jnp.bfloat16).reshape(n_row * seat_cap, own_nodes)

    enter_home = seat_of_node(targets).T
    enter_partner = seat_of_node(partners)
    both = jnp.dot(enter_partner, jnp.concatenate([features, cotangent], axis=1))
    both = both.reshape(n_row, seat_cap, -1)
    enter_partner = enter_partner.T
    pieces = trade(pieces, "row")
    both, codes = lax.optimization_barrier((both, codes))
    both = [both[step] for step in range(n_row)]
    both[1] = to_partner(both[1], 1)
    fits, others = decide(codes)
    group_col = lax.dynamic_index_in_dim(group, col, 1, False)
    seats_col = lax.dynamic_index_in_dim(seats, col, 1, False)
    places_col = lax.dynamic_index_in_dim(places, col, 1, False)
    seated = (group_col == row)[:, None, :] & (
        seats_col[:, None, :] == jnp.arange(seat_cap)[None, :, None]
    )
    place_of_seat = jnp.max(jnp.where(seated, places_col[:, None, :], -1), axis=2)
    from_partner = jnp.max(
        jnp.where((partners[:, None] == targets)[:, :, None], place_of_seat[None], -1), axis=1
    )
    arrive = from_partner.reshape(1, -1) == jnp.arange(own_cap)[:, None]
    arrive = arrive.astype(jnp.bfloat16)
    leave_group = place_of_seat.reshape(-1, 1) == jnp.arange(own_cap)
    leave_group = leave_group.astype(jnp.bfloat16)
    leave_partner = jnp.concatenate([from_partner[::2], from_partner[1::2]])
    leave_partner = leave_partner.reshape(-1, 1) == jnp.arange(own_cap)
    leave_partner = leave_partner.astype(jnp.bfloat16)
    held_count = jnp.sum(group_col == row)
    valid_rows = (jnp.arange(own_cap) < held_count).astype(jnp.float32)[:, None]
    place = jnp.stack([chip, core]).astype(jnp.int32)
    quarters = jnp.stack([col, (1 - chip) * 2 + core, chip * 2 + 1 - core, 3 - col])
    quarters = jnp.concatenate([fits, quarters.astype(jnp.int32)])
    own_halves = jnp.concatenate([fits, jnp.stack([core, 1 - core]).astype(jnp.int32)])
    scalars = (chip, 1 - chip, col * own_cap)
    scalars = tuple(value.astype(jnp.uint32) for value in scalars) + (chip == 0, core == 0, place)
    scalars = scalars + (quarters, own_halves)
    homes = enter_home, enter_partner, leave_group, leave_partner
    pieces, both, keys, arrive, homes, valid_rows, others, scalars = lax.optimization_barrier(
        (pieces, both, keys, arrive, homes, valid_rows, others, scalars)
    )
    enter_home, enter_partner, leave_group, leave_partner = homes
    this_chip, other_chip, own_start, first_chip, first_core = scalars[:5]
    place, quarters, own_halves = scalars[5:]

    own_block, quadrant = unpacked_block(pieces, keys, place, own_cap, span)
    quadrant = swap(quadrant, "chip")
    both = both[:2] + [to_partner(both[step], step) for step in range(2, n_row)]
    sibling = swap(own_block, "core")
    quadrant, *early = lax.optimization_barrier((quadrant, *both[:-2]))
    adjacency = normalized_block(own_block, sibling, quadrant, swap(quadrant, "core"), place)
    adjacency, *late = lax.optimization_barrier((adjacency, *both[-2:]))
    both = early + late
    mine = jnp.dot(arrive, jnp.concatenate(both))
    features_own, cotangent_own = mine[:, :in_width], mine[:, in_width:]
    sibling = swap(features_own, "core")

    first = (own_start + jnp.arange(own_cap, dtype=jnp.uint32))[:, None]
    first = first == jnp.arange(span, dtype=jnp.uint32)[None, :]
    previous = first.astype(jnp.float32)
    current = -lax.dynamic_slice_in_dim(adjacency, own_start, own_cap, 0).astype(jnp.float32)
    lowered = [current.astype(jnp.bfloat16)]
    for position in range(2, ORDER):
        upcoming = (
            -2.0 * jnp.dot(lowered[-1], adjacency, preferred_element_type=jnp.float32) - previous
        )
        low = upcoming.astype(jnp.bfloat16)
        if position == 4:
            low, sibling = lax.optimization_barrier((low, sibling))
            features_chip = joined(features_own, sibling, first_core)
            partner = swap(features_chip, "chip")
        if position == 8:
            low, partner = lax.optimization_barrier((low, partner))
            features_all = joined(features_chip, partner, first_chip)
        previous, current = current, upcoming
        lowered.append(low)
    powers = jnp.concatenate(lowered, axis=0).reshape(ORDER - 1, own_cap, span)

    def everywhere(value_low):
        return lax.all_gather(value_low, COL, axis=0, tiled=True)

    def chosen(value, other):
        return jnp.where(quarters[0] == 1, value.astype(jnp.float32), other.astype(jnp.float32))

    def shaped(*shape, dtype=jnp.bfloat16):
        return jax.ShapeDtypeStruct(shape, dtype)

    part_one, part_two = ORDER * in_width // 2, ORDER * width // n_col
    padded = -(-(part_one + 16) // (16 * n_row)) * (16 * n_row)
    hidden, turned_one, mixed_one = layer_pass(
        layer_one_kernel,
        "layer_one",
        None,
        powers,
        features_all,
        features_own,
        weight_one,
        [bias_one[None], gain_one[None], shift_one[None], valid_rows],
        [
            shaped(own_cap, width),
            shaped(2 * part_one, own_cap),
            shaped(own_cap, width, dtype=jnp.float32),
        ],
        [],
    )
    activations, low_two, rest_two, mine, other = layer_pass(
        layer_two_kernel,
        "layer_two",
        place,
        powers,
        everywhere(hidden),
        hidden,
        weight_two,
        [bias_two[None], gain_two[None], shift_two[None], valid_rows, cotangent_own],
        [
            shaped(own_cap, width),
            shaped(own_cap, width),
            shaped(3, width, dtype=jnp.float32),
            shaped(2, part_two, width),
            shaped(2, part_two, width),
        ],
        [((n_col * part_two, own_cap), jnp.bfloat16), ((own_cap, width), jnp.float32)],
    )

    def add_cores(mine, other, axis=0):
        got = swap(other, "core")
        return tuple(
            added(
                lax.dynamic_index_in_dim(mine, index, axis, False),
                lax.dynamic_index_in_dim(got, index, axis, False),
            )
            for index in (this_chip, other_chip)
        )

    leaving = jnp.dot(leave_partner, activations).reshape(n_row, seat_cap, width)
    near, far = leaving[: n_row // 2], leaving[n_row // 2 :]
    far = to_partner(far, 1)
    here, there = add_cores(mine, other)
    everyone_two, there, far = lax.optimization_barrier((everywhere(low_two), there, far))
    there = swap(there, "chip")
    arrived = [jnp.stack([near[0], far[0]])] + [
        to_partner(jnp.stack([near[half], far[half]]), 2 * half) for half in range(1, n_row // 2)
    ]
    low_one, mine, other = layer_pass(
        back_two_kernel,
        "back_two",
        place,
        powers,
        everyone_two,
        low_two,
        weight_two,
        [turned_one, mixed_one, gain_one[None], valid_rows, rest_two],
        [shaped(own_cap, width), shaped(1, padded, width), shaped(1, padded, width)],
        [((own_cap, width), jnp.float32)],
    )
    low_one, there, arrived = lax.optimization_barrier((low_one, there, arrived))
    second = added(here, there).reshape(n_row, -1, width)
    many = second.shape[1]
    low_one, second = lax.optimization_barrier((low_one, second))
    second = trade(second, "row")
    mine, other = (value.reshape(n_row, 2, -1, width) for value in (mine, other))
    here, there = add_cores(mine, other, 1)
    there = swap(there, "chip")
    first = added(here, there)
    second = jnp.sum(second.astype(jnp.float32), axis=0).astype(jnp.bfloat16)
    second = jnp.broadcast_to(second[None], (n_row,) + second.shape)
    mixed = jnp.concatenate([second, first], axis=1)
    low_one, mixed = lax.optimization_barrier((low_one, mixed))
    everyone_one = everywhere(low_one)
    mixed = trade(mixed, "row")
    (input_grad,) = layer_pass(
        back_one_kernel,
        "back_one",
        None,
        powers,
        everyone_one,
        low_one,
        weight_one,
        [],
        [shaped(own_cap, in_width)],
        [((own_cap, in_width), jnp.float32)],
    )
    leaving = jnp.dot(leave_group, input_grad)
    leaving = leaving.reshape(n_row, seat_cap * in_width // width, width)
    arrived = jnp.concatenate(arrived).reshape(-1, width)
    home = jnp.dot(enter_partner, arrived, preferred_element_type=jnp.float32)
    home = chosen(home, others[0])
    mixed, leaving, home = lax.optimization_barrier((mixed, leaving, home))
    first = jnp.sum(mixed[:, many:].astype(jnp.float32), axis=0).astype(jnp.bfloat16)
    partner, mixed = lax.optimization_barrier((swap(first, "chip"), mixed))
    second = mixed[:, :many].reshape(1, -1, width)
    partner_two = swap(second, "chip")
    first = joined(first, partner, first_chip)
    share = first.shape[0]
    first = jnp.broadcast_to(first[None], (n_row,) + first.shape)
    first = trade(jnp.concatenate([first, leaving], axis=1), "row")
    second = jnp.concatenate([second, partner_two])
    (second,) = finished(quarters, second, swap(second, "core"), others[3])
    first, second = lax.optimization_barrier((first, second))
    mine = first[:, :share].reshape(1, -1, width)
    siblings = swap(mine, "core")
    back = first[:, share:].reshape(n_row * seat_cap, in_width)
    home_grad = jnp.dot(enter_home, back, preferred_element_type=jnp.float32)
    home_grad = chosen(home_grad, others[1])
    first, small = finished(own_halves, mine, siblings, others[2], True)
    return home, home_grad, first, second, chosen(small[:6], others[4])


def general(
    codes,
    features,
    block_keep,
    edge_weight,
    weight_one,
    bias_one,
    gain_one,
    shift_one,
    weight_two,
    bias_two,
    gain_two,
    shift_two,
    cotangent,
    node_valid,
):
    row, col = lax.axis_index("row"), lax.axis_index(COL)
    row_codes = lax.dynamic_index_in_dim(codes, row, 0, False).reshape(-1)
    col_codes = lax.dynamic_index_in_dim(codes, col, 1, False).reshape(-1)
    tile_rows, tile_cols = edge_weight.shape
    blocks_down, blocks_across = block_keep.shape
    block_side = tile_rows // blocks_down
    linked = (row_codes[:, None] == col_codes[None, :]) & (row_codes[:, None] & 1 == 1)
    linked = linked.reshape(blocks_down, block_side, blocks_across, block_side) & (
        block_keep[:, None, :, None] == 1
    )
    masked = edge_weight * linked.reshape(tile_rows, tile_cols).astype(jnp.bfloat16)
    degree_rows = 1.0 + lax.psum(jnp.sum(masked, axis=1, dtype=jnp.float32), COL)
    own_nodes = features.shape[0]
    own_degree = lax.dynamic_slice_in_dim(
        degree_rows, lax.axis_index(COL) * own_nodes, own_nodes, 0
    )
    degree_cols = lax.all_gather(own_degree, "row", axis=0, tiled=True)
    adjacency = (
        masked.astype(jnp.float32)
        * lax.rsqrt(degree_rows)[:, None]
        * lax.rsqrt(degree_cols)[None, :]
    ).astype(jnp.bfloat16)
    valid_rows = node_valid.astype(jnp.float32)
    stacked_one, mixed_one, hidden = layer_forward(
        adjacency,
        features.astype(jnp.float32),
        weight_one,
        bias_one,
        gain_one,
        shift_one,
        valid_rows,
    )
    stacked_two, mixed_two, activations = layer_forward(
        adjacency, hidden, weight_two, bias_two, gain_two, shift_two, valid_rows
    )
    hidden_grad, weight_two_grad, bias_two_grad, gain_two_grad, shift_two_grad = layer_backward(
        adjacency,
        stacked_two,
        mixed_two,
        cotangent.astype(jnp.float32),
        weight_two,
        gain_two,
        shift_two,
        valid_rows,
    )
    input_grad, weight_one_grad, bias_one_grad, gain_one_grad, shift_one_grad = layer_backward(
        adjacency, stacked_one, mixed_one, hidden_grad, weight_one, gain_one, shift_one, valid_rows
    )
    summed = lax.psum(
        (
            weight_one_grad,
            bias_one_grad,
            gain_one_grad,
            shift_one_grad,
            weight_two_grad,
            bias_two_grad,
            gain_two_grad,
            shift_two_grad,
        ),
        ("row",) + COL,
    )
    weight_one_grad, bias_one_grad, gain_one_grad, shift_one_grad = (
        summed[0],
        summed[1],
        summed[2],
        summed[3],
    )
    weight_two_grad, bias_two_grad, gain_two_grad, shift_two_grad = (
        summed[4],
        summed[5],
        summed[6],
        summed[7],
    )
    return (
        activations,
        input_grad,
        weight_one_grad,
        bias_one_grad,
        gain_one_grad,
        shift_one_grad,
        weight_two_grad,
        bias_two_grad,
        gain_two_grad,
        shift_two_grad,
    )


def local(n_row, n_col, *args):
    (
        features,
        node_valid,
        cluster,
        block_keep,
        edge_weight,
        weight_one,
        bias_one,
        gain_one,
        shift_one,
        weight_two,
        bias_two,
        gain_two,
        shift_two,
        cotangent,
    ) = args
    own_nodes, in_width = features.shape
    own_cap = own_nodes * n_row * 5 // 16
    send_cap = own_nodes * n_col * 11 // 32
    seat_cap = own_nodes * 7 // 16
    codes = broadcast_along(cluster * 2 + node_valid, ("row",) + COL, n_row * n_col)
    codes = codes.reshape(n_row, n_col, own_nodes)
    shared = (
        block_keep,
        edge_weight,
        weight_one,
        bias_one,
        gain_one,
        shift_one,
        weight_two,
        bias_two,
        gain_two,
        shift_two,
        cotangent,
    )

    def slow():
        return general(codes, features, *shared, node_valid)

    held = (ORDER - 1) * own_cap * own_cap * n_col * 2
    if held > HELD_BYTES or n_col != 4 or n_row < 2 or n_row & (n_row - 1):
        return slow()
    group = assign(codes, n_row)

    def member_of(group):
        return group[None] == jnp.arange(n_row)[:, None, None, None]

    def places_of(group):
        member = member_of(group).transpose(0, 2, 1, 3).reshape(n_row, n_col, -1)
        places = jnp.sum(jnp.where(member, exclusive_counts(member), 0), axis=0)
        return places.reshape(n_col, n_row, own_nodes).transpose(1, 0, 2)

    def slots_of(group):
        member = member_of(group).reshape(n_row, n_row, -1)
        slots = jnp.sum(jnp.where(member, exclusive_counts(member), 0), axis=0)
        return slots.reshape(n_row, n_col, own_nodes)

    def seats_of(group):
        member = member_of(group)
        return jnp.sum(jnp.where(member, exclusive_counts(member), 0), axis=0)

    width = weight_two.shape[2]

    def instead(state):
        made = slow()
        small = jnp.stack([made[place] for place in (3, 4, 5, 7, 8, 9)])
        return (jnp.ones_like(state[0]),) + tuple(
            value.astype(jnp.bfloat16).reshape(like.shape)
            for value, like in zip((made[0], made[1], made[2], made[6], small), state[1:])
        )

    shapes = (
        (own_nodes, width),
        (own_nodes, in_width),
        (2, ORDER * in_width // 2, width),
        (n_col, ORDER * width // n_col, width),
        (6, width),
    )

    def decide(codes):
        fits = fits_in(codes, n_row, (own_cap, send_cap, seat_cap))
        others = lax.while_loop(
            lambda state: state[0][0] == 0,
            instead,
            (fits,) + tuple(jnp.zeros(shape, jnp.bfloat16) for shape in shapes),
        )[1:]
        return fits, others

    home, home_grad, first, second, small = compact(
        codes,
        group,
        features,
        *shared,
        places_of,
        slots_of,
        seats_of,
        decide,
        (n_row, n_col),
        (own_cap, send_cap, seat_cap),
    )
    return (
        home,
        home_grad,
        first.reshape(weight_one.shape),
        small[0],
        small[1],
        small[2],
        second.reshape(weight_two.shape),
        small[3],
        small[4],
        small[5],
    )


def solution(mesh):
    n_row, n_col = mesh.shape["row"], mesh.shape["col"]
    by_core = jax.sharding.Mesh(
        mesh.devices.reshape(n_row, n_col // 2, 2), ("row", "chip", "core")
    )
    nodes = ("row", "chip", "core")
    placed = (
        P(nodes, None),
        P(nodes),
        P(nodes),
        P("row", COL),
        P("row", COL),
        P(),
        P(),
        P(),
        P(),
        P(),
        P(),
        P(),
        P(),
        P(nodes, None),
    )
    return jax.shard_map(
        functools.partial(local, n_row, n_col),
        mesh=by_core,
        in_specs=placed,
        out_specs=(P(nodes, None), P(nodes, None), P(), P(), P(), P(), P(), P(), P(), P()),
        check_vma=False,
    )
```

```python
import functools
import math

import jax
import jax.numpy as jnp
from jax import lax
from jax.experimental import pallas as pl
from jax.experimental.pallas import tpu as pltpu
from jax.sharding import PartitionSpec as P

ORDER = 13
CLUSTERS = 16
HELD_BYTES = 1 << 25
VMEM_BYTES = 32 << 20
TERMS = 3
NO_COST = pl.CostEstimate(flops=1, bytes_accessed=1, transcendentals=0)
COL = ("chip", "core")


def finish(mixed, gain, shift, valid_rows):
    active = jax.nn.gelu(mixed, approximate=False)
    centered = active - jnp.mean(active, axis=-1, keepdims=True)
    variance = jnp.mean(centered * centered, axis=-1, keepdims=True)
    return (centered * lax.rsqrt(variance + 1e-05) * gain + shift) * valid_rows[:, None]


def forward_product(adjacency, piece_low):
    partial_value = jnp.dot(
        adjacency,
        lax.all_gather(piece_low, "row", axis=0, tiled=True),
        preferred_element_type=jnp.float32,
    )
    return lax.psum_scatter(partial_value, COL, scatter_dimension=0, tiled=True)


def backward_product(adjacency, piece_low):
    partial_value = lax.dot_general(
        adjacency,
        lax.all_gather(piece_low, COL, axis=0, tiled=True),
        (((0,), (0,)), ((), ())),
        preferred_element_type=jnp.float32,
    )
    return lax.psum_scatter(
        partial_value.astype(jnp.bfloat16), "row", scatter_dimension=0, tiled=True
    ).astype(jnp.float32)


def layer_forward(adjacency, inputs, weight, bias, gain, shift, valid_rows):
    first_low = inputs.astype(jnp.bfloat16)
    second = -forward_product(adjacency, first_low)
    second_low = second.astype(jnp.bfloat16)

    def advance(state_pair, unused):
        previous, current, current_low = state_pair
        upcoming = -2.0 * forward_product(adjacency, current_low) - previous
        upcoming_low = upcoming.astype(jnp.bfloat16)
        return ((current, upcoming, upcoming_low), upcoming_low)

    ignored, others = lax.scan(advance, (inputs, second, second_low), None, length=ORDER - 2)
    stacked = jnp.concatenate([first_low[None], second_low[None], others], axis=0)
    mixed = jnp.einsum("kni,kio->no", stacked, weight, preferred_element_type=jnp.float32) + bias
    return (stacked, mixed, finish(mixed, gain, shift, valid_rows))


def layer_backward(adjacency, stacked, mixed, upstream, weight, gain, shift, valid_rows):

    def local_finish(mixed_in, gain_in, shift_in):
        return finish(mixed_in, gain_in, shift_in, valid_rows)

    ignored, pullback = jax.vjp(local_finish, mixed, gain, shift)
    mixed_grad, gain_grad, shift_grad = pullback(upstream)
    mixed_low = mixed_grad.astype(jnp.bfloat16)
    bias_grad = jnp.sum(mixed_low.astype(jnp.float32), axis=0)
    weight_grad = jnp.einsum("kni,no->kio", stacked, mixed_low, preferred_element_type=jnp.float32)
    direct = jnp.einsum("no,kio->kni", mixed_low, weight, preferred_element_type=jnp.float32)

    def retreat(state_pair, direct_term):
        later_two, later_one = state_pair
        current = (
            direct_term
            - 2.0 * backward_product(adjacency, later_one.astype(jnp.bfloat16))
            - later_two
        )
        return ((later_one, current), None)

    start_pair = (jnp.zeros_like(direct[0]), direct[ORDER - 1])
    (second_grad, first_grad), unused = lax.scan(
        retreat, start_pair, direct[1 : ORDER - 1], reverse=True
    )
    input_grad = (
        direct[0] - backward_product(adjacency, first_grad.astype(jnp.bfloat16)) - second_grad
    )
    return (input_grad, weight_grad, bias_grad, gain_grad, shift_grad)


def swap(value, axis):
    return lax.ppermute(value, axis, [(0, 1), (1, 0)])


def trade(pieces, axis):
    return lax.all_to_all(pieces, axis, 0, 0, tiled=False)


def broadcast_along(value, axis, size):
    return trade(jnp.broadcast_to(value[None], (size,) + value.shape), axis)


def joined(mine, other, mine_first):
    return jnp.where(
        mine_first, jnp.concatenate([mine, other]), jnp.concatenate([other, mine])
    )


def added(mine, received):
    return (mine.astype(jnp.float32) + received.astype(jnp.float32)).astype(jnp.bfloat16)


def assemble(place_ref, own_ref, sibling_ref, near_ref, far_ref, out_ref, done):
    chip, core = place_ref[0], place_ref[1]
    own_cap, span = own_ref.shape
    half = span // 2

    def rows(of_chip, of_core):
        return pl.ds(pl.multiple_of((2 * of_chip + of_core) * own_cap, own_cap), own_cap)

    def fetch(source, of_chip, of_core, columns, place):
        target = out_ref.at[rows(of_chip, of_core), columns]
        return pltpu.make_async_copy(source, target, done.at[place])

    def quadrant_copies(here):
        there = 1 - here
        columns = pl.ds(there * half, half)
        return (
            fetch(near_ref, there, core, columns, 2),
            fetch(far_ref, there, 1 - core, columns, 3),
        )

    everything = pl.ds(0, span)
    top = (
        fetch(own_ref, chip, core, everything, 0),
        fetch(sibling_ref, chip, 1 - core, everything, 1),
    )

    def of_chip(here):
        there = 1 - here
        copies = top + quadrant_copies(here)
        for copy in copies:
            copy.start()
        for copy in copies:
            copy.wait()
        here_rows = pl.ds(here * half, half)
        for tile in range(half // 128):
            columns = pl.ds(there * half + tile * 128, 128)
            strip = out_ref[here_rows, columns]
            turned = jnp.transpose(strip.astype(jnp.float32)).astype(jnp.bfloat16)
            out_ref[columns, here_rows] = turned

    @pl.when(chip == 0)
    def first():
        of_chip(0)

    @pl.when(chip == 1)
    def second():
        of_chip(1)

    across = jnp.ones((1, span), jnp.float32)
    for tile in range(span // 128):
        across = across + jnp.sum(
            out_ref[pl.ds(tile * 128, 128), :].astype(jnp.float32), axis=0, keepdims=True
        )
    across = lax.rsqrt(across)
    for tile in range(span // 128):
        strip = out_ref[pl.ds(tile * 128, 128), :].astype(jnp.float32)
        down = lax.rsqrt(1.0 + jnp.sum(strip, axis=1, keepdims=True))
        out_ref[pl.ds(tile * 128, 128), :] = (strip * down * across).astype(jnp.bfloat16)


def normalized_block(own, sibling, near, far, place):
    span = own.shape[1]
    return pl.pallas_call(
        assemble,
        out_shape=jax.ShapeDtypeStruct((span, span), jnp.bfloat16),
        in_specs=[pl.BlockSpec(memory_space=pltpu.SMEM)]
        + [pl.BlockSpec(memory_space=pltpu.HBM)] * 4,
        out_specs=pl.BlockSpec(memory_space=pltpu.VMEM),
        scratch_shapes=[pltpu.SemaphoreType.DMA((4,))],
        compiler_params=pltpu.CompilerParams(vmem_limit_bytes=VMEM_BYTES),
        cost_estimate=NO_COST,
        name="normalized_block",
    )(place, own, sibling, near, far)


def pack_kernel(
    keep_ref, row_codes_ref, col_codes_ref, row_keys_ref, col_keys_ref, weight_ref, out_ref,
    masked, picked, rows_hot, cols_hot
):
    tile_rows, tile_cols = weight_ref.shape
    blocks_down, blocks_across = keep_ref.shape
    groups, ignored, lanes = out_ref.shape
    send_cap, own_cap = rows_hot.shape[0] // groups, cols_hot.shape[0] // groups
    high, wide = tile_rows // blocks_down, tile_cols // blocks_across
    for down in range(blocks_down):
        for across in range(blocks_across):
            rows, columns = pl.ds(down * high, high), pl.ds(across * wide, wide)
            own, other = row_codes_ref[rows, :], col_codes_ref[:, columns]
            linked = (own == other) & (own % 2 == 1) & (keep_ref[down, across] == 1)
            weight = weight_ref[rows, columns].astype(jnp.float32)
            masked[rows, columns] = jnp.where(linked, weight, 0.0).astype(jnp.bfloat16)

    def one_hot(keys, start, count):
        standing = lax.broadcasted_iota(jnp.int32, (count, keys.shape[1]), 0) + start
        return jnp.where(standing == keys, 1.0, 0.0).astype(jnp.bfloat16)

    for group in range(groups):
        rows_hot[pl.ds(group * send_cap, send_cap), :] = one_hot(
            row_keys_ref[...], group * send_cap, send_cap
        )
        cols_hot[pl.ds(group * own_cap, own_cap), :] = one_hot(
            col_keys_ref[...], group * own_cap, own_cap
        )
    for tile in range(tile_cols // 256):
        columns = pl.ds(tile * 256, 256)
        picked[:, columns] = jnp.dot(
            rows_hot[...], masked[:, columns], preferred_element_type=jnp.float32
        ).astype(jnp.bfloat16)
    whole, half = own_cap // lanes, send_cap // 2
    for group in range(groups):
        packed = lax.dot_general(
            cols_hot[pl.ds(group * own_cap, own_cap), :],
            picked[pl.ds(group * send_cap, send_cap), :],
            (((1,), (1,)), ((), ())),
            preferred_element_type=jnp.float32,
        ).T
        for tile in range(whole):
            out_ref[group, pl.ds(tile * send_cap, send_cap), :] = packed[
                :, tile * lanes : (tile + 1) * lanes
            ].astype(jnp.bfloat16)
        ends = jnp.concatenate(
            [packed[:half, whole * lanes :], packed[half:, whole * lanes :]], axis=1
        )
        out_ref[group, pl.ds(whole * send_cap, half), :] = ends.astype(jnp.bfloat16)


def packed_pieces(block_keep, row_codes, col_codes, row_keys, col_keys, edge_weight, caps, groups):
    own_cap, send_cap = caps
    tile_rows, tile_cols = edge_weight.shape
    high = own_cap // 128 * send_cap + send_cap // 2
    vector = pl.BlockSpec(memory_space=pltpu.VMEM)
    return pl.pallas_call(
        pack_kernel,
        out_shape=jax.ShapeDtypeStruct((groups, high, 128), jnp.bfloat16),
        in_specs=[pl.BlockSpec(memory_space=pltpu.SMEM)] + [vector] * 5,
        out_specs=vector,
        scratch_shapes=[
            pltpu.VMEM((tile_rows, tile_cols), jnp.bfloat16),
            pltpu.VMEM((groups * send_cap, tile_cols), jnp.bfloat16),
            pltpu.VMEM((groups * send_cap, tile_rows), jnp.bfloat16),
            pltpu.VMEM((groups * own_cap, tile_cols), jnp.bfloat16),
        ],
        compiler_params=pltpu.CompilerParams(vmem_limit_bytes=VMEM_BYTES),
        cost_estimate=NO_COST,
        name="packed_pieces",
    )(block_keep, row_codes[:, None], col_codes[None], row_keys[None], col_keys[None], edge_weight)


def normal_share(mixed):
    return 0.5 * (1.0 + lax.erf(mixed * 0.5**0.5))


def norm_forward(mixed):
    active = mixed * normal_share(mixed)
    centered = active - jnp.mean(active, axis=-1, keepdims=True)
    scale = lax.rsqrt(jnp.mean(centered * centered, axis=-1, keepdims=True) + 1e-05)
    return centered * scale, scale


def norm_backward(mixed, upstream, gain, valid):
    normed, scale = norm_forward(mixed)
    upstream = upstream * valid
    inner = upstream * gain
    inner = inner - jnp.mean(inner, axis=-1, keepdims=True) - normed * jnp.mean(
        inner * normed, axis=-1, keepdims=True
    )
    density = jnp.exp(-0.5 * mixed * mixed) * (1.0 / (2.0 * math.pi) ** 0.5)
    low = (inner * scale * (normal_share(mixed) + mixed * density)).astype(jnp.bfloat16)
    rest = [low.astype(jnp.float32), upstream * normed, upstream]
    return low, [jnp.sum(value, axis=0, keepdims=True) for value in rest]


def weight_gradient(turned_ref, low, core, mine_ref, other_ref):
    parts = mine_ref.shape[0]
    part = turned_ref.shape[0] // (2 * parts)

    def halves(first_ref, second_ref):
        for place in range(2 * parts):
            out_ref = second_ref if place % 2 else first_ref
            out_ref[place // 2, :part, :] = jnp.dot(
                turned_ref[place * part : (place + 1) * part, :],
                low,
                preferred_element_type=jnp.float32,
            ).astype(jnp.bfloat16)

    @pl.when(core == 0)
    def low_half_first():
        halves(mine_ref, other_ref)

    @pl.when(core == 1)
    def high_half_first():
        halves(other_ref, mine_ref)


def forward_step(step, powers_ref, all_ref, own_ref, weights, bias_ref, turned, mixed):
    terms, own_cap, span = powers_ref.shape
    fan_in = own_ref.shape[1]

    @pl.when(step == 0)
    def first():
        turned[:fan_in, :] = own_ref[...].T
        mixed[...] = bias_ref[...] + jnp.dot(
            own_ref[...], weights[0][0], preferred_element_type=jnp.float32
        )

    low = jnp.dot(
        powers_ref[...].reshape(terms * own_cap, span),
        all_ref[...],
        preferred_element_type=jnp.float32,
    ).astype(jnp.bfloat16)
    total = mixed[...]
    for term in range(terms):
        part = low[term * own_cap : (term + 1) * own_cap]
        start = pl.multiple_of((1 + step * terms + term) * fan_in, fan_in)
        turned[pl.ds(start, fan_in), :] = part.T
        total = total + jnp.dot(part, weights[1 + term][0], preferred_element_type=jnp.float32)
    mixed[...] = total


def layer_one_kernel(
    powers_ref,
    all_ref,
    own_ref,
    weight_0,
    weight_a,
    weight_b,
    weight_c,
    bias_ref,
    gain_ref,
    shift_ref,
    valid_ref,
    hidden_ref,
    turned_ref,
    mixed_ref,
):
    step = pl.program_id(0)
    weights = (weight_0, weight_a, weight_b, weight_c)
    forward_step(step, powers_ref, all_ref, own_ref, weights, bias_ref, turned_ref, mixed_ref)

    @pl.when(step == pl.num_programs(0) - 1)
    def finish_layer():
        normed, ignored = norm_forward(mixed_ref[...])
        hidden = (normed * gain_ref[...] + shift_ref[...]) * valid_ref[...]
        hidden_ref[...] = hidden.astype(jnp.bfloat16)


def layer_two_kernel(
    place_ref,
    powers_ref,
    all_ref,
    own_ref,
    weight_0,
    weight_a,
    weight_b,
    weight_c,
    bias_ref,
    gain_ref,
    shift_ref,
    valid_ref,
    upstream_ref,
    active_ref,
    low_ref,
    rest_ref,
    mine_ref,
    other_ref,
    turned,
    mixed,
):
    step = pl.program_id(0)
    weights = (weight_0, weight_a, weight_b, weight_c)
    forward_step(step, powers_ref, all_ref, own_ref, weights, bias_ref, turned, mixed)

    @pl.when(step == pl.num_programs(0) - 1)
    def finish_layer():
        normed, ignored = norm_forward(mixed[...])
        active = (normed * gain_ref[...] + shift_ref[...]) * valid_ref[...]
        active_ref[...] = active.astype(jnp.bfloat16)
        low, rest = norm_backward(
            mixed[...], upstream_ref[...].astype(jnp.float32), gain_ref[...], valid_ref[...]
        )
        low_ref[...] = low
        for place in range(3):
            rest_ref[place : place + 1, :] = rest[place]
        weight_gradient(turned, low, place_ref[1], mine_ref, other_ref)


def backward_step(step, powers_ref, all_ref, own_ref, weights, total):
    terms, own_cap, span = powers_ref.shape
    transposed = (((1,), (1,)), ((), ()))

    @pl.when(step == 0)
    def first():
        total[...] = lax.dot_general(
            own_ref[...], weights[0][0], transposed, preferred_element_type=jnp.float32
        )

    low = jnp.dot(
        powers_ref[...].reshape(terms * own_cap, span),
        all_ref[...],
        preferred_element_type=jnp.float32,
    ).astype(jnp.bfloat16)
    value = total[...]
    for term in range(terms):
        value = value + lax.dot_general(
            low[term * own_cap : (term + 1) * own_cap],
            weights[1 + term][0],
            transposed,
            preferred_element_type=jnp.float32,
        )
    total[...] = value


def back_two_kernel(
    place_ref,
    powers_ref,
    all_ref,
    own_ref,
    weight_0,
    weight_a,
    weight_b,
    weight_c,
    turned_ref,
    mixed_ref,
    gain_ref,
    valid_ref,
    rest_ref,
    low_ref,
    mine_ref,
    other_ref,
    total,
):
    step = pl.program_id(0)
    weights = (weight_0, weight_a, weight_b, weight_c)
    backward_step(step, powers_ref, all_ref, own_ref, weights, total)

    @pl.when(step == pl.num_programs(0) - 1)
    def finish_layer():
        low, rest = norm_backward(mixed_ref[...], total[...], gain_ref[...], valid_ref[...])
        low_ref[...] = low
        weight_gradient(turned_ref, low, place_ref[1], mine_ref, other_ref)
        part = turned_ref.shape[0] // 2
        extra = jnp.zeros((1, mine_ref.shape[1] - part, mine_ref.shape[2]), jnp.bfloat16)
        rows = rest + [rest_ref[place : place + 1, :] for place in range(3)]
        rows = jnp.concatenate(rows + [jnp.zeros((10, rows[0].shape[1]), jnp.float32)], axis=0)

        def below(first_ref, second_ref):
            first_ref[:, part:, :] = extra
            second_ref[:, part:, :] = extra
            first_ref[0, part : part + 16, :] = rows.astype(jnp.bfloat16)

        @pl.when(place_ref[1] == 0)
        def low_half_here():
            below(mine_ref, other_ref)

        @pl.when(place_ref[1] == 1)
        def low_half_there():
            below(other_ref, mine_ref)


def back_one_kernel(
    powers_ref, all_ref, own_ref, weight_0, weight_a, weight_b, weight_c, out_ref, total
):
    step = pl.program_id(0)
    weights = (weight_0, weight_a, weight_b, weight_c)
    backward_step(step, powers_ref, all_ref, own_ref, weights, total)

    @pl.when(step == pl.num_programs(0) - 1)
    def finish_layer():
        out_ref[...] = total[...].astype(jnp.bfloat16)


def layer_pass(kernel, name, place, powers, everyone, own, weight, others, outs, scratch):
    ignored, own_cap, span = powers.shape
    fan_in, width = weight.shape[1:]

    def whole(value):
        return pl.BlockSpec(value.shape, lambda step: (0,) * len(value.shape))

    def term_weight(term):
        return pl.BlockSpec((1, fan_in, width), lambda step: (1 + step * TERMS + term, 0, 0))

    in_specs = [
        pl.BlockSpec((TERMS, own_cap, span), lambda step: (step, 0, 0)),
        whole(everyone),
        whole(own),
        pl.BlockSpec((1, fan_in, width), lambda step: (0, 0, 0)),
    ]
    in_specs += [term_weight(term) for term in range(TERMS)] + [whole(value) for value in others]
    operands = [powers, everyone, own] + [weight] * (1 + TERMS) + list(others)
    if place is not None:
        in_specs = [pl.BlockSpec(memory_space=pltpu.SMEM)] + in_specs
        operands = [place] + operands
    return pl.pallas_call(
        kernel,
        grid=((ORDER - 1) // TERMS,),
        out_shape=outs,
        in_specs=in_specs,
        out_specs=[whole(value) for value in outs],
        scratch_shapes=[pltpu.VMEM(shape, dtype) for shape, dtype in scratch],
        compiler_params=pltpu.CompilerParams(vmem_limit_bytes=VMEM_BYTES),
        cost_estimate=NO_COST,
        name=name,
    )(*operands)


def finish_kernel(scalars_ref, pair_ref, siblings_ref, other_ref, out_ref, *small_refs):
    step = pl.program_id(0)
    part = out_ref.shape[1]
    held = pl.num_programs(0) // 2
    for here, values_ref in ((step < held, pair_ref), (step >= held, siblings_ref)):
        @pl.when(here & (scalars_ref[0] == 1))
        def fast_form():
            out_ref[0] = values_ref[0, :part, :].astype(jnp.float32)

        for small_ref in small_refs:
            @pl.when(here & (scalars_ref[1 + step] == 0))
            def small_sums():
                small_ref[...] = values_ref[0, part : part + 16, :].astype(jnp.float32)

    @pl.when(scalars_ref[0] == 0)
    def general_form():
        out_ref[0] = other_ref[0].astype(jnp.float32)


def finished(scalars, pair, siblings, other, with_small=False):
    count, part, width = other.shape
    out, held = (1, part, width), (1,) + pair.shape[1:]
    out_specs = [pl.BlockSpec(out, lambda step, ref: (ref[1 + step], 0, 0))]
    out_shape = [jax.ShapeDtypeStruct(other.shape, jnp.float32)]
    if with_small:
        out_specs.append(pl.BlockSpec((16, width), lambda step, ref: (0, 0)))
        out_shape.append(jax.ShapeDtypeStruct((16, width), jnp.float32))
    return pl.pallas_call(
        finish_kernel,
        grid_spec=pltpu.PrefetchScalarGridSpec(
            num_scalar_prefetch=1,
            grid=(count,),
            in_specs=[
                pl.BlockSpec(held, lambda step, ref: (jnp.minimum(step, count // 2 - 1), 0, 0)),
                pl.BlockSpec(held, lambda step, ref: (jnp.maximum(step - count // 2, 0), 0, 0)),
                pl.BlockSpec(out, lambda step, ref: ((1 - ref[0]) * ref[1 + step], 0, 0)),
            ],
            out_specs=out_specs,
        ),
        out_shape=out_shape,
        compiler_params=pltpu.CompilerParams(vmem_limit_bytes=VMEM_BYTES),
        cost_estimate=pl.CostEstimate(
            flops=other.size, bytes_accessed=6 * other.size, transcendentals=0
        ),
        name="finished",
    )(scalars, pair, siblings, other)


def unpack_kernel(place_ref, pieces_ref, keys_ref, own_ref, quadrant_ref, columns, hot):
    groups, high, lanes = pieces_ref.shape
    own_cap, span = own_ref.shape
    whole = own_cap // lanes
    send_cap = keys_ref.shape[1] // groups
    half, rest = send_cap // 2, own_cap - whole * lanes
    for group in range(groups):
        start = group * send_cap
        for tile in range(whole):
            columns[start : start + send_cap, tile * lanes : (tile + 1) * lanes] = pieces_ref[
                group, tile * send_cap : (tile + 1) * send_cap, :
            ]
        ends = pieces_ref[group, whole * send_cap :, :]
        columns[start : start + half, whole * lanes :] = ends[:, :rest]
        columns[start + half : start + send_cap, whole * lanes :] = ends[:, rest:]
    standing = lax.broadcasted_iota(jnp.int32, hot.shape, 0)
    hot[...] = jnp.where(standing == keys_ref[...], 1.0, 0.0).astype(jnp.bfloat16)
    block = jnp.dot(hot[...], columns[...], preferred_element_type=jnp.float32)
    own_ref[...] = block.T.astype(jnp.bfloat16)
    middle = span // 2

    @pl.when(place_ref[0] == 0)
    def first():
        quadrant_ref[...] = own_ref[:, :middle]

    @pl.when(place_ref[0] == 1)
    def second():
        quadrant_ref[...] = own_ref[:, middle:]


def unpacked_block(pieces, keys, place, own_cap, span):
    vector = pl.BlockSpec(memory_space=pltpu.VMEM)
    return pl.pallas_call(
        unpack_kernel,
        out_shape=[
            jax.ShapeDtypeStruct((own_cap, span), jnp.bfloat16),
            jax.ShapeDtypeStruct((own_cap, span // 2), jnp.bfloat16),
        ],
        in_specs=[pl.BlockSpec(memory_space=pltpu.SMEM), vector, vector],
        out_specs=[vector, vector],
        scratch_shapes=[
            pltpu.VMEM((keys.shape[1], own_cap), jnp.bfloat16),
            pltpu.VMEM((span, keys.shape[1]), jnp.bfloat16),
        ],
        compiler_params=pltpu.CompilerParams(vmem_limit_bytes=VMEM_BYTES),
        cost_estimate=NO_COST,
        name="unpacked_block",
    )(place, pieces, keys)


def fit_kernel(codes_ref, out_ref, *, n_row, caps):
    own_cap, send_cap, seat_cap = caps
    codes = codes_ref[...]
    devices = codes.shape[0]
    n_col = devices // n_row
    label = lax.broadcasted_iota(jnp.int32, (devices, 128), 1)
    counts = jnp.zeros((devices, 128), jnp.float32)
    for cluster in range(CLUSTERS):
        here = jnp.where(codes == 2 * cluster + 1, 1.0, 0.0)
        counts = counts + jnp.where(
            label == cluster, jnp.sum(here, axis=1, keepdims=True), 0.0
        )
    sizes = jnp.sum(counts, axis=0, keepdims=True)
    across = jnp.broadcast_to(sizes, (128, 128))
    down = across.T
    first = lax.broadcasted_iota(jnp.int32, (128, 128), 0)
    second = lax.broadcasted_iota(jnp.int32, (128, 128), 1)
    ahead = (across > down) | ((across == down) & (second < first))
    ahead = ahead & (second < CLUSTERS)
    rank = jnp.sum(jnp.where(ahead, 1.0, 0.0), axis=1, keepdims=True).astype(jnp.int32)
    others = n_row - 1
    later = rank > others
    turn = jnp.zeros_like(rank)
    for count in range(1, CLUSTERS // others + 1):
        turn = turn + jnp.where(rank - 1 >= count * others, 1, 0)
    place = rank - 1 - turn * others
    group = jnp.where(rank == 0, 0, 1 + jnp.where(later, others - 1 - place, place))
    member = (group == second) & (first < CLUSTERS)
    held = jnp.dot(
        counts.astype(jnp.bfloat16),
        jnp.where(member, 1.0, 0.0).astype(jnp.bfloat16),
        preferred_element_type=jnp.float32,
    )
    by_row = jnp.zeros((1, 128), jnp.float32)
    for row in range(n_row):
        rows = jnp.sum(held[row * n_col : (row + 1) * n_col], axis=0, keepdims=True)
        by_row = jnp.maximum(by_row, rows)
    device = lax.broadcasted_iota(jnp.int32, (devices, 128), 0)
    by_col = jnp.zeros((1, 128), jnp.float32)
    for col in range(n_col):
        cols = jnp.where(device % n_col == col, held, 0.0)
        by_col = jnp.maximum(by_col, jnp.sum(cols, axis=0, keepdims=True))
    fits = (
        (jnp.max(by_col) <= own_cap) & (jnp.max(by_row) <= send_cap) & (jnp.max(held) <= seat_cap)
    )
    out_ref[0] = jnp.where(fits, 1, 0)


def fits_in(codes, n_row, caps):
    fits = pl.pallas_call(
        functools.partial(fit_kernel, n_row=n_row, caps=caps),
        out_shape=jax.ShapeDtypeStruct((1,), jnp.int32),
        in_specs=[pl.BlockSpec(memory_space=pltpu.VMEM)],
        out_specs=pl.BlockSpec(memory_space=pltpu.SMEM),
        cost_estimate=NO_COST,
        name="fits",
    )(codes.reshape(-1, codes.shape[-1]))
    return fits


def exclusive_counts(member):
    count = member.shape[-1]
    before = jnp.arange(count)[:, None] < jnp.arange(count)[None, :]
    return jnp.dot(
        member.astype(jnp.bfloat16),
        before.astype(jnp.bfloat16),
        preferred_element_type=jnp.float32,
    ).astype(jnp.int32)


def assign(codes, n_row):
    cluster, valid = codes >> 1, codes & 1
    labels = jnp.arange(CLUSTERS)
    sizes = jnp.sum(
        (cluster.reshape(1, -1) == labels[:, None]) & (valid.reshape(1, -1) == 1), axis=1
    )
    ahead = (sizes[None, :] > sizes[:, None]) | (
        (sizes[None, :] == sizes[:, None]) & (labels[None, :] < labels[:, None])
    )
    rank = jnp.sum(ahead, axis=1)
    others = n_row - 1
    turn, place = (rank - 1) // others, (rank - 1) % others
    group = jnp.where(rank == 0, 0, 1 + jnp.where(turn == 0, place, others - 1 - place))
    of_node = jnp.sum(
        jnp.where(cluster[None] == labels[:, None, None, None], group[:, None, None, None], 0),
        axis=0,
    )
    return jnp.where(valid == 1, of_node, n_row)


def compact(
    codes,
    group,
    features,
    block_keep,
    edge_weight,
    weight_one,
    bias_one,
    gain_one,
    shift_one,
    weight_two,
    bias_two,
    gain_two,
    shift_two,
    cotangent,
    places_of,
    slots_of,
    seats_of,
    decide,
    sizes,
    caps,
):
    row, col = lax.axis_index("row"), lax.axis_index(COL)
    chip, core = lax.axis_index("chip"), lax.axis_index("core")
    n_row, n_col = sizes
    own_cap, send_cap, seat_cap = caps
    own_nodes, in_width = features.shape
    width = weight_two.shape[2]
    span = n_col * own_cap
    targets = jnp.arange(n_row)

    def in_col(value):
        return lax.dynamic_index_in_dim(value, col, 1, False).reshape(-1)

    def in_row(value):
        return lax.dynamic_index_in_dim(value, row, 0, False).reshape(-1)

    row_group, col_group = in_row(group), in_col(group)
    row_slots, col_places = in_row(slots_of(group)), in_col(places_of(group))
    row_keys = jnp.where(row_slots < send_cap, row_group * send_cap + row_slots, -1)
    col_keys = jnp.where(col_places < own_cap, col_group * own_cap + col_places, -1)
    pieces = packed_pieces(
        block_keep,
        in_row(codes),
        in_col(codes),
        row_keys,
        col_keys,
        edge_weight,
        (own_cap, send_cap),
        n_row,
    )
    pieces, codes = lax.optimization_barrier((pieces, codes))
    group = assign(codes, n_row)
    places, slots, seats = places_of(group), slots_of(group), seats_of(group)

    standing = jnp.arange(n_col)[None, :, None] * own_cap + places
    fits_here = jnp.where(group == row, standing, -1).reshape(n_row, -1)
    slot_of = slots.reshape(n_row, -1)
    target = jnp.max(
        jnp.where(
            slot_of[:, None, :] == jnp.arange(send_cap)[None, :, None], fits_here[:, None, :], -1
        ),
        axis=2,
    )
    keys = target.reshape(1, -1)

    def to_partner(value, step):
        return lax.ppermute(value, "row", [(place, place ^ step) for place in range(n_row)])

    partners = row ^ targets
    group_here = lax.dynamic_index_in_dim(in_row(group).reshape(n_col, -1), col, 0, False)
    seat_here = lax.dynamic_index_in_dim(in_row(seats).reshape(n_col, -1), col, 0, False)

    def seat_of_node(groups):
        hot = (group_here[None, None, :] == groups[:, None, None]) & (
            seat_here[None, None, :] == jnp.arange(seat_cap)[None, :, None]
        )
        return hot.astype(jnp.bfloat16).reshape(n_row * seat_cap, own_nodes)

    enter_home = seat_of_node(targets).T
    enter_partner = seat_of_node(partners)
    both = jnp.dot(enter_partner, jnp.concatenate([features, cotangent], axis=1))
    both = both.reshape(n_row, seat_cap, -1)
    enter_partner = enter_partner.T
    pieces = trade(pieces, "row")
    both, codes = lax.optimization_barrier((both, codes))
    both = [both[step] for step in range(n_row)]
    nearest = jnp.concatenate([both[0], to_partner(both[1], 1)])
    both = both[2:]
    fits, others = decide(codes)
    group_col = lax.dynamic_index_in_dim(group, col, 1, False)
    seats_col = lax.dynamic_index_in_dim(seats, col, 1, False)
    places_col = lax.dynamic_index_in_dim(places, col, 1, False)
    seated = (group_col == row)[:, None, :] & (
        seats_col[:, None, :] == jnp.arange(seat_cap)[None, :, None]
    )
    place_of_seat = jnp.max(jnp.where(seated, places_col[:, None, :], -1), axis=2)
    from_partner = jnp.max(
        jnp.where((partners[:, None] == targets)[:, :, None], place_of_seat[None], -1), axis=1
    )
    arrive = from_partner.reshape(1, -1) == jnp.arange(own_cap)[:, None]
    arrive = arrive.astype(jnp.bfloat16)
    leave_group = place_of_seat.reshape(-1, 1) == jnp.arange(own_cap)
    leave_group = leave_group.astype(jnp.bfloat16)
    mine = jnp.dot(arrive[:, : 2 * seat_cap], nearest)
    arrive = arrive[:, 2 * seat_cap :]
    leave_partner = jnp.concatenate([from_partner[::2], from_partner[1::2]])
    leave_partner = leave_partner.reshape(-1, 1) == jnp.arange(own_cap)
    leave_partner = leave_partner.astype(jnp.bfloat16)
    held_count = jnp.sum(group_col == row)
    valid_rows = (jnp.arange(own_cap) < held_count).astype(jnp.float32)[:, None]
    place = jnp.stack([chip, core]).astype(jnp.int32)
    quarters = jnp.stack([col, (1 - chip) * 2 + core, chip * 2 + 1 - core, 3 - col])
    quarters = jnp.concatenate([fits, quarters.astype(jnp.int32)])
    own_halves = jnp.concatenate([fits, jnp.stack([core, 1 - core]).astype(jnp.int32)])
    scalars = (chip, 1 - chip, col * own_cap)
    scalars = tuple(value.astype(jnp.uint32) for value in scalars) + (chip == 0, core == 0, place)
    scalars = scalars + (quarters, own_halves)
    homes = enter_home, enter_partner, leave_group, leave_partner
    pieces, mine, both, keys, arrive, homes, valid_rows, others, scalars = lax.optimization_barrier(
        (pieces, mine, both, keys, arrive, homes, valid_rows, others, scalars)
    )
    enter_home, enter_partner, leave_group, leave_partner = homes
    this_chip, other_chip, own_start, first_chip, first_core = scalars[:5]
    place, quarters, own_halves = scalars[5:]

    own_block, quadrant = unpacked_block(pieces, keys, place, own_cap, span)
    quadrant = swap(quadrant, "chip")
    both = [to_partner(both[step - 2], step) for step in range(2, n_row)]
    sibling = swap(own_block, "core")
    quadrant, *early = lax.optimization_barrier((quadrant, *both[:-2]))
    adjacency = normalized_block(own_block, sibling, quadrant, swap(quadrant, "core"), place)
    adjacency, *late = lax.optimization_barrier((adjacency, *both[-2:]))
    both = early + late
    mine = mine + jnp.dot(arrive, jnp.concatenate(both))
    features_own, cotangent_own = mine[:, :in_width], mine[:, in_width:]
    sibling = swap(features_own, "core")

    first = (own_start + jnp.arange(own_cap, dtype=jnp.uint32))[:, None]
    first = first == jnp.arange(span, dtype=jnp.uint32)[None, :]
    previous = first.astype(jnp.float32)
    current = -lax.dynamic_slice_in_dim(adjacency, own_start, own_cap, 0).astype(jnp.float32)
    lowered = [current.astype(jnp.bfloat16)]
    for position in range(2, ORDER):
        upcoming = (
            -2.0 * jnp.dot(lowered[-1], adjacency, preferred_element_type=jnp.float32) - previous
        )
        low = upcoming.astype(jnp.bfloat16)
        if position == 4:
            low, sibling = lax.optimization_barrier((low, sibling))
            features_chip = joined(features_own, sibling, first_core)
            partner = swap(features_chip, "chip")
        if position == 8:
            low, partner = lax.optimization_barrier((low, partner))
            features_all = joined(features_chip, partner, first_chip)
        previous, current = current, upcoming
        lowered.append(low)
    powers = jnp.concatenate(lowered, axis=0).reshape(ORDER - 1, own_cap, span)

    def everywhere(value_low):
        return lax.all_gather(value_low, COL, axis=0, tiled=True)

    def chosen(value, other):
        return jnp.where(quarters[0] == 1, value.astype(jnp.float32), other.astype(jnp.float32))

    def shaped(*shape, dtype=jnp.bfloat16):
        return jax.ShapeDtypeStruct(shape, dtype)

    part_one, part_two = ORDER * in_width // 2, ORDER * width // n_col
    padded = -(-(part_one + 16) // (16 * n_row)) * (16 * n_row)
    hidden, turned_one, mixed_one = layer_pass(
        layer_one_kernel,
        "layer_one",
        None,
        powers,
        features_all,
        features_own,
        weight_one,
        [bias_one[None], gain_one[None], shift_one[None], valid_rows],
        [
            shaped(own_cap, width),
            shaped(2 * part_one, own_cap),
            shaped(own_cap, width, dtype=jnp.float32),
        ],
        [],
    )
    activations, low_two, rest_two, mine, other = layer_pass(
        layer_two_kernel,
        "layer_two",
        place,
        powers,
        everywhere(hidden),
        hidden,
        weight_two,
        [bias_two[None], gain_two[None], shift_two[None], valid_rows, cotangent_own],
        [
            shaped(own_cap, width),
            shaped(own_cap, width),
            shaped(3, width, dtype=jnp.float32),
            shaped(2, part_two, width),
            shaped(2, part_two, width),
        ],
        [((n_col * part_two, own_cap), jnp.bfloat16), ((own_cap, width), jnp.float32)],
    )

    def add_cores(mine, other, axis=0):
        got = swap(other, "core")
        return tuple(
            added(
                lax.dynamic_index_in_dim(mine, index, axis, False),
                lax.dynamic_index_in_dim(got, index, axis, False),
            )
            for index in (this_chip, other_chip)
        )

    leaving = jnp.dot(leave_partner, activations).reshape(n_row, seat_cap, width)
    near, far = leaving[: n_row // 2], leaving[n_row // 2 :]
    far = to_partner(far, 1)
    here, there = add_cores(mine, other)
    everyone_two, there, far = lax.optimization_barrier((everywhere(low_two), there, far))
    there = swap(there, "chip")
    arrived = [jnp.stack([near[0], far[0]])] + [
        to_partner(jnp.stack([near[half], far[half]]), 2 * half) for half in range(1, n_row // 2)
    ]
    low_one, mine, other = layer_pass(
        back_two_kernel,
        "back_two",
        place,
        powers,
        everyone_two,
        low_two,
        weight_two,
        [turned_one, mixed_one, gain_one[None], valid_rows, rest_two],
        [shaped(own_cap, width), shaped(1, padded, width), shaped(1, padded, width)],
        [((own_cap, width), jnp.float32)],
    )
    low_one, there, arrived = lax.optimization_barrier((low_one, there, arrived))
    second = added(here, there).reshape(n_row, -1, width)
    many = second.shape[1]
    low_one, second = lax.optimization_barrier((low_one, second))
    second = trade(second, "row")
    mine, other = (value.reshape(n_row, 2, -1, width) for value in (mine, other))
    here, there = add_cores(mine, other, 1)
    there = swap(there, "chip")
    first = added(here, there)
    second = jnp.sum(second.astype(jnp.float32), axis=0).astype(jnp.bfloat16)
    second = jnp.broadcast_to(second[None], (n_row,) + second.shape)
    mixed = jnp.concatenate([second, first], axis=1)
    low_one, mixed = lax.optimization_barrier((low_one, mixed))
    everyone_one = everywhere(low_one)
    mixed = trade(mixed, "row")
    (input_grad,) = layer_pass(
        back_one_kernel,
        "back_one",
        None,
        powers,
        everyone_one,
        low_one,
        weight_one,
        [],
        [shaped(own_cap, in_width)],
        [((own_cap, in_width), jnp.float32)],
    )
    leaving = jnp.dot(leave_group, input_grad)
    leaving = leaving.reshape(n_row, seat_cap * in_width // width, width)
    arrived = jnp.concatenate(arrived).reshape(-1, width)
    home = jnp.dot(enter_partner, arrived, preferred_element_type=jnp.float32)
    home = chosen(home, others[0])
    mixed, leaving, home = lax.optimization_barrier((mixed, leaving, home))
    first = jnp.sum(mixed[:, many:].astype(jnp.float32), axis=0).astype(jnp.bfloat16)
    partner, mixed = lax.optimization_barrier((swap(first, "chip"), mixed))
    second = mixed[:, :many].reshape(1, -1, width)
    partner_two = swap(second, "chip")
    first = joined(first, partner, first_chip)
    share = first.shape[0]
    first = jnp.broadcast_to(first[None], (n_row,) + first.shape)
    first = trade(jnp.concatenate([first, leaving], axis=1), "row")
    second = jnp.concatenate([second, partner_two])
    (second,) = finished(quarters, second, swap(second, "core"), others[3])
    first, second = lax.optimization_barrier((first, second))
    mine = first[:, :share].reshape(1, -1, width)
    siblings = swap(mine, "core")
    back = first[:, share:].reshape(n_row * seat_cap, in_width)
    home_grad = jnp.dot(enter_home, back, preferred_element_type=jnp.float32)
    home_grad = chosen(home_grad, others[1])
    first, small = finished(own_halves, mine, siblings, others[2], True)
    return home, home_grad, first, second, chosen(small[:6], others[4])


def general(
    codes,
    features,
    block_keep,
    edge_weight,
    weight_one,
    bias_one,
    gain_one,
    shift_one,
    weight_two,
    bias_two,
    gain_two,
    shift_two,
    cotangent,
    node_valid,
):
    row, col = lax.axis_index("row"), lax.axis_index(COL)
    row_codes = lax.dynamic_index_in_dim(codes, row, 0, False).reshape(-1)
    col_codes = lax.dynamic_index_in_dim(codes, col, 1, False).reshape(-1)
    tile_rows, tile_cols = edge_weight.shape
    blocks_down, blocks_across = block_keep.shape
    block_side = tile_rows // blocks_down
    linked = (row_codes[:, None] == col_codes[None, :]) & (row_codes[:, None] & 1 == 1)
    linked = linked.reshape(blocks_down, block_side, blocks_across, block_side) & (
        block_keep[:, None, :, None] == 1
    )
    masked = edge_weight * linked.reshape(tile_rows, tile_cols).astype(jnp.bfloat16)
    degree_rows = 1.0 + lax.psum(jnp.sum(masked, axis=1, dtype=jnp.float32), COL)
    own_nodes = features.shape[0]
    own_degree = lax.dynamic_slice_in_dim(
        degree_rows, lax.axis_index(COL) * own_nodes, own_nodes, 0
    )
    degree_cols = lax.all_gather(own_degree, "row", axis=0, tiled=True)
    adjacency = (
        masked.astype(jnp.float32)
        * lax.rsqrt(degree_rows)[:, None]
        * lax.rsqrt(degree_cols)[None, :]
    ).astype(jnp.bfloat16)
    valid_rows = node_valid.astype(jnp.float32)
    stacked_one, mixed_one, hidden = layer_forward(
        adjacency,
        features.astype(jnp.float32),
        weight_one,
        bias_one,
        gain_one,
        shift_one,
        valid_rows,
    )
    stacked_two, mixed_two, activations = layer_forward(
        adjacency, hidden, weight_two, bias_two, gain_two, shift_two, valid_rows
    )
    hidden_grad, weight_two_grad, bias_two_grad, gain_two_grad, shift_two_grad = layer_backward(
        adjacency,
        stacked_two,
        mixed_two,
        cotangent.astype(jnp.float32),
        weight_two,
        gain_two,
        shift_two,
        valid_rows,
    )
    input_grad, weight_one_grad, bias_one_grad, gain_one_grad, shift_one_grad = layer_backward(
        adjacency, stacked_one, mixed_one, hidden_grad, weight_one, gain_one, shift_one, valid_rows
    )
    summed = lax.psum(
        (
            weight_one_grad,
            bias_one_grad,
            gain_one_grad,
            shift_one_grad,
            weight_two_grad,
            bias_two_grad,
            gain_two_grad,
            shift_two_grad,
        ),
        ("row",) + COL,
    )
    weight_one_grad, bias_one_grad, gain_one_grad, shift_one_grad = (
        summed[0],
        summed[1],
        summed[2],
        summed[3],
    )
    weight_two_grad, bias_two_grad, gain_two_grad, shift_two_grad = (
        summed[4],
        summed[5],
        summed[6],
        summed[7],
    )
    return (
        activations,
        input_grad,
        weight_one_grad,
        bias_one_grad,
        gain_one_grad,
        shift_one_grad,
        weight_two_grad,
        bias_two_grad,
        gain_two_grad,
        shift_two_grad,
    )


def local(n_row, n_col, *args):
    (
        features,
        node_valid,
        cluster,
        block_keep,
        edge_weight,
        weight_one,
        bias_one,
        gain_one,
        shift_one,
        weight_two,
        bias_two,
        gain_two,
        shift_two,
        cotangent,
    ) = args
    own_nodes, in_width = features.shape
    own_cap = own_nodes * n_row * 5 // 16
    send_cap = own_nodes * n_col * 11 // 32
    seat_cap = own_nodes * 7 // 16
    codes = broadcast_along(cluster * 2 + node_valid, ("row",) + COL, n_row * n_col)
    codes = codes.reshape(n_row, n_col, own_nodes)
    shared = (
        block_keep,
        edge_weight,
        weight_one,
        bias_one,
        gain_one,
        shift_one,
        weight_two,
        bias_two,
        gain_two,
        shift_two,
        cotangent,
    )

    def slow():
        return general(codes, features, *shared, node_valid)

    held = (ORDER - 1) * own_cap * own_cap * n_col * 2
    if held > HELD_BYTES or n_col != 4 or n_row < 2 or n_row & (n_row - 1):
        return slow()
    group = assign(codes, n_row)

    def member_of(group):
        return group[None] == jnp.arange(n_row)[:, None, None, None]

    def places_of(group):
        member = member_of(group).transpose(0, 2, 1, 3).reshape(n_row, n_col, -1)
        places = jnp.sum(jnp.where(member, exclusive_counts(member), 0), axis=0)
        return places.reshape(n_col, n_row, own_nodes).transpose(1, 0, 2)

    def slots_of(group):
        member = member_of(group).reshape(n_row, n_row, -1)
        slots = jnp.sum(jnp.where(member, exclusive_counts(member), 0), axis=0)
        return slots.reshape(n_row, n_col, own_nodes)

    def seats_of(group):
        member = member_of(group)
        return jnp.sum(jnp.where(member, exclusive_counts(member), 0), axis=0)

    width = weight_two.shape[2]

    def instead(state):
        made = slow()
        small = jnp.stack([made[place] for place in (3, 4, 5, 7, 8, 9)])
        return (jnp.ones_like(state[0]),) + tuple(
            value.astype(jnp.bfloat16).reshape(like.shape)
            for value, like in zip((made[0], made[1], made[2], made[6], small), state[1:])
        )

    shapes = (
        (own_nodes, width),
        (own_nodes, in_width),
        (2, ORDER * in_width // 2, width),
        (n_col, ORDER * width // n_col, width),
        (6, width),
    )

    def decide(codes):
        fits = fits_in(codes, n_row, (own_cap, send_cap, seat_cap))
        others = lax.while_loop(
            lambda state: state[0][0] == 0,
            instead,
            (fits,) + tuple(jnp.zeros(shape, jnp.bfloat16) for shape in shapes),
        )[1:]
        return fits, others

    home, home_grad, first, second, small = compact(
        codes,
        group,
        features,
        *shared,
        places_of,
        slots_of,
        seats_of,
        decide,
        (n_row, n_col),
        (own_cap, send_cap, seat_cap),
    )
    return (
        home,
        home_grad,
        first.reshape(weight_one.shape),
        small[0],
        small[1],
        small[2],
        second.reshape(weight_two.shape),
        small[3],
        small[4],
        small[5],
    )


def solution(mesh):
    n_row, n_col = mesh.shape["row"], mesh.shape["col"]
    by_core = jax.sharding.Mesh(
        mesh.devices.reshape(n_row, n_col // 2, 2), ("row", "chip", "core")
    )
    nodes = ("row", "chip", "core")
    placed = (
        P(nodes, None),
        P(nodes),
        P(nodes),
        P("row", COL),
        P("row", COL),
        P(),
        P(),
        P(),
        P(),
        P(),
        P(),
        P(),
        P(),
        P(nodes, None),
    )
    return jax.shard_map(
        functools.partial(local, n_row, n_col),
        mesh=by_core,
        in_specs=placed,
        out_specs=(P(nodes, None), P(nodes, None), P(), P(), P(), P(), P(), P(), P(), P()),
        check_vma=False,
    )
```

```python
import functools
import math

import jax
import jax.numpy as jnp
from jax import lax
from jax.experimental import pallas as pl
from jax.experimental.pallas import tpu as pltpu
from jax.sharding import PartitionSpec as P

ORDER = 13
CLUSTERS = 16
HELD_BYTES = 1 << 25
VMEM_BYTES = 32 << 20
TERMS = 3
NO_COST = pl.CostEstimate(flops=1, bytes_accessed=1, transcendentals=0)
COL = ("chip", "core")


def finish(mixed, gain, shift, valid_rows):
    active = jax.nn.gelu(mixed, approximate=False)
    centered = active - jnp.mean(active, axis=-1, keepdims=True)
    variance = jnp.mean(centered * centered, axis=-1, keepdims=True)
    return (centered * lax.rsqrt(variance + 1e-05) * gain + shift) * valid_rows[:, None]


def forward_product(adjacency, piece_low):
    partial_value = jnp.dot(
        adjacency,
        lax.all_gather(piece_low, "row", axis=0, tiled=True),
        preferred_element_type=jnp.float32,
    )
    return lax.psum_scatter(partial_value, COL, scatter_dimension=0, tiled=True)


def backward_product(adjacency, piece_low):
    partial_value = lax.dot_general(
        adjacency,
        lax.all_gather(piece_low, COL, axis=0, tiled=True),
        (((0,), (0,)), ((), ())),
        preferred_element_type=jnp.float32,
    )
    return lax.psum_scatter(
        partial_value.astype(jnp.bfloat16), "row", scatter_dimension=0, tiled=True
    ).astype(jnp.float32)


def layer_forward(adjacency, inputs, weight, bias, gain, shift, valid_rows):
    first_low = inputs.astype(jnp.bfloat16)
    second = -forward_product(adjacency, first_low)
    second_low = second.astype(jnp.bfloat16)

    def advance(state_pair, unused):
        previous, current, current_low = state_pair
        upcoming = -2.0 * forward_product(adjacency, current_low) - previous
        upcoming_low = upcoming.astype(jnp.bfloat16)
        return ((current, upcoming, upcoming_low), upcoming_low)

    ignored, others = lax.scan(advance, (inputs, second, second_low), None, length=ORDER - 2)
    stacked = jnp.concatenate([first_low[None], second_low[None], others], axis=0)
    mixed = jnp.einsum("kni,kio->no", stacked, weight, preferred_element_type=jnp.float32) + bias
    return (stacked, mixed, finish(mixed, gain, shift, valid_rows))


def layer_backward(adjacency, stacked, mixed, upstream, weight, gain, shift, valid_rows):

    def local_finish(mixed_in, gain_in, shift_in):
        return finish(mixed_in, gain_in, shift_in, valid_rows)

    ignored, pullback = jax.vjp(local_finish, mixed, gain, shift)
    mixed_grad, gain_grad, shift_grad = pullback(upstream)
    mixed_low = mixed_grad.astype(jnp.bfloat16)
    bias_grad = jnp.sum(mixed_low.astype(jnp.float32), axis=0)
    weight_grad = jnp.einsum("kni,no->kio", stacked, mixed_low, preferred_element_type=jnp.float32)
    direct = jnp.einsum("no,kio->kni", mixed_low, weight, preferred_element_type=jnp.float32)

    def retreat(state_pair, direct_term):
        later_two, later_one = state_pair
        current = (
            direct_term
            - 2.0 * backward_product(adjacency, later_one.astype(jnp.bfloat16))
            - later_two
        )
        return ((later_one, current), None)

    start_pair = (jnp.zeros_like(direct[0]), direct[ORDER - 1])
    (second_grad, first_grad), unused = lax.scan(
        retreat, start_pair, direct[1 : ORDER - 1], reverse=True
    )
    input_grad = (
        direct[0] - backward_product(adjacency, first_grad.astype(jnp.bfloat16)) - second_grad
    )
    return (input_grad, weight_grad, bias_grad, gain_grad, shift_grad)


def swap(value, axis):
    return lax.ppermute(value, axis, [(0, 1), (1, 0)])


def trade(pieces, axis):
    return lax.all_to_all(pieces, axis, 0, 0, tiled=False)


def broadcast_along(value, axis, size):
    return trade(jnp.broadcast_to(value[None], (size,) + value.shape), axis)


def joined(mine, other, mine_first):
    return jnp.where(
        mine_first, jnp.concatenate([mine, other]), jnp.concatenate([other, mine])
    )


def added(mine, received):
    return (mine.astype(jnp.float32) + received.astype(jnp.float32)).astype(jnp.bfloat16)


def assemble(place_ref, own_ref, sibling_ref, near_ref, far_ref, out_ref, done):
    chip, core = place_ref[0], place_ref[1]
    own_cap, span = own_ref.shape
    half = span // 2

    def rows(of_chip, of_core):
        return pl.ds(pl.multiple_of((2 * of_chip + of_core) * own_cap, own_cap), own_cap)

    def fetch(source, of_chip, of_core, columns, place):
        target = out_ref.at[rows(of_chip, of_core), columns]
        return pltpu.make_async_copy(source, target, done.at[place])

    def quadrant_copies(here):
        there = 1 - here
        columns = pl.ds(there * half, half)
        return (
            fetch(near_ref, there, core, columns, 2),
            fetch(far_ref, there, 1 - core, columns, 3),
        )

    everything = pl.ds(0, span)
    top = (
        fetch(own_ref, chip, core, everything, 0),
        fetch(sibling_ref, chip, 1 - core, everything, 1),
    )

    def of_chip(here):
        there = 1 - here
        copies = top + quadrant_copies(here)
        for copy in copies:
            copy.start()
        for copy in copies:
            copy.wait()
        here_rows = pl.ds(here * half, half)
        for tile in range(half // 128):
            columns = pl.ds(there * half + tile * 128, 128)
            strip = out_ref[here_rows, columns]
            turned = jnp.transpose(strip.astype(jnp.float32)).astype(jnp.bfloat16)
            out_ref[columns, here_rows] = turned

    @pl.when(chip == 0)
    def first():
        of_chip(0)

    @pl.when(chip == 1)
    def second():
        of_chip(1)

    across = jnp.ones((1, span), jnp.float32)
    for tile in range(span // 128):
        across = across + jnp.sum(
            out_ref[pl.ds(tile * 128, 128), :].astype(jnp.float32), axis=0, keepdims=True
        )
    across = lax.rsqrt(across)
    for tile in range(span // 128):
        strip = out_ref[pl.ds(tile * 128, 128), :].astype(jnp.float32)
        down = lax.rsqrt(1.0 + jnp.sum(strip, axis=1, keepdims=True))
        out_ref[pl.ds(tile * 128, 128), :] = (strip * down * across).astype(jnp.bfloat16)


def normalized_block(own, sibling, near, far, place):
    span = own.shape[1]
    return pl.pallas_call(
        assemble,
        out_shape=jax.ShapeDtypeStruct((span, span), jnp.bfloat16),
        in_specs=[pl.BlockSpec(memory_space=pltpu.SMEM)]
        + [pl.BlockSpec(memory_space=pltpu.HBM)] * 4,
        out_specs=pl.BlockSpec(memory_space=pltpu.VMEM),
        scratch_shapes=[pltpu.SemaphoreType.DMA((4,))],
        compiler_params=pltpu.CompilerParams(vmem_limit_bytes=VMEM_BYTES),
        cost_estimate=NO_COST,
        name="normalized_block",
    )(place, own, sibling, near, far)


def pack_kernel(
    keep_ref, row_codes_ref, col_codes_ref, row_keys_ref, col_keys_ref, weight_ref, out_ref,
    masked, picked, rows_hot, cols_hot
):
    tile_rows, tile_cols = weight_ref.shape
    blocks_down, blocks_across = keep_ref.shape
    groups, ignored, lanes = out_ref.shape
    send_cap, own_cap = rows_hot.shape[0] // groups, cols_hot.shape[0] // groups
    high, wide = tile_rows // blocks_down, tile_cols // blocks_across
    for down in range(blocks_down):
        for across in range(blocks_across):
            rows, columns = pl.ds(down * high, high), pl.ds(across * wide, wide)
            own, other = row_codes_ref[rows, :], col_codes_ref[:, columns]
            linked = (own == other) & (own % 2 == 1) & (keep_ref[down, across] == 1)
            weight = weight_ref[rows, columns].astype(jnp.float32)
            masked[rows, columns] = jnp.where(linked, weight, 0.0).astype(jnp.bfloat16)

    def one_hot(keys, start, count):
        standing = lax.broadcasted_iota(jnp.int32, (count, keys.shape[1]), 0) + start
        return jnp.where(standing == keys, 1.0, 0.0).astype(jnp.bfloat16)

    for group in range(groups):
        rows_hot[pl.ds(group * send_cap, send_cap), :] = one_hot(
            row_keys_ref[...], group * send_cap, send_cap
        )
        cols_hot[pl.ds(group * own_cap, own_cap), :] = one_hot(
            col_keys_ref[...], group * own_cap, own_cap
        )
    for tile in range(tile_cols // 256):
        columns = pl.ds(tile * 256, 256)
        picked[:, columns] = jnp.dot(
            rows_hot[...], masked[:, columns], preferred_element_type=jnp.float32
        ).astype(jnp.bfloat16)
    whole, half = own_cap // lanes, send_cap // 2
    for group in range(groups):
        packed = lax.dot_general(
            cols_hot[pl.ds(group * own_cap, own_cap), :],
            picked[pl.ds(group * send_cap, send_cap), :],
            (((1,), (1,)), ((), ())),
            preferred_element_type=jnp.float32,
        ).T
        for tile in range(whole):
            out_ref[group, pl.ds(tile * send_cap, send_cap), :] = packed[
                :, tile * lanes : (tile + 1) * lanes
            ].astype(jnp.bfloat16)
        ends = jnp.concatenate(
            [packed[:half, whole * lanes :], packed[half:, whole * lanes :]], axis=1
        )
        out_ref[group, pl.ds(whole * send_cap, half), :] = ends.astype(jnp.bfloat16)


def packed_pieces(block_keep, row_codes, col_codes, row_keys, col_keys, edge_weight, caps, groups):
    own_cap, send_cap = caps
    tile_rows, tile_cols = edge_weight.shape
    high = own_cap // 128 * send_cap + send_cap // 2
    vector = pl.BlockSpec(memory_space=pltpu.VMEM)
    return pl.pallas_call(
        pack_kernel,
        out_shape=jax.ShapeDtypeStruct((groups, high, 128), jnp.bfloat16),
        in_specs=[pl.BlockSpec(memory_space=pltpu.SMEM)] + [vector] * 5,
        out_specs=vector,
        scratch_shapes=[
            pltpu.VMEM((tile_rows, tile_cols), jnp.bfloat16),
            pltpu.VMEM((groups * send_cap, tile_cols), jnp.bfloat16),
            pltpu.VMEM((groups * send_cap, tile_rows), jnp.bfloat16),
            pltpu.VMEM((groups * own_cap, tile_cols), jnp.bfloat16),
        ],
        compiler_params=pltpu.CompilerParams(vmem_limit_bytes=VMEM_BYTES),
        cost_estimate=NO_COST,
        name="packed_pieces",
    )(block_keep, row_codes[:, None], col_codes[None], row_keys[None], col_keys[None], edge_weight)


def normal_share(mixed):
    return 0.5 * (1.0 + lax.erf(mixed * 0.5**0.5))


def norm_forward(mixed):
    active = mixed * normal_share(mixed)
    centered = active - jnp.mean(active, axis=-1, keepdims=True)
    scale = lax.rsqrt(jnp.mean(centered * centered, axis=-1, keepdims=True) + 1e-05)
    return centered * scale, scale


def norm_backward(mixed, upstream, gain, valid):
    normed, scale = norm_forward(mixed)
    upstream = upstream * valid
    inner = upstream * gain
    inner = inner - jnp.mean(inner, axis=-1, keepdims=True) - normed * jnp.mean(
        inner * normed, axis=-1, keepdims=True
    )
    density = jnp.exp(-0.5 * mixed * mixed) * (1.0 / (2.0 * math.pi) ** 0.5)
    low = (inner * scale * (normal_share(mixed) + mixed * density)).astype(jnp.bfloat16)
    rest = [low.astype(jnp.float32), upstream * normed, upstream]
    return low, [jnp.sum(value, axis=0, keepdims=True) for value in rest]


def weight_gradient(turned_ref, low, core, mine_ref, other_ref):
    parts = mine_ref.shape[0]
    part = turned_ref.shape[0] // (2 * parts)

    def halves(first_ref, second_ref):
        for place in range(2 * parts):
            out_ref = second_ref if place % 2 else first_ref
            out_ref[place // 2, :part, :] = jnp.dot(
                turned_ref[place * part : (place + 1) * part, :],
                low,
                preferred_element_type=jnp.float32,
            ).astype(jnp.bfloat16)

    @pl.when(core == 0)
    def low_half_first():
        halves(mine_ref, other_ref)

    @pl.when(core == 1)
    def high_half_first():
        halves(other_ref, mine_ref)


def forward_step(step, powers_ref, all_ref, own_ref, weights, bias_ref, turned, mixed):
    terms, own_cap, span = powers_ref.shape
    fan_in = own_ref.shape[1]

    @pl.when(step == 0)
    def first():
        turned[:fan_in, :] = own_ref[...].T
        mixed[...] = bias_ref[...] + jnp.dot(
            own_ref[...], weights[0][0], preferred_element_type=jnp.float32
        )

    low = jnp.dot(
        powers_ref[...].reshape(terms * own_cap, span),
        all_ref[...],
        preferred_element_type=jnp.float32,
    ).astype(jnp.bfloat16)
    total = mixed[...]
    for term in range(terms):
        part = low[term * own_cap : (term + 1) * own_cap]
        start = pl.multiple_of((1 + step * terms + term) * fan_in, fan_in)
        turned[pl.ds(start, fan_in), :] = part.T
        total = total + jnp.dot(part, weights[1 + term][0], preferred_element_type=jnp.float32)
    mixed[...] = total


def layer_one_kernel(
    powers_ref,
    all_ref,
    own_ref,
    weight_0,
    weight_a,
    weight_b,
    weight_c,
    bias_ref,
    gain_ref,
    shift_ref,
    valid_ref,
    hidden_ref,
    turned_ref,
    mixed_ref,
):
    step = pl.program_id(0)
    weights = (weight_0, weight_a, weight_b, weight_c)
    forward_step(step, powers_ref, all_ref, own_ref, weights, bias_ref, turned_ref, mixed_ref)

    @pl.when(step == pl.num_programs(0) - 1)
    def finish_layer():
        normed, ignored = norm_forward(mixed_ref[...])
        hidden = (normed * gain_ref[...] + shift_ref[...]) * valid_ref[...]
        hidden_ref[...] = hidden.astype(jnp.bfloat16)


def layer_two_kernel(
    place_ref,
    powers_ref,
    all_ref,
    own_ref,
    weight_0,
    weight_a,
    weight_b,
    weight_c,
    bias_ref,
    gain_ref,
    shift_ref,
    valid_ref,
    upstream_ref,
    active_ref,
    low_ref,
    rest_ref,
    mine_ref,
    other_ref,
    turned,
    mixed,
):
    step = pl.program_id(0)
    weights = (weight_0, weight_a, weight_b, weight_c)
    forward_step(step, powers_ref, all_ref, own_ref, weights, bias_ref, turned, mixed)

    @pl.when(step == pl.num_programs(0) - 1)
    def finish_layer():
        normed, ignored = norm_forward(mixed[...])
        active = (normed * gain_ref[...] + shift_ref[...]) * valid_ref[...]
        active_ref[...] = active.astype(jnp.bfloat16)
        low, rest = norm_backward(
            mixed[...], upstream_ref[...].astype(jnp.float32), gain_ref[...], valid_ref[...]
        )
        low_ref[...] = low
        for place in range(3):
            rest_ref[place : place + 1, :] = rest[place]
        weight_gradient(turned, low, place_ref[1], mine_ref, other_ref)


def backward_step(step, powers_ref, all_ref, own_ref, weights, total):
    terms, own_cap, span = powers_ref.shape
    transposed = (((1,), (1,)), ((), ()))

    @pl.when(step == 0)
    def first():
        total[...] = lax.dot_general(
            own_ref[...], weights[0][0], transposed, preferred_element_type=jnp.float32
        )

    low = jnp.dot(
        powers_ref[...].reshape(terms * own_cap, span),
        all_ref[...],
        preferred_element_type=jnp.float32,
    ).astype(jnp.bfloat16)
    value = total[...]
    for term in range(terms):
        value = value + lax.dot_general(
            low[term * own_cap : (term + 1) * own_cap],
            weights[1 + term][0],
            transposed,
            preferred_element_type=jnp.float32,
        )
    total[...] = value


def back_two_kernel(
    place_ref,
    powers_ref,
    all_ref,
    own_ref,
    weight_0,
    weight_a,
    weight_b,
    weight_c,
    turned_ref,
    mixed_ref,
    gain_ref,
    valid_ref,
    rest_ref,
    low_ref,
    mine_ref,
    other_ref,
    total,
):
    step = pl.program_id(0)
    weights = (weight_0, weight_a, weight_b, weight_c)
    backward_step(step, powers_ref, all_ref, own_ref, weights, total)

    @pl.when(step == pl.num_programs(0) - 1)
    def finish_layer():
        low, rest = norm_backward(mixed_ref[...], total[...], gain_ref[...], valid_ref[...])
        low_ref[...] = low
        weight_gradient(turned_ref, low, place_ref[1], mine_ref, other_ref)
        part = turned_ref.shape[0] // 2
        extra = jnp.zeros((1, mine_ref.shape[1] - part, mine_ref.shape[2]), jnp.bfloat16)
        rows = rest + [rest_ref[place : place + 1, :] for place in range(3)]
        rows = jnp.concatenate(rows + [jnp.zeros((10, rows[0].shape[1]), jnp.float32)], axis=0)

        def below(first_ref, second_ref):
            first_ref[:, part:, :] = extra
            second_ref[:, part:, :] = extra
            first_ref[0, part : part + 16, :] = rows.astype(jnp.bfloat16)

        @pl.when(place_ref[1] == 0)
        def low_half_here():
            below(mine_ref, other_ref)

        @pl.when(place_ref[1] == 1)
        def low_half_there():
            below(other_ref, mine_ref)


def back_one_kernel(
    powers_ref, all_ref, own_ref, weight_0, weight_a, weight_b, weight_c, out_ref, total
):
    step = pl.program_id(0)
    weights = (weight_0, weight_a, weight_b, weight_c)
    backward_step(step, powers_ref, all_ref, own_ref, weights, total)

    @pl.when(step == pl.num_programs(0) - 1)
    def finish_layer():
        out_ref[...] = total[...].astype(jnp.bfloat16)


def layer_pass(kernel, name, place, powers, everyone, own, weight, others, outs, scratch):
    ignored, own_cap, span = powers.shape
    fan_in, width = weight.shape[1:]

    def whole(value):
        return pl.BlockSpec(value.shape, lambda step: (0,) * len(value.shape))

    def term_weight(term):
        return pl.BlockSpec((1, fan_in, width), lambda step: (1 + step * TERMS + term, 0, 0))

    in_specs = [
        pl.BlockSpec((TERMS, own_cap, span), lambda step: (step, 0, 0)),
        whole(everyone),
        whole(own),
        pl.BlockSpec((1, fan_in, width), lambda step: (0, 0, 0)),
    ]
    in_specs += [term_weight(term) for term in range(TERMS)] + [whole(value) for value in others]
    operands = [powers, everyone, own] + [weight] * (1 + TERMS) + list(others)
    if place is not None:
        in_specs = [pl.BlockSpec(memory_space=pltpu.SMEM)] + in_specs
        operands = [place] + operands
    return pl.pallas_call(
        kernel,
        grid=((ORDER - 1) // TERMS,),
        out_shape=outs,
        in_specs=in_specs,
        out_specs=[whole(value) for value in outs],
        scratch_shapes=[pltpu.VMEM(shape, dtype) for shape, dtype in scratch],
        compiler_params=pltpu.CompilerParams(vmem_limit_bytes=VMEM_BYTES),
        cost_estimate=NO_COST,
        name=name,
    )(*operands)


def finish_kernel(scalars_ref, pair_ref, siblings_ref, other_ref, out_ref, *small_refs):
    step = pl.program_id(0)
    part = out_ref.shape[1]
    held = pl.num_programs(0) // 2
    for here, values_ref in ((step < held, pair_ref), (step >= held, siblings_ref)):
        @pl.when(here & (scalars_ref[0] == 1))
        def fast_form():
            out_ref[0] = values_ref[0, :part, :].astype(jnp.float32)

        for small_ref in small_refs:
            @pl.when(here & (scalars_ref[1 + step] == 0))
            def small_sums():
                small_ref[...] = values_ref[0, part : part + 16, :].astype(jnp.float32)

    @pl.when(scalars_ref[0] == 0)
    def general_form():
        out_ref[0] = other_ref[0].astype(jnp.float32)


def finished(scalars, pair, siblings, other, with_small=False):
    count, part, width = other.shape
    out, held = (1, part, width), (1,) + pair.shape[1:]
    out_specs = [pl.BlockSpec(out, lambda step, ref: (ref[1 + step], 0, 0))]
    out_shape = [jax.ShapeDtypeStruct(other.shape, jnp.float32)]
    if with_small:
        out_specs.append(pl.BlockSpec((16, width), lambda step, ref: (0, 0)))
        out_shape.append(jax.ShapeDtypeStruct((16, width), jnp.float32))
    return pl.pallas_call(
        finish_kernel,
        grid_spec=pltpu.PrefetchScalarGridSpec(
            num_scalar_prefetch=1,
            grid=(count,),
            in_specs=[
                pl.BlockSpec(held, lambda step, ref: (jnp.minimum(step, count // 2 - 1), 0, 0)),
                pl.BlockSpec(held, lambda step, ref: (jnp.maximum(step - count // 2, 0), 0, 0)),
                pl.BlockSpec(out, lambda step, ref: ((1 - ref[0]) * ref[1 + step], 0, 0)),
            ],
            out_specs=out_specs,
        ),
        out_shape=out_shape,
        compiler_params=pltpu.CompilerParams(vmem_limit_bytes=VMEM_BYTES),
        cost_estimate=pl.CostEstimate(
            flops=other.size, bytes_accessed=6 * other.size, transcendentals=0
        ),
        name="finished",
    )(scalars, pair, siblings, other)


def unpack_kernel(place_ref, pieces_ref, keys_ref, own_ref, quadrant_ref, columns, hot):
    groups, high, lanes = pieces_ref.shape
    own_cap, span = own_ref.shape
    whole = own_cap // lanes
    send_cap = keys_ref.shape[1] // groups
    half, rest = send_cap // 2, own_cap - whole * lanes
    for group in range(groups):
        start = group * send_cap
        for tile in range(whole):
            columns[start : start + send_cap, tile * lanes : (tile + 1) * lanes] = pieces_ref[
                group, tile * send_cap : (tile + 1) * send_cap, :
            ]
        ends = pieces_ref[group, whole * send_cap :, :]
        columns[start : start + half, whole * lanes :] = ends[:, :rest]
        columns[start + half : start + send_cap, whole * lanes :] = ends[:, rest:]
    standing = lax.broadcasted_iota(jnp.int32, hot.shape, 0)
    hot[...] = jnp.where(standing == keys_ref[...], 1.0, 0.0).astype(jnp.bfloat16)
    block = jnp.dot(hot[...], columns[...], preferred_element_type=jnp.float32)
    own_ref[...] = block.T.astype(jnp.bfloat16)
    middle = span // 2

    @pl.when(place_ref[0] == 0)
    def first():
        quadrant_ref[...] = own_ref[:, :middle]

    @pl.when(place_ref[0] == 1)
    def second():
        quadrant_ref[...] = own_ref[:, middle:]


def unpacked_block(pieces, keys, place, own_cap, span):
    vector = pl.BlockSpec(memory_space=pltpu.VMEM)
    return pl.pallas_call(
        unpack_kernel,
        out_shape=[
            jax.ShapeDtypeStruct((own_cap, span), jnp.bfloat16),
            jax.ShapeDtypeStruct((own_cap, span // 2), jnp.bfloat16),
        ],
        in_specs=[pl.BlockSpec(memory_space=pltpu.SMEM), vector, vector],
        out_specs=[vector, vector],
        scratch_shapes=[
            pltpu.VMEM((keys.shape[1], own_cap), jnp.bfloat16),
            pltpu.VMEM((span, keys.shape[1]), jnp.bfloat16),
        ],
        compiler_params=pltpu.CompilerParams(vmem_limit_bytes=VMEM_BYTES),
        cost_estimate=NO_COST,
        name="unpacked_block",
    )(place, pieces, keys)


def fit_kernel(codes_ref, out_ref, *, n_row, caps):
    own_cap, send_cap, seat_cap = caps
    codes = codes_ref[...]
    devices = codes.shape[0]
    n_col = devices // n_row
    label = lax.broadcasted_iota(jnp.int32, (devices, 128), 1)
    counts = jnp.zeros((devices, 128), jnp.float32)
    for cluster in range(CLUSTERS):
        here = jnp.where(codes == 2 * cluster + 1, 1.0, 0.0)
        counts = counts + jnp.where(
            label == cluster, jnp.sum(here, axis=1, keepdims=True), 0.0
        )
    sizes = jnp.sum(counts, axis=0, keepdims=True)
    across = jnp.broadcast_to(sizes, (128, 128))
    down = across.T
    first = lax.broadcasted_iota(jnp.int32, (128, 128), 0)
    second = lax.broadcasted_iota(jnp.int32, (128, 128), 1)
    ahead = (across > down) | ((across == down) & (second < first))
    ahead = ahead & (second < CLUSTERS)
    rank = jnp.sum(jnp.where(ahead, 1.0, 0.0), axis=1, keepdims=True).astype(jnp.int32)
    others = n_row - 1
    later = rank > others
    turn = jnp.zeros_like(rank)
    for count in range(1, CLUSTERS // others + 1):
        turn = turn + jnp.where(rank - 1 >= count * others, 1, 0)
    place = rank - 1 - turn * others
    group = jnp.where(rank == 0, 0, 1 + jnp.where(later, others - 1 - place, place))
    member = (group == second) & (first < CLUSTERS)
    held = jnp.dot(
        counts.astype(jnp.bfloat16),
        jnp.where(member, 1.0, 0.0).astype(jnp.bfloat16),
        preferred_element_type=jnp.float32,
    )
    by_row = jnp.zeros((1, 128), jnp.float32)
    for row in range(n_row):
        rows = jnp.sum(held[row * n_col : (row + 1) * n_col], axis=0, keepdims=True)
        by_row = jnp.maximum(by_row, rows)
    device = lax.broadcasted_iota(jnp.int32, (devices, 128), 0)
    by_col = jnp.zeros((1, 128), jnp.float32)
    for col in range(n_col):
        cols = jnp.where(device % n_col == col, held, 0.0)
        by_col = jnp.maximum(by_col, jnp.sum(cols, axis=0, keepdims=True))
    fits = (
        (jnp.max(by_col) <= own_cap) & (jnp.max(by_row) <= send_cap) & (jnp.max(held) <= seat_cap)
    )
    out_ref[0] = jnp.where(fits, 1, 0)


def fits_in(codes, n_row, caps):
    fits = pl.pallas_call(
        functools.partial(fit_kernel, n_row=n_row, caps=caps),
        out_shape=jax.ShapeDtypeStruct((1,), jnp.int32),
        in_specs=[pl.BlockSpec(memory_space=pltpu.VMEM)],
        out_specs=pl.BlockSpec(memory_space=pltpu.SMEM),
        cost_estimate=NO_COST,
        name="fits",
    )(codes.reshape(-1, codes.shape[-1]))
    return fits


def exclusive_counts(member):
    count = member.shape[-1]
    before = jnp.arange(count)[:, None] < jnp.arange(count)[None, :]
    return jnp.dot(
        member.astype(jnp.bfloat16),
        before.astype(jnp.bfloat16),
        preferred_element_type=jnp.float32,
    ).astype(jnp.int32)


def assign(codes, n_row):
    cluster, valid = codes >> 1, codes & 1
    labels = jnp.arange(CLUSTERS)
    sizes = jnp.sum(
        (cluster.reshape(1, -1) == labels[:, None]) & (valid.reshape(1, -1) == 1), axis=1
    )
    ahead = (sizes[None, :] > sizes[:, None]) | (
        (sizes[None, :] == sizes[:, None]) & (labels[None, :] < labels[:, None])
    )
    rank = jnp.sum(ahead, axis=1)
    others = n_row - 1
    turn, place = (rank - 1) // others, (rank - 1) % others
    group = jnp.where(rank == 0, 0, 1 + jnp.where(turn == 0, place, others - 1 - place))
    of_node = jnp.sum(
        jnp.where(cluster[None] == labels[:, None, None, None], group[:, None, None, None], 0),
        axis=0,
    )
    return jnp.where(valid == 1, of_node, n_row)


def compact(
    codes,
    group,
    features,
    block_keep,
    edge_weight,
    weight_one,
    bias_one,
    gain_one,
    shift_one,
    weight_two,
    bias_two,
    gain_two,
    shift_two,
    cotangent,
    places_of,
    slots_of,
    seats_of,
    decide,
    sizes,
    caps,
):
    row, col = lax.axis_index("row"), lax.axis_index(COL)
    chip, core = lax.axis_index("chip"), lax.axis_index("core")
    n_row, n_col = sizes
    own_cap, send_cap, seat_cap = caps
    own_nodes, in_width = features.shape
    width = weight_two.shape[2]
    span = n_col * own_cap
    targets = jnp.arange(n_row)

    def in_col(value):
        return lax.dynamic_index_in_dim(value, col, 1, False).reshape(-1)

    def in_row(value):
        return lax.dynamic_index_in_dim(value, row, 0, False).reshape(-1)

    row_group, col_group = in_row(group), in_col(group)
    row_slots, col_places = in_row(slots_of(group)), in_col(places_of(group))
    row_keys = jnp.where(row_slots < send_cap, row_group * send_cap + row_slots, -1)
    col_keys = jnp.where(col_places < own_cap, col_group * own_cap + col_places, -1)
    pieces = packed_pieces(
        block_keep,
        in_row(codes),
        in_col(codes),
        row_keys,
        col_keys,
        edge_weight,
        (own_cap, send_cap),
        n_row,
    )
    pieces, codes = lax.optimization_barrier((pieces, codes))
    group = assign(codes, n_row)
    places, slots, seats = places_of(group), slots_of(group), seats_of(group)

    standing = jnp.arange(n_col)[None, :, None] * own_cap + places
    fits_here = jnp.where(group == row, standing, -1).reshape(n_row, -1)
    slot_of = slots.reshape(n_row, -1)
    target = jnp.max(
        jnp.where(
            slot_of[:, None, :] == jnp.arange(send_cap)[None, :, None], fits_here[:, None, :], -1
        ),
        axis=2,
    )
    keys = target.reshape(1, -1)

    def to_partner(value, step):
        return lax.ppermute(value, "row", [(place, place ^ step) for place in range(n_row)])

    partners = row ^ targets
    group_here = lax.dynamic_index_in_dim(in_row(group).reshape(n_col, -1), col, 0, False)
    seat_here = lax.dynamic_index_in_dim(in_row(seats).reshape(n_col, -1), col, 0, False)

    def seat_of_node(groups):
        hot = (group_here[None, None, :] == groups[:, None, None]) & (
            seat_here[None, None, :] == jnp.arange(seat_cap)[None, :, None]
        )
        return hot.astype(jnp.bfloat16).reshape(n_row * seat_cap, own_nodes)

    enter_home = seat_of_node(targets).T
    enter_partner = seat_of_node(partners)
    both = jnp.dot(enter_partner, jnp.concatenate([features, cotangent], axis=1))
    both = both.reshape(n_row, seat_cap, -1)
    enter_partner = enter_partner.T
    pieces = trade(pieces, "row")
    both, codes = lax.optimization_barrier((both, codes))
    both = [both[step] for step in range(n_row)]
    both[1] = to_partner(both[1], 1)
    fits, others = decide(codes)
    group_col = lax.dynamic_index_in_dim(group, col, 1, False)
    seats_col = lax.dynamic_index_in_dim(seats, col, 1, False)
    places_col = lax.dynamic_index_in_dim(places, col, 1, False)
    seated = (group_col == row)[:, None, :] & (
        seats_col[:, None, :] == jnp.arange(seat_cap)[None, :, None]
    )
    place_of_seat = jnp.max(jnp.where(seated, places_col[:, None, :], -1), axis=2)
    from_partner = jnp.max(
        jnp.where((partners[:, None] == targets)[:, :, None], place_of_seat[None], -1), axis=1
    )
    arrive = from_partner.reshape(1, -1) == jnp.arange(own_cap)[:, None]
    arrive = arrive.astype(jnp.bfloat16)
    leave_group = place_of_seat.reshape(-1, 1) == jnp.arange(own_cap)
    leave_group = leave_group.astype(jnp.bfloat16)
    leave_partner = jnp.concatenate([from_partner[::2], from_partner[1::2]])
    leave_partner = leave_partner.reshape(-1, 1) == jnp.arange(own_cap)
    leave_partner = leave_partner.astype(jnp.bfloat16)
    held_count = jnp.sum(group_col == row)
    valid_rows = (jnp.arange(own_cap) < held_count).astype(jnp.float32)[:, None]
    place = jnp.stack([chip, core]).astype(jnp.int32)
    quarters = jnp.stack([col, (1 - chip) * 2 + core, chip * 2 + 1 - core, 3 - col])
    quarters = jnp.concatenate([fits, quarters.astype(jnp.int32)])
    own_halves = jnp.concatenate([fits, jnp.stack([core, 1 - core]).astype(jnp.int32)])
    scalars = (chip, 1 - chip, col * own_cap)
    scalars = tuple(value.astype(jnp.uint32) for value in scalars) + (chip == 0, core == 0, place)
    scalars = scalars + (quarters, own_halves)
    homes = enter_home, enter_partner, leave_group, leave_partner
    pieces, both, keys, arrive, homes, valid_rows, others, scalars = lax.optimization_barrier(
        (pieces, both, keys, arrive, homes, valid_rows, others, scalars)
    )
    enter_home, enter_partner, leave_group, leave_partner = homes
    this_chip, other_chip, own_start, first_chip, first_core = scalars[:5]
    place, quarters, own_halves = scalars[5:]

    own_block, quadrant = unpacked_block(pieces, keys, place, own_cap, span)
    quadrant = swap(quadrant, "chip")
    both = both[:2] + [to_partner(both[step], step) for step in range(2, n_row)]
    sibling = swap(own_block, "core")
    quadrant, *early = lax.optimization_barrier((quadrant, *both[:-2]))
    adjacency = normalized_block(own_block, sibling, quadrant, swap(quadrant, "core"), place)
    adjacency, *late = lax.optimization_barrier((adjacency, *both[-2:]))
    both = early + late
    mine = jnp.dot(arrive, jnp.concatenate(both))
    features_own, cotangent_own = mine[:, :in_width], mine[:, in_width:]
    sibling = swap(features_own, "core")

    first = (own_start + jnp.arange(own_cap, dtype=jnp.uint32))[:, None]
    first = first == jnp.arange(span, dtype=jnp.uint32)[None, :]
    previous = first.astype(jnp.float32)
    current = -lax.dynamic_slice_in_dim(adjacency, own_start, own_cap, 0).astype(jnp.float32)
    lowered = [current.astype(jnp.bfloat16)]
    for position in range(2, ORDER):
        upcoming = (
            -2.0 * jnp.dot(lowered[-1], adjacency, preferred_element_type=jnp.float32) - previous
        )
        low = upcoming.astype(jnp.bfloat16)
        if position == 4:
            low, sibling = lax.optimization_barrier((low, sibling))
            features_chip = joined(features_own, sibling, first_core)
            partner = swap(features_chip, "chip")
        if position == 8:
            low, partner = lax.optimization_barrier((low, partner))
            features_all = joined(features_chip, partner, first_chip)
        previous, current = current, upcoming
        lowered.append(low)
    powers = jnp.concatenate(lowered, axis=0).reshape(ORDER - 1, own_cap, span)

    def everywhere(value_low):
        return lax.all_gather(value_low, COL, axis=0, tiled=True)

    def chosen(value, other):
        return jnp.where(quarters[0] == 1, value.astype(jnp.float32), other.astype(jnp.float32))

    def shaped(*shape, dtype=jnp.bfloat16):
        return jax.ShapeDtypeStruct(shape, dtype)

    part_one, part_two = ORDER * in_width // 2, ORDER * width // n_col
    padded = -(-(part_one + 16) // (16 * n_row)) * (16 * n_row)
    hidden, turned_one, mixed_one = layer_pass(
        layer_one_kernel,
        "layer_one",
        None,
        powers,
        features_all,
        features_own,
        weight_one,
        [bias_one[None], gain_one[None], shift_one[None], valid_rows],
        [
            shaped(own_cap, width),
            shaped(2 * part_one, own_cap),
            shaped(own_cap, width, dtype=jnp.float32),
        ],
        [],
    )
    activations, low_two, rest_two, mine, other = layer_pass(
        layer_two_kernel,
        "layer_two",
        place,
        powers,
        everywhere(hidden),
        hidden,
        weight_two,
        [bias_two[None], gain_two[None], shift_two[None], valid_rows, cotangent_own],
        [
            shaped(own_cap, width),
            shaped(own_cap, width),
            shaped(3, width, dtype=jnp.float32),
            shaped(2, part_two, width),
            shaped(2, part_two, width),
        ],
        [((n_col * part_two, own_cap), jnp.bfloat16), ((own_cap, width), jnp.float32)],
    )

    def add_cores(mine, other, axis=0):
        got = swap(other, "core")
        return tuple(
            added(
                lax.dynamic_index_in_dim(mine, index, axis, False),
                lax.dynamic_index_in_dim(got, index, axis, False),
            )
            for index in (this_chip, other_chip)
        )

    leaving = jnp.dot(leave_partner, activations).reshape(n_row, seat_cap, width)
    near, far = leaving[: n_row // 2], leaving[n_row // 2 :]
    far = to_partner(far, 1)
    here, there = add_cores(mine, other)
    everyone_two, there, far = lax.optimization_barrier((everywhere(low_two), there, far))
    there = swap(there, "chip")
    arrived = [jnp.stack([near[0], far[0]])] + [
        to_partner(jnp.stack([near[half], far[half]]), 2 * half) for half in range(1, n_row // 2)
    ]
    low_one, mine, other = layer_pass(
        back_two_kernel,
        "back_two",
        place,
        powers,
        everyone_two,
        low_two,
        weight_two,
        [turned_one, mixed_one, gain_one[None], valid_rows, rest_two],
        [shaped(own_cap, width), shaped(1, padded, width), shaped(1, padded, width)],
        [((own_cap, width), jnp.float32)],
    )
    low_one, there, arrived = lax.optimization_barrier((low_one, there, arrived))
    second = added(here, there).reshape(n_row, -1, width)
    many = second.shape[1]
    low_one, second = lax.optimization_barrier((low_one, second))
    second = trade(second, "row")
    mine, other = (value.reshape(n_row, 2, -1, width) for value in (mine, other))
    here, there = add_cores(mine, other, 1)
    there = swap(there, "chip")
    first = added(here, there)
    second = jnp.sum(second.astype(jnp.float32), axis=0).astype(jnp.bfloat16)
    second = jnp.broadcast_to(second[None], (n_row,) + second.shape)
    mixed = jnp.concatenate([second, first], axis=1)
    low_one, mixed = lax.optimization_barrier((low_one, mixed))
    everyone_one = everywhere(low_one)
    mixed = trade(mixed, "row")
    (input_grad,) = layer_pass(
        back_one_kernel,
        "back_one",
        None,
        powers,
        everyone_one,
        low_one,
        weight_one,
        [],
        [shaped(own_cap, in_width)],
        [((own_cap, in_width), jnp.float32)],
    )
    leaving = jnp.dot(leave_group, input_grad)
    leaving = leaving.reshape(n_row, seat_cap * in_width // width, width)
    mixed, leaving, arrived = lax.optimization_barrier((mixed, leaving, arrived))
    first = jnp.sum(mixed[:, many:].astype(jnp.float32), axis=0).astype(jnp.bfloat16)
    partner, mixed = lax.optimization_barrier((swap(first, "chip"), mixed))
    second = mixed[:, :many].reshape(1, -1, width)
    partner_two = swap(second, "chip")
    first = joined(first, partner, first_chip)
    share = first.shape[0]
    first = jnp.broadcast_to(first[None], (n_row,) + first.shape)
    first = trade(jnp.concatenate([first, leaving], axis=1), "row")
    second = jnp.concatenate([second, partner_two])
    (second,) = finished(quarters, second, swap(second, "core"), others[3])
    arrived = jnp.concatenate(arrived).reshape(-1, width)
    home = jnp.dot(enter_partner, arrived, preferred_element_type=jnp.float32)
    home = chosen(home, others[0])
    first, second, home = lax.optimization_barrier((first, second, home))
    mine = first[:, :share].reshape(1, -1, width)
    siblings = swap(mine, "core")
    back = first[:, share:].reshape(n_row * seat_cap, in_width)
    home_grad = jnp.dot(enter_home, back, preferred_element_type=jnp.float32)
    home_grad = chosen(home_grad, others[1])
    first, small = finished(own_halves, mine, siblings, others[2], True)
    return home, home_grad, first, second, chosen(small[:6], others[4])


def general(
    codes,
    features,
    block_keep,
    edge_weight,
    weight_one,
    bias_one,
    gain_one,
    shift_one,
    weight_two,
    bias_two,
    gain_two,
    shift_two,
    cotangent,
    node_valid,
):
    row, col = lax.axis_index("row"), lax.axis_index(COL)
    row_codes = lax.dynamic_index_in_dim(codes, row, 0, False).reshape(-1)
    col_codes = lax.dynamic_index_in_dim(codes, col, 1, False).reshape(-1)
    tile_rows, tile_cols = edge_weight.shape
    blocks_down, blocks_across = block_keep.shape
    block_side = tile_rows // blocks_down
    linked = (row_codes[:, None] == col_codes[None, :]) & (row_codes[:, None] & 1 == 1)
    linked = linked.reshape(blocks_down, block_side, blocks_across, block_side) & (
        block_keep[:, None, :, None] == 1
    )
    masked = edge_weight * linked.reshape(tile_rows, tile_cols).astype(jnp.bfloat16)
    degree_rows = 1.0 + lax.psum(jnp.sum(masked, axis=1, dtype=jnp.float32), COL)
    own_nodes = features.shape[0]
    own_degree = lax.dynamic_slice_in_dim(
        degree_rows, lax.axis_index(COL) * own_nodes, own_nodes, 0
    )
    degree_cols = lax.all_gather(own_degree, "row", axis=0, tiled=True)
    adjacency = (
        masked.astype(jnp.float32)
        * lax.rsqrt(degree_rows)[:, None]
        * lax.rsqrt(degree_cols)[None, :]
    ).astype(jnp.bfloat16)
    valid_rows = node_valid.astype(jnp.float32)
    stacked_one, mixed_one, hidden = layer_forward(
        adjacency,
        features.astype(jnp.float32),
        weight_one,
        bias_one,
        gain_one,
        shift_one,
        valid_rows,
    )
    stacked_two, mixed_two, activations = layer_forward(
        adjacency, hidden, weight_two, bias_two, gain_two, shift_two, valid_rows
    )
    hidden_grad, weight_two_grad, bias_two_grad, gain_two_grad, shift_two_grad = layer_backward(
        adjacency,
        stacked_two,
        mixed_two,
        cotangent.astype(jnp.float32),
        weight_two,
        gain_two,
        shift_two,
        valid_rows,
    )
    input_grad, weight_one_grad, bias_one_grad, gain_one_grad, shift_one_grad = layer_backward(
        adjacency, stacked_one, mixed_one, hidden_grad, weight_one, gain_one, shift_one, valid_rows
    )
    summed = lax.psum(
        (
            weight_one_grad,
            bias_one_grad,
            gain_one_grad,
            shift_one_grad,
            weight_two_grad,
            bias_two_grad,
            gain_two_grad,
            shift_two_grad,
        ),
        ("row",) + COL,
    )
    weight_one_grad, bias_one_grad, gain_one_grad, shift_one_grad = (
        summed[0],
        summed[1],
        summed[2],
        summed[3],
    )
    weight_two_grad, bias_two_grad, gain_two_grad, shift_two_grad = (
        summed[4],
        summed[5],
        summed[6],
        summed[7],
    )
    return (
        activations,
        input_grad,
        weight_one_grad,
        bias_one_grad,
        gain_one_grad,
        shift_one_grad,
        weight_two_grad,
        bias_two_grad,
        gain_two_grad,
        shift_two_grad,
    )


def local(n_row, n_col, *args):
    (
        features,
        node_valid,
        cluster,
        block_keep,
        edge_weight,
        weight_one,
        bias_one,
        gain_one,
        shift_one,
        weight_two,
        bias_two,
        gain_two,
        shift_two,
        cotangent,
    ) = args
    own_nodes, in_width = features.shape
    own_cap = own_nodes * n_row * 5 // 16
    send_cap = own_nodes * n_col * 11 // 32
    seat_cap = own_nodes * 7 // 16
    codes = broadcast_along(cluster * 2 + node_valid, ("row",) + COL, n_row * n_col)
    codes = codes.reshape(n_row, n_col, own_nodes)
    shared = (
        block_keep,
        edge_weight,
        weight_one,
        bias_one,
        gain_one,
        shift_one,
        weight_two,
        bias_two,
        gain_two,
        shift_two,
        cotangent,
    )

    def slow():
        return general(codes, features, *shared, node_valid)

    held = (ORDER - 1) * own_cap * own_cap * n_col * 2
    if held > HELD_BYTES or n_col != 4 or n_row < 2 or n_row & (n_row - 1):
        return slow()
    group = assign(codes, n_row)

    def member_of(group):
        return group[None] == jnp.arange(n_row)[:, None, None, None]

    def places_of(group):
        member = member_of(group).transpose(0, 2, 1, 3).reshape(n_row, n_col, -1)
        places = jnp.sum(jnp.where(member, exclusive_counts(member), 0), axis=0)
        return places.reshape(n_col, n_row, own_nodes).transpose(1, 0, 2)

    def slots_of(group):
        member = member_of(group).reshape(n_row, n_row, -1)
        slots = jnp.sum(jnp.where(member, exclusive_counts(member), 0), axis=0)
        return slots.reshape(n_row, n_col, own_nodes)

    def seats_of(group):
        member = member_of(group)
        return jnp.sum(jnp.where(member, exclusive_counts(member), 0), axis=0)

    width = weight_two.shape[2]

    def instead(state):
        made = slow()
        small = jnp.stack([made[place] for place in (3, 4, 5, 7, 8, 9)])
        return (jnp.ones_like(state[0]),) + tuple(
            value.astype(jnp.bfloat16).reshape(like.shape)
            for value, like in zip((made[0], made[1], made[2], made[6], small), state[1:])
        )

    shapes = (
        (own_nodes, width),
        (own_nodes, in_width),
        (2, ORDER * in_width // 2, width),
        (n_col, ORDER * width // n_col, width),
        (6, width),
    )

    def decide(codes):
        fits = fits_in(codes, n_row, (own_cap, send_cap, seat_cap))
        others = lax.while_loop(
            lambda state: state[0][0] == 0,
            instead,
            (fits,) + tuple(jnp.zeros(shape, jnp.bfloat16) for shape in shapes),
        )[1:]
        return fits, others

    home, home_grad, first, second, small = compact(
        codes,
        group,
        features,
        *shared,
        places_of,
        slots_of,
        seats_of,
        decide,
        (n_row, n_col),
        (own_cap, send_cap, seat_cap),
    )
    return (
        home,
        home_grad,
        first.reshape(weight_one.shape),
        small[0],
        small[1],
        small[2],
        second.reshape(weight_two.shape),
        small[3],
        small[4],
        small[5],
    )


def solution(mesh):
    n_row, n_col = mesh.shape["row"], mesh.shape["col"]
    by_core = jax.sharding.Mesh(
        mesh.devices.reshape(n_row, n_col // 2, 2), ("row", "chip", "core")
    )
    nodes = ("row", "chip", "core")
    placed = (
        P(nodes, None),
        P(nodes),
        P(nodes),
        P("row", COL),
        P("row", COL),
        P(),
        P(),
        P(),
        P(),
        P(),
        P(),
        P(),
        P(),
        P(nodes, None),
    )
    return jax.shard_map(
        functools.partial(local, n_row, n_col),
        mesh=by_core,
        in_specs=placed,
        out_specs=(P(nodes, None), P(nodes, None), P(), P(), P(), P(), P(), P(), P(), P()),
        check_vma=False,
    )
```
